32 devices in a mesh: load: 2 (over core), sy: 4 (over y, x), sz: 4 (over z).
Axes of the slice: x: 2, y: 2, z: 4, core: 2. Of those that a mesh axis runs over, the one named last changes fastest.
Arguments:
- displacements: float32 [4, 3, 16, 64, 512], P('load', None, 'sz', 'sy'), may hold values from -2.4 to 2.4
- density: float32 [16, 64, 512], P('sz', 'sy'), may hold values from 0.05 to 1
- solid: int32 [16, 64, 512], P('sz', 'sy'), may hold values 0 or 1
- fixed: int32 [16, 64, 512], P('sz', 'sy'), may hold values 0 or 1
Outputs:
- sensitivity: float32 [16, 64, 512], P('sz', 'sy')
The draws below stay inside these ranges and needn't reach their ends.
All inputs are finite; a program needn't handle non-finite values. No bound on the sum of `solid` or of `fixed` on one device may be relied on, other than what follows from the above.
Results may differ from the reference program's by a relative error of at most 0.0001.
Values sent between devices are 32-bit elements; how exact they have to be, the bound alone decides.
No kernel may reach another device: no remote copies, remote signals or barrier semaphores. Data moves between devices by JAX's collectives and lax.ppermute only.
A program may use at most 64 MiB of HBM per device.

```python
import math
import jax
import jax.numpy as jnp
import numpy as np
from jax import lax

NX = 512
LOADS = 4
NY = 64
NZ = 16


def with_ends(drawn, rng, least, high):
    extent = drawn.shape
    spot = [jax.random.randint(jax.random.fold_in(rng, axis), (), 0, extent[axis]) for axis in range(len(extent))]
    drawn = drawn.at[tuple(spot)].set(least)
    longest = extent.index(max(extent))
    spot[longest] = (spot[longest] + 1) % extent[longest]
    return drawn.at[tuple(spot)].set(high)


def shard_levels(stream_key, dims, shards, least, high):
    level = 1.0
    for dim, blocks in shards:
        draws = jax.random.uniform(jax.random.fold_in(jax.random.fold_in(stream_key, 6), dim), (blocks,), jnp.float32, least / len(shards), high / len(shards))
        level = level * jnp.repeat(jnp.exp(draws), dims[dim] // blocks).reshape((-1,) + (1,) * (len(dims) - 1 - dim))
    return level


def gaussian(stream_key, extent, deviation, reach, shards=(), kind=jnp.bfloat16):
    values = jax.random.normal(stream_key, extent, jnp.float32) * deviation
    if len(shards) > 0:
        values = shard_levels(stream_key, extent, shards, -0.22, 0.18) * values
    return jnp.clip(values, min=-reach, max=reach).astype(kind)


def setup_inputs(seed: int = 0) -> dict:
    arg_keys = jax.random.split(jax.random.key(seed), 5)
    displacements = gaussian(arg_keys[0], (LOADS, 3, NZ, NY, NX), 0.3, 2.4, ((0, 2), (2, 4), (3, 4)), jnp.float32)
    density = jnp.clip(jnp.exp(math.log(1.0) - 2.9957323 * jax.random.uniform(arg_keys[1], (NZ, NY, NX), jnp.float32) ** shard_levels(arg_keys[1], (NZ, NY, NX), ((0, 4), (1, 4)), -0.2, 0.2)), 0.05, 1.0)
    solid = with_ends((jax.random.randint(arg_keys[2], (NZ, NY, NX), 0, 4) < 3).astype(jnp.int32), jax.random.fold_in(arg_keys[2], 1), 0, 1)
    fixed = with_ends((jax.random.randint(arg_keys[3], (NZ, NY, NX), 0, 8) < 1).astype(jnp.int32), jax.random.fold_in(arg_keys[3], 1), 0, 1)
    return dict(displacements=displacements, density=density, solid=solid, fixed=fixed)


def element_matrix():
    corners = np.array([[-1.0, -1.0, -1.0], [1.0, -1.0, -1.0], [1.0, 1.0, -1.0], [-1.0, 1.0, -1.0], [-1.0, -1.0, 1.0], [1.0, -1.0, 1.0], [1.0, 1.0, 1.0], [-1.0, 1.0, 1.0]])
    poisson = 0.3
    lame = poisson / ((1.0 + poisson) * (1.0 - 2.0 * poisson))
    shear = 1.0 / (2.0 * (1.0 + poisson))
    elastic = np.zeros((6, 6))
    elastic[:3, :3] = lame
    for k in range(3):
        elastic[k, k] += 2.0 * shear
        elastic[3 + k, 3 + k] = shear
    gauss = 1.0 / np.sqrt(3.0)
    stiffness = np.zeros((24, 24))
    for gi in range(2):
        for gj in range(2):
            for gk in range(2):
                point = np.array([(2 * gi - 1) * gauss, (2 * gj - 1) * gauss, (2 * gk - 1) * gauss])
                strain = np.zeros((6, 24))
                for node in range(8):
                    grads = np.zeros(3)
                    for k in range(3):
                        value = corners[node, k] / 8.0
                        for m in range(3):
                            if m != k:
                                value = value * (1.0 + point[m] * corners[node, m])
                        grads[k] = 2.0 * value
                    col = 3 * node
                    strain[0, col] = grads[0]
                    strain[1, col + 1] = grads[1]
                    strain[2, col + 2] = grads[2]
                    strain[3, col] = grads[1]
                    strain[3, col + 1] = grads[0]
                    strain[4, col + 1] = grads[2]
                    strain[4, col + 2] = grads[1]
                    strain[5, col] = grads[2]
                    strain[5, col + 2] = grads[0]
                stiffness += strain.T @ elastic @ strain / 8.0
    return stiffness
OFFSETS = [(0, 0, 0), (1, 0, 0), (1, 1, 0), (0, 1, 0), (0, 0, 1), (1, 0, 1), (1, 1, 1), (0, 1, 1)]

def weight_line(coord, count):
    total = jnp.zeros(coord.shape, jnp.float32)
    for step in range(-3, 4):
        inside = (coord + step >= 0) & (coord + step < count)
        total = total + jnp.where(inside, 4.0 - abs(step), 0.0).astype(jnp.float32)
    return total

def spread_axis(padded, axis, length):
    total = None
    for k in range(7):
        piece = (4.0 - abs(k - 3)) * lax.slice_in_dim(padded, k, k + length, axis=axis)
        total = piece if total is None else total + piece
    return total

def reference(displacements, density, solid, fixed):
    stiffness = jnp.asarray(element_matrix(), jnp.float32)
    held = displacements * (1 - fixed).astype(jnp.float32)[None, None]
    padded = jnp.pad(held, ((0, 0), (0, 0), (0, 1), (0, 1), (0, 1)))

    def slab_energy(zidx):
        block = lax.dynamic_slice_in_dim(padded, zidx, 2, axis=2)
        nodes = [block[:, :, c, b:b + NY, a:a + NX] for a, b, c in OFFSETS]
        local = jnp.stack(nodes, axis=1).reshape(LOADS, 24, NY * NX)
        image = jnp.einsum('ij,ljc->lic', stiffness, local, precision=lax.Precision.HIGHEST)
        return lax.optimization_barrier(jnp.sum(local * image, axis=(0, 1))).reshape(NY, NX)
    energy = lax.map(slab_energy, jnp.arange(NZ, dtype=jnp.int32))
    term = solid.astype(jnp.float32) * (-3.0 * density * density) * energy
    hz = weight_line(jnp.arange(NZ, dtype=jnp.int32), NZ)
    hy = weight_line(jnp.arange(NY, dtype=jnp.int32), NY)
    hx = weight_line(jnp.arange(NX, dtype=jnp.int32), NX)
    quotient = term / (hz[:, None, None] * hy[None, :, None] * hx[None, None, :])
    padq = jnp.pad(quotient, 3)
    result = spread_axis(padq, 2, NX)
    result = spread_axis(result, 1, NY)
    result = spread_axis(result, 0, NZ)
    return result
```

```python
import jax
import jax.numpy as jnp
import numpy as np
from jax import lax
from jax.experimental import pallas as pl
from jax.experimental.pallas import tpu as pltpu
from jax.sharding import PartitionSpec as P

OFFSETS = [(0, 0, 0), (1, 0, 0), (1, 1, 0), (0, 1, 0), (0, 0, 1), (1, 0, 1), (1, 1, 1), (0, 1, 1)]
REACH = 3
ROWS = REACH + 1
TILE = 8
LANES = 128


def element_matrix():
    corners = np.array(
        [
            [-1.0, -1.0, -1.0],
            [1.0, -1.0, -1.0],
            [1.0, 1.0, -1.0],
            [-1.0, 1.0, -1.0],
            [-1.0, -1.0, 1.0],
            [1.0, -1.0, 1.0],
            [1.0, 1.0, 1.0],
            [-1.0, 1.0, 1.0],
        ]
    )
    poisson = 0.3
    lame = poisson / ((1.0 + poisson) * (1.0 - 2.0 * poisson))
    shear = 1.0 / (2.0 * (1.0 + poisson))
    elastic = np.zeros((6, 6))
    elastic[:3, :3] = lame
    for k in range(3):
        elastic[k, k] += 2.0 * shear
        elastic[3 + k, 3 + k] = shear
    gauss = 1.0 / np.sqrt(3.0)
    stiffness = np.zeros((24, 24))
    for gi in range(2):
        for gj in range(2):
            for gk in range(2):
                point = np.array([(2 * gi - 1) * gauss, (2 * gj - 1) * gauss, (2 * gk - 1) * gauss])
                strain = np.zeros((6, 24))
                for node in range(8):
                    grads = np.zeros(3)
                    for k in range(3):
                        value = corners[node, k] / 8.0
                        for m in range(3):
                            if m != k:
                                value = value * (1.0 + point[m] * corners[node, m])
                        grads[k] = 2.0 * value
                    col = 3 * node
                    strain[0, col] = grads[0]
                    strain[1, col + 1] = grads[1]
                    strain[2, col + 2] = grads[2]
                    strain[3, col] = grads[1]
                    strain[3, col + 1] = grads[0]
                    strain[4, col + 1] = grads[2]
                    strain[4, col + 2] = grads[1]
                    strain[5, col] = grads[2]
                    strain[5, col + 2] = grads[0]
                stiffness += strain.T @ elastic @ strain / 8.0
    return stiffness


def mode_weights():
    modes = [(i, j, k) for k in (0, 1) for j in (0, 1) for i in (0, 1)]
    sums = np.zeros((24, 24))
    for m, mode in enumerate(modes):
        for n, corner in enumerate(OFFSETS):
            sign = np.prod([(1 if corner[d] else -1) if mode[d] else 1 for d in range(3)])
            for comp in range(3):
                sums[3 * m + comp, 3 * n + comp] = sign
    form = sums @ element_matrix() @ sums.T / 64.0

    def at(first, second):
        return form[3 * modes.index(first[1]) + first[0], 3 * modes.index(second[1]) + second[0]]

    ux, vy, uy = (0, (1, 0, 0)), (1, (0, 1, 0)), (0, (0, 1, 0))
    uxy, wyz = (0, (1, 1, 0)), (2, (0, 1, 1))
    wxy, vxz, uxyz = (2, (1, 1, 0)), (1, (1, 0, 1)), (0, (1, 1, 1))
    return dict(
        normal=at(ux, ux) - at(ux, vy),
        trace=at(ux, vy),
        shear=at(uy, uy),
        plus=(at(uxy, uxy) + at(uxy, wyz)) / 2,
        minus=(at(uxy, uxy) - at(uxy, wyz)) / 2,
        twist=at(wxy, wxy) - at(wxy, vxz),
        twist_sum=at(wxy, vxz),
        corner=at(uxyz, uxyz),
    )


def square(value):
    return value * value


def quadratic(low, high, weights):
    x = [low[c][1] + high[c][1] for c in range(3)]
    y = [low[c][2] + high[c][2] for c in range(3)]
    z = [high[c][0] - low[c][0] for c in range(3)]
    xy = [low[c][3] + high[c][3] for c in range(3)]
    xz = [high[c][1] - low[c][1] for c in range(3)]
    yz = [high[c][2] - low[c][2] for c in range(3)]
    xyz = [high[c][3] - low[c][3] for c in range(3)]
    normal = square(x[0]) + square(y[1]) + square(z[2])
    trace = square(x[0] + y[1] + z[2])
    shear = square(y[0] + x[1]) + square(z[0] + x[2]) + square(z[1] + y[2])
    pairs = ((xy[0], yz[2]), (xy[1], xz[2]), (xz[0], yz[1]))
    plus = sum(square(p + q) for p, q in pairs)
    minus = sum(square(p - q) for p, q in pairs)
    twist = square(xy[2]) + square(xz[1]) + square(yz[0])
    twist_sum = square(xy[2] + xz[1] + yz[0])
    corner = square(xyz[0]) + square(xyz[1]) + square(xyz[2])
    groups = dict(
        normal=normal, trace=trace, shear=shear, plus=plus, minus=minus, twist=twist, twist_sum=twist_sum, corner=corner
    )
    return sum(np.float32(weights[name]) * group for name, group in groups.items())


def line_weight(coord, count):
    def outside(distance):
        missing = jnp.maximum(REACH - distance, 0)
        return missing * (missing + 1) // 2

    whole = (REACH + 1) * (REACH + 1)
    return (whole - outside(coord) - outside(count - 1 - coord)).astype(jnp.float32)


def voxel_factor(density, solid, plane, first_row, total_z, total_y):
    rows, length = density.shape
    row = lax.broadcasted_iota(jnp.int32, (rows, length), 0) + first_row
    column = lax.broadcasted_iota(jnp.int32, (rows, length), 1)
    weight = line_weight(row, total_y) * line_weight(column, length)
    weight = weight * line_weight(jnp.full((rows, length), plane, jnp.int32), total_z)
    return solid.astype(jnp.float32) * (-3.0 * density * density) / weight


def spread_x(value):
    rows, length = value.shape
    wide = jnp.concatenate([value, jnp.zeros((rows, LANES), jnp.float32)], axis=1)
    span = length + LANES
    wide = wide + pltpu.roll(wide, span - 1, 1)
    wide = wide + pltpu.roll(wide, span - 2, 1)
    wide = wide + pltpu.roll(wide, 1, 1)
    wide = wide + pltpu.roll(wide, 2, 1)
    return wide[:, :length]


def spread_layers(layers):
    for step in (1, 2, 1, 2):
        layers = [layers[k] + layers[k + step] for k in range(len(layers) - step)]
    return layers


def lead_kernel(totals, disp, fixed, density, solid, z_out, y_out, d_out):
    loads, comps, zlen, ylen, _ = disp.shape
    total_z, total_y = totals
    base_z = lax.axis_index("sz") * zlen
    base_y = lax.axis_index("sy") * ylen
    free = [1.0 - fixed[z].astype(jnp.float32) for z in range(zlen)]
    for case in range(loads):
        for comp in range(comps):
            k = case * comps + comp
            layer = disp[case, comp, 0] * free[0]
            z_out[k] = layer
            d_out[ROWS * k : ROWS * (k + 1)] = layer[:ROWS]
            y_out[k, :ROWS] = layer[:ROWS]
            for z in range(1, zlen):
                y_out[k, ROWS * z : ROWS * (z + 1)] = disp[case, comp, z, :ROWS] * free[z][:ROWS]
    for z in range(zlen):
        factor = voxel_factor(density[z, :TILE], solid[z, :TILE], base_z + z, base_y, total_z, total_y)
        y_out[loads * comps, ROWS * z : ROWS * (z + 1)] = factor[:ROWS]


def energy_kernel(totals, disp, fixed, density, solid, z_in, y_in, d_in, own_out, up_out, plus, diff, factor, quotient):
    loads, comps, zlen, ylen, xlen = disp.shape
    total_z, total_y = totals
    base_z = lax.axis_index("sz") * zlen
    base_y = lax.axis_index("sy") * ylen
    weights = mode_weights()

    def split_x(value):
        column = lax.broadcasted_iota(jnp.int32, value.shape, 1)
        ahead = jnp.where(column == xlen - 1, 0.0, pltpu.roll(value, xlen - 1, 1))
        return value + ahead, ahead - value

    @pl.loop(0, loads * comps)
    def _(k):
        case, comp = k // comps, k % comps
        for z in range(zlen):
            whole, change = split_x(disp[case, comp, z] * (1.0 - fixed[z].astype(jnp.float32)))
            plus[k, z, :ylen] = whole
            diff[k, z, :ylen] = change
        whole, change = split_x(z_in[k])
        plus[k, zlen, :ylen] = whole
        diff[k, zlen, :ylen] = change
        whole, change = split_x(y_in[k])
        for z in range(zlen):
            plus[k, z, ylen : ylen + ROWS] = whole[ROWS * z : ROWS * (z + 1)]
            diff[k, z, ylen : ylen + ROWS] = change[ROWS * z : ROWS * (z + 1)]

    whole, change = split_x(d_in[...])
    for k in range(loads * comps):
        plus[k, zlen, ylen : ylen + ROWS] = whole[ROWS * k : ROWS * (k + 1)]
        diff[k, zlen, ylen : ylen + ROWS] = change[ROWS * k : ROWS * (k + 1)]

    for z in range(zlen):
        factor[z, :ylen] = voxel_factor(density[z], solid[z], base_z + z, base_y, total_z, total_y)
        factor[z, ylen : ylen + ROWS] = y_in[loads * comps, ROWS * z : ROWS * (z + 1)]

    for first in range(0, ylen + REACH, TILE):

        @pl.loop(0, xlen // LANES)
        def _(chunk):
            lanes = pl.ds(pl.multiple_of(chunk * LANES, LANES), LANES)

            def faces(k, z):
                whole, whole_next = plus[k, z, first : first + TILE, lanes], plus[k, z, first + 1 : first + TILE + 1, lanes]
                change, change_next = diff[k, z, first : first + TILE, lanes], diff[k, z, first + 1 : first + TILE + 1, lanes]
                return whole + whole_next, change + change_next, whole_next - whole, change_next - change

            energy = [None] * zlen
            for case in range(loads):
                low = None
                for z in range(zlen + 1):
                    high = [faces(case * comps + comp, z) for comp in range(comps)]
                    if low is not None:
                        part = quadratic(low, high, weights)
                        energy[z - 1] = part if energy[z - 1] is None else energy[z - 1] + part
                    low = high
            for z in range(zlen):
                quotient[z, first + TILE : first + 2 * TILE, lanes] = energy[z] * factor[z, first : first + TILE, lanes]

    for z in range(zlen):
        quotient[z, :TILE] = jnp.zeros((TILE, xlen), jnp.float32)
        rows = [quotient[z, TILE + step : TILE + step + ylen] for step in range(-REACH, REACH + 1)]
        own_out[z] = sum((ROWS - abs(k - REACH)) * rows[k] for k in range(2 * REACH + 1))
        top = quotient[z, ylen : ylen + TILE]
        last = [top[TILE - 1 - k : TILE - k] for k in range(REACH)]
        up = [
            sum(float(REACH - row - k) * last[k] for k in range(REACH - row)) for row in range(REACH)
        ]
        up_out[ROWS * z : ROWS * (z + 1)] = jnp.concatenate(up + [jnp.zeros((1, xlen), jnp.float32)], axis=0)


def rows_kernel(own, up_in, h_out, down_out, up_out):
    zlen = own.shape[0]
    for z in range(zlen):
        h_out[z] = own[z]
        h_out[z, :ROWS] = own[z, :ROWS] + up_in[ROWS * z : ROWS * (z + 1)]
    down_out[...] = h_out[:REACH]
    up_out[...] = h_out[zlen - REACH :]


def layers_kernel(h, below, above, out):
    zlen = h.shape[0]
    layers = [below[k] for k in range(REACH)] + [h[z] for z in range(zlen)] + [above[k] for k in range(REACH)]
    for z, layer in enumerate(spread_layers(layers)):
        out[z] = spread_x(layer)


def sum_kernel(parts, out):
    out[...] = parts[0] + parts[1]


def vmem(count):
    return [pl.BlockSpec(memory_space=pltpu.VMEM)] * count


def call(kernel, outs, args, scratch=(), **kwargs):
    shapes = [jax.ShapeDtypeStruct(shape, jnp.float32) for shape in outs]
    result = pl.pallas_call(
        kernel,
        out_shape=shapes,
        in_specs=vmem(len(args)),
        out_specs=vmem(len(outs)),
        scratch_shapes=list(scratch),
        compiler_params=pltpu.CompilerParams(vmem_limit_bytes=32 * 1024 * 1024),
        **kwargs,
    )(*args)
    return result


def moved(value, axes, steps):
    sizes = [lax.axis_size(axis) for axis in axes]
    pairs = []
    for flat in range(int(np.prod(sizes))):
        place = np.unravel_index(flat, sizes)
        source = [int(p) + s for p, s in zip(place, steps)]
        if all(0 <= s < size for s, size in zip(source, sizes)):
            pairs.append((int(np.ravel_multi_index(source, sizes)), flat))
    return lax.ppermute(value, axes if len(axes) > 1 else axes[0], pairs)


def body(displacements, density, solid, fixed):
    loads, comps, zlen, ylen, xlen = displacements.shape
    planes = loads * comps
    totals = (zlen * lax.axis_size("sz"), ylen * lax.axis_size("sy"))

    def bound(kernel):
        def run(*refs):
            kernel(totals, *refs)

        return run

    z_send, y_send, d_send = call(
        bound(lead_kernel),
        [(planes, ylen, xlen), (planes + 1, ROWS * zlen, xlen), (ROWS * planes, xlen)],
        (displacements, fixed, density, solid),
    )
    z_in = moved(z_send, ("sz",), (1,))
    y_in = moved(y_send, ("sy",), (1,))
    d_in = moved(d_send, ("sy", "sz"), (1, 1))
    high = ylen + 2 * TILE
    own, up_send = call(
        bound(energy_kernel),
        [(zlen, ylen, xlen), (ROWS * zlen, xlen)],
        (displacements, fixed, density, solid, z_in, y_in, d_in),
        scratch=[
            pltpu.VMEM((planes, zlen + 1, high, xlen), jnp.float32),
            pltpu.VMEM((planes, zlen + 1, high, xlen), jnp.float32),
            pltpu.VMEM((zlen, ylen + TILE, xlen), jnp.float32),
            pltpu.VMEM((zlen, ylen + 2 * TILE, xlen), jnp.float32),
        ],
    )
    up_in = moved(up_send, ("sy",), (-1,))
    h, down_send, over_send = call(
        rows_kernel, [(zlen, ylen, xlen), (REACH, ylen, xlen), (REACH, ylen, xlen)], (own, up_in)
    )
    above = moved(down_send, ("sz",), (1,))
    below = moved(over_send, ("sz",), (-1,))
    (part,) = call(layers_kernel, [(zlen, ylen, xlen)], (h, below, above))
    parts = lax.all_gather(part, "load", axis=0)
    (out,) = call(sum_kernel, [(zlen, ylen, xlen)], (parts,))
    return out


def solution(mesh):
    return jax.shard_map(
        body,
        mesh=mesh,
        in_specs=(
            P("load", None, "sz", "sy", None),
            P("sz", "sy", None),
            P("sz", "sy", None),
            P("sz", "sy", None),
        ),
        out_specs=P("sz", "sy", None),
        check_vma=False,
    )
```

```python
import jax
import jax.numpy as jnp
import numpy as np
from jax import lax
from jax.experimental import pallas as pl
from jax.experimental.pallas import tpu as pltpu
from jax.sharding import PartitionSpec as P

OFFSETS = [(0, 0, 0), (1, 0, 0), (1, 1, 0), (0, 1, 0), (0, 0, 1), (1, 0, 1), (1, 1, 1), (0, 1, 1)]
REACH = 3
ROWS = REACH + 1
TILE = 8
LANES = 128


def element_matrix():
    corners = np.array(
        [
            [-1.0, -1.0, -1.0],
            [1.0, -1.0, -1.0],
            [1.0, 1.0, -1.0],
            [-1.0, 1.0, -1.0],
            [-1.0, -1.0, 1.0],
            [1.0, -1.0, 1.0],
            [1.0, 1.0, 1.0],
            [-1.0, 1.0, 1.0],
        ]
    )
    poisson = 0.3
    lame = poisson / ((1.0 + poisson) * (1.0 - 2.0 * poisson))
    shear = 1.0 / (2.0 * (1.0 + poisson))
    elastic = np.zeros((6, 6))
    elastic[:3, :3] = lame
    for k in range(3):
        elastic[k, k] += 2.0 * shear
        elastic[3 + k, 3 + k] = shear
    gauss = 1.0 / np.sqrt(3.0)
    stiffness = np.zeros((24, 24))
    for gi in range(2):
        for gj in range(2):
            for gk in range(2):
                point = np.array([(2 * gi - 1) * gauss, (2 * gj - 1) * gauss, (2 * gk - 1) * gauss])
                strain = np.zeros((6, 24))
                for node in range(8):
                    grads = np.zeros(3)
                    for k in range(3):
                        value = corners[node, k] / 8.0
                        for m in range(3):
                            if m != k:
                                value = value * (1.0 + point[m] * corners[node, m])
                        grads[k] = 2.0 * value
                    col = 3 * node
                    strain[0, col] = grads[0]
                    strain[1, col + 1] = grads[1]
                    strain[2, col + 2] = grads[2]
                    strain[3, col] = grads[1]
                    strain[3, col + 1] = grads[0]
                    strain[4, col + 1] = grads[2]
                    strain[4, col + 2] = grads[1]
                    strain[5, col] = grads[2]
                    strain[5, col + 2] = grads[0]
                stiffness += strain.T @ elastic @ strain / 8.0
    return stiffness


def mode_weights():
    modes = [(i, j, k) for k in (0, 1) for j in (0, 1) for i in (0, 1)]
    sums = np.zeros((24, 24))
    for m, mode in enumerate(modes):
        for n, corner in enumerate(OFFSETS):
            sign = np.prod([(1 if corner[d] else -1) if mode[d] else 1 for d in range(3)])
            for comp in range(3):
                sums[3 * m + comp, 3 * n + comp] = sign
    form = sums @ element_matrix() @ sums.T / 64.0

    def at(first, second):
        return form[3 * modes.index(first[1]) + first[0], 3 * modes.index(second[1]) + second[0]]

    ux, vy, uy = (0, (1, 0, 0)), (1, (0, 1, 0)), (0, (0, 1, 0))
    uxy, wyz = (0, (1, 1, 0)), (2, (0, 1, 1))
    wxy, vxz, uxyz = (2, (1, 1, 0)), (1, (1, 0, 1)), (0, (1, 1, 1))
    return dict(
        normal=at(ux, ux) - at(ux, vy),
        trace=at(ux, vy),
        shear=at(uy, uy),
        plus=(at(uxy, uxy) + at(uxy, wyz)) / 2,
        minus=(at(uxy, uxy) - at(uxy, wyz)) / 2,
        twist=at(wxy, wxy) - at(wxy, vxz),
        twist_sum=at(wxy, vxz),
        corner=at(uxyz, uxyz),
    )


def square(value):
    return value * value


def quadratic(low, high, weights):
    x = [low[c][1] + high[c][1] for c in range(3)]
    y = [low[c][2] + high[c][2] for c in range(3)]
    z = [high[c][0] - low[c][0] for c in range(3)]
    xy = [low[c][3] + high[c][3] for c in range(3)]
    xz = [high[c][1] - low[c][1] for c in range(3)]
    yz = [high[c][2] - low[c][2] for c in range(3)]
    xyz = [high[c][3] - low[c][3] for c in range(3)]
    normal = square(x[0]) + square(y[1]) + square(z[2])
    trace = square(x[0] + y[1] + z[2])
    shear = square(y[0] + x[1]) + square(z[0] + x[2]) + square(z[1] + y[2])
    pairs = ((xy[0], yz[2]), (xy[1], xz[2]), (xz[0], yz[1]))
    plus = sum(square(p + q) for p, q in pairs)
    minus = sum(square(p - q) for p, q in pairs)
    twist = square(xy[2]) + square(xz[1]) + square(yz[0])
    twist_sum = square(xy[2] + xz[1] + yz[0])
    corner = square(xyz[0]) + square(xyz[1]) + square(xyz[2])
    groups = dict(
        normal=normal, trace=trace, shear=shear, plus=plus, minus=minus, twist=twist, twist_sum=twist_sum, corner=corner
    )
    return sum(np.float32(weights[name]) * group for name, group in groups.items())


def line_weight(coord, count):
    def outside(distance):
        missing = jnp.maximum(REACH - distance, 0)
        return missing * (missing + 1) // 2

    whole = (REACH + 1) * (REACH + 1)
    return (whole - outside(coord) - outside(count - 1 - coord)).astype(jnp.float32)


def voxel_factor(density, solid, plane, first_row, total_z, total_y):
    rows, length = density.shape
    row = lax.broadcasted_iota(jnp.int32, (rows, length), 0) + first_row
    column = lax.broadcasted_iota(jnp.int32, (rows, length), 1)
    weight = line_weight(row, total_y) * line_weight(column, length)
    weight = weight * line_weight(jnp.full((rows, length), plane, jnp.int32), total_z)
    return solid.astype(jnp.float32) * (-3.0 * density * density) / weight


def spread_x(value):
    rows, length = value.shape
    wide = jnp.concatenate([value, jnp.zeros((rows, LANES), jnp.float32)], axis=1)
    span = length + LANES
    wide = wide + pltpu.roll(wide, span - 1, 1)
    wide = wide + pltpu.roll(wide, span - 2, 1)
    wide = wide + pltpu.roll(wide, 1, 1)
    wide = wide + pltpu.roll(wide, 2, 1)
    return wide[:, :length]


def spread_layers(layers):
    for step in (1, 2, 1, 2):
        layers = [layers[k] + layers[k + step] for k in range(len(layers) - step)]
    return layers


def lead_kernel(disp_hbm, fixed_hbm, density_hbm, solid_hbm, disp, fixed, density, solid, z_out, y_out, d_out, sems):
    loads, comps, zlen, _, _ = disp.shape
    copies = [
        pltpu.make_async_copy(source, target, sems.at[k])
        for k, (source, target) in enumerate(
            ((disp_hbm, disp), (fixed_hbm, fixed), (density_hbm, density), (solid_hbm, solid))
        )
    ]
    for copy in copies:
        copy.start()
    for copy in copies:
        copy.wait()
    free = [1.0 - fixed[z].astype(jnp.float32) for z in range(zlen)]
    d_out[...] = jnp.zeros(d_out.shape, jnp.float32)
    for case in range(loads):
        for comp in range(comps):
            k = case * comps + comp
            layer = disp[case, comp, 0] * free[0]
            z_out[k] = layer
            d_out[k : k + 1] = layer[:1]
            y_out[zlen * k : zlen * k + 1] = layer[:1]
            for z in range(1, zlen):
                y_out[zlen * k + z : zlen * k + z + 1] = disp[case, comp, z, :1] * free[z][:1]


def energy_kernel(totals, disp, fixed, density, solid, z_in, y_in, d_in, own_out, a_out, b_out, plus, diff, quotient):
    loads, comps, zlen, ylen, xlen = disp.shape
    total_z, total_y = totals
    index_y = lax.axis_index("sy")
    base_z = lax.axis_index("sz") * zlen
    base_y = index_y * ylen
    weights = mode_weights()

    def split_x(value):
        column = lax.broadcasted_iota(jnp.int32, value.shape, 1)
        ahead = jnp.where(column == xlen - 1, 0.0, pltpu.roll(value, xlen - 1, 1))
        return value + ahead, ahead - value

    @pl.loop(0, loads * comps)
    def _(k):
        case, comp = k // comps, k % comps
        for z in range(zlen):
            whole, change = split_x(disp[case, comp, z] * (1.0 - fixed[z].astype(jnp.float32)))
            plus[k, z, :ylen] = whole
            diff[k, z, :ylen] = change
        whole, change = split_x(z_in[k])
        plus[k, zlen, :ylen] = whole
        diff[k, zlen, :ylen] = change

    whole, change = split_x(y_in[...])
    for k in range(loads * comps):
        for z in range(zlen):
            plus[k, z, ylen : ylen + 1] = whole[zlen * k + z : zlen * k + z + 1]
            diff[k, z, ylen : ylen + 1] = change[zlen * k + z : zlen * k + z + 1]
    whole, change = split_x(d_in[...])
    for k in range(loads * comps):
        plus[k, zlen, ylen : ylen + 1] = whole[k : k + 1]
        diff[k, zlen, ylen : ylen + 1] = change[k : k + 1]

    zeros = jnp.zeros((TILE, xlen), jnp.float32)
    for z in range(zlen):
        quotient[z, :TILE] = zeros
        quotient[z, TILE : TILE + ylen] = voxel_factor(density[z], solid[z], base_z + z, base_y, total_z, total_y)
        quotient[z, TILE + ylen :] = zeros

    for first in range(0, ylen, TILE):

        @pl.loop(0, xlen // LANES)
        def _(chunk):
            lanes = pl.ds(pl.multiple_of(chunk * LANES, LANES), LANES)

            def faces(k, z):
                whole, whole_next = plus[k, z, first : first + TILE, lanes], plus[k, z, first + 1 : first + TILE + 1, lanes]
                change, change_next = diff[k, z, first : first + TILE, lanes], diff[k, z, first + 1 : first + TILE + 1, lanes]
                return whole + whole_next, change + change_next, whole_next - whole, change_next - change

            energy = [None] * zlen
            for case in range(loads):
                low = None
                for z in range(zlen + 1):
                    high = [faces(case * comps + comp, z) for comp in range(comps)]
                    if low is not None:
                        part = quadratic(low, high, weights)
                        energy[z - 1] = part if energy[z - 1] is None else energy[z - 1] + part
                    low = high
            for z in range(zlen):
                here = quotient[z, first + TILE : first + 2 * TILE, lanes]
                quotient[z, first + TILE : first + 2 * TILE, lanes] = energy[z] * here

    even = index_y % 2 == 0
    for z in range(zlen):
        rows = [quotient[z, TILE + step : TILE + step + ylen] for step in range(-REACH, REACH + 1)]
        own_out[z] = sum((ROWS - abs(k - REACH)) * rows[k] for k in range(2 * REACH + 1))
        top = quotient[z, ylen : ylen + TILE]
        base = quotient[z, TILE : 2 * TILE]
        ahead, back = [], []
        for row in range(REACH):
            ahead.append(sum(float(REACH - row - k) * top[TILE - 1 - k : TILE - k] for k in range(REACH - row)))
            back.append(sum(float(row + 1 - k) * base[k : k + 1] for k in range(row + 1)))
        blank = jnp.zeros((1, xlen), jnp.float32)
        ahead = jnp.concatenate(ahead + [blank], axis=0)
        back = jnp.concatenate([blank] + back, axis=0)
        a_out[ROWS * z : ROWS * (z + 1)] = jnp.where(even, ahead, back)
        b_out[ROWS * z : ROWS * (z + 1)] = jnp.where(even, back, ahead)


def rows_kernel(own, a_in, b_in, h_out, a_out, b_out):
    zlen, ylen, _ = own.shape
    even = lax.axis_index("sy") % 2 == 0
    for z in range(zlen):
        part = slice(ROWS * z, ROWS * (z + 1))
        from_low = jnp.where(even, b_in[part], a_in[part])
        from_high = jnp.where(even, a_in[part], b_in[part])
        h_out[z] = own[z]
        h_out[z, :ROWS] = own[z, :ROWS] + from_low
        h_out[z, ylen - ROWS :] = own[z, ylen - ROWS :] + from_high
    top = (zlen - REACH) * (lax.axis_index("sz") % 2 == 0).astype(jnp.int32)
    a_out[...] = h_out[pl.ds(top, REACH)]
    b_out[...] = h_out[pl.ds(zlen - REACH - top, REACH)]


def layers_kernel(h, a_in, b_in, out):
    zlen = h.shape[0]
    even = lax.axis_index("sz") % 2 == 0
    below = [jnp.where(even, b_in[k], a_in[k]) for k in range(REACH)]
    above = [jnp.where(even, a_in[k], b_in[k]) for k in range(REACH)]
    layers = below + [h[z] for z in range(zlen)] + above
    for z, layer in enumerate(spread_layers(layers)):
        out[z] = spread_x(layer)


def sum_kernel(parts, out):
    out[...] = parts[0] + parts[1]


def call(kernel, outs, args, scratch=(), space=pltpu.VMEM):
    shapes = [jax.ShapeDtypeStruct(out, jnp.float32) if isinstance(out, tuple) else out for out in outs]
    return pl.pallas_call(
        kernel,
        out_shape=shapes,
        in_specs=[pl.BlockSpec(memory_space=space)] * len(args),
        out_specs=[pl.BlockSpec(memory_space=pltpu.VMEM)] * len(outs),
        scratch_shapes=list(scratch),
        compiler_params=pltpu.CompilerParams(vmem_limit_bytes=32 * 1024 * 1024),
    )(*args)


def moved(value, axes, steps):
    sizes = [lax.axis_size(axis) for axis in axes]
    pairs = []
    for flat in range(int(np.prod(sizes))):
        place = np.unravel_index(flat, sizes)
        source = [int(p) + s for p, s in zip(place, steps)]
        if all(0 <= s < size for s, size in zip(source, sizes)):
            pairs.append((int(np.ravel_multi_index(source, sizes)), flat))
    return lax.ppermute(value, axes if len(axes) > 1 else axes[0], pairs)


def swapped(value, axis, first):
    pairs = []
    for low in range(first, lax.axis_size(axis) - 1, 2):
        pairs += [(low, low + 1), (low + 1, low)]
    return lax.ppermute(value, axis, pairs)


def body(displacements, density, solid, fixed):
    loads, comps, zlen, ylen, xlen = displacements.shape
    planes = loads * comps
    totals = (zlen * lax.axis_size("sz"), ylen * lax.axis_size("sy"))
    args = [
        pltpu.with_memory_space_constraint(arg, pltpu.HBM) for arg in (displacements, fixed, density, solid)
    ]

    disp, fixed, density, solid, z_send, y_send, d_send = call(
        lead_kernel,
        [jax.ShapeDtypeStruct(arg.shape, arg.dtype) for arg in args]
        + [(planes, ylen, xlen), (planes * zlen, xlen), (TILE, xlen)],
        args,
        scratch=[pltpu.SemaphoreType.DMA((len(args),))],
        space=pltpu.HBM,
    )
    z_in = moved(z_send, ("sz",), (1,))
    y_in = moved(y_send, ("sy",), (1,))
    d_in = moved(d_send, ("sy", "sz"), (1, 1))
    own, a_send, b_send = call(
        lambda *refs: energy_kernel(totals, *refs),
        [(zlen, ylen, xlen), (ROWS * zlen, xlen), (ROWS * zlen, xlen)],
        (disp, fixed, density, solid, z_in, y_in, d_in),
        scratch=[
            pltpu.VMEM((planes, zlen + 1, ylen + TILE, xlen), jnp.float32),
            pltpu.VMEM((planes, zlen + 1, ylen + TILE, xlen), jnp.float32),
            pltpu.VMEM((zlen, ylen + 2 * TILE, xlen), jnp.float32),
        ],
    )
    a_in = swapped(a_send, "sy", 0)
    b_in = swapped(b_send, "sy", 1)
    h, a_send, b_send = call(
        rows_kernel, [(zlen, ylen, xlen), (REACH, ylen, xlen), (REACH, ylen, xlen)], (own, a_in, b_in)
    )
    a_in = swapped(a_send, "sz", 0)
    b_in = swapped(b_send, "sz", 1)
    (part,) = call(layers_kernel, [(zlen, ylen, xlen)], (h, a_in, b_in))
    parts = lax.all_gather(part, "load", axis=0)
    (out,) = call(sum_kernel, [(zlen, ylen, xlen)], (parts,))
    return out


def solution(mesh):
    return jax.shard_map(
        body,
        mesh=mesh,
        in_specs=(
            P("load", None, "sz", "sy", None),
            P("sz", "sy", None),
            P("sz", "sy", None),
            P("sz", "sy", None),
        ),
        out_specs=P("sz", "sy", None),
        check_vma=False,
    )
```

```python
import jax
import jax.numpy as jnp
import numpy as np
from jax import lax
from jax.experimental import pallas as pl
from jax.experimental.pallas import tpu as pltpu
from jax.sharding import PartitionSpec as P

OFFSETS = [(0, 0, 0), (1, 0, 0), (1, 1, 0), (0, 1, 0), (0, 0, 1), (1, 0, 1), (1, 1, 1), (0, 1, 1)]
REACH = 3
ROWS = REACH + 1
TILE = 8
LANES = 128


def element_matrix():
    corners = np.array(
        [
            [-1.0, -1.0, -1.0],
            [1.0, -1.0, -1.0],
            [1.0, 1.0, -1.0],
            [-1.0, 1.0, -1.0],
            [-1.0, -1.0, 1.0],
            [1.0, -1.0, 1.0],
            [1.0, 1.0, 1.0],
            [-1.0, 1.0, 1.0],
        ]
    )
    poisson = 0.3
    lame = poisson / ((1.0 + poisson) * (1.0 - 2.0 * poisson))
    shear = 1.0 / (2.0 * (1.0 + poisson))
    elastic = np.zeros((6, 6))
    elastic[:3, :3] = lame
    for k in range(3):
        elastic[k, k] += 2.0 * shear
        elastic[3 + k, 3 + k] = shear
    gauss = 1.0 / np.sqrt(3.0)
    stiffness = np.zeros((24, 24))
    for gi in range(2):
        for gj in range(2):
            for gk in range(2):
                point = np.array([(2 * gi - 1) * gauss, (2 * gj - 1) * gauss, (2 * gk - 1) * gauss])
                strain = np.zeros((6, 24))
                for node in range(8):
                    grads = np.zeros(3)
                    for k in range(3):
                        value = corners[node, k] / 8.0
                        for m in range(3):
                            if m != k:
                                value = value * (1.0 + point[m] * corners[node, m])
                        grads[k] = 2.0 * value
                    col = 3 * node
                    strain[0, col] = grads[0]
                    strain[1, col + 1] = grads[1]
                    strain[2, col + 2] = grads[2]
                    strain[3, col] = grads[1]
                    strain[3, col + 1] = grads[0]
                    strain[4, col + 1] = grads[2]
                    strain[4, col + 2] = grads[1]
                    strain[5, col] = grads[2]
                    strain[5, col + 2] = grads[0]
                stiffness += strain.T @ elastic @ strain / 8.0
    return stiffness


def mode_weights():
    modes = [(i, j, k) for k in (0, 1) for j in (0, 1) for i in (0, 1)]
    sums = np.zeros((24, 24))
    for m, mode in enumerate(modes):
        for n, corner in enumerate(OFFSETS):
            sign = np.prod([(1 if corner[d] else -1) if mode[d] else 1 for d in range(3)])
            for comp in range(3):
                sums[3 * m + comp, 3 * n + comp] = sign
    form = sums @ element_matrix() @ sums.T / 64.0

    def at(first, second):
        return form[3 * modes.index(first[1]) + first[0], 3 * modes.index(second[1]) + second[0]]

    ux, vy, uy = (0, (1, 0, 0)), (1, (0, 1, 0)), (0, (0, 1, 0))
    uxy, wyz = (0, (1, 1, 0)), (2, (0, 1, 1))
    wxy, vxz, uxyz = (2, (1, 1, 0)), (1, (1, 0, 1)), (0, (1, 1, 1))
    return dict(
        normal=at(ux, ux) - at(ux, vy),
        trace=at(ux, vy),
        shear=at(uy, uy),
        plus=(at(uxy, uxy) + at(uxy, wyz)) / 2,
        minus=(at(uxy, uxy) - at(uxy, wyz)) / 2,
        twist=at(wxy, wxy) - at(wxy, vxz),
        twist_sum=at(wxy, vxz),
        corner=at(uxyz, uxyz),
    )


def square(value):
    return value * value


def quadratic(low, high, weights):
    x = [low[c][1] + high[c][1] for c in range(3)]
    y = [low[c][2] + high[c][2] for c in range(3)]
    z = [high[c][0] - low[c][0] for c in range(3)]
    xy = [low[c][3] + high[c][3] for c in range(3)]
    xz = [high[c][1] - low[c][1] for c in range(3)]
    yz = [high[c][2] - low[c][2] for c in range(3)]
    xyz = [high[c][3] - low[c][3] for c in range(3)]
    normal = square(x[0]) + square(y[1]) + square(z[2])
    trace = square(x[0] + y[1] + z[2])
    shear = square(y[0] + x[1]) + square(z[0] + x[2]) + square(z[1] + y[2])
    pairs = ((xy[0], yz[2]), (xy[1], xz[2]), (xz[0], yz[1]))
    plus = sum(square(p + q) for p, q in pairs)
    minus = sum(square(p - q) for p, q in pairs)
    twist = square(xy[2]) + square(xz[1]) + square(yz[0])
    twist_sum = square(xy[2] + xz[1] + yz[0])
    corner = square(xyz[0]) + square(xyz[1]) + square(xyz[2])
    groups = dict(
        normal=normal, trace=trace, shear=shear, plus=plus, minus=minus, twist=twist, twist_sum=twist_sum, corner=corner
    )
    return sum(np.float32(weights[name]) * group for name, group in groups.items())


def line_weight(coord, count):
    def outside(distance):
        missing = jnp.maximum(REACH - distance, 0)
        return missing * (missing + 1) // 2

    whole = (REACH + 1) * (REACH + 1)
    return (whole - outside(coord) - outside(count - 1 - coord)).astype(jnp.float32)


def voxel_factor(density, solid, plane, first_row, total_z, total_y):
    rows, length = density.shape
    row = lax.broadcasted_iota(jnp.int32, (rows, length), 0) + first_row
    column = lax.broadcasted_iota(jnp.int32, (rows, length), 1)
    weight = line_weight(row, total_y) * line_weight(column, length)
    weight = weight * line_weight(jnp.full((rows, length), plane, jnp.int32), total_z)
    return solid.astype(jnp.float32) * (-3.0 * density * density) / weight


def spread_x(value):
    rows, length = value.shape
    wide = jnp.concatenate([value, jnp.zeros((rows, LANES), jnp.float32)], axis=1)
    span = length + LANES
    wide = wide + pltpu.roll(wide, span - 1, 1)
    wide = wide + pltpu.roll(wide, span - 2, 1)
    wide = wide + pltpu.roll(wide, 1, 1)
    wide = wide + pltpu.roll(wide, 2, 1)
    return wide[:, :length]


def spread_layers(layers):
    for step in (1, 2, 1, 2):
        layers = [layers[k] + layers[k + step] for k in range(len(layers) - step)]
    return layers


def lead_kernel(disp_hbm, fixed_hbm, density_hbm, solid_hbm, disp, fixed, density, solid, z_out, y_out, d_out, sems):
    loads, comps, zlen, _, _ = disp.shape
    copies = [
        pltpu.make_async_copy(source, target, sems.at[k])
        for k, (source, target) in enumerate(
            ((disp_hbm, disp), (fixed_hbm, fixed), (density_hbm, density), (solid_hbm, solid))
        )
    ]
    for copy in copies:
        copy.start()
    for copy in copies:
        copy.wait()
    free = [1.0 - fixed[z].astype(jnp.float32) for z in range(zlen)]
    d_out[...] = jnp.zeros(d_out.shape, jnp.float32)
    for case in range(loads):
        for comp in range(comps):
            k = case * comps + comp
            layer = disp[case, comp, 0] * free[0]
            z_out[k] = layer
            d_out[k : k + 1] = layer[:1]
            y_out[zlen * k : zlen * k + 1] = layer[:1]
            for z in range(1, zlen):
                y_out[zlen * k + z : zlen * k + z + 1] = disp[case, comp, z, :1] * free[z][:1]


def energy_kernel(totals, disp, fixed, density, solid, z_in, y_in, d_in, own_out, ends_out, plus, diff, quotient):
    loads, comps, zlen, ylen, xlen = disp.shape
    total_z, total_y = totals
    index_y = lax.axis_index("sy")
    base_z = lax.axis_index("sz") * zlen
    base_y = index_y * ylen
    weights = mode_weights()

    def split_x(value):
        column = lax.broadcasted_iota(jnp.int32, value.shape, 1)
        ahead = jnp.where(column == xlen - 1, 0.0, pltpu.roll(value, xlen - 1, 1))
        return value + ahead, ahead - value

    @pl.loop(0, loads * comps)
    def _(k):
        case, comp = k // comps, k % comps
        for z in range(zlen):
            whole, change = split_x(disp[case, comp, z] * (1.0 - fixed[z].astype(jnp.float32)))
            plus[k, z, :ylen] = whole
            diff[k, z, :ylen] = change
        whole, change = split_x(z_in[k])
        plus[k, zlen, :ylen] = whole
        diff[k, zlen, :ylen] = change

    whole, change = split_x(y_in[...])
    for k in range(loads * comps):
        for z in range(zlen):
            plus[k, z, ylen : ylen + 1] = whole[zlen * k + z : zlen * k + z + 1]
            diff[k, z, ylen : ylen + 1] = change[zlen * k + z : zlen * k + z + 1]
    whole, change = split_x(d_in[...])
    for k in range(loads * comps):
        plus[k, zlen, ylen : ylen + 1] = whole[k : k + 1]
        diff[k, zlen, ylen : ylen + 1] = change[k : k + 1]

    zeros = jnp.zeros((TILE, xlen), jnp.float32)
    for z in range(zlen):
        quotient[z, :TILE] = zeros
        quotient[z, TILE : TILE + ylen] = voxel_factor(density[z], solid[z], base_z + z, base_y, total_z, total_y)
        quotient[z, TILE + ylen :] = zeros

    for first in range(0, ylen, TILE):

        @pl.loop(0, xlen // LANES)
        def _(chunk):
            lanes = pl.ds(pl.multiple_of(chunk * LANES, LANES), LANES)

            def faces(k, z):
                whole, whole_next = plus[k, z, first : first + TILE, lanes], plus[k, z, first + 1 : first + TILE + 1, lanes]
                change, change_next = diff[k, z, first : first + TILE, lanes], diff[k, z, first + 1 : first + TILE + 1, lanes]
                return whole + whole_next, change + change_next, whole_next - whole, change_next - change

            energy = [None] * zlen
            for case in range(loads):
                low = None
                for z in range(zlen + 1):
                    high = [faces(case * comps + comp, z) for comp in range(comps)]
                    if low is not None:
                        part = quadratic(low, high, weights)
                        energy[z - 1] = part if energy[z - 1] is None else energy[z - 1] + part
                    low = high
            for z in range(zlen):
                here = quotient[z, first + TILE : first + 2 * TILE, lanes]
                quotient[z, first + TILE : first + 2 * TILE, lanes] = energy[z] * here

    for z in range(zlen):
        rows = [quotient[z, TILE + step : TILE + step + ylen] for step in range(-REACH, REACH + 1)]
        own_out[z] = sum((ROWS - abs(k - REACH)) * rows[k] for k in range(2 * REACH + 1))
        top = quotient[z, ylen : ylen + TILE]
        base = quotient[z, TILE : 2 * TILE]
        ahead, back = [], []
        for row in range(REACH):
            ahead.append(sum(float(REACH - row - k) * top[TILE - 1 - k : TILE - k] for k in range(REACH - row)))
            back.append(sum(float(row + 1 - k) * base[k : k + 1] for k in range(row + 1)))
        blank = jnp.zeros((1, xlen), jnp.float32)
        ends_out[0, ROWS * z : ROWS * (z + 1)] = jnp.concatenate(ahead + [blank], axis=0)
        ends_out[1, ROWS * z : ROWS * (z + 1)] = jnp.concatenate([blank] + back, axis=0)


def rows_kernel(own, ends, h_out, a_out, b_out):
    zlen, ylen, _ = own.shape
    index = lax.axis_index("sy")
    last = ends.shape[0] - 1
    low, high = jnp.maximum(index - 1, 0), jnp.minimum(index + 1, last)
    for z in range(zlen):
        part = slice(ROWS * z, ROWS * (z + 1))
        from_low = jnp.where(index > 0, ends[low, 0, part], 0.0)
        from_high = jnp.where(index < last, ends[high, 1, part], 0.0)
        h_out[z] = own[z]
        h_out[z, :ROWS] = own[z, :ROWS] + from_low
        h_out[z, ylen - ROWS :] = own[z, ylen - ROWS :] + from_high
    top = (zlen - REACH) * (lax.axis_index("sz") % 2 == 0).astype(jnp.int32)
    a_out[...] = h_out[pl.ds(top, REACH)]
    b_out[...] = h_out[pl.ds(zlen - REACH - top, REACH)]


def layers_kernel(h, a_in, b_in, out):
    zlen = h.shape[0]
    even = lax.axis_index("sz") % 2 == 0
    below = [jnp.where(even, b_in[k], a_in[k]) for k in range(REACH)]
    above = [jnp.where(even, a_in[k], b_in[k]) for k in range(REACH)]
    layers = below + [h[z] for z in range(zlen)] + above
    for z, layer in enumerate(spread_layers(layers)):
        out[z] = spread_x(layer)


def sum_kernel(parts, out):
    out[...] = parts[0] + parts[1]


def call(kernel, outs, args, scratch=(), space=pltpu.VMEM):
    shapes = [jax.ShapeDtypeStruct(out, jnp.float32) if isinstance(out, tuple) else out for out in outs]
    return pl.pallas_call(
        kernel,
        out_shape=shapes,
        in_specs=[pl.BlockSpec(memory_space=space)] * len(args),
        out_specs=[pl.BlockSpec(memory_space=pltpu.VMEM)] * len(outs),
        scratch_shapes=list(scratch),
        compiler_params=pltpu.CompilerParams(vmem_limit_bytes=32 * 1024 * 1024),
    )(*args)


def moved(value, axes, steps):
    sizes = [lax.axis_size(axis) for axis in axes]
    pairs = []
    for flat in range(int(np.prod(sizes))):
        place = np.unravel_index(flat, sizes)
        source = [int(p) + s for p, s in zip(place, steps)]
        if all(0 <= s < size for s, size in zip(source, sizes)):
            pairs.append((int(np.ravel_multi_index(source, sizes)), flat))
    return lax.ppermute(value, axes if len(axes) > 1 else axes[0], pairs)


def swapped(value, axis, first):
    pairs = []
    for low in range(first, lax.axis_size(axis) - 1, 2):
        pairs += [(low, low + 1), (low + 1, low)]
    return lax.ppermute(value, axis, pairs)


def body(displacements, density, solid, fixed):
    loads, comps, zlen, ylen, xlen = displacements.shape
    planes = loads * comps
    totals = (zlen * lax.axis_size("sz"), ylen * lax.axis_size("sy"))
    args = [
        pltpu.with_memory_space_constraint(arg, pltpu.HBM) for arg in (displacements, fixed, density, solid)
    ]

    disp, fixed, density, solid, z_send, y_send, d_send = call(
        lead_kernel,
        [jax.ShapeDtypeStruct(arg.shape, arg.dtype) for arg in args]
        + [(planes, ylen, xlen), (planes * zlen, xlen), (TILE, xlen)],
        args,
        scratch=[pltpu.SemaphoreType.DMA((len(args),))],
        space=pltpu.HBM,
    )
    z_in = moved(z_send, ("sz",), (1,))
    y_in = moved(y_send, ("sy",), (1,))
    d_in = moved(d_send, ("sy", "sz"), (1, 1))
    own, ends = call(
        lambda *refs: energy_kernel(totals, *refs),
        [(zlen, ylen, xlen), (2, ROWS * zlen, xlen)],
        (disp, fixed, density, solid, z_in, y_in, d_in),
        scratch=[
            pltpu.VMEM((planes, zlen + 1, ylen + TILE, xlen), jnp.float32),
            pltpu.VMEM((planes, zlen + 1, ylen + TILE, xlen), jnp.float32),
            pltpu.VMEM((zlen, ylen + 2 * TILE, xlen), jnp.float32),
        ],
    )
    ends = lax.all_gather(ends, "sy", axis=0)
    h, a_send, b_send = call(rows_kernel, [(zlen, ylen, xlen), (REACH, ylen, xlen), (REACH, ylen, xlen)], (own, ends))
    a_in = swapped(a_send, "sz", 0)
    b_in = swapped(b_send, "sz", 1)
    (part,) = call(layers_kernel, [(zlen, ylen, xlen)], (h, a_in, b_in))
    parts = lax.all_gather(part, "load", axis=0)
    (out,) = call(sum_kernel, [(zlen, ylen, xlen)], (parts,))
    return out


def solution(mesh):
    return jax.shard_map(
        body,
        mesh=mesh,
        in_specs=(
            P("load", None, "sz", "sy", None),
            P("sz", "sy", None),
            P("sz", "sy", None),
            P("sz", "sy", None),
        ),
        out_specs=P("sz", "sy", None),
        check_vma=False,
    )
```

```python
import jax
import jax.numpy as jnp
import numpy as np
from jax import lax
from jax.experimental import pallas as pl
from jax.experimental.pallas import tpu as pltpu
from jax.sharding import PartitionSpec as P

OFFSETS = [(0, 0, 0), (1, 0, 0), (1, 1, 0), (0, 1, 0), (0, 0, 1), (1, 0, 1), (1, 1, 1), (0, 1, 1)]
REACH = 3
ROWS = REACH + 1
TILE = 8
LANES = 128


def element_matrix():
    corners = np.array(
        [
            [-1.0, -1.0, -1.0],
            [1.0, -1.0, -1.0],
            [1.0, 1.0, -1.0],
            [-1.0, 1.0, -1.0],
            [-1.0, -1.0, 1.0],
            [1.0, -1.0, 1.0],
            [1.0, 1.0, 1.0],
            [-1.0, 1.0, 1.0],
        ]
    )
    poisson = 0.3
    lame = poisson / ((1.0 + poisson) * (1.0 - 2.0 * poisson))
    shear = 1.0 / (2.0 * (1.0 + poisson))
    elastic = np.zeros((6, 6))
    elastic[:3, :3] = lame
    for k in range(3):
        elastic[k, k] += 2.0 * shear
        elastic[3 + k, 3 + k] = shear
    gauss = 1.0 / np.sqrt(3.0)
    stiffness = np.zeros((24, 24))
    for gi in range(2):
        for gj in range(2):
            for gk in range(2):
                point = np.array([(2 * gi - 1) * gauss, (2 * gj - 1) * gauss, (2 * gk - 1) * gauss])
                strain = np.zeros((6, 24))
                for node in range(8):
                    grads = np.zeros(3)
                    for k in range(3):
                        value = corners[node, k] / 8.0
                        for m in range(3):
                            if m != k:
                                value = value * (1.0 + point[m] * corners[node, m])
                        grads[k] = 2.0 * value
                    col = 3 * node
                    strain[0, col] = grads[0]
                    strain[1, col + 1] = grads[1]
                    strain[2, col + 2] = grads[2]
                    strain[3, col] = grads[1]
                    strain[3, col + 1] = grads[0]
                    strain[4, col + 1] = grads[2]
                    strain[4, col + 2] = grads[1]
                    strain[5, col] = grads[2]
                    strain[5, col + 2] = grads[0]
                stiffness += strain.T @ elastic @ strain / 8.0
    return stiffness


def mode_weights():
    modes = [(i, j, k) for k in (0, 1) for j in (0, 1) for i in (0, 1)]
    sums = np.zeros((24, 24))
    for m, mode in enumerate(modes):
        for n, corner in enumerate(OFFSETS):
            sign = np.prod([(1 if corner[d] else -1) if mode[d] else 1 for d in range(3)])
            for comp in range(3):
                sums[3 * m + comp, 3 * n + comp] = sign
    form = sums @ element_matrix() @ sums.T / 64.0

    def at(first, second):
        return form[3 * modes.index(first[1]) + first[0], 3 * modes.index(second[1]) + second[0]]

    ux, vy, uy = (0, (1, 0, 0)), (1, (0, 1, 0)), (0, (0, 1, 0))
    uxy, wyz = (0, (1, 1, 0)), (2, (0, 1, 1))
    wxy, vxz, uxyz = (2, (1, 1, 0)), (1, (1, 0, 1)), (0, (1, 1, 1))
    return dict(
        normal=at(ux, ux) - at(ux, vy),
        trace=at(ux, vy),
        shear=at(uy, uy),
        plus=(at(uxy, uxy) + at(uxy, wyz)) / 2,
        minus=(at(uxy, uxy) - at(uxy, wyz)) / 2,
        twist=at(wxy, wxy) - at(wxy, vxz),
        twist_sum=at(wxy, vxz),
        corner=at(uxyz, uxyz),
    )


def square(value):
    return value * value


def quadratic(low, high, weights):
    x = [low[c][1] + high[c][1] for c in range(3)]
    y = [low[c][2] + high[c][2] for c in range(3)]
    z = [high[c][0] - low[c][0] for c in range(3)]
    xy = [low[c][3] + high[c][3] for c in range(3)]
    xz = [high[c][1] - low[c][1] for c in range(3)]
    yz = [high[c][2] - low[c][2] for c in range(3)]
    xyz = [high[c][3] - low[c][3] for c in range(3)]
    normal = square(x[0]) + square(y[1]) + square(z[2])
    trace = square(x[0] + y[1] + z[2])
    shear = square(y[0] + x[1]) + square(z[0] + x[2]) + square(z[1] + y[2])
    pairs = ((xy[0], yz[2]), (xy[1], xz[2]), (xz[0], yz[1]))
    plus = sum(square(p + q) for p, q in pairs)
    minus = sum(square(p - q) for p, q in pairs)
    twist = square(xy[2]) + square(xz[1]) + square(yz[0])
    twist_sum = square(xy[2] + xz[1] + yz[0])
    corner = square(xyz[0]) + square(xyz[1]) + square(xyz[2])
    groups = dict(
        normal=normal, trace=trace, shear=shear, plus=plus, minus=minus, twist=twist, twist_sum=twist_sum, corner=corner
    )
    return sum(np.float32(weights[name]) * group for name, group in groups.items())


def line_weight(coord, count):
    def outside(distance):
        missing = jnp.maximum(REACH - distance, 0)
        return missing * (missing + 1) // 2

    whole = (REACH + 1) * (REACH + 1)
    return (whole - outside(coord) - outside(count - 1 - coord)).astype(jnp.float32)


def voxel_factor(density, solid, plane, first_row, total_z, total_y):
    rows, length = density.shape
    row = lax.broadcasted_iota(jnp.int32, (rows, length), 0) + first_row
    column = lax.broadcasted_iota(jnp.int32, (rows, length), 1)
    weight = line_weight(row, total_y) * line_weight(column, length)
    weight = weight * line_weight(jnp.full((rows, length), plane, jnp.int32), total_z)
    return solid.astype(jnp.float32) * (-3.0 * density * density) / weight


def spread_x(value):
    rows, length = value.shape
    wide = jnp.concatenate([value, jnp.zeros((rows, LANES), jnp.float32)], axis=1)
    span = length + LANES
    wide = wide + pltpu.roll(wide, span - 1, 1)
    wide = wide + pltpu.roll(wide, span - 2, 1)
    wide = wide + pltpu.roll(wide, 1, 1)
    wide = wide + pltpu.roll(wide, 2, 1)
    return wide[:, :length]


def spread_layers(layers):
    for step in (1, 2, 1, 2):
        layers = [layers[k] + layers[k + step] for k in range(len(layers) - step)]
    return layers


def held(disp, fixed, case, comp, z, rows):
    return disp[case, comp, z, rows] * (1.0 - fixed[z, rows].astype(jnp.float32))


def split_x(value):
    length = value.shape[1]
    column = lax.broadcasted_iota(jnp.int32, value.shape, 1)
    ahead = jnp.where(column == length - 1, 0.0, pltpu.roll(value, length - 1, 1))
    return value + ahead, ahead - value


def spread_y(quotient, ylen):
    rows = [quotient[TILE + step : TILE + step + ylen] for step in range(-REACH, REACH + 1)]
    return sum((ROWS - abs(k - REACH)) * rows[k] for k in range(2 * REACH + 1))


def to_neighbours(quotient, ylen):
    top = quotient[ylen : ylen + TILE]
    base = quotient[TILE : 2 * TILE]
    ahead, back = [], []
    for row in range(REACH):
        ahead.append(sum(float(REACH - row - k) * top[TILE - 1 - k : TILE - k] for k in range(REACH - row)))
        back.append(sum(float(row + 1 - k) * base[k : k + 1] for k in range(row + 1)))
    return ahead, back


def lead_kernel(disp_hbm, fixed_hbm, density_hbm, solid_hbm, disp, fixed, density, solid, z_out, sems):
    loads, comps, _, _, _ = disp.shape
    copies = [
        pltpu.make_async_copy(source, target, sems.at[k])
        for k, (source, target) in enumerate(
            ((disp_hbm, disp), (fixed_hbm, fixed), (density_hbm, density), (solid_hbm, solid))
        )
    ]
    for copy in copies:
        copy.start()
    for copy in copies:
        copy.wait()
    for case in range(loads):
        for comp in range(comps):
            z_out[case * comps + comp] = held(disp, fixed, case, comp, 0, slice(None))


def tile_energies(plus, diff, first, lanes, layers, loads, comps):
    weights = mode_weights()

    def faces(k, z):
        near, far = slice(first, first + TILE), slice(first + 1, first + TILE + 1)
        whole, whole_next = plus[k, z, near, lanes], plus[k, z, far, lanes]
        change, change_next = diff[k, z, near, lanes], diff[k, z, far, lanes]
        return whole + whole_next, change + change_next, whole_next - whole, change_next - change

    energy = [None] * layers
    for case in range(loads):
        low = None
        for z in range(layers + 1):
            high = [faces(case * comps + comp, z) for comp in range(comps)]
            if low is not None:
                part = quadratic(low, high, weights)
                energy[z - 1] = part if energy[z - 1] is None else energy[z - 1] + part
            low = high
    return energy


def blank_last(value, first, ylen):
    row = lax.broadcasted_iota(jnp.int32, value.shape, 0) + first
    return jnp.where(row == ylen - 1, 0.0, value)


def inner_kernel(totals, disp, fixed, density, solid, own, lines, sends, last_plus, last_diff, last_factor, plus, diff, quotient):
    loads, comps, zlen, ylen, xlen = disp.shape
    total_z, total_y = totals
    base_z = lax.axis_index("sz") * zlen
    base_y = lax.axis_index("sy") * ylen
    inner = zlen - 1

    @pl.loop(0, loads * comps)
    def _(k):
        case, comp = k // comps, k % comps
        for z in range(zlen):
            whole, change = split_x(held(disp, fixed, case, comp, z, slice(None)))
            plus[k, z, :ylen] = whole
            diff[k, z, :ylen] = change
        last_plus[k] = whole
        last_diff[k] = change

    for comp in range(comps):
        for case in range(loads):
            for z in range(zlen):
                at = (comp * loads + case) * zlen + z
                lines[0, at : at + 1] = held(disp, fixed, case, comp, z, slice(0, 1))
                lines[1, at : at + 1] = held(disp, fixed, case, comp, z, slice(ylen - 1, ylen))

    zeros = jnp.zeros((TILE, xlen), jnp.float32)
    for z in range(zlen):
        factor = voxel_factor(density[z], solid[z], base_z + z, base_y, total_z, total_y)
        sends[0, ROWS * z + REACH : ROWS * (z + 1)] = factor[ylen - 1 :]
        sends[1, ROWS * z : ROWS * z + 1] = zeros[:1]
        if z == inner:
            last_factor[...] = factor
        else:
            quotient[z, :TILE] = zeros
            quotient[z, TILE : TILE + ylen] = factor
            quotient[z, TILE + ylen :] = zeros

    for first in range(0, ylen, TILE):

        @pl.loop(0, xlen // LANES)
        def _(chunk):
            lanes = pl.ds(pl.multiple_of(chunk * LANES, LANES), LANES)
            energy = tile_energies(plus, diff, first, lanes, inner, loads, comps)
            for z in range(inner):
                here = quotient[z, first + TILE : first + 2 * TILE, lanes]
                quotient[z, first + TILE : first + 2 * TILE, lanes] = blank_last(energy[z] * here, first, ylen)

    for z in range(inner):
        own[z] = spread_x(spread_y(quotient.at[z], ylen))
        ahead, back = to_neighbours(quotient.at[z], ylen)
        ends = spread_x(jnp.concatenate(ahead + back + [zeros[:2]], axis=0))
        sends[0, ROWS * z : ROWS * z + REACH] = ends[:REACH]
        sends[1, ROWS * z + 1 : ROWS * (z + 1)] = ends[REACH : 2 * REACH]


def outer_kernel(
    shape, z_in, own_in, lines_in, sends_in, last_plus, last_diff, last_factor, own, lines, a_out, b_out, plus, diff, quotient
):
    loads, comps, zlen, ylen, xlen = shape
    planes = loads * comps
    for k in range(planes):
        plus[k, 0, :ylen] = last_plus[k]
        diff[k, 0, :ylen] = last_diff[k]
        whole, change = split_x(z_in[k])
        plus[k, 1, :ylen] = whole
        diff[k, 1, :ylen] = change

    zeros = jnp.zeros((TILE, xlen), jnp.float32)
    quotient[:TILE] = zeros
    quotient[TILE + ylen :] = zeros
    for first in range(0, ylen, TILE):

        @pl.loop(0, xlen // LANES)
        def _(chunk):
            lanes = pl.ds(pl.multiple_of(chunk * LANES, LANES), LANES)
            (energy,) = tile_energies(plus, diff, first, lanes, 1, loads, comps)
            here = energy * last_factor[first : first + TILE, lanes]
            quotient[first + TILE : first + 2 * TILE, lanes] = blank_last(here, first, ylen)

    own[: zlen - 1] = own_in[: zlen - 1]
    own[zlen - 1] = spread_x(spread_y(quotient, ylen))
    ahead, back = to_neighbours(quotient, ylen)
    ends = spread_x(jnp.concatenate(ahead + back + [zeros[:2]], axis=0))

    stored = planes * zlen
    for end, row in ((0, 0), (1, ylen - 1)):
        lines[end, :stored] = lines_in[end]
        for comp in range(comps):
            for case in range(loads):
                at = stored + comp * loads + case
                lines[end, at : at + 1] = z_in[case * comps + comp, row : row + 1]
        lines[end, stored + planes :] = jnp.zeros((lines.shape[1] - stored - planes, xlen), jnp.float32)
    even = lax.axis_index("sy") % 2 == 0
    size = lines.shape[1]
    last = ROWS * (zlen - 1)
    up = jnp.concatenate([sends_in[0, :last], ends[:REACH], sends_in[0, last + REACH :]], axis=0)
    down = jnp.concatenate([sends_in[1, : last + 1], ends[REACH : 2 * REACH]], axis=0)
    a_out[:size] = jnp.where(even, lines[1], lines[0])
    b_out[:size] = jnp.where(even, lines[0], lines[1])
    a_out[size:] = jnp.where(even, up, down)
    b_out[size:] = jnp.where(even, down, up)


def line_quotients(near, far, factor, loads, comps, zlen):
    count = loads * zlen
    stored = comps * count

    def face(rows, comp):
        low = rows[comp * count : (comp + 1) * count]
        end = rows[stored + comp * loads : stored + (comp + 1) * loads]
        parts = []
        for case in range(loads):
            parts += [low[case * zlen + 1 : (case + 1) * zlen], end[case : case + 1]]
        return low, jnp.concatenate(parts, axis=0)

    low, high = [], []
    for comp in range(comps):
        for rows_near, rows_far, into in zip(face(near, comp), face(far, comp), (low, high)):
            (whole, change), (whole_next, change_next) = split_x(rows_near), split_x(rows_far)
            into.append((whole + whole_next, change + change_next, whole_next - whole, change_next - change))
    energy = quadratic(low, high, mode_weights())
    return sum(energy[case * zlen : (case + 1) * zlen] for case in range(loads)) * factor


def rows_kernel(loads, comps, own, lines, factors, a_in, b_in, h_out, a_out, b_out):
    zlen, ylen, _ = own.shape
    even = lax.axis_index("sy") % 2 == 0
    size = lines.shape[1]
    from_low = jnp.where(even, b_in[...], a_in[...])
    from_high = jnp.where(even, a_in[...], b_in[...])
    rows = [ROWS * z + REACH for z in range(zlen)]
    own_factor = jnp.concatenate([factors[0, r : r + 1] for r in rows], axis=0)
    low_factor = jnp.concatenate([from_low[size + r : size + r + 1] for r in rows], axis=0)
    first = line_quotients(from_low, lines[0], low_factor, loads, comps, zlen)
    last = line_quotients(lines[1], from_high, own_factor, loads, comps, zlen)
    both = spread_x(jnp.concatenate([first, last], axis=0))
    row = lax.broadcasted_iota(jnp.int32, (TILE, own.shape[2]), 0)
    rising = jnp.maximum(row - (TILE - 1 - ROWS), 0).astype(jnp.float32)
    falling = jnp.maximum(REACH - row, 0).astype(jnp.float32)
    blank = jnp.zeros((TILE - ROWS, own.shape[2]), jnp.float32)
    for z in range(zlen):
        part = slice(size + ROWS * z, size + ROWS * (z + 1))
        head = jnp.concatenate([from_low[part], blank], axis=0)
        head = jnp.where(row < REACH, head, 0.0) + falling * both[z : z + 1]
        tail = jnp.concatenate([blank, from_high[part]], axis=0)
        tail = jnp.where(row >= TILE - REACH, tail, 0.0) + rising * both[zlen + z : zlen + z + 1]
        h_out[z] = own[z]
        h_out[z, :TILE] += head
        h_out[z, ylen - TILE :] += tail
    top = (zlen - REACH) * (lax.axis_index("sz") % 2 == 0).astype(jnp.int32)
    a_out[...] = h_out[pl.ds(top, REACH)]
    b_out[...] = h_out[pl.ds(zlen - REACH - top, REACH)]


def layers_kernel(h, a_in, b_in, out):
    zlen = h.shape[0]
    even = lax.axis_index("sz") % 2 == 0
    below = [jnp.where(even, b_in[k], a_in[k]) for k in range(REACH)]
    above = [jnp.where(even, a_in[k], b_in[k]) for k in range(REACH)]
    layers = below + [h[z] for z in range(zlen)] + above
    for z, layer in enumerate(spread_layers(layers)):
        out[z] = layer


def sum_kernel(parts, out):
    out[...] = parts[0] + parts[1]


def call(kernel, outs, args, scratch=(), space=pltpu.VMEM):
    shapes = [jax.ShapeDtypeStruct(out, jnp.float32) if isinstance(out, tuple) else out for out in outs]
    return pl.pallas_call(
        kernel,
        out_shape=shapes,
        in_specs=[pl.BlockSpec(memory_space=space)] * len(args),
        out_specs=[pl.BlockSpec(memory_space=pltpu.VMEM)] * len(outs),
        scratch_shapes=list(scratch),
        compiler_params=pltpu.CompilerParams(vmem_limit_bytes=32 * 1024 * 1024),
    )(*args)


def moved(value, axes, steps):
    sizes = [lax.axis_size(axis) for axis in axes]
    pairs = []
    for flat in range(int(np.prod(sizes))):
        place = np.unravel_index(flat, sizes)
        source = [int(p) + s for p, s in zip(place, steps)]
        if all(0 <= s < size for s, size in zip(source, sizes)):
            pairs.append((int(np.ravel_multi_index(source, sizes)), flat))
    return lax.ppermute(value, axes if len(axes) > 1 else axes[0], pairs)


def swapped(value, axis, first):
    pairs = []
    for low in range(first, lax.axis_size(axis) - 1, 2):
        pairs += [(low, low + 1), (low + 1, low)]
    return lax.ppermute(value, axis, pairs)


def body(displacements, density, solid, fixed):
    loads, comps, zlen, ylen, xlen = displacements.shape
    planes = loads * comps
    totals = (zlen * lax.axis_size("sz"), ylen * lax.axis_size("sy"))
    args = [
        pltpu.with_memory_space_constraint(arg, pltpu.HBM) for arg in (displacements, fixed, density, solid)
    ]

    rows = planes * zlen
    size = rows + -(-planes // TILE) * TILE
    disp, fixed, density, solid, z_send = call(
        lead_kernel,
        [jax.ShapeDtypeStruct(arg.shape, arg.dtype) for arg in args] + [(planes, ylen, xlen)],
        args,
        scratch=[pltpu.SemaphoreType.DMA((len(args),))],
        space=pltpu.HBM,
    )
    z_in = moved(z_send, ("sz",), (1,))
    nodes = lambda layers: pltpu.VMEM((planes, layers, ylen + TILE, xlen), jnp.float32)
    inner = call(
        lambda *refs: inner_kernel(totals, *refs),
        [
            (zlen, ylen, xlen),
            (2, rows, xlen),
            (2, ROWS * zlen, xlen),
            (planes, ylen, xlen),
            (planes, ylen, xlen),
            (ylen, xlen),
        ],
        (disp, fixed, density, solid),
        scratch=[nodes(zlen), nodes(zlen), pltpu.VMEM((zlen - 1, ylen + 2 * TILE, xlen), jnp.float32)],
    )
    own, lines, a_send, b_send = call(
        lambda *refs: outer_kernel(displacements.shape, *refs),
        [(zlen, ylen, xlen), (2, size, xlen), (size + ROWS * zlen, xlen), (size + ROWS * zlen, xlen)],
        (z_in, *inner),
        scratch=[nodes(2), nodes(2), pltpu.VMEM((ylen + 2 * TILE, xlen), jnp.float32)],
    )
    a_in = swapped(a_send, "sy", 0)
    b_in = swapped(b_send, "sy", 1)
    h, a_send, b_send = call(
        lambda *refs: rows_kernel(loads, comps, *refs),
        [(zlen, ylen, xlen), (REACH, ylen, xlen), (REACH, ylen, xlen)],
        (own, lines, inner[2], a_in, b_in),
    )
    a_in = swapped(a_send, "sz", 0)
    b_in = swapped(b_send, "sz", 1)
    (part,) = call(layers_kernel, [(zlen, ylen, xlen)], (h, a_in, b_in))
    parts = lax.all_gather(part, "load", axis=0)
    (out,) = call(sum_kernel, [(zlen, ylen, xlen)], (parts,))
    return out


def solution(mesh):
    return jax.shard_map(
        body,
        mesh=mesh,
        in_specs=(
            P("load", None, "sz", "sy", None),
            P("sz", "sy", None),
            P("sz", "sy", None),
            P("sz", "sy", None),
        ),
        out_specs=P("sz", "sy", None),
        check_vma=False,
    )
```

```python
import jax
import jax.numpy as jnp
import numpy as np
from jax import lax
from jax.experimental import pallas as pl
from jax.experimental.pallas import tpu as pltpu
from jax.sharding import PartitionSpec as P

OFFSETS = [(0, 0, 0), (1, 0, 0), (1, 1, 0), (0, 1, 0), (0, 0, 1), (1, 0, 1), (1, 1, 1), (0, 1, 1)]
REACH = 3
ROWS = REACH + 1
TILE = 8
LANES = 128


def element_matrix():
    corners = np.array(
        [
            [-1.0, -1.0, -1.0],
            [1.0, -1.0, -1.0],
            [1.0, 1.0, -1.0],
            [-1.0, 1.0, -1.0],
            [-1.0, -1.0, 1.0],
            [1.0, -1.0, 1.0],
            [1.0, 1.0, 1.0],
            [-1.0, 1.0, 1.0],
        ]
    )
    poisson = 0.3
    lame = poisson / ((1.0 + poisson) * (1.0 - 2.0 * poisson))
    shear = 1.0 / (2.0 * (1.0 + poisson))
    elastic = np.zeros((6, 6))
    elastic[:3, :3] = lame
    for k in range(3):
        elastic[k, k] += 2.0 * shear
        elastic[3 + k, 3 + k] = shear
    gauss = 1.0 / np.sqrt(3.0)
    stiffness = np.zeros((24, 24))
    for gi in range(2):
        for gj in range(2):
            for gk in range(2):
                point = np.array([(2 * gi - 1) * gauss, (2 * gj - 1) * gauss, (2 * gk - 1) * gauss])
                strain = np.zeros((6, 24))
                for node in range(8):
                    grads = np.zeros(3)
                    for k in range(3):
                        value = corners[node, k] / 8.0
                        for m in range(3):
                            if m != k:
                                value = value * (1.0 + point[m] * corners[node, m])
                        grads[k] = 2.0 * value
                    col = 3 * node
                    strain[0, col] = grads[0]
                    strain[1, col + 1] = grads[1]
                    strain[2, col + 2] = grads[2]
                    strain[3, col] = grads[1]
                    strain[3, col + 1] = grads[0]
                    strain[4, col + 1] = grads[2]
                    strain[4, col + 2] = grads[1]
                    strain[5, col] = grads[2]
                    strain[5, col + 2] = grads[0]
                stiffness += strain.T @ elastic @ strain / 8.0
    return stiffness


def mode_weights():
    modes = [(i, j, k) for k in (0, 1) for j in (0, 1) for i in (0, 1)]
    sums = np.zeros((24, 24))
    for m, mode in enumerate(modes):
        for n, corner in enumerate(OFFSETS):
            sign = np.prod([(1 if corner[d] else -1) if mode[d] else 1 for d in range(3)])
            for comp in range(3):
                sums[3 * m + comp, 3 * n + comp] = sign
    form = sums @ element_matrix() @ sums.T / 64.0

    def at(first, second):
        return form[3 * modes.index(first[1]) + first[0], 3 * modes.index(second[1]) + second[0]]

    ux, vy, uy = (0, (1, 0, 0)), (1, (0, 1, 0)), (0, (0, 1, 0))
    uxy, wyz = (0, (1, 1, 0)), (2, (0, 1, 1))
    wxy, vxz, uxyz = (2, (1, 1, 0)), (1, (1, 0, 1)), (0, (1, 1, 1))
    return dict(
        normal=at(ux, ux) - at(ux, vy),
        trace=at(ux, vy),
        shear=at(uy, uy),
        plus=(at(uxy, uxy) + at(uxy, wyz)) / 2,
        minus=(at(uxy, uxy) - at(uxy, wyz)) / 2,
        twist=at(wxy, wxy) - at(wxy, vxz),
        twist_sum=at(wxy, vxz),
        corner=at(uxyz, uxyz),
    )


def square(value):
    return value * value


def quadratic(low, high, weights):
    x = [low[c][1] + high[c][1] for c in range(3)]
    y = [low[c][2] + high[c][2] for c in range(3)]
    z = [high[c][0] - low[c][0] for c in range(3)]
    xy = [low[c][3] + high[c][3] for c in range(3)]
    xz = [high[c][1] - low[c][1] for c in range(3)]
    yz = [high[c][2] - low[c][2] for c in range(3)]
    xyz = [high[c][3] - low[c][3] for c in range(3)]
    normal = square(x[0]) + square(y[1]) + square(z[2])
    trace = square(x[0] + y[1] + z[2])
    shear = square(y[0] + x[1]) + square(z[0] + x[2]) + square(z[1] + y[2])
    pairs = ((xy[0], yz[2]), (xy[1], xz[2]), (xz[0], yz[1]))
    plus = sum(square(p + q) for p, q in pairs)
    minus = sum(square(p - q) for p, q in pairs)
    twist = square(xy[2]) + square(xz[1]) + square(yz[0])
    twist_sum = square(xy[2] + xz[1] + yz[0])
    corner = square(xyz[0]) + square(xyz[1]) + square(xyz[2])
    groups = dict(
        normal=normal, trace=trace, shear=shear, plus=plus, minus=minus, twist=twist, twist_sum=twist_sum, corner=corner
    )
    return sum(np.float32(weights[name]) * group for name, group in groups.items())


def line_weight(coord, count):
    def outside(distance):
        missing = jnp.maximum(REACH - distance, 0)
        return missing * (missing + 1) // 2

    whole = (REACH + 1) * (REACH + 1)
    return (whole - outside(coord) - outside(count - 1 - coord)).astype(jnp.float32)


def voxel_factor(density, solid, plane, first_row, total_z, total_y):
    rows, length = density.shape
    row = lax.broadcasted_iota(jnp.int32, (rows, length), 0) + first_row
    column = lax.broadcasted_iota(jnp.int32, (rows, length), 1)
    weight = line_weight(row, total_y) * line_weight(column, length)
    weight = weight * line_weight(jnp.full((rows, length), plane, jnp.int32), total_z)
    return solid.astype(jnp.float32) * (-3.0 * density * density) / weight


def spread_x(value):
    rows, length = value.shape
    wide = jnp.concatenate([value, jnp.zeros((rows, LANES), jnp.float32)], axis=1)
    span = length + LANES
    wide = wide + pltpu.roll(wide, span - 1, 1)
    wide = wide + pltpu.roll(wide, span - 2, 1)
    wide = wide + pltpu.roll(wide, 1, 1)
    wide = wide + pltpu.roll(wide, 2, 1)
    return wide[:, :length]


def spread_layers(layers):
    for step in (1, 2, 1, 2):
        layers = [layers[k] + layers[k + step] for k in range(len(layers) - step)]
    return layers


def held(disp, fixed, case, comp, z, rows):
    return disp[case, comp, z, rows] * (1.0 - fixed[z, rows].astype(jnp.float32))


def split_x(value):
    length = value.shape[1]
    column = lax.broadcasted_iota(jnp.int32, value.shape, 1)
    ahead = jnp.where(column == length - 1, 0.0, pltpu.roll(value, length - 1, 1))
    return value + ahead, ahead - value


def spread_y(quotient, ylen):
    rows = [quotient[TILE + step : TILE + step + ylen] for step in range(-REACH, REACH + 1)]
    return sum((ROWS - abs(k - REACH)) * rows[k] for k in range(2 * REACH + 1))


def to_neighbours(quotient, ylen):
    top = quotient[ylen : ylen + TILE]
    base = quotient[TILE : 2 * TILE]
    ahead, back = [], []
    for row in range(REACH):
        ahead.append(sum(float(REACH - row - k) * top[TILE - 1 - k : TILE - k] for k in range(REACH - row)))
        back.append(sum(float(row + 1 - k) * base[k : k + 1] for k in range(row + 1)))
    return ahead, back


def lead_kernel(disp_hbm, fixed_hbm, density_hbm, solid_hbm, disp, fixed, density, solid, z_out, y_out, sems):
    loads, comps, zlen, _, _ = disp.shape
    copies = [
        pltpu.make_async_copy(source, target, sems.at[k])
        for k, (source, target) in enumerate(
            ((disp_hbm, disp), (fixed_hbm, fixed), (density_hbm, density), (solid_hbm, solid))
        )
    ]
    for copy in copies:
        copy.start()
    for copy in copies:
        copy.wait()
    for case in range(loads):
        for comp in range(comps):
            z_out[case * comps + comp] = held(disp, fixed, case, comp, 0, slice(None))
            for z in range(zlen):
                at = (comp * loads + case) * zlen + z
                y_out[at : at + 1] = held(disp, fixed, case, comp, z, slice(0, 1))


def tile_energies(plus, diff, first, lanes, layers, loads, comps):
    weights = mode_weights()

    def faces(k, z):
        near, far = slice(first, first + TILE), slice(first + 1, first + TILE + 1)
        whole, whole_next = plus[k, z, near, lanes], plus[k, z, far, lanes]
        change, change_next = diff[k, z, near, lanes], diff[k, z, far, lanes]
        return whole + whole_next, change + change_next, whole_next - whole, change_next - change

    energy = [None] * layers
    for case in range(loads):
        low = None
        for z in range(layers + 1):
            high = [faces(case * comps + comp, z) for comp in range(comps)]
            if low is not None:
                part = quadratic(low, high, weights)
                energy[z - 1] = part if energy[z - 1] is None else energy[z - 1] + part
            low = high
    return energy


def blank_last(value, first, ylen):
    row = lax.broadcasted_iota(jnp.int32, value.shape, 0) + first
    return jnp.where(row == ylen - 1, 0.0, value)


def inner_kernel(totals, disp, fixed, density, solid, own, line, sends, last_plus, last_diff, last_factor, edge, plus, diff, quotient):
    loads, comps, zlen, ylen, xlen = disp.shape
    total_z, total_y = totals
    base_z = lax.axis_index("sz") * zlen
    base_y = lax.axis_index("sy") * ylen
    inner = zlen - 1

    @pl.loop(0, loads * comps)
    def _(k):
        case, comp = k // comps, k % comps
        for z in range(zlen):
            whole, change = split_x(held(disp, fixed, case, comp, z, slice(None)))
            plus[k, z, :ylen] = whole
            diff[k, z, :ylen] = change
        last_plus[k] = whole
        last_diff[k] = change

    for comp in range(comps):
        for case in range(loads):
            for z in range(zlen):
                at = (comp * loads + case) * zlen + z
                line[0, at : at + 1] = plus[case * comps + comp, z, ylen - 1 : ylen]
                line[1, at : at + 1] = diff[case * comps + comp, z, ylen - 1 : ylen]

    zeros = jnp.zeros((TILE, xlen), jnp.float32)
    edge[...] = jnp.zeros(edge.shape, jnp.float32)
    for z in range(zlen):
        factor = voxel_factor(density[z], solid[z], base_z + z, base_y, total_z, total_y)
        edge[z : z + 1] = factor[ylen - 1 :]
        if z == inner:
            last_factor[...] = factor
        else:
            quotient[z, :TILE] = zeros
            quotient[z, TILE : TILE + ylen] = factor
            quotient[z, TILE + ylen :] = zeros

    for first in range(0, ylen, TILE):

        @pl.loop(0, xlen // LANES)
        def _(chunk):
            lanes = pl.ds(pl.multiple_of(chunk * LANES, LANES), LANES)
            energy = tile_energies(plus, diff, first, lanes, inner, loads, comps)
            for z in range(inner):
                here = quotient[z, first + TILE : first + 2 * TILE, lanes]
                quotient[z, first + TILE : first + 2 * TILE, lanes] = blank_last(energy[z] * here, first, ylen)

    for z in range(inner):
        own[z] = spread_x(spread_y(quotient.at[z], ylen))
        ahead, back = to_neighbours(quotient.at[z], ylen)
        ends = spread_x(jnp.concatenate(ahead + back + [zeros[:2]], axis=0))
        sends[0, REACH * z : REACH * (z + 1)] = ends[:REACH]
        sends[1, REACH * z : REACH * (z + 1)] = ends[REACH : 2 * REACH]


def outer_kernel(
    shape, z_in, y_in, disp, fixed, own_in, line, sends, last_plus, last_diff, last_factor, edge, own, known, a_out, b_out, plus, diff, quotient
):
    loads, comps, zlen, ylen, xlen = shape
    planes = loads * comps
    inner = zlen - 1
    for k in range(planes):
        plus[k, 0, :ylen] = last_plus[k]
        diff[k, 0, :ylen] = last_diff[k]
        whole, change = split_x(z_in[k])
        plus[k, 1, :ylen] = whole
        diff[k, 1, :ylen] = change

    zeros = jnp.zeros((TILE, xlen), jnp.float32)
    quotient[:TILE] = zeros
    quotient[TILE + ylen :] = zeros
    for first in range(0, ylen, TILE):

        @pl.loop(0, xlen // LANES)
        def _(chunk):
            lanes = pl.ds(pl.multiple_of(chunk * LANES, LANES), LANES)
            (energy,) = tile_energies(plus, diff, first, lanes, 1, loads, comps)
            here = energy * last_factor[first : first + TILE, lanes]
            quotient[first + TILE : first + 2 * TILE, lanes] = blank_last(here, first, ylen)

    count = loads * zlen
    low, high = [], []
    for comp in range(comps):
        part = slice(comp * count, (comp + 1) * count)
        whole, change = line[0, part], line[1, part]
        whole_next, change_next = split_x(y_in[part])
        face = (whole + whole_next, change + change_next, whole_next - whole, change_next - change)
        low.append(face)
        high.append([pltpu.roll(value, count - 1, 0) for value in face])
    energy = quadratic(low, high, mode_weights())
    energy = sum(energy[case * zlen : case * zlen + inner] for case in range(loads)) * edge[:inner]
    last = spread_x(jnp.concatenate([energy, jnp.zeros((TILE - inner, xlen), jnp.float32)], axis=0))

    row = lax.broadcasted_iota(jnp.int32, (TILE, xlen), 0)
    rising = jnp.maximum(row - (TILE - 1 - ROWS), 0).astype(jnp.float32)
    ups, downs = [], []
    for z in range(inner):
        own[z] = own_in[z]
        own[z, ylen - TILE :] += rising * last[z : z + 1]
        here = sends[0, REACH * z : REACH * (z + 1)]
        ups += [here[r : r + 1] + float(REACH - r) * last[z : z + 1] for r in range(REACH)]
        downs.append(sends[1, REACH * z : REACH * (z + 1)])
    own[inner] = spread_x(spread_y(quotient, ylen))
    ahead, back = to_neighbours(quotient, ylen)
    ends = spread_x(jnp.concatenate(ahead + back + [zeros[:2]], axis=0))
    ups += [ends[: REACH - 1], edge[inner:zlen]]
    downs.append(ends[REACH : 2 * REACH])

    pairs = [(case, comp) for comp in range(comps) for case in range(loads)]
    here_last = [held(disp, fixed, case, comp, inner, slice(ylen - 1, ylen)) for case, comp in pairs]
    here_first = [held(disp, fixed, case, comp, inner, slice(0, 1)) for case, comp in pairs]
    next_row = [y_in[(k + 1) * zlen - 1 : (k + 1) * zlen] for k in range(planes)]
    over_last = [z_in[case * comps + comp, ylen - 1 : ylen] for case, comp in pairs]
    over_first = [z_in[case * comps + comp, 0:1] for case, comp in pairs]
    rows = here_last + over_last + next_row + here_first + over_first
    known[: len(rows)] = jnp.concatenate(rows, axis=0)
    known[len(rows) :] = jnp.zeros((known.shape[0] - len(rows), xlen), jnp.float32)
    up = jnp.concatenate(ups + here_last + over_last, axis=0)
    down = jnp.concatenate(downs + over_first + [jnp.zeros((planes, xlen), jnp.float32)], axis=0)
    even = lax.axis_index("sy") % 2 == 0
    a_out[...] = jnp.where(even, up, down)
    b_out[...] = jnp.where(even, down, up)


def rows_kernel(loads, comps, own, known, edge, a_in, b_in, h_out, a_out, b_out):
    zlen, ylen, xlen = own.shape
    planes = loads * comps
    even = lax.axis_index("sy") % 2 == 0
    from_low = jnp.where(even, b_in[...], a_in[...])
    from_high = jnp.where(even, a_in[...], b_in[...])
    ends = REACH * zlen

    def nodes(first, second, comp):
        part = slice(comp * loads, (comp + 1) * loads)
        rows = jnp.concatenate([first[part], second[part]], axis=0)
        return split_x(jnp.concatenate([rows, rows], axis=0))

    def face(near_own, near_in, far_own, far_in, comp):
        whole, change = nodes(near_own, near_in, comp)
        whole_next, change_next = nodes(far_own, far_in, comp)
        return whole + whole_next, change + change_next, whole_next - whole, change_next - change

    here_last, over_last, next_row, here_first, over_first = (known[planes * k : planes * (k + 1)] for k in range(5))
    low_last, low_over = from_low[ends : ends + planes], from_low[ends + planes : ends + 2 * planes]
    next_over = from_high[ends : ends + planes]
    low = [face(here_last, low_last, next_row, here_first, comp) for comp in range(comps)]
    high = [face(over_last, low_over, next_over, over_first, comp) for comp in range(comps)]
    energy = quadratic(low, high, mode_weights())
    lines = [sum(energy[loads * k + case : loads * k + case + 1] for case in range(loads)) for k in range(2)]
    lines = [lines[0] * edge[zlen - 1 : zlen], lines[1] * from_low[ends - 1 : ends]]
    lines = spread_x(jnp.concatenate(lines + [jnp.zeros((TILE - 2, xlen), jnp.float32)], axis=0))

    row = lax.broadcasted_iota(jnp.int32, (TILE, xlen), 0)
    rising = jnp.maximum(row - (TILE - 1 - ROWS), 0).astype(jnp.float32)
    falling = jnp.maximum(REACH - row, 0).astype(jnp.float32)
    blank = jnp.zeros((TILE - REACH, xlen), jnp.float32)
    for z in range(zlen):
        part = slice(REACH * z, REACH * (z + 1))
        head = jnp.concatenate([from_low[part], blank], axis=0)
        tail = jnp.concatenate([blank, from_high[part]], axis=0)
        if z == zlen - 1:
            head = jnp.where(row == REACH - 1, 0.0, head) + falling * lines[1:2]
            tail = tail + rising * lines[0:1]
        h_out[z] = own[z]
        h_out[z, :TILE] += head
        h_out[z, ylen - TILE :] += tail
    top = (zlen - REACH) * (lax.axis_index("sz") % 2 == 0).astype(jnp.int32)
    a_out[...] = h_out[pl.ds(top, REACH)]
    b_out[...] = h_out[pl.ds(zlen - REACH - top, REACH)]


def layers_kernel(h, a_in, b_in, out):
    zlen = h.shape[0]
    even = lax.axis_index("sz") % 2 == 0
    below = [jnp.where(even, b_in[k], a_in[k]) for k in range(REACH)]
    above = [jnp.where(even, a_in[k], b_in[k]) for k in range(REACH)]
    layers = below + [h[z] for z in range(zlen)] + above
    for z, layer in enumerate(spread_layers(layers)):
        out[z] = layer


def sum_kernel(parts, out):
    out[...] = parts[0] + parts[1]


def call(kernel, outs, args, scratch=(), space=pltpu.VMEM):
    shapes = [jax.ShapeDtypeStruct(out, jnp.float32) if isinstance(out, tuple) else out for out in outs]
    return pl.pallas_call(
        kernel,
        out_shape=shapes,
        in_specs=[pl.BlockSpec(memory_space=space)] * len(args),
        out_specs=[pl.BlockSpec(memory_space=pltpu.VMEM)] * len(outs),
        scratch_shapes=list(scratch),
        compiler_params=pltpu.CompilerParams(vmem_limit_bytes=32 * 1024 * 1024),
    )(*args)


def moved(value, axes, steps):
    sizes = [lax.axis_size(axis) for axis in axes]
    pairs = []
    for flat in range(int(np.prod(sizes))):
        place = np.unravel_index(flat, sizes)
        source = [int(p) + s for p, s in zip(place, steps)]
        if all(0 <= s < size for s, size in zip(source, sizes)):
            pairs.append((int(np.ravel_multi_index(source, sizes)), flat))
    return lax.ppermute(value, axes if len(axes) > 1 else axes[0], pairs)


def swapped(value, axis, first):
    pairs = []
    for low in range(first, lax.axis_size(axis) - 1, 2):
        pairs += [(low, low + 1), (low + 1, low)]
    return lax.ppermute(value, axis, pairs)


def body(displacements, density, solid, fixed):
    loads, comps, zlen, ylen, xlen = displacements.shape
    planes = loads * comps
    totals = (zlen * lax.axis_size("sz"), ylen * lax.axis_size("sy"))
    args = [
        pltpu.with_memory_space_constraint(arg, pltpu.HBM) for arg in (displacements, fixed, density, solid)
    ]

    disp, fixed, density, solid, z_send, y_send = call(
        lead_kernel,
        [jax.ShapeDtypeStruct(arg.shape, arg.dtype) for arg in args] + [(planes, ylen, xlen), (planes * zlen, xlen)],
        args,
        scratch=[pltpu.SemaphoreType.DMA((len(args),))],
        space=pltpu.HBM,
    )
    z_in = moved(z_send, ("sz",), (1,))
    y_in = moved(y_send, ("sy",), (1,))
    nodes = lambda layers: pltpu.VMEM((planes, layers, ylen + TILE, xlen), jnp.float32)
    inner = call(
        lambda *refs: inner_kernel(totals, *refs),
        [
            (zlen, ylen, xlen),
            (2, planes * zlen, xlen),
            (2, REACH * (zlen - 1), xlen),
            (planes, ylen, xlen),
            (planes, ylen, xlen),
            (ylen, xlen),
            (TILE, xlen),
        ],
        (disp, fixed, density, solid),
        scratch=[nodes(zlen), nodes(zlen), pltpu.VMEM((zlen - 1, ylen + 2 * TILE, xlen), jnp.float32)],
    )
    size = REACH * zlen + 2 * planes
    own, known, a_send, b_send = call(
        lambda *refs: outer_kernel(displacements.shape, *refs),
        [(zlen, ylen, xlen), (-(-5 * planes // TILE) * TILE, xlen), (size, xlen), (size, xlen)],
        (z_in, y_in, disp, fixed, *inner),
        scratch=[nodes(2), nodes(2), pltpu.VMEM((ylen + 2 * TILE, xlen), jnp.float32)],
    )
    a_in = swapped(a_send, "sy", 0)
    b_in = swapped(b_send, "sy", 1)
    h, a_send, b_send = call(
        lambda *refs: rows_kernel(loads, comps, *refs),
        [(zlen, ylen, xlen), (REACH, ylen, xlen), (REACH, ylen, xlen)],
        (own, known, inner[-1], a_in, b_in),
    )
    a_in = swapped(a_send, "sz", 0)
    b_in = swapped(b_send, "sz", 1)
    (part,) = call(layers_kernel, [(zlen, ylen, xlen)], (h, a_in, b_in))
    parts = lax.all_gather(part, "load", axis=0)
    (out,) = call(sum_kernel, [(zlen, ylen, xlen)], (parts,))
    return out


def solution(mesh):
    return jax.shard_map(
        body,
        mesh=mesh,
        in_specs=(
            P("load", None, "sz", "sy", None),
            P("sz", "sy", None),
            P("sz", "sy", None),
            P("sz", "sy", None),
        ),
        out_specs=P("sz", "sy", None),
        check_vma=False,
    )
```

```python
import jax
import jax.numpy as jnp
import numpy as np
from jax import lax
from jax.experimental import pallas as pl
from jax.experimental.pallas import tpu as pltpu
from jax.sharding import PartitionSpec as P

OFFSETS = [(0, 0, 0), (1, 0, 0), (1, 1, 0), (0, 1, 0), (0, 0, 1), (1, 0, 1), (1, 1, 1), (0, 1, 1)]
REACH = 3
ROWS = REACH + 1
TILE = 8
LANES = 128


def element_matrix():
    corners = np.array(
        [
            [-1.0, -1.0, -1.0],
            [1.0, -1.0, -1.0],
            [1.0, 1.0, -1.0],
            [-1.0, 1.0, -1.0],
            [-1.0, -1.0, 1.0],
            [1.0, -1.0, 1.0],
            [1.0, 1.0, 1.0],
            [-1.0, 1.0, 1.0],
        ]
    )
    poisson = 0.3
    lame = poisson / ((1.0 + poisson) * (1.0 - 2.0 * poisson))
    shear = 1.0 / (2.0 * (1.0 + poisson))
    elastic = np.zeros((6, 6))
    elastic[:3, :3] = lame
    for k in range(3):
        elastic[k, k] += 2.0 * shear
        elastic[3 + k, 3 + k] = shear
    gauss = 1.0 / np.sqrt(3.0)
    stiffness = np.zeros((24, 24))
    for gi in range(2):
        for gj in range(2):
            for gk in range(2):
                point = np.array([(2 * gi - 1) * gauss, (2 * gj - 1) * gauss, (2 * gk - 1) * gauss])
                strain = np.zeros((6, 24))
                for node in range(8):
                    grads = np.zeros(3)
                    for k in range(3):
                        value = corners[node, k] / 8.0
                        for m in range(3):
                            if m != k:
                                value = value * (1.0 + point[m] * corners[node, m])
                        grads[k] = 2.0 * value
                    col = 3 * node
                    strain[0, col] = grads[0]
                    strain[1, col + 1] = grads[1]
                    strain[2, col + 2] = grads[2]
                    strain[3, col] = grads[1]
                    strain[3, col + 1] = grads[0]
                    strain[4, col + 1] = grads[2]
                    strain[4, col + 2] = grads[1]
                    strain[5, col] = grads[2]
                    strain[5, col + 2] = grads[0]
                stiffness += strain.T @ elastic @ strain / 8.0
    return stiffness


def mode_weights():
    modes = [(i, j, k) for k in (0, 1) for j in (0, 1) for i in (0, 1)]
    sums = np.zeros((24, 24))
    for m, mode in enumerate(modes):
        for n, corner in enumerate(OFFSETS):
            sign = np.prod([(1 if corner[d] else -1) if mode[d] else 1 for d in range(3)])
            for comp in range(3):
                sums[3 * m + comp, 3 * n + comp] = sign
    form = sums @ element_matrix() @ sums.T / 64.0

    def at(first, second):
        return form[3 * modes.index(first[1]) + first[0], 3 * modes.index(second[1]) + second[0]]

    ux, vy, uy = (0, (1, 0, 0)), (1, (0, 1, 0)), (0, (0, 1, 0))
    uxy, wyz = (0, (1, 1, 0)), (2, (0, 1, 1))
    wxy, vxz, uxyz = (2, (1, 1, 0)), (1, (1, 0, 1)), (0, (1, 1, 1))
    return dict(
        normal=at(ux, ux) - at(ux, vy),
        trace=at(ux, vy),
        shear=at(uy, uy),
        plus=(at(uxy, uxy) + at(uxy, wyz)) / 2,
        minus=(at(uxy, uxy) - at(uxy, wyz)) / 2,
        twist=at(wxy, wxy) - at(wxy, vxz),
        twist_sum=at(wxy, vxz),
        corner=at(uxyz, uxyz),
    )


def square(value):
    return value * value


def quadratic(low, high, weights):
    x = [low[c][1] + high[c][1] for c in range(3)]
    y = [low[c][2] + high[c][2] for c in range(3)]
    z = [high[c][0] - low[c][0] for c in range(3)]
    xy = [low[c][3] + high[c][3] for c in range(3)]
    xz = [high[c][1] - low[c][1] for c in range(3)]
    yz = [high[c][2] - low[c][2] for c in range(3)]
    xyz = [high[c][3] - low[c][3] for c in range(3)]
    normal = square(x[0]) + square(y[1]) + square(z[2])
    trace = square(x[0] + y[1] + z[2])
    shear = square(y[0] + x[1]) + square(z[0] + x[2]) + square(z[1] + y[2])
    pairs = ((xy[0], yz[2]), (xy[1], xz[2]), (xz[0], yz[1]))
    plus = sum(square(p + q) for p, q in pairs)
    minus = sum(square(p - q) for p, q in pairs)
    twist = square(xy[2]) + square(xz[1]) + square(yz[0])
    twist_sum = square(xy[2] + xz[1] + yz[0])
    corner = square(xyz[0]) + square(xyz[1]) + square(xyz[2])
    groups = dict(
        normal=normal, trace=trace, shear=shear, plus=plus, minus=minus, twist=twist, twist_sum=twist_sum, corner=corner
    )
    return sum(np.float32(weights[name]) * group for name, group in groups.items())


def line_weight(coord, count):
    def outside(distance):
        missing = jnp.maximum(REACH - distance, 0)
        return missing * (missing + 1) // 2

    whole = (REACH + 1) * (REACH + 1)
    return (whole - outside(coord) - outside(count - 1 - coord)).astype(jnp.float32)


def voxel_factor(density, solid, plane, first_row, total_z, total_y):
    rows, length = density.shape
    row = lax.broadcasted_iota(jnp.int32, (rows, length), 0) + first_row
    column = lax.broadcasted_iota(jnp.int32, (rows, length), 1)
    weight = line_weight(row, total_y) * line_weight(column, length)
    weight = weight * line_weight(jnp.full((rows, length), plane, jnp.int32), total_z)
    return solid.astype(jnp.float32) * (-3.0 * density * density) / weight


def spread_x(value):
    rows, length = value.shape
    wide = jnp.concatenate([value, jnp.zeros((rows, LANES), jnp.float32)], axis=1)
    span = length + LANES
    wide = wide + pltpu.roll(wide, span - 1, 1)
    wide = wide + pltpu.roll(wide, span - 2, 1)
    wide = wide + pltpu.roll(wide, 1, 1)
    wide = wide + pltpu.roll(wide, 2, 1)
    return wide[:, :length]


def spread_layers(layers):
    for step in (1, 2, 1, 2):
        layers = [layers[k] + layers[k + step] for k in range(len(layers) - step)]
    return layers


def held(disp, fixed, case, comp, z, rows):
    return disp[case, comp, z, rows] * (1.0 - fixed[z, rows].astype(jnp.float32))


def split_x(value):
    length = value.shape[1]
    column = lax.broadcasted_iota(jnp.int32, value.shape, 1)
    ahead = jnp.where(column == length - 1, 0.0, pltpu.roll(value, length - 1, 1))
    return value + ahead, ahead - value


def spread_y(quotient, ylen):
    rows = [quotient[TILE + step : TILE + step + ylen] for step in range(-REACH, REACH + 1)]
    return sum((ROWS - abs(k - REACH)) * rows[k] for k in range(2 * REACH + 1))


def to_neighbours(quotient, ylen):
    top = quotient[ylen : ylen + TILE]
    base = quotient[TILE : 2 * TILE]
    ahead, back = [], []
    for row in range(REACH):
        ahead.append(sum(float(REACH - row - k) * top[TILE - 1 - k : TILE - k] for k in range(REACH - row)))
        back.append(sum(float(row + 1 - k) * base[k : k + 1] for k in range(row + 1)))
    return ahead, back


def lead_kernel(disp_hbm, fixed_hbm, density_hbm, solid_hbm, disp, fixed, density, solid, z_out, y_out, sems):
    loads, comps, zlen, _, _ = disp.shape
    copies = [
        pltpu.make_async_copy(source, target, sems.at[k])
        for k, (source, target) in enumerate(
            ((disp_hbm, disp), (fixed_hbm, fixed), (density_hbm, density), (solid_hbm, solid))
        )
    ]
    for copy in copies:
        copy.start()
    for copy in copies:
        copy.wait()
    for case in range(loads):
        for comp in range(comps):
            z_out[case * comps + comp] = held(disp, fixed, case, comp, 0, slice(None))
            for z in range(zlen):
                at = (comp * loads + case) * zlen + z
                y_out[at : at + 1] = held(disp, fixed, case, comp, z, slice(0, 1))


def tile_energies(plus, diff, first, lanes, layers, loads, comps):
    weights = mode_weights()

    def faces(k, z):
        near, far = slice(first, first + TILE), slice(first + 1, first + TILE + 1)
        whole, whole_next = plus[k, z, near, lanes], plus[k, z, far, lanes]
        change, change_next = diff[k, z, near, lanes], diff[k, z, far, lanes]
        return whole + whole_next, change + change_next, whole_next - whole, change_next - change

    energy = [None] * layers
    for case in range(loads):
        low = None
        for z in range(layers + 1):
            high = [faces(case * comps + comp, z) for comp in range(comps)]
            if low is not None:
                part = quadratic(low, high, weights)
                energy[z - 1] = part if energy[z - 1] is None else energy[z - 1] + part
            low = high
    return energy


def blank_last(value, first, ylen):
    row = lax.broadcasted_iota(jnp.int32, value.shape, 0) + first
    return jnp.where(row == ylen - 1, 0.0, value)


def inner_kernel(totals, disp, fixed, density, solid, own, line, sends, last_plus, last_diff, last_factor, edge, plus, diff, quotient):
    loads, comps, zlen, ylen, xlen = disp.shape
    total_z, total_y = totals
    base_z = lax.axis_index("sz") * zlen
    base_y = lax.axis_index("sy") * ylen
    inner = zlen - 1

    @pl.loop(0, loads * comps)
    def _(k):
        case, comp = k // comps, k % comps
        for z in range(zlen):
            whole, change = split_x(held(disp, fixed, case, comp, z, slice(None)))
            plus[k, z, :ylen] = whole
            diff[k, z, :ylen] = change
        last_plus[k] = whole
        last_diff[k] = change

    for comp in range(comps):
        for case in range(loads):
            for z in range(zlen):
                at = (comp * loads + case) * zlen + z
                line[0, at : at + 1] = plus[case * comps + comp, z, ylen - 1 : ylen]
                line[1, at : at + 1] = diff[case * comps + comp, z, ylen - 1 : ylen]

    zeros = jnp.zeros((TILE, xlen), jnp.float32)
    edge[...] = jnp.zeros(edge.shape, jnp.float32)
    for z in range(zlen):
        factor = voxel_factor(density[z], solid[z], base_z + z, base_y, total_z, total_y)
        edge[z : z + 1] = factor[ylen - 1 :]
        if z == inner:
            last_factor[...] = factor
        else:
            quotient[z, :TILE] = zeros
            quotient[z, TILE : TILE + ylen] = factor
            quotient[z, TILE + ylen :] = zeros

    for first in range(0, ylen, TILE):

        @pl.loop(0, xlen // LANES)
        def _(chunk):
            lanes = pl.ds(pl.multiple_of(chunk * LANES, LANES), LANES)
            energy = tile_energies(plus, diff, first, lanes, inner, loads, comps)
            for z in range(inner):
                here = quotient[z, first + TILE : first + 2 * TILE, lanes]
                quotient[z, first + TILE : first + 2 * TILE, lanes] = blank_last(energy[z] * here, first, ylen)

    for z in range(inner):
        own[z] = spread_x(spread_y(quotient.at[z], ylen))
        ahead, back = to_neighbours(quotient.at[z], ylen)
        ends = spread_x(jnp.concatenate(ahead + back + [zeros[:2]], axis=0))
        sends[0, REACH * z : REACH * (z + 1)] = ends[:REACH]
        sends[1, REACH * z : REACH * (z + 1)] = ends[REACH : 2 * REACH]


def outer_kernel(
    shape, z_in, y_in, disp, fixed, own_in, line, sends, last_plus, last_diff, last_factor, edge, own, known, a_out, b_out, plus, diff, quotient
):
    loads, comps, zlen, ylen, xlen = shape
    planes = loads * comps
    inner = zlen - 1
    for k in range(planes):
        plus[k, 0, :ylen] = last_plus[k]
        diff[k, 0, :ylen] = last_diff[k]
        whole, change = split_x(z_in[k])
        plus[k, 1, :ylen] = whole
        diff[k, 1, :ylen] = change

    zeros = jnp.zeros((TILE, xlen), jnp.float32)
    quotient[:TILE] = zeros
    quotient[TILE + ylen :] = zeros
    for first in range(0, ylen, TILE):

        @pl.loop(0, xlen // LANES)
        def _(chunk):
            lanes = pl.ds(pl.multiple_of(chunk * LANES, LANES), LANES)
            (energy,) = tile_energies(plus, diff, first, lanes, 1, loads, comps)
            here = energy * last_factor[first : first + TILE, lanes]
            quotient[first + TILE : first + 2 * TILE, lanes] = blank_last(here, first, ylen)

    count = loads * zlen
    low, high = [], []
    for comp in range(comps):
        part = slice(comp * count, (comp + 1) * count)
        whole, change = line[0, part], line[1, part]
        whole_next, change_next = split_x(y_in[part])
        face = (whole + whole_next, change + change_next, whole_next - whole, change_next - change)
        low.append(face)
        high.append([pltpu.roll(value, count - 1, 0) for value in face])
    energy = quadratic(low, high, mode_weights())
    energy = sum(energy[case * zlen : case * zlen + inner] for case in range(loads)) * edge[:inner]
    last = spread_x(jnp.concatenate([energy, jnp.zeros((TILE - inner, xlen), jnp.float32)], axis=0))

    row = lax.broadcasted_iota(jnp.int32, (TILE, xlen), 0)
    rising = jnp.maximum(row - (TILE - 1 - ROWS), 0).astype(jnp.float32)
    ups, downs = [], []
    for z in range(inner):
        own[z] = own_in[z]
        own[z, ylen - TILE :] += rising * last[z : z + 1]
        here = sends[0, REACH * z : REACH * (z + 1)]
        ups += [here[r : r + 1] + float(REACH - r) * last[z : z + 1] for r in range(REACH)]
        downs.append(sends[1, REACH * z : REACH * (z + 1)])
    own[inner] = spread_x(spread_y(quotient, ylen))
    ahead, back = to_neighbours(quotient, ylen)
    ends = spread_x(jnp.concatenate(ahead + back + [zeros[:2]], axis=0))
    ups += [ends[: REACH - 1], edge[inner:zlen]]
    downs.append(ends[REACH : 2 * REACH])

    pairs = [(case, comp) for comp in range(comps) for case in range(loads)]
    here_last = [held(disp, fixed, case, comp, inner, slice(ylen - 1, ylen)) for case, comp in pairs]
    here_first = [held(disp, fixed, case, comp, inner, slice(0, 1)) for case, comp in pairs]
    next_row = [y_in[(k + 1) * zlen - 1 : (k + 1) * zlen] for k in range(planes)]
    over_last = [z_in[case * comps + comp, ylen - 1 : ylen] for case, comp in pairs]
    over_first = [z_in[case * comps + comp, 0:1] for case, comp in pairs]
    rows = here_last + over_last + next_row + here_first + over_first
    known[: len(rows)] = jnp.concatenate(rows, axis=0)
    known[len(rows) :] = jnp.zeros((known.shape[0] - len(rows), xlen), jnp.float32)
    up = jnp.concatenate(ups + here_last + over_last, axis=0)
    down = jnp.concatenate(downs + over_first + [jnp.zeros((planes, xlen), jnp.float32)], axis=0)
    even = lax.axis_index("sy") % 2 == 0
    a_out[...] = jnp.where(even, up, down)
    b_out[...] = jnp.where(even, down, up)


def rows_kernel(loads, comps, own, known, edge, b_in, a_in, h_out):
    zlen, ylen, xlen = own.shape
    planes = loads * comps
    even = lax.axis_index("sy") % 2 == 0
    from_low = jnp.where(even, b_in[...], a_in[...])
    from_high = jnp.where(even, a_in[...], b_in[...])
    ends = REACH * zlen

    def nodes(first, second, comp):
        part = slice(comp * loads, (comp + 1) * loads)
        rows = jnp.concatenate([first[part], second[part]], axis=0)
        return split_x(jnp.concatenate([rows, rows], axis=0))

    def face(near_own, near_in, far_own, far_in, comp):
        whole, change = nodes(near_own, near_in, comp)
        whole_next, change_next = nodes(far_own, far_in, comp)
        return whole + whole_next, change + change_next, whole_next - whole, change_next - change

    here_last, over_last, next_row, here_first, over_first = (known[planes * k : planes * (k + 1)] for k in range(5))
    low_last, low_over = from_low[ends : ends + planes], from_low[ends + planes : ends + 2 * planes]
    next_over = from_high[ends : ends + planes]
    low = [face(here_last, low_last, next_row, here_first, comp) for comp in range(comps)]
    high = [face(over_last, low_over, next_over, over_first, comp) for comp in range(comps)]
    energy = quadratic(low, high, mode_weights())
    lines = [sum(energy[loads * k + case : loads * k + case + 1] for case in range(loads)) for k in range(2)]
    lines = [lines[0] * edge[zlen - 1 : zlen], lines[1] * from_low[ends - 1 : ends]]
    lines = spread_x(jnp.concatenate(lines + [jnp.zeros((TILE - 2, xlen), jnp.float32)], axis=0))

    row = lax.broadcasted_iota(jnp.int32, (TILE, xlen), 0)
    rising = jnp.maximum(row - (TILE - 1 - ROWS), 0).astype(jnp.float32)
    falling = jnp.maximum(REACH - row, 0).astype(jnp.float32)
    blank = jnp.zeros((TILE - REACH, xlen), jnp.float32)
    for z in range(zlen):
        part = slice(REACH * z, REACH * (z + 1))
        head = jnp.concatenate([from_low[part], blank], axis=0)
        tail = jnp.concatenate([blank, from_high[part]], axis=0)
        if z == zlen - 1:
            head = jnp.where(row == REACH - 1, 0.0, head) + falling * lines[1:2]
            tail = tail + rising * lines[0:1]
        h_out[z] = own[z]
        h_out[z, :TILE] += head
        h_out[z, ylen - TILE :] += tail


def upper_side():
    return (lax.axis_index("sz") + lax.axis_index("load")) % 2 == 0


def total_kernel(parts, h_out, z_out):
    zlen = h_out.shape[0]
    for z in range(zlen):
        h_out[z] = parts[0, z] + parts[1, z]
    top = (zlen - REACH) * upper_side().astype(jnp.int32)
    z_out[...] = h_out[pl.ds(top, REACH)]


def layers_kernel(h, z_in, out):
    zlen = h.shape[0]
    upper = upper_side()
    first = lax.axis_index("load") == 0
    zero = jnp.zeros(h.shape[1:], jnp.float32)
    below = [jnp.where(upper, zero, z_in[k]) for k in range(REACH)]
    above = [jnp.where(upper, z_in[k], zero) for k in range(REACH)]
    layers = below + [jnp.where(first, h[z], zero) for z in range(zlen)] + above
    for z, layer in enumerate(spread_layers(layers)):
        out[z] = layer


def sum_kernel(parts, out):
    out[...] = parts[0] + parts[1]


def call(kernel, outs, args, scratch=(), space=pltpu.VMEM):
    shapes = [jax.ShapeDtypeStruct(out, jnp.float32) if isinstance(out, tuple) else out for out in outs]
    return pl.pallas_call(
        kernel,
        out_shape=shapes,
        in_specs=[pl.BlockSpec(memory_space=space)] * len(args),
        out_specs=[pl.BlockSpec(memory_space=pltpu.VMEM)] * len(outs),
        scratch_shapes=list(scratch),
        compiler_params=pltpu.CompilerParams(vmem_limit_bytes=32 * 1024 * 1024),
    )(*args)


def moved(value, axes, steps):
    sizes = [lax.axis_size(axis) for axis in axes]
    pairs = []
    for flat in range(int(np.prod(sizes))):
        place = np.unravel_index(flat, sizes)
        source = [int(p) + s for p, s in zip(place, steps)]
        if all(0 <= s < size for s, size in zip(source, sizes)):
            pairs.append((int(np.ravel_multi_index(source, sizes)), flat))
    return lax.ppermute(value, axes if len(axes) > 1 else axes[0], pairs)


def swapped(value, axis, first):
    pairs = []
    for low in range(first, lax.axis_size(axis) - 1, 2):
        pairs += [(low, low + 1), (low + 1, low)]
    return lax.ppermute(value, axis, pairs)


def shared(value):
    cores, size = lax.axis_size("load"), lax.axis_size("sz")
    pairs = []
    for core in range(cores):
        for low in range(core % 2, size - 1, 2):
            ends = core * size + low, core * size + low + 1
            pairs += [ends, ends[::-1]]
    return lax.ppermute(value, ("load", "sz"), pairs)


def body(displacements, density, solid, fixed):
    loads, comps, zlen, ylen, xlen = displacements.shape
    planes = loads * comps
    totals = (zlen * lax.axis_size("sz"), ylen * lax.axis_size("sy"))
    args = [
        pltpu.with_memory_space_constraint(arg, pltpu.HBM) for arg in (displacements, fixed, density, solid)
    ]

    disp, fixed, density, solid, z_send, y_send = call(
        lead_kernel,
        [jax.ShapeDtypeStruct(arg.shape, arg.dtype) for arg in args] + [(planes, ylen, xlen), (planes * zlen, xlen)],
        args,
        scratch=[pltpu.SemaphoreType.DMA((len(args),))],
        space=pltpu.HBM,
    )
    z_in = moved(z_send, ("sz",), (1,))
    y_in = moved(y_send, ("sy",), (1,))
    nodes = lambda layers: pltpu.VMEM((planes, layers, ylen + TILE, xlen), jnp.float32)
    inner = call(
        lambda *refs: inner_kernel(totals, *refs),
        [
            (zlen, ylen, xlen),
            (2, planes * zlen, xlen),
            (2, REACH * (zlen - 1), xlen),
            (planes, ylen, xlen),
            (planes, ylen, xlen),
            (ylen, xlen),
            (TILE, xlen),
        ],
        (disp, fixed, density, solid),
        scratch=[nodes(zlen), nodes(zlen), pltpu.VMEM((zlen - 1, ylen + 2 * TILE, xlen), jnp.float32)],
    )
    size = REACH * zlen + 2 * planes
    own, known, a_send, b_send = call(
        lambda *refs: outer_kernel(displacements.shape, *refs),
        [(zlen, ylen, xlen), (-(-5 * planes // TILE) * TILE, xlen), (size, xlen), (size, xlen)],
        (z_in, y_in, disp, fixed, *inner),
        scratch=[nodes(2), nodes(2), pltpu.VMEM((ylen + 2 * TILE, xlen), jnp.float32)],
    )
    b_in = swapped(b_send, "sy", 1)
    a_in = swapped(a_send, "sy", 0)
    (h,) = call(
        lambda *refs: rows_kernel(loads, comps, *refs), [(zlen, ylen, xlen)], (own, known, inner[-1], b_in, a_in)
    )
    parts = lax.all_gather(h, "load", axis=0)
    h, z_send = call(total_kernel, [(zlen, ylen, xlen), (REACH, ylen, xlen)], (parts,))
    (part,) = call(layers_kernel, [(zlen, ylen, xlen)], (h, shared(z_send)))
    parts = lax.all_gather(part, "load", axis=0)
    (out,) = call(sum_kernel, [(zlen, ylen, xlen)], (parts,))
    return out


def solution(mesh):
    return jax.shard_map(
        body,
        mesh=mesh,
        in_specs=(
            P("load", None, "sz", "sy", None),
            P("sz", "sy", None),
            P("sz", "sy", None),
            P("sz", "sy", None),
        ),
        out_specs=P("sz", "sy", None),
        check_vma=False,
    )
```

```python
import jax
import jax.numpy as jnp
import numpy as np
from jax import lax
from jax.experimental import pallas as pl
from jax.experimental.pallas import tpu as pltpu
from jax.sharding import PartitionSpec as P

OFFSETS = [(0, 0, 0), (1, 0, 0), (1, 1, 0), (0, 1, 0), (0, 0, 1), (1, 0, 1), (1, 1, 1), (0, 1, 1)]
REACH = 3
ROWS = REACH + 1
TILE = 8
LANES = 128


def element_matrix():
    corners = np.array(
        [
            [-1.0, -1.0, -1.0],
            [1.0, -1.0, -1.0],
            [1.0, 1.0, -1.0],
            [-1.0, 1.0, -1.0],
            [-1.0, -1.0, 1.0],
            [1.0, -1.0, 1.0],
            [1.0, 1.0, 1.0],
            [-1.0, 1.0, 1.0],
        ]
    )
    poisson = 0.3
    lame = poisson / ((1.0 + poisson) * (1.0 - 2.0 * poisson))
    shear = 1.0 / (2.0 * (1.0 + poisson))
    elastic = np.zeros((6, 6))
    elastic[:3, :3] = lame
    for k in range(3):
        elastic[k, k] += 2.0 * shear
        elastic[3 + k, 3 + k] = shear
    gauss = 1.0 / np.sqrt(3.0)
    stiffness = np.zeros((24, 24))
    for gi in range(2):
        for gj in range(2):
            for gk in range(2):
                point = np.array([(2 * gi - 1) * gauss, (2 * gj - 1) * gauss, (2 * gk - 1) * gauss])
                strain = np.zeros((6, 24))
                for node in range(8):
                    grads = np.zeros(3)
                    for k in range(3):
                        value = corners[node, k] / 8.0
                        for m in range(3):
                            if m != k:
                                value = value * (1.0 + point[m] * corners[node, m])
                        grads[k] = 2.0 * value
                    col = 3 * node
                    strain[0, col] = grads[0]
                    strain[1, col + 1] = grads[1]
                    strain[2, col + 2] = grads[2]
                    strain[3, col] = grads[1]
                    strain[3, col + 1] = grads[0]
                    strain[4, col + 1] = grads[2]
                    strain[4, col + 2] = grads[1]
                    strain[5, col] = grads[2]
                    strain[5, col + 2] = grads[0]
                stiffness += strain.T @ elastic @ strain / 8.0
    return stiffness


def mode_weights():
    modes = [(i, j, k) for k in (0, 1) for j in (0, 1) for i in (0, 1)]
    sums = np.zeros((24, 24))
    for m, mode in enumerate(modes):
        for n, corner in enumerate(OFFSETS):
            sign = np.prod([(1 if corner[d] else -1) if mode[d] else 1 for d in range(3)])
            for comp in range(3):
                sums[3 * m + comp, 3 * n + comp] = sign
    form = sums @ element_matrix() @ sums.T / 64.0

    def at(first, second):
        return form[3 * modes.index(first[1]) + first[0], 3 * modes.index(second[1]) + second[0]]

    ux, vy, uy = (0, (1, 0, 0)), (1, (0, 1, 0)), (0, (0, 1, 0))
    uxy, wyz = (0, (1, 1, 0)), (2, (0, 1, 1))
    wxy, vxz, uxyz = (2, (1, 1, 0)), (1, (1, 0, 1)), (0, (1, 1, 1))
    return dict(
        normal=at(ux, ux) - at(ux, vy),
        trace=at(ux, vy),
        shear=at(uy, uy),
        plus=(at(uxy, uxy) + at(uxy, wyz)) / 2,
        minus=(at(uxy, uxy) - at(uxy, wyz)) / 2,
        twist=at(wxy, wxy) - at(wxy, vxz),
        twist_sum=at(wxy, vxz),
        corner=at(uxyz, uxyz),
    )


def square(value):
    return value * value


def quadratic(low, high, weights):
    x = [low[c][1] + high[c][1] for c in range(3)]
    y = [low[c][2] + high[c][2] for c in range(3)]
    z = [high[c][0] - low[c][0] for c in range(3)]
    xy = [low[c][3] + high[c][3] for c in range(3)]
    xz = [high[c][1] - low[c][1] for c in range(3)]
    yz = [high[c][2] - low[c][2] for c in range(3)]
    xyz = [high[c][3] - low[c][3] for c in range(3)]
    normal = square(x[0]) + square(y[1]) + square(z[2])
    trace = square(x[0] + y[1] + z[2])
    shear = square(y[0] + x[1]) + square(z[0] + x[2]) + square(z[1] + y[2])
    pairs = ((xy[0], yz[2]), (xy[1], xz[2]), (xz[0], yz[1]))
    plus = sum(square(p + q) for p, q in pairs)
    minus = sum(square(p - q) for p, q in pairs)
    twist = square(xy[2]) + square(xz[1]) + square(yz[0])
    twist_sum = square(xy[2] + xz[1] + yz[0])
    corner = square(xyz[0]) + square(xyz[1]) + square(xyz[2])
    groups = dict(
        normal=normal, trace=trace, shear=shear, plus=plus, minus=minus, twist=twist, twist_sum=twist_sum, corner=corner
    )
    return sum(np.float32(weights[name]) * group for name, group in groups.items())


def line_weight(coord, count):
    def outside(distance):
        missing = jnp.maximum(REACH - distance, 0)
        return missing * (missing + 1) // 2

    whole = (REACH + 1) * (REACH + 1)
    return (whole - outside(coord) - outside(count - 1 - coord)).astype(jnp.float32)


def voxel_factor(density, solid, plane, first_row, total_z, total_y):
    rows, length = density.shape
    row = lax.broadcasted_iota(jnp.int32, (rows, length), 0) + first_row
    column = lax.broadcasted_iota(jnp.int32, (rows, length), 1)
    weight = line_weight(row, total_y) * line_weight(column, length)
    weight = weight * line_weight(jnp.full((rows, length), plane, jnp.int32), total_z)
    return solid.astype(jnp.float32) * (-3.0 * density * density) / weight


def spread_x(value):
    rows, length = value.shape
    wide = jnp.concatenate([value, jnp.zeros((rows, LANES), jnp.float32)], axis=1)
    span = length + LANES
    wide = wide + pltpu.roll(wide, span - 1, 1)
    wide = wide + pltpu.roll(wide, span - 2, 1)
    wide = wide + pltpu.roll(wide, 1, 1)
    wide = wide + pltpu.roll(wide, 2, 1)
    return wide[:, :length]


def spread_layers(layers):
    for step in (1, 2, 1, 2):
        layers = [layers[k] + layers[k + step] for k in range(len(layers) - step)]
    return layers


def held(disp, fixed, case, comp, z, rows):
    return disp[case, comp, z, rows] * (1.0 - fixed[z, rows].astype(jnp.float32))


def split_x(value):
    length = value.shape[1]
    column = lax.broadcasted_iota(jnp.int32, value.shape, 1)
    ahead = jnp.where(column == length - 1, 0.0, pltpu.roll(value, length - 1, 1))
    return value + ahead, ahead - value


def spread_y(quotient, ylen):
    rows = [quotient[TILE + step : TILE + step + ylen] for step in range(-REACH, REACH + 1)]
    return sum((ROWS - abs(k - REACH)) * rows[k] for k in range(2 * REACH + 1))


def to_neighbours(quotient, ylen):
    top = quotient[ylen : ylen + TILE]
    base = quotient[TILE : 2 * TILE]
    ahead, back = [], []
    for row in range(REACH):
        ahead.append(sum(float(REACH - row - k) * top[TILE - 1 - k : TILE - k] for k in range(REACH - row)))
        back.append(sum(float(row + 1 - k) * base[k : k + 1] for k in range(row + 1)))
    return ahead, back


def lead_kernel(disp_hbm, fixed_hbm, density_hbm, solid_hbm, disp, fixed, density, solid, z_out, y_out, sems):
    loads, comps, zlen, _, _ = disp.shape
    copies = [
        pltpu.make_async_copy(source, target, sems.at[k])
        for k, (source, target) in enumerate(
            ((disp_hbm, disp), (fixed_hbm, fixed), (density_hbm, density), (solid_hbm, solid))
        )
    ]
    for copy in copies:
        copy.start()
    for copy in copies:
        copy.wait()
    for case in range(loads):
        for comp in range(comps):
            z_out[case * comps + comp] = held(disp, fixed, case, comp, 0, slice(None))
            for z in range(zlen):
                at = (comp * loads + case) * zlen + z
                y_out[at : at + 1] = held(disp, fixed, case, comp, z, slice(0, 1))


def tile_energies(plus, diff, first, lanes, layers, loads, comps):
    weights = mode_weights()

    def faces(k, z):
        near, far = slice(first, first + TILE), slice(first + 1, first + TILE + 1)
        whole, whole_next = plus[k, z, near, lanes], plus[k, z, far, lanes]
        change, change_next = diff[k, z, near, lanes], diff[k, z, far, lanes]
        return whole + whole_next, change + change_next, whole_next - whole, change_next - change

    energy = [None] * layers
    for case in range(loads):
        low = None
        for z in range(layers + 1):
            high = [faces(case * comps + comp, z) for comp in range(comps)]
            if low is not None:
                part = quadratic(low, high, weights)
                energy[z - 1] = part if energy[z - 1] is None else energy[z - 1] + part
            low = high
    return energy


def blank_last(value, first, ylen):
    row = lax.broadcasted_iota(jnp.int32, value.shape, 0) + first
    return jnp.where(row == ylen - 1, 0.0, value)


def inner_kernel(totals, disp, fixed, density, solid, own, line, sends, last_plus, last_diff, last_factor, edge, plus, diff, quotient):
    loads, comps, zlen, ylen, xlen = disp.shape
    total_z, total_y = totals
    base_z = lax.axis_index("sz") * zlen
    base_y = lax.axis_index("sy") * ylen
    inner = zlen - 1

    @pl.loop(0, loads * comps)
    def _(k):
        case, comp = k // comps, k % comps
        for z in range(zlen):
            whole, change = split_x(held(disp, fixed, case, comp, z, slice(None)))
            plus[k, z, :ylen] = whole
            diff[k, z, :ylen] = change
        last_plus[k] = whole
        last_diff[k] = change

    for comp in range(comps):
        for case in range(loads):
            for z in range(zlen):
                at = (comp * loads + case) * zlen + z
                line[0, at : at + 1] = plus[case * comps + comp, z, ylen - 1 : ylen]
                line[1, at : at + 1] = diff[case * comps + comp, z, ylen - 1 : ylen]

    zeros = jnp.zeros((TILE, xlen), jnp.float32)
    edge[...] = jnp.zeros(edge.shape, jnp.float32)
    for z in range(zlen):
        factor = voxel_factor(density[z], solid[z], base_z + z, base_y, total_z, total_y)
        edge[z : z + 1] = factor[ylen - 1 :]
        if z == inner:
            last_factor[...] = factor
        else:
            quotient[z, :TILE] = zeros
            quotient[z, TILE : TILE + ylen] = factor
            quotient[z, TILE + ylen :] = zeros

    for first in range(0, ylen, TILE):

        @pl.loop(0, xlen // LANES)
        def _(chunk):
            lanes = pl.ds(pl.multiple_of(chunk * LANES, LANES), LANES)
            energy = tile_energies(plus, diff, first, lanes, inner, loads, comps)
            for z in range(inner):
                here = quotient[z, first + TILE : first + 2 * TILE, lanes]
                quotient[z, first + TILE : first + 2 * TILE, lanes] = blank_last(energy[z] * here, first, ylen)

    for z in range(inner):
        own[z] = spread_x(spread_y(quotient.at[z], ylen))
        ahead, back = to_neighbours(quotient.at[z], ylen)
        ends = spread_x(jnp.concatenate(ahead + back + [zeros[:2]], axis=0))
        sends[0, REACH * z : REACH * (z + 1)] = ends[:REACH]
        sends[1, REACH * z : REACH * (z + 1)] = ends[REACH : 2 * REACH]


def outer_kernel(
    shape, z_in, y_in, disp, fixed, own_in, line, sends, last_plus, last_diff, last_factor, edge, share, plus, diff, quotient
):
    loads, comps, zlen, ylen, xlen = shape
    planes = loads * comps
    inner = zlen - 1
    for k in range(planes):
        plus[k, 0, :ylen] = last_plus[k]
        diff[k, 0, :ylen] = last_diff[k]
        whole, change = split_x(z_in[k])
        plus[k, 1, :ylen] = whole
        diff[k, 1, :ylen] = change

    zeros = jnp.zeros((TILE, xlen), jnp.float32)
    quotient[:TILE] = zeros
    quotient[TILE + ylen :] = zeros
    for first in range(0, ylen, TILE):

        @pl.loop(0, xlen // LANES)
        def _(chunk):
            lanes = pl.ds(pl.multiple_of(chunk * LANES, LANES), LANES)
            (energy,) = tile_energies(plus, diff, first, lanes, 1, loads, comps)
            here = energy * last_factor[first : first + TILE, lanes]
            quotient[first + TILE : first + 2 * TILE, lanes] = blank_last(here, first, ylen)

    count = loads * zlen
    low, high = [], []
    for comp in range(comps):
        part = slice(comp * count, (comp + 1) * count)
        whole, change = line[0, part], line[1, part]
        whole_next, change_next = split_x(y_in[part])
        face = (whole + whole_next, change + change_next, whole_next - whole, change_next - change)
        low.append(face)
        high.append([pltpu.roll(value, count - 1, 0) for value in face])
    energy = quadratic(low, high, mode_weights())
    energy = sum(energy[case * zlen : case * zlen + inner] for case in range(loads)) * edge[:inner]
    last = spread_x(jnp.concatenate([energy, jnp.zeros((TILE - inner, xlen), jnp.float32)], axis=0))

    row = lax.broadcasted_iota(jnp.int32, (TILE, xlen), 0)
    rising = jnp.maximum(row - (TILE - 1 - ROWS), 0).astype(jnp.float32)
    ups, downs = [], []
    for z in range(inner):
        share[ylen * z : ylen * (z + 1)] = own_in[z]
        share[ylen * (z + 1) - TILE : ylen * (z + 1)] += rising * last[z : z + 1]
        here = sends[0, REACH * z : REACH * (z + 1)]
        ups += [here[r : r + 1] + float(REACH - r) * last[z : z + 1] for r in range(REACH)]
        downs.append(sends[1, REACH * z : REACH * (z + 1)])
    share[ylen * inner : ylen * zlen] = spread_x(spread_y(quotient, ylen))
    ahead, back = to_neighbours(quotient, ylen)
    ends = spread_x(jnp.concatenate(ahead + back + [zeros[:2]], axis=0))
    ups += [ends[: REACH - 1], edge[inner:zlen]]
    downs.append(ends[REACH : 2 * REACH])

    pairs = [(case, comp) for comp in range(comps) for case in range(loads)]
    here_last = [held(disp, fixed, case, comp, inner, slice(ylen - 1, ylen)) for case, comp in pairs]
    here_first = [held(disp, fixed, case, comp, inner, slice(0, 1)) for case, comp in pairs]
    next_row = [y_in[(k + 1) * zlen - 1 : (k + 1) * zlen] for k in range(planes)]
    over_last = [z_in[case * comps + comp, ylen - 1 : ylen] for case, comp in pairs]
    over_first = [z_in[case * comps + comp, 0:1] for case, comp in pairs]
    rows = ups + downs + here_last + over_last + next_row + here_first + over_first
    rows.append(jnp.zeros((share.shape[0] - ylen * zlen - 2 * REACH * zlen - 5 * planes, xlen), jnp.float32))
    share[ylen * zlen :] = jnp.concatenate(rows, axis=0)


class Shared:
    def __init__(self, shape):
        self.loads, self.comps, self.zlen, self.ylen, self.xlen = shape
        self.planes = self.loads * self.comps
        self.reach = REACH * self.zlen
        self.ups = self.ylen * self.zlen
        self.downs = self.ups + self.reach
        self.nodes = self.downs + self.reach
        self.rows = -(-(self.nodes + 5 * self.planes) // TILE) * TILE

    def group(self, parts, core, k):
        return parts[core, self.nodes + k * self.planes : self.nodes + (k + 1) * self.planes]

    def payload(self, cores):
        return -(-(self.reach + 2 * self.planes * cores) // TILE) * TILE


def meet_kernel(at, parts, b_out, a_out):
    cores = parts.shape[0]
    size = a_out.shape[0]
    ups = sum(parts[core, at.ups : at.downs - 1] for core in range(cores))
    downs = sum(parts[core, at.downs : at.nodes] for core in range(cores))
    up = [ups, parts[0, at.downs - 1 : at.downs]] + [at.group(parts, core, k) for k in range(2) for core in range(cores)]
    down = [downs] + [at.group(parts, core, 4) for core in range(cores)]
    up.append(jnp.zeros((size - at.reach - 2 * cores * at.planes, at.xlen), jnp.float32))
    down.append(jnp.zeros((size - at.reach - cores * at.planes, at.xlen), jnp.float32))
    up, down = (jnp.concatenate([piece for piece in rows if piece.shape[0]], axis=0) for rows in (up, down))
    even = lax.axis_index("sy") % 2 == 0
    a_out[...] = jnp.where(even, up, down)
    b_out[...] = jnp.where(even, down, up)


def rows_kernel(at, parts, edge, b_in, a_in, h_out, a_out, b_out):
    zlen, ylen, xlen = h_out.shape
    cores, loads, comps, ends = parts.shape[0], at.loads, at.comps, at.reach
    cases = cores * loads
    even = lax.axis_index("sy") % 2 == 0
    from_low = jnp.where(even, b_in[...], a_in[...])
    from_high = jnp.where(even, a_in[...], b_in[...])

    def here(k):
        return [at.group(parts, core, k) for core in range(cores)]

    def there(rows, k):
        first = ends + k * cores * at.planes
        return [rows[first + core * at.planes : first + (core + 1) * at.planes] for core in range(cores)]

    def nodes(first, second, comp):
        part = slice(comp * loads, (comp + 1) * loads)
        return split_x(jnp.concatenate([value[part] for value in first + second], axis=0))

    def face(near_own, near_in, far_own, far_in, comp):
        whole, change = nodes(near_own, near_in, comp)
        whole_next, change_next = nodes(far_own, far_in, comp)
        return whole + whole_next, change + change_next, whole_next - whole, change_next - change

    low = [face(here(0), there(from_low, 0), here(2), here(3), comp) for comp in range(comps)]
    high = [face(here(1), there(from_low, 1), there(from_high, 0), here(4), comp) for comp in range(comps)]
    energy = quadratic(low, high, mode_weights())
    lines = [sum(energy[cases * k + case : cases * k + case + 1] for case in range(cases)) for k in range(2)]
    lines = [lines[0] * edge[zlen - 1 : zlen], lines[1] * from_low[ends - 1 : ends]]
    lines = spread_x(jnp.concatenate(lines + [jnp.zeros((TILE - 2, xlen), jnp.float32)], axis=0))

    row = lax.broadcasted_iota(jnp.int32, (TILE, xlen), 0)
    rising = jnp.maximum(row - (TILE - 1 - ROWS), 0).astype(jnp.float32)
    falling = jnp.maximum(REACH - row, 0).astype(jnp.float32)
    blank = jnp.zeros((TILE - REACH, xlen), jnp.float32)
    for z in range(zlen):
        part = slice(REACH * z, REACH * (z + 1))
        head = jnp.concatenate([from_low[part], blank], axis=0)
        tail = jnp.concatenate([blank, from_high[part]], axis=0)
        if z == zlen - 1:
            head = jnp.where(row == REACH - 1, 0.0, head) + falling * lines[1:2]
            tail = tail + rising * lines[0:1]
        h_out[z] = sum(parts[core, ylen * z : ylen * (z + 1)] for core in range(cores))
        h_out[z, :TILE] += head
        h_out[z, ylen - TILE :] += tail
    top = (zlen - REACH) * (lax.axis_index("sz") % 2 == 0).astype(jnp.int32)
    a_out[...] = h_out[pl.ds(top, REACH)]
    b_out[...] = h_out[pl.ds(zlen - REACH - top, REACH)]


def layers_kernel(h, a_in, b_in, out):
    zlen = h.shape[0]
    even = lax.axis_index("sz") % 2 == 0
    below = [jnp.where(even, b_in[k], a_in[k]) for k in range(REACH)]
    above = [jnp.where(even, a_in[k], b_in[k]) for k in range(REACH)]
    layers = below + [h[z] for z in range(zlen)] + above
    for z, layer in enumerate(spread_layers(layers)):
        out[z] = layer


def pick_kernel(parts, out):
    out[...] = parts[parts.shape[0] - 1]


def call(kernel, outs, args, scratch=(), space=pltpu.VMEM):
    shapes = [jax.ShapeDtypeStruct(out, jnp.float32) if isinstance(out, tuple) else out for out in outs]
    return pl.pallas_call(
        kernel,
        out_shape=shapes,
        in_specs=[pl.BlockSpec(memory_space=space)] * len(args),
        out_specs=[pl.BlockSpec(memory_space=pltpu.VMEM)] * len(outs),
        scratch_shapes=list(scratch),
        compiler_params=pltpu.CompilerParams(vmem_limit_bytes=32 * 1024 * 1024),
    )(*args)


def moved(value, axes, steps):
    sizes = [lax.axis_size(axis) for axis in axes]
    pairs = []
    for flat in range(int(np.prod(sizes))):
        place = np.unravel_index(flat, sizes)
        source = [int(p) + s for p, s in zip(place, steps)]
        if all(0 <= s < size for s, size in zip(source, sizes)):
            pairs.append((int(np.ravel_multi_index(source, sizes)), flat))
    return lax.ppermute(value, axes if len(axes) > 1 else axes[0], pairs)


def swapped(value, axis, first):
    cores, size = lax.axis_size("load"), lax.axis_size(axis)
    pairs = []
    for low in range((cores - 1) * size + first, cores * size - 1, 2):
        pairs += [(low, low + 1), (low + 1, low)]
    return lax.ppermute(value, ("load", axis), pairs)


def body(displacements, density, solid, fixed):
    loads, comps, zlen, ylen, xlen = displacements.shape
    planes = loads * comps
    totals = (zlen * lax.axis_size("sz"), ylen * lax.axis_size("sy"))
    args = [
        pltpu.with_memory_space_constraint(arg, pltpu.HBM) for arg in (displacements, fixed, density, solid)
    ]

    disp, fixed, density, solid, z_send, y_send = call(
        lead_kernel,
        [jax.ShapeDtypeStruct(arg.shape, arg.dtype) for arg in args] + [(planes, ylen, xlen), (planes * zlen, xlen)],
        args,
        scratch=[pltpu.SemaphoreType.DMA((len(args),))],
        space=pltpu.HBM,
    )
    z_in = moved(z_send, ("sz",), (1,))
    y_in = moved(y_send, ("sy",), (1,))
    nodes = lambda layers: pltpu.VMEM((planes, layers, ylen + TILE, xlen), jnp.float32)
    inner = call(
        lambda *refs: inner_kernel(totals, *refs),
        [
            (zlen, ylen, xlen),
            (2, planes * zlen, xlen),
            (2, REACH * (zlen - 1), xlen),
            (planes, ylen, xlen),
            (planes, ylen, xlen),
            (ylen, xlen),
            (TILE, xlen),
        ],
        (disp, fixed, density, solid),
        scratch=[nodes(zlen), nodes(zlen), pltpu.VMEM((zlen - 1, ylen + 2 * TILE, xlen), jnp.float32)],
    )
    at = Shared(displacements.shape)
    (share,) = call(
        lambda *refs: outer_kernel(displacements.shape, *refs),
        [(at.rows, xlen)],
        (z_in, y_in, disp, fixed, *inner),
        scratch=[nodes(2), nodes(2), pltpu.VMEM((ylen + 2 * TILE, xlen), jnp.float32)],
    )
    parts = lax.all_gather(share, "load", axis=0)
    size = at.payload(parts.shape[0])
    b_send, a_send = call(lambda *refs: meet_kernel(at, *refs), [(size, xlen), (size, xlen)], (parts,))
    b_in = swapped(b_send, "sy", 1)
    a_in = swapped(a_send, "sy", 0)
    h, a_send, b_send = call(
        lambda *refs: rows_kernel(at, *refs),
        [(zlen, ylen, xlen), (REACH, ylen, xlen), (REACH, ylen, xlen)],
        (parts, inner[-1], b_in, a_in),
    )
    a_in = swapped(a_send, "sz", 0)
    b_in = swapped(b_send, "sz", 1)
    (part,) = call(layers_kernel, [(zlen, ylen, xlen)], (h, a_in, b_in))
    parts = lax.all_gather(part, "load", axis=0)
    (out,) = call(pick_kernel, [(zlen, ylen, xlen)], (parts,))
    return out


def solution(mesh):
    return jax.shard_map(
        body,
        mesh=mesh,
        in_specs=(
            P("load", None, "sz", "sy", None),
            P("sz", "sy", None),
            P("sz", "sy", None),
            P("sz", "sy", None),
        ),
        out_specs=P("sz", "sy", None),
        check_vma=False,
    )
```

```python
import jax
import jax.numpy as jnp
import numpy as np
from jax import lax
from jax.experimental import pallas as pl
from jax.experimental.pallas import tpu as pltpu
from jax.sharding import PartitionSpec as P

OFFSETS = [(0, 0, 0), (1, 0, 0), (1, 1, 0), (0, 1, 0), (0, 0, 1), (1, 0, 1), (1, 1, 1), (0, 1, 1)]
REACH = 3
ROWS = REACH + 1
TILE = 8
LANES = 128


def element_matrix():
    corners = np.array(
        [
            [-1.0, -1.0, -1.0],
            [1.0, -1.0, -1.0],
            [1.0, 1.0, -1.0],
            [-1.0, 1.0, -1.0],
            [-1.0, -1.0, 1.0],
            [1.0, -1.0, 1.0],
            [1.0, 1.0, 1.0],
            [-1.0, 1.0, 1.0],
        ]
    )
    poisson = 0.3
    lame = poisson / ((1.0 + poisson) * (1.0 - 2.0 * poisson))
    shear = 1.0 / (2.0 * (1.0 + poisson))
    elastic = np.zeros((6, 6))
    elastic[:3, :3] = lame
    for k in range(3):
        elastic[k, k] += 2.0 * shear
        elastic[3 + k, 3 + k] = shear
    gauss = 1.0 / np.sqrt(3.0)
    stiffness = np.zeros((24, 24))
    for gi in range(2):
        for gj in range(2):
            for gk in range(2):
                point = np.array([(2 * gi - 1) * gauss, (2 * gj - 1) * gauss, (2 * gk - 1) * gauss])
                strain = np.zeros((6, 24))
                for node in range(8):
                    grads = np.zeros(3)
                    for k in range(3):
                        value = corners[node, k] / 8.0
                        for m in range(3):
                            if m != k:
                                value = value * (1.0 + point[m] * corners[node, m])
                        grads[k] = 2.0 * value
                    col = 3 * node
                    strain[0, col] = grads[0]
                    strain[1, col + 1] = grads[1]
                    strain[2, col + 2] = grads[2]
                    strain[3, col] = grads[1]
                    strain[3, col + 1] = grads[0]
                    strain[4, col + 1] = grads[2]
                    strain[4, col + 2] = grads[1]
                    strain[5, col] = grads[2]
                    strain[5, col + 2] = grads[0]
                stiffness += strain.T @ elastic @ strain / 8.0
    return stiffness


def mode_weights():
    modes = [(i, j, k) for k in (0, 1) for j in (0, 1) for i in (0, 1)]
    sums = np.zeros((24, 24))
    for m, mode in enumerate(modes):
        for n, corner in enumerate(OFFSETS):
            sign = np.prod([(1 if corner[d] else -1) if mode[d] else 1 for d in range(3)])
            for comp in range(3):
                sums[3 * m + comp, 3 * n + comp] = sign
    form = sums @ element_matrix() @ sums.T / 64.0

    def at(first, second):
        return form[3 * modes.index(first[1]) + first[0], 3 * modes.index(second[1]) + second[0]]

    ux, vy, uy = (0, (1, 0, 0)), (1, (0, 1, 0)), (0, (0, 1, 0))
    uxy, wyz = (0, (1, 1, 0)), (2, (0, 1, 1))
    wxy, vxz, uxyz = (2, (1, 1, 0)), (1, (1, 0, 1)), (0, (1, 1, 1))
    return dict(
        normal=at(ux, ux) - at(ux, vy),
        trace=at(ux, vy),
        shear=at(uy, uy),
        plus=(at(uxy, uxy) + at(uxy, wyz)) / 2,
        minus=(at(uxy, uxy) - at(uxy, wyz)) / 2,
        twist=at(wxy, wxy) - at(wxy, vxz),
        twist_sum=at(wxy, vxz),
        corner=at(uxyz, uxyz),
    )


def square(value):
    return value * value


def quadratic(low, high, weights):
    x = [low[c][1] + high[c][1] for c in range(3)]
    y = [low[c][2] + high[c][2] for c in range(3)]
    z = [high[c][0] - low[c][0] for c in range(3)]
    xy = [low[c][3] + high[c][3] for c in range(3)]
    xz = [high[c][1] - low[c][1] for c in range(3)]
    yz = [high[c][2] - low[c][2] for c in range(3)]
    xyz = [high[c][3] - low[c][3] for c in range(3)]
    normal = square(x[0]) + square(y[1]) + square(z[2])
    trace = square(x[0] + y[1] + z[2])
    shear = square(y[0] + x[1]) + square(z[0] + x[2]) + square(z[1] + y[2])
    pairs = ((xy[0], yz[2]), (xy[1], xz[2]), (xz[0], yz[1]))
    plus = sum(square(p + q) for p, q in pairs)
    minus = sum(square(p - q) for p, q in pairs)
    twist = square(xy[2]) + square(xz[1]) + square(yz[0])
    twist_sum = square(xy[2] + xz[1] + yz[0])
    corner = square(xyz[0]) + square(xyz[1]) + square(xyz[2])
    groups = dict(
        normal=normal, trace=trace, shear=shear, plus=plus, minus=minus, twist=twist, twist_sum=twist_sum, corner=corner
    )
    return sum(np.float32(weights[name]) * group for name, group in groups.items())


def line_weight(coord, count):
    def outside(distance):
        missing = jnp.maximum(REACH - distance, 0)
        return missing * (missing + 1) // 2

    whole = (REACH + 1) * (REACH + 1)
    return (whole - outside(coord) - outside(count - 1 - coord)).astype(jnp.float32)


def voxel_factor(density, solid, plane, first_row, total_z, total_y):
    rows, length = density.shape
    row = lax.broadcasted_iota(jnp.int32, (rows, length), 0) + first_row
    column = lax.broadcasted_iota(jnp.int32, (rows, length), 1)
    weight = line_weight(row, total_y) * line_weight(column, length)
    weight = weight * line_weight(jnp.full((rows, length), plane, jnp.int32), total_z)
    return solid.astype(jnp.float32) * (-3.0 * density * density) / weight


def spread_x(value):
    rows, length = value.shape
    wide = jnp.concatenate([value, jnp.zeros((rows, LANES), jnp.float32)], axis=1)
    span = length + LANES
    wide = wide + pltpu.roll(wide, span - 1, 1)
    wide = wide + pltpu.roll(wide, span - 2, 1)
    wide = wide + pltpu.roll(wide, 1, 1)
    wide = wide + pltpu.roll(wide, 2, 1)
    return wide[:, :length]


def spread_layers(layers):
    for step in (1, 2, 1, 2):
        layers = [layers[k] + layers[k + step] for k in range(len(layers) - step)]
    return layers


def held(disp, fixed, case, comp, z, rows):
    return disp[case, comp, z, rows] * (1.0 - fixed[z, rows].astype(jnp.float32))


def split_x(value):
    length = value.shape[1]
    column = lax.broadcasted_iota(jnp.int32, value.shape, 1)
    ahead = jnp.where(column == length - 1, 0.0, pltpu.roll(value, length - 1, 1))
    return value + ahead, ahead - value


def spread_y(quotient, ylen):
    rows = [quotient[TILE + step : TILE + step + ylen] for step in range(-REACH, REACH + 1)]
    return sum((ROWS - abs(k - REACH)) * rows[k] for k in range(2 * REACH + 1))


def to_neighbours(quotient, ylen):
    top = quotient[ylen : ylen + TILE]
    base = quotient[TILE : 2 * TILE]
    ahead, back = [], []
    for row in range(REACH):
        ahead.append(sum(float(REACH - row - k) * top[TILE - 1 - k : TILE - k] for k in range(REACH - row)))
        back.append(sum(float(row + 1 - k) * base[k : k + 1] for k in range(row + 1)))
    return ahead, back


def lead_kernel(disp_hbm, fixed_hbm, density_hbm, solid_hbm, disp, fixed, density, solid, z_out, y_out, sems):
    loads, comps, zlen, _, _ = disp.shape
    copies = [
        pltpu.make_async_copy(source, target, sems.at[k])
        for k, (source, target) in enumerate(
            ((disp_hbm, disp), (fixed_hbm, fixed), (density_hbm, density), (solid_hbm, solid))
        )
    ]
    for copy in copies:
        copy.start()
    for copy in copies:
        copy.wait()
    for case in range(loads):
        for comp in range(comps):
            z_out[case * comps + comp] = held(disp, fixed, case, comp, 0, slice(None))
            for z in range(zlen):
                at = (comp * loads + case) * zlen + z
                y_out[at : at + 1] = held(disp, fixed, case, comp, z, slice(0, 1))


def tile_energies(plus, diff, first, lanes, layers, loads, comps):
    weights = mode_weights()

    def faces(k, z):
        near, far = slice(first, first + TILE), slice(first + 1, first + TILE + 1)
        whole, whole_next = plus[k, z, near, lanes], plus[k, z, far, lanes]
        change, change_next = diff[k, z, near, lanes], diff[k, z, far, lanes]
        return whole + whole_next, change + change_next, whole_next - whole, change_next - change

    energy = [None] * layers
    for case in range(loads):
        low = None
        for z in range(layers + 1):
            high = [faces(case * comps + comp, z) for comp in range(comps)]
            if low is not None:
                part = quadratic(low, high, weights)
                energy[z - 1] = part if energy[z - 1] is None else energy[z - 1] + part
            low = high
    return energy


def blank_last(value, first, ylen):
    row = lax.broadcasted_iota(jnp.int32, value.shape, 0) + first
    return jnp.where(row == ylen - 1, 0.0, value)


def inner_kernel(totals, disp, fixed, density, solid, own, line, sends, last_plus, last_diff, last_factor, edge, plus, diff, quotient):
    loads, comps, zlen, ylen, xlen = disp.shape
    total_z, total_y = totals
    base_z = lax.axis_index("sz") * zlen
    base_y = lax.axis_index("sy") * ylen
    inner = zlen - 1

    @pl.loop(0, loads * comps)
    def _(k):
        case, comp = k // comps, k % comps
        for z in range(zlen):
            whole, change = split_x(held(disp, fixed, case, comp, z, slice(None)))
            plus[k, z, :ylen] = whole
            diff[k, z, :ylen] = change
        last_plus[k] = whole
        last_diff[k] = change

    for comp in range(comps):
        for case in range(loads):
            for z in range(zlen):
                at = (comp * loads + case) * zlen + z
                line[0, at : at + 1] = plus[case * comps + comp, z, ylen - 1 : ylen]
                line[1, at : at + 1] = diff[case * comps + comp, z, ylen - 1 : ylen]

    zeros = jnp.zeros((TILE, xlen), jnp.float32)
    edge[...] = jnp.zeros(edge.shape, jnp.float32)
    for z in range(zlen):
        factor = voxel_factor(density[z], solid[z], base_z + z, base_y, total_z, total_y)
        edge[z : z + 1] = factor[ylen - 1 :]
        if z == inner:
            last_factor[...] = factor
        else:
            quotient[z, :TILE] = zeros
            quotient[z, TILE : TILE + ylen] = factor
            quotient[z, TILE + ylen :] = zeros

    for first in range(0, ylen, TILE):

        @pl.loop(0, xlen // LANES)
        def _(chunk):
            lanes = pl.ds(pl.multiple_of(chunk * LANES, LANES), LANES)
            energy = tile_energies(plus, diff, first, lanes, inner, loads, comps)
            for z in range(inner):
                here = quotient[z, first + TILE : first + 2 * TILE, lanes]
                quotient[z, first + TILE : first + 2 * TILE, lanes] = blank_last(energy[z] * here, first, ylen)

    for z in range(inner):
        own[z] = spread_x(spread_y(quotient.at[z], ylen))
        ahead, back = to_neighbours(quotient.at[z], ylen)
        ends = spread_x(jnp.concatenate(ahead + back + [zeros[:2]], axis=0))
        sends[0, REACH * z : REACH * (z + 1)] = ends[:REACH]
        sends[1, REACH * z : REACH * (z + 1)] = ends[REACH : 2 * REACH]


def outer_kernel(
    shape, z_in, y_in, disp, fixed, own_in, line, sends, last_plus, last_diff, last_factor, edge, own, known, a_out, b_out, plus, diff, quotient
):
    loads, comps, zlen, ylen, xlen = shape
    planes = loads * comps
    inner = zlen - 1
    for k in range(planes):
        plus[k, 0, :ylen] = last_plus[k]
        diff[k, 0, :ylen] = last_diff[k]
        whole, change = split_x(z_in[k])
        plus[k, 1, :ylen] = whole
        diff[k, 1, :ylen] = change

    zeros = jnp.zeros((TILE, xlen), jnp.float32)
    quotient[:TILE] = zeros
    quotient[TILE + ylen :] = zeros
    for first in range(0, ylen, TILE):

        @pl.loop(0, xlen // LANES)
        def _(chunk):
            lanes = pl.ds(pl.multiple_of(chunk * LANES, LANES), LANES)
            (energy,) = tile_energies(plus, diff, first, lanes, 1, loads, comps)
            here = energy * last_factor[first : first + TILE, lanes]
            quotient[first + TILE : first + 2 * TILE, lanes] = blank_last(here, first, ylen)

    count = loads * zlen
    low, high = [], []
    for comp in range(comps):
        part = slice(comp * count, (comp + 1) * count)
        whole, change = line[0, part], line[1, part]
        whole_next, change_next = split_x(y_in[part])
        face = (whole + whole_next, change + change_next, whole_next - whole, change_next - change)
        low.append(face)
        high.append([pltpu.roll(value, count - 1, 0) for value in face])
    energy = quadratic(low, high, mode_weights())
    energy = sum(energy[case * zlen : case * zlen + inner] for case in range(loads)) * edge[:inner]
    last = spread_x(jnp.concatenate([energy, jnp.zeros((TILE - inner, xlen), jnp.float32)], axis=0))

    row = lax.broadcasted_iota(jnp.int32, (TILE, xlen), 0)
    rising = jnp.maximum(row - (TILE - 1 - ROWS), 0).astype(jnp.float32)
    ups, downs = [], []
    for z in range(inner):
        own[z] = own_in[z]
        own[z, ylen - TILE :] += rising * last[z : z + 1]
        here = sends[0, REACH * z : REACH * (z + 1)]
        ups += [here[r : r + 1] + float(REACH - r) * last[z : z + 1] for r in range(REACH)]
        downs.append(sends[1, REACH * z : REACH * (z + 1)])
    own[inner] = spread_x(spread_y(quotient, ylen))
    ahead, back = to_neighbours(quotient, ylen)
    ends = spread_x(jnp.concatenate(ahead + back + [zeros[:2]], axis=0))
    ups += [ends[: REACH - 1], edge[inner:zlen]]
    downs.append(ends[REACH : 2 * REACH])

    pairs = [(case, comp) for comp in range(comps) for case in range(loads)]
    here_last = [held(disp, fixed, case, comp, inner, slice(ylen - 1, ylen)) for case, comp in pairs]
    here_first = [held(disp, fixed, case, comp, inner, slice(0, 1)) for case, comp in pairs]
    next_row = [y_in[(k + 1) * zlen - 1 : (k + 1) * zlen] for k in range(planes)]
    over_last = [z_in[case * comps + comp, ylen - 1 : ylen] for case, comp in pairs]
    over_first = [z_in[case * comps + comp, 0:1] for case, comp in pairs]
    rows = here_last + over_last + next_row + here_first + over_first
    known[: len(rows)] = jnp.concatenate(rows, axis=0)
    known[len(rows) :] = jnp.zeros((known.shape[0] - len(rows), xlen), jnp.float32)
    up = jnp.concatenate(ups + here_last + over_last, axis=0)
    down = jnp.concatenate(downs + over_first + [jnp.zeros((planes, xlen), jnp.float32)], axis=0)
    even = lax.axis_index("sy") % 2 == 0
    a_out[...] = jnp.where(even, up, down)
    b_out[...] = jnp.where(even, down, up)


def rows_kernel(loads, comps, own, known, edge, a_in, b_in, h_out, a_out, b_out):
    zlen, ylen, xlen = own.shape
    planes = loads * comps
    index, last = lax.axis_index("sy"), lax.axis_size("sy") - 1
    even = index % 2 == 0
    from_low = jnp.where(index > 0, jnp.where(even, b_in[...], a_in[...]), 0.0)
    from_high = jnp.where(index < last, jnp.where(even, a_in[...], b_in[...]), 0.0)
    ends = REACH * zlen

    def nodes(first, second, comp):
        part = slice(comp * loads, (comp + 1) * loads)
        rows = jnp.concatenate([first[part], second[part]], axis=0)
        return split_x(jnp.concatenate([rows, rows], axis=0))

    def face(near_own, near_in, far_own, far_in, comp):
        whole, change = nodes(near_own, near_in, comp)
        whole_next, change_next = nodes(far_own, far_in, comp)
        return whole + whole_next, change + change_next, whole_next - whole, change_next - change

    here_last, over_last, next_row, here_first, over_first = (known[planes * k : planes * (k + 1)] for k in range(5))
    low_last, low_over = from_low[ends : ends + planes], from_low[ends + planes : ends + 2 * planes]
    next_over = from_high[ends : ends + planes]
    low = [face(here_last, low_last, next_row, here_first, comp) for comp in range(comps)]
    high = [face(over_last, low_over, next_over, over_first, comp) for comp in range(comps)]
    energy = quadratic(low, high, mode_weights())
    lines = [sum(energy[loads * k + case : loads * k + case + 1] for case in range(loads)) for k in range(2)]
    lines = [lines[0] * edge[zlen - 1 : zlen], lines[1] * from_low[ends - 1 : ends]]
    lines = spread_x(jnp.concatenate(lines + [jnp.zeros((TILE - 2, xlen), jnp.float32)], axis=0))

    row = lax.broadcasted_iota(jnp.int32, (TILE, xlen), 0)
    rising = jnp.maximum(row - (TILE - 1 - ROWS), 0).astype(jnp.float32)
    falling = jnp.maximum(REACH - row, 0).astype(jnp.float32)
    blank = jnp.zeros((TILE - REACH, xlen), jnp.float32)
    for z in range(zlen):
        part = slice(REACH * z, REACH * (z + 1))
        head = jnp.concatenate([from_low[part], blank], axis=0)
        tail = jnp.concatenate([blank, from_high[part]], axis=0)
        if z == zlen - 1:
            head = jnp.where(row == REACH - 1, 0.0, head) + falling * lines[1:2]
            tail = tail + rising * lines[0:1]
        h_out[z] = own[z]
        h_out[z, :TILE] += head
        h_out[z, ylen - TILE :] += tail
    top = (zlen - REACH) * (lax.axis_index("sz") % 2 == 0).astype(jnp.int32)
    a_out[...] = h_out[pl.ds(top, REACH)]
    b_out[...] = h_out[pl.ds(zlen - REACH - top, REACH)]


def layers_kernel(h, a_in, b_in, out):
    zlen = h.shape[0]
    index, last = lax.axis_index("sz"), lax.axis_size("sz") - 1
    even = index % 2 == 0
    below = [jnp.where(index > 0, jnp.where(even, b_in[k], a_in[k]), 0.0) for k in range(REACH)]
    above = [jnp.where(index < last, jnp.where(even, a_in[k], b_in[k]), 0.0) for k in range(REACH)]
    layers = below + [h[z] for z in range(zlen)] + above
    for z, layer in enumerate(spread_layers(layers)):
        out[z] = layer


def sum_kernel(parts, out):
    out[...] = parts[0] + parts[1]


def call(kernel, outs, args, scratch=(), space=pltpu.VMEM):
    shapes = [jax.ShapeDtypeStruct(out, jnp.float32) if isinstance(out, tuple) else out for out in outs]
    return pl.pallas_call(
        kernel,
        out_shape=shapes,
        in_specs=[pl.BlockSpec(memory_space=space)] * len(args),
        out_specs=[pl.BlockSpec(memory_space=pltpu.VMEM)] * len(outs),
        scratch_shapes=list(scratch),
        compiler_params=pltpu.CompilerParams(vmem_limit_bytes=32 * 1024 * 1024),
    )(*args)


def moved(value, axes, steps):
    sizes = [lax.axis_size(axis) for axis in axes]
    pairs = []
    for flat in range(int(np.prod(sizes))):
        place = np.unravel_index(flat, sizes)
        source = [int(p) + s for p, s in zip(place, steps)]
        if all(0 <= s < size for s, size in zip(source, sizes)):
            pairs.append((int(np.ravel_multi_index(source, sizes)), flat))
    return lax.ppermute(value, axes if len(axes) > 1 else axes[0], pairs)


def swapped(value, axis, first):
    size = lax.axis_size(axis)
    pairs = {k: k for k in range(size)}
    for low in range(first, size - 1, 2):
        pairs[low], pairs[low + 1] = low + 1, low
    return lax.ppermute(value, axis, list(pairs.items()))


def body(displacements, density, solid, fixed):
    loads, comps, zlen, ylen, xlen = displacements.shape
    planes = loads * comps
    totals = (zlen * lax.axis_size("sz"), ylen * lax.axis_size("sy"))
    args = [
        pltpu.with_memory_space_constraint(arg, pltpu.HBM) for arg in (displacements, fixed, density, solid)
    ]

    disp, fixed, density, solid, z_send, y_send = call(
        lead_kernel,
        [jax.ShapeDtypeStruct(arg.shape, arg.dtype) for arg in args] + [(planes, ylen, xlen), (planes * zlen, xlen)],
        args,
        scratch=[pltpu.SemaphoreType.DMA((len(args),))],
        space=pltpu.HBM,
    )
    z_in = moved(z_send, ("sz",), (1,))
    y_in = moved(y_send, ("sy",), (1,))
    nodes = lambda layers: pltpu.VMEM((planes, layers, ylen + TILE, xlen), jnp.float32)
    inner = call(
        lambda *refs: inner_kernel(totals, *refs),
        [
            (zlen, ylen, xlen),
            (2, planes * zlen, xlen),
            (2, REACH * (zlen - 1), xlen),
            (planes, ylen, xlen),
            (planes, ylen, xlen),
            (ylen, xlen),
            (TILE, xlen),
        ],
        (disp, fixed, density, solid),
        scratch=[nodes(zlen), nodes(zlen), pltpu.VMEM((zlen - 1, ylen + 2 * TILE, xlen), jnp.float32)],
    )
    size = REACH * zlen + 2 * planes
    own, known, a_send, b_send = call(
        lambda *refs: outer_kernel(displacements.shape, *refs),
        [(zlen, ylen, xlen), (-(-5 * planes // TILE) * TILE, xlen), (size, xlen), (size, xlen)],
        (z_in, y_in, disp, fixed, *inner),
        scratch=[nodes(2), nodes(2), pltpu.VMEM((ylen + 2 * TILE, xlen), jnp.float32)],
    )
    a_in = swapped(a_send, "sy", 0)
    b_in = swapped(b_send, "sy", 1)
    h, a_send, b_send = call(
        lambda *refs: rows_kernel(loads, comps, *refs),
        [(zlen, ylen, xlen), (REACH, ylen, xlen), (REACH, ylen, xlen)],
        (own, known, inner[-1], a_in, b_in),
    )
    a_in = swapped(a_send, "sz", 0)
    b_in = swapped(b_send, "sz", 1)
    (part,) = call(layers_kernel, [(zlen, ylen, xlen)], (h, a_in, b_in))
    parts = lax.all_gather(part, "load", axis=0)
    (out,) = call(sum_kernel, [(zlen, ylen, xlen)], (parts,))
    return out


def solution(mesh):
    return jax.shard_map(
        body,
        mesh=mesh,
        in_specs=(
            P("load", None, "sz", "sy", None),
            P("sz", "sy", None),
            P("sz", "sy", None),
            P("sz", "sy", None),
        ),
        out_specs=P("sz", "sy", None),
        check_vma=False,
    )
```

```python
import jax
import jax.numpy as jnp
import numpy as np
from jax import lax
from jax.experimental import pallas as pl
from jax.experimental.pallas import tpu as pltpu
from jax.sharding import PartitionSpec as P

OFFSETS = [(0, 0, 0), (1, 0, 0), (1, 1, 0), (0, 1, 0), (0, 0, 1), (1, 0, 1), (1, 1, 1), (0, 1, 1)]
REACH = 3
ROWS = REACH + 1
TILE = 8
LANES = 128


def element_matrix():
    corners = np.array(
        [
            [-1.0, -1.0, -1.0],
            [1.0, -1.0, -1.0],
            [1.0, 1.0, -1.0],
            [-1.0, 1.0, -1.0],
            [-1.0, -1.0, 1.0],
            [1.0, -1.0, 1.0],
            [1.0, 1.0, 1.0],
            [-1.0, 1.0, 1.0],
        ]
    )
    poisson = 0.3
    lame = poisson / ((1.0 + poisson) * (1.0 - 2.0 * poisson))
    shear = 1.0 / (2.0 * (1.0 + poisson))
    elastic = np.zeros((6, 6))
    elastic[:3, :3] = lame
    for k in range(3):
        elastic[k, k] += 2.0 * shear
        elastic[3 + k, 3 + k] = shear
    gauss = 1.0 / np.sqrt(3.0)
    stiffness = np.zeros((24, 24))
    for gi in range(2):
        for gj in range(2):
            for gk in range(2):
                point = np.array([(2 * gi - 1) * gauss, (2 * gj - 1) * gauss, (2 * gk - 1) * gauss])
                strain = np.zeros((6, 24))
                for node in range(8):
                    grads = np.zeros(3)
                    for k in range(3):
                        value = corners[node, k] / 8.0
                        for m in range(3):
                            if m != k:
                                value = value * (1.0 + point[m] * corners[node, m])
                        grads[k] = 2.0 * value
                    col = 3 * node
                    strain[0, col] = grads[0]
                    strain[1, col + 1] = grads[1]
                    strain[2, col + 2] = grads[2]
                    strain[3, col] = grads[1]
                    strain[3, col + 1] = grads[0]
                    strain[4, col + 1] = grads[2]
                    strain[4, col + 2] = grads[1]
                    strain[5, col] = grads[2]
                    strain[5, col + 2] = grads[0]
                stiffness += strain.T @ elastic @ strain / 8.0
    return stiffness


def mode_weights():
    modes = [(i, j, k) for k in (0, 1) for j in (0, 1) for i in (0, 1)]
    sums = np.zeros((24, 24))
    for m, mode in enumerate(modes):
        for n, corner in enumerate(OFFSETS):
            sign = np.prod([(1 if corner[d] else -1) if mode[d] else 1 for d in range(3)])
            for comp in range(3):
                sums[3 * m + comp, 3 * n + comp] = sign
    form = sums @ element_matrix() @ sums.T / 64.0

    def at(first, second):
        return form[3 * modes.index(first[1]) + first[0], 3 * modes.index(second[1]) + second[0]]

    ux, vy, uy = (0, (1, 0, 0)), (1, (0, 1, 0)), (0, (0, 1, 0))
    uxy, wyz = (0, (1, 1, 0)), (2, (0, 1, 1))
    wxy, vxz, uxyz = (2, (1, 1, 0)), (1, (1, 0, 1)), (0, (1, 1, 1))
    return dict(
        normal=at(ux, ux) - at(ux, vy),
        trace=at(ux, vy),
        shear=at(uy, uy),
        plus=(at(uxy, uxy) + at(uxy, wyz)) / 2,
        minus=(at(uxy, uxy) - at(uxy, wyz)) / 2,
        twist=at(wxy, wxy) - at(wxy, vxz),
        twist_sum=at(wxy, vxz),
        corner=at(uxyz, uxyz),
    )


def square(value):
    return value * value


def quadratic(low, high, weights):
    x = [low[c][1] + high[c][1] for c in range(3)]
    y = [low[c][2] + high[c][2] for c in range(3)]
    z = [high[c][0] - low[c][0] for c in range(3)]
    xy = [low[c][3] + high[c][3] for c in range(3)]
    xz = [high[c][1] - low[c][1] for c in range(3)]
    yz = [high[c][2] - low[c][2] for c in range(3)]
    xyz = [high[c][3] - low[c][3] for c in range(3)]
    normal = square(x[0]) + square(y[1]) + square(z[2])
    trace = square(x[0] + y[1] + z[2])
    shear = square(y[0] + x[1]) + square(z[0] + x[2]) + square(z[1] + y[2])
    pairs = ((xy[0], yz[2]), (xy[1], xz[2]), (xz[0], yz[1]))
    plus = sum(square(p + q) for p, q in pairs)
    minus = sum(square(p - q) for p, q in pairs)
    twist = square(xy[2]) + square(xz[1]) + square(yz[0])
    twist_sum = square(xy[2] + xz[1] + yz[0])
    corner = square(xyz[0]) + square(xyz[1]) + square(xyz[2])
    groups = dict(
        normal=normal, trace=trace, shear=shear, plus=plus, minus=minus, twist=twist, twist_sum=twist_sum, corner=corner
    )
    return sum(np.float32(weights[name]) * group for name, group in groups.items())


def line_weight(coord, count):
    def outside(distance):
        missing = jnp.maximum(REACH - distance, 0)
        return missing * (missing + 1) // 2

    whole = (REACH + 1) * (REACH + 1)
    return (whole - outside(coord) - outside(count - 1 - coord)).astype(jnp.float32)


def voxel_factor(density, solid, plane, first_row, total_z, total_y):
    rows, length = density.shape
    row = lax.broadcasted_iota(jnp.int32, (rows, length), 0) + first_row
    column = lax.broadcasted_iota(jnp.int32, (rows, length), 1)
    weight = line_weight(row, total_y) * line_weight(column, length)
    weight = weight * line_weight(jnp.full((rows, length), plane, jnp.int32), total_z)
    return solid.astype(jnp.float32) * (-3.0 * density * density) / weight


def spread_x(value):
    rows, length = value.shape
    wide = jnp.concatenate([value, jnp.zeros((rows, LANES), jnp.float32)], axis=1)
    span = length + LANES
    wide = wide + pltpu.roll(wide, span - 1, 1)
    wide = wide + pltpu.roll(wide, span - 2, 1)
    wide = wide + pltpu.roll(wide, 1, 1)
    wide = wide + pltpu.roll(wide, 2, 1)
    return wide[:, :length]


def spread_layers(layers):
    for step in (1, 2, 1, 2):
        layers = [layers[k] + layers[k + step] for k in range(len(layers) - step)]
    return layers


def held(disp, fixed, case, comp, z, rows):
    return disp[case, comp, z, rows] * (1.0 - fixed[z, rows].astype(jnp.float32))


def split_x(value):
    length = value.shape[1]
    column = lax.broadcasted_iota(jnp.int32, value.shape, 1)
    ahead = jnp.where(column == length - 1, 0.0, pltpu.roll(value, length - 1, 1))
    return value + ahead, ahead - value


def spread_y(quotient, ylen):
    rows = [quotient[TILE + step : TILE + step + ylen] for step in range(-REACH, REACH + 1)]
    return sum((ROWS - abs(k - REACH)) * rows[k] for k in range(2 * REACH + 1))


def to_neighbours(quotient, ylen):
    top = quotient[ylen : ylen + TILE]
    base = quotient[TILE : 2 * TILE]
    ahead, back = [], []
    for row in range(REACH):
        ahead.append(sum(float(REACH - row - k) * top[TILE - 1 - k : TILE - k] for k in range(REACH - row)))
        back.append(sum(float(row + 1 - k) * base[k : k + 1] for k in range(row + 1)))
    return ahead, back


def lead_kernel(disp_hbm, fixed_hbm, density_hbm, solid_hbm, disp, fixed, density, solid, z_out, y_out, sems):
    loads, comps, zlen, _, _ = disp.shape
    copies = [
        pltpu.make_async_copy(source, target, sems.at[k])
        for k, (source, target) in enumerate(
            ((disp_hbm, disp), (fixed_hbm, fixed), (density_hbm, density), (solid_hbm, solid))
        )
    ]
    for copy in copies:
        copy.start()
    for copy in copies:
        copy.wait()
    for case in range(loads):
        for comp in range(comps):
            z_out[case * comps + comp] = held(disp, fixed, case, comp, 0, slice(None))
            for z in range(zlen):
                at = (comp * loads + case) * zlen + z
                y_out[at : at + 1] = held(disp, fixed, case, comp, z, slice(0, 1))


def tile_energies(plus, diff, first, lanes, layers, loads, comps):
    weights = mode_weights()

    def faces(k, z):
        near, far = slice(first, first + TILE), slice(first + 1, first + TILE + 1)
        whole, whole_next = plus[k, z, near, lanes], plus[k, z, far, lanes]
        change, change_next = diff[k, z, near, lanes], diff[k, z, far, lanes]
        return whole + whole_next, change + change_next, whole_next - whole, change_next - change

    energy = [None] * layers
    for case in range(loads):
        low = None
        for z in range(layers + 1):
            high = [faces(case * comps + comp, z) for comp in range(comps)]
            if low is not None:
                part = quadratic(low, high, weights)
                energy[z - 1] = part if energy[z - 1] is None else energy[z - 1] + part
            low = high
    return energy


def blank_last(value, first, ylen):
    row = lax.broadcasted_iota(jnp.int32, value.shape, 0) + first
    return jnp.where(row == ylen - 1, 0.0, value)


def inner_kernel(totals, disp, fixed, density, solid, own, line, sends, last_plus, last_diff, last_factor, edge, plus, diff, quotient):
    loads, comps, zlen, ylen, xlen = disp.shape
    total_z, total_y = totals
    base_z = lax.axis_index("sz") * zlen
    base_y = lax.axis_index("sy") * ylen
    inner = zlen - 1

    @pl.loop(0, loads * comps)
    def _(k):
        case, comp = k // comps, k % comps
        for z in range(zlen):
            whole, change = split_x(held(disp, fixed, case, comp, z, slice(None)))
            plus[k, z, :ylen] = whole
            diff[k, z, :ylen] = change
        last_plus[k] = whole
        last_diff[k] = change

    for comp in range(comps):
        for case in range(loads):
            for z in range(zlen):
                at = (comp * loads + case) * zlen + z
                line[0, at : at + 1] = plus[case * comps + comp, z, ylen - 1 : ylen]
                line[1, at : at + 1] = diff[case * comps + comp, z, ylen - 1 : ylen]

    zeros = jnp.zeros((TILE, xlen), jnp.float32)
    edge[...] = jnp.zeros(edge.shape, jnp.float32)
    for z in range(zlen):
        factor = voxel_factor(density[z], solid[z], base_z + z, base_y, total_z, total_y)
        edge[z : z + 1] = factor[ylen - 1 :]
        if z == inner:
            last_factor[...] = factor
        else:
            quotient[z, :TILE] = zeros
            quotient[z, TILE : TILE + ylen] = factor
            quotient[z, TILE + ylen :] = zeros

    for first in range(0, ylen, TILE):

        @pl.loop(0, xlen // LANES)
        def _(chunk):
            lanes = pl.ds(pl.multiple_of(chunk * LANES, LANES), LANES)
            energy = tile_energies(plus, diff, first, lanes, inner, loads, comps)
            for z in range(inner):
                here = quotient[z, first + TILE : first + 2 * TILE, lanes]
                quotient[z, first + TILE : first + 2 * TILE, lanes] = blank_last(energy[z] * here, first, ylen)

    for z in range(inner):
        own[z] = spread_x(spread_y(quotient.at[z], ylen))
        ahead, back = to_neighbours(quotient.at[z], ylen)
        ends = spread_x(jnp.concatenate(ahead + back + [zeros[:2]], axis=0))
        sends[0, REACH * z : REACH * (z + 1)] = ends[:REACH]
        sends[1, REACH * z : REACH * (z + 1)] = ends[REACH : 2 * REACH]


def outer_kernel(
    shape, z_in, y_in, disp, fixed, own_in, line, sends, last_plus, last_diff, last_factor, edge, own, known, a_out, b_out, plus, diff, quotient
):
    loads, comps, zlen, ylen, xlen = shape
    planes = loads * comps
    inner = zlen - 1
    for k in range(planes):
        plus[k, 0, :ylen] = last_plus[k]
        diff[k, 0, :ylen] = last_diff[k]
        whole, change = split_x(z_in[k])
        plus[k, 1, :ylen] = whole
        diff[k, 1, :ylen] = change

    zeros = jnp.zeros((TILE, xlen), jnp.float32)
    quotient[:TILE] = zeros
    quotient[TILE + ylen :] = zeros
    for first in range(0, ylen, TILE):

        @pl.loop(0, xlen // LANES)
        def _(chunk):
            lanes = pl.ds(pl.multiple_of(chunk * LANES, LANES), LANES)
            (energy,) = tile_energies(plus, diff, first, lanes, 1, loads, comps)
            here = energy * last_factor[first : first + TILE, lanes]
            quotient[first + TILE : first + 2 * TILE, lanes] = blank_last(here, first, ylen)

    count = loads * zlen
    more = lax.axis_index("sy") < lax.axis_size("sy") - 1
    low, high = [], []
    for comp in range(comps):
        part = slice(comp * count, (comp + 1) * count)
        whole, change = line[0, part], line[1, part]
        whole_next, change_next = split_x(jnp.where(more, y_in[part], 0.0))
        face = (whole + whole_next, change + change_next, whole_next - whole, change_next - change)
        low.append(face)
        high.append([pltpu.roll(value, count - 1, 0) for value in face])
    energy = quadratic(low, high, mode_weights())
    energy = sum(energy[case * zlen : case * zlen + inner] for case in range(loads)) * edge[:inner]
    last = spread_x(jnp.concatenate([energy, jnp.zeros((TILE - inner, xlen), jnp.float32)], axis=0))

    row = lax.broadcasted_iota(jnp.int32, (TILE, xlen), 0)
    rising = jnp.maximum(row - (TILE - 1 - ROWS), 0).astype(jnp.float32)
    ups, downs = [], []
    for z in range(inner):
        own[z] = own_in[z]
        own[z, ylen - TILE :] += rising * last[z : z + 1]
        here = sends[0, REACH * z : REACH * (z + 1)]
        ups += [here[r : r + 1] + float(REACH - r) * last[z : z + 1] for r in range(REACH)]
        downs.append(sends[1, REACH * z : REACH * (z + 1)])
    own[inner] = spread_x(spread_y(quotient, ylen))
    ahead, back = to_neighbours(quotient, ylen)
    ends = spread_x(jnp.concatenate(ahead + back + [zeros[:2]], axis=0))
    ups += [ends[: REACH - 1], edge[inner:zlen]]
    downs.append(ends[REACH : 2 * REACH])

    pairs = [(case, comp) for comp in range(comps) for case in range(loads)]
    here_last = [held(disp, fixed, case, comp, inner, slice(ylen - 1, ylen)) for case, comp in pairs]
    here_first = [held(disp, fixed, case, comp, inner, slice(0, 1)) for case, comp in pairs]
    next_row = [jnp.where(more, y_in[(k + 1) * zlen - 1 : (k + 1) * zlen], 0.0) for k in range(planes)]
    over_last = [z_in[case * comps + comp, ylen - 1 : ylen] for case, comp in pairs]
    over_first = [z_in[case * comps + comp, 0:1] for case, comp in pairs]
    rows = here_last + over_last + next_row + here_first + over_first
    known[: len(rows)] = jnp.concatenate(rows, axis=0)
    known[len(rows) :] = jnp.zeros((known.shape[0] - len(rows), xlen), jnp.float32)
    up = jnp.concatenate(ups + here_last + over_last, axis=0)
    down = jnp.concatenate(downs + over_first + [jnp.zeros((planes, xlen), jnp.float32)], axis=0)
    even = lax.axis_index("sy") % 2 == 0
    a_out[...] = jnp.where(even, up, down)
    b_out[...] = jnp.where(even, down, up)


def rows_kernel(loads, comps, own, known, edge, a_in, b_in, h_out, a_out, b_out):
    zlen, ylen, xlen = own.shape
    planes = loads * comps
    index, last = lax.axis_index("sy"), lax.axis_size("sy") - 1
    even = index % 2 == 0
    from_low = jnp.where(index > 0, jnp.where(even, b_in[...], a_in[...]), 0.0)
    from_high = jnp.where(index < last, jnp.where(even, a_in[...], b_in[...]), 0.0)
    ends = REACH * zlen

    def nodes(first, second, comp):
        part = slice(comp * loads, (comp + 1) * loads)
        rows = jnp.concatenate([first[part], second[part]], axis=0)
        return split_x(jnp.concatenate([rows, rows], axis=0))

    def face(near_own, near_in, far_own, far_in, comp):
        whole, change = nodes(near_own, near_in, comp)
        whole_next, change_next = nodes(far_own, far_in, comp)
        return whole + whole_next, change + change_next, whole_next - whole, change_next - change

    here_last, over_last, next_row, here_first, over_first = (known[planes * k : planes * (k + 1)] for k in range(5))
    low_last, low_over = from_low[ends : ends + planes], from_low[ends + planes : ends + 2 * planes]
    next_over = from_high[ends : ends + planes]
    low = [face(here_last, low_last, next_row, here_first, comp) for comp in range(comps)]
    high = [face(over_last, low_over, next_over, over_first, comp) for comp in range(comps)]
    energy = quadratic(low, high, mode_weights())
    lines = [sum(energy[loads * k + case : loads * k + case + 1] for case in range(loads)) for k in range(2)]
    lines = [lines[0] * edge[zlen - 1 : zlen], lines[1] * from_low[ends - 1 : ends]]
    lines = spread_x(jnp.concatenate(lines + [jnp.zeros((TILE - 2, xlen), jnp.float32)], axis=0))

    row = lax.broadcasted_iota(jnp.int32, (TILE, xlen), 0)
    rising = jnp.maximum(row - (TILE - 1 - ROWS), 0).astype(jnp.float32)
    falling = jnp.maximum(REACH - row, 0).astype(jnp.float32)
    blank = jnp.zeros((TILE - REACH, xlen), jnp.float32)
    for z in range(zlen):
        part = slice(REACH * z, REACH * (z + 1))
        head = jnp.concatenate([from_low[part], blank], axis=0)
        tail = jnp.concatenate([blank, from_high[part]], axis=0)
        if z == zlen - 1:
            head = jnp.where(row == REACH - 1, 0.0, head) + falling * lines[1:2]
            tail = tail + rising * lines[0:1]
        h_out[z] = own[z]
        h_out[z, :TILE] += head
        h_out[z, ylen - TILE :] += tail
    top = (zlen - REACH) * (lax.axis_index("sz") % 2 == 0).astype(jnp.int32)
    a_out[...] = h_out[pl.ds(top, REACH)]
    b_out[...] = h_out[pl.ds(zlen - REACH - top, REACH)]


def layers_kernel(h, a_in, b_in, out):
    zlen = h.shape[0]
    index, last = lax.axis_index("sz"), lax.axis_size("sz") - 1
    even = index % 2 == 0
    below = [jnp.where(index > 0, jnp.where(even, b_in[k], a_in[k]), 0.0) for k in range(REACH)]
    above = [jnp.where(index < last, jnp.where(even, a_in[k], b_in[k]), 0.0) for k in range(REACH)]
    layers = below + [h[z] for z in range(zlen)] + above
    for z, layer in enumerate(spread_layers(layers)):
        out[z] = layer


def sum_kernel(parts, out):
    out[...] = parts[0] + parts[1]


def call(kernel, outs, args, scratch=(), space=pltpu.VMEM):
    shapes = [jax.ShapeDtypeStruct(out, jnp.float32) if isinstance(out, tuple) else out for out in outs]
    return pl.pallas_call(
        kernel,
        out_shape=shapes,
        in_specs=[pl.BlockSpec(memory_space=space)] * len(args),
        out_specs=[pl.BlockSpec(memory_space=pltpu.VMEM)] * len(outs),
        scratch_shapes=list(scratch),
        compiler_params=pltpu.CompilerParams(vmem_limit_bytes=32 * 1024 * 1024),
    )(*args)


def moved(value, axis):
    size = lax.axis_size(axis)
    return lax.ppermute(value, axis, [(k + 1, k) for k in range(size - 1)])


def ring_moved(value, axis):
    size = lax.axis_size(axis)
    return lax.ppermute(value, axis, [((k + 1) % size, k) for k in range(size)])


def swapped(value, axis, first):
    size = lax.axis_size(axis)
    pairs = {k: k for k in range(size)}
    for low in range(first, size + first - 1, 2):
        high = (low + 1) % size
        pairs[low], pairs[high] = high, low
    return lax.ppermute(value, axis, list(pairs.items()))


def swapped_inside(value, axis, other):
    size, rows = lax.axis_size(axis), lax.axis_size(other)
    pairs = []
    for row in range(rows):
        beside = row ^ 1 if (row ^ 1) < rows else row
        for k in range(size):
            inside = k + 1 if k % 2 else k - 1
            target = (row, inside) if 0 <= inside < size else (beside, k)
            pairs.append((row * size + k, target[0] * size + target[1]))
    return lax.ppermute(value, (other, axis), pairs)


def body(displacements, density, solid, fixed):
    loads, comps, zlen, ylen, xlen = displacements.shape
    planes = loads * comps
    totals = (zlen * lax.axis_size("sz"), ylen * lax.axis_size("sy"))
    args = [
        pltpu.with_memory_space_constraint(arg, pltpu.HBM) for arg in (displacements, fixed, density, solid)
    ]

    disp, fixed, density, solid, z_send, y_send = call(
        lead_kernel,
        [jax.ShapeDtypeStruct(arg.shape, arg.dtype) for arg in args] + [(planes, ylen, xlen), (planes * zlen, xlen)],
        args,
        scratch=[pltpu.SemaphoreType.DMA((len(args),))],
        space=pltpu.HBM,
    )
    z_in = moved(z_send, "sz")
    y_in = ring_moved(y_send, "sy")
    nodes = lambda layers: pltpu.VMEM((planes, layers, ylen + TILE, xlen), jnp.float32)
    inner = call(
        lambda *refs: inner_kernel(totals, *refs),
        [
            (zlen, ylen, xlen),
            (2, planes * zlen, xlen),
            (2, REACH * (zlen - 1), xlen),
            (planes, ylen, xlen),
            (planes, ylen, xlen),
            (ylen, xlen),
            (TILE, xlen),
        ],
        (disp, fixed, density, solid),
        scratch=[nodes(zlen), nodes(zlen), pltpu.VMEM((zlen - 1, ylen + 2 * TILE, xlen), jnp.float32)],
    )
    size = REACH * zlen + 2 * planes
    own, known, a_send, b_send = call(
        lambda *refs: outer_kernel(displacements.shape, *refs),
        [(zlen, ylen, xlen), (-(-5 * planes // TILE) * TILE, xlen), (size, xlen), (size, xlen)],
        (z_in, y_in, disp, fixed, *inner),
        scratch=[nodes(2), nodes(2), pltpu.VMEM((ylen + 2 * TILE, xlen), jnp.float32)],
    )
    a_in = swapped(a_send, "sy", 0)
    b_in = swapped(b_send, "sy", 1)
    h, a_send, b_send = call(
        lambda *refs: rows_kernel(loads, comps, *refs),
        [(zlen, ylen, xlen), (REACH, ylen, xlen), (REACH, ylen, xlen)],
        (own, known, inner[-1], a_in, b_in),
    )
    a_in = swapped(a_send, "sz", 0)
    b_in = swapped_inside(b_send, "sz", "sy")
    (part,) = call(layers_kernel, [(zlen, ylen, xlen)], (h, a_in, b_in))
    parts = lax.all_gather(part, "load", axis=0)
    (out,) = call(sum_kernel, [(zlen, ylen, xlen)], (parts,))
    return out


def solution(mesh):
    return jax.shard_map(
        body,
        mesh=mesh,
        in_specs=(
            P("load", None, "sz", "sy", None),
            P("sz", "sy", None),
            P("sz", "sy", None),
            P("sz", "sy", None),
        ),
        out_specs=P("sz", "sy", None),
        check_vma=False,
    )
```

```python
import jax
import jax.numpy as jnp
import numpy as np
from jax import lax
from jax.experimental import pallas as pl
from jax.experimental.pallas import tpu as pltpu
from jax.sharding import PartitionSpec as P

OFFSETS = [(0, 0, 0), (1, 0, 0), (1, 1, 0), (0, 1, 0), (0, 0, 1), (1, 0, 1), (1, 1, 1), (0, 1, 1)]
REACH = 3
ROWS = REACH + 1
TILE = 8
LANES = 128


def element_matrix():
    corners = np.array(
        [
            [-1.0, -1.0, -1.0],
            [1.0, -1.0, -1.0],
            [1.0, 1.0, -1.0],
            [-1.0, 1.0, -1.0],
            [-1.0, -1.0, 1.0],
            [1.0, -1.0, 1.0],
            [1.0, 1.0, 1.0],
            [-1.0, 1.0, 1.0],
        ]
    )
    poisson = 0.3
    lame = poisson / ((1.0 + poisson) * (1.0 - 2.0 * poisson))
    shear = 1.0 / (2.0 * (1.0 + poisson))
    elastic = np.zeros((6, 6))
    elastic[:3, :3] = lame
    for k in range(3):
        elastic[k, k] += 2.0 * shear
        elastic[3 + k, 3 + k] = shear
    gauss = 1.0 / np.sqrt(3.0)
    stiffness = np.zeros((24, 24))
    for gi in range(2):
        for gj in range(2):
            for gk in range(2):
                point = np.array([(2 * gi - 1) * gauss, (2 * gj - 1) * gauss, (2 * gk - 1) * gauss])
                strain = np.zeros((6, 24))
                for node in range(8):
                    grads = np.zeros(3)
                    for k in range(3):
                        value = corners[node, k] / 8.0
                        for m in range(3):
                            if m != k:
                                value = value * (1.0 + point[m] * corners[node, m])
                        grads[k] = 2.0 * value
                    col = 3 * node
                    strain[0, col] = grads[0]
                    strain[1, col + 1] = grads[1]
                    strain[2, col + 2] = grads[2]
                    strain[3, col] = grads[1]
                    strain[3, col + 1] = grads[0]
                    strain[4, col + 1] = grads[2]
                    strain[4, col + 2] = grads[1]
                    strain[5, col] = grads[2]
                    strain[5, col + 2] = grads[0]
                stiffness += strain.T @ elastic @ strain / 8.0
    return stiffness


def mode_weights():
    modes = [(i, j, k) for k in (0, 1) for j in (0, 1) for i in (0, 1)]
    sums = np.zeros((24, 24))
    for m, mode in enumerate(modes):
        for n, corner in enumerate(OFFSETS):
            sign = np.prod([(1 if corner[d] else -1) if mode[d] else 1 for d in range(3)])
            for comp in range(3):
                sums[3 * m + comp, 3 * n + comp] = sign
    form = sums @ element_matrix() @ sums.T / 64.0

    def at(first, second):
        return form[3 * modes.index(first[1]) + first[0], 3 * modes.index(second[1]) + second[0]]

    ux, vy, uy = (0, (1, 0, 0)), (1, (0, 1, 0)), (0, (0, 1, 0))
    uxy, wyz = (0, (1, 1, 0)), (2, (0, 1, 1))
    wxy, vxz, uxyz = (2, (1, 1, 0)), (1, (1, 0, 1)), (0, (1, 1, 1))
    return dict(
        normal=at(ux, ux) - at(ux, vy),
        trace=at(ux, vy),
        shear=at(uy, uy),
        plus=(at(uxy, uxy) + at(uxy, wyz)) / 2,
        minus=(at(uxy, uxy) - at(uxy, wyz)) / 2,
        twist=at(wxy, wxy) - at(wxy, vxz),
        twist_sum=at(wxy, vxz),
        corner=at(uxyz, uxyz),
    )


def square(value):
    return value * value


def quadratic(low, high, weights):
    x = [low[c][1] + high[c][1] for c in range(3)]
    y = [low[c][2] + high[c][2] for c in range(3)]
    z = [high[c][0] - low[c][0] for c in range(3)]
    xy = [low[c][3] + high[c][3] for c in range(3)]
    xz = [high[c][1] - low[c][1] for c in range(3)]
    yz = [high[c][2] - low[c][2] for c in range(3)]
    xyz = [high[c][3] - low[c][3] for c in range(3)]
    normal = square(x[0]) + square(y[1]) + square(z[2])
    trace = square(x[0] + y[1] + z[2])
    shear = square(y[0] + x[1]) + square(z[0] + x[2]) + square(z[1] + y[2])
    pairs = ((xy[0], yz[2]), (xy[1], xz[2]), (xz[0], yz[1]))
    plus = sum(square(p + q) for p, q in pairs)
    minus = sum(square(p - q) for p, q in pairs)
    twist = square(xy[2]) + square(xz[1]) + square(yz[0])
    twist_sum = square(xy[2] + xz[1] + yz[0])
    corner = square(xyz[0]) + square(xyz[1]) + square(xyz[2])
    groups = dict(
        normal=normal, trace=trace, shear=shear, plus=plus, minus=minus, twist=twist, twist_sum=twist_sum, corner=corner
    )
    return sum(np.float32(weights[name]) * group for name, group in groups.items())


def line_weight(coord, count):
    def outside(distance):
        missing = jnp.maximum(REACH - distance, 0)
        return missing * (missing + 1) // 2

    whole = (REACH + 1) * (REACH + 1)
    return (whole - outside(coord) - outside(count - 1 - coord)).astype(jnp.float32)


def voxel_factor(density, solid, plane, first_row, total_z, total_y):
    rows, length = density.shape
    row = lax.broadcasted_iota(jnp.int32, (rows, length), 0) + first_row
    column = lax.broadcasted_iota(jnp.int32, (rows, length), 1)
    weight = line_weight(row, total_y) * line_weight(column, length)
    weight = weight * line_weight(jnp.full((rows, length), plane, jnp.int32), total_z)
    return solid.astype(jnp.float32) * (-3.0 * density * density) / weight


def spread_x(value):
    rows, length = value.shape
    wide = jnp.concatenate([value, jnp.zeros((rows, LANES), jnp.float32)], axis=1)
    span = length + LANES
    wide = wide + pltpu.roll(wide, span - 1, 1)
    wide = wide + pltpu.roll(wide, span - 2, 1)
    wide = wide + pltpu.roll(wide, 1, 1)
    wide = wide + pltpu.roll(wide, 2, 1)
    return wide[:, :length]


def spread_layers(layers):
    for step in (1, 2, 1, 2):
        layers = [layers[k] + layers[k + step] for k in range(len(layers) - step)]
    return layers


def held(disp, fixed, case, comp, z, rows):
    return disp[case, comp, z, rows] * (1.0 - fixed[z, rows].astype(jnp.float32))


def split_x(value):
    length = value.shape[1]
    column = lax.broadcasted_iota(jnp.int32, value.shape, 1)
    ahead = jnp.where(column == length - 1, 0.0, pltpu.roll(value, length - 1, 1))
    return value + ahead, ahead - value


def spread_y(quotient, ylen):
    rows = [quotient[TILE + step : TILE + step + ylen] for step in range(-REACH, REACH + 1)]
    return sum((ROWS - abs(k - REACH)) * rows[k] for k in range(2 * REACH + 1))


def to_neighbours(quotient, ylen):
    top = quotient[ylen : ylen + TILE]
    base = quotient[TILE : 2 * TILE]
    ahead, back = [], []
    for row in range(REACH):
        ahead.append(sum(float(REACH - row - k) * top[TILE - 1 - k : TILE - k] for k in range(REACH - row)))
        back.append(sum(float(row + 1 - k) * base[k : k + 1] for k in range(row + 1)))
    return ahead, back


def on_first():
    return lax.axis_index("load") == 0


def lead_kernel(totals, disp_hbm, fixed_hbm, density_hbm, solid_hbm, disp, fixed, density, solid, z_out, y_out, sems):
    loads, comps, zlen, ylen, _ = disp.shape
    copies = [
        pltpu.make_async_copy(source, target, sems.at[k])
        for k, (source, target) in enumerate(
            ((disp_hbm, disp), (fixed_hbm, fixed), (density_hbm, density), (solid_hbm, solid))
        )
    ]
    for copy in copies:
        copy.start()
    for copy in copies:
        copy.wait()
    gives = jnp.where(on_first(), 0, zlen - 1)
    plane = lax.axis_index("sz") * zlen + gives
    base_y = lax.axis_index("sy") * ylen
    z_out[loads * comps] = voxel_factor(density[gives], solid[gives], plane, base_y, *totals)
    for case in range(loads):
        for comp in range(comps):
            z_out[case * comps + comp] = held(disp, fixed, case, comp, gives, slice(None))
            for z in range(zlen):
                at = (comp * loads + case) * zlen + z
                y_out[at : at + 1] = held(disp, fixed, case, comp, z, slice(0, 1))


def tile_energies(plus, diff, first, lanes, layers, loads, comps, base=0):
    weights = mode_weights()

    def faces(k, z):
        near, far = slice(first, first + TILE), slice(first + 1, first + TILE + 1)
        whole, whole_next = plus[k, z, near, lanes], plus[k, z, far, lanes]
        change, change_next = diff[k, z, near, lanes], diff[k, z, far, lanes]
        return whole + whole_next, change + change_next, whole_next - whole, change_next - change

    energy = [None] * layers
    for case in range(loads):
        low = None
        for z in range(layers + 1):
            high = [faces(case * comps + comp, base + z) for comp in range(comps)]
            if low is not None:
                part = quadratic(low, high, weights)
                energy[z - 1] = part if energy[z - 1] is None else energy[z - 1] + part
            low = high
    return energy


def blank_last(value, first, ylen):
    row = lax.broadcasted_iota(jnp.int32, value.shape, 0) + first
    return jnp.where(row == ylen - 1, 0.0, value)


def inner_kernel(totals, disp, fixed, density, solid, own, line, sends, last_plus, last_diff, last_factor, edge, plus, diff, quotient):
    loads, comps, zlen, ylen, xlen = disp.shape
    total_z, total_y = totals
    base_z = lax.axis_index("sz") * zlen
    base_y = lax.axis_index("sy") * ylen
    inner = zlen - 1
    keeps = jnp.where(on_first(), inner, 0)

    @pl.loop(0, loads * comps)
    def _(k):
        case, comp = k // comps, k % comps
        for z in range(zlen):
            whole, change = split_x(held(disp, fixed, case, comp, z, slice(None)))
            plus[k, z, :ylen] = whole
            diff[k, z, :ylen] = change
        last_plus[k] = plus[k, keeps, :ylen]
        last_diff[k] = diff[k, keeps, :ylen]

    for comp in range(comps):
        for case in range(loads):
            for z in range(zlen):
                at = (comp * loads + case) * zlen + z
                line[0, at : at + 1] = plus[case * comps + comp, z, ylen - 1 : ylen]
                line[1, at : at + 1] = diff[case * comps + comp, z, ylen - 1 : ylen]

    zeros = jnp.zeros((TILE, xlen), jnp.float32)
    edge[...] = jnp.zeros(edge.shape, jnp.float32)
    for z in range(zlen):
        factor = voxel_factor(density[z], solid[z], base_z + z, base_y, total_z, total_y)
        edge[z : z + 1] = factor[ylen - 1 :]
        if z == inner:
            last_factor[...] = factor
        else:
            quotient[z, :TILE] = zeros
            quotient[z, TILE : TILE + ylen] = factor
            quotient[z, TILE + ylen :] = zeros

    for first in range(0, ylen, TILE):

        @pl.loop(0, xlen // LANES)
        def _(chunk):
            lanes = pl.ds(pl.multiple_of(chunk * LANES, LANES), LANES)
            energy = tile_energies(plus, diff, first, lanes, inner, loads, comps)
            for z in range(inner):
                here = quotient[z, first + TILE : first + 2 * TILE, lanes]
                quotient[z, first + TILE : first + 2 * TILE, lanes] = blank_last(energy[z] * here, first, ylen)

    for z in range(inner):
        own[z] = spread_x(spread_y(quotient.at[z], ylen))
        ahead, back = to_neighbours(quotient.at[z], ylen)
        ends = spread_x(jnp.concatenate(ahead + back + [zeros[:2]], axis=0))
        sends[0, REACH * z : REACH * (z + 1)] = ends[:REACH]
        sends[1, REACH * z : REACH * (z + 1)] = ends[REACH : 2 * REACH]


def outer_kernel(
    shape, z_in, y_in, disp, fixed, own_in, line, sends, last_plus, last_diff, last_factor, edge, own, known, a_out, b_out, plus, diff, quotient, factor
):
    loads, comps, zlen, ylen, xlen = shape
    planes = loads * comps
    inner = zlen - 1
    first_core, index = on_first(), lax.axis_index("sz")
    top = first_core & (index == lax.axis_size("sz") - 1)
    keeps = jnp.where(first_core, inner, 0)
    stays, comes = jnp.where(first_core, 0, 1), jnp.where(first_core, jnp.where(top, 2, 1), 0)
    for k in range(planes):
        plus[k, stays, :ylen] = last_plus[k]
        diff[k, stays, :ylen] = last_diff[k]
        whole, change = split_x(z_in[k])
        plus[k, comes, :ylen] = whole
        diff[k, comes, :ylen] = change
    below = jnp.where(index > 0, z_in[planes], 0.0)
    factor[...] = jnp.where(first_core, last_factor[...], below)

    @pl.when(top)
    def _():
        clamped = jnp.zeros((ylen + TILE, xlen), jnp.float32)
        for k in range(planes):
            for slot in (1, 3):
                plus[k, slot] = clamped
                diff[k, slot] = clamped

    zeros = jnp.zeros((TILE, xlen), jnp.float32)
    quotient[:TILE] = zeros
    quotient[TILE + ylen :] = zeros
    for first in range(0, ylen, TILE):

        @pl.loop(0, xlen // LANES)
        def _(chunk):
            lanes = pl.ds(pl.multiple_of(chunk * LANES, LANES), LANES)
            (energy,) = tile_energies(plus, diff, first, lanes, 1, loads, comps)
            here = energy * factor[first : first + TILE, lanes]
            quotient[first + TILE : first + 2 * TILE, lanes] = blank_last(here, first, ylen)

    @pl.when(top)
    def _():
        for first in range(0, ylen, TILE):

            @pl.loop(0, xlen // LANES)
            def _(chunk):
                lanes = pl.ds(pl.multiple_of(chunk * LANES, LANES), LANES)
                (energy,) = tile_energies(plus, diff, first, lanes, 1, loads, comps, base=2)
                here = energy * factor[first : first + TILE, lanes]
                quotient[first + TILE : first + 2 * TILE, lanes] += blank_last(here, first, ylen)

    count = loads * zlen
    more = lax.axis_index("sy") < lax.axis_size("sy") - 1
    low, high = [], []
    for comp in range(comps):
        part = slice(comp * count, (comp + 1) * count)
        whole, change = line[0, part], line[1, part]
        whole_next, change_next = split_x(jnp.where(more, y_in[part], 0.0))
        face = (whole + whole_next, change + change_next, whole_next - whole, change_next - change)
        low.append(face)
        high.append([pltpu.roll(value, count - 1, 0) for value in face])
    energy = quadratic(low, high, mode_weights())
    energy = sum(energy[case * zlen : case * zlen + inner] for case in range(loads)) * edge[:inner]
    last = spread_x(jnp.concatenate([energy, jnp.zeros((TILE - inner, xlen), jnp.float32)], axis=0))

    row = lax.broadcasted_iota(jnp.int32, (TILE, xlen), 0)
    rising = jnp.maximum(row - (TILE - 1 - ROWS), 0).astype(jnp.float32)
    ups, downs = [], []
    for z in range(inner):
        own[z] = own_in[z]
        own[z, ylen - TILE :] += rising * last[z : z + 1]
        here = sends[0, REACH * z : REACH * (z + 1)]
        ups += [here[r : r + 1] + float(REACH - r) * last[z : z + 1] for r in range(REACH)]
        downs.append(sends[1, REACH * z : REACH * (z + 1)])
    own[inner] = spread_x(spread_y(quotient, ylen))
    ahead, back = to_neighbours(quotient, ylen)
    ends = spread_x(jnp.concatenate(ahead + back + [zeros[:2]], axis=0))
    ups += [ends[: REACH - 1], factor[ylen - 1 :]]
    downs.append(ends[REACH : 2 * REACH])

    pairs = [(case, comp) for comp in range(comps) for case in range(loads)]
    here_last = [held(disp, fixed, case, comp, keeps, slice(ylen - 1, ylen)) for case, comp in pairs]
    here_first = [held(disp, fixed, case, comp, keeps, slice(0, 1)) for case, comp in pairs]
    next_row = [jnp.where(first_core, y_in[k * zlen + inner : (k + 1) * zlen], y_in[k * zlen : k * zlen + 1]) for k in range(planes)]
    next_row = [jnp.where(more, row, 0.0) for row in next_row]
    come_last = [z_in[case * comps + comp, ylen - 1 : ylen] for case, comp in pairs]
    come_first = [z_in[case * comps + comp, 0:1] for case, comp in pairs]
    rows = here_last + come_last + next_row + here_first + come_first + [factor[ylen - 1 :]]
    known[: len(rows)] = jnp.concatenate(rows, axis=0)
    known[len(rows) :] = jnp.zeros((known.shape[0] - len(rows), xlen), jnp.float32)
    up = jnp.concatenate(ups + here_last + come_last, axis=0)
    down = jnp.concatenate(downs + come_first + [jnp.zeros((planes, xlen), jnp.float32)], axis=0)
    even = lax.axis_index("sy") % 2 == 0
    a_out[...] = jnp.where(even, up, down)
    b_out[...] = jnp.where(even, down, up)


def rows_kernel(loads, comps, own, known, a_in, b_in, h_out, a_out, b_out):
    zlen, ylen, xlen = own.shape
    planes = loads * comps
    index, last = lax.axis_index("sy"), lax.axis_size("sy") - 1
    even = index % 2 == 0
    from_low = jnp.where(index > 0, jnp.where(even, b_in[...], a_in[...]), 0.0)
    from_high = jnp.where(index < last, jnp.where(even, a_in[...], b_in[...]), 0.0)
    ends = REACH * zlen
    first_core = on_first()
    top = first_core & (lax.axis_index("sz") == lax.axis_size("sz") - 1)

    def nodes(first, second, comp):
        part = slice(comp * loads, (comp + 1) * loads)
        zero = jnp.zeros((loads, xlen), jnp.float32)
        (first, first_more), (second, second_more) = first, second
        pieces = [first, first_more, second, second_more]
        return split_x(jnp.concatenate([zero if piece is None else piece[part] for piece in pieces], axis=0))

    def under(stays, comes):
        return jnp.where(first_core, stays, comes), jnp.where(top, comes, 0.0)

    def over(stays, comes):
        return jnp.where(first_core, jnp.where(top, 0.0, comes), stays), None

    def face(near_own, near_in, far_own, far_in, comp):
        whole, change = nodes(near_own, near_in, comp)
        whole_next, change_next = nodes(far_own, far_in, comp)
        return whole + whole_next, change + change_next, whole_next - whole, change_next - change

    here_last, come_last, next_row, here_first, come_first = (known[planes * k : planes * (k + 1)] for k in range(5))
    low_last, low_come = from_low[ends : ends + planes], from_low[ends + planes : ends + 2 * planes]
    next_come = from_high[ends : ends + planes]
    corners = [(here_last, come_last), (low_last, low_come), (next_row, next_come), (here_first, come_first)]
    low = [face(*(under(*corner) for corner in corners), comp) for comp in range(comps)]
    high = [face(*(over(*corner) for corner in corners), comp) for comp in range(comps)]
    energy = quadratic(low, high, mode_weights())
    cases = 2 * loads
    lines = [sum(energy[cases * k + case : cases * k + case + 1] for case in range(cases)) for k in range(2)]
    lines = [lines[0] * known[5 * planes : 5 * planes + 1], lines[1] * from_low[ends - 1 : ends]]
    lines = spread_x(jnp.concatenate(lines + [jnp.zeros((TILE - 2, xlen), jnp.float32)], axis=0))

    row = lax.broadcasted_iota(jnp.int32, (TILE, xlen), 0)
    rising = jnp.maximum(row - (TILE - 1 - ROWS), 0).astype(jnp.float32)
    falling = jnp.maximum(REACH - row, 0).astype(jnp.float32)
    blank = jnp.zeros((TILE - REACH, xlen), jnp.float32)
    between = jnp.where(first_core, zlen, 0)
    h_out[zlen - between] = jnp.zeros((ylen, xlen), jnp.float32)
    for z in range(zlen):
        part = slice(REACH * z, REACH * (z + 1))
        head = jnp.concatenate([from_low[part], blank], axis=0)
        tail = jnp.concatenate([blank, from_high[part]], axis=0)
        at = z + 1
        if z == zlen - 1:
            head = jnp.where(row == REACH - 1, 0.0, head) + falling * lines[1:2]
            tail = tail + rising * lines[0:1]
            at = between
        h_out[at] = own[z]
        h_out[at, :TILE] += head
        h_out[at, ylen - TILE :] += tail
    high = (lax.axis_index("sz") % 2 == 0).astype(jnp.int32)
    a_out[...] = h_out[pl.ds(high, zlen)]
    b_out[...] = h_out[pl.ds(1 - high, zlen)]


def layers_kernel(h, a_in, b_in, out):
    zlen = out.shape[0]
    index, last = lax.axis_index("sz"), lax.axis_size("sz") - 1
    even = index % 2 == 0
    below = [jnp.where(index > 0, jnp.where(even, b_in[k], a_in[k]), 0.0) for k in range(zlen - REACH, zlen)]
    above = [jnp.where(index < last, jnp.where(even, a_in[k], b_in[k]), 0.0) for k in range(zlen)]
    layers = below[:-1] + [below[-1] + h[0]] + [h[z] for z in range(1, zlen)] + [h[zlen] + above[0]] + above[1:]
    for z, layer in enumerate(spread_layers(layers)):
        out[z] = layer


def sum_kernel(parts, out):
    out[...] = parts[0] + parts[1]


def call(kernel, outs, args, scratch=(), space=pltpu.VMEM):
    shapes = [jax.ShapeDtypeStruct(out, jnp.float32) if isinstance(out, tuple) else out for out in outs]
    return pl.pallas_call(
        kernel,
        out_shape=shapes,
        in_specs=[pl.BlockSpec(memory_space=space)] * len(args),
        out_specs=[pl.BlockSpec(memory_space=pltpu.VMEM)] * len(outs),
        scratch_shapes=list(scratch),
        compiler_params=pltpu.CompilerParams(vmem_limit_bytes=32 * 1024 * 1024),
    )(*args)


def column_moved(value):
    size = lax.axis_size("sz")
    ring = list(range(size - 1, -1, -1)) + [size + k for k in range(size)]
    return lax.ppermute(value, ("load", "sz"), [(ring[k - 1], ring[k]) for k in range(len(ring))])


def ring_moved(value, axis):
    size = lax.axis_size(axis)
    return lax.ppermute(value, axis, [((k + 1) % size, k) for k in range(size)])


def swapped(value, axis, first):
    cores, size = lax.axis_size("load"), lax.axis_size(axis)
    pairs = []
    for core in range(cores):
        for k in range(size):
            other = k + 1 if (k - first) % 2 == 0 else k - 1
            target = core * size + other if 0 <= other < size else (cores - 1 - core) * size + k
            pairs.append((core * size + k, target))
    return lax.ppermute(value, ("load", axis), pairs)


def body(displacements, density, solid, fixed):
    loads, comps, zlen, ylen, xlen = displacements.shape
    planes = loads * comps
    totals = (zlen * lax.axis_size("sz"), ylen * lax.axis_size("sy"))
    args = [
        pltpu.with_memory_space_constraint(arg, pltpu.HBM) for arg in (displacements, fixed, density, solid)
    ]

    disp, fixed, density, solid, z_send, y_send = call(
        lambda *refs: lead_kernel(totals, *refs),
        [jax.ShapeDtypeStruct(arg.shape, arg.dtype) for arg in args]
        + [(planes + 1, ylen, xlen), (planes * zlen, xlen)],
        args,
        scratch=[pltpu.SemaphoreType.DMA((len(args),))],
        space=pltpu.HBM,
    )
    z_in = column_moved(z_send)
    y_in = ring_moved(y_send, "sy")
    nodes = lambda layers: pltpu.VMEM((planes, layers, ylen + TILE, xlen), jnp.float32)
    inner = call(
        lambda *refs: inner_kernel(totals, *refs),
        [
            (zlen, ylen, xlen),
            (2, planes * zlen, xlen),
            (2, REACH * (zlen - 1), xlen),
            (planes, ylen, xlen),
            (planes, ylen, xlen),
            (ylen, xlen),
            (TILE, xlen),
        ],
        (disp, fixed, density, solid),
        scratch=[nodes(zlen), nodes(zlen), pltpu.VMEM((zlen - 1, ylen + 2 * TILE, xlen), jnp.float32)],
    )
    size = REACH * zlen + 2 * planes
    own, known, a_send, b_send = call(
        lambda *refs: outer_kernel(displacements.shape, *refs),
        [(zlen, ylen, xlen), (-(-(5 * planes + 1) // TILE) * TILE, xlen), (size, xlen), (size, xlen)],
        (z_in, y_in, disp, fixed, *inner),
        scratch=[
            nodes(4),
            nodes(4),
            pltpu.VMEM((ylen + 2 * TILE, xlen), jnp.float32),
            pltpu.VMEM((ylen, xlen), jnp.float32),
        ],
    )
    a_in = swapped(a_send, "sy", 0)
    b_in = swapped(b_send, "sy", 1)
    h, a_send, b_send = call(
        lambda *refs: rows_kernel(loads, comps, *refs),
        [(zlen + 1, ylen, xlen), (zlen, ylen, xlen), (zlen, ylen, xlen)],
        (own, known, a_in, b_in),
    )
    a_in = swapped(a_send, "sz", 0)
    b_in = swapped(b_send, "sz", 1)
    (part,) = call(layers_kernel, [(zlen, ylen, xlen)], (h, a_in, b_in))
    parts = lax.all_gather(part, "load", axis=0)
    (out,) = call(sum_kernel, [(zlen, ylen, xlen)], (parts,))
    return out


def solution(mesh):
    return jax.shard_map(
        body,
        mesh=mesh,
        in_specs=(
            P("load", None, "sz", "sy", None),
            P("sz", "sy", None),
            P("sz", "sy", None),
            P("sz", "sy", None),
        ),
        out_specs=P("sz", "sy", None),
        check_vma=False,
    )
```

```python
import jax
import jax.numpy as jnp
import numpy as np
from jax import lax
from jax.experimental import pallas as pl
from jax.experimental.pallas import tpu as pltpu
from jax.sharding import PartitionSpec as P

OFFSETS = [(0, 0, 0), (1, 0, 0), (1, 1, 0), (0, 1, 0), (0, 0, 1), (1, 0, 1), (1, 1, 1), (0, 1, 1)]
REACH = 3
ROWS = REACH + 1
TILE = 8
LANES = 128


def element_matrix():
    corners = np.array(
        [
            [-1.0, -1.0, -1.0],
            [1.0, -1.0, -1.0],
            [1.0, 1.0, -1.0],
            [-1.0, 1.0, -1.0],
            [-1.0, -1.0, 1.0],
            [1.0, -1.0, 1.0],
            [1.0, 1.0, 1.0],
            [-1.0, 1.0, 1.0],
        ]
    )
    poisson = 0.3
    lame = poisson / ((1.0 + poisson) * (1.0 - 2.0 * poisson))
    shear = 1.0 / (2.0 * (1.0 + poisson))
    elastic = np.zeros((6, 6))
    elastic[:3, :3] = lame
    for k in range(3):
        elastic[k, k] += 2.0 * shear
        elastic[3 + k, 3 + k] = shear
    gauss = 1.0 / np.sqrt(3.0)
    stiffness = np.zeros((24, 24))
    for gi in range(2):
        for gj in range(2):
            for gk in range(2):
                point = np.array([(2 * gi - 1) * gauss, (2 * gj - 1) * gauss, (2 * gk - 1) * gauss])
                strain = np.zeros((6, 24))
                for node in range(8):
                    grads = np.zeros(3)
                    for k in range(3):
                        value = corners[node, k] / 8.0
                        for m in range(3):
                            if m != k:
                                value = value * (1.0 + point[m] * corners[node, m])
                        grads[k] = 2.0 * value
                    col = 3 * node
                    strain[0, col] = grads[0]
                    strain[1, col + 1] = grads[1]
                    strain[2, col + 2] = grads[2]
                    strain[3, col] = grads[1]
                    strain[3, col + 1] = grads[0]
                    strain[4, col + 1] = grads[2]
                    strain[4, col + 2] = grads[1]
                    strain[5, col] = grads[2]
                    strain[5, col + 2] = grads[0]
                stiffness += strain.T @ elastic @ strain / 8.0
    return stiffness


def mode_weights():
    modes = [(i, j, k) for k in (0, 1) for j in (0, 1) for i in (0, 1)]
    sums = np.zeros((24, 24))
    for m, mode in enumerate(modes):
        for n, corner in enumerate(OFFSETS):
            sign = np.prod([(1 if corner[d] else -1) if mode[d] else 1 for d in range(3)])
            for comp in range(3):
                sums[3 * m + comp, 3 * n + comp] = sign
    form = sums @ element_matrix() @ sums.T / 64.0

    def at(first, second):
        return form[3 * modes.index(first[1]) + first[0], 3 * modes.index(second[1]) + second[0]]

    ux, vy, uy = (0, (1, 0, 0)), (1, (0, 1, 0)), (0, (0, 1, 0))
    uxy, wyz = (0, (1, 1, 0)), (2, (0, 1, 1))
    wxy, vxz, uxyz = (2, (1, 1, 0)), (1, (1, 0, 1)), (0, (1, 1, 1))
    return dict(
        normal=at(ux, ux) - at(ux, vy),
        trace=at(ux, vy),
        shear=at(uy, uy),
        plus=(at(uxy, uxy) + at(uxy, wyz)) / 2,
        minus=(at(uxy, uxy) - at(uxy, wyz)) / 2,
        twist=at(wxy, wxy) - at(wxy, vxz),
        twist_sum=at(wxy, vxz),
        corner=at(uxyz, uxyz),
    )


def square(value):
    return value * value


def quadratic(low, high, weights):
    x = [low[c][1] + high[c][1] for c in range(3)]
    y = [low[c][2] + high[c][2] for c in range(3)]
    z = [high[c][0] - low[c][0] for c in range(3)]
    xy = [low[c][3] + high[c][3] for c in range(3)]
    xz = [high[c][1] - low[c][1] for c in range(3)]
    yz = [high[c][2] - low[c][2] for c in range(3)]
    xyz = [high[c][3] - low[c][3] for c in range(3)]
    normal = square(x[0]) + square(y[1]) + square(z[2])
    trace = square(x[0] + y[1] + z[2])
    shear = square(y[0] + x[1]) + square(z[0] + x[2]) + square(z[1] + y[2])
    pairs = ((xy[0], yz[2]), (xy[1], xz[2]), (xz[0], yz[1]))
    plus = sum(square(p + q) for p, q in pairs)
    minus = sum(square(p - q) for p, q in pairs)
    twist = square(xy[2]) + square(xz[1]) + square(yz[0])
    twist_sum = square(xy[2] + xz[1] + yz[0])
    corner = square(xyz[0]) + square(xyz[1]) + square(xyz[2])
    groups = dict(
        normal=normal, trace=trace, shear=shear, plus=plus, minus=minus, twist=twist, twist_sum=twist_sum, corner=corner
    )
    return sum(np.float32(weights[name]) * group for name, group in groups.items())


def line_weight(coord, count):
    def outside(distance):
        missing = jnp.maximum(REACH - distance, 0)
        return missing * (missing + 1) // 2

    whole = (REACH + 1) * (REACH + 1)
    return (whole - outside(coord) - outside(count - 1 - coord)).astype(jnp.float32)


def voxel_factor(density, solid, plane, first_row, total_z, total_y):
    rows, length = density.shape
    row = lax.broadcasted_iota(jnp.int32, (rows, length), 0) + first_row
    column = lax.broadcasted_iota(jnp.int32, (rows, length), 1)
    weight = line_weight(row, total_y) * line_weight(column, length)
    weight = weight * line_weight(jnp.full((rows, length), plane, jnp.int32), total_z)
    return solid.astype(jnp.float32) * (-3.0 * density * density) / weight


def spread_x(value):
    rows, length = value.shape
    wide = jnp.concatenate([value, jnp.zeros((rows, LANES), jnp.float32)], axis=1)
    span = length + LANES
    wide = wide + pltpu.roll(wide, span - 1, 1)
    wide = wide + pltpu.roll(wide, span - 2, 1)
    wide = wide + pltpu.roll(wide, 1, 1)
    wide = wide + pltpu.roll(wide, 2, 1)
    return wide[:, :length]


def spread_layers(layers):
    for step in (1, 2, 1, 2):
        layers = [layers[k] + layers[k + step] for k in range(len(layers) - step)]
    return layers


def held(disp, fixed, case, comp, z, rows):
    return disp[case, comp, z, rows] * (1.0 - fixed[z, rows].astype(jnp.float32))


def split_x(value):
    length = value.shape[1]
    column = lax.broadcasted_iota(jnp.int32, value.shape, 1)
    ahead = jnp.where(column == length - 1, 0.0, pltpu.roll(value, length - 1, 1))
    return value + ahead, ahead - value


def spread_y(quotient, ylen):
    rows = [quotient[TILE + step : TILE + step + ylen] for step in range(-REACH, REACH + 1)]
    return sum((ROWS - abs(k - REACH)) * rows[k] for k in range(2 * REACH + 1))


def to_neighbours(quotient, ylen):
    top = quotient[ylen : ylen + TILE]
    base = quotient[TILE : 2 * TILE]
    ahead, back = [], []
    for row in range(REACH):
        ahead.append(sum(float(REACH - row - k) * top[TILE - 1 - k : TILE - k] for k in range(REACH - row)))
        back.append(sum(float(row + 1 - k) * base[k : k + 1] for k in range(row + 1)))
    return ahead, back


def on_first():
    return lax.axis_index("load") == 0


def lead_kernel(totals, disp_hbm, fixed_hbm, density_hbm, solid_hbm, disp, fixed, density, solid, z_out, y_out, sems):
    loads, comps, zlen, ylen, _ = disp.shape
    copies = [
        pltpu.make_async_copy(source, target, sems.at[k])
        for k, (source, target) in enumerate(
            ((disp_hbm, disp), (fixed_hbm, fixed), (density_hbm, density), (solid_hbm, solid))
        )
    ]
    for copy in copies:
        copy.start()
    for copy in copies:
        copy.wait()
    gives = jnp.where(on_first(), 0, zlen - 1)
    plane = lax.axis_index("sz") * zlen + gives
    base_y = lax.axis_index("sy") * ylen
    z_out[loads * comps] = voxel_factor(density[gives], solid[gives], plane, base_y, *totals)
    for case in range(loads):
        for comp in range(comps):
            z_out[case * comps + comp] = held(disp, fixed, case, comp, gives, slice(None))
            for z in range(zlen):
                at = (comp * loads + case) * zlen + z
                y_out[at : at + 1] = held(disp, fixed, case, comp, z, slice(0, 1))


def tile_energies(plus, diff, first, lanes, layers, loads, comps, base=0):
    weights = mode_weights()

    def faces(k, z):
        near, far = slice(first, first + TILE), slice(first + 1, first + TILE + 1)
        whole, whole_next = plus[k, z, near, lanes], plus[k, z, far, lanes]
        change, change_next = diff[k, z, near, lanes], diff[k, z, far, lanes]
        return whole + whole_next, change + change_next, whole_next - whole, change_next - change

    energy = [None] * layers
    for case in range(loads):
        low = None
        for z in range(layers + 1):
            high = [faces(case * comps + comp, base + z) for comp in range(comps)]
            if low is not None:
                part = quadratic(low, high, weights)
                energy[z - 1] = part if energy[z - 1] is None else energy[z - 1] + part
            low = high
    return energy


def blank_last(value, first, ylen):
    row = lax.broadcasted_iota(jnp.int32, value.shape, 0) + first
    return jnp.where(row == ylen - 1, 0.0, value)


def inner_kernel(totals, disp, fixed, density, solid, own, line, sends, last_plus, last_diff, last_factor, edge, plus, diff, quotient):
    loads, comps, zlen, ylen, xlen = disp.shape
    total_z, total_y = totals
    base_z = lax.axis_index("sz") * zlen
    base_y = lax.axis_index("sy") * ylen
    inner = zlen - 1
    keeps = jnp.where(on_first(), inner, 0)

    @pl.loop(0, loads * comps)
    def _(k):
        case, comp = k // comps, k % comps
        for z in range(zlen):
            whole, change = split_x(held(disp, fixed, case, comp, z, slice(None)))
            plus[k, z, :ylen] = whole
            diff[k, z, :ylen] = change
        last_plus[k] = plus[k, keeps, :ylen]
        last_diff[k] = diff[k, keeps, :ylen]

    for comp in range(comps):
        for case in range(loads):
            for z in range(zlen):
                at = (comp * loads + case) * zlen + z
                line[0, at : at + 1] = plus[case * comps + comp, z, ylen - 1 : ylen]
                line[1, at : at + 1] = diff[case * comps + comp, z, ylen - 1 : ylen]

    zeros = jnp.zeros((TILE, xlen), jnp.float32)
    edge[...] = jnp.zeros(edge.shape, jnp.float32)
    for z in range(zlen):
        factor = voxel_factor(density[z], solid[z], base_z + z, base_y, total_z, total_y)
        edge[z : z + 1] = factor[ylen - 1 :]
        if z == inner:
            last_factor[...] = factor
        else:
            quotient[z, :TILE] = zeros
            quotient[z, TILE : TILE + ylen] = factor
            quotient[z, TILE + ylen :] = zeros

    for first in range(0, ylen, TILE):

        @pl.loop(0, xlen // LANES)
        def _(chunk):
            lanes = pl.ds(pl.multiple_of(chunk * LANES, LANES), LANES)
            energy = tile_energies(plus, diff, first, lanes, inner, loads, comps)
            for z in range(inner):
                here = quotient[z, first + TILE : first + 2 * TILE, lanes]
                quotient[z, first + TILE : first + 2 * TILE, lanes] = blank_last(energy[z] * here, first, ylen)

    for z in range(inner):
        own[z] = spread_x(spread_y(quotient.at[z], ylen))
        ahead, back = to_neighbours(quotient.at[z], ylen)
        ends = spread_x(jnp.concatenate(ahead + back + [zeros[:2]], axis=0))
        sends[0, REACH * z : REACH * (z + 1)] = ends[:REACH]
        sends[1, REACH * z : REACH * (z + 1)] = ends[REACH : 2 * REACH]


def outer_kernel(
    shape, z_in, y_in, disp, fixed, own_in, line, sends, last_plus, last_diff, last_factor, edge, own, known, a_out, b_out, plus, diff, quotient, factor
):
    loads, comps, zlen, ylen, xlen = shape
    planes = loads * comps
    inner = zlen - 1
    first_core, index = on_first(), lax.axis_index("sz")
    top = first_core & (index == lax.axis_size("sz") - 1)
    keeps = jnp.where(first_core, inner, 0)
    stays, comes = jnp.where(first_core, 0, 1), jnp.where(first_core, jnp.where(top, 2, 1), 0)
    for k in range(planes):
        plus[k, stays, :ylen] = last_plus[k]
        diff[k, stays, :ylen] = last_diff[k]
        whole, change = split_x(z_in[k])
        plus[k, comes, :ylen] = whole
        diff[k, comes, :ylen] = change
    below = jnp.where(index > 0, z_in[planes], 0.0)
    factor[...] = jnp.where(first_core, last_factor[...], below)

    @pl.when(top)
    def _():
        clamped = jnp.zeros((ylen + TILE, xlen), jnp.float32)
        for k in range(planes):
            for slot in (1, 3):
                plus[k, slot] = clamped
                diff[k, slot] = clamped

    zeros = jnp.zeros((TILE, xlen), jnp.float32)
    quotient[:TILE] = zeros
    quotient[TILE + ylen :] = zeros
    for first in range(0, ylen, TILE):

        @pl.loop(0, xlen // LANES)
        def _(chunk):
            lanes = pl.ds(pl.multiple_of(chunk * LANES, LANES), LANES)
            (energy,) = tile_energies(plus, diff, first, lanes, 1, loads, comps)
            here = energy * factor[first : first + TILE, lanes]
            quotient[first + TILE : first + 2 * TILE, lanes] = blank_last(here, first, ylen)

    @pl.when(top)
    def _():
        for first in range(0, ylen, TILE):

            @pl.loop(0, xlen // LANES)
            def _(chunk):
                lanes = pl.ds(pl.multiple_of(chunk * LANES, LANES), LANES)
                (energy,) = tile_energies(plus, diff, first, lanes, 1, loads, comps, base=2)
                here = energy * factor[first : first + TILE, lanes]
                quotient[first + TILE : first + 2 * TILE, lanes] += blank_last(here, first, ylen)

    count = loads * zlen
    more = lax.axis_index("sy") < lax.axis_size("sy") - 1
    low, high = [], []
    for comp in range(comps):
        part = slice(comp * count, (comp + 1) * count)
        whole, change = line[0, part], line[1, part]
        whole_next, change_next = split_x(jnp.where(more, y_in[part], 0.0))
        face = (whole + whole_next, change + change_next, whole_next - whole, change_next - change)
        low.append(face)
        high.append([pltpu.roll(value, count - 1, 0) for value in face])
    energy = quadratic(low, high, mode_weights())
    energy = sum(energy[case * zlen : case * zlen + inner] for case in range(loads)) * edge[:inner]
    last = spread_x(jnp.concatenate([energy, jnp.zeros((TILE - inner, xlen), jnp.float32)], axis=0))

    row = lax.broadcasted_iota(jnp.int32, (TILE, xlen), 0)
    rising = jnp.maximum(row - (TILE - 1 - ROWS), 0).astype(jnp.float32)
    ups, downs = [], []
    for z in range(inner):
        own[z] = own_in[z]
        own[z, ylen - TILE :] += rising * last[z : z + 1]
        here = sends[0, REACH * z : REACH * (z + 1)]
        ups += [here[r : r + 1] + float(REACH - r) * last[z : z + 1] for r in range(REACH)]
        downs.append(sends[1, REACH * z : REACH * (z + 1)])
    own[inner] = spread_x(spread_y(quotient, ylen))
    ahead, back = to_neighbours(quotient, ylen)
    ends = spread_x(jnp.concatenate(ahead + back + [zeros[:2]], axis=0))
    ups += [ends[: REACH - 1], factor[ylen - 1 :]]
    downs.append(ends[REACH : 2 * REACH])

    pairs = [(case, comp) for comp in range(comps) for case in range(loads)]
    here_last = [held(disp, fixed, case, comp, keeps, slice(ylen - 1, ylen)) for case, comp in pairs]
    here_first = [held(disp, fixed, case, comp, keeps, slice(0, 1)) for case, comp in pairs]
    next_row = [jnp.where(first_core, y_in[k * zlen + inner : (k + 1) * zlen], y_in[k * zlen : k * zlen + 1]) for k in range(planes)]
    next_row = [jnp.where(more, row, 0.0) for row in next_row]
    come_last = [z_in[case * comps + comp, ylen - 1 : ylen] for case, comp in pairs]
    come_first = [z_in[case * comps + comp, 0:1] for case, comp in pairs]
    rows = here_last + come_last + next_row + here_first + come_first + [factor[ylen - 1 :]]
    known[: len(rows)] = jnp.concatenate(rows, axis=0)
    known[len(rows) :] = jnp.zeros((known.shape[0] - len(rows), xlen), jnp.float32)
    up = jnp.concatenate(ups + here_last + come_last, axis=0)
    down = jnp.concatenate(downs + come_first + [jnp.zeros((planes, xlen), jnp.float32)], axis=0)
    even = lax.axis_index("sy") % 2 == 0
    a_out[...] = jnp.where(even, up, down)
    b_out[...] = jnp.where(even, down, up)


def rows_kernel(loads, comps, own, known, b_in, a_in, h_out, p_out, q_out):
    zlen, ylen, xlen = own.shape
    planes = loads * comps
    index, last = lax.axis_index("sy"), lax.axis_size("sy") - 1
    even = index % 2 == 0
    from_low = jnp.where(index > 0, jnp.where(even, b_in[...], a_in[...]), 0.0)
    from_high = jnp.where(index < last, jnp.where(even, a_in[...], b_in[...]), 0.0)
    ends = REACH * zlen
    first_core = on_first()
    top = first_core & (lax.axis_index("sz") == lax.axis_size("sz") - 1)

    def nodes(first, second, comp):
        part = slice(comp * loads, (comp + 1) * loads)
        zero = jnp.zeros((loads, xlen), jnp.float32)
        (first, first_more), (second, second_more) = first, second
        pieces = [first, first_more, second, second_more]
        return split_x(jnp.concatenate([zero if piece is None else piece[part] for piece in pieces], axis=0))

    def under(stays, comes):
        return jnp.where(first_core, stays, comes), jnp.where(top, comes, 0.0)

    def over(stays, comes):
        return jnp.where(first_core, jnp.where(top, 0.0, comes), stays), None

    def face(near_own, near_in, far_own, far_in, comp):
        whole, change = nodes(near_own, near_in, comp)
        whole_next, change_next = nodes(far_own, far_in, comp)
        return whole + whole_next, change + change_next, whole_next - whole, change_next - change

    here_last, come_last, next_row, here_first, come_first = (known[planes * k : planes * (k + 1)] for k in range(5))
    low_last, low_come = from_low[ends : ends + planes], from_low[ends + planes : ends + 2 * planes]
    next_come = from_high[ends : ends + planes]
    corners = [(here_last, come_last), (low_last, low_come), (next_row, next_come), (here_first, come_first)]
    low = [face(*(under(*corner) for corner in corners), comp) for comp in range(comps)]
    high = [face(*(over(*corner) for corner in corners), comp) for comp in range(comps)]
    energy = quadratic(low, high, mode_weights())
    cases = 2 * loads
    lines = [sum(energy[cases * k + case : cases * k + case + 1] for case in range(cases)) for k in range(2)]
    lines = [lines[0] * known[5 * planes : 5 * planes + 1], lines[1] * from_low[ends - 1 : ends]]
    lines = spread_x(jnp.concatenate(lines + [jnp.zeros((TILE - 2, xlen), jnp.float32)], axis=0))

    row = lax.broadcasted_iota(jnp.int32, (TILE, xlen), 0)
    rising = jnp.maximum(row - (TILE - 1 - ROWS), 0).astype(jnp.float32)
    falling = jnp.maximum(REACH - row, 0).astype(jnp.float32)
    blank = jnp.zeros((TILE - REACH, xlen), jnp.float32)
    between = jnp.where(first_core, zlen, 0)
    h_out[zlen - between] = jnp.zeros((ylen, xlen), jnp.float32)
    for z in range(zlen):
        part = slice(REACH * z, REACH * (z + 1))
        head = jnp.concatenate([from_low[part], blank], axis=0)
        tail = jnp.concatenate([blank, from_high[part]], axis=0)
        at = z + 1
        if z == zlen - 1:
            head = jnp.where(row == REACH - 1, 0.0, head) + falling * lines[1:2]
            tail = tail + rising * lines[0:1]
            at = between
        h_out[at] = own[z]
        h_out[at, :TILE] += head
        h_out[at, ylen - TILE :] += tail
    p_out[...] = h_out[pl.ds(jnp.where(first_core, 1, zlen + 1 - REACH), REACH)]
    q_out[...] = h_out[pl.ds(jnp.where(first_core, 1, 0), zlen)]


def layers_kernel(h, p_in, q_in, out):
    zlen = out.shape[0]
    index, last = lax.axis_index("sz"), lax.axis_size("sz") - 1
    first_core = on_first()
    below = [jnp.where(first_core, q_in[zlen - REACH + k], p_in[k]) for k in range(REACH)]
    above = [jnp.where(first_core, p_in[k - 1] if k else 0.0, q_in[k]) for k in range(zlen)]
    below = [jnp.where(index > 0, layer, 0.0) for layer in below]
    above = [jnp.where(index < last, layer, 0.0) for layer in above]
    layers = below[:-1] + [below[-1] + h[0]] + [h[z] for z in range(1, zlen)] + [h[zlen] + above[0]] + above[1:]
    for z, layer in enumerate(spread_layers(layers)):
        out[z] = layer


def sum_kernel(parts, out):
    out[...] = parts[0] + parts[1]


def call(kernel, outs, args, scratch=(), space=pltpu.VMEM):
    shapes = [jax.ShapeDtypeStruct(out, jnp.float32) if isinstance(out, tuple) else out for out in outs]
    return pl.pallas_call(
        kernel,
        out_shape=shapes,
        in_specs=[pl.BlockSpec(memory_space=space)] * len(args),
        out_specs=[pl.BlockSpec(memory_space=pltpu.VMEM)] * len(outs),
        scratch_shapes=list(scratch),
        compiler_params=pltpu.CompilerParams(vmem_limit_bytes=32 * 1024 * 1024),
    )(*args)


def column_moved(value, back=False):
    size = lax.axis_size("sz")
    ring = list(range(size - 1, -1, -1)) + [size + k for k in range(size)]
    if back:
        ring.reverse()
    return lax.ppermute(value, ("load", "sz"), [(ring[k - 1], ring[k]) for k in range(len(ring))])


def ring_moved(value, axis):
    size = lax.axis_size(axis)
    return lax.ppermute(value, axis, [((k + 1) % size, k) for k in range(size)])


def swapped(value, axis, first):
    cores, size = lax.axis_size("load"), lax.axis_size(axis)
    pairs = []
    for core in range(cores):
        for k in range(size):
            other = k + 1 if (k - first) % 2 == 0 else k - 1
            target = core * size + other if 0 <= other < size else (cores - 1 - core) * size + k
            pairs.append((core * size + k, target))
    return lax.ppermute(value, ("load", axis), pairs)


def body(displacements, density, solid, fixed):
    loads, comps, zlen, ylen, xlen = displacements.shape
    planes = loads * comps
    totals = (zlen * lax.axis_size("sz"), ylen * lax.axis_size("sy"))
    args = [
        pltpu.with_memory_space_constraint(arg, pltpu.HBM) for arg in (displacements, fixed, density, solid)
    ]

    disp, fixed, density, solid, z_send, y_send = call(
        lambda *refs: lead_kernel(totals, *refs),
        [jax.ShapeDtypeStruct(arg.shape, arg.dtype) for arg in args]
        + [(planes + 1, ylen, xlen), (planes * zlen, xlen)],
        args,
        scratch=[pltpu.SemaphoreType.DMA((len(args),))],
        space=pltpu.HBM,
    )
    z_in = column_moved(z_send)
    y_in = ring_moved(y_send, "sy")
    nodes = lambda layers: pltpu.VMEM((planes, layers, ylen + TILE, xlen), jnp.float32)
    inner = call(
        lambda *refs: inner_kernel(totals, *refs),
        [
            (zlen, ylen, xlen),
            (2, planes * zlen, xlen),
            (2, REACH * (zlen - 1), xlen),
            (planes, ylen, xlen),
            (planes, ylen, xlen),
            (ylen, xlen),
            (TILE, xlen),
        ],
        (disp, fixed, density, solid),
        scratch=[nodes(zlen), nodes(zlen), pltpu.VMEM((zlen - 1, ylen + 2 * TILE, xlen), jnp.float32)],
    )
    size = REACH * zlen + 2 * planes
    own, known, a_send, b_send = call(
        lambda *refs: outer_kernel(displacements.shape, *refs),
        [(zlen, ylen, xlen), (-(-(5 * planes + 1) // TILE) * TILE, xlen), (size, xlen), (size, xlen)],
        (z_in, y_in, disp, fixed, *inner),
        scratch=[
            nodes(4),
            nodes(4),
            pltpu.VMEM((ylen + 2 * TILE, xlen), jnp.float32),
            pltpu.VMEM((ylen, xlen), jnp.float32),
        ],
    )
    b_in = swapped(b_send, "sy", 1)
    a_in = swapped(a_send, "sy", 0)
    h, p_send, q_send = call(
        lambda *refs: rows_kernel(loads, comps, *refs),
        [(zlen + 1, ylen, xlen), (REACH, ylen, xlen), (zlen, ylen, xlen)],
        (own, known, b_in, a_in),
    )
    p_in = column_moved(p_send)
    q_in = column_moved(q_send, back=True)
    (part,) = call(layers_kernel, [(zlen, ylen, xlen)], (h, p_in, q_in))
    parts = lax.all_gather(part, "load", axis=0)
    (out,) = call(sum_kernel, [(zlen, ylen, xlen)], (parts,))
    return out


def solution(mesh):
    return jax.shard_map(
        body,
        mesh=mesh,
        in_specs=(
            P("load", None, "sz", "sy", None),
            P("sz", "sy", None),
            P("sz", "sy", None),
            P("sz", "sy", None),
        ),
        out_specs=P("sz", "sy", None),
        check_vma=False,
    )
```

```python
import jax
import jax.numpy as jnp
import numpy as np
from jax import lax
from jax.experimental import pallas as pl
from jax.experimental.pallas import tpu as pltpu
from jax.sharding import PartitionSpec as P

OFFSETS = [(0, 0, 0), (1, 0, 0), (1, 1, 0), (0, 1, 0), (0, 0, 1), (1, 0, 1), (1, 1, 1), (0, 1, 1)]
REACH = 3
ROWS = REACH + 1
TILE = 8
LANES = 128


def element_matrix():
    corners = np.array(
        [
            [-1.0, -1.0, -1.0],
            [1.0, -1.0, -1.0],
            [1.0, 1.0, -1.0],
            [-1.0, 1.0, -1.0],
            [-1.0, -1.0, 1.0],
            [1.0, -1.0, 1.0],
            [1.0, 1.0, 1.0],
            [-1.0, 1.0, 1.0],
        ]
    )
    poisson = 0.3
    lame = poisson / ((1.0 + poisson) * (1.0 - 2.0 * poisson))
    shear = 1.0 / (2.0 * (1.0 + poisson))
    elastic = np.zeros((6, 6))
    elastic[:3, :3] = lame
    for k in range(3):
        elastic[k, k] += 2.0 * shear
        elastic[3 + k, 3 + k] = shear
    gauss = 1.0 / np.sqrt(3.0)
    stiffness = np.zeros((24, 24))
    for gi in range(2):
        for gj in range(2):
            for gk in range(2):
                point = np.array([(2 * gi - 1) * gauss, (2 * gj - 1) * gauss, (2 * gk - 1) * gauss])
                strain = np.zeros((6, 24))
                for node in range(8):
                    grads = np.zeros(3)
                    for k in range(3):
                        value = corners[node, k] / 8.0
                        for m in range(3):
                            if m != k:
                                value = value * (1.0 + point[m] * corners[node, m])
                        grads[k] = 2.0 * value
                    col = 3 * node
                    strain[0, col] = grads[0]
                    strain[1, col + 1] = grads[1]
                    strain[2, col + 2] = grads[2]
                    strain[3, col] = grads[1]
                    strain[3, col + 1] = grads[0]
                    strain[4, col + 1] = grads[2]
                    strain[4, col + 2] = grads[1]
                    strain[5, col] = grads[2]
                    strain[5, col + 2] = grads[0]
                stiffness += strain.T @ elastic @ strain / 8.0
    return stiffness


def mode_weights():
    modes = [(i, j, k) for k in (0, 1) for j in (0, 1) for i in (0, 1)]
    sums = np.zeros((24, 24))
    for m, mode in enumerate(modes):
        for n, corner in enumerate(OFFSETS):
            sign = np.prod([(1 if corner[d] else -1) if mode[d] else 1 for d in range(3)])
            for comp in range(3):
                sums[3 * m + comp, 3 * n + comp] = sign
    form = sums @ element_matrix() @ sums.T / 64.0

    def at(first, second):
        return form[3 * modes.index(first[1]) + first[0], 3 * modes.index(second[1]) + second[0]]

    ux, vy, uy = (0, (1, 0, 0)), (1, (0, 1, 0)), (0, (0, 1, 0))
    uxy, wyz = (0, (1, 1, 0)), (2, (0, 1, 1))
    wxy, vxz, uxyz = (2, (1, 1, 0)), (1, (1, 0, 1)), (0, (1, 1, 1))
    return dict(
        normal=at(ux, ux) - at(ux, vy),
        trace=at(ux, vy),
        shear=at(uy, uy),
        plus=(at(uxy, uxy) + at(uxy, wyz)) / 2,
        minus=(at(uxy, uxy) - at(uxy, wyz)) / 2,
        twist=at(wxy, wxy) - at(wxy, vxz),
        twist_sum=at(wxy, vxz),
        corner=at(uxyz, uxyz),
    )


def square(value):
    return value * value


def quadratic(low, high, weights):
    x = [low[c][1] + high[c][1] for c in range(3)]
    y = [low[c][2] + high[c][2] for c in range(3)]
    z = [high[c][0] - low[c][0] for c in range(3)]
    xy = [low[c][3] + high[c][3] for c in range(3)]
    xz = [high[c][1] - low[c][1] for c in range(3)]
    yz = [high[c][2] - low[c][2] for c in range(3)]
    xyz = [high[c][3] - low[c][3] for c in range(3)]
    normal = square(x[0]) + square(y[1]) + square(z[2])
    trace = square(x[0] + y[1] + z[2])
    shear = square(y[0] + x[1]) + square(z[0] + x[2]) + square(z[1] + y[2])
    pairs = ((xy[0], yz[2]), (xy[1], xz[2]), (xz[0], yz[1]))
    plus = sum(square(p + q) for p, q in pairs)
    minus = sum(square(p - q) for p, q in pairs)
    twist = square(xy[2]) + square(xz[1]) + square(yz[0])
    twist_sum = square(xy[2] + xz[1] + yz[0])
    corner = square(xyz[0]) + square(xyz[1]) + square(xyz[2])
    groups = dict(
        normal=normal, trace=trace, shear=shear, plus=plus, minus=minus, twist=twist, twist_sum=twist_sum, corner=corner
    )
    return sum(np.float32(weights[name]) * group for name, group in groups.items())


def line_weight(coord, count):
    def outside(distance):
        missing = jnp.maximum(REACH - distance, 0)
        return missing * (missing + 1) // 2

    whole = (REACH + 1) * (REACH + 1)
    return (whole - outside(coord) - outside(count - 1 - coord)).astype(jnp.float32)


def voxel_factor(density, solid, plane, first_row, total_z, total_y):
    rows, length = density.shape
    row = lax.broadcasted_iota(jnp.int32, (rows, length), 0) + first_row
    column = lax.broadcasted_iota(jnp.int32, (rows, length), 1)
    weight = line_weight(row, total_y) * line_weight(column, length)
    weight = weight * line_weight(jnp.full((rows, length), plane, jnp.int32), total_z)
    return solid.astype(jnp.float32) * (-3.0 * density * density) / weight


def spread_x(value):
    rows, length = value.shape
    wide = jnp.concatenate([value, jnp.zeros((rows, LANES), jnp.float32)], axis=1)
    span = length + LANES
    total = float(ROWS) * value
    for step in range(1, ROWS):
        both = pltpu.roll(wide, span - step, 1) + pltpu.roll(wide, step, 1)
        total = total + float(ROWS - step) * both[:, :length]
    return total


def spread_layers(layers):
    for step in (1, 2, 1, 2):
        layers = [layers[k] + layers[k + step] for k in range(len(layers) - step)]
    return layers


def held(disp, fixed, case, comp, z, rows):
    return disp[case, comp, z, rows] * (1.0 - fixed[z, rows].astype(jnp.float32))


def split_x(value):
    length = value.shape[1]
    column = lax.broadcasted_iota(jnp.int32, value.shape, 1)
    ahead = jnp.where(column == length - 1, 0.0, pltpu.roll(value, length - 1, 1))
    return value + ahead, ahead - value


def spread_y(quotient, ylen):
    rows = [quotient[TILE + step : TILE + step + ylen] for step in range(-REACH, REACH + 1)]
    return sum((ROWS - abs(k - REACH)) * rows[k] for k in range(2 * REACH + 1))


def to_neighbours(quotient, ylen):
    top = quotient[ylen : ylen + TILE]
    base = quotient[TILE : 2 * TILE]
    ahead, back = [], []
    for row in range(REACH):
        ahead.append(sum(float(REACH - row - k) * top[TILE - 1 - k : TILE - k] for k in range(REACH - row)))
        back.append(sum(float(row + 1 - k) * base[k : k + 1] for k in range(row + 1)))
    return ahead, back


def on_first():
    return lax.axis_index("load") == 0


def lead_kernel(totals, disp_hbm, fixed_hbm, density_hbm, solid_hbm, disp, fixed, density, solid, z_out, y_out, sems):
    loads, comps, zlen, ylen, _ = disp.shape
    copies = [
        pltpu.make_async_copy(source, target, sems.at[k])
        for k, (source, target) in enumerate(
            ((disp_hbm, disp), (fixed_hbm, fixed), (density_hbm, density), (solid_hbm, solid))
        )
    ]
    for copy in copies:
        copy.start()
    for copy in copies:
        copy.wait()
    gives = jnp.where(on_first(), 0, zlen - 1)
    plane = lax.axis_index("sz") * zlen + gives
    base_y = lax.axis_index("sy") * ylen
    z_out[loads * comps] = voxel_factor(density[gives], solid[gives], plane, base_y, *totals)
    for case in range(loads):
        for comp in range(comps):
            z_out[case * comps + comp] = held(disp, fixed, case, comp, gives, slice(None))
            for z in range(zlen):
                at = (comp * loads + case) * zlen + z
                y_out[at : at + 1] = held(disp, fixed, case, comp, z, slice(0, 1))


def tile_energies(plus, diff, first, lanes, layers, loads, comps, base=0):
    weights = mode_weights()

    def faces(k, z):
        near, far = slice(first, first + TILE), slice(first + 1, first + TILE + 1)
        whole, whole_next = plus[k, z, near, lanes], plus[k, z, far, lanes]
        change, change_next = diff[k, z, near, lanes], diff[k, z, far, lanes]
        return whole + whole_next, change + change_next, whole_next - whole, change_next - change

    energy = [None] * layers
    for case in range(loads):
        low = None
        for z in range(layers + 1):
            high = [faces(case * comps + comp, base + z) for comp in range(comps)]
            if low is not None:
                part = quadratic(low, high, weights)
                energy[z - 1] = part if energy[z - 1] is None else energy[z - 1] + part
            low = high
    return energy


def blank_last(value, first, ylen):
    row = lax.broadcasted_iota(jnp.int32, value.shape, 0) + first
    return jnp.where(row == ylen - 1, 0.0, value)


def inner_kernel(totals, disp, fixed, density, solid, own, line, sends, last_plus, last_diff, last_factor, edge, plus, diff, quotient):
    loads, comps, zlen, ylen, xlen = disp.shape
    total_z, total_y = totals
    base_z = lax.axis_index("sz") * zlen
    base_y = lax.axis_index("sy") * ylen
    inner = zlen - 1
    keeps = jnp.where(on_first(), inner, 0)

    @pl.loop(0, loads * comps)
    def _(k):
        case, comp = k // comps, k % comps
        for z in range(zlen):
            whole, change = split_x(held(disp, fixed, case, comp, z, slice(None)))
            plus[k, z, :ylen] = whole
            diff[k, z, :ylen] = change
        last_plus[k] = plus[k, keeps, :ylen]
        last_diff[k] = diff[k, keeps, :ylen]

    for comp in range(comps):
        for case in range(loads):
            for z in range(zlen):
                at = (comp * loads + case) * zlen + z
                line[0, at : at + 1] = plus[case * comps + comp, z, ylen - 1 : ylen]
                line[1, at : at + 1] = diff[case * comps + comp, z, ylen - 1 : ylen]

    zeros = jnp.zeros((TILE, xlen), jnp.float32)
    edge[...] = jnp.zeros(edge.shape, jnp.float32)
    for z in range(zlen):
        factor = voxel_factor(density[z], solid[z], base_z + z, base_y, total_z, total_y)
        edge[z : z + 1] = factor[ylen - 1 :]
        if z == inner:
            last_factor[...] = factor
        else:
            quotient[z, :TILE] = zeros
            quotient[z, TILE : TILE + ylen] = factor
            quotient[z, TILE + ylen :] = zeros

    for first in range(0, ylen, TILE):

        @pl.loop(0, xlen // LANES)
        def _(chunk):
            lanes = pl.ds(pl.multiple_of(chunk * LANES, LANES), LANES)
            energy = tile_energies(plus, diff, first, lanes, inner, loads, comps)
            for z in range(inner):
                here = quotient[z, first + TILE : first + 2 * TILE, lanes]
                quotient[z, first + TILE : first + 2 * TILE, lanes] = blank_last(energy[z] * here, first, ylen)

    for z in range(inner):
        own[z] = spread_x(spread_y(quotient.at[z], ylen))
        ahead, back = to_neighbours(quotient.at[z], ylen)
        ends = spread_x(jnp.concatenate(ahead + back + [zeros[:2]], axis=0))
        sends[0, REACH * z : REACH * (z + 1)] = ends[:REACH]
        sends[1, REACH * z : REACH * (z + 1)] = ends[REACH : 2 * REACH]


def outer_kernel(
    shape, z_in, y_in, disp, fixed, own_in, line, sends, last_plus, last_diff, last_factor, edge, own, known, a_out, b_out, plus, diff, quotient, factor
):
    loads, comps, zlen, ylen, xlen = shape
    planes = loads * comps
    inner = zlen - 1
    first_core, index = on_first(), lax.axis_index("sz")
    top = first_core & (index == lax.axis_size("sz") - 1)
    keeps = jnp.where(first_core, inner, 0)
    stays, comes = jnp.where(first_core, 0, 1), jnp.where(first_core, jnp.where(top, 2, 1), 0)
    for k in range(planes):
        plus[k, stays, :ylen] = last_plus[k]
        diff[k, stays, :ylen] = last_diff[k]
        whole, change = split_x(z_in[k])
        plus[k, comes, :ylen] = whole
        diff[k, comes, :ylen] = change
    below = jnp.where(index > 0, z_in[planes], 0.0)
    factor[...] = jnp.where(first_core, last_factor[...], below)

    @pl.when(top)
    def _():
        clamped = jnp.zeros((ylen + TILE, xlen), jnp.float32)
        for k in range(planes):
            for slot in (1, 3):
                plus[k, slot] = clamped
                diff[k, slot] = clamped

    zeros = jnp.zeros((TILE, xlen), jnp.float32)
    quotient[:TILE] = zeros
    quotient[TILE + ylen :] = zeros
    for first in range(0, ylen, TILE):

        @pl.loop(0, xlen // LANES)
        def _(chunk):
            lanes = pl.ds(pl.multiple_of(chunk * LANES, LANES), LANES)
            (energy,) = tile_energies(plus, diff, first, lanes, 1, loads, comps)
            here = energy * factor[first : first + TILE, lanes]
            quotient[first + TILE : first + 2 * TILE, lanes] = blank_last(here, first, ylen)

    @pl.when(top)
    def _():
        for first in range(0, ylen, TILE):

            @pl.loop(0, xlen // LANES)
            def _(chunk):
                lanes = pl.ds(pl.multiple_of(chunk * LANES, LANES), LANES)
                (energy,) = tile_energies(plus, diff, first, lanes, 1, loads, comps, base=2)
                here = energy * factor[first : first + TILE, lanes]
                quotient[first + TILE : first + 2 * TILE, lanes] += blank_last(here, first, ylen)

    count = loads * zlen
    more = lax.axis_index("sy") < lax.axis_size("sy") - 1
    low, high = [], []
    for comp in range(comps):
        part = slice(comp * count, (comp + 1) * count)
        whole, change = line[0, part], line[1, part]
        whole_next, change_next = split_x(jnp.where(more, y_in[part], 0.0))
        face = (whole + whole_next, change + change_next, whole_next - whole, change_next - change)
        low.append(face)
        high.append([pltpu.roll(value, count - 1, 0) for value in face])
    energy = quadratic(low, high, mode_weights())
    energy = sum(energy[case * zlen : case * zlen + inner] for case in range(loads)) * edge[:inner]
    last = spread_x(jnp.concatenate([energy, jnp.zeros((TILE - inner, xlen), jnp.float32)], axis=0))

    row = lax.broadcasted_iota(jnp.int32, (TILE, xlen), 0)
    rising = jnp.maximum(row - (TILE - 1 - ROWS), 0).astype(jnp.float32)
    ups, downs = [], []
    for z in range(inner):
        own[z] = own_in[z]
        own[z, ylen - TILE :] += rising * last[z : z + 1]
        here = sends[0, REACH * z : REACH * (z + 1)]
        ups += [here[r : r + 1] + float(REACH - r) * last[z : z + 1] for r in range(REACH)]
        downs.append(sends[1, REACH * z : REACH * (z + 1)])
    own[inner] = spread_x(spread_y(quotient, ylen))
    ahead, back = to_neighbours(quotient, ylen)
    ends = spread_x(jnp.concatenate(ahead + back + [zeros[:2]], axis=0))
    ups += [ends[: REACH - 1], factor[ylen - 1 :]]
    downs.append(ends[REACH : 2 * REACH])

    pairs = [(case, comp) for comp in range(comps) for case in range(loads)]
    here_last = [held(disp, fixed, case, comp, keeps, slice(ylen - 1, ylen)) for case, comp in pairs]
    here_first = [held(disp, fixed, case, comp, keeps, slice(0, 1)) for case, comp in pairs]
    next_row = [jnp.where(first_core, y_in[k * zlen + inner : (k + 1) * zlen], y_in[k * zlen : k * zlen + 1]) for k in range(planes)]
    next_row = [jnp.where(more, row, 0.0) for row in next_row]
    come_last = [z_in[case * comps + comp, ylen - 1 : ylen] for case, comp in pairs]
    come_first = [z_in[case * comps + comp, 0:1] for case, comp in pairs]
    rows = here_last + come_last + next_row + here_first + come_first + [factor[ylen - 1 :]]
    known[: len(rows)] = jnp.concatenate(rows, axis=0)
    known[len(rows) :] = jnp.zeros((known.shape[0] - len(rows), xlen), jnp.float32)
    up = jnp.concatenate(ups + here_last + come_last, axis=0)
    down = jnp.concatenate(downs + come_first + [jnp.zeros((planes, xlen), jnp.float32)], axis=0)
    even = lax.axis_index("sy") % 2 == 0
    a_out[...] = jnp.where(even, up, down)
    b_out[...] = jnp.where(even, down, up)


def rows_kernel(loads, comps, own, known, b_in, a_in, h_out, p_out, q_out):
    zlen, ylen, xlen = own.shape
    planes = loads * comps
    index, last = lax.axis_index("sy"), lax.axis_size("sy") - 1
    even = index % 2 == 0
    from_low = jnp.where(index > 0, jnp.where(even, b_in[...], a_in[...]), 0.0)
    from_high = jnp.where(index < last, jnp.where(even, a_in[...], b_in[...]), 0.0)
    ends = REACH * zlen
    first_core = on_first()
    top = first_core & (lax.axis_index("sz") == lax.axis_size("sz") - 1)

    def nodes(first, second, comp):
        part = slice(comp * loads, (comp + 1) * loads)
        zero = jnp.zeros((loads, xlen), jnp.float32)
        (first, first_more), (second, second_more) = first, second
        pieces = [first, first_more, second, second_more]
        return split_x(jnp.concatenate([zero if piece is None else piece[part] for piece in pieces], axis=0))

    def under(stays, comes):
        return jnp.where(first_core, stays, comes), jnp.where(top, comes, 0.0)

    def over(stays, comes):
        return jnp.where(first_core, jnp.where(top, 0.0, comes), stays), None

    def face(near_own, near_in, far_own, far_in, comp):
        whole, change = nodes(near_own, near_in, comp)
        whole_next, change_next = nodes(far_own, far_in, comp)
        return whole + whole_next, change + change_next, whole_next - whole, change_next - change

    here_last, come_last, next_row, here_first, come_first = (known[planes * k : planes * (k + 1)] for k in range(5))
    low_last, low_come = from_low[ends : ends + planes], from_low[ends + planes : ends + 2 * planes]
    next_come = from_high[ends : ends + planes]
    corners = [(here_last, come_last), (low_last, low_come), (next_row, next_come), (here_first, come_first)]
    low = [face(*(under(*corner) for corner in corners), comp) for comp in range(comps)]
    high = [face(*(over(*corner) for corner in corners), comp) for comp in range(comps)]
    energy = quadratic(low, high, mode_weights())
    cases = 2 * loads
    lines = [sum(energy[cases * k + case : cases * k + case + 1] for case in range(cases)) for k in range(2)]
    lines = [lines[0] * known[5 * planes : 5 * planes + 1], lines[1] * from_low[ends - 1 : ends]]
    lines = spread_x(jnp.concatenate(lines + [jnp.zeros((TILE - 2, xlen), jnp.float32)], axis=0))

    row = lax.broadcasted_iota(jnp.int32, (TILE, xlen), 0)
    rising = jnp.maximum(row - (TILE - 1 - ROWS), 0).astype(jnp.float32)
    falling = jnp.maximum(REACH - row, 0).astype(jnp.float32)
    blank = jnp.zeros((TILE - REACH, xlen), jnp.float32)
    between = jnp.where(first_core, zlen, 0)
    h_out[zlen - between] = jnp.zeros((ylen, xlen), jnp.float32)
    for z in range(zlen):
        part = slice(REACH * z, REACH * (z + 1))
        head = jnp.concatenate([from_low[part], blank], axis=0)
        tail = jnp.concatenate([blank, from_high[part]], axis=0)
        at = z + 1
        if z == zlen - 1:
            head = jnp.where(row == REACH - 1, 0.0, head) + falling * lines[1:2]
            tail = tail + rising * lines[0:1]
            at = between
        h_out[at] = own[z]
        h_out[at, :TILE] += head
        h_out[at, ylen - TILE :] += tail
    p_out[...] = h_out[pl.ds(jnp.where(first_core, 1, zlen + 1 - REACH), REACH)]
    q_out[...] = h_out[pl.ds(jnp.where(first_core, 1, 0), zlen)]


def layers_kernel(h, p_in, q_in, out):
    zlen = out.shape[0]
    index, last = lax.axis_index("sz"), lax.axis_size("sz") - 1
    first_core = on_first()
    below = [jnp.where(first_core, q_in[zlen - REACH + k], p_in[k]) for k in range(REACH)]
    above = [jnp.where(first_core, p_in[k - 1] if k else 0.0, q_in[k]) for k in range(zlen)]
    below = [jnp.where(index > 0, layer, 0.0) for layer in below]
    above = [jnp.where(index < last, layer, 0.0) for layer in above]
    layers = below[:-1] + [below[-1] + h[0]] + [h[z] for z in range(1, zlen)] + [h[zlen] + above[0]] + above[1:]
    for z, layer in enumerate(spread_layers(layers)):
        out[z] = layer


def sum_kernel(part, other, out):
    out[...] = part[...] + other[...]


def call(kernel, outs, args, scratch=(), space=pltpu.VMEM):
    shapes = [jax.ShapeDtypeStruct(out, jnp.float32) if isinstance(out, tuple) else out for out in outs]
    return pl.pallas_call(
        kernel,
        out_shape=shapes,
        in_specs=[pl.BlockSpec(memory_space=space)] * len(args),
        out_specs=[pl.BlockSpec(memory_space=pltpu.VMEM)] * len(outs),
        scratch_shapes=list(scratch),
        compiler_params=pltpu.CompilerParams(vmem_limit_bytes=32 * 1024 * 1024),
    )(*args)


def column_moved(value, back=False):
    size = lax.axis_size("sz")
    ring = list(range(size - 1, -1, -1)) + [size + k for k in range(size)]
    if back:
        ring.reverse()
    return lax.ppermute(value, ("load", "sz"), [(ring[k - 1], ring[k]) for k in range(len(ring))])


def ring_moved(value, axis):
    size = lax.axis_size(axis)
    return lax.ppermute(value, axis, [((k + 1) % size, k) for k in range(size)])


def swapped(value, axis, first):
    cores, size = lax.axis_size("load"), lax.axis_size(axis)
    pairs = []
    for core in range(cores):
        for k in range(size):
            other = k + 1 if (k - first) % 2 == 0 else k - 1
            target = core * size + other if 0 <= other < size else (cores - 1 - core) * size + k
            pairs.append((core * size + k, target))
    return lax.ppermute(value, ("load", axis), pairs)


def body(displacements, density, solid, fixed):
    loads, comps, zlen, ylen, xlen = displacements.shape
    planes = loads * comps
    totals = (zlen * lax.axis_size("sz"), ylen * lax.axis_size("sy"))
    args = [
        pltpu.with_memory_space_constraint(arg, pltpu.HBM) for arg in (displacements, fixed, density, solid)
    ]

    disp, fixed, density, solid, z_send, y_send = call(
        lambda *refs: lead_kernel(totals, *refs),
        [jax.ShapeDtypeStruct(arg.shape, arg.dtype) for arg in args]
        + [(planes + 1, ylen, xlen), (planes * zlen, xlen)],
        args,
        scratch=[pltpu.SemaphoreType.DMA((len(args),))],
        space=pltpu.HBM,
    )
    z_in = column_moved(z_send)
    y_in = ring_moved(y_send, "sy")
    nodes = lambda layers: pltpu.VMEM((planes, layers, ylen + TILE, xlen), jnp.float32)
    inner = call(
        lambda *refs: inner_kernel(totals, *refs),
        [
            (zlen, ylen, xlen),
            (2, planes * zlen, xlen),
            (2, REACH * (zlen - 1), xlen),
            (planes, ylen, xlen),
            (planes, ylen, xlen),
            (ylen, xlen),
            (TILE, xlen),
        ],
        (disp, fixed, density, solid),
        scratch=[nodes(zlen), nodes(zlen), pltpu.VMEM((zlen - 1, ylen + 2 * TILE, xlen), jnp.float32)],
    )
    size = REACH * zlen + 2 * planes
    own, known, a_send, b_send = call(
        lambda *refs: outer_kernel(displacements.shape, *refs),
        [(zlen, ylen, xlen), (-(-(5 * planes + 1) // TILE) * TILE, xlen), (size, xlen), (size, xlen)],
        (z_in, y_in, disp, fixed, *inner),
        scratch=[
            nodes(4),
            nodes(4),
            pltpu.VMEM((ylen + 2 * TILE, xlen), jnp.float32),
            pltpu.VMEM((ylen, xlen), jnp.float32),
        ],
    )
    b_in = swapped(b_send, "sy", 1)
    a_in = swapped(a_send, "sy", 0)
    h, p_send, q_send = call(
        lambda *refs: rows_kernel(loads, comps, *refs),
        [(zlen + 1, ylen, xlen), (REACH, ylen, xlen), (zlen, ylen, xlen)],
        (own, known, b_in, a_in),
    )
    p_in = column_moved(p_send)
    q_in = column_moved(q_send, back=True)
    (part,) = call(layers_kernel, [(zlen, ylen, xlen)], (h, p_in, q_in))
    cores = lax.axis_size("load")
    other = lax.ppermute(part, "load", [(core, cores - 1 - core) for core in range(cores)])
    (out,) = call(sum_kernel, [(zlen, ylen, xlen)], (part, other))
    return out


def solution(mesh):
    return jax.shard_map(
        body,
        mesh=mesh,
        in_specs=(
            P("load", None, "sz", "sy", None),
            P("sz", "sy", None),
            P("sz", "sy", None),
            P("sz", "sy", None),
        ),
        out_specs=P("sz", "sy", None),
        check_vma=False,
    )
```

```python
import jax
import jax.numpy as jnp
import numpy as np
from jax import lax
from jax.experimental import pallas as pl
from jax.experimental.pallas import tpu as pltpu
from jax.sharding import PartitionSpec as P

OFFSETS = [(0, 0, 0), (1, 0, 0), (1, 1, 0), (0, 1, 0), (0, 0, 1), (1, 0, 1), (1, 1, 1), (0, 1, 1)]
REACH = 3
ROWS = REACH + 1
TILE = 8
LANES = 128


def element_matrix():
    corners = np.array(
        [
            [-1.0, -1.0, -1.0],
            [1.0, -1.0, -1.0],
            [1.0, 1.0, -1.0],
            [-1.0, 1.0, -1.0],
            [-1.0, -1.0, 1.0],
            [1.0, -1.0, 1.0],
            [1.0, 1.0, 1.0],
            [-1.0, 1.0, 1.0],
        ]
    )
    poisson = 0.3
    lame = poisson / ((1.0 + poisson) * (1.0 - 2.0 * poisson))
    shear = 1.0 / (2.0 * (1.0 + poisson))
    elastic = np.zeros((6, 6))
    elastic[:3, :3] = lame
    for k in range(3):
        elastic[k, k] += 2.0 * shear
        elastic[3 + k, 3 + k] = shear
    gauss = 1.0 / np.sqrt(3.0)
    stiffness = np.zeros((24, 24))
    for gi in range(2):
        for gj in range(2):
            for gk in range(2):
                point = np.array([(2 * gi - 1) * gauss, (2 * gj - 1) * gauss, (2 * gk - 1) * gauss])
                strain = np.zeros((6, 24))
                for node in range(8):
                    grads = np.zeros(3)
                    for k in range(3):
                        value = corners[node, k] / 8.0
                        for m in range(3):
                            if m != k:
                                value = value * (1.0 + point[m] * corners[node, m])
                        grads[k] = 2.0 * value
                    col = 3 * node
                    strain[0, col] = grads[0]
                    strain[1, col + 1] = grads[1]
                    strain[2, col + 2] = grads[2]
                    strain[3, col] = grads[1]
                    strain[3, col + 1] = grads[0]
                    strain[4, col + 1] = grads[2]
                    strain[4, col + 2] = grads[1]
                    strain[5, col] = grads[2]
                    strain[5, col + 2] = grads[0]
                stiffness += strain.T @ elastic @ strain / 8.0
    return stiffness


def mode_weights():
    modes = [(i, j, k) for k in (0, 1) for j in (0, 1) for i in (0, 1)]
    sums = np.zeros((24, 24))
    for m, mode in enumerate(modes):
        for n, corner in enumerate(OFFSETS):
            sign = np.prod([(1 if corner[d] else -1) if mode[d] else 1 for d in range(3)])
            for comp in range(3):
                sums[3 * m + comp, 3 * n + comp] = sign
    form = sums @ element_matrix() @ sums.T / 64.0

    def at(first, second):
        return form[3 * modes.index(first[1]) + first[0], 3 * modes.index(second[1]) + second[0]]

    ux, vy, uy = (0, (1, 0, 0)), (1, (0, 1, 0)), (0, (0, 1, 0))
    uxy, wyz = (0, (1, 1, 0)), (2, (0, 1, 1))
    wxy, vxz, uxyz = (2, (1, 1, 0)), (1, (1, 0, 1)), (0, (1, 1, 1))
    return dict(
        normal=at(ux, ux) - at(ux, vy),
        trace=at(ux, vy),
        shear=at(uy, uy),
        plus=(at(uxy, uxy) + at(uxy, wyz)) / 2,
        minus=(at(uxy, uxy) - at(uxy, wyz)) / 2,
        twist=at(wxy, wxy) - at(wxy, vxz),
        twist_sum=at(wxy, vxz),
        corner=at(uxyz, uxyz),
    )


def square(value):
    return value * value


def quadratic(low, high, weights):
    x = [low[c][1] + high[c][1] for c in range(3)]
    y = [low[c][2] + high[c][2] for c in range(3)]
    z = [high[c][0] - low[c][0] for c in range(3)]
    xy = [low[c][3] + high[c][3] for c in range(3)]
    xz = [high[c][1] - low[c][1] for c in range(3)]
    yz = [high[c][2] - low[c][2] for c in range(3)]
    xyz = [high[c][3] - low[c][3] for c in range(3)]
    normal = square(x[0]) + square(y[1]) + square(z[2])
    trace = square(x[0] + y[1] + z[2])
    shear = square(y[0] + x[1]) + square(z[0] + x[2]) + square(z[1] + y[2])
    pairs = ((xy[0], yz[2]), (xy[1], xz[2]), (xz[0], yz[1]))
    plus = sum(square(p + q) for p, q in pairs)
    minus = sum(square(p - q) for p, q in pairs)
    twist = square(xy[2]) + square(xz[1]) + square(yz[0])
    twist_sum = square(xy[2] + xz[1] + yz[0])
    corner = square(xyz[0]) + square(xyz[1]) + square(xyz[2])
    groups = dict(
        normal=normal, trace=trace, shear=shear, plus=plus, minus=minus, twist=twist, twist_sum=twist_sum, corner=corner
    )
    return sum(np.float32(weights[name]) * group for name, group in groups.items())


def line_weight(coord, count):
    def outside(distance):
        missing = jnp.maximum(REACH - distance, 0)
        return missing * (missing + 1) // 2

    whole = (REACH + 1) * (REACH + 1)
    return (whole - outside(coord) - outside(count - 1 - coord)).astype(jnp.float32)


def voxel_factor(density, solid, plane, first_row, total_z, total_y):
    rows, length = density.shape
    row = lax.broadcasted_iota(jnp.int32, (rows, length), 0) + first_row
    column = lax.broadcasted_iota(jnp.int32, (rows, length), 1)
    weight = line_weight(row, total_y) * line_weight(column, length)
    weight = weight * line_weight(jnp.full((rows, length), plane, jnp.int32), total_z)
    return solid.astype(jnp.float32) * (-3.0 * density * density) / weight


def spread_x(value):
    rows, length = value.shape
    wide = jnp.concatenate([value, jnp.zeros((rows, LANES), jnp.float32)], axis=1)
    span = length + LANES
    total = float(ROWS) * value
    for step in range(1, ROWS):
        both = pltpu.roll(wide, span - step, 1) + pltpu.roll(wide, step, 1)
        total = total + float(ROWS - step) * both[:, :length]
    return total


def spread_layers(layers):
    for step in (1, 2, 1, 2):
        layers = [layers[k] + layers[k + step] for k in range(len(layers) - step)]
    return layers


def held(disp, fixed, case, comp, z, rows):
    return disp[case, comp, z, rows] * (1.0 - fixed[z, rows].astype(jnp.float32))


def split_x(value):
    length = value.shape[1]
    column = lax.broadcasted_iota(jnp.int32, value.shape, 1)
    ahead = jnp.where(column == length - 1, 0.0, pltpu.roll(value, length - 1, 1))
    return value + ahead, ahead - value


def spread_y(quotient, ylen):
    rows = [quotient[TILE + step : TILE + step + ylen] for step in range(-REACH, REACH + 1)]
    return sum((ROWS - abs(k - REACH)) * rows[k] for k in range(2 * REACH + 1))


def to_neighbours(quotient, ylen):
    top = quotient[ylen : ylen + TILE]
    base = quotient[TILE : 2 * TILE]
    ahead, back = [], []
    for row in range(REACH):
        ahead.append(sum(float(REACH - row - k) * top[TILE - 1 - k : TILE - k] for k in range(REACH - row)))
        back.append(sum(float(row + 1 - k) * base[k : k + 1] for k in range(row + 1)))
    return ahead, back


def on_first():
    return lax.axis_index("load") == 0


def lead_kernel(totals, disp_hbm, fixed_hbm, density_hbm, solid_hbm, disp, fixed, density, solid, z_out, y_out, sems):
    loads, comps, zlen, ylen, _ = disp.shape
    copies = [
        pltpu.make_async_copy(source, target, sems.at[k])
        for k, (source, target) in enumerate(
            ((disp_hbm, disp), (fixed_hbm, fixed), (density_hbm, density), (solid_hbm, solid))
        )
    ]
    for copy in copies:
        copy.start()
    for copy in copies:
        copy.wait()
    gives = jnp.where(on_first(), 0, zlen - 1)
    plane = lax.axis_index("sz") * zlen + gives
    base_y = lax.axis_index("sy") * ylen
    z_out[loads * comps] = voxel_factor(density[gives], solid[gives], plane, base_y, *totals)
    for case in range(loads):
        for comp in range(comps):
            z_out[case * comps + comp] = held(disp, fixed, case, comp, gives, slice(None))
            for z in range(zlen):
                at = (comp * loads + case) * zlen + z
                y_out[at : at + 1] = held(disp, fixed, case, comp, z, slice(0, 1))


def tile_energies(plus, diff, first, lanes, layers, loads, comps, base=0):
    weights = mode_weights()

    def faces(k, z):
        near, far = slice(first, first + TILE), slice(first + 1, first + TILE + 1)
        whole, whole_next = plus[k, z, near, lanes], plus[k, z, far, lanes]
        change, change_next = diff[k, z, near, lanes], diff[k, z, far, lanes]
        return whole + whole_next, change + change_next, whole_next - whole, change_next - change

    energy = [None] * layers
    for case in range(loads):
        low = None
        for z in range(layers + 1):
            high = [faces(case * comps + comp, base + z) for comp in range(comps)]
            if low is not None:
                part = quadratic(low, high, weights)
                energy[z - 1] = part if energy[z - 1] is None else energy[z - 1] + part
            low = high
    return energy


def blank_last(value, first, ylen):
    row = lax.broadcasted_iota(jnp.int32, value.shape, 0) + first
    return jnp.where(row == ylen - 1, 0.0, value)


def inner_kernel(totals, disp, fixed, density, solid, own, line, sends, last_plus, last_diff, last_factor, edge, plus, diff, quotient):
    loads, comps, zlen, ylen, xlen = disp.shape
    total_z, total_y = totals
    base_z = lax.axis_index("sz") * zlen
    base_y = lax.axis_index("sy") * ylen
    inner = zlen - 1
    keeps = jnp.where(on_first(), inner, 0)

    @pl.loop(0, loads * comps)
    def _(k):
        case, comp = k // comps, k % comps
        for z in range(zlen):
            whole, change = split_x(held(disp, fixed, case, comp, z, slice(None)))
            plus[k, z, :ylen] = whole
            diff[k, z, :ylen] = change
        last_plus[k] = plus[k, keeps, :ylen]
        last_diff[k] = diff[k, keeps, :ylen]

    for comp in range(comps):
        for case in range(loads):
            for z in range(zlen):
                at = (comp * loads + case) * zlen + z
                line[0, at : at + 1] = plus[case * comps + comp, z, ylen - 1 : ylen]
                line[1, at : at + 1] = diff[case * comps + comp, z, ylen - 1 : ylen]

    zeros = jnp.zeros((TILE, xlen), jnp.float32)
    edge[...] = jnp.zeros(edge.shape, jnp.float32)
    for z in range(zlen):
        factor = voxel_factor(density[z], solid[z], base_z + z, base_y, total_z, total_y)
        edge[z : z + 1] = factor[ylen - 1 :]
        if z == inner:
            last_factor[...] = factor
        else:
            quotient[z, :TILE] = zeros
            quotient[z, TILE : TILE + ylen] = factor
            quotient[z, TILE + ylen :] = zeros

    for first in range(0, ylen, TILE):

        @pl.loop(0, xlen // LANES)
        def _(chunk):
            lanes = pl.ds(pl.multiple_of(chunk * LANES, LANES), LANES)
            energy = tile_energies(plus, diff, first, lanes, inner, loads, comps)
            for z in range(inner):
                here = quotient[z, first + TILE : first + 2 * TILE, lanes]
                quotient[z, first + TILE : first + 2 * TILE, lanes] = blank_last(energy[z] * here, first, ylen)

    for z in range(inner):
        own[z] = spread_x(spread_y(quotient.at[z], ylen))
        ahead, back = to_neighbours(quotient.at[z], ylen)
        ends = spread_x(jnp.concatenate(ahead + back + [zeros[:2]], axis=0))
        sends[0, REACH * z : REACH * (z + 1)] = ends[:REACH]
        sends[1, REACH * z : REACH * (z + 1)] = ends[REACH : 2 * REACH]


def outer_kernel(
    shape, z_in, y_in, disp, fixed, own_in, line, sends, last_plus, last_diff, last_factor, edge, own, known, a_out, b_out, plus, diff, quotient, factor
):
    loads, comps, zlen, ylen, xlen = shape
    planes = loads * comps
    inner = zlen - 1
    first_core, index = on_first(), lax.axis_index("sz")
    top = first_core & (index == lax.axis_size("sz") - 1)
    keeps = jnp.where(first_core, inner, 0)
    stays, comes = jnp.where(first_core, 0, 1), jnp.where(first_core, jnp.where(top, 2, 1), 0)
    for k in range(planes):
        plus[k, stays, :ylen] = last_plus[k]
        diff[k, stays, :ylen] = last_diff[k]
        whole, change = split_x(z_in[k])
        plus[k, comes, :ylen] = whole
        diff[k, comes, :ylen] = change
    below = jnp.where(index > 0, z_in[planes], 0.0)
    factor[...] = jnp.where(first_core, last_factor[...], below)

    @pl.when(top)
    def _():
        clamped = jnp.zeros((ylen + TILE, xlen), jnp.float32)
        for k in range(planes):
            for slot in (1, 3):
                plus[k, slot] = clamped
                diff[k, slot] = clamped

    zeros = jnp.zeros((TILE, xlen), jnp.float32)
    quotient[:TILE] = zeros
    quotient[TILE + ylen :] = zeros
    for first in range(0, ylen, TILE):

        @pl.loop(0, xlen // LANES)
        def _(chunk):
            lanes = pl.ds(pl.multiple_of(chunk * LANES, LANES), LANES)
            (energy,) = tile_energies(plus, diff, first, lanes, 1, loads, comps)
            here = energy * factor[first : first + TILE, lanes]
            quotient[first + TILE : first + 2 * TILE, lanes] = blank_last(here, first, ylen)

    @pl.when(top)
    def _():
        for first in range(0, ylen, TILE):

            @pl.loop(0, xlen // LANES)
            def _(chunk):
                lanes = pl.ds(pl.multiple_of(chunk * LANES, LANES), LANES)
                (energy,) = tile_energies(plus, diff, first, lanes, 1, loads, comps, base=2)
                here = energy * factor[first : first + TILE, lanes]
                quotient[first + TILE : first + 2 * TILE, lanes] += blank_last(here, first, ylen)

    count = loads * zlen
    more = lax.axis_index("sy") < lax.axis_size("sy") - 1
    low, high = [], []
    for comp in range(comps):
        part = slice(comp * count, (comp + 1) * count)
        whole, change = line[0, part], line[1, part]
        whole_next, change_next = split_x(jnp.where(more, y_in[part], 0.0))
        face = (whole + whole_next, change + change_next, whole_next - whole, change_next - change)
        low.append(face)
        high.append([pltpu.roll(value, count - 1, 0) for value in face])
    energy = quadratic(low, high, mode_weights())
    energy = sum(energy[case * zlen : case * zlen + inner] for case in range(loads)) * edge[:inner]
    last = spread_x(jnp.concatenate([energy, jnp.zeros((TILE - inner, xlen), jnp.float32)], axis=0))

    row = lax.broadcasted_iota(jnp.int32, (TILE, xlen), 0)
    rising = jnp.maximum(row - (TILE - 1 - ROWS), 0).astype(jnp.float32)
    ups, downs = [], []
    for z in range(inner):
        own[z] = own_in[z]
        own[z, ylen - TILE :] += rising * last[z : z + 1]
        here = sends[0, REACH * z : REACH * (z + 1)]
        ups += [here[r : r + 1] + float(REACH - r) * last[z : z + 1] for r in range(REACH)]
        downs.append(sends[1, REACH * z : REACH * (z + 1)])
    own[inner] = spread_x(spread_y(quotient, ylen))
    ahead, back = to_neighbours(quotient, ylen)
    ends = spread_x(jnp.concatenate(ahead + back + [zeros[:2]], axis=0))
    ups += [ends[: REACH - 1], factor[ylen - 1 :]]
    downs.append(ends[REACH : 2 * REACH])

    pairs = [(case, comp) for comp in range(comps) for case in range(loads)]
    here_last = [held(disp, fixed, case, comp, keeps, slice(ylen - 1, ylen)) for case, comp in pairs]
    here_first = [held(disp, fixed, case, comp, keeps, slice(0, 1)) for case, comp in pairs]
    next_row = [jnp.where(first_core, y_in[k * zlen + inner : (k + 1) * zlen], y_in[k * zlen : k * zlen + 1]) for k in range(planes)]
    next_row = [jnp.where(more, row, 0.0) for row in next_row]
    come_last = [z_in[case * comps + comp, ylen - 1 : ylen] for case, comp in pairs]
    come_first = [z_in[case * comps + comp, 0:1] for case, comp in pairs]
    rows = here_last + come_last + next_row + here_first + come_first + [factor[ylen - 1 :]]
    known[: len(rows)] = jnp.concatenate(rows, axis=0)
    known[len(rows) :] = jnp.zeros((known.shape[0] - len(rows), xlen), jnp.float32)
    up = jnp.concatenate(ups + here_last + come_last, axis=0)
    down = jnp.concatenate(downs + come_first + [jnp.zeros((planes, xlen), jnp.float32)], axis=0)
    even = lax.axis_index("sy") % 2 == 0
    a_out[...] = jnp.where(even, up, down)
    b_out[...] = jnp.where(even, down, up)


def rows_kernel(loads, comps, own, known, b_in, a_in, h_out, a_out, b_out):
    zlen, ylen, xlen = own.shape
    planes = loads * comps
    index, last = lax.axis_index("sy"), lax.axis_size("sy") - 1
    even = index % 2 == 0
    from_low = jnp.where(index > 0, jnp.where(even, b_in[...], a_in[...]), 0.0)
    from_high = jnp.where(index < last, jnp.where(even, a_in[...], b_in[...]), 0.0)
    ends = REACH * zlen
    first_core = on_first()
    top = first_core & (lax.axis_index("sz") == lax.axis_size("sz") - 1)

    def nodes(first, second, comp):
        part = slice(comp * loads, (comp + 1) * loads)
        zero = jnp.zeros((loads, xlen), jnp.float32)
        (first, first_more), (second, second_more) = first, second
        pieces = [first, first_more, second, second_more]
        return split_x(jnp.concatenate([zero if piece is None else piece[part] for piece in pieces], axis=0))

    def under(stays, comes):
        return jnp.where(first_core, stays, comes), jnp.where(top, comes, 0.0)

    def over(stays, comes):
        return jnp.where(first_core, jnp.where(top, 0.0, comes), stays), None

    def face(near_own, near_in, far_own, far_in, comp):
        whole, change = nodes(near_own, near_in, comp)
        whole_next, change_next = nodes(far_own, far_in, comp)
        return whole + whole_next, change + change_next, whole_next - whole, change_next - change

    here_last, come_last, next_row, here_first, come_first = (known[planes * k : planes * (k + 1)] for k in range(5))
    low_last, low_come = from_low[ends : ends + planes], from_low[ends + planes : ends + 2 * planes]
    next_come = from_high[ends : ends + planes]
    corners = [(here_last, come_last), (low_last, low_come), (next_row, next_come), (here_first, come_first)]
    low = [face(*(under(*corner) for corner in corners), comp) for comp in range(comps)]
    high = [face(*(over(*corner) for corner in corners), comp) for comp in range(comps)]
    energy = quadratic(low, high, mode_weights())
    cases = 2 * loads
    lines = [sum(energy[cases * k + case : cases * k + case + 1] for case in range(cases)) for k in range(2)]
    lines = [lines[0] * known[5 * planes : 5 * planes + 1], lines[1] * from_low[ends - 1 : ends]]
    lines = spread_x(jnp.concatenate(lines + [jnp.zeros((TILE - 2, xlen), jnp.float32)], axis=0))

    row = lax.broadcasted_iota(jnp.int32, (TILE, xlen), 0)
    rising = jnp.maximum(row - (TILE - 1 - ROWS), 0).astype(jnp.float32)
    falling = jnp.maximum(REACH - row, 0).astype(jnp.float32)
    blank = jnp.zeros((TILE - REACH, xlen), jnp.float32)
    between = jnp.where(first_core, zlen, 0)
    h_out[zlen - between] = jnp.zeros((ylen, xlen), jnp.float32)
    for z in range(zlen):
        part = slice(REACH * z, REACH * (z + 1))
        head = jnp.concatenate([from_low[part], blank], axis=0)
        tail = jnp.concatenate([blank, from_high[part]], axis=0)
        at = z + 1
        if z == zlen - 1:
            head = jnp.where(row == REACH - 1, 0.0, head) + falling * lines[1:2]
            tail = tail + rising * lines[0:1]
            at = between
        h_out[at] = own[z]
        h_out[at, :TILE] += head
        h_out[at, ylen - TILE :] += tail
    high = (lax.axis_index("sz") % 2 == 0).astype(jnp.int32)
    a_out[...] = h_out[pl.ds(high, zlen)]
    b_out[...] = h_out[pl.ds(1 - high, zlen)]


def layers_kernel(h, a_in, b_in, out):
    zlen = out.shape[0]
    index, last = lax.axis_index("sz"), lax.axis_size("sz") - 1
    even = index % 2 == 0
    below = [jnp.where(index > 0, jnp.where(even, b_in[k], a_in[k]), 0.0) for k in range(zlen - REACH, zlen)]
    above = [jnp.where(index < last, jnp.where(even, a_in[k], b_in[k]), 0.0) for k in range(zlen)]
    layers = below[:-1] + [below[-1] + h[0]] + [h[z] for z in range(1, zlen)] + [h[zlen] + above[0]] + above[1:]
    for z, layer in enumerate(spread_layers(layers)):
        out[z] = layer


def sum_kernel(part, other, out):
    out[...] = part[...] + other[...]


def call(kernel, outs, args, scratch=(), space=pltpu.VMEM):
    shapes = [jax.ShapeDtypeStruct(out, jnp.float32) if isinstance(out, tuple) else out for out in outs]
    return pl.pallas_call(
        kernel,
        out_shape=shapes,
        in_specs=[pl.BlockSpec(memory_space=space)] * len(args),
        out_specs=[pl.BlockSpec(memory_space=pltpu.VMEM)] * len(outs),
        scratch_shapes=list(scratch),
        compiler_params=pltpu.CompilerParams(vmem_limit_bytes=32 * 1024 * 1024),
    )(*args)


def column_moved(value):
    size = lax.axis_size("sz")
    ring = list(range(size - 1, -1, -1)) + [size + k for k in range(size)]
    return lax.ppermute(value, ("load", "sz"), [(ring[k - 1], ring[k]) for k in range(len(ring))])


def ring_moved(value, axis):
    size = lax.axis_size(axis)
    return lax.ppermute(value, axis, [((k + 1) % size, k) for k in range(size)])


def swapped(value, axis, first, crossed=False):
    cores, size = lax.axis_size("load"), lax.axis_size(axis)
    pairs = []
    for core in range(cores):
        for k in range(size):
            other = k + 1 if (k - first) % 2 == 0 else k - 1
            inside = 0 <= other < size
            side = cores - 1 - core if crossed or not inside else core
            pairs.append((core * size + k, side * size + (other if inside else k)))
    return lax.ppermute(value, ("load", axis), pairs)


def body(displacements, density, solid, fixed):
    loads, comps, zlen, ylen, xlen = displacements.shape
    planes = loads * comps
    totals = (zlen * lax.axis_size("sz"), ylen * lax.axis_size("sy"))
    args = [
        pltpu.with_memory_space_constraint(arg, pltpu.HBM) for arg in (displacements, fixed, density, solid)
    ]

    disp, fixed, density, solid, z_send, y_send = call(
        lambda *refs: lead_kernel(totals, *refs),
        [jax.ShapeDtypeStruct(arg.shape, arg.dtype) for arg in args]
        + [(planes + 1, ylen, xlen), (planes * zlen, xlen)],
        args,
        scratch=[pltpu.SemaphoreType.DMA((len(args),))],
        space=pltpu.HBM,
    )
    z_in = column_moved(z_send)
    y_in = ring_moved(y_send, "sy")
    nodes = lambda layers: pltpu.VMEM((planes, layers, ylen + TILE, xlen), jnp.float32)
    inner = call(
        lambda *refs: inner_kernel(totals, *refs),
        [
            (zlen, ylen, xlen),
            (2, planes * zlen, xlen),
            (2, REACH * (zlen - 1), xlen),
            (planes, ylen, xlen),
            (planes, ylen, xlen),
            (ylen, xlen),
            (TILE, xlen),
        ],
        (disp, fixed, density, solid),
        scratch=[nodes(zlen), nodes(zlen), pltpu.VMEM((zlen - 1, ylen + 2 * TILE, xlen), jnp.float32)],
    )
    size = REACH * zlen + 2 * planes
    own, known, a_send, b_send = call(
        lambda *refs: outer_kernel(displacements.shape, *refs),
        [(zlen, ylen, xlen), (-(-(5 * planes + 1) // TILE) * TILE, xlen), (size, xlen), (size, xlen)],
        (z_in, y_in, disp, fixed, *inner),
        scratch=[
            nodes(4),
            nodes(4),
            pltpu.VMEM((ylen + 2 * TILE, xlen), jnp.float32),
            pltpu.VMEM((ylen, xlen), jnp.float32),
        ],
    )
    b_in = swapped(b_send, "sy", 1)
    a_in = swapped(a_send, "sy", 0)
    h, a_send, b_send = call(
        lambda *refs: rows_kernel(loads, comps, *refs),
        [(zlen + 1, ylen, xlen), (zlen, ylen, xlen), (zlen, ylen, xlen)],
        (own, known, b_in, a_in),
    )
    a_in = swapped(a_send, "sz", 0, crossed=True)
    b_in = swapped(b_send, "sz", 1, crossed=True)
    (part,) = call(layers_kernel, [(zlen, ylen, xlen)], (h, a_in, b_in))
    cores = lax.axis_size("load")
    other = lax.ppermute(part, "load", [(core, cores - 1 - core) for core in range(cores)])
    (out,) = call(sum_kernel, [(zlen, ylen, xlen)], (part, other))
    return out


def solution(mesh):
    return jax.shard_map(
        body,
        mesh=mesh,
        in_specs=(
            P("load", None, "sz", "sy", None),
            P("sz", "sy", None),
            P("sz", "sy", None),
            P("sz", "sy", None),
        ),
        out_specs=P("sz", "sy", None),
        check_vma=False,
    )
```

```python
import jax
import jax.numpy as jnp
import numpy as np
from jax import lax
from jax.experimental import pallas as pl
from jax.experimental.pallas import tpu as pltpu
from jax.sharding import PartitionSpec as P

OFFSETS = [(0, 0, 0), (1, 0, 0), (1, 1, 0), (0, 1, 0), (0, 0, 1), (1, 0, 1), (1, 1, 1), (0, 1, 1)]
REACH = 3
ROWS = REACH + 1
TILE = 8
LANES = 128


def element_matrix():
    corners = np.array(
        [
            [-1.0, -1.0, -1.0],
            [1.0, -1.0, -1.0],
            [1.0, 1.0, -1.0],
            [-1.0, 1.0, -1.0],
            [-1.0, -1.0, 1.0],
            [1.0, -1.0, 1.0],
            [1.0, 1.0, 1.0],
            [-1.0, 1.0, 1.0],
        ]
    )
    poisson = 0.3
    lame = poisson / ((1.0 + poisson) * (1.0 - 2.0 * poisson))
    shear = 1.0 / (2.0 * (1.0 + poisson))
    elastic = np.zeros((6, 6))
    elastic[:3, :3] = lame
    for k in range(3):
        elastic[k, k] += 2.0 * shear
        elastic[3 + k, 3 + k] = shear
    gauss = 1.0 / np.sqrt(3.0)
    stiffness = np.zeros((24, 24))
    for gi in range(2):
        for gj in range(2):
            for gk in range(2):
                point = np.array([(2 * gi - 1) * gauss, (2 * gj - 1) * gauss, (2 * gk - 1) * gauss])
                strain = np.zeros((6, 24))
                for node in range(8):
                    grads = np.zeros(3)
                    for k in range(3):
                        value = corners[node, k] / 8.0
                        for m in range(3):
                            if m != k:
                                value = value * (1.0 + point[m] * corners[node, m])
                        grads[k] = 2.0 * value
                    col = 3 * node
                    strain[0, col] = grads[0]
                    strain[1, col + 1] = grads[1]
                    strain[2, col + 2] = grads[2]
                    strain[3, col] = grads[1]
                    strain[3, col + 1] = grads[0]
                    strain[4, col + 1] = grads[2]
                    strain[4, col + 2] = grads[1]
                    strain[5, col] = grads[2]
                    strain[5, col + 2] = grads[0]
                stiffness += strain.T @ elastic @ strain / 8.0
    return stiffness


def mode_weights():
    modes = [(i, j, k) for k in (0, 1) for j in (0, 1) for i in (0, 1)]
    sums = np.zeros((24, 24))
    for m, mode in enumerate(modes):
        for n, corner in enumerate(OFFSETS):
            sign = np.prod([(1 if corner[d] else -1) if mode[d] else 1 for d in range(3)])
            for comp in range(3):
                sums[3 * m + comp, 3 * n + comp] = sign
    form = sums @ element_matrix() @ sums.T / 64.0

    def at(first, second):
        return form[3 * modes.index(first[1]) + first[0], 3 * modes.index(second[1]) + second[0]]

    ux, vy, uy = (0, (1, 0, 0)), (1, (0, 1, 0)), (0, (0, 1, 0))
    uxy, wyz = (0, (1, 1, 0)), (2, (0, 1, 1))
    wxy, vxz, uxyz = (2, (1, 1, 0)), (1, (1, 0, 1)), (0, (1, 1, 1))
    return dict(
        normal=at(ux, ux) - at(ux, vy),
        trace=at(ux, vy),
        shear=at(uy, uy),
        plus=(at(uxy, uxy) + at(uxy, wyz)) / 2,
        minus=(at(uxy, uxy) - at(uxy, wyz)) / 2,
        twist=at(wxy, wxy) - at(wxy, vxz),
        twist_sum=at(wxy, vxz),
        corner=at(uxyz, uxyz),
    )


def square(value):
    return value * value


def quadratic(low, high, weights):
    x = [low[c][1] + high[c][1] for c in range(3)]
    y = [low[c][2] + high[c][2] for c in range(3)]
    z = [high[c][0] - low[c][0] for c in range(3)]
    xy = [low[c][3] + high[c][3] for c in range(3)]
    xz = [high[c][1] - low[c][1] for c in range(3)]
    yz = [high[c][2] - low[c][2] for c in range(3)]
    xyz = [high[c][3] - low[c][3] for c in range(3)]
    normal = square(x[0]) + square(y[1]) + square(z[2])
    trace = square(x[0] + y[1] + z[2])
    shear = square(y[0] + x[1]) + square(z[0] + x[2]) + square(z[1] + y[2])
    pairs = ((xy[0], yz[2]), (xy[1], xz[2]), (xz[0], yz[1]))
    plus = sum(square(p + q) for p, q in pairs)
    minus = sum(square(p - q) for p, q in pairs)
    twist = square(xy[2]) + square(xz[1]) + square(yz[0])
    twist_sum = square(xy[2] + xz[1] + yz[0])
    corner = square(xyz[0]) + square(xyz[1]) + square(xyz[2])
    groups = dict(
        normal=normal, trace=trace, shear=shear, plus=plus, minus=minus, twist=twist, twist_sum=twist_sum, corner=corner
    )
    return sum(np.float32(weights[name]) * group for name, group in groups.items())


def line_weight(coord, count):
    def outside(distance):
        missing = jnp.maximum(REACH - distance, 0)
        return missing * (missing + 1) // 2

    whole = (REACH + 1) * (REACH + 1)
    return (whole - outside(coord) - outside(count - 1 - coord)).astype(jnp.float32)


def voxel_factor(density, solid, plane, first_row, total_z, total_y):
    rows, length = density.shape
    row = lax.broadcasted_iota(jnp.int32, (rows, length), 0) + first_row
    column = lax.broadcasted_iota(jnp.int32, (rows, length), 1)
    weight = line_weight(row, total_y) * line_weight(column, length)
    weight = weight * line_weight(jnp.full((rows, length), plane, jnp.int32), total_z)
    return solid.astype(jnp.float32) * (-3.0 * density * density) / weight


def spread_x(value):
    rows, length = value.shape
    wide = jnp.concatenate([value, jnp.zeros((rows, LANES), jnp.float32)], axis=1)
    span = length + LANES
    total = float(ROWS) * value
    for step in range(1, ROWS):
        both = pltpu.roll(wide, span - step, 1) + pltpu.roll(wide, step, 1)
        total = total + float(ROWS - step) * both[:, :length]
    return total


def spread_layers(layers):
    for step in (1, 2, 1, 2):
        layers = [layers[k] + layers[k + step] for k in range(len(layers) - step)]
    return layers


def held(disp, fixed, case, comp, z, rows):
    return disp[case, comp, z, rows] * (1.0 - fixed[z, rows].astype(jnp.float32))


def split_x(value):
    length = value.shape[1]
    column = lax.broadcasted_iota(jnp.int32, value.shape, 1)
    ahead = jnp.where(column == length - 1, 0.0, pltpu.roll(value, length - 1, 1))
    return value + ahead, ahead - value


def spread_y(quotient, ylen):
    rows = [quotient[TILE + step : TILE + step + ylen] for step in range(-REACH, REACH + 1)]
    return sum((ROWS - abs(k - REACH)) * rows[k] for k in range(2 * REACH + 1))


def to_neighbours(quotient, ylen):
    top = quotient[ylen : ylen + TILE]
    base = quotient[TILE : 2 * TILE]
    ahead, back = [], []
    for row in range(REACH):
        ahead.append(sum(float(REACH - row - k) * top[TILE - 1 - k : TILE - k] for k in range(REACH - row)))
        back.append(sum(float(row + 1 - k) * base[k : k + 1] for k in range(row + 1)))
    return ahead, back


def on_first():
    return lax.axis_index("load") == 0


def lead_kernel(totals, disp_hbm, fixed_hbm, density_hbm, solid_hbm, disp, fixed, density, solid, z_out, y_out, sems):
    loads, comps, zlen, ylen, _ = disp.shape
    gives = jnp.where(on_first(), 0, zlen - 1)
    arrays = ((disp_hbm, disp), (fixed_hbm, fixed), (density_hbm, density), (solid_hbm, solid))

    def copies(layer, sem):
        layer = lax.rem(layer, zlen)
        parts = [(source.at[:, :, layer], target.at[:, :, layer]) for source, target in arrays[:1]]
        parts += [(source.at[layer], target.at[layer]) for source, target in arrays[1:]]
        return [pltpu.make_async_copy(source, target, sems.at[sem, k]) for k, (source, target) in enumerate(parts)]

    started = [copies(gives + step, step) for step in range(zlen)]
    for group in started:
        for copy in group:
            copy.start()
    for copy in started[0]:
        copy.wait()
    plane = lax.axis_index("sz") * zlen + gives
    base_y = lax.axis_index("sy") * ylen
    z_out[loads * comps] = voxel_factor(density[gives], solid[gives], plane, base_y, *totals)
    for case in range(loads):
        for comp in range(comps):
            z_out[case * comps + comp] = held(disp, fixed, case, comp, gives, slice(None))
    for group in started[1:]:
        for copy in group:
            copy.wait()
    for case in range(loads):
        for comp in range(comps):
            for z in range(zlen):
                at = (comp * loads + case) * zlen + z
                y_out[at : at + 1] = held(disp, fixed, case, comp, z, slice(0, 1))


def tile_energies(plus, diff, first, lanes, layers, loads, comps, base=0):
    weights = mode_weights()

    def faces(k, z):
        near, far = slice(first, first + TILE), slice(first + 1, first + TILE + 1)
        whole, whole_next = plus[k, z, near, lanes], plus[k, z, far, lanes]
        change, change_next = diff[k, z, near, lanes], diff[k, z, far, lanes]
        return whole + whole_next, change + change_next, whole_next - whole, change_next - change

    energy = [None] * layers
    for case in range(loads):
        low = None
        for z in range(layers + 1):
            high = [faces(case * comps + comp, base + z) for comp in range(comps)]
            if low is not None:
                part = quadratic(low, high, weights)
                energy[z - 1] = part if energy[z - 1] is None else energy[z - 1] + part
            low = high
    return energy


def blank_last(value, first, ylen):
    row = lax.broadcasted_iota(jnp.int32, value.shape, 0) + first
    return jnp.where(row == ylen - 1, 0.0, value)


def inner_kernel(totals, disp, fixed, density, solid, own, line, sends, last_plus, last_diff, last_factor, edge, plus, diff, quotient):
    loads, comps, zlen, ylen, xlen = disp.shape
    total_z, total_y = totals
    base_z = lax.axis_index("sz") * zlen
    base_y = lax.axis_index("sy") * ylen
    inner = zlen - 1
    keeps = jnp.where(on_first(), inner, 0)

    @pl.loop(0, loads * comps)
    def _(k):
        case, comp = k // comps, k % comps
        for z in range(zlen):
            whole, change = split_x(held(disp, fixed, case, comp, z, slice(None)))
            plus[k, z, :ylen] = whole
            diff[k, z, :ylen] = change
        last_plus[k] = plus[k, keeps, :ylen]
        last_diff[k] = diff[k, keeps, :ylen]

    for comp in range(comps):
        for case in range(loads):
            for z in range(zlen):
                at = (comp * loads + case) * zlen + z
                line[0, at : at + 1] = plus[case * comps + comp, z, ylen - 1 : ylen]
                line[1, at : at + 1] = diff[case * comps + comp, z, ylen - 1 : ylen]

    zeros = jnp.zeros((TILE, xlen), jnp.float32)
    edge[...] = jnp.zeros(edge.shape, jnp.float32)
    for z in range(zlen):
        factor = voxel_factor(density[z], solid[z], base_z + z, base_y, total_z, total_y)
        edge[z : z + 1] = factor[ylen - 1 :]
        if z == inner:
            last_factor[...] = factor
        else:
            quotient[z, :TILE] = zeros
            quotient[z, TILE : TILE + ylen] = factor
            quotient[z, TILE + ylen :] = zeros

    for first in range(0, ylen, TILE):

        @pl.loop(0, xlen // LANES)
        def _(chunk):
            lanes = pl.ds(pl.multiple_of(chunk * LANES, LANES), LANES)
            energy = tile_energies(plus, diff, first, lanes, inner, loads, comps)
            for z in range(inner):
                here = quotient[z, first + TILE : first + 2 * TILE, lanes]
                quotient[z, first + TILE : first + 2 * TILE, lanes] = blank_last(energy[z] * here, first, ylen)

    for z in range(inner):
        own[z] = spread_x(spread_y(quotient.at[z], ylen))
        ahead, back = to_neighbours(quotient.at[z], ylen)
        ends = spread_x(jnp.concatenate(ahead + back + [zeros[:2]], axis=0))
        sends[0, REACH * z : REACH * (z + 1)] = ends[:REACH]
        sends[1, REACH * z : REACH * (z + 1)] = ends[REACH : 2 * REACH]


def outer_kernel(
    shape, z_in, y_in, disp, fixed, own_in, line, sends, last_plus, last_diff, last_factor, edge, own, known, a_out, b_out, plus, diff, quotient, factor
):
    loads, comps, zlen, ylen, xlen = shape
    planes = loads * comps
    inner = zlen - 1
    first_core, index = on_first(), lax.axis_index("sz")
    top = first_core & (index == lax.axis_size("sz") - 1)
    keeps = jnp.where(first_core, inner, 0)
    stays, comes = jnp.where(first_core, 0, 1), jnp.where(first_core, jnp.where(top, 2, 1), 0)
    for k in range(planes):
        plus[k, stays, :ylen] = last_plus[k]
        diff[k, stays, :ylen] = last_diff[k]
        whole, change = split_x(z_in[k])
        plus[k, comes, :ylen] = whole
        diff[k, comes, :ylen] = change
    below = jnp.where(index > 0, z_in[planes], 0.0)
    factor[...] = jnp.where(first_core, last_factor[...], below)

    @pl.when(top)
    def _():
        clamped = jnp.zeros((ylen + TILE, xlen), jnp.float32)
        for k in range(planes):
            for slot in (1, 3):
                plus[k, slot] = clamped
                diff[k, slot] = clamped

    zeros = jnp.zeros((TILE, xlen), jnp.float32)
    quotient[:TILE] = zeros
    quotient[TILE + ylen :] = zeros
    for first in range(0, ylen, TILE):

        @pl.loop(0, xlen // LANES)
        def _(chunk):
            lanes = pl.ds(pl.multiple_of(chunk * LANES, LANES), LANES)
            (energy,) = tile_energies(plus, diff, first, lanes, 1, loads, comps)
            here = energy * factor[first : first + TILE, lanes]
            quotient[first + TILE : first + 2 * TILE, lanes] = blank_last(here, first, ylen)

    @pl.when(top)
    def _():
        for first in range(0, ylen, TILE):

            @pl.loop(0, xlen // LANES)
            def _(chunk):
                lanes = pl.ds(pl.multiple_of(chunk * LANES, LANES), LANES)
                (energy,) = tile_energies(plus, diff, first, lanes, 1, loads, comps, base=2)
                here = energy * factor[first : first + TILE, lanes]
                quotient[first + TILE : first + 2 * TILE, lanes] += blank_last(here, first, ylen)

    count = loads * zlen
    more = lax.axis_index("sy") < lax.axis_size("sy") - 1
    low, high = [], []
    for comp in range(comps):
        part = slice(comp * count, (comp + 1) * count)
        whole, change = line[0, part], line[1, part]
        whole_next, change_next = split_x(jnp.where(more, y_in[part], 0.0))
        face = (whole + whole_next, change + change_next, whole_next - whole, change_next - change)
        low.append(face)
        high.append([pltpu.roll(value, count - 1, 0) for value in face])
    energy = quadratic(low, high, mode_weights())
    energy = sum(energy[case * zlen : case * zlen + inner] for case in range(loads)) * edge[:inner]
    last = spread_x(jnp.concatenate([energy, jnp.zeros((TILE - inner, xlen), jnp.float32)], axis=0))

    row = lax.broadcasted_iota(jnp.int32, (TILE, xlen), 0)
    rising = jnp.maximum(row - (TILE - 1 - ROWS), 0).astype(jnp.float32)
    ups, downs = [], []
    for z in range(inner):
        own[z] = own_in[z]
        own[z, ylen - TILE :] += rising * last[z : z + 1]
        here = sends[0, REACH * z : REACH * (z + 1)]
        ups += [here[r : r + 1] + float(REACH - r) * last[z : z + 1] for r in range(REACH)]
        downs.append(sends[1, REACH * z : REACH * (z + 1)])
    own[inner] = spread_x(spread_y(quotient, ylen))
    ahead, back = to_neighbours(quotient, ylen)
    ends = spread_x(jnp.concatenate(ahead + back + [zeros[:2]], axis=0))
    ups += [ends[: REACH - 1], factor[ylen - 1 :]]
    downs.append(ends[REACH : 2 * REACH])

    pairs = [(case, comp) for comp in range(comps) for case in range(loads)]
    here_last = [held(disp, fixed, case, comp, keeps, slice(ylen - 1, ylen)) for case, comp in pairs]
    here_first = [held(disp, fixed, case, comp, keeps, slice(0, 1)) for case, comp in pairs]
    next_row = [jnp.where(first_core, y_in[k * zlen + inner : (k + 1) * zlen], y_in[k * zlen : k * zlen + 1]) for k in range(planes)]
    next_row = [jnp.where(more, row, 0.0) for row in next_row]
    come_last = [z_in[case * comps + comp, ylen - 1 : ylen] for case, comp in pairs]
    come_first = [z_in[case * comps + comp, 0:1] for case, comp in pairs]
    rows = here_last + come_last + next_row + here_first + come_first + [factor[ylen - 1 :]]
    known[: len(rows)] = jnp.concatenate(rows, axis=0)
    known[len(rows) :] = jnp.zeros((known.shape[0] - len(rows), xlen), jnp.float32)
    up = jnp.concatenate(ups + here_last + come_last, axis=0)
    down = jnp.concatenate(downs + come_first + [jnp.zeros((planes, xlen), jnp.float32)], axis=0)
    even = lax.axis_index("sy") % 2 == 0
    a_out[...] = jnp.where(even, up, down)
    b_out[...] = jnp.where(even, down, up)


def rows_kernel(loads, comps, own, b_in, a_in, known, h_out, a_out, b_out):
    zlen, ylen, xlen = own.shape
    planes = loads * comps
    index, last = lax.axis_index("sy"), lax.axis_size("sy") - 1
    even = index % 2 == 0
    from_low = jnp.where(index > 0, jnp.where(even, b_in[...], a_in[...]), 0.0)
    from_high = jnp.where(index < last, jnp.where(even, a_in[...], b_in[...]), 0.0)
    ends = REACH * zlen
    first_core = jnp.logical_not(on_first())
    top = first_core & (lax.axis_index("sz") == lax.axis_size("sz") - 1)

    def nodes(first, second, comp):
        part = slice(comp * loads, (comp + 1) * loads)
        zero = jnp.zeros((loads, xlen), jnp.float32)
        (first, first_more), (second, second_more) = first, second
        pieces = [first, first_more, second, second_more]
        return split_x(jnp.concatenate([zero if piece is None else piece[part] for piece in pieces], axis=0))

    def under(stays, comes):
        return jnp.where(first_core, stays, comes), jnp.where(top, comes, 0.0)

    def over(stays, comes):
        return jnp.where(first_core, jnp.where(top, 0.0, comes), stays), None

    def face(near_own, near_in, far_own, far_in, comp):
        whole, change = nodes(near_own, near_in, comp)
        whole_next, change_next = nodes(far_own, far_in, comp)
        return whole + whole_next, change + change_next, whole_next - whole, change_next - change

    here_last, come_last, next_row, here_first, come_first = (known[planes * k : planes * (k + 1)] for k in range(5))
    low_last, low_come = from_low[ends : ends + planes], from_low[ends + planes : ends + 2 * planes]
    next_come = from_high[ends : ends + planes]
    corners = [(here_last, come_last), (low_last, low_come), (next_row, next_come), (here_first, come_first)]
    low = [face(*(under(*corner) for corner in corners), comp) for comp in range(comps)]
    high = [face(*(over(*corner) for corner in corners), comp) for comp in range(comps)]
    energy = quadratic(low, high, mode_weights())
    cases = 2 * loads
    lines = [sum(energy[cases * k + case : cases * k + case + 1] for case in range(cases)) for k in range(2)]
    lines = [lines[0] * known[5 * planes : 5 * planes + 1], lines[1] * from_low[ends - 1 : ends]]
    lines = spread_x(jnp.concatenate(lines + [jnp.zeros((TILE - 2, xlen), jnp.float32)], axis=0))

    row = lax.broadcasted_iota(jnp.int32, (TILE, xlen), 0)
    rising = jnp.maximum(row - (TILE - 1 - ROWS), 0).astype(jnp.float32)
    falling = jnp.maximum(REACH - row, 0).astype(jnp.float32)
    blank = jnp.zeros((TILE - REACH, xlen), jnp.float32)
    theirs = jnp.where(first_core, zlen, 0)
    h_out[zlen - theirs] = own[zlen - 1]
    h_out[theirs] = jnp.zeros((ylen, xlen), jnp.float32)
    for z in range(zlen):
        part = slice(REACH * z, REACH * (z + 1))
        head = jnp.concatenate([from_low[part], blank], axis=0)
        tail = jnp.concatenate([blank, from_high[part]], axis=0)
        at = z + 1
        if z == zlen - 1:
            head = jnp.where(row == REACH - 1, 0.0, head) + falling * lines[1:2]
            tail = tail + rising * lines[0:1]
            at = theirs
        else:
            h_out[at] = own[z]
        h_out[at, :TILE] += head
        h_out[at, ylen - TILE :] += tail
    high = (lax.axis_index("sz") % 2 == 0).astype(jnp.int32)
    a_out[...] = h_out[pl.ds(high, zlen)]
    b_out[...] = h_out[pl.ds(1 - high, zlen)]


def layers_kernel(h, a_in, b_in, out):
    zlen = out.shape[0]
    index, last = lax.axis_index("sz"), lax.axis_size("sz") - 1
    even = index % 2 == 0
    below = [jnp.where(index > 0, jnp.where(even, b_in[k], a_in[k]), 0.0) for k in range(zlen - REACH, zlen)]
    above = [jnp.where(index < last, jnp.where(even, a_in[k], b_in[k]), 0.0) for k in range(zlen)]
    layers = below[:-1] + [below[-1] + h[0]] + [h[z] for z in range(1, zlen)] + [h[zlen] + above[0]] + above[1:]
    for z, layer in enumerate(spread_layers(layers)):
        out[z] = layer


def sum_kernel(part, other, out):
    out[...] = part[...] + other[...]


def call(kernel, outs, args, scratch=(), space=pltpu.VMEM):
    shapes = [jax.ShapeDtypeStruct(out, jnp.float32) if isinstance(out, tuple) else out for out in outs]
    return pl.pallas_call(
        kernel,
        out_shape=shapes,
        in_specs=[pl.BlockSpec(memory_space=space)] * len(args),
        out_specs=[pl.BlockSpec(memory_space=pltpu.VMEM)] * len(outs),
        scratch_shapes=list(scratch),
        compiler_params=pltpu.CompilerParams(vmem_limit_bytes=32 * 1024 * 1024),
    )(*args)


def column_moved(value):
    size = lax.axis_size("sz")
    ring = list(range(size - 1, -1, -1)) + [size + k for k in range(size)]
    return lax.ppermute(value, ("load", "sz"), [(ring[k - 1], ring[k]) for k in range(len(ring))])


def ring_moved(value, axis):
    size = lax.axis_size(axis)
    return lax.ppermute(value, axis, [((k + 1) % size, k) for k in range(size)])


def swapped(value, axis, first, crossed=False):
    cores, size = lax.axis_size("load"), lax.axis_size(axis)
    pairs = []
    for core in range(cores):
        for k in range(size):
            other = k + 1 if (k - first) % 2 == 0 else k - 1
            inside = 0 <= other < size
            side = cores - 1 - core if crossed or not inside else core
            pairs.append((core * size + k, side * size + (other if inside else k)))
    return lax.ppermute(value, ("load", axis), pairs)


def chip_swapped(value):
    cores = lax.axis_size("load")
    return lax.ppermute(value, "load", [(core, cores - 1 - core) for core in range(cores)])


def body(displacements, density, solid, fixed):
    loads, comps, zlen, ylen, xlen = displacements.shape
    planes = loads * comps
    totals = (zlen * lax.axis_size("sz"), ylen * lax.axis_size("sy"))
    args = [
        pltpu.with_memory_space_constraint(arg, pltpu.HBM) for arg in (displacements, fixed, density, solid)
    ]

    disp, fixed, density, solid, z_send, y_send = call(
        lambda *refs: lead_kernel(totals, *refs),
        [jax.ShapeDtypeStruct(arg.shape, arg.dtype) for arg in args]
        + [(planes + 1, ylen, xlen), (planes * zlen, xlen)],
        args,
        scratch=[pltpu.SemaphoreType.DMA((zlen, len(args)))],
        space=pltpu.HBM,
    )
    z_in = column_moved(z_send)
    y_in = ring_moved(y_send, "sy")
    nodes = lambda layers: pltpu.VMEM((planes, layers, ylen + TILE, xlen), jnp.float32)
    inner = call(
        lambda *refs: inner_kernel(totals, *refs),
        [
            (zlen, ylen, xlen),
            (2, planes * zlen, xlen),
            (2, REACH * (zlen - 1), xlen),
            (planes, ylen, xlen),
            (planes, ylen, xlen),
            (ylen, xlen),
            (TILE, xlen),
        ],
        (disp, fixed, density, solid),
        scratch=[nodes(zlen), nodes(zlen), pltpu.VMEM((zlen - 1, ylen + 2 * TILE, xlen), jnp.float32)],
    )
    size = REACH * zlen + 2 * planes
    own, known, a_send, b_send = call(
        lambda *refs: outer_kernel(displacements.shape, *refs),
        [(zlen, ylen, xlen), (-(-(5 * planes + 1) // TILE) * TILE, xlen), (size, xlen), (size, xlen)],
        (z_in, y_in, disp, fixed, *inner),
        scratch=[
            nodes(4),
            nodes(4),
            pltpu.VMEM((ylen + 2 * TILE, xlen), jnp.float32),
            pltpu.VMEM((ylen, xlen), jnp.float32),
        ],
    )
    b_in = swapped(b_send, "sy", 1, crossed=True)
    a_in = swapped(a_send, "sy", 0, crossed=True)
    h, a_send, b_send = call(
        lambda *refs: rows_kernel(loads, comps, *refs),
        [(zlen + 1, ylen, xlen), (zlen, ylen, xlen), (zlen, ylen, xlen)],
        (own, b_in, a_in, chip_swapped(known)),
    )
    a_in = swapped(a_send, "sz", 0, crossed=True)
    b_in = swapped(b_send, "sz", 1, crossed=True)
    (part,) = call(layers_kernel, [(zlen, ylen, xlen)], (h, a_in, b_in))
    (out,) = call(sum_kernel, [(zlen, ylen, xlen)], (part, chip_swapped(part)))
    return out


def solution(mesh):
    return jax.shard_map(
        body,
        mesh=mesh,
        in_specs=(
            P("load", None, "sz", "sy", None),
            P("sz", "sy", None),
            P("sz", "sy", None),
            P("sz", "sy", None),
        ),
        out_specs=P("sz", "sy", None),
        check_vma=False,
    )
```

```python
import jax
import jax.numpy as jnp
import numpy as np
from jax import lax
from jax.experimental import pallas as pl
from jax.experimental.pallas import tpu as pltpu
from jax.sharding import PartitionSpec as P

OFFSETS = [(0, 0, 0), (1, 0, 0), (1, 1, 0), (0, 1, 0), (0, 0, 1), (1, 0, 1), (1, 1, 1), (0, 1, 1)]
REACH = 3
ROWS = REACH + 1
TILE = 8
LANES = 128


def element_matrix():
    corners = np.array(
        [
            [-1.0, -1.0, -1.0],
            [1.0, -1.0, -1.0],
            [1.0, 1.0, -1.0],
            [-1.0, 1.0, -1.0],
            [-1.0, -1.0, 1.0],
            [1.0, -1.0, 1.0],
            [1.0, 1.0, 1.0],
            [-1.0, 1.0, 1.0],
        ]
    )
    poisson = 0.3
    lame = poisson / ((1.0 + poisson) * (1.0 - 2.0 * poisson))
    shear = 1.0 / (2.0 * (1.0 + poisson))
    elastic = np.zeros((6, 6))
    elastic[:3, :3] = lame
    for k in range(3):
        elastic[k, k] += 2.0 * shear
        elastic[3 + k, 3 + k] = shear
    gauss = 1.0 / np.sqrt(3.0)
    stiffness = np.zeros((24, 24))
    for gi in range(2):
        for gj in range(2):
            for gk in range(2):
                point = np.array([(2 * gi - 1) * gauss, (2 * gj - 1) * gauss, (2 * gk - 1) * gauss])
                strain = np.zeros((6, 24))
                for node in range(8):
                    grads = np.zeros(3)
                    for k in range(3):
                        value = corners[node, k] / 8.0
                        for m in range(3):
                            if m != k:
                                value = value * (1.0 + point[m] * corners[node, m])
                        grads[k] = 2.0 * value
                    col = 3 * node
                    strain[0, col] = grads[0]
                    strain[1, col + 1] = grads[1]
                    strain[2, col + 2] = grads[2]
                    strain[3, col] = grads[1]
                    strain[3, col + 1] = grads[0]
                    strain[4, col + 1] = grads[2]
                    strain[4, col + 2] = grads[1]
                    strain[5, col] = grads[2]
                    strain[5, col + 2] = grads[0]
                stiffness += strain.T @ elastic @ strain / 8.0
    return stiffness


def mode_weights():
    modes = [(i, j, k) for k in (0, 1) for j in (0, 1) for i in (0, 1)]
    sums = np.zeros((24, 24))
    for m, mode in enumerate(modes):
        for n, corner in enumerate(OFFSETS):
            sign = np.prod([(1 if corner[d] else -1) if mode[d] else 1 for d in range(3)])
            for comp in range(3):
                sums[3 * m + comp, 3 * n + comp] = sign
    form = sums @ element_matrix() @ sums.T / 64.0

    def at(first, second):
        return form[3 * modes.index(first[1]) + first[0], 3 * modes.index(second[1]) + second[0]]

    ux, vy, uy = (0, (1, 0, 0)), (1, (0, 1, 0)), (0, (0, 1, 0))
    uxy, wyz = (0, (1, 1, 0)), (2, (0, 1, 1))
    wxy, vxz, uxyz = (2, (1, 1, 0)), (1, (1, 0, 1)), (0, (1, 1, 1))
    return dict(
        normal=at(ux, ux) - at(ux, vy),
        trace=at(ux, vy),
        shear=at(uy, uy),
        plus=(at(uxy, uxy) + at(uxy, wyz)) / 2,
        minus=(at(uxy, uxy) - at(uxy, wyz)) / 2,
        twist=at(wxy, wxy) - at(wxy, vxz),
        twist_sum=at(wxy, vxz),
        corner=at(uxyz, uxyz),
    )


def square(value):
    return value * value


def quadratic(low, high, weights):
    x = [low[c][1] + high[c][1] for c in range(3)]
    y = [low[c][2] + high[c][2] for c in range(3)]
    z = [high[c][0] - low[c][0] for c in range(3)]
    xy = [low[c][3] + high[c][3] for c in range(3)]
    xz = [high[c][1] - low[c][1] for c in range(3)]
    yz = [high[c][2] - low[c][2] for c in range(3)]
    xyz = [high[c][3] - low[c][3] for c in range(3)]
    normal = square(x[0]) + square(y[1]) + square(z[2])
    trace = square(x[0] + y[1] + z[2])
    shear = square(y[0] + x[1]) + square(z[0] + x[2]) + square(z[1] + y[2])
    pairs = ((xy[0], yz[2]), (xy[1], xz[2]), (xz[0], yz[1]))
    plus = sum(square(p + q) for p, q in pairs)
    minus = sum(square(p - q) for p, q in pairs)
    twist = square(xy[2]) + square(xz[1]) + square(yz[0])
    twist_sum = square(xy[2] + xz[1] + yz[0])
    corner = square(xyz[0]) + square(xyz[1]) + square(xyz[2])
    groups = dict(
        normal=normal, trace=trace, shear=shear, plus=plus, minus=minus, twist=twist, twist_sum=twist_sum, corner=corner
    )
    return sum(np.float32(weights[name]) * group for name, group in groups.items())


def line_weight(coord, count):
    def outside(distance):
        missing = jnp.maximum(REACH - distance, 0)
        return missing * (missing + 1) // 2

    whole = (REACH + 1) * (REACH + 1)
    return (whole - outside(coord) - outside(count - 1 - coord)).astype(jnp.float32)


def voxel_factor(density, solid, plane, first_row, total_z, total_y):
    rows, length = density.shape
    row = lax.broadcasted_iota(jnp.int32, (rows, length), 0) + first_row
    column = lax.broadcasted_iota(jnp.int32, (rows, length), 1)
    weight = line_weight(row, total_y) * line_weight(column, length)
    weight = weight * line_weight(jnp.full((rows, length), plane, jnp.int32), total_z)
    return solid.astype(jnp.float32) * (-3.0 * density * density) / weight


def spread_x(value):
    rows, length = value.shape
    wide = jnp.concatenate([value, jnp.zeros((rows, LANES), jnp.float32)], axis=1)
    span = length + LANES
    total = float(ROWS) * value
    for step in range(1, ROWS):
        both = pltpu.roll(wide, span - step, 1) + pltpu.roll(wide, step, 1)
        total = total + float(ROWS - step) * both[:, :length]
    return total


def spread_layers(layers):
    for step in (1, 2, 1, 2):
        layers = [layers[k] + layers[k + step] for k in range(len(layers) - step)]
    return layers


def held(disp, fixed, case, comp, z, rows):
    return disp[case, comp, z, rows] * (1.0 - fixed[z, rows].astype(jnp.float32))


def split_x(value):
    length = value.shape[1]
    column = lax.broadcasted_iota(jnp.int32, value.shape, 1)
    ahead = jnp.where(column == length - 1, 0.0, pltpu.roll(value, length - 1, 1))
    return value + ahead, ahead - value


def spread_y(quotient, ylen):
    rows = [quotient[TILE + step : TILE + step + ylen] for step in range(-REACH, REACH + 1)]
    return sum((ROWS - abs(k - REACH)) * rows[k] for k in range(2 * REACH + 1))


def to_neighbours(quotient, ylen):
    top = quotient[ylen : ylen + TILE]
    base = quotient[TILE : 2 * TILE]
    ahead, back = [], []
    for row in range(REACH):
        ahead.append(sum(float(REACH - row - k) * top[TILE - 1 - k : TILE - k] for k in range(REACH - row)))
        back.append(sum(float(row + 1 - k) * base[k : k + 1] for k in range(row + 1)))
    return ahead, back


def on_first():
    return lax.axis_index("load") == 0


def lead_kernel(totals, disp_hbm, fixed_hbm, density_hbm, solid_hbm, disp, fixed, density, solid, z_out, y_out, sems):
    loads, comps, zlen, ylen, _ = disp.shape
    copies = [
        pltpu.make_async_copy(source, target, sems.at[k])
        for k, (source, target) in enumerate(
            ((disp_hbm, disp), (fixed_hbm, fixed), (density_hbm, density), (solid_hbm, solid))
        )
    ]
    for copy in copies:
        copy.start()
    for copy in copies:
        copy.wait()
    gives = jnp.where(on_first(), 0, zlen - 1)
    plane = lax.axis_index("sz") * zlen + gives
    base_y = lax.axis_index("sy") * ylen
    z_out[loads * comps] = voxel_factor(density[gives], solid[gives], plane, base_y, *totals)
    for case in range(loads):
        for comp in range(comps):
            z_out[case * comps + comp] = held(disp, fixed, case, comp, gives, slice(None))
            for z in range(zlen):
                at = (comp * loads + case) * zlen + z
                y_out[at : at + 1] = held(disp, fixed, case, comp, z, slice(0, 1))


def tile_energies(plus, diff, first, lanes, layers, loads, comps, base=0):
    weights = mode_weights()

    def faces(k, z):
        near, far = slice(first, first + TILE), slice(first + 1, first + TILE + 1)
        whole, whole_next = plus[k, z, near, lanes], plus[k, z, far, lanes]
        change, change_next = diff[k, z, near, lanes], diff[k, z, far, lanes]
        return whole + whole_next, change + change_next, whole_next - whole, change_next - change

    energy = [None] * layers
    for case in range(loads):
        low = None
        for z in range(layers + 1):
            high = [faces(case * comps + comp, base + z) for comp in range(comps)]
            if low is not None:
                part = quadratic(low, high, weights)
                energy[z - 1] = part if energy[z - 1] is None else energy[z - 1] + part
            low = high
    return energy


def blank_last(value, first, ylen):
    row = lax.broadcasted_iota(jnp.int32, value.shape, 0) + first
    return jnp.where(row == ylen - 1, 0.0, value)


def inner_kernel(totals, disp, fixed, density, solid, own, line, sends, last_plus, last_diff, last_factor, edge, plus, diff, quotient):
    loads, comps, zlen, ylen, xlen = disp.shape
    total_z, total_y = totals
    base_z = lax.axis_index("sz") * zlen
    base_y = lax.axis_index("sy") * ylen
    inner = zlen - 1
    keeps = jnp.where(on_first(), inner, 0)

    @pl.loop(0, loads * comps)
    def _(k):
        case, comp = k // comps, k % comps
        for z in range(zlen):
            whole, change = split_x(held(disp, fixed, case, comp, z, slice(None)))
            plus[k, z, :ylen] = whole
            diff[k, z, :ylen] = change
        last_plus[k] = plus[k, keeps, :ylen]
        last_diff[k] = diff[k, keeps, :ylen]

    for comp in range(comps):
        for case in range(loads):
            for z in range(zlen):
                at = (comp * loads + case) * zlen + z
                line[0, at : at + 1] = plus[case * comps + comp, z, ylen - 1 : ylen]
                line[1, at : at + 1] = diff[case * comps + comp, z, ylen - 1 : ylen]

    zeros = jnp.zeros((TILE, xlen), jnp.float32)
    edge[...] = jnp.zeros(edge.shape, jnp.float32)
    for z in range(zlen):
        factor = voxel_factor(density[z], solid[z], base_z + z, base_y, total_z, total_y)
        edge[z : z + 1] = factor[ylen - 1 :]
        if z == inner:
            last_factor[...] = factor
        else:
            quotient[z, :TILE] = zeros
            quotient[z, TILE : TILE + ylen] = factor
            quotient[z, TILE + ylen :] = zeros

    for first in range(0, ylen, TILE):

        @pl.loop(0, xlen // LANES)
        def _(chunk):
            lanes = pl.ds(pl.multiple_of(chunk * LANES, LANES), LANES)
            energy = tile_energies(plus, diff, first, lanes, inner, loads, comps)
            for z in range(inner):
                here = quotient[z, first + TILE : first + 2 * TILE, lanes]
                quotient[z, first + TILE : first + 2 * TILE, lanes] = blank_last(energy[z] * here, first, ylen)

    for z in range(inner):
        own[z] = spread_x(spread_y(quotient.at[z], ylen))
        ahead, back = to_neighbours(quotient.at[z], ylen)
        ends = spread_x(jnp.concatenate(ahead + back + [zeros[:2]], axis=0))
        sends[0, REACH * z : REACH * (z + 1)] = ends[:REACH]
        sends[1, REACH * z : REACH * (z + 1)] = ends[REACH : 2 * REACH]


def outer_kernel(
    shape, z_in, y_in, disp, fixed, own_in, line, sends, last_plus, last_diff, last_factor, edge, own, known, a_out, b_out, plus, diff, quotient, factor
):
    loads, comps, zlen, ylen, xlen = shape
    planes = loads * comps
    inner = zlen - 1
    first_core, index = on_first(), lax.axis_index("sz")
    top = first_core & (index == lax.axis_size("sz") - 1)
    keeps = jnp.where(first_core, inner, 0)
    stays, comes = jnp.where(first_core, 0, 1), jnp.where(first_core, jnp.where(top, 2, 1), 0)
    for k in range(planes):
        plus[k, stays, :ylen] = last_plus[k]
        diff[k, stays, :ylen] = last_diff[k]
        whole, change = split_x(z_in[k])
        plus[k, comes, :ylen] = whole
        diff[k, comes, :ylen] = change
    below = jnp.where(index > 0, z_in[planes], 0.0)
    factor[...] = jnp.where(first_core, last_factor[...], below)

    @pl.when(top)
    def _():
        clamped = jnp.zeros((ylen + TILE, xlen), jnp.float32)
        for k in range(planes):
            for slot in (1, 3):
                plus[k, slot] = clamped
                diff[k, slot] = clamped

    zeros = jnp.zeros((TILE, xlen), jnp.float32)
    quotient[:TILE] = zeros
    quotient[TILE + ylen :] = zeros
    for first in range(0, ylen, TILE):

        @pl.loop(0, xlen // LANES)
        def _(chunk):
            lanes = pl.ds(pl.multiple_of(chunk * LANES, LANES), LANES)
            (energy,) = tile_energies(plus, diff, first, lanes, 1, loads, comps)
            here = energy * factor[first : first + TILE, lanes]
            quotient[first + TILE : first + 2 * TILE, lanes] = blank_last(here, first, ylen)

    @pl.when(top)
    def _():
        for first in range(0, ylen, TILE):

            @pl.loop(0, xlen // LANES)
            def _(chunk):
                lanes = pl.ds(pl.multiple_of(chunk * LANES, LANES), LANES)
                (energy,) = tile_energies(plus, diff, first, lanes, 1, loads, comps, base=2)
                here = energy * factor[first : first + TILE, lanes]
                quotient[first + TILE : first + 2 * TILE, lanes] += blank_last(here, first, ylen)

    count = loads * zlen
    more = lax.axis_index("sy") < lax.axis_size("sy") - 1
    low, high = [], []
    for comp in range(comps):
        part = slice(comp * count, (comp + 1) * count)
        whole, change = line[0, part], line[1, part]
        whole_next, change_next = split_x(jnp.where(more, y_in[part], 0.0))
        face = (whole + whole_next, change + change_next, whole_next - whole, change_next - change)
        low.append(face)
        high.append([pltpu.roll(value, count - 1, 0) for value in face])
    energy = quadratic(low, high, mode_weights())
    energy = sum(energy[case * zlen : case * zlen + inner] for case in range(loads)) * edge[:inner]
    last = spread_x(jnp.concatenate([energy, jnp.zeros((TILE - inner, xlen), jnp.float32)], axis=0))

    row = lax.broadcasted_iota(jnp.int32, (TILE, xlen), 0)
    rising = jnp.maximum(row - (TILE - 1 - ROWS), 0).astype(jnp.float32)
    ups, downs = [], []
    for z in range(inner):
        own[z] = own_in[z]
        own[z, ylen - TILE :] += rising * last[z : z + 1]
        here = sends[0, REACH * z : REACH * (z + 1)]
        ups += [here[r : r + 1] + float(REACH - r) * last[z : z + 1] for r in range(REACH)]
        downs.append(sends[1, REACH * z : REACH * (z + 1)])
    own[inner] = spread_x(spread_y(quotient, ylen))
    ahead, back = to_neighbours(quotient, ylen)
    ends = spread_x(jnp.concatenate(ahead + back + [zeros[:2]], axis=0))
    ups += [ends[: REACH - 1], factor[ylen - 1 :]]
    downs.append(ends[REACH : 2 * REACH])

    pairs = [(case, comp) for comp in range(comps) for case in range(loads)]
    here_last = [held(disp, fixed, case, comp, keeps, slice(ylen - 1, ylen)) for case, comp in pairs]
    here_first = [held(disp, fixed, case, comp, keeps, slice(0, 1)) for case, comp in pairs]
    next_row = [jnp.where(first_core, y_in[k * zlen + inner : (k + 1) * zlen], y_in[k * zlen : k * zlen + 1]) for k in range(planes)]
    next_row = [jnp.where(more, row, 0.0) for row in next_row]
    come_last = [z_in[case * comps + comp, ylen - 1 : ylen] for case, comp in pairs]
    come_first = [z_in[case * comps + comp, 0:1] for case, comp in pairs]
    rows = here_last + come_last + next_row + here_first + come_first + [factor[ylen - 1 :]]
    known[: len(rows)] = jnp.concatenate(rows, axis=0)
    known[len(rows) :] = jnp.zeros((known.shape[0] - len(rows), xlen), jnp.float32)
    up = jnp.concatenate(ups + here_last + come_last, axis=0)
    down = jnp.concatenate(downs + come_first + [jnp.zeros((planes, xlen), jnp.float32)], axis=0)
    even = lax.axis_index("sy") % 2 == 0
    a_out[...] = jnp.where(even, up, down)
    b_out[...] = jnp.where(even, down, up)


def rows_kernel(loads, comps, own, known, b_in, a_in, h_out):
    zlen, ylen, xlen = own.shape
    planes = loads * comps
    index, last = lax.axis_index("sy"), lax.axis_size("sy") - 1
    even = index % 2 == 0
    from_low = jnp.where(index > 0, jnp.where(even, b_in[...], a_in[...]), 0.0)
    from_high = jnp.where(index < last, jnp.where(even, a_in[...], b_in[...]), 0.0)
    ends = REACH * zlen
    first_core = on_first()
    top = first_core & (lax.axis_index("sz") == lax.axis_size("sz") - 1)

    def nodes(first, second, comp):
        part = slice(comp * loads, (comp + 1) * loads)
        zero = jnp.zeros((loads, xlen), jnp.float32)
        (first, first_more), (second, second_more) = first, second
        pieces = [first, first_more, second, second_more]
        return split_x(jnp.concatenate([zero if piece is None else piece[part] for piece in pieces], axis=0))

    def under(stays, comes):
        return jnp.where(first_core, stays, comes), jnp.where(top, comes, 0.0)

    def over(stays, comes):
        return jnp.where(first_core, jnp.where(top, 0.0, comes), stays), None

    def face(near_own, near_in, far_own, far_in, comp):
        whole, change = nodes(near_own, near_in, comp)
        whole_next, change_next = nodes(far_own, far_in, comp)
        return whole + whole_next, change + change_next, whole_next - whole, change_next - change

    here_last, come_last, next_row, here_first, come_first = (known[planes * k : planes * (k + 1)] for k in range(5))
    low_last, low_come = from_low[ends : ends + planes], from_low[ends + planes : ends + 2 * planes]
    next_come = from_high[ends : ends + planes]
    corners = [(here_last, come_last), (low_last, low_come), (next_row, next_come), (here_first, come_first)]
    low = [face(*(under(*corner) for corner in corners), comp) for comp in range(comps)]
    high = [face(*(over(*corner) for corner in corners), comp) for comp in range(comps)]
    energy = quadratic(low, high, mode_weights())
    cases = 2 * loads
    lines = [sum(energy[cases * k + case : cases * k + case + 1] for case in range(cases)) for k in range(2)]
    lines = [lines[0] * known[5 * planes : 5 * planes + 1], lines[1] * from_low[ends - 1 : ends]]
    lines = spread_x(jnp.concatenate(lines + [jnp.zeros((TILE - 2, xlen), jnp.float32)], axis=0))

    row = lax.broadcasted_iota(jnp.int32, (TILE, xlen), 0)
    rising = jnp.maximum(row - (TILE - 1 - ROWS), 0).astype(jnp.float32)
    falling = jnp.maximum(REACH - row, 0).astype(jnp.float32)
    blank = jnp.zeros((TILE - REACH, xlen), jnp.float32)
    between = jnp.where(first_core, zlen, 0)
    h_out[zlen - between] = jnp.zeros((ylen, xlen), jnp.float32)
    for z in range(zlen):
        part = slice(REACH * z, REACH * (z + 1))
        head = jnp.concatenate([from_low[part], blank], axis=0)
        tail = jnp.concatenate([blank, from_high[part]], axis=0)
        at = z + 1
        if z == zlen - 1:
            head = jnp.where(row == REACH - 1, 0.0, head) + falling * lines[1:2]
            tail = tail + rising * lines[0:1]
            at = between
        h_out[at] = own[z]
        h_out[at, :TILE] += head
        h_out[at, ylen - TILE :] += tail


def total_kernel(h, other, h_out, z_out):
    for k in range(h.shape[0]):
        h_out[k] = h[k] + other[k]
    z_out[...] = h_out[pl.ds(jnp.where(on_first(), 0, 1), z_out.shape[0])]


def layers_kernel(h, z_in, out):
    zlen = out.shape[0]
    first_core = on_first()
    inside = lax.axis_index("sz") > 0, lax.axis_index("sz") < lax.axis_size("sz") - 1
    under, over = jnp.logical_not(first_core) & inside[0], first_core & inside[1]
    below = [jnp.where(under, z_in[k], 0.0) for k in range(zlen - REACH, zlen)]
    above = [jnp.where(over, z_in[k], 0.0) for k in range(zlen)]
    own = [jnp.where(first_core, h[k], 0.0) for k in range(zlen + 1)]
    layers = below[:-1] + [below[-1] + own[0]] + own[1:-1] + [own[-1] + above[0]] + above[1:]
    for z, layer in enumerate(spread_layers(layers)):
        out[z] = layer


def sum_kernel(part, other, out):
    out[...] = part[...] + other[...]


def call(kernel, outs, args, scratch=(), space=pltpu.VMEM):
    shapes = [jax.ShapeDtypeStruct(out, jnp.float32) if isinstance(out, tuple) else out for out in outs]
    return pl.pallas_call(
        kernel,
        out_shape=shapes,
        in_specs=[pl.BlockSpec(memory_space=space)] * len(args),
        out_specs=[pl.BlockSpec(memory_space=pltpu.VMEM)] * len(outs),
        scratch_shapes=list(scratch),
        compiler_params=pltpu.CompilerParams(vmem_limit_bytes=32 * 1024 * 1024),
    )(*args)


def column_moved(value):
    size = lax.axis_size("sz")
    ring = list(range(size - 1, -1, -1)) + [size + k for k in range(size)]
    return lax.ppermute(value, ("load", "sz"), [(ring[k - 1], ring[k]) for k in range(len(ring))])


def ring_moved(value, axis):
    size = lax.axis_size(axis)
    return lax.ppermute(value, axis, [((k + 1) % size, k) for k in range(size)])


def swapped(value, axis, first):
    cores, size = lax.axis_size("load"), lax.axis_size(axis)
    pairs = []
    for core in range(cores):
        for k in range(size):
            other = k + 1 if (k - first) % 2 == 0 else k - 1
            inside = 0 <= other < size
            side = core if inside else cores - 1 - core
            pairs.append((core * size + k, side * size + (other if inside else k)))
    return lax.ppermute(value, ("load", axis), pairs)


def chip_swapped(value):
    cores = lax.axis_size("load")
    return lax.ppermute(value, "load", [(core, cores - 1 - core) for core in range(cores)])


def body(displacements, density, solid, fixed):
    loads, comps, zlen, ylen, xlen = displacements.shape
    planes = loads * comps
    totals = (zlen * lax.axis_size("sz"), ylen * lax.axis_size("sy"))
    args = [
        pltpu.with_memory_space_constraint(arg, pltpu.HBM) for arg in (displacements, fixed, density, solid)
    ]

    disp, fixed, density, solid, z_send, y_send = call(
        lambda *refs: lead_kernel(totals, *refs),
        [jax.ShapeDtypeStruct(arg.shape, arg.dtype) for arg in args]
        + [(planes + 1, ylen, xlen), (planes * zlen, xlen)],
        args,
        scratch=[pltpu.SemaphoreType.DMA((len(args),))],
        space=pltpu.HBM,
    )
    z_in = column_moved(z_send)
    y_in = ring_moved(y_send, "sy")
    nodes = lambda layers: pltpu.VMEM((planes, layers, ylen + TILE, xlen), jnp.float32)
    inner = call(
        lambda *refs: inner_kernel(totals, *refs),
        [
            (zlen, ylen, xlen),
            (2, planes * zlen, xlen),
            (2, REACH * (zlen - 1), xlen),
            (planes, ylen, xlen),
            (planes, ylen, xlen),
            (ylen, xlen),
            (TILE, xlen),
        ],
        (disp, fixed, density, solid),
        scratch=[nodes(zlen), nodes(zlen), pltpu.VMEM((zlen - 1, ylen + 2 * TILE, xlen), jnp.float32)],
    )
    size = REACH * zlen + 2 * planes
    own, known, a_send, b_send = call(
        lambda *refs: outer_kernel(displacements.shape, *refs),
        [(zlen, ylen, xlen), (-(-(5 * planes + 1) // TILE) * TILE, xlen), (size, xlen), (size, xlen)],
        (z_in, y_in, disp, fixed, *inner),
        scratch=[
            nodes(4),
            nodes(4),
            pltpu.VMEM((ylen + 2 * TILE, xlen), jnp.float32),
            pltpu.VMEM((ylen, xlen), jnp.float32),
        ],
    )
    b_in = swapped(b_send, "sy", 1)
    a_in = swapped(a_send, "sy", 0)
    (h,) = call(
        lambda *refs: rows_kernel(loads, comps, *refs), [(zlen + 1, ylen, xlen)], (own, known, b_in, a_in)
    )
    h, z_send = call(total_kernel, [(zlen + 1, ylen, xlen), (zlen, ylen, xlen)], (h, chip_swapped(h)))
    (part,) = call(layers_kernel, [(zlen, ylen, xlen)], (h, column_moved(z_send)))
    (out,) = call(sum_kernel, [(zlen, ylen, xlen)], (part, chip_swapped(part)))
    return out


def solution(mesh):
    return jax.shard_map(
        body,
        mesh=mesh,
        in_specs=(
            P("load", None, "sz", "sy", None),
            P("sz", "sy", None),
            P("sz", "sy", None),
            P("sz", "sy", None),
        ),
        out_specs=P("sz", "sy", None),
        check_vma=False,
    )
```

```python
import jax
import jax.numpy as jnp
import numpy as np
from jax import lax
from jax.experimental import pallas as pl
from jax.experimental.pallas import tpu as pltpu
from jax.sharding import PartitionSpec as P

OFFSETS = [(0, 0, 0), (1, 0, 0), (1, 1, 0), (0, 1, 0), (0, 0, 1), (1, 0, 1), (1, 1, 1), (0, 1, 1)]
REACH = 3
ROWS = REACH + 1
TILE = 8
LANES = 128


def element_matrix():
    corners = np.array(
        [
            [-1.0, -1.0, -1.0],
            [1.0, -1.0, -1.0],
            [1.0, 1.0, -1.0],
            [-1.0, 1.0, -1.0],
            [-1.0, -1.0, 1.0],
            [1.0, -1.0, 1.0],
            [1.0, 1.0, 1.0],
            [-1.0, 1.0, 1.0],
        ]
    )
    poisson = 0.3
    lame = poisson / ((1.0 + poisson) * (1.0 - 2.0 * poisson))
    shear = 1.0 / (2.0 * (1.0 + poisson))
    elastic = np.zeros((6, 6))
    elastic[:3, :3] = lame
    for k in range(3):
        elastic[k, k] += 2.0 * shear
        elastic[3 + k, 3 + k] = shear
    gauss = 1.0 / np.sqrt(3.0)
    stiffness = np.zeros((24, 24))
    for gi in range(2):
        for gj in range(2):
            for gk in range(2):
                point = np.array([(2 * gi - 1) * gauss, (2 * gj - 1) * gauss, (2 * gk - 1) * gauss])
                strain = np.zeros((6, 24))
                for node in range(8):
                    grads = np.zeros(3)
                    for k in range(3):
                        value = corners[node, k] / 8.0
                        for m in range(3):
                            if m != k:
                                value = value * (1.0 + point[m] * corners[node, m])
                        grads[k] = 2.0 * value
                    col = 3 * node
                    strain[0, col] = grads[0]
                    strain[1, col + 1] = grads[1]
                    strain[2, col + 2] = grads[2]
                    strain[3, col] = grads[1]
                    strain[3, col + 1] = grads[0]
                    strain[4, col + 1] = grads[2]
                    strain[4, col + 2] = grads[1]
                    strain[5, col] = grads[2]
                    strain[5, col + 2] = grads[0]
                stiffness += strain.T @ elastic @ strain / 8.0
    return stiffness


def mode_weights():
    modes = [(i, j, k) for k in (0, 1) for j in (0, 1) for i in (0, 1)]
    sums = np.zeros((24, 24))
    for m, mode in enumerate(modes):
        for n, corner in enumerate(OFFSETS):
            sign = np.prod([(1 if corner[d] else -1) if mode[d] else 1 for d in range(3)])
            for comp in range(3):
                sums[3 * m + comp, 3 * n + comp] = sign
    form = sums @ element_matrix() @ sums.T / 64.0

    def at(first, second):
        return form[3 * modes.index(first[1]) + first[0], 3 * modes.index(second[1]) + second[0]]

    ux, vy, uy = (0, (1, 0, 0)), (1, (0, 1, 0)), (0, (0, 1, 0))
    uxy, wyz = (0, (1, 1, 0)), (2, (0, 1, 1))
    wxy, vxz, uxyz = (2, (1, 1, 0)), (1, (1, 0, 1)), (0, (1, 1, 1))
    return dict(
        normal=at(ux, ux) - at(ux, vy),
        trace=at(ux, vy),
        shear=at(uy, uy),
        plus=(at(uxy, uxy) + at(uxy, wyz)) / 2,
        minus=(at(uxy, uxy) - at(uxy, wyz)) / 2,
        twist=at(wxy, wxy) - at(wxy, vxz),
        twist_sum=at(wxy, vxz),
        corner=at(uxyz, uxyz),
    )


def square(value):
    return value * value


def quadratic(low, high, weights):
    x = [low[c][1] + high[c][1] for c in range(3)]
    y = [low[c][2] + high[c][2] for c in range(3)]
    z = [high[c][0] - low[c][0] for c in range(3)]
    xy = [low[c][3] + high[c][3] for c in range(3)]
    xz = [high[c][1] - low[c][1] for c in range(3)]
    yz = [high[c][2] - low[c][2] for c in range(3)]
    xyz = [high[c][3] - low[c][3] for c in range(3)]
    normal = square(x[0]) + square(y[1]) + square(z[2])
    trace = square(x[0] + y[1] + z[2])
    shear = square(y[0] + x[1]) + square(z[0] + x[2]) + square(z[1] + y[2])
    pairs = ((xy[0], yz[2]), (xy[1], xz[2]), (xz[0], yz[1]))
    plus = sum(square(p + q) for p, q in pairs)
    minus = sum(square(p - q) for p, q in pairs)
    twist = square(xy[2]) + square(xz[1]) + square(yz[0])
    twist_sum = square(xy[2] + xz[1] + yz[0])
    corner = square(xyz[0]) + square(xyz[1]) + square(xyz[2])
    groups = dict(
        normal=normal, trace=trace, shear=shear, plus=plus, minus=minus, twist=twist, twist_sum=twist_sum, corner=corner
    )
    return sum(np.float32(weights[name]) * group for name, group in groups.items())


def line_weight(coord, count):
    def outside(distance):
        missing = jnp.maximum(REACH - distance, 0)
        return missing * (missing + 1) // 2

    whole = (REACH + 1) * (REACH + 1)
    return (whole - outside(coord) - outside(count - 1 - coord)).astype(jnp.float32)


def voxel_factor(density, solid, plane, first_row, total_z, total_y):
    rows, length = density.shape
    row = lax.broadcasted_iota(jnp.int32, (rows, length), 0) + first_row
    column = lax.broadcasted_iota(jnp.int32, (rows, length), 1)
    weight = line_weight(row, total_y) * line_weight(column, length)
    weight = weight * line_weight(jnp.full((rows, length), plane, jnp.int32), total_z)
    return solid.astype(jnp.float32) * (-3.0 * density * density) / weight


def spread_x(value):
    rows, length = value.shape
    wide = jnp.concatenate([value, jnp.zeros((rows, LANES), jnp.float32)], axis=1)
    span = length + LANES
    total = float(ROWS) * value
    for step in range(1, ROWS):
        both = pltpu.roll(wide, span - step, 1) + pltpu.roll(wide, step, 1)
        total = total + float(ROWS - step) * both[:, :length]
    return total


def spread_layers(layers):
    for step in (1, 2, 1, 2):
        layers = [layers[k] + layers[k + step] for k in range(len(layers) - step)]
    return layers


def held(disp, fixed, case, comp, z, rows):
    return disp[case, comp, z, rows] * (1.0 - fixed[z, rows].astype(jnp.float32))


def split_x(value):
    length = value.shape[1]
    column = lax.broadcasted_iota(jnp.int32, value.shape, 1)
    ahead = jnp.where(column == length - 1, 0.0, pltpu.roll(value, length - 1, 1))
    return value + ahead, ahead - value


def spread_y(quotient, ylen):
    rows = [quotient[TILE + step : TILE + step + ylen] for step in range(-REACH, REACH + 1)]
    return sum((ROWS - abs(k - REACH)) * rows[k] for k in range(2 * REACH + 1))


def to_neighbours(quotient, ylen):
    top = quotient[ylen : ylen + TILE]
    base = quotient[TILE : 2 * TILE]
    ahead, back = [], []
    for row in range(REACH):
        ahead.append(sum(float(REACH - row - k) * top[TILE - 1 - k : TILE - k] for k in range(REACH - row)))
        back.append(sum(float(row + 1 - k) * base[k : k + 1] for k in range(row + 1)))
    return ahead, back


def on_first():
    return lax.axis_index("load") == 0


def lead_kernel(totals, disp_hbm, fixed_hbm, density_hbm, solid_hbm, disp, fixed, density, solid, d_out, z_out, y_out, sems):
    loads, comps, zlen, ylen, _ = disp.shape
    copies = [
        pltpu.make_async_copy(source, target, sems.at[k])
        for k, (source, target) in enumerate(
            ((disp_hbm, disp), (fixed_hbm, fixed), (density_hbm, density), (solid_hbm, solid))
        )
    ]
    for copy in copies:
        copy.start()
    for copy in copies:
        copy.wait()
    gives = jnp.where(on_first(), 0, zlen - 1)
    plane = lax.axis_index("sz") * zlen + gives
    base_y = lax.axis_index("sy") * ylen
    d_out[...] = jnp.zeros(d_out.shape, jnp.float32)
    z_out[loads * comps] = voxel_factor(density[gives], solid[gives], plane, base_y, *totals)
    for case in range(loads):
        for comp in range(comps):
            k = case * comps + comp
            z_out[k] = held(disp, fixed, case, comp, gives, slice(None))
            d_out[k : k + 1] = z_out[k, :1]
            for z in range(zlen):
                at = (comp * loads + case) * zlen + z
                y_out[at : at + 1] = held(disp, fixed, case, comp, z, slice(0, 1))


def tile_energies(plus, diff, first, lanes, layers, loads, comps, base=0):
    weights = mode_weights()

    def faces(k, z):
        near, far = slice(first, first + TILE), slice(first + 1, first + TILE + 1)
        whole, whole_next = plus[k, z, near, lanes], plus[k, z, far, lanes]
        change, change_next = diff[k, z, near, lanes], diff[k, z, far, lanes]
        return whole + whole_next, change + change_next, whole_next - whole, change_next - change

    energy = [None] * layers
    for case in range(loads):
        low = None
        for z in range(layers + 1):
            high = [faces(case * comps + comp, base + z) for comp in range(comps)]
            if low is not None:
                part = quadratic(low, high, weights)
                energy[z - 1] = part if energy[z - 1] is None else energy[z - 1] + part
            low = high
    return energy


def blank_last(value, first, ylen):
    row = lax.broadcasted_iota(jnp.int32, value.shape, 0) + first
    return jnp.where(row == ylen - 1, 0.0, value)


def inner_kernel(totals, disp, fixed, density, solid, own, line, sends, last_plus, last_diff, last_factor, edge, plus, diff, quotient):
    loads, comps, zlen, ylen, xlen = disp.shape
    total_z, total_y = totals
    base_z = lax.axis_index("sz") * zlen
    base_y = lax.axis_index("sy") * ylen
    inner = zlen - 1
    keeps = jnp.where(on_first(), inner, 0)

    @pl.loop(0, loads * comps)
    def _(k):
        case, comp = k // comps, k % comps
        for z in range(zlen):
            whole, change = split_x(held(disp, fixed, case, comp, z, slice(None)))
            plus[k, z, :ylen] = whole
            diff[k, z, :ylen] = change
        last_plus[k] = plus[k, keeps, :ylen]
        last_diff[k] = diff[k, keeps, :ylen]

    for comp in range(comps):
        for case in range(loads):
            for z in range(zlen):
                at = (comp * loads + case) * zlen + z
                line[0, at : at + 1] = plus[case * comps + comp, z, ylen - 1 : ylen]
                line[1, at : at + 1] = diff[case * comps + comp, z, ylen - 1 : ylen]

    zeros = jnp.zeros((TILE, xlen), jnp.float32)
    edge[...] = jnp.zeros(edge.shape, jnp.float32)
    for z in range(zlen):
        factor = voxel_factor(density[z], solid[z], base_z + z, base_y, total_z, total_y)
        edge[z : z + 1] = factor[ylen - 1 :]
        if z == inner:
            last_factor[...] = factor
        else:
            quotient[z, :TILE] = zeros
            quotient[z, TILE : TILE + ylen] = factor
            quotient[z, TILE + ylen :] = zeros

    for first in range(0, ylen, TILE):

        @pl.loop(0, xlen // LANES)
        def _(chunk):
            lanes = pl.ds(pl.multiple_of(chunk * LANES, LANES), LANES)
            energy = tile_energies(plus, diff, first, lanes, inner, loads, comps)
            for z in range(inner):
                here = quotient[z, first + TILE : first + 2 * TILE, lanes]
                quotient[z, first + TILE : first + 2 * TILE, lanes] = blank_last(energy[z] * here, first, ylen)

    for z in range(inner):
        own[z] = spread_x(spread_y(quotient.at[z], ylen))
        ahead, back = to_neighbours(quotient.at[z], ylen)
        ends = spread_x(jnp.concatenate(ahead + back + [zeros[:2]], axis=0))
        sends[0, REACH * z : REACH * (z + 1)] = ends[:REACH]
        sends[1, REACH * z : REACH * (z + 1)] = ends[REACH : 2 * REACH]


def outer_kernel(
    shape, d_in, z_in, y_in, own_in, line, sends, last_plus, last_diff, last_factor, edge, share, plus, diff, quotient, factor
):
    loads, comps, zlen, ylen, xlen = shape
    planes = loads * comps
    inner = zlen - 1
    first_core, index = on_first(), lax.axis_index("sz")
    top = first_core & (index == lax.axis_size("sz") - 1)
    more = lax.axis_index("sy") < lax.axis_size("sy") - 1
    stays, comes = jnp.where(first_core, 0, 1), jnp.where(first_core, jnp.where(top, 2, 1), 0)
    y_rows = jnp.where(more, y_in[...], 0.0)
    y_plus, y_diff = split_x(y_rows)
    d_plus, d_diff = split_x(jnp.where(more, d_in[...], 0.0))
    for k in range(planes):
        case, comp = k // comps, k % comps
        at = (comp * loads + case) * zlen
        beside = jnp.where(first_core, y_plus[at + inner : at + zlen], y_plus[at : at + 1])
        beside_diff = jnp.where(first_core, y_diff[at + inner : at + zlen], y_diff[at : at + 1])
        plus[k, stays, :ylen] = last_plus[k]
        diff[k, stays, :ylen] = last_diff[k]
        plus[k, stays, ylen : ylen + 1] = beside
        diff[k, stays, ylen : ylen + 1] = beside_diff
        whole, change = split_x(z_in[k])
        plus[k, comes, :ylen] = whole
        diff[k, comes, :ylen] = change
        plus[k, comes, ylen : ylen + 1] = d_plus[k : k + 1]
        diff[k, comes, ylen : ylen + 1] = d_diff[k : k + 1]
    below = jnp.where(index > 0, z_in[planes], 0.0)
    factor[...] = jnp.where(first_core, last_factor[...], below)

    @pl.when(top)
    def _():
        clamped = jnp.zeros((ylen + TILE, xlen), jnp.float32)
        for k in range(planes):
            for slot in (1, 3):
                plus[k, slot] = clamped
                diff[k, slot] = clamped

    zeros = jnp.zeros((TILE, xlen), jnp.float32)
    quotient[:TILE] = zeros
    quotient[TILE + ylen :] = zeros
    for first in range(0, ylen, TILE):

        @pl.loop(0, xlen // LANES)
        def _(chunk):
            lanes = pl.ds(pl.multiple_of(chunk * LANES, LANES), LANES)
            (energy,) = tile_energies(plus, diff, first, lanes, 1, loads, comps)
            quotient[first + TILE : first + 2 * TILE, lanes] = energy * factor[first : first + TILE, lanes]

    @pl.when(top)
    def _():
        for first in range(0, ylen, TILE):

            @pl.loop(0, xlen // LANES)
            def _(chunk):
                lanes = pl.ds(pl.multiple_of(chunk * LANES, LANES), LANES)
                (energy,) = tile_energies(plus, diff, first, lanes, 1, loads, comps, base=2)
                quotient[first + TILE : first + 2 * TILE, lanes] += energy * factor[first : first + TILE, lanes]

    count = loads * zlen
    low, high = [], []
    for comp in range(comps):
        part = slice(comp * count, (comp + 1) * count)
        whole, change = line[0, part], line[1, part]
        whole_next, change_next = y_plus[part], y_diff[part]
        face = (whole + whole_next, change + change_next, whole_next - whole, change_next - change)
        low.append(face)
        high.append([pltpu.roll(value, count - 1, 0) for value in face])
    energy = quadratic(low, high, mode_weights())
    energy = sum(energy[case * zlen : case * zlen + inner] for case in range(loads)) * edge[:inner]
    last = spread_x(jnp.concatenate([energy, jnp.zeros((TILE - inner, xlen), jnp.float32)], axis=0))

    row = lax.broadcasted_iota(jnp.int32, (TILE, xlen), 0)
    rising = jnp.maximum(row - (TILE - 1 - ROWS), 0).astype(jnp.float32)
    ups, downs = [], []
    for z in range(inner):
        share[ylen * z : ylen * (z + 1)] = own_in[z]
        share[ylen * (z + 1) - TILE : ylen * (z + 1)] += rising * last[z : z + 1]
        here = sends[0, REACH * z : REACH * (z + 1)]
        ups += [here[r : r + 1] + float(REACH - r) * last[z : z + 1] for r in range(REACH)]
        downs.append(sends[1, REACH * z : REACH * (z + 1)])
    share[ylen * inner : ylen * zlen] = spread_x(spread_y(quotient, ylen))
    ahead, back = to_neighbours(quotient, ylen)
    ends = spread_x(jnp.concatenate(ahead + back + [zeros[:2]], axis=0))
    share[ylen * zlen :] = jnp.concatenate(ups + [ends[:REACH]] + downs + [ends[REACH : 2 * REACH]], axis=0)


def total_kernel(shape, share, other, h_out, z_out, y_out, d_out, e_out):
    _, _, zlen, ylen, xlen = shape
    first_core = on_first()
    inner, rows = zlen - 1, ylen * zlen
    reach = REACH * zlen

    def layers(first, count):
        mine, theirs = share[first + inner * count : first + zlen * count], other[first + inner * count : first + zlen * count]
        middle = share[first : first + inner * count] + other[first : first + inner * count]
        return jnp.where(first_core, theirs, mine), middle, jnp.where(first_core, mine, theirs)

    lowest, middle, highest = layers(0, ylen)
    h_out[0] = lowest
    for z in range(inner):
        h_out[z + 1] = middle[ylen * z : ylen * (z + 1)]
    h_out[zlen] = highest
    z_out[...] = h_out[pl.ds(jnp.where(first_core, 0, 1), zlen)]
    ups = jnp.concatenate(layers(rows, REACH), axis=0)
    downs = jnp.concatenate(layers(rows + reach, REACH), axis=0)
    blank = jnp.zeros((y_out.shape[0] - reach - REACH, xlen), jnp.float32)
    y_out[...] = jnp.concatenate([jnp.where(first_core, downs, ups), blank], axis=0)
    d_out[...] = jnp.where(first_core, downs[:reach], ups[REACH:])
    e_out[...] = jnp.where(first_core, ups[:reach], downs[REACH:])


def layers_kernel(h, z_in, y_in, d_in, e_in, out):
    zlen, ylen, xlen = out.shape
    reach = REACH * zlen
    first_core = on_first()
    z_index, z_last = lax.axis_index("sz"), lax.axis_size("sz") - 1
    y_index, y_last = lax.axis_index("sy"), lax.axis_size("sy") - 1
    z_side = jnp.where(first_core, z_index < z_last, z_index > 0)
    y_side = jnp.where(first_core, y_index < y_last, y_index > 0)
    y_other = jnp.where(first_core, y_index > 0, y_index < y_last)
    blank = jnp.zeros((TILE - REACH, xlen), jnp.float32)

    def at_start(rows):
        return jnp.concatenate([rows, blank], axis=0)

    def at_end(rows):
        return jnp.concatenate([blank, rows], axis=0)

    def ends(rows, keep, at_last):
        rows = jnp.where(keep, rows, 0.0)
        return at_start(jnp.where(at_last, 0.0, rows)), at_end(jnp.where(at_last, rows, 0.0))

    def with_ends(layer, *pairs):
        head, tail = layer[:TILE], layer[ylen - TILE :]
        for first, last in pairs:
            head, tail = head + first, tail + last
        return jnp.concatenate([head, layer[TILE : ylen - TILE], tail] if ylen > 2 * TILE else [head, tail], axis=0)

    own = []
    for k in range(zlen + 1):
        layer = jnp.where(first_core, h[k], 0.0)
        own.append(with_ends(layer, ends(y_in[REACH * k : REACH * (k + 1)], y_side, first_core)))
    come = []
    for k in range(zlen):
        part = slice(REACH * k, REACH * (k + 1))
        layer = jnp.where(z_side, z_in[k], 0.0)
        straight = ends(d_in[part], z_side & y_side, first_core)
        across = ends(e_in[part], z_side & y_other, jnp.logical_not(first_core))
        come.append(with_ends(layer, straight, across))
    below = [jnp.where(first_core, 0.0, layer) for layer in come[zlen - REACH :]]
    above = [jnp.where(first_core, layer, 0.0) for layer in come]
    layers = below[:-1] + [below[-1] + own[0]] + own[1:-1] + [own[-1] + above[0]] + above[1:]
    for z, layer in enumerate(spread_layers(layers)):
        out[z] = layer


def sum_kernel(part, other, out):
    out[...] = part[...] + other[...]


def call(kernel, outs, args, scratch=(), space=pltpu.VMEM):
    shapes = [jax.ShapeDtypeStruct(out, jnp.float32) if isinstance(out, tuple) else out for out in outs]
    return pl.pallas_call(
        kernel,
        out_shape=shapes,
        in_specs=[pl.BlockSpec(memory_space=space)] * len(args),
        out_specs=[pl.BlockSpec(memory_space=pltpu.VMEM)] * len(outs),
        scratch_shapes=list(scratch),
        compiler_params=pltpu.CompilerParams(vmem_limit_bytes=32 * 1024 * 1024),
    )(*args)


def ring_moved(value, axis):
    size = lax.axis_size(axis)
    return lax.ppermute(value, axis, [((k + 1) % size, k) for k in range(size)])


def chip_swapped(value):
    cores = lax.axis_size("load")
    return lax.ppermute(value, "load", [(core, cores - 1 - core) for core in range(cores)])


def opposed(value, z_step, y_step, y_shift=0):
    cores, rows, size = lax.axis_size("load"), lax.axis_size("sy"), lax.axis_size("sz")
    pairs = []
    for core in range(cores):
        sign = -1 if core else 1
        for y in range(rows):
            for z in range(size):
                to_y, to_z, side = y + sign * y_step, z + sign * z_step, core
                if not (0 <= to_y < rows and 0 <= to_z < size):
                    to_y, to_z, side = y, z, cores - 1 - core
                to_y = (to_y + y_shift) % rows
                pairs.append(((core * rows + y) * size + z, (side * rows + to_y) * size + to_z))
    return lax.ppermute(value, ("load", "sy", "sz"), pairs)


def body(displacements, density, solid, fixed):
    loads, comps, zlen, ylen, xlen = displacements.shape
    planes = loads * comps
    totals = (zlen * lax.axis_size("sz"), ylen * lax.axis_size("sy"))
    args = [
        pltpu.with_memory_space_constraint(arg, pltpu.HBM) for arg in (displacements, fixed, density, solid)
    ]

    disp, fixed, density, solid, d_send, z_send, y_send = call(
        lambda *refs: lead_kernel(totals, *refs),
        [jax.ShapeDtypeStruct(arg.shape, arg.dtype) for arg in args]
        + [(-(-planes // TILE) * TILE, xlen), (planes + 1, ylen, xlen), (planes * zlen, xlen)],
        args,
        scratch=[pltpu.SemaphoreType.DMA((len(args),))],
        space=pltpu.HBM,
    )
    d_in = opposed(d_send, -1, 0, y_shift=-1)
    z_in = opposed(z_send, -1, 0)
    y_in = ring_moved(y_send, "sy")
    nodes = lambda layers: pltpu.VMEM((planes, layers, ylen + TILE, xlen), jnp.float32)
    inner = call(
        lambda *refs: inner_kernel(totals, *refs),
        [
            (zlen, ylen, xlen),
            (2, planes * zlen, xlen),
            (2, REACH * (zlen - 1), xlen),
            (planes, ylen, xlen),
            (planes, ylen, xlen),
            (ylen, xlen),
            (TILE, xlen),
        ],
        (disp, fixed, density, solid),
        scratch=[nodes(zlen), nodes(zlen), pltpu.VMEM((zlen - 1, ylen + 2 * TILE, xlen), jnp.float32)],
    )
    reach = REACH * zlen
    (share,) = call(
        lambda *refs: outer_kernel(displacements.shape, *refs),
        [(ylen * zlen + 2 * reach, xlen)],
        (d_in, z_in, y_in, *inner),
        scratch=[
            nodes(4),
            nodes(4),
            pltpu.VMEM((ylen + 2 * TILE, xlen), jnp.float32),
            pltpu.VMEM((ylen, xlen), jnp.float32),
        ],
    )
    h, z_send, y_send, d_send, e_send = call(
        lambda *refs: total_kernel(displacements.shape, *refs),
        [
            (zlen + 1, ylen, xlen),
            (zlen, ylen, xlen),
            (-(-(reach + REACH) // TILE) * TILE, xlen),
            (reach, xlen),
            (reach, xlen),
        ],
        (share, chip_swapped(share)),
    )
    d_in = opposed(d_send, -1, -1)
    e_in = opposed(e_send, -1, 1)
    y_in = opposed(y_send, 0, -1)
    z_in = opposed(z_send, -1, 0)
    (part,) = call(layers_kernel, [(zlen, ylen, xlen)], (h, z_in, y_in, d_in, e_in))
    (out,) = call(sum_kernel, [(zlen, ylen, xlen)], (part, chip_swapped(part)))
    return out


def solution(mesh):
    return jax.shard_map(
        body,
        mesh=mesh,
        in_specs=(
            P("load", None, "sz", "sy", None),
            P("sz", "sy", None),
            P("sz", "sy", None),
            P("sz", "sy", None),
        ),
        out_specs=P("sz", "sy", None),
        check_vma=False,
    )
```

```python
import jax
import jax.numpy as jnp
import numpy as np
from jax import lax
from jax.experimental import pallas as pl
from jax.experimental.pallas import tpu as pltpu
from jax.sharding import PartitionSpec as P

OFFSETS = [(0, 0, 0), (1, 0, 0), (1, 1, 0), (0, 1, 0), (0, 0, 1), (1, 0, 1), (1, 1, 1), (0, 1, 1)]
REACH = 3
ROWS = REACH + 1
TILE = 8
LANES = 128


def element_matrix():
    corners = np.array(
        [
            [-1.0, -1.0, -1.0],
            [1.0, -1.0, -1.0],
            [1.0, 1.0, -1.0],
            [-1.0, 1.0, -1.0],
            [-1.0, -1.0, 1.0],
            [1.0, -1.0, 1.0],
            [1.0, 1.0, 1.0],
            [-1.0, 1.0, 1.0],
        ]
    )
    poisson = 0.3
    lame = poisson / ((1.0 + poisson) * (1.0 - 2.0 * poisson))
    shear = 1.0 / (2.0 * (1.0 + poisson))
    elastic = np.zeros((6, 6))
    elastic[:3, :3] = lame
    for k in range(3):
        elastic[k, k] += 2.0 * shear
        elastic[3 + k, 3 + k] = shear
    gauss = 1.0 / np.sqrt(3.0)
    stiffness = np.zeros((24, 24))
    for gi in range(2):
        for gj in range(2):
            for gk in range(2):
                point = np.array([(2 * gi - 1) * gauss, (2 * gj - 1) * gauss, (2 * gk - 1) * gauss])
                strain = np.zeros((6, 24))
                for node in range(8):
                    grads = np.zeros(3)
                    for k in range(3):
                        value = corners[node, k] / 8.0
                        for m in range(3):
                            if m != k:
                                value = value * (1.0 + point[m] * corners[node, m])
                        grads[k] = 2.0 * value
                    col = 3 * node
                    strain[0, col] = grads[0]
                    strain[1, col + 1] = grads[1]
                    strain[2, col + 2] = grads[2]
                    strain[3, col] = grads[1]
                    strain[3, col + 1] = grads[0]
                    strain[4, col + 1] = grads[2]
                    strain[4, col + 2] = grads[1]
                    strain[5, col] = grads[2]
                    strain[5, col + 2] = grads[0]
                stiffness += strain.T @ elastic @ strain / 8.0
    return stiffness


def mode_weights():
    modes = [(i, j, k) for k in (0, 1) for j in (0, 1) for i in (0, 1)]
    sums = np.zeros((24, 24))
    for m, mode in enumerate(modes):
        for n, corner in enumerate(OFFSETS):
            sign = np.prod([(1 if corner[d] else -1) if mode[d] else 1 for d in range(3)])
            for comp in range(3):
                sums[3 * m + comp, 3 * n + comp] = sign
    form = sums @ element_matrix() @ sums.T / 64.0

    def at(first, second):
        return form[3 * modes.index(first[1]) + first[0], 3 * modes.index(second[1]) + second[0]]

    ux, vy, uy = (0, (1, 0, 0)), (1, (0, 1, 0)), (0, (0, 1, 0))
    uxy, wyz = (0, (1, 1, 0)), (2, (0, 1, 1))
    wxy, vxz, uxyz = (2, (1, 1, 0)), (1, (1, 0, 1)), (0, (1, 1, 1))
    return dict(
        normal=at(ux, ux) - at(ux, vy),
        trace=at(ux, vy),
        shear=at(uy, uy),
        plus=(at(uxy, uxy) + at(uxy, wyz)) / 2,
        minus=(at(uxy, uxy) - at(uxy, wyz)) / 2,
        twist=at(wxy, wxy) - at(wxy, vxz),
        twist_sum=at(wxy, vxz),
        corner=at(uxyz, uxyz),
    )


def square(value):
    return value * value


def quadratic(low, high, weights):
    x = [low[c][1] + high[c][1] for c in range(3)]
    y = [low[c][2] + high[c][2] for c in range(3)]
    z = [high[c][0] - low[c][0] for c in range(3)]
    xy = [low[c][3] + high[c][3] for c in range(3)]
    xz = [high[c][1] - low[c][1] for c in range(3)]
    yz = [high[c][2] - low[c][2] for c in range(3)]
    xyz = [high[c][3] - low[c][3] for c in range(3)]
    normal = square(x[0]) + square(y[1]) + square(z[2])
    trace = square(x[0] + y[1] + z[2])
    shear = square(y[0] + x[1]) + square(z[0] + x[2]) + square(z[1] + y[2])
    pairs = ((xy[0], yz[2]), (xy[1], xz[2]), (xz[0], yz[1]))
    plus = sum(square(p + q) for p, q in pairs)
    minus = sum(square(p - q) for p, q in pairs)
    twist = square(xy[2]) + square(xz[1]) + square(yz[0])
    twist_sum = square(xy[2] + xz[1] + yz[0])
    corner = square(xyz[0]) + square(xyz[1]) + square(xyz[2])
    groups = dict(
        normal=normal, trace=trace, shear=shear, plus=plus, minus=minus, twist=twist, twist_sum=twist_sum, corner=corner
    )
    return sum(np.float32(weights[name]) * group for name, group in groups.items())


def line_weight(coord, count):
    def outside(distance):
        missing = jnp.maximum(REACH - distance, 0)
        return missing * (missing + 1) // 2

    whole = (REACH + 1) * (REACH + 1)
    return (whole - outside(coord) - outside(count - 1 - coord)).astype(jnp.float32)


def voxel_factor(density, solid, plane, first_row, total_z, total_y):
    rows, length = density.shape
    row = lax.broadcasted_iota(jnp.int32, (rows, length), 0) + first_row
    column = lax.broadcasted_iota(jnp.int32, (rows, length), 1)
    weight = line_weight(row, total_y) * line_weight(column, length)
    weight = weight * line_weight(jnp.full((rows, length), plane, jnp.int32), total_z)
    return solid.astype(jnp.float32) * (-3.0 * density * density) / weight


def spread_x(value):
    rows, length = value.shape
    wide = jnp.concatenate([value, jnp.zeros((rows, LANES), jnp.float32)], axis=1)
    span = length + LANES
    total = float(ROWS) * value
    for step in range(1, ROWS):
        both = pltpu.roll(wide, span - step, 1) + pltpu.roll(wide, step, 1)
        total = total + float(ROWS - step) * both[:, :length]
    return total


def spread_layers(layers):
    for step in (1, 2, 1, 2):
        layers = [layers[k] + layers[k + step] for k in range(len(layers) - step)]
    return layers


def held(disp, fixed, case, comp, z, rows):
    return disp[case, comp, z, rows] * (1.0 - fixed[z, rows].astype(jnp.float32))


def split_x(value):
    length = value.shape[1]
    column = lax.broadcasted_iota(jnp.int32, value.shape, 1)
    ahead = jnp.where(column == length - 1, 0.0, pltpu.roll(value, length - 1, 1))
    return value + ahead, ahead - value


def spread_y(quotient, ylen):
    rows = [quotient[TILE + step : TILE + step + ylen] for step in range(-REACH, REACH + 1)]
    return sum((ROWS - abs(k - REACH)) * rows[k] for k in range(2 * REACH + 1))


def to_neighbours(quotient, ylen):
    top = quotient[ylen : ylen + TILE]
    base = quotient[TILE : 2 * TILE]
    ahead, back = [], []
    for row in range(REACH):
        ahead.append(sum(float(REACH - row - k) * top[TILE - 1 - k : TILE - k] for k in range(REACH - row)))
        back.append(sum(float(row + 1 - k) * base[k : k + 1] for k in range(row + 1)))
    return ahead, back


def on_first():
    return lax.axis_index("load") == 0


def lead_kernel(totals, disp_hbm, fixed_hbm, density_hbm, solid_hbm, disp, fixed, density, solid, d_out, z_out, y_out, sems):
    loads, comps, zlen, ylen, _ = disp.shape
    copies = [
        pltpu.make_async_copy(source, target, sems.at[k])
        for k, (source, target) in enumerate(
            ((disp_hbm, disp), (fixed_hbm, fixed), (density_hbm, density), (solid_hbm, solid))
        )
    ]
    for copy in copies:
        copy.start()
    for copy in copies:
        copy.wait()
    gives = jnp.where(on_first(), 0, zlen - 1)
    plane = lax.axis_index("sz") * zlen + gives
    base_y = lax.axis_index("sy") * ylen
    d_out[...] = jnp.zeros(d_out.shape, jnp.float32)
    z_out[loads * comps] = voxel_factor(density[gives], solid[gives], plane, base_y, *totals)
    for case in range(loads):
        for comp in range(comps):
            k = case * comps + comp
            z_out[k] = held(disp, fixed, case, comp, gives, slice(None))
            d_out[k : k + 1] = z_out[k, :1]
            for z in range(zlen):
                at = (comp * loads + case) * zlen + z
                y_out[at : at + 1] = held(disp, fixed, case, comp, z, slice(0, 1))


def tile_energies(plus, diff, first, lanes, layers, loads, comps, base=0):
    weights = mode_weights()

    def faces(k, z):
        near, far = slice(first, first + TILE), slice(first + 1, first + TILE + 1)
        whole, whole_next = plus[k, z, near, lanes], plus[k, z, far, lanes]
        change, change_next = diff[k, z, near, lanes], diff[k, z, far, lanes]
        return whole + whole_next, change + change_next, whole_next - whole, change_next - change

    energy = [None] * layers
    for case in range(loads):
        low = None
        for z in range(layers + 1):
            high = [faces(case * comps + comp, base + z) for comp in range(comps)]
            if low is not None:
                part = quadratic(low, high, weights)
                energy[z - 1] = part if energy[z - 1] is None else energy[z - 1] + part
            low = high
    return energy


def blank_last(value, first, ylen):
    row = lax.broadcasted_iota(jnp.int32, value.shape, 0) + first
    return jnp.where(row == ylen - 1, 0.0, value)


def inner_kernel(totals, disp, fixed, density, solid, own, line, sends, last_plus, last_diff, last_factor, edge, plus, diff, quotient):
    loads, comps, zlen, ylen, xlen = disp.shape
    total_z, total_y = totals
    base_z = lax.axis_index("sz") * zlen
    base_y = lax.axis_index("sy") * ylen
    inner = zlen - 1
    keeps = jnp.where(on_first(), inner, 0)

    @pl.loop(0, loads * comps)
    def _(k):
        case, comp = k // comps, k % comps
        for z in range(zlen):
            whole, change = split_x(held(disp, fixed, case, comp, z, slice(None)))
            plus[k, z, :ylen] = whole
            diff[k, z, :ylen] = change
        last_plus[k] = plus[k, keeps, :ylen]
        last_diff[k] = diff[k, keeps, :ylen]

    for comp in range(comps):
        for case in range(loads):
            for z in range(zlen):
                at = (comp * loads + case) * zlen + z
                line[0, at : at + 1] = plus[case * comps + comp, z, ylen - 1 : ylen]
                line[1, at : at + 1] = diff[case * comps + comp, z, ylen - 1 : ylen]

    zeros = jnp.zeros((TILE, xlen), jnp.float32)
    edge[...] = jnp.zeros(edge.shape, jnp.float32)
    for z in range(zlen):
        factor = voxel_factor(density[z], solid[z], base_z + z, base_y, total_z, total_y)
        edge[z : z + 1] = factor[ylen - 1 :]
        if z == inner:
            last_factor[...] = factor
        else:
            quotient[z, :TILE] = zeros
            quotient[z, TILE : TILE + ylen] = factor
            quotient[z, TILE + ylen :] = zeros

    for first in range(0, ylen, TILE):

        @pl.loop(0, xlen // LANES)
        def _(chunk):
            lanes = pl.ds(pl.multiple_of(chunk * LANES, LANES), LANES)
            energy = tile_energies(plus, diff, first, lanes, inner, loads, comps)
            for z in range(inner):
                here = quotient[z, first + TILE : first + 2 * TILE, lanes]
                quotient[z, first + TILE : first + 2 * TILE, lanes] = blank_last(energy[z] * here, first, ylen)

    for z in range(inner):
        own[z] = spread_x(spread_y(quotient.at[z], ylen))
        ahead, back = to_neighbours(quotient.at[z], ylen)
        ends = spread_x(jnp.concatenate(ahead + back + [zeros[:2]], axis=0))
        sends[0, REACH * z : REACH * (z + 1)] = ends[:REACH]
        sends[1, REACH * z : REACH * (z + 1)] = ends[REACH : 2 * REACH]


def outer_kernel(
    shape, d_in, z_in, y_in, own_in, line, sends, last_plus, last_diff, last_factor, edge, share, plus, diff, quotient, factor
):
    loads, comps, zlen, ylen, xlen = shape
    planes = loads * comps
    inner = zlen - 1
    first_core, index = on_first(), lax.axis_index("sz")
    top = first_core & (index == lax.axis_size("sz") - 1)
    more = lax.axis_index("sy") < lax.axis_size("sy") - 1
    stays, comes = jnp.where(first_core, 0, 1), jnp.where(first_core, jnp.where(top, 2, 1), 0)
    y_rows = jnp.where(more, y_in[...], 0.0)
    y_plus, y_diff = split_x(y_rows)
    d_plus, d_diff = split_x(jnp.where(more, d_in[...], 0.0))
    for k in range(planes):
        case, comp = k // comps, k % comps
        at = (comp * loads + case) * zlen
        beside = jnp.where(first_core, y_plus[at + inner : at + zlen], y_plus[at : at + 1])
        beside_diff = jnp.where(first_core, y_diff[at + inner : at + zlen], y_diff[at : at + 1])
        plus[k, stays, :ylen] = last_plus[k]
        diff[k, stays, :ylen] = last_diff[k]
        plus[k, stays, ylen : ylen + 1] = beside
        diff[k, stays, ylen : ylen + 1] = beside_diff
        whole, change = split_x(z_in[k])
        plus[k, comes, :ylen] = whole
        diff[k, comes, :ylen] = change
        plus[k, comes, ylen : ylen + 1] = d_plus[k : k + 1]
        diff[k, comes, ylen : ylen + 1] = d_diff[k : k + 1]
    below = jnp.where(index > 0, z_in[planes], 0.0)
    factor[...] = jnp.where(first_core, last_factor[...], below)

    @pl.when(top)
    def _():
        clamped = jnp.zeros((ylen + TILE, xlen), jnp.float32)
        for k in range(planes):
            for slot in (1, 3):
                plus[k, slot] = clamped
                diff[k, slot] = clamped

    zeros = jnp.zeros((TILE, xlen), jnp.float32)
    quotient[:TILE] = zeros
    quotient[TILE + ylen :] = zeros
    for first in range(0, ylen, TILE):

        @pl.loop(0, xlen // LANES)
        def _(chunk):
            lanes = pl.ds(pl.multiple_of(chunk * LANES, LANES), LANES)
            (energy,) = tile_energies(plus, diff, first, lanes, 1, loads, comps)
            quotient[first + TILE : first + 2 * TILE, lanes] = energy * factor[first : first + TILE, lanes]

    @pl.when(top)
    def _():
        for first in range(0, ylen, TILE):

            @pl.loop(0, xlen // LANES)
            def _(chunk):
                lanes = pl.ds(pl.multiple_of(chunk * LANES, LANES), LANES)
                (energy,) = tile_energies(plus, diff, first, lanes, 1, loads, comps, base=2)
                quotient[first + TILE : first + 2 * TILE, lanes] += energy * factor[first : first + TILE, lanes]

    count = loads * zlen
    low, high = [], []
    for comp in range(comps):
        part = slice(comp * count, (comp + 1) * count)
        whole, change = line[0, part], line[1, part]
        whole_next, change_next = y_plus[part], y_diff[part]
        face = (whole + whole_next, change + change_next, whole_next - whole, change_next - change)
        low.append(face)
        high.append([pltpu.roll(value, count - 1, 0) for value in face])
    energy = quadratic(low, high, mode_weights())
    energy = sum(energy[case * zlen : case * zlen + inner] for case in range(loads)) * edge[:inner]
    last = spread_x(jnp.concatenate([energy, jnp.zeros((TILE - inner, xlen), jnp.float32)], axis=0))

    row = lax.broadcasted_iota(jnp.int32, (TILE, xlen), 0)
    rising = jnp.maximum(row - (TILE - 1 - ROWS), 0).astype(jnp.float32)
    ups, downs = [], []
    for z in range(inner):
        share[ylen * z : ylen * (z + 1)] = own_in[z]
        share[ylen * (z + 1) - TILE : ylen * (z + 1)] += rising * last[z : z + 1]
        here = sends[0, REACH * z : REACH * (z + 1)]
        ups += [here[r : r + 1] + float(REACH - r) * last[z : z + 1] for r in range(REACH)]
        downs.append(sends[1, REACH * z : REACH * (z + 1)])
    share[ylen * inner : ylen * zlen] = spread_x(spread_y(quotient, ylen))
    ahead, back = to_neighbours(quotient, ylen)
    ends = spread_x(jnp.concatenate(ahead + back + [zeros[:2]], axis=0))
    share[ylen * zlen :] = jnp.concatenate(ups + [ends[:REACH]] + downs + [ends[REACH : 2 * REACH]], axis=0)


def total_kernel(shape, share, other, h_out, d_out, e_out, y_out, *z_outs):
    _, _, zlen, ylen, xlen = shape
    first_core = on_first()
    inner, rows = zlen - 1, ylen * zlen
    reach = REACH * zlen

    def layers(first, count):
        mine, theirs = share[first + inner * count : first + zlen * count], other[first + inner * count : first + zlen * count]
        middle = share[first : first + inner * count] + other[first : first + inner * count]
        return jnp.where(first_core, theirs, mine), middle, jnp.where(first_core, mine, theirs)

    lowest, middle, highest = layers(0, ylen)
    h_out[0] = lowest
    for z in range(inner):
        h_out[z + 1] = middle[ylen * z : ylen * (z + 1)]
    h_out[zlen] = highest
    for k, z_out in enumerate(z_outs):
        z_out[...] = h_out[jnp.where(first_core, k, k + 1)]
    ups = jnp.concatenate(layers(rows, REACH), axis=0)
    downs = jnp.concatenate(layers(rows + reach, REACH), axis=0)
    y_out[: reach + REACH] = jnp.where(first_core, downs, ups)
    for out, used in ((y_out, reach + REACH), (d_out, reach), (e_out, reach)):
        out[used:] = jnp.zeros((out.shape[0] - used, xlen), jnp.float32)
    d_out[:reach] = jnp.where(first_core, downs[:reach], ups[REACH:])
    e_out[:reach] = jnp.where(first_core, ups[:reach], downs[REACH:])


def layers_kernel(h, d_in, e_in, y_in, *rest):
    *z_in, out = rest
    zlen, ylen, xlen = out.shape
    first_core = on_first()
    z_index, z_last = lax.axis_index("sz"), lax.axis_size("sz") - 1
    y_index, y_last = lax.axis_index("sy"), lax.axis_size("sy") - 1
    z_side = jnp.where(first_core, z_index < z_last, z_index > 0)
    y_side = jnp.where(first_core, y_index < y_last, y_index > 0)
    y_other = jnp.where(first_core, y_index > 0, y_index < y_last)
    blank = jnp.zeros((TILE - REACH, xlen), jnp.float32)

    def at_start(rows):
        return jnp.concatenate([rows, blank], axis=0)

    def at_end(rows):
        return jnp.concatenate([blank, rows], axis=0)

    def ends(rows, keep, at_last):
        rows = jnp.where(keep, rows, 0.0)
        return at_start(jnp.where(at_last, 0.0, rows)), at_end(jnp.where(at_last, rows, 0.0))

    def with_ends(layer, *pairs):
        head, tail = layer[:TILE], layer[ylen - TILE :]
        for first, last in pairs:
            head, tail = head + first, tail + last
        return jnp.concatenate([head, layer[TILE : ylen - TILE], tail] if ylen > 2 * TILE else [head, tail], axis=0)

    own = []
    for k in range(zlen + 1):
        layer = jnp.where(first_core, h[k], 0.0)
        own.append(with_ends(layer, ends(y_in[REACH * k : REACH * (k + 1)], y_side, first_core)))
    come = []
    for k in range(zlen):
        part = slice(REACH * k, REACH * (k + 1))
        layer = jnp.where(z_side, z_in[k][...], 0.0)
        straight = ends(d_in[part], z_side & y_side, first_core)
        across = ends(e_in[part], z_side & y_other, jnp.logical_not(first_core))
        come.append(with_ends(layer, straight, across))
    below = [jnp.where(first_core, 0.0, layer) for layer in come[zlen - REACH :]]
    above = [jnp.where(first_core, layer, 0.0) for layer in come]
    layers = below[:-1] + [below[-1] + own[0]] + own[1:-1] + [own[-1] + above[0]] + above[1:]
    for z, layer in enumerate(spread_layers(layers)):
        out[z] = layer


def sum_kernel(part, other, out):
    out[...] = part[...] + other[...]


def call(kernel, outs, args, scratch=(), space=pltpu.VMEM):
    shapes = [jax.ShapeDtypeStruct(out, jnp.float32) if isinstance(out, tuple) else out for out in outs]
    return pl.pallas_call(
        kernel,
        out_shape=shapes,
        in_specs=[pl.BlockSpec(memory_space=space)] * len(args),
        out_specs=[pl.BlockSpec(memory_space=pltpu.VMEM)] * len(outs),
        scratch_shapes=list(scratch),
        compiler_params=pltpu.CompilerParams(vmem_limit_bytes=32 * 1024 * 1024),
    )(*args)


def ring_moved(value, axis):
    size = lax.axis_size(axis)
    return lax.ppermute(value, axis, [((k + 1) % size, k) for k in range(size)])


def chip_swapped(value):
    cores = lax.axis_size("load")
    return lax.ppermute(value, "load", [(core, cores - 1 - core) for core in range(cores)])


def opposed(value, z_step, y_step, y_shift=0):
    cores, rows, size = lax.axis_size("load"), lax.axis_size("sy"), lax.axis_size("sz")
    pairs = []
    for core in range(cores):
        sign = -1 if core else 1
        for y in range(rows):
            for z in range(size):
                to_y, to_z, side = y + sign * y_step, z + sign * z_step, core
                if not (0 <= to_y < rows and 0 <= to_z < size):
                    to_y, to_z, side = y, z, cores - 1 - core
                to_y = (to_y + y_shift) % rows
                pairs.append(((core * rows + y) * size + z, (side * rows + to_y) * size + to_z))
    return lax.ppermute(value, ("load", "sy", "sz"), pairs)


def body(displacements, density, solid, fixed):
    loads, comps, zlen, ylen, xlen = displacements.shape
    planes = loads * comps
    totals = (zlen * lax.axis_size("sz"), ylen * lax.axis_size("sy"))
    args = [
        pltpu.with_memory_space_constraint(arg, pltpu.HBM) for arg in (displacements, fixed, density, solid)
    ]

    disp, fixed, density, solid, d_send, z_send, y_send = call(
        lambda *refs: lead_kernel(totals, *refs),
        [jax.ShapeDtypeStruct(arg.shape, arg.dtype) for arg in args]
        + [(-(-planes // TILE) * TILE, xlen), (planes + 1, ylen, xlen), (planes * zlen, xlen)],
        args,
        scratch=[pltpu.SemaphoreType.DMA((len(args),))],
        space=pltpu.HBM,
    )
    d_in = opposed(d_send, -1, 0, y_shift=-1)
    z_in = opposed(z_send, -1, 0)
    y_in = ring_moved(y_send, "sy")
    nodes = lambda layers: pltpu.VMEM((planes, layers, ylen + TILE, xlen), jnp.float32)
    inner = call(
        lambda *refs: inner_kernel(totals, *refs),
        [
            (zlen, ylen, xlen),
            (2, planes * zlen, xlen),
            (2, REACH * (zlen - 1), xlen),
            (planes, ylen, xlen),
            (planes, ylen, xlen),
            (ylen, xlen),
            (TILE, xlen),
        ],
        (disp, fixed, density, solid),
        scratch=[nodes(zlen), nodes(zlen), pltpu.VMEM((zlen - 1, ylen + 2 * TILE, xlen), jnp.float32)],
    )
    reach = REACH * zlen
    (share,) = call(
        lambda *refs: outer_kernel(displacements.shape, *refs),
        [(ylen * zlen + 2 * reach, xlen)],
        (d_in, z_in, y_in, *inner),
        scratch=[
            nodes(4),
            nodes(4),
            pltpu.VMEM((ylen + 2 * TILE, xlen), jnp.float32),
            pltpu.VMEM((ylen, xlen), jnp.float32),
        ],
    )
    sent = (-(-(reach + REACH) // TILE) * TILE, xlen)
    h, d_send, e_send, y_send, *z_sends = call(
        lambda *refs: total_kernel(displacements.shape, *refs),
        [(zlen + 1, ylen, xlen)] + 3 * [sent] + zlen * [(ylen, xlen)],
        (share, chip_swapped(share)),
    )
    d_in = opposed(d_send, -1, -1)
    e_in = opposed(e_send, -1, 1)
    y_in = opposed(y_send, 0, -1)
    z_in = [opposed(z_send, -1, 0) for z_send in z_sends]
    (part,) = call(layers_kernel, [(zlen, ylen, xlen)], (h, d_in, e_in, y_in, *z_in))
    (out,) = call(sum_kernel, [(zlen, ylen, xlen)], (part, chip_swapped(part)))
    return out


def solution(mesh):
    return jax.shard_map(
        body,
        mesh=mesh,
        in_specs=(
            P("load", None, "sz", "sy", None),
            P("sz", "sy", None),
            P("sz", "sy", None),
            P("sz", "sy", None),
        ),
        out_specs=P("sz", "sy", None),
        check_vma=False,
    )
```

```python
import jax
import jax.numpy as jnp
import numpy as np
from jax import lax
from jax.experimental import pallas as pl
from jax.experimental.pallas import tpu as pltpu
from jax.sharding import PartitionSpec as P

OFFSETS = [(0, 0, 0), (1, 0, 0), (1, 1, 0), (0, 1, 0), (0, 0, 1), (1, 0, 1), (1, 1, 1), (0, 1, 1)]
REACH = 3
ROWS = REACH + 1
TILE = 8
LANES = 128


def element_matrix():
    corners = np.array(
        [
            [-1.0, -1.0, -1.0],
            [1.0, -1.0, -1.0],
            [1.0, 1.0, -1.0],
            [-1.0, 1.0, -1.0],
            [-1.0, -1.0, 1.0],
            [1.0, -1.0, 1.0],
            [1.0, 1.0, 1.0],
            [-1.0, 1.0, 1.0],
        ]
    )
    poisson = 0.3
    lame = poisson / ((1.0 + poisson) * (1.0 - 2.0 * poisson))
    shear = 1.0 / (2.0 * (1.0 + poisson))
    elastic = np.zeros((6, 6))
    elastic[:3, :3] = lame
    for k in range(3):
        elastic[k, k] += 2.0 * shear
        elastic[3 + k, 3 + k] = shear
    gauss = 1.0 / np.sqrt(3.0)
    stiffness = np.zeros((24, 24))
    for gi in range(2):
        for gj in range(2):
            for gk in range(2):
                point = np.array([(2 * gi - 1) * gauss, (2 * gj - 1) * gauss, (2 * gk - 1) * gauss])
                strain = np.zeros((6, 24))
                for node in range(8):
                    grads = np.zeros(3)
                    for k in range(3):
                        value = corners[node, k] / 8.0
                        for m in range(3):
                            if m != k:
                                value = value * (1.0 + point[m] * corners[node, m])
                        grads[k] = 2.0 * value
                    col = 3 * node
                    strain[0, col] = grads[0]
                    strain[1, col + 1] = grads[1]
                    strain[2, col + 2] = grads[2]
                    strain[3, col] = grads[1]
                    strain[3, col + 1] = grads[0]
                    strain[4, col + 1] = grads[2]
                    strain[4, col + 2] = grads[1]
                    strain[5, col] = grads[2]
                    strain[5, col + 2] = grads[0]
                stiffness += strain.T @ elastic @ strain / 8.0
    return stiffness


def mode_weights():
    modes = [(i, j, k) for k in (0, 1) for j in (0, 1) for i in (0, 1)]
    sums = np.zeros((24, 24))
    for m, mode in enumerate(modes):
        for n, corner in enumerate(OFFSETS):
            sign = np.prod([(1 if corner[d] else -1) if mode[d] else 1 for d in range(3)])
            for comp in range(3):
                sums[3 * m + comp, 3 * n + comp] = sign
    form = sums @ element_matrix() @ sums.T / 64.0

    def at(first, second):
        return form[3 * modes.index(first[1]) + first[0], 3 * modes.index(second[1]) + second[0]]

    ux, vy, uy = (0, (1, 0, 0)), (1, (0, 1, 0)), (0, (0, 1, 0))
    uxy, wyz = (0, (1, 1, 0)), (2, (0, 1, 1))
    wxy, vxz, uxyz = (2, (1, 1, 0)), (1, (1, 0, 1)), (0, (1, 1, 1))
    return dict(
        normal=at(ux, ux) - at(ux, vy),
        trace=at(ux, vy),
        shear=at(uy, uy),
        plus=(at(uxy, uxy) + at(uxy, wyz)) / 2,
        minus=(at(uxy, uxy) - at(uxy, wyz)) / 2,
        twist=at(wxy, wxy) - at(wxy, vxz),
        twist_sum=at(wxy, vxz),
        corner=at(uxyz, uxyz),
    )


def square(value):
    return value * value


def quadratic(low, high, weights):
    x = [low[c][1] + high[c][1] for c in range(3)]
    y = [low[c][2] + high[c][2] for c in range(3)]
    z = [high[c][0] - low[c][0] for c in range(3)]
    xy = [low[c][3] + high[c][3] for c in range(3)]
    xz = [high[c][1] - low[c][1] for c in range(3)]
    yz = [high[c][2] - low[c][2] for c in range(3)]
    xyz = [high[c][3] - low[c][3] for c in range(3)]
    normal = square(x[0]) + square(y[1]) + square(z[2])
    trace = square(x[0] + y[1] + z[2])
    shear = square(y[0] + x[1]) + square(z[0] + x[2]) + square(z[1] + y[2])
    pairs = ((xy[0], yz[2]), (xy[1], xz[2]), (xz[0], yz[1]))
    plus = sum(square(p + q) for p, q in pairs)
    minus = sum(square(p - q) for p, q in pairs)
    twist = square(xy[2]) + square(xz[1]) + square(yz[0])
    twist_sum = square(xy[2] + xz[1] + yz[0])
    corner = square(xyz[0]) + square(xyz[1]) + square(xyz[2])
    groups = dict(
        normal=normal, trace=trace, shear=shear, plus=plus, minus=minus, twist=twist, twist_sum=twist_sum, corner=corner
    )
    return sum(np.float32(weights[name]) * group for name, group in groups.items())


def line_weight(coord, count):
    def outside(distance):
        missing = jnp.maximum(REACH - distance, 0)
        return missing * (missing + 1) // 2

    whole = (REACH + 1) * (REACH + 1)
    return (whole - outside(coord) - outside(count - 1 - coord)).astype(jnp.float32)


def voxel_factor(density, solid, plane, first_row, total_z, total_y):
    rows, length = density.shape
    row = lax.broadcasted_iota(jnp.int32, (rows, length), 0) + first_row
    column = lax.broadcasted_iota(jnp.int32, (rows, length), 1)
    weight = line_weight(row, total_y) * line_weight(column, length)
    weight = weight * line_weight(jnp.full((rows, length), plane, jnp.int32), total_z)
    return solid.astype(jnp.float32) * (-3.0 * density * density) / weight


def spread_x(value):
    rows, length = value.shape
    wide = jnp.concatenate([value, jnp.zeros((rows, LANES), jnp.float32)], axis=1)
    span = length + LANES
    total = float(ROWS) * value
    for step in range(1, ROWS):
        both = pltpu.roll(wide, span - step, 1) + pltpu.roll(wide, step, 1)
        total = total + float(ROWS - step) * both[:, :length]
    return total


def spread_layers(layers):
    for step in (1, 2, 1, 2):
        layers = [layers[k] + layers[k + step] for k in range(len(layers) - step)]
    return layers


def held(disp, fixed, case, comp, z, rows):
    return disp[case, comp, z, rows] * (1.0 - fixed[z, rows].astype(jnp.float32))


def split_x(value):
    length = value.shape[1]
    column = lax.broadcasted_iota(jnp.int32, value.shape, 1)
    ahead = jnp.where(column == length - 1, 0.0, pltpu.roll(value, length - 1, 1))
    return value + ahead, ahead - value


def spread_y(quotient, ylen):
    rows = [quotient[TILE + step : TILE + step + ylen] for step in range(-REACH, REACH + 1)]
    return sum((ROWS - abs(k - REACH)) * rows[k] for k in range(2 * REACH + 1))


def to_neighbours(quotient, ylen):
    top = quotient[ylen : ylen + TILE]
    base = quotient[TILE : 2 * TILE]
    ahead, back = [], []
    for row in range(REACH):
        ahead.append(sum(float(REACH - row - k) * top[TILE - 1 - k : TILE - k] for k in range(REACH - row)))
        back.append(sum(float(row + 1 - k) * base[k : k + 1] for k in range(row + 1)))
    return ahead, back


def on_first():
    return lax.axis_index("load") == 0


def lead_kernel(totals, disp_hbm, fixed_hbm, density_hbm, solid_hbm, disp, fixed, density, solid, d_out, z_out, y_out, sems):
    loads, comps, zlen, ylen, _ = disp.shape
    copies = [
        pltpu.make_async_copy(source, target, sems.at[k])
        for k, (source, target) in enumerate(
            ((disp_hbm, disp), (fixed_hbm, fixed), (density_hbm, density), (solid_hbm, solid))
        )
    ]
    for copy in copies:
        copy.start()
    for copy in copies:
        copy.wait()
    gives = jnp.where(on_first(), 0, zlen - 1)
    plane = lax.axis_index("sz") * zlen + gives
    base_y = lax.axis_index("sy") * ylen
    d_out[...] = jnp.zeros(d_out.shape, jnp.float32)
    z_out[loads * comps] = voxel_factor(density[gives], solid[gives], plane, base_y, *totals)
    for case in range(loads):
        for comp in range(comps):
            k = case * comps + comp
            z_out[k] = held(disp, fixed, case, comp, gives, slice(None))
            d_out[k : k + 1] = z_out[k, :1]
            for z in range(zlen):
                at = (comp * loads + case) * zlen + z
                y_out[at : at + 1] = held(disp, fixed, case, comp, z, slice(0, 1))


def tile_energies(plus, diff, first, lanes, layers, loads, comps, base=0):
    weights = mode_weights()

    def faces(k, z):
        near, far = slice(first, first + TILE), slice(first + 1, first + TILE + 1)
        whole, whole_next = plus[k, z, near, lanes], plus[k, z, far, lanes]
        change, change_next = diff[k, z, near, lanes], diff[k, z, far, lanes]
        return whole + whole_next, change + change_next, whole_next - whole, change_next - change

    energy = [None] * layers
    for case in range(loads):
        low = None
        for z in range(layers + 1):
            high = [faces(case * comps + comp, base + z) for comp in range(comps)]
            if low is not None:
                part = quadratic(low, high, weights)
                energy[z - 1] = part if energy[z - 1] is None else energy[z - 1] + part
            low = high
    return energy


def blank_last(value, first, ylen):
    row = lax.broadcasted_iota(jnp.int32, value.shape, 0) + first
    return jnp.where(row == ylen - 1, 0.0, value)


def inner_kernel(totals, disp, fixed, density, solid, own, line, sends, last_plus, last_diff, last_factor, edge, plus, diff, quotient):
    loads, comps, zlen, ylen, xlen = disp.shape
    total_z, total_y = totals
    base_z = lax.axis_index("sz") * zlen
    base_y = lax.axis_index("sy") * ylen
    inner = zlen - 1
    keeps = jnp.where(on_first(), inner, 0)

    @pl.loop(0, loads * comps)
    def _(k):
        case, comp = k // comps, k % comps
        for z in range(zlen):
            whole, change = split_x(held(disp, fixed, case, comp, z, slice(None)))
            plus[k, z, :ylen] = whole
            diff[k, z, :ylen] = change
        last_plus[k] = plus[k, keeps, :ylen]
        last_diff[k] = diff[k, keeps, :ylen]

    for comp in range(comps):
        for case in range(loads):
            for z in range(zlen):
                at = (comp * loads + case) * zlen + z
                line[0, at : at + 1] = plus[case * comps + comp, z, ylen - 1 : ylen]
                line[1, at : at + 1] = diff[case * comps + comp, z, ylen - 1 : ylen]

    zeros = jnp.zeros((TILE, xlen), jnp.float32)
    edge[...] = jnp.zeros(edge.shape, jnp.float32)
    for z in range(zlen):
        factor = voxel_factor(density[z], solid[z], base_z + z, base_y, total_z, total_y)
        edge[z : z + 1] = factor[ylen - 1 :]
        if z == inner:
            last_factor[...] = factor
        else:
            quotient[z, :TILE] = zeros
            quotient[z, TILE : TILE + ylen] = factor
            quotient[z, TILE + ylen :] = zeros

    for first in range(0, ylen, TILE):

        @pl.loop(0, xlen // LANES)
        def _(chunk):
            lanes = pl.ds(pl.multiple_of(chunk * LANES, LANES), LANES)
            energy = tile_energies(plus, diff, first, lanes, inner, loads, comps)
            for z in range(inner):
                here = quotient[z, first + TILE : first + 2 * TILE, lanes]
                quotient[z, first + TILE : first + 2 * TILE, lanes] = blank_last(energy[z] * here, first, ylen)

    for z in range(inner):
        own[z] = spread_x(spread_y(quotient.at[z], ylen))
        ahead, back = to_neighbours(quotient.at[z], ylen)
        ends = spread_x(jnp.concatenate(ahead + back + [zeros[:2]], axis=0))
        sends[0, REACH * z : REACH * (z + 1)] = ends[:REACH]
        sends[1, REACH * z : REACH * (z + 1)] = ends[REACH : 2 * REACH]


def outer_kernel(
    shape, d_in, z_in, y_in, own_in, line, sends, last_plus, last_diff, last_factor, edge, share, plus, diff, quotient, factor
):
    loads, comps, zlen, ylen, xlen = shape
    planes = loads * comps
    inner = zlen - 1
    first_core, index = on_first(), lax.axis_index("sz")
    top = first_core & (index == lax.axis_size("sz") - 1)
    more = lax.axis_index("sy") < lax.axis_size("sy") - 1
    stays, comes = jnp.where(first_core, 0, 1), jnp.where(first_core, jnp.where(top, 2, 1), 0)
    y_rows = jnp.where(more, y_in[...], 0.0)
    y_plus, y_diff = split_x(y_rows)
    d_plus, d_diff = split_x(jnp.where(more, d_in[...], 0.0))
    for k in range(planes):
        case, comp = k // comps, k % comps
        at = (comp * loads + case) * zlen
        beside = jnp.where(first_core, y_plus[at + inner : at + zlen], y_plus[at : at + 1])
        beside_diff = jnp.where(first_core, y_diff[at + inner : at + zlen], y_diff[at : at + 1])
        plus[k, stays, :ylen] = last_plus[k]
        diff[k, stays, :ylen] = last_diff[k]
        plus[k, stays, ylen : ylen + 1] = beside
        diff[k, stays, ylen : ylen + 1] = beside_diff
        whole, change = split_x(z_in[k])
        plus[k, comes, :ylen] = whole
        diff[k, comes, :ylen] = change
        plus[k, comes, ylen : ylen + 1] = d_plus[k : k + 1]
        diff[k, comes, ylen : ylen + 1] = d_diff[k : k + 1]
    below = jnp.where(index > 0, z_in[planes], 0.0)
    factor[...] = jnp.where(first_core, last_factor[...], below)

    @pl.when(top)
    def _():
        clamped = jnp.zeros((ylen + TILE, xlen), jnp.float32)
        for k in range(planes):
            for slot in (1, 3):
                plus[k, slot] = clamped
                diff[k, slot] = clamped

    zeros = jnp.zeros((TILE, xlen), jnp.float32)
    quotient[:TILE] = zeros
    quotient[TILE + ylen :] = zeros
    for first in range(0, ylen, TILE):

        @pl.loop(0, xlen // LANES)
        def _(chunk):
            lanes = pl.ds(pl.multiple_of(chunk * LANES, LANES), LANES)
            (energy,) = tile_energies(plus, diff, first, lanes, 1, loads, comps)
            quotient[first + TILE : first + 2 * TILE, lanes] = energy * factor[first : first + TILE, lanes]

    @pl.when(top)
    def _():
        for first in range(0, ylen, TILE):

            @pl.loop(0, xlen // LANES)
            def _(chunk):
                lanes = pl.ds(pl.multiple_of(chunk * LANES, LANES), LANES)
                (energy,) = tile_energies(plus, diff, first, lanes, 1, loads, comps, base=2)
                quotient[first + TILE : first + 2 * TILE, lanes] += energy * factor[first : first + TILE, lanes]

    count = loads * zlen
    low, high = [], []
    for comp in range(comps):
        part = slice(comp * count, (comp + 1) * count)
        whole, change = line[0, part], line[1, part]
        whole_next, change_next = y_plus[part], y_diff[part]
        face = (whole + whole_next, change + change_next, whole_next - whole, change_next - change)
        low.append(face)
        high.append([pltpu.roll(value, count - 1, 0) for value in face])
    energy = quadratic(low, high, mode_weights())
    energy = sum(energy[case * zlen : case * zlen + inner] for case in range(loads)) * edge[:inner]
    last = spread_x(jnp.concatenate([energy, jnp.zeros((TILE - inner, xlen), jnp.float32)], axis=0))

    row = lax.broadcasted_iota(jnp.int32, (TILE, xlen), 0)
    rising = jnp.maximum(row - (TILE - 1 - ROWS), 0).astype(jnp.float32)
    ups, downs = [], []
    for z in range(inner):
        share[ylen * z : ylen * (z + 1)] = own_in[z]
        share[ylen * (z + 1) - TILE : ylen * (z + 1)] += rising * last[z : z + 1]
        here = sends[0, REACH * z : REACH * (z + 1)]
        ups += [here[r : r + 1] + float(REACH - r) * last[z : z + 1] for r in range(REACH)]
        downs.append(sends[1, REACH * z : REACH * (z + 1)])
    share[ylen * inner : ylen * zlen] = spread_x(spread_y(quotient, ylen))
    ahead, back = to_neighbours(quotient, ylen)
    ends = spread_x(jnp.concatenate(ahead + back + [zeros[:2]], axis=0))
    share[ylen * zlen :] = jnp.concatenate(ups + [ends[:REACH]] + downs + [ends[REACH : 2 * REACH]], axis=0)


def total_kernel(shape, share, other, h_out, z_out, y_out, d_out, e_out):
    _, _, zlen, ylen, xlen = shape
    first_core = on_first()
    inner, rows = zlen - 1, ylen * zlen
    reach = REACH * zlen

    def layers(first, count):
        mine, theirs = share[first + inner * count : first + zlen * count], other[first + inner * count : first + zlen * count]
        middle = share[first : first + inner * count] + other[first : first + inner * count]
        return jnp.where(first_core, theirs, mine), middle, jnp.where(first_core, mine, theirs)

    lowest, middle, highest = layers(0, ylen)
    h_out[0] = lowest
    for z in range(inner):
        h_out[z + 1] = middle[ylen * z : ylen * (z + 1)]
    h_out[zlen] = highest
    z_out[...] = h_out[pl.ds(jnp.where(first_core, 0, 1), zlen)]
    ups = jnp.concatenate(layers(rows, REACH), axis=0)
    downs = jnp.concatenate(layers(rows + reach, REACH), axis=0)
    y_out[: reach + REACH] = jnp.where(first_core, downs, ups)
    for out, used in ((y_out, reach + REACH), (d_out, reach), (e_out, reach)):
        out[used:] = jnp.zeros((out.shape[0] - used, xlen), jnp.float32)
    d_out[:reach] = jnp.where(first_core, downs[:reach], ups[REACH:])
    e_out[:reach] = jnp.where(first_core, ups[:reach], downs[REACH:])


def layers_kernel(h, d_in, e_in, y_in, z_in, out):
    zlen, ylen, xlen = out.shape
    reach = REACH * zlen
    first_core = on_first()
    z_index, z_last = lax.axis_index("sz"), lax.axis_size("sz") - 1
    y_index, y_last = lax.axis_index("sy"), lax.axis_size("sy") - 1
    z_side = jnp.where(first_core, z_index < z_last, z_index > 0)
    y_side = jnp.where(first_core, y_index < y_last, y_index > 0)
    y_other = jnp.where(first_core, y_index > 0, y_index < y_last)
    blank = jnp.zeros((TILE - REACH, xlen), jnp.float32)

    def at_start(rows):
        return jnp.concatenate([rows, blank], axis=0)

    def at_end(rows):
        return jnp.concatenate([blank, rows], axis=0)

    def ends(rows, keep, at_last):
        rows = jnp.where(keep, rows, 0.0)
        return at_start(jnp.where(at_last, 0.0, rows)), at_end(jnp.where(at_last, rows, 0.0))

    def with_ends(layer, *pairs):
        head, tail = layer[:TILE], layer[ylen - TILE :]
        for first, last in pairs:
            head, tail = head + first, tail + last
        return jnp.concatenate([head, layer[TILE : ylen - TILE], tail] if ylen > 2 * TILE else [head, tail], axis=0)

    own = []
    for k in range(zlen + 1):
        layer = jnp.where(first_core, h[k], 0.0)
        own.append(with_ends(layer, ends(y_in[REACH * k : REACH * (k + 1)], y_side, first_core)))
    come = []
    for k in range(zlen):
        part = slice(REACH * k, REACH * (k + 1))
        layer = jnp.where(z_side, z_in[k], 0.0)
        straight = ends(d_in[part], z_side & y_side, first_core)
        across = ends(e_in[part], z_side & y_other, jnp.logical_not(first_core))
        come.append(with_ends(layer, straight, across))
    below = [jnp.where(first_core, 0.0, layer) for layer in come[zlen - REACH :]]
    above = [jnp.where(first_core, layer, 0.0) for layer in come]
    layers = below[:-1] + [below[-1] + own[0]] + own[1:-1] + [own[-1] + above[0]] + above[1:]
    for z, layer in enumerate(spread_layers(layers)):
        out[z] = layer


def sum_kernel(part, other, out):
    out[...] = part[...] + other[...]


def call(kernel, outs, args, scratch=(), space=pltpu.VMEM):
    shapes = [jax.ShapeDtypeStruct(out, jnp.float32) if isinstance(out, tuple) else out for out in outs]
    return pl.pallas_call(
        kernel,
        out_shape=shapes,
        in_specs=[pl.BlockSpec(memory_space=space)] * len(args),
        out_specs=[pl.BlockSpec(memory_space=pltpu.VMEM)] * len(outs),
        scratch_shapes=list(scratch),
        compiler_params=pltpu.CompilerParams(vmem_limit_bytes=32 * 1024 * 1024),
    )(*args)


def ring_moved(value, axis):
    size = lax.axis_size(axis)
    return lax.ppermute(value, axis, [((k + 1) % size, k) for k in range(size)])


def chip_swapped(value):
    cores = lax.axis_size("load")
    return lax.ppermute(value, "load", [(core, cores - 1 - core) for core in range(cores)])


def opposed(value, z_step, y_step, y_shift=0):
    cores, rows, size = lax.axis_size("load"), lax.axis_size("sy"), lax.axis_size("sz")
    pairs = []
    for core in range(cores):
        sign = -1 if core else 1
        for y in range(rows):
            for z in range(size):
                to_y, to_z, side = y + sign * y_step, z + sign * z_step, core
                if not (0 <= to_y < rows and 0 <= to_z < size):
                    to_y, to_z, side = y, z, cores - 1 - core
                to_y = (to_y + y_shift) % rows
                pairs.append(((core * rows + y) * size + z, (side * rows + to_y) * size + to_z))
    return lax.ppermute(value, ("load", "sy", "sz"), pairs)


def body(displacements, density, solid, fixed):
    loads, comps, zlen, ylen, xlen = displacements.shape
    planes = loads * comps
    totals = (zlen * lax.axis_size("sz"), ylen * lax.axis_size("sy"))
    args = [
        pltpu.with_memory_space_constraint(arg, pltpu.HBM) for arg in (displacements, fixed, density, solid)
    ]

    disp, fixed, density, solid, d_send, z_send, y_send = call(
        lambda *refs: lead_kernel(totals, *refs),
        [jax.ShapeDtypeStruct(arg.shape, arg.dtype) for arg in args]
        + [(-(-planes // TILE) * TILE, xlen), (planes + 1, ylen, xlen), (planes * zlen, xlen)],
        args,
        scratch=[pltpu.SemaphoreType.DMA((len(args),))],
        space=pltpu.HBM,
    )
    d_in = opposed(d_send, -1, 0, y_shift=-1)
    z_in = opposed(z_send, -1, 0)
    y_in = ring_moved(y_send, "sy")
    nodes = lambda layers: pltpu.VMEM((planes, layers, ylen + TILE, xlen), jnp.float32)
    inner = call(
        lambda *refs: inner_kernel(totals, *refs),
        [
            (zlen, ylen, xlen),
            (2, planes * zlen, xlen),
            (2, REACH * (zlen - 1), xlen),
            (planes, ylen, xlen),
            (planes, ylen, xlen),
            (ylen, xlen),
            (TILE, xlen),
        ],
        (disp, fixed, density, solid),
        scratch=[nodes(zlen), nodes(zlen), pltpu.VMEM((zlen - 1, ylen + 2 * TILE, xlen), jnp.float32)],
    )
    reach = REACH * zlen
    (share,) = call(
        lambda *refs: outer_kernel(displacements.shape, *refs),
        [(ylen * zlen + 2 * reach, xlen)],
        (d_in, z_in, y_in, *inner),
        scratch=[
            nodes(4),
            nodes(4),
            pltpu.VMEM((ylen + 2 * TILE, xlen), jnp.float32),
            pltpu.VMEM((ylen, xlen), jnp.float32),
        ],
    )
    sent = (-(-(reach + REACH) // TILE) * TILE, xlen)
    h, z_send, y_send, d_send, e_send = call(
        lambda *refs: total_kernel(displacements.shape, *refs),
        [
            (zlen + 1, ylen, xlen),
            (zlen, ylen, xlen),
            sent,
            sent,
            sent,
        ],
        (share, chip_swapped(share)),
    )
    d_in = opposed(d_send, -1, -1)
    e_in = opposed(e_send, -1, 1)
    y_in = opposed(y_send, 0, -1)
    z_in = opposed(z_send, -1, 0)
    (part,) = call(layers_kernel, [(zlen, ylen, xlen)], (h, d_in, e_in, y_in, z_in))
    (out,) = call(sum_kernel, [(zlen, ylen, xlen)], (part, chip_swapped(part)))
    return out


def solution(mesh):
    return jax.shard_map(
        body,
        mesh=mesh,
        in_specs=(
            P("load", None, "sz", "sy", None),
            P("sz", "sy", None),
            P("sz", "sy", None),
            P("sz", "sy", None),
        ),
        out_specs=P("sz", "sy", None),
        check_vma=False,
    )
```

```python
import jax
import jax.numpy as jnp
import numpy as np
from jax import lax
from jax.experimental import pallas as pl
from jax.experimental.pallas import tpu as pltpu
from jax.sharding import PartitionSpec as P

OFFSETS = [(0, 0, 0), (1, 0, 0), (1, 1, 0), (0, 1, 0), (0, 0, 1), (1, 0, 1), (1, 1, 1), (0, 1, 1)]
REACH = 3
ROWS = REACH + 1
TILE = 8
LANES = 128


def element_matrix():
    corners = np.array(
        [
            [-1.0, -1.0, -1.0],
            [1.0, -1.0, -1.0],
            [1.0, 1.0, -1.0],
            [-1.0, 1.0, -1.0],
            [-1.0, -1.0, 1.0],
            [1.0, -1.0, 1.0],
            [1.0, 1.0, 1.0],
            [-1.0, 1.0, 1.0],
        ]
    )
    poisson = 0.3
    lame = poisson / ((1.0 + poisson) * (1.0 - 2.0 * poisson))
    shear = 1.0 / (2.0 * (1.0 + poisson))
    elastic = np.zeros((6, 6))
    elastic[:3, :3] = lame
    for k in range(3):
        elastic[k, k] += 2.0 * shear
        elastic[3 + k, 3 + k] = shear
    gauss = 1.0 / np.sqrt(3.0)
    stiffness = np.zeros((24, 24))
    for gi in range(2):
        for gj in range(2):
            for gk in range(2):
                point = np.array([(2 * gi - 1) * gauss, (2 * gj - 1) * gauss, (2 * gk - 1) * gauss])
                strain = np.zeros((6, 24))
                for node in range(8):
                    grads = np.zeros(3)
                    for k in range(3):
                        value = corners[node, k] / 8.0
                        for m in range(3):
                            if m != k:
                                value = value * (1.0 + point[m] * corners[node, m])
                        grads[k] = 2.0 * value
                    col = 3 * node
                    strain[0, col] = grads[0]
                    strain[1, col + 1] = grads[1]
                    strain[2, col + 2] = grads[2]
                    strain[3, col] = grads[1]
                    strain[3, col + 1] = grads[0]
                    strain[4, col + 1] = grads[2]
                    strain[4, col + 2] = grads[1]
                    strain[5, col] = grads[2]
                    strain[5, col + 2] = grads[0]
                stiffness += strain.T @ elastic @ strain / 8.0
    return stiffness


def mode_weights():
    modes = [(i, j, k) for k in (0, 1) for j in (0, 1) for i in (0, 1)]
    sums = np.zeros((24, 24))
    for m, mode in enumerate(modes):
        for n, corner in enumerate(OFFSETS):
            sign = np.prod([(1 if corner[d] else -1) if mode[d] else 1 for d in range(3)])
            for comp in range(3):
                sums[3 * m + comp, 3 * n + comp] = sign
    form = sums @ element_matrix() @ sums.T / 64.0

    def at(first, second):
        return form[3 * modes.index(first[1]) + first[0], 3 * modes.index(second[1]) + second[0]]

    ux, vy, uy = (0, (1, 0, 0)), (1, (0, 1, 0)), (0, (0, 1, 0))
    uxy, wyz = (0, (1, 1, 0)), (2, (0, 1, 1))
    wxy, vxz, uxyz = (2, (1, 1, 0)), (1, (1, 0, 1)), (0, (1, 1, 1))
    return dict(
        normal=at(ux, ux) - at(ux, vy),
        trace=at(ux, vy),
        shear=at(uy, uy),
        plus=(at(uxy, uxy) + at(uxy, wyz)) / 2,
        minus=(at(uxy, uxy) - at(uxy, wyz)) / 2,
        twist=at(wxy, wxy) - at(wxy, vxz),
        twist_sum=at(wxy, vxz),
        corner=at(uxyz, uxyz),
    )


def square(value):
    return value * value


def quadratic(low, high, weights):
    x = [low[c][1] + high[c][1] for c in range(3)]
    y = [low[c][2] + high[c][2] for c in range(3)]
    z = [high[c][0] - low[c][0] for c in range(3)]
    xy = [low[c][3] + high[c][3] for c in range(3)]
    xz = [high[c][1] - low[c][1] for c in range(3)]
    yz = [high[c][2] - low[c][2] for c in range(3)]
    xyz = [high[c][3] - low[c][3] for c in range(3)]
    normal = square(x[0]) + square(y[1]) + square(z[2])
    trace = square(x[0] + y[1] + z[2])
    shear = square(y[0] + x[1]) + square(z[0] + x[2]) + square(z[1] + y[2])
    pairs = ((xy[0], yz[2]), (xy[1], xz[2]), (xz[0], yz[1]))
    plus = sum(square(p + q) for p, q in pairs)
    minus = sum(square(p - q) for p, q in pairs)
    twist = square(xy[2]) + square(xz[1]) + square(yz[0])
    twist_sum = square(xy[2] + xz[1] + yz[0])
    corner = square(xyz[0]) + square(xyz[1]) + square(xyz[2])
    groups = dict(
        normal=normal, trace=trace, shear=shear, plus=plus, minus=minus, twist=twist, twist_sum=twist_sum, corner=corner
    )
    return sum(np.float32(weights[name]) * group for name, group in groups.items())


def line_weight(coord, count):
    def outside(distance):
        missing = jnp.maximum(REACH - distance, 0)
        return missing * (missing + 1) // 2

    whole = (REACH + 1) * (REACH + 1)
    return (whole - outside(coord) - outside(count - 1 - coord)).astype(jnp.float32)


def voxel_factor(density, solid, plane, first_row, total_z, total_y):
    rows, length = density.shape
    row = lax.broadcasted_iota(jnp.int32, (rows, length), 0) + first_row
    column = lax.broadcasted_iota(jnp.int32, (rows, length), 1)
    weight = line_weight(row, total_y) * line_weight(column, length)
    weight = weight * line_weight(jnp.full((rows, length), plane, jnp.int32), total_z)
    return solid.astype(jnp.float32) * (-3.0 * density * density) / weight


def spread_x(value):
    rows, length = value.shape
    wide = jnp.concatenate([value, jnp.zeros((rows, LANES), jnp.float32)], axis=1)
    span = length + LANES
    total = float(ROWS) * value
    for step in range(1, ROWS):
        both = pltpu.roll(wide, span - step, 1) + pltpu.roll(wide, step, 1)
        total = total + float(ROWS - step) * both[:, :length]
    return total


def spread_layers(layers):
    for step in (1, 2, 1, 2):
        layers = [layers[k] + layers[k + step] for k in range(len(layers) - step)]
    return layers


def held(disp, fixed, case, comp, z, rows):
    return disp[case, comp, z, rows] * (1.0 - fixed[z, rows].astype(jnp.float32))


def split_x(value):
    length = value.shape[1]
    column = lax.broadcasted_iota(jnp.int32, value.shape, 1)
    ahead = jnp.where(column == length - 1, 0.0, pltpu.roll(value, length - 1, 1))
    return value + ahead, ahead - value


def spread_y(quotient, ylen):
    rows = [quotient[TILE + step : TILE + step + ylen] for step in range(-REACH, REACH + 1)]
    return sum((ROWS - abs(k - REACH)) * rows[k] for k in range(2 * REACH + 1))


def to_neighbours(quotient, ylen):
    top = quotient[ylen : ylen + TILE]
    base = quotient[TILE : 2 * TILE]
    ahead, back = [], []
    for row in range(REACH):
        ahead.append(sum(float(REACH - row - k) * top[TILE - 1 - k : TILE - k] for k in range(REACH - row)))
        back.append(sum(float(row + 1 - k) * base[k : k + 1] for k in range(row + 1)))
    return ahead, back


def on_first():
    return lax.axis_index("load") == 0


def lead_kernel(totals, disp_hbm, fixed_hbm, density_hbm, solid_hbm, disp, fixed, density, solid, z_out, y_out, sems):
    loads, comps, zlen, ylen, _ = disp.shape
    copies = [
        pltpu.make_async_copy(source, target, sems.at[k])
        for k, (source, target) in enumerate(
            ((disp_hbm, disp), (fixed_hbm, fixed), (density_hbm, density), (solid_hbm, solid))
        )
    ]
    for copy in copies:
        copy.start()
    for copy in copies:
        copy.wait()
    gives = jnp.where(on_first(), 0, zlen - 1)
    plane = lax.axis_index("sz") * zlen + gives
    base_y = lax.axis_index("sy") * ylen
    z_out[loads * comps] = voxel_factor(density[gives], solid[gives], plane, base_y, *totals)
    for case in range(loads):
        for comp in range(comps):
            z_out[case * comps + comp] = held(disp, fixed, case, comp, gives, slice(None))
            for z in range(zlen):
                at = (comp * loads + case) * zlen + z
                y_out[at : at + 1] = held(disp, fixed, case, comp, z, slice(0, 1))


def tile_energies(plus, diff, first, lanes, layers, loads, comps, base=0):
    weights = mode_weights()

    def faces(k, z):
        near, far = slice(first, first + TILE), slice(first + 1, first + TILE + 1)
        whole, whole_next = plus[k, z, near, lanes], plus[k, z, far, lanes]
        change, change_next = diff[k, z, near, lanes], diff[k, z, far, lanes]
        return whole + whole_next, change + change_next, whole_next - whole, change_next - change

    energy = [None] * layers
    for case in range(loads):
        low = None
        for z in range(layers + 1):
            high = [faces(case * comps + comp, base + z) for comp in range(comps)]
            if low is not None:
                part = quadratic(low, high, weights)
                energy[z - 1] = part if energy[z - 1] is None else energy[z - 1] + part
            low = high
    return energy


def blank_last(value, first, ylen):
    row = lax.broadcasted_iota(jnp.int32, value.shape, 0) + first
    return jnp.where(row == ylen - 1, 0.0, value)


def inner_kernel(totals, disp, fixed, density, solid, own, line, sends, last_plus, last_diff, last_factor, edge, plus, diff, quotient):
    loads, comps, zlen, ylen, xlen = disp.shape
    total_z, total_y = totals
    base_z = lax.axis_index("sz") * zlen
    base_y = lax.axis_index("sy") * ylen
    inner = zlen - 1
    keeps = jnp.where(on_first(), inner, 0)

    @pl.loop(0, loads * comps)
    def _(k):
        case, comp = k // comps, k % comps
        for z in range(zlen):
            whole, change = split_x(held(disp, fixed, case, comp, z, slice(None)))
            plus[k, z, :ylen] = whole
            diff[k, z, :ylen] = change
        last_plus[k] = plus[k, keeps, :ylen]
        last_diff[k] = diff[k, keeps, :ylen]

    for comp in range(comps):
        for case in range(loads):
            for z in range(zlen):
                at = (comp * loads + case) * zlen + z
                line[0, at : at + 1] = plus[case * comps + comp, z, ylen - 1 : ylen]
                line[1, at : at + 1] = diff[case * comps + comp, z, ylen - 1 : ylen]

    zeros = jnp.zeros((TILE, xlen), jnp.float32)
    edge[...] = jnp.zeros(edge.shape, jnp.float32)
    for z in range(zlen):
        factor = voxel_factor(density[z], solid[z], base_z + z, base_y, total_z, total_y)
        edge[z : z + 1] = factor[ylen - 1 :]
        if z == inner:
            last_factor[...] = factor
        else:
            quotient[z, :TILE] = zeros
            quotient[z, TILE : TILE + ylen] = factor
            quotient[z, TILE + ylen :] = zeros

    for first in range(0, ylen, TILE):

        @pl.loop(0, xlen // LANES)
        def _(chunk):
            lanes = pl.ds(pl.multiple_of(chunk * LANES, LANES), LANES)
            energy = tile_energies(plus, diff, first, lanes, inner, loads, comps)
            for z in range(inner):
                here = quotient[z, first + TILE : first + 2 * TILE, lanes]
                quotient[z, first + TILE : first + 2 * TILE, lanes] = blank_last(energy[z] * here, first, ylen)

    for z in range(inner):
        own[z] = spread_x(spread_y(quotient.at[z], ylen))
        ahead, back = to_neighbours(quotient.at[z], ylen)
        ends = spread_x(jnp.concatenate(ahead + back + [zeros[:2]], axis=0))
        sends[0, REACH * z : REACH * (z + 1)] = ends[:REACH]
        sends[1, REACH * z : REACH * (z + 1)] = ends[REACH : 2 * REACH]


def pass_kernel(shape, y_in, d_out):
    loads, comps, zlen, _, _ = shape
    first_core = on_first()
    d_out[...] = jnp.zeros(d_out.shape, jnp.float32)
    for k in range(loads * comps):
        at = (k % comps * loads + k // comps) * zlen
        d_out[k : k + 1] = jnp.where(first_core, y_in[at : at + 1], y_in[at + zlen - 1 : at + zlen])


def lines_kernel(shape, y_in, own, line, sends, edge, share):
    loads, comps, zlen, ylen, xlen = shape
    inner = zlen - 1
    more = lax.axis_index("sy") < lax.axis_size("sy") - 1
    count = loads * zlen
    low, high = [], []
    for comp in range(comps):
        part = slice(comp * count, (comp + 1) * count)
        whole, change = line[0, part], line[1, part]
        whole_next, change_next = split_x(jnp.where(more, y_in[part], 0.0))
        face = (whole + whole_next, change + change_next, whole_next - whole, change_next - change)
        low.append(face)
        high.append([pltpu.roll(value, count - 1, 0) for value in face])
    energy = quadratic(low, high, mode_weights())
    energy = sum(energy[case * zlen : case * zlen + inner] for case in range(loads)) * edge[:inner]
    last = spread_x(jnp.concatenate([energy, jnp.zeros((TILE - inner, xlen), jnp.float32)], axis=0))

    row = lax.broadcasted_iota(jnp.int32, (TILE, xlen), 0)
    rising = jnp.maximum(row - (TILE - 1 - ROWS), 0).astype(jnp.float32)
    ups, downs = [], []
    for z in range(inner):
        share[ylen * z : ylen * (z + 1)] = own[z]
        share[ylen * (z + 1) - TILE : ylen * (z + 1)] += rising * last[z : z + 1]
        here = sends[0, REACH * z : REACH * (z + 1)]
        ups += [here[r : r + 1] + float(REACH - r) * last[z : z + 1] for r in range(REACH)]
        downs.append(sends[1, REACH * z : REACH * (z + 1)])
    share[ylen * inner :] = jnp.concatenate(ups + downs, axis=0)


def outer_kernel(shape, z_in, last_plus, last_diff, last_factor, own, ends, corner, plus, diff, quotient, factor):
    loads, comps, zlen, ylen, xlen = shape
    planes = loads * comps
    first_core, index = on_first(), lax.axis_index("sz")
    top = first_core & (index == lax.axis_size("sz") - 1)
    stays, comes = jnp.where(first_core, 0, 1), jnp.where(first_core, jnp.where(top, 2, 1), 0)
    for k in range(planes):
        plus[k, stays, :ylen] = last_plus[k]
        diff[k, stays, :ylen] = last_diff[k]
        whole, change = split_x(z_in[k])
        plus[k, comes, :ylen] = whole
        diff[k, comes, :ylen] = change
        for group, value in enumerate((last_plus[k, ylen - 1 :], last_diff[k, ylen - 1 :], whole[ylen - 1 :], change[ylen - 1 :])):
            corner[group, k : k + 1] = value
    below = jnp.where(index > 0, z_in[planes], 0.0)
    factor[...] = jnp.where(first_core, last_factor[...], below)
    corner[0, planes : planes + 1] = factor[ylen - 1 :]

    @pl.when(top)
    def _():
        clamped = jnp.zeros((ylen + TILE, xlen), jnp.float32)
        for k in range(planes):
            for slot in (1, 3):
                plus[k, slot] = clamped
                diff[k, slot] = clamped

    zeros = jnp.zeros((TILE, xlen), jnp.float32)
    quotient[:TILE] = zeros
    quotient[TILE + ylen :] = zeros
    for first in range(0, ylen, TILE):

        @pl.loop(0, xlen // LANES)
        def _(chunk):
            lanes = pl.ds(pl.multiple_of(chunk * LANES, LANES), LANES)
            (energy,) = tile_energies(plus, diff, first, lanes, 1, loads, comps)
            here = energy * factor[first : first + TILE, lanes]
            quotient[first + TILE : first + 2 * TILE, lanes] = blank_last(here, first, ylen)

    @pl.when(top)
    def _():
        for first in range(0, ylen, TILE):

            @pl.loop(0, xlen // LANES)
            def _(chunk):
                lanes = pl.ds(pl.multiple_of(chunk * LANES, LANES), LANES)
                (energy,) = tile_energies(plus, diff, first, lanes, 1, loads, comps, base=2)
                here = energy * factor[first : first + TILE, lanes]
                quotient[first + TILE : first + 2 * TILE, lanes] += blank_last(here, first, ylen)

    own[...] = spread_x(spread_y(quotient, ylen))
    ahead, back = to_neighbours(quotient, ylen)
    ends[...] = spread_x(jnp.concatenate(ahead + back + [zeros[: TILE - 2 * REACH]], axis=0))


def corner_line(shape, corner, y_in, d_in):
    loads, comps, zlen, ylen, xlen = shape
    planes = loads * comps
    first_core = on_first()
    top = first_core & (lax.axis_index("sz") == lax.axis_size("sz") - 1)
    more = lax.axis_index("sy") < lax.axis_size("sy") - 1
    rows = []
    for k in range(planes):
        at = (k % comps * loads + k // comps) * zlen
        rows.append(jnp.where(first_core, y_in[at + zlen - 1 : at + zlen], y_in[at : at + 1]))
    rows.append(jnp.zeros((-planes % TILE, xlen), jnp.float32))
    stays_next = split_x(jnp.where(more, jnp.concatenate(rows, axis=0), 0.0))
    comes_next = split_x(jnp.where(more, d_in[...], 0.0))

    def faces(stays, comes, comp):
        zero = jnp.zeros((1, xlen), jnp.float32)
        under, over = [], []
        for own, other in zip(stays, comes):
            own, other = ([value[case * comps + comp : case * comps + comp + 1] for case in range(loads)] for value in (own, other))
            low = [jnp.where(first_core, a, b) for a, b in zip(own, other)] + [jnp.where(top, b, 0.0) for b in other]
            high = [jnp.where(first_core, jnp.where(top, 0.0, b), a) for a, b in zip(own, other)] + [zero] * loads
            under.append(jnp.concatenate(low, axis=0))
            over.append(jnp.concatenate(high, axis=0))
        return under, over

    low, high = [], []
    for comp in range(comps):
        near = faces((corner[0], corner[1]), (corner[2], corner[3]), comp)
        far = faces(stays_next, comes_next, comp)
        for (whole, change), (whole_next, change_next), into in zip(near, far, (low, high)):
            into.append((whole + whole_next, change + change_next, whole_next - whole, change_next - change))
    energy = quadratic(low, high, mode_weights())
    line = sum(energy[case : case + 1] for case in range(2 * loads)) * corner[0, planes : planes + 1]
    return spread_x(jnp.concatenate([line, jnp.zeros((TILE - 1, xlen), jnp.float32)], axis=0))[:1]


def total_kernel(shape, share, other, own, ends, corner, y_in, d_in, h_out, d_out, e_out, y_out, z_out, i_out):
    _, _, zlen, ylen, xlen = shape
    inner = zlen - 1
    first_core = on_first()
    line = corner_line(shape, corner, y_in, d_in)
    row = lax.broadcasted_iota(jnp.int32, (TILE, xlen), 0)
    rising = jnp.maximum(row - (TILE - 1 - ROWS), 0).astype(jnp.float32)
    for z in range(inner):
        h_out[z] = share[ylen * z : ylen * (z + 1)] + other[ylen * z : ylen * (z + 1)]
    h_out[inner] = own[...]
    h_out[inner, ylen - TILE :] += rising * line
    shift = jnp.where(first_core, 0, 1)
    for z in range(inner):
        z_out[z + shift] = h_out[z]
    z_out[jnp.where(first_core, inner, 0)] = h_out[inner]
    first, reach = ylen * inner, REACH * inner
    ups, downs = (share[at : at + reach] + other[at : at + reach] for at in (first, first + reach))
    weights = jnp.maximum(REACH - lax.broadcasted_iota(jnp.int32, (REACH, xlen), 0), 0).astype(jnp.float32)
    between_ups, between_downs = ends[:REACH] + weights * line, ends[REACH : 2 * REACH]

    def stacked(rows, between):
        return jnp.where(first_core, jnp.concatenate([rows, between], axis=0), jnp.concatenate([between, rows], axis=0))

    used = reach + REACH
    all_ups, all_downs = stacked(ups, between_ups), stacked(downs, between_downs)
    y_out[:used] = jnp.where(first_core, all_downs, all_ups)
    d_out[:used] = jnp.where(first_core, all_ups, all_downs)
    e_out[:used] = jnp.where(first_core, all_downs, all_ups)
    for out in (y_out, d_out, e_out):
        out[used:] = jnp.zeros((out.shape[0] - used, xlen), jnp.float32)
    i_out[:REACH] = jnp.where(first_core, between_ups, between_downs)
    i_out[REACH:] = jnp.zeros((i_out.shape[0] - REACH, xlen), jnp.float32)


def layers_kernel(h, d_in, e_in, y_in, z_in, i_in, out):
    zlen, ylen, xlen = out.shape
    inner = zlen - 1
    first_core = on_first()
    z_index, z_last = lax.axis_index("sz"), lax.axis_size("sz") - 1
    y_index, y_last = lax.axis_index("sy"), lax.axis_size("sy") - 1
    not_first, not_last = y_index > 0, y_index < y_last
    z_side = jnp.where(first_core, z_index > 0, z_index < z_last)
    blank = jnp.zeros((TILE - REACH, xlen), jnp.float32)

    def ends(rows, keep, at_last):
        rows = jnp.where(keep, rows, 0.0)
        at_start, at_end = jnp.where(at_last, 0.0, rows), jnp.where(at_last, rows, 0.0)
        return jnp.concatenate([at_start, blank], axis=0), jnp.concatenate([blank, at_end], axis=0)

    def with_ends(layer, *pairs):
        head, tail = layer[:TILE], layer[ylen - TILE :]
        for first, last in pairs:
            head, tail = head + first, tail + last
        return jnp.concatenate([head, layer[TILE : ylen - TILE], tail] if ylen > 2 * TILE else [head, tail], axis=0)

    second_core = jnp.logical_not(first_core)
    y_side = jnp.where(first_core, not_last, not_first)
    y_other = jnp.where(first_core, not_first, not_last)
    own, come = [], []
    for k in range(zlen):
        part = slice(REACH * k, REACH * (k + 1))
        at = jnp.where(first_core, k, k - 1 if k else inner)
        layer = h[at]
        keep = first_core | (k == 0)
        pairs = [ends(y_in[part], y_side, first_core)]
        if k in (0, inner):
            between = first_core if k else second_core
            pairs.append(ends(i_in[:REACH], y_other & between, second_core))
        own.append(with_ends(jnp.where(keep, layer, 0.0), *pairs))
        straight = ends(d_in[part], z_side & jnp.where(first_core, not_first, not_last), second_core)
        across = ends(e_in[part], z_side & jnp.where(first_core, not_last, not_first), first_core)
        come.append(with_ends(jnp.where(z_side, z_in[k], 0.0), straight, across))
    zero = jnp.zeros((ylen, xlen), jnp.float32)
    own = [jnp.where(first_core, a, b) for a, b in zip([zero] + own, own + [zero])]
    below = [jnp.where(first_core, layer, 0.0) for layer in come[zlen - REACH :]]
    above = [jnp.where(first_core, 0.0, layer) for layer in come]
    layers = below[:-1] + [below[-1] + own[0]] + own[1:-1] + [own[-1] + above[0]] + above[1:]
    for z, layer in enumerate(spread_layers(layers)):
        out[z] = layer


def sum_kernel(part, other, out):
    out[...] = part[...] + other[...]


def call(kernel, outs, args, scratch=(), space=pltpu.VMEM):
    shapes = [jax.ShapeDtypeStruct(out, jnp.float32) if isinstance(out, tuple) else out for out in outs]
    return pl.pallas_call(
        kernel,
        out_shape=shapes,
        in_specs=[pl.BlockSpec(memory_space=space)] * len(args),
        out_specs=[pl.BlockSpec(memory_space=pltpu.VMEM)] * len(outs),
        scratch_shapes=list(scratch),
        compiler_params=pltpu.CompilerParams(vmem_limit_bytes=32 * 1024 * 1024),
    )(*args)


def ring_moved(value, axis):
    size = lax.axis_size(axis)
    return lax.ppermute(value, axis, [((k + 1) % size, k) for k in range(size)])


def chip_swapped(value):
    cores = lax.axis_size("load")
    return lax.ppermute(value, "load", [(core, cores - 1 - core) for core in range(cores)])


def opposed(value, z_step, y_step):
    cores, rows, size = lax.axis_size("load"), lax.axis_size("sy"), lax.axis_size("sz")
    pairs = []
    for core in range(cores):
        sign = -1 if core else 1
        for y in range(rows):
            for z in range(size):
                to_y, to_z, side = y + sign * y_step, z + sign * z_step, core
                if not (0 <= to_y < rows and 0 <= to_z < size):
                    to_y, to_z, side = y, z, cores - 1 - core
                pairs.append(((core * rows + y) * size + z, (side * rows + to_y) * size + to_z))
    return lax.ppermute(value, ("load", "sy", "sz"), pairs)


def body(displacements, density, solid, fixed):
    loads, comps, zlen, ylen, xlen = displacements.shape
    planes = loads * comps
    totals = (zlen * lax.axis_size("sz"), ylen * lax.axis_size("sy"))
    args = [
        pltpu.with_memory_space_constraint(arg, pltpu.HBM) for arg in (displacements, fixed, density, solid)
    ]

    disp, fixed, density, solid, z_send, y_send = call(
        lambda *refs: lead_kernel(totals, *refs),
        [jax.ShapeDtypeStruct(arg.shape, arg.dtype) for arg in args]
        + [(planes + 1, ylen, xlen), (planes * zlen, xlen)],
        args,
        scratch=[pltpu.SemaphoreType.DMA((len(args),))],
        space=pltpu.HBM,
    )
    z_in = opposed(z_send, -1, 0)
    y_in = ring_moved(y_send, "sy")
    nodes = lambda layers: pltpu.VMEM((planes, layers, ylen + TILE, xlen), jnp.float32)
    inner = call(
        lambda *refs: inner_kernel(totals, *refs),
        [
            (zlen, ylen, xlen),
            (2, planes * zlen, xlen),
            (2, REACH * (zlen - 1), xlen),
            (planes, ylen, xlen),
            (planes, ylen, xlen),
            (ylen, xlen),
            (TILE, xlen),
        ],
        (disp, fixed, density, solid),
        scratch=[nodes(zlen), nodes(zlen), pltpu.VMEM((zlen - 1, ylen + 2 * TILE, xlen), jnp.float32)],
    )
    own, line, sends, last_plus, last_diff, last_factor, edge = inner
    shape = displacements.shape
    padded = -(-(planes + 1) // TILE) * TILE
    (d_send,) = call(lambda *refs: pass_kernel(shape, *refs), [(-(-planes // TILE) * TILE, xlen)], (y_in,))
    d_in = opposed(d_send, -1, 0)
    (share,) = call(
        lambda *refs: lines_kernel(shape, *refs),
        [((zlen - 1) * (ylen + 2 * REACH), xlen)],
        (y_in, own, line, sends, edge),
    )
    own, ends, corner = call(
        lambda *refs: outer_kernel(shape, *refs),
        [(ylen, xlen), (TILE, xlen), (4, padded, xlen)],
        (z_in, last_plus, last_diff, last_factor),
        scratch=[
            nodes(4),
            nodes(4),
            pltpu.VMEM((ylen + 2 * TILE, xlen), jnp.float32),
            pltpu.VMEM((ylen, xlen), jnp.float32),
        ],
    )
    sent = (-(-REACH * zlen // TILE) * TILE, xlen)
    h, d_send, e_send, y_send, z_send, i_send = call(
        lambda *refs: total_kernel(shape, *refs),
        [(zlen, ylen, xlen), sent, sent, sent, (zlen, ylen, xlen), (TILE, xlen)],
        (share, chip_swapped(share), own, ends, corner, y_in, d_in),
    )
    d_in = opposed(d_send, 1, 1)
    e_in = opposed(e_send, 1, -1)
    y_in = opposed(y_send, 0, -1)
    z_in = opposed(z_send, 1, 0)
    i_in = opposed(i_send, 0, 1)
    (part,) = call(layers_kernel, [(zlen, ylen, xlen)], (h, d_in, e_in, y_in, z_in, i_in))
    (out,) = call(sum_kernel, [(zlen, ylen, xlen)], (part, chip_swapped(part)))
    return out


def solution(mesh):
    return jax.shard_map(
        body,
        mesh=mesh,
        in_specs=(
            P("load", None, "sz", "sy", None),
            P("sz", "sy", None),
            P("sz", "sy", None),
            P("sz", "sy", None),
        ),
        out_specs=P("sz", "sy", None),
        check_vma=False,
    )
```

```python
import jax
import jax.numpy as jnp
import numpy as np
from jax import lax
from jax.experimental import pallas as pl
from jax.experimental.pallas import tpu as pltpu
from jax.sharding import PartitionSpec as P

OFFSETS = [(0, 0, 0), (1, 0, 0), (1, 1, 0), (0, 1, 0), (0, 0, 1), (1, 0, 1), (1, 1, 1), (0, 1, 1)]
REACH = 3
ROWS = REACH + 1
TILE = 8
LANES = 128


def element_matrix():
    corners = np.array(
        [
            [-1.0, -1.0, -1.0],
            [1.0, -1.0, -1.0],
            [1.0, 1.0, -1.0],
            [-1.0, 1.0, -1.0],
            [-1.0, -1.0, 1.0],
            [1.0, -1.0, 1.0],
            [1.0, 1.0, 1.0],
            [-1.0, 1.0, 1.0],
        ]
    )
    poisson = 0.3
    lame = poisson / ((1.0 + poisson) * (1.0 - 2.0 * poisson))
    shear = 1.0 / (2.0 * (1.0 + poisson))
    elastic = np.zeros((6, 6))
    elastic[:3, :3] = lame
    for k in range(3):
        elastic[k, k] += 2.0 * shear
        elastic[3 + k, 3 + k] = shear
    gauss = 1.0 / np.sqrt(3.0)
    stiffness = np.zeros((24, 24))
    for gi in range(2):
        for gj in range(2):
            for gk in range(2):
                point = np.array([(2 * gi - 1) * gauss, (2 * gj - 1) * gauss, (2 * gk - 1) * gauss])
                strain = np.zeros((6, 24))
                for node in range(8):
                    grads = np.zeros(3)
                    for k in range(3):
                        value = corners[node, k] / 8.0
                        for m in range(3):
                            if m != k:
                                value = value * (1.0 + point[m] * corners[node, m])
                        grads[k] = 2.0 * value
                    col = 3 * node
                    strain[0, col] = grads[0]
                    strain[1, col + 1] = grads[1]
                    strain[2, col + 2] = grads[2]
                    strain[3, col] = grads[1]
                    strain[3, col + 1] = grads[0]
                    strain[4, col + 1] = grads[2]
                    strain[4, col + 2] = grads[1]
                    strain[5, col] = grads[2]
                    strain[5, col + 2] = grads[0]
                stiffness += strain.T @ elastic @ strain / 8.0
    return stiffness


def mode_weights():
    modes = [(i, j, k) for k in (0, 1) for j in (0, 1) for i in (0, 1)]
    sums = np.zeros((24, 24))
    for m, mode in enumerate(modes):
        for n, corner in enumerate(OFFSETS):
            sign = np.prod([(1 if corner[d] else -1) if mode[d] else 1 for d in range(3)])
            for comp in range(3):
                sums[3 * m + comp, 3 * n + comp] = sign
    form = sums @ element_matrix() @ sums.T / 64.0

    def at(first, second):
        return form[3 * modes.index(first[1]) + first[0], 3 * modes.index(second[1]) + second[0]]

    ux, vy, uy = (0, (1, 0, 0)), (1, (0, 1, 0)), (0, (0, 1, 0))
    uxy, wyz = (0, (1, 1, 0)), (2, (0, 1, 1))
    wxy, vxz, uxyz = (2, (1, 1, 0)), (1, (1, 0, 1)), (0, (1, 1, 1))
    return dict(
        normal=at(ux, ux) - at(ux, vy),
        trace=at(ux, vy),
        shear=at(uy, uy),
        plus=(at(uxy, uxy) + at(uxy, wyz)) / 2,
        minus=(at(uxy, uxy) - at(uxy, wyz)) / 2,
        twist=at(wxy, wxy) - at(wxy, vxz),
        twist_sum=at(wxy, vxz),
        corner=at(uxyz, uxyz),
    )


def square(value):
    return value * value


def quadratic(low, high, weights):
    x = [low[c][1] + high[c][1] for c in range(3)]
    y = [low[c][2] + high[c][2] for c in range(3)]
    z = [high[c][0] - low[c][0] for c in range(3)]
    xy = [low[c][3] + high[c][3] for c in range(3)]
    xz = [high[c][1] - low[c][1] for c in range(3)]
    yz = [high[c][2] - low[c][2] for c in range(3)]
    xyz = [high[c][3] - low[c][3] for c in range(3)]
    normal = square(x[0]) + square(y[1]) + square(z[2])
    trace = square(x[0] + y[1] + z[2])
    shear = square(y[0] + x[1]) + square(z[0] + x[2]) + square(z[1] + y[2])
    pairs = ((xy[0], yz[2]), (xy[1], xz[2]), (xz[0], yz[1]))
    plus = sum(square(p + q) for p, q in pairs)
    minus = sum(square(p - q) for p, q in pairs)
    twist = square(xy[2]) + square(xz[1]) + square(yz[0])
    twist_sum = square(xy[2] + xz[1] + yz[0])
    corner = square(xyz[0]) + square(xyz[1]) + square(xyz[2])
    groups = dict(
        normal=normal, trace=trace, shear=shear, plus=plus, minus=minus, twist=twist, twist_sum=twist_sum, corner=corner
    )
    return sum(np.float32(weights[name]) * group for name, group in groups.items())


def line_weight(coord, count):
    def outside(distance):
        missing = jnp.maximum(REACH - distance, 0)
        return missing * (missing + 1) // 2

    whole = (REACH + 1) * (REACH + 1)
    return (whole - outside(coord) - outside(count - 1 - coord)).astype(jnp.float32)


def voxel_factor(density, solid, plane, first_row, total_z, total_y):
    rows, length = density.shape
    row = lax.broadcasted_iota(jnp.int32, (rows, length), 0) + first_row
    column = lax.broadcasted_iota(jnp.int32, (rows, length), 1)
    weight = line_weight(row, total_y) * line_weight(column, length)
    weight = weight * line_weight(jnp.full((rows, length), plane, jnp.int32), total_z)
    return solid.astype(jnp.float32) * (-3.0 * density * density) / weight


def spread_x(value):
    rows, length = value.shape
    wide = jnp.concatenate([value, jnp.zeros((rows, LANES), jnp.float32)], axis=1)
    span = length + LANES
    total = float(ROWS) * value
    for step in range(1, ROWS):
        both = pltpu.roll(wide, span - step, 1) + pltpu.roll(wide, step, 1)
        total = total + float(ROWS - step) * both[:, :length]
    return total


def spread_layers(layers):
    for step in (1, 2, 1, 2):
        layers = [layers[k] + layers[k + step] for k in range(len(layers) - step)]
    return layers


def held(disp, fixed, case, comp, z, rows):
    return disp[case, comp, z, rows] * (1.0 - fixed[z, rows].astype(jnp.float32))


def split_x(value):
    length = value.shape[1]
    column = lax.broadcasted_iota(jnp.int32, value.shape, 1)
    ahead = jnp.where(column == length - 1, 0.0, pltpu.roll(value, length - 1, 1))
    return value + ahead, ahead - value


def spread_y(quotient, ylen):
    rows = [quotient[TILE + step : TILE + step + ylen] for step in range(-REACH, REACH + 1)]
    return sum((ROWS - abs(k - REACH)) * rows[k] for k in range(2 * REACH + 1))


def to_neighbours(quotient, ylen):
    top = quotient[ylen : ylen + TILE]
    base = quotient[TILE : 2 * TILE]
    ahead, back = [], []
    for row in range(REACH):
        ahead.append(sum(float(REACH - row - k) * top[TILE - 1 - k : TILE - k] for k in range(REACH - row)))
        back.append(sum(float(row + 1 - k) * base[k : k + 1] for k in range(row + 1)))
    return ahead, back


def on_first():
    return lax.axis_index("load") == 0


def lead_kernel(totals, disp_hbm, fixed_hbm, density_hbm, solid_hbm, disp, fixed, density, solid, d_out, z_out, y_out, sems):
    loads, comps, zlen, ylen, _ = disp.shape
    copies = [
        pltpu.make_async_copy(source, target, sems.at[k])
        for k, (source, target) in enumerate(
            ((disp_hbm, disp), (fixed_hbm, fixed), (density_hbm, density), (solid_hbm, solid))
        )
    ]
    for copy in copies:
        copy.start()
    for copy in copies:
        copy.wait()
    gives = jnp.where(on_first(), 0, zlen - 1)
    plane = lax.axis_index("sz") * zlen + gives
    base_y = lax.axis_index("sy") * ylen
    d_out[...] = jnp.zeros(d_out.shape, jnp.float32)
    z_out[loads * comps] = voxel_factor(density[gives], solid[gives], plane, base_y, *totals)
    for case in range(loads):
        for comp in range(comps):
            k = case * comps + comp
            z_out[k] = held(disp, fixed, case, comp, gives, slice(None))
            d_out[k : k + 1] = z_out[k, :1]
            for z in range(zlen):
                at = (comp * loads + case) * zlen + z
                y_out[at : at + 1] = held(disp, fixed, case, comp, z, slice(0, 1))


def tile_energies(plus, diff, first, lanes, layers, loads, comps, base=0):
    weights = mode_weights()

    def faces(k, z):
        near, far = slice(first, first + TILE), slice(first + 1, first + TILE + 1)
        whole, whole_next = plus[k, z, near, lanes], plus[k, z, far, lanes]
        change, change_next = diff[k, z, near, lanes], diff[k, z, far, lanes]
        return whole + whole_next, change + change_next, whole_next - whole, change_next - change

    energy = [None] * layers
    for case in range(loads):
        low = None
        for z in range(layers + 1):
            high = [faces(case * comps + comp, base + z) for comp in range(comps)]
            if low is not None:
                part = quadratic(low, high, weights)
                energy[z - 1] = part if energy[z - 1] is None else energy[z - 1] + part
            low = high
    return energy


def blank_last(value, first, ylen):
    row = lax.broadcasted_iota(jnp.int32, value.shape, 0) + first
    return jnp.where(row == ylen - 1, 0.0, value)


def inner_kernel(totals, disp, fixed, density, solid, own, line, sends, last_plus, last_diff, last_factor, edge, plus, diff, quotient):
    loads, comps, zlen, ylen, xlen = disp.shape
    total_z, total_y = totals
    base_z = lax.axis_index("sz") * zlen
    base_y = lax.axis_index("sy") * ylen
    inner = zlen - 1
    keeps = jnp.where(on_first(), inner, 0)

    @pl.loop(0, loads * comps, unroll=True)
    def _(k):
        case, comp = k // comps, k % comps
        for z in range(zlen):
            whole, change = split_x(held(disp, fixed, case, comp, z, slice(None)))
            plus[k, z, :ylen] = whole
            diff[k, z, :ylen] = change
        last_plus[k] = plus[k, keeps, :ylen]
        last_diff[k] = diff[k, keeps, :ylen]

    for comp in range(comps):
        for case in range(loads):
            for z in range(zlen):
                at = (comp * loads + case) * zlen + z
                line[0, at : at + 1] = plus[case * comps + comp, z, ylen - 1 : ylen]
                line[1, at : at + 1] = diff[case * comps + comp, z, ylen - 1 : ylen]

    zeros = jnp.zeros((TILE, xlen), jnp.float32)
    edge[...] = jnp.zeros(edge.shape, jnp.float32)
    for z in range(zlen):
        factor = voxel_factor(density[z], solid[z], base_z + z, base_y, total_z, total_y)
        edge[z : z + 1] = factor[ylen - 1 :]
        if z == inner:
            last_factor[...] = factor
        else:
            quotient[z, :TILE] = zeros
            quotient[z, TILE : TILE + ylen] = factor
            quotient[z, TILE + ylen :] = zeros

    for first in range(0, ylen, TILE):

        @pl.loop(0, xlen // LANES, unroll=True)
        def _(chunk):
            lanes = pl.ds(pl.multiple_of(chunk * LANES, LANES), LANES)
            energy = tile_energies(plus, diff, first, lanes, inner, loads, comps)
            for z in range(inner):
                here = quotient[z, first + TILE : first + 2 * TILE, lanes]
                quotient[z, first + TILE : first + 2 * TILE, lanes] = blank_last(energy[z] * here, first, ylen)

    for z in range(inner):
        own[z] = spread_x(spread_y(quotient.at[z], ylen))
        ahead, back = to_neighbours(quotient.at[z], ylen)
        ends = spread_x(jnp.concatenate(ahead + back + [zeros[:2]], axis=0))
        sends[0, REACH * z : REACH * (z + 1)] = ends[:REACH]
        sends[1, REACH * z : REACH * (z + 1)] = ends[REACH : 2 * REACH]


def outer_kernel(
    shape, d_in, z_in, y_in, own_in, line, sends, last_plus, last_diff, last_factor, edge, share, plus, diff, quotient, factor
):
    loads, comps, zlen, ylen, xlen = shape
    planes = loads * comps
    inner = zlen - 1
    first_core, index = on_first(), lax.axis_index("sz")
    top = first_core & (index == lax.axis_size("sz") - 1)
    more = lax.axis_index("sy") < lax.axis_size("sy") - 1
    stays, comes = jnp.where(first_core, 0, 1), jnp.where(first_core, jnp.where(top, 2, 1), 0)
    y_rows = jnp.where(more, y_in[...], 0.0)
    y_plus, y_diff = split_x(y_rows)
    d_plus, d_diff = split_x(jnp.where(more, d_in[...], 0.0))
    for k in range(planes):
        case, comp = k // comps, k % comps
        at = (comp * loads + case) * zlen
        beside = jnp.where(first_core, y_plus[at + inner : at + zlen], y_plus[at : at + 1])
        beside_diff = jnp.where(first_core, y_diff[at + inner : at + zlen], y_diff[at : at + 1])
        plus[k, stays, :ylen] = last_plus[k]
        diff[k, stays, :ylen] = last_diff[k]
        plus[k, stays, ylen : ylen + 1] = beside
        diff[k, stays, ylen : ylen + 1] = beside_diff
        whole, change = split_x(z_in[k])
        plus[k, comes, :ylen] = whole
        diff[k, comes, :ylen] = change
        plus[k, comes, ylen : ylen + 1] = d_plus[k : k + 1]
        diff[k, comes, ylen : ylen + 1] = d_diff[k : k + 1]
    below = jnp.where(index > 0, z_in[planes], 0.0)
    factor[...] = jnp.where(first_core, last_factor[...], below)

    @pl.when(top)
    def _():
        clamped = jnp.zeros((ylen + TILE, xlen), jnp.float32)
        for k in range(planes):
            for slot in (1, 3):
                plus[k, slot] = clamped
                diff[k, slot] = clamped

    zeros = jnp.zeros((TILE, xlen), jnp.float32)
    quotient[:TILE] = zeros
    quotient[TILE + ylen :] = zeros
    for first in range(0, ylen, TILE):

        @pl.loop(0, xlen // LANES, unroll=True)
        def _(chunk):
            lanes = pl.ds(pl.multiple_of(chunk * LANES, LANES), LANES)
            (energy,) = tile_energies(plus, diff, first, lanes, 1, loads, comps)
            quotient[first + TILE : first + 2 * TILE, lanes] = energy * factor[first : first + TILE, lanes]

    @pl.when(top)
    def _():
        for first in range(0, ylen, TILE):

            @pl.loop(0, xlen // LANES, unroll=True)
            def _(chunk):
                lanes = pl.ds(pl.multiple_of(chunk * LANES, LANES), LANES)
                (energy,) = tile_energies(plus, diff, first, lanes, 1, loads, comps, base=2)
                quotient[first + TILE : first + 2 * TILE, lanes] += energy * factor[first : first + TILE, lanes]

    count = loads * zlen
    low, high = [], []
    for comp in range(comps):
        part = slice(comp * count, (comp + 1) * count)
        whole, change = line[0, part], line[1, part]
        whole_next, change_next = y_plus[part], y_diff[part]
        face = (whole + whole_next, change + change_next, whole_next - whole, change_next - change)
        low.append(face)
        high.append([pltpu.roll(value, count - 1, 0) for value in face])
    energy = quadratic(low, high, mode_weights())
    energy = sum(energy[case * zlen : case * zlen + inner] for case in range(loads)) * edge[:inner]
    last = spread_x(jnp.concatenate([energy, jnp.zeros((TILE - inner, xlen), jnp.float32)], axis=0))

    row = lax.broadcasted_iota(jnp.int32, (TILE, xlen), 0)
    rising = jnp.maximum(row - (TILE - 1 - ROWS), 0).astype(jnp.float32)
    ups, downs = [], []
    for z in range(inner):
        share[ylen * z : ylen * (z + 1)] = own_in[z]
        share[ylen * (z + 1) - TILE : ylen * (z + 1)] += rising * last[z : z + 1]
        here = sends[0, REACH * z : REACH * (z + 1)]
        ups += [here[r : r + 1] + float(REACH - r) * last[z : z + 1] for r in range(REACH)]
        downs.append(sends[1, REACH * z : REACH * (z + 1)])
    share[ylen * inner : ylen * zlen] = spread_x(spread_y(quotient, ylen))
    ahead, back = to_neighbours(quotient, ylen)
    ends = spread_x(jnp.concatenate(ahead + back + [zeros[:2]], axis=0))
    share[ylen * zlen :] = jnp.concatenate(ups + [ends[:REACH]] + downs + [ends[REACH : 2 * REACH]], axis=0)


def total_kernel(shape, share, other, h_out, z_out, y_out, d_out, e_out):
    _, _, zlen, ylen, xlen = shape
    first_core = on_first()
    inner, rows = zlen - 1, ylen * zlen
    reach = REACH * zlen

    def layers(first, count):
        mine, theirs = share[first + inner * count : first + zlen * count], other[first + inner * count : first + zlen * count]
        middle = share[first : first + inner * count] + other[first : first + inner * count]
        return jnp.where(first_core, theirs, mine), middle, jnp.where(first_core, mine, theirs)

    lowest, middle, highest = layers(0, ylen)
    h_out[0] = lowest
    for z in range(inner):
        h_out[z + 1] = middle[ylen * z : ylen * (z + 1)]
    h_out[zlen] = highest
    z_out[...] = h_out[pl.ds(jnp.where(first_core, 0, 1), zlen)]
    ups = jnp.concatenate(layers(rows, REACH), axis=0)
    downs = jnp.concatenate(layers(rows + reach, REACH), axis=0)
    y_out[: reach + REACH] = jnp.where(first_core, downs, ups)
    for out, used in ((y_out, reach + REACH), (d_out, reach), (e_out, reach)):
        out[used:] = jnp.zeros((out.shape[0] - used, xlen), jnp.float32)
    d_out[:reach] = jnp.where(first_core, downs[:reach], ups[REACH:])
    e_out[:reach] = jnp.where(first_core, ups[:reach], downs[REACH:])


def layers_kernel(h, d_in, e_in, y_in, z_in, out):
    zlen, ylen, xlen = out.shape
    reach = REACH * zlen
    first_core = on_first()
    z_index, z_last = lax.axis_index("sz"), lax.axis_size("sz") - 1
    y_index, y_last = lax.axis_index("sy"), lax.axis_size("sy") - 1
    z_side = jnp.where(first_core, z_index < z_last, z_index > 0)
    y_side = jnp.where(first_core, y_index < y_last, y_index > 0)
    y_other = jnp.where(first_core, y_index > 0, y_index < y_last)
    blank = jnp.zeros((TILE - REACH, xlen), jnp.float32)

    def at_start(rows):
        return jnp.concatenate([rows, blank], axis=0)

    def at_end(rows):
        return jnp.concatenate([blank, rows], axis=0)

    def ends(rows, keep, at_last):
        rows = jnp.where(keep, rows, 0.0)
        return at_start(jnp.where(at_last, 0.0, rows)), at_end(jnp.where(at_last, rows, 0.0))

    def with_ends(layer, *pairs):
        head, tail = layer[:TILE], layer[ylen - TILE :]
        for first, last in pairs:
            head, tail = head + first, tail + last
        return jnp.concatenate([head, layer[TILE : ylen - TILE], tail] if ylen > 2 * TILE else [head, tail], axis=0)

    own = []
    for k in range(zlen + 1):
        layer = jnp.where(first_core, h[k], 0.0)
        own.append(with_ends(layer, ends(y_in[REACH * k : REACH * (k + 1)], y_side, first_core)))
    come = []
    for k in range(zlen):
        part = slice(REACH * k, REACH * (k + 1))
        layer = jnp.where(z_side, z_in[k], 0.0)
        straight = ends(d_in[part], z_side & y_side, first_core)
        across = ends(e_in[part], z_side & y_other, jnp.logical_not(first_core))
        come.append(with_ends(layer, straight, across))
    below = [jnp.where(first_core, 0.0, layer) for layer in come[zlen - REACH :]]
    above = [jnp.where(first_core, layer, 0.0) for layer in come]
    layers = below[:-1] + [below[-1] + own[0]] + own[1:-1] + [own[-1] + above[0]] + above[1:]
    for z, layer in enumerate(spread_layers(layers)):
        out[z] = layer


def sum_kernel(part, other, out):
    out[...] = part[...] + other[...]


def call(kernel, outs, args, scratch=(), space=pltpu.VMEM):
    shapes = [jax.ShapeDtypeStruct(out, jnp.float32) if isinstance(out, tuple) else out for out in outs]
    return pl.pallas_call(
        kernel,
        out_shape=shapes,
        in_specs=[pl.BlockSpec(memory_space=space)] * len(args),
        out_specs=[pl.BlockSpec(memory_space=pltpu.VMEM)] * len(outs),
        scratch_shapes=list(scratch),
        compiler_params=pltpu.CompilerParams(vmem_limit_bytes=32 * 1024 * 1024),
    )(*args)


def ring_moved(value, axis):
    size = lax.axis_size(axis)
    return lax.ppermute(value, axis, [((k + 1) % size, k) for k in range(size)])


def chip_swapped(value):
    cores = lax.axis_size("load")
    return lax.ppermute(value, "load", [(core, cores - 1 - core) for core in range(cores)])


def opposed(value, z_step, y_step, y_shift=0):
    cores, rows, size = lax.axis_size("load"), lax.axis_size("sy"), lax.axis_size("sz")
    pairs = []
    for core in range(cores):
        sign = -1 if core else 1
        for y in range(rows):
            for z in range(size):
                to_y, to_z, side = y + sign * y_step, z + sign * z_step, core
                if not (0 <= to_y < rows and 0 <= to_z < size):
                    to_y, to_z, side = y, z, cores - 1 - core
                to_y = (to_y + y_shift) % rows
                pairs.append(((core * rows + y) * size + z, (side * rows + to_y) * size + to_z))
    return lax.ppermute(value, ("load", "sy", "sz"), pairs)


def body(displacements, density, solid, fixed):
    loads, comps, zlen, ylen, xlen = displacements.shape
    planes = loads * comps
    totals = (zlen * lax.axis_size("sz"), ylen * lax.axis_size("sy"))
    args = [
        pltpu.with_memory_space_constraint(arg, pltpu.HBM) for arg in (displacements, fixed, density, solid)
    ]

    disp, fixed, density, solid, d_send, z_send, y_send = call(
        lambda *refs: lead_kernel(totals, *refs),
        [jax.ShapeDtypeStruct(arg.shape, arg.dtype) for arg in args]
        + [(-(-planes // TILE) * TILE, xlen), (planes + 1, ylen, xlen), (planes * zlen, xlen)],
        args,
        scratch=[pltpu.SemaphoreType.DMA((len(args),))],
        space=pltpu.HBM,
    )
    d_in = opposed(d_send, -1, 0, y_shift=-1)
    z_in = opposed(z_send, -1, 0)
    y_in = ring_moved(y_send, "sy")
    nodes = lambda layers: pltpu.VMEM((planes, layers, ylen + TILE, xlen), jnp.float32)
    inner = call(
        lambda *refs: inner_kernel(totals, *refs),
        [
            (zlen, ylen, xlen),
            (2, planes * zlen, xlen),
            (2, REACH * (zlen - 1), xlen),
            (planes, ylen, xlen),
            (planes, ylen, xlen),
            (ylen, xlen),
            (TILE, xlen),
        ],
        (disp, fixed, density, solid),
        scratch=[nodes(zlen), nodes(zlen), pltpu.VMEM((zlen - 1, ylen + 2 * TILE, xlen), jnp.float32)],
    )
    reach = REACH * zlen
    (share,) = call(
        lambda *refs: outer_kernel(displacements.shape, *refs),
        [(ylen * zlen + 2 * reach, xlen)],
        (d_in, z_in, y_in, *inner),
        scratch=[
            nodes(4),
            nodes(4),
            pltpu.VMEM((ylen + 2 * TILE, xlen), jnp.float32),
            pltpu.VMEM((ylen, xlen), jnp.float32),
        ],
    )
    sent = (-(-(reach + REACH) // TILE) * TILE, xlen)
    h, z_send, y_send, d_send, e_send = call(
        lambda *refs: total_kernel(displacements.shape, *refs),
        [
            (zlen + 1, ylen, xlen),
            (zlen, ylen, xlen),
            sent,
            sent,
            sent,
        ],
        (share, chip_swapped(share)),
    )
    d_in = opposed(d_send, -1, -1)
    e_in = opposed(e_send, -1, 1)
    y_in = opposed(y_send, 0, -1)
    z_in = opposed(z_send, -1, 0)
    (part,) = call(layers_kernel, [(zlen, ylen, xlen)], (h, d_in, e_in, y_in, z_in))
    (out,) = call(sum_kernel, [(zlen, ylen, xlen)], (part, chip_swapped(part)))
    return out


def solution(mesh):
    return jax.shard_map(
        body,
        mesh=mesh,
        in_specs=(
            P("load", None, "sz", "sy", None),
            P("sz", "sy", None),
            P("sz", "sy", None),
            P("sz", "sy", None),
        ),
        out_specs=P("sz", "sy", None),
        check_vma=False,
    )
```

```python
import jax
import jax.numpy as jnp
import numpy as np
from jax import lax
from jax.experimental import pallas as pl
from jax.experimental.pallas import tpu as pltpu
from jax.sharding import PartitionSpec as P

OFFSETS = [(0, 0, 0), (1, 0, 0), (1, 1, 0), (0, 1, 0), (0, 0, 1), (1, 0, 1), (1, 1, 1), (0, 1, 1)]
REACH = 3
ROWS = REACH + 1
TILE = 8
LANES = 128


def element_matrix():
    corners = np.array(
        [
            [-1.0, -1.0, -1.0],
            [1.0, -1.0, -1.0],
            [1.0, 1.0, -1.0],
            [-1.0, 1.0, -1.0],
            [-1.0, -1.0, 1.0],
            [1.0, -1.0, 1.0],
            [1.0, 1.0, 1.0],
            [-1.0, 1.0, 1.0],
        ]
    )
    poisson = 0.3
    lame = poisson / ((1.0 + poisson) * (1.0 - 2.0 * poisson))
    shear = 1.0 / (2.0 * (1.0 + poisson))
    elastic = np.zeros((6, 6))
    elastic[:3, :3] = lame
    for k in range(3):
        elastic[k, k] += 2.0 * shear
        elastic[3 + k, 3 + k] = shear
    gauss = 1.0 / np.sqrt(3.0)
    stiffness = np.zeros((24, 24))
    for gi in range(2):
        for gj in range(2):
            for gk in range(2):
                point = np.array([(2 * gi - 1) * gauss, (2 * gj - 1) * gauss, (2 * gk - 1) * gauss])
                strain = np.zeros((6, 24))
                for node in range(8):
                    grads = np.zeros(3)
                    for k in range(3):
                        value = corners[node, k] / 8.0
                        for m in range(3):
                            if m != k:
                                value = value * (1.0 + point[m] * corners[node, m])
                        grads[k] = 2.0 * value
                    col = 3 * node
                    strain[0, col] = grads[0]
                    strain[1, col + 1] = grads[1]
                    strain[2, col + 2] = grads[2]
                    strain[3, col] = grads[1]
                    strain[3, col + 1] = grads[0]
                    strain[4, col + 1] = grads[2]
                    strain[4, col + 2] = grads[1]
                    strain[5, col] = grads[2]
                    strain[5, col + 2] = grads[0]
                stiffness += strain.T @ elastic @ strain / 8.0
    return stiffness


def mode_weights():
    modes = [(i, j, k) for k in (0, 1) for j in (0, 1) for i in (0, 1)]
    sums = np.zeros((24, 24))
    for m, mode in enumerate(modes):
        for n, corner in enumerate(OFFSETS):
            sign = np.prod([(1 if corner[d] else -1) if mode[d] else 1 for d in range(3)])
            for comp in range(3):
                sums[3 * m + comp, 3 * n + comp] = sign
    form = sums @ element_matrix() @ sums.T / 64.0

    def at(first, second):
        return form[3 * modes.index(first[1]) + first[0], 3 * modes.index(second[1]) + second[0]]

    ux, vy, uy = (0, (1, 0, 0)), (1, (0, 1, 0)), (0, (0, 1, 0))
    uxy, wyz = (0, (1, 1, 0)), (2, (0, 1, 1))
    wxy, vxz, uxyz = (2, (1, 1, 0)), (1, (1, 0, 1)), (0, (1, 1, 1))
    return dict(
        normal=at(ux, ux) - at(ux, vy),
        trace=at(ux, vy),
        shear=at(uy, uy),
        plus=(at(uxy, uxy) + at(uxy, wyz)) / 2,
        minus=(at(uxy, uxy) - at(uxy, wyz)) / 2,
        twist=at(wxy, wxy) - at(wxy, vxz),
        twist_sum=at(wxy, vxz),
        corner=at(uxyz, uxyz),
    )


def square(value):
    return value * value


def quadratic(low, high, weights):
    x = [low[c][1] + high[c][1] for c in range(3)]
    y = [low[c][2] + high[c][2] for c in range(3)]
    z = [high[c][0] - low[c][0] for c in range(3)]
    xy = [low[c][3] + high[c][3] for c in range(3)]
    xz = [high[c][1] - low[c][1] for c in range(3)]
    yz = [high[c][2] - low[c][2] for c in range(3)]
    xyz = [high[c][3] - low[c][3] for c in range(3)]
    normal = square(x[0]) + square(y[1]) + square(z[2])
    trace = square(x[0] + y[1] + z[2])
    shear = square(y[0] + x[1]) + square(z[0] + x[2]) + square(z[1] + y[2])
    pairs = ((xy[0], yz[2]), (xy[1], xz[2]), (xz[0], yz[1]))
    plus = sum(square(p + q) for p, q in pairs)
    minus = sum(square(p - q) for p, q in pairs)
    twist = square(xy[2]) + square(xz[1]) + square(yz[0])
    twist_sum = square(xy[2] + xz[1] + yz[0])
    corner = square(xyz[0]) + square(xyz[1]) + square(xyz[2])
    groups = dict(
        normal=normal, trace=trace, shear=shear, plus=plus, minus=minus, twist=twist, twist_sum=twist_sum, corner=corner
    )
    return sum(np.float32(weights[name]) * group for name, group in groups.items())


def line_weight(coord, count):
    def outside(distance):
        missing = jnp.maximum(REACH - distance, 0)
        return missing * (missing + 1) // 2

    whole = (REACH + 1) * (REACH + 1)
    return (whole - outside(coord) - outside(count - 1 - coord)).astype(jnp.float32)


def voxel_factor(density, solid, plane, first_row, total_z, total_y):
    rows, length = density.shape
    row = lax.broadcasted_iota(jnp.int32, (rows, length), 0) + first_row
    column = lax.broadcasted_iota(jnp.int32, (rows, length), 1)
    weight = line_weight(row, total_y) * line_weight(column, length)
    weight = weight * line_weight(jnp.full((rows, length), plane, jnp.int32), total_z)
    return solid.astype(jnp.float32) * (-3.0 * density * density) / weight


def spread_x(value):
    rows, length = value.shape
    wide = jnp.concatenate([value, jnp.zeros((rows, LANES), jnp.float32)], axis=1)
    span = length + LANES
    total = float(ROWS) * value
    for step in range(1, ROWS):
        both = pltpu.roll(wide, span - step, 1) + pltpu.roll(wide, step, 1)
        total = total + float(ROWS - step) * both[:, :length]
    return total


def spread_layers(layers):
    for step in (1, 2, 1, 2):
        layers = [layers[k] + layers[k + step] for k in range(len(layers) - step)]
    return layers


def held(disp, fixed, case, comp, z, rows):
    return disp[case, comp, z, rows] * (1.0 - fixed[z, rows].astype(jnp.float32))


def split_x(value):
    length = value.shape[1]
    column = lax.broadcasted_iota(jnp.int32, value.shape, 1)
    ahead = jnp.where(column == length - 1, 0.0, pltpu.roll(value, length - 1, 1))
    return value + ahead, ahead - value


def spread_y(quotient, ylen):
    rows = [quotient[TILE + step : TILE + step + ylen] for step in range(-REACH, REACH + 1)]
    return sum((ROWS - abs(k - REACH)) * rows[k] for k in range(2 * REACH + 1))


def to_neighbours(quotient, ylen):
    top = quotient[ylen : ylen + TILE]
    base = quotient[TILE : 2 * TILE]
    ahead, back = [], []
    for row in range(REACH):
        ahead.append(sum(float(REACH - row - k) * top[TILE - 1 - k : TILE - k] for k in range(REACH - row)))
        back.append(sum(float(row + 1 - k) * base[k : k + 1] for k in range(row + 1)))
    return ahead, back


def on_first():
    return lax.axis_index("load") == 0


def lead_kernel(totals, disp_hbm, fixed_hbm, density_hbm, solid_hbm, d_out, z_out, y_out, layer, layer_fixed, density, solid, rows, rows_fixed, sems):
    loads, comps, zlen, ylen, _ = disp_hbm.shape
    gives = jnp.where(on_first(), 0, zlen - 1)
    copies = [
        pltpu.make_async_copy(source, target, sems.at[k])
        for k, (source, target) in enumerate(
            (
                (density_hbm.at[gives], density),
                (solid_hbm.at[gives], solid),
                (fixed_hbm.at[gives], layer_fixed),
                (disp_hbm.at[:, :, gives], layer),
                (fixed_hbm.at[:, :TILE], rows_fixed),
                (disp_hbm.at[:, :, :, :TILE], rows),
            )
        )
    ]
    for copy in copies:
        copy.start()
    for copy in copies[:2]:
        copy.wait()
    plane = lax.axis_index("sz") * zlen + gives
    base_y = lax.axis_index("sy") * ylen
    d_out[...] = jnp.zeros(d_out.shape, jnp.float32)
    z_out[loads * comps] = voxel_factor(density[...], solid[...], plane, base_y, *totals)
    for copy in copies[2:4]:
        copy.wait()
    free = 1.0 - layer_fixed[...].astype(jnp.float32)
    for case in range(loads):
        for comp in range(comps):
            k = case * comps + comp
            z_out[k] = layer[case, comp] * free
            d_out[k : k + 1] = z_out[k, :1]
    for copy in copies[4:]:
        copy.wait()
    for z in range(zlen):
        free = 1.0 - rows_fixed[z, :1].astype(jnp.float32)
        for case in range(loads):
            for comp in range(comps):
                at = (comp * loads + case) * zlen + z
                y_out[at : at + 1] = rows[case, comp, z, :1] * free


def tile_energies(plus, diff, first, lanes, layers, loads, comps, base=0):
    weights = mode_weights()

    def faces(k, z):
        near, far = slice(first, first + TILE), slice(first + 1, first + TILE + 1)
        whole, whole_next = plus[k, z, near, lanes], plus[k, z, far, lanes]
        change, change_next = diff[k, z, near, lanes], diff[k, z, far, lanes]
        return whole + whole_next, change + change_next, whole_next - whole, change_next - change

    energy = [None] * layers
    for case in range(loads):
        low = None
        for z in range(layers + 1):
            high = [faces(case * comps + comp, base + z) for comp in range(comps)]
            if low is not None:
                part = quadratic(low, high, weights)
                energy[z - 1] = part if energy[z - 1] is None else energy[z - 1] + part
            low = high
    return energy


def blank_last(value, first, ylen):
    row = lax.broadcasted_iota(jnp.int32, value.shape, 0) + first
    return jnp.where(row == ylen - 1, 0.0, value)


def inner_kernel(totals, disp, fixed, density, solid, own, line, sends, last_plus, last_diff, last_factor, edge, plus, diff, quotient):
    loads, comps, zlen, ylen, xlen = disp.shape
    total_z, total_y = totals
    base_z = lax.axis_index("sz") * zlen
    base_y = lax.axis_index("sy") * ylen
    inner = zlen - 1
    keeps = jnp.where(on_first(), inner, 0)

    @pl.loop(0, loads * comps, unroll=True)
    def _(k):
        case, comp = k // comps, k % comps
        for z in range(zlen):
            whole, change = split_x(held(disp, fixed, case, comp, z, slice(None)))
            plus[k, z, :ylen] = whole
            diff[k, z, :ylen] = change
        last_plus[k] = plus[k, keeps, :ylen]
        last_diff[k] = diff[k, keeps, :ylen]

    for comp in range(comps):
        for case in range(loads):
            for z in range(zlen):
                at = (comp * loads + case) * zlen + z
                line[0, at : at + 1] = plus[case * comps + comp, z, ylen - 1 : ylen]
                line[1, at : at + 1] = diff[case * comps + comp, z, ylen - 1 : ylen]

    zeros = jnp.zeros((TILE, xlen), jnp.float32)
    edge[...] = jnp.zeros(edge.shape, jnp.float32)
    for z in range(zlen):
        factor = voxel_factor(density[z], solid[z], base_z + z, base_y, total_z, total_y)
        edge[z : z + 1] = factor[ylen - 1 :]
        if z == inner:
            last_factor[...] = factor
        else:
            quotient[z, :TILE] = zeros
            quotient[z, TILE : TILE + ylen] = factor
            quotient[z, TILE + ylen :] = zeros

    for first in range(0, ylen, TILE):

        @pl.loop(0, xlen // LANES, unroll=True)
        def _(chunk):
            lanes = pl.ds(pl.multiple_of(chunk * LANES, LANES), LANES)
            energy = tile_energies(plus, diff, first, lanes, inner, loads, comps)
            for z in range(inner):
                here = quotient[z, first + TILE : first + 2 * TILE, lanes]
                quotient[z, first + TILE : first + 2 * TILE, lanes] = blank_last(energy[z] * here, first, ylen)

    for z in range(inner):
        own[z] = spread_x(spread_y(quotient.at[z], ylen))
        ahead, back = to_neighbours(quotient.at[z], ylen)
        ends = spread_x(jnp.concatenate(ahead + back + [zeros[:2]], axis=0))
        sends[0, REACH * z : REACH * (z + 1)] = ends[:REACH]
        sends[1, REACH * z : REACH * (z + 1)] = ends[REACH : 2 * REACH]


def outer_kernel(
    shape, z_in, y_in, own_in, line, sends, last_plus, last_diff, last_factor, edge, share, corner, plus, diff, quotient, factor
):
    loads, comps, zlen, ylen, xlen = shape
    planes = loads * comps
    inner = zlen - 1
    first_core, index = on_first(), lax.axis_index("sz")
    top = first_core & (index == lax.axis_size("sz") - 1)
    more = lax.axis_index("sy") < lax.axis_size("sy") - 1
    stays, comes = jnp.where(first_core, 0, 1), jnp.where(first_core, jnp.where(top, 2, 1), 0)
    y_plus, y_diff = split_x(jnp.where(more, y_in[...], 0.0))
    for k in range(planes):
        plus[k, stays, :ylen] = last_plus[k]
        diff[k, stays, :ylen] = last_diff[k]
        whole, change = split_x(z_in[k])
        plus[k, comes, :ylen] = whole
        diff[k, comes, :ylen] = change
        for group, value in enumerate((last_plus[k, ylen - 1 :], last_diff[k, ylen - 1 :], whole[ylen - 1 :], change[ylen - 1 :])):
            corner[group, k : k + 1] = value
    below = jnp.where(index > 0, z_in[planes], 0.0)
    factor[...] = jnp.where(first_core, last_factor[...], below)
    corner[0, planes : planes + 1] = factor[ylen - 1 :]

    @pl.when(top)
    def _():
        clamped = jnp.zeros((ylen + TILE, xlen), jnp.float32)
        for k in range(planes):
            for slot in (1, 3):
                plus[k, slot] = clamped
                diff[k, slot] = clamped

    zeros = jnp.zeros((TILE, xlen), jnp.float32)
    quotient[:TILE] = zeros
    quotient[TILE + ylen :] = zeros
    for first in range(0, ylen, TILE):

        @pl.loop(0, xlen // LANES, unroll=True)
        def _(chunk):
            lanes = pl.ds(pl.multiple_of(chunk * LANES, LANES), LANES)
            (energy,) = tile_energies(plus, diff, first, lanes, 1, loads, comps)
            here = energy * factor[first : first + TILE, lanes]
            quotient[first + TILE : first + 2 * TILE, lanes] = blank_last(here, first, ylen)

    @pl.when(top)
    def _():
        for first in range(0, ylen, TILE):

            @pl.loop(0, xlen // LANES, unroll=True)
            def _(chunk):
                lanes = pl.ds(pl.multiple_of(chunk * LANES, LANES), LANES)
                (energy,) = tile_energies(plus, diff, first, lanes, 1, loads, comps, base=2)
                here = energy * factor[first : first + TILE, lanes]
                quotient[first + TILE : first + 2 * TILE, lanes] += blank_last(here, first, ylen)

    count = loads * zlen
    low, high = [], []
    for comp in range(comps):
        part = slice(comp * count, (comp + 1) * count)
        whole, change = line[0, part], line[1, part]
        whole_next, change_next = y_plus[part], y_diff[part]
        face = (whole + whole_next, change + change_next, whole_next - whole, change_next - change)
        low.append(face)
        high.append([pltpu.roll(value, count - 1, 0) for value in face])
    energy = quadratic(low, high, mode_weights())
    energy = sum(energy[case * zlen : case * zlen + inner] for case in range(loads)) * edge[:inner]
    last = spread_x(jnp.concatenate([energy, jnp.zeros((TILE - inner, xlen), jnp.float32)], axis=0))

    row = lax.broadcasted_iota(jnp.int32, (TILE, xlen), 0)
    rising = jnp.maximum(row - (TILE - 1 - ROWS), 0).astype(jnp.float32)
    ups, downs = [], []
    for z in range(inner):
        share[ylen * z : ylen * (z + 1)] = own_in[z]
        share[ylen * (z + 1) - TILE : ylen * (z + 1)] += rising * last[z : z + 1]
        here = sends[0, REACH * z : REACH * (z + 1)]
        ups += [here[r : r + 1] + float(REACH - r) * last[z : z + 1] for r in range(REACH)]
        downs.append(sends[1, REACH * z : REACH * (z + 1)])
    share[ylen * inner : ylen * zlen] = spread_x(spread_y(quotient, ylen))
    ahead, back = to_neighbours(quotient, ylen)
    ends = spread_x(jnp.concatenate(ahead + back + [zeros[:2]], axis=0))
    share[ylen * zlen :] = jnp.concatenate(ups + [ends[:REACH]] + downs + [ends[REACH : 2 * REACH]], axis=0)


def corner_line(shape, corner, y_in, d_in):
    loads, comps, zlen, ylen, xlen = shape
    planes = loads * comps
    first_core = on_first()
    top = first_core & (lax.axis_index("sz") == lax.axis_size("sz") - 1)
    more = lax.axis_index("sy") < lax.axis_size("sy") - 1
    rows = []
    for k in range(planes):
        at = (k % comps * loads + k // comps) * zlen
        rows.append(jnp.where(first_core, y_in[at + zlen - 1 : at + zlen], y_in[at : at + 1]))
    rows.append(jnp.zeros((-planes % TILE, xlen), jnp.float32))
    stays_next = split_x(jnp.where(more, jnp.concatenate(rows, axis=0), 0.0))
    comes_next = split_x(jnp.where(more, d_in[...], 0.0))

    def faces(stays, comes, comp):
        zero = jnp.zeros((1, xlen), jnp.float32)
        under, over = [], []
        for own, other in zip(stays, comes):
            own, other = ([value[case * comps + comp : case * comps + comp + 1] for case in range(loads)] for value in (own, other))
            low = [jnp.where(first_core, a, b) for a, b in zip(own, other)] + [jnp.where(top, b, 0.0) for b in other]
            high = [jnp.where(first_core, jnp.where(top, 0.0, b), a) for a, b in zip(own, other)] + [zero] * loads
            under.append(jnp.concatenate(low, axis=0))
            over.append(jnp.concatenate(high, axis=0))
        return under, over

    low, high = [], []
    for comp in range(comps):
        near = faces((corner[0], corner[1]), (corner[2], corner[3]), comp)
        far = faces(stays_next, comes_next, comp)
        for (whole, change), (whole_next, change_next), into in zip(near, far, (low, high)):
            into.append((whole + whole_next, change + change_next, whole_next - whole, change_next - change))
    energy = quadratic(low, high, mode_weights())
    line = sum(energy[case : case + 1] for case in range(2 * loads)) * corner[0, planes : planes + 1]
    return spread_x(jnp.concatenate([line, jnp.zeros((TILE - 1, xlen), jnp.float32)], axis=0))[:1]


def corner_kernel(shape, share_in, corner, y_in, d_in, share):
    _, _, zlen, ylen, xlen = shape
    line = corner_line(shape, corner, y_in, d_in)
    rising = jnp.maximum(lax.broadcasted_iota(jnp.int32, (TILE, xlen), 0) - (TILE - 1 - ROWS), 0).astype(jnp.float32)
    falling = (REACH - lax.broadcasted_iota(jnp.int32, (REACH, xlen), 0)).astype(jnp.float32)
    share[...] = share_in[...]
    share[ylen * zlen - TILE : ylen * zlen] += rising * line
    share[ylen * zlen + REACH * (zlen - 1) : ylen * zlen + REACH * zlen] += falling * line


def total_kernel(shape, share, other, h_out, z_out, y_out, d_out, e_out):
    _, _, zlen, ylen, xlen = shape
    first_core = on_first()
    inner, rows = zlen - 1, ylen * zlen
    reach = REACH * zlen

    def layers(first, count):
        mine, theirs = share[first + inner * count : first + zlen * count], other[first + inner * count : first + zlen * count]
        middle = share[first : first + inner * count] + other[first : first + inner * count]
        return jnp.where(first_core, theirs, mine), middle, jnp.where(first_core, mine, theirs)

    lowest, middle, highest = layers(0, ylen)
    h_out[0] = lowest
    for z in range(inner):
        h_out[z + 1] = middle[ylen * z : ylen * (z + 1)]
    h_out[zlen] = highest
    z_out[...] = h_out[pl.ds(jnp.where(first_core, 0, 1), zlen)]
    ups = jnp.concatenate(layers(rows, REACH), axis=0)
    downs = jnp.concatenate(layers(rows + reach, REACH), axis=0)
    y_out[: reach + REACH] = jnp.where(first_core, downs, ups)
    for out, used in ((y_out, reach + REACH), (d_out, reach), (e_out, reach)):
        out[used:] = jnp.zeros((out.shape[0] - used, xlen), jnp.float32)
    d_out[:reach] = jnp.where(first_core, downs[:reach], ups[REACH:])
    e_out[:reach] = jnp.where(first_core, ups[:reach], downs[REACH:])


def layers_kernel(h, d_in, e_in, y_in, z_in, out):
    zlen, ylen, xlen = out.shape
    reach = REACH * zlen
    first_core = on_first()
    z_index, z_last = lax.axis_index("sz"), lax.axis_size("sz") - 1
    y_index, y_last = lax.axis_index("sy"), lax.axis_size("sy") - 1
    z_side = jnp.where(first_core, z_index < z_last, z_index > 0)
    y_side = jnp.where(first_core, y_index < y_last, y_index > 0)
    y_other = jnp.where(first_core, y_index > 0, y_index < y_last)
    blank = jnp.zeros((TILE - REACH, xlen), jnp.float32)

    def at_start(rows):
        return jnp.concatenate([rows, blank], axis=0)

    def at_end(rows):
        return jnp.concatenate([blank, rows], axis=0)

    def ends(rows, keep, at_last):
        rows = jnp.where(keep, rows, 0.0)
        return at_start(jnp.where(at_last, 0.0, rows)), at_end(jnp.where(at_last, rows, 0.0))

    def with_ends(layer, *pairs):
        head, tail = layer[:TILE], layer[ylen - TILE :]
        for first, last in pairs:
            head, tail = head + first, tail + last
        return jnp.concatenate([head, layer[TILE : ylen - TILE], tail] if ylen > 2 * TILE else [head, tail], axis=0)

    own = []
    for k in range(zlen + 1):
        layer = jnp.where(first_core, h[k], 0.0)
        own.append(with_ends(layer, ends(y_in[REACH * k : REACH * (k + 1)], y_side, first_core)))
    come = []
    for k in range(zlen):
        part = slice(REACH * k, REACH * (k + 1))
        layer = jnp.where(z_side, z_in[k], 0.0)
        straight = ends(d_in[part], z_side & y_side, first_core)
        across = ends(e_in[part], z_side & y_other, jnp.logical_not(first_core))
        come.append(with_ends(layer, straight, across))
    below = [jnp.where(first_core, 0.0, layer) for layer in come[zlen - REACH :]]
    above = [jnp.where(first_core, layer, 0.0) for layer in come]
    layers = below[:-1] + [below[-1] + own[0]] + own[1:-1] + [own[-1] + above[0]] + above[1:]
    for z, layer in enumerate(spread_layers(layers)):
        out[z] = layer


def sum_kernel(part, other, out):
    out[...] = part[...] + other[...]


def call(kernel, outs, args, scratch=(), space=pltpu.VMEM):
    shapes = [jax.ShapeDtypeStruct(out, jnp.float32) if isinstance(out, tuple) else out for out in outs]
    return pl.pallas_call(
        kernel,
        out_shape=shapes,
        in_specs=[pl.BlockSpec(memory_space=space)] * len(args),
        out_specs=[pl.BlockSpec(memory_space=pltpu.VMEM)] * len(outs),
        scratch_shapes=list(scratch),
        compiler_params=pltpu.CompilerParams(vmem_limit_bytes=32 * 1024 * 1024),
    )(*args)


def ring_moved(value, axis):
    size = lax.axis_size(axis)
    return lax.ppermute(value, axis, [((k + 1) % size, k) for k in range(size)])


def chip_swapped(value):
    cores = lax.axis_size("load")
    return lax.ppermute(value, "load", [(core, cores - 1 - core) for core in range(cores)])


def opposed(value, z_step, y_step, y_shift=0):
    cores, rows, size = lax.axis_size("load"), lax.axis_size("sy"), lax.axis_size("sz")
    pairs = []
    for core in range(cores):
        sign = -1 if core else 1
        for y in range(rows):
            for z in range(size):
                to_y, to_z, side = y + sign * y_step, z + sign * z_step, core
                if not (0 <= to_y < rows and 0 <= to_z < size):
                    to_y, to_z, side = y, z, cores - 1 - core
                to_y = (to_y + y_shift) % rows
                pairs.append(((core * rows + y) * size + z, (side * rows + to_y) * size + to_z))
    return lax.ppermute(value, ("load", "sy", "sz"), pairs)


def body(displacements, density, solid, fixed):
    loads, comps, zlen, ylen, xlen = displacements.shape
    planes = loads * comps
    totals = (zlen * lax.axis_size("sz"), ylen * lax.axis_size("sy"))
    args = [
        pltpu.with_memory_space_constraint(arg, pltpu.HBM) for arg in (displacements, fixed, density, solid)
    ]

    d_send, z_send, y_send = call(
        lambda *refs: lead_kernel(totals, *refs),
        [(-(-planes // TILE) * TILE, xlen), (planes + 1, ylen, xlen), (planes * zlen, xlen)],
        args,
        scratch=[
            pltpu.VMEM((loads, comps, ylen, xlen), jnp.float32),
            pltpu.VMEM((ylen, xlen), jnp.int32),
            pltpu.VMEM((ylen, xlen), jnp.float32),
            pltpu.VMEM((ylen, xlen), jnp.int32),
            pltpu.VMEM((loads, comps, zlen, TILE, xlen), jnp.float32),
            pltpu.VMEM((zlen, TILE, xlen), jnp.int32),
            pltpu.SemaphoreType.DMA((6,)),
        ],
        space=pltpu.HBM,
    )
    d_in = opposed(d_send, -1, 0, y_shift=-1)
    z_in = opposed(z_send, -1, 0)
    y_in = ring_moved(y_send, "sy")
    nodes = lambda layers: pltpu.VMEM((planes, layers, ylen + TILE, xlen), jnp.float32)
    inner = call(
        lambda *refs: inner_kernel(totals, *refs),
        [
            (zlen, ylen, xlen),
            (2, planes * zlen, xlen),
            (2, REACH * (zlen - 1), xlen),
            (planes, ylen, xlen),
            (planes, ylen, xlen),
            (ylen, xlen),
            (TILE, xlen),
        ],
        (displacements, fixed, density, solid),
        scratch=[nodes(zlen), nodes(zlen), pltpu.VMEM((zlen - 1, ylen + 2 * TILE, xlen), jnp.float32)],
    )
    reach = REACH * zlen
    shape = displacements.shape
    share, corner = call(
        lambda *refs: outer_kernel(shape, *refs),
        [(ylen * zlen + 2 * reach, xlen), (4, -(-(planes + 1) // TILE) * TILE, xlen)],
        (z_in, y_in, *inner),
        scratch=[
            nodes(4),
            nodes(4),
            pltpu.VMEM((ylen + 2 * TILE, xlen), jnp.float32),
            pltpu.VMEM((ylen, xlen), jnp.float32),
        ],
    )
    (share,) = call(
        lambda *refs: corner_kernel(shape, *refs), [(ylen * zlen + 2 * reach, xlen)], (share, corner, y_in, d_in)
    )
    sent = (-(-(reach + REACH) // TILE) * TILE, xlen)
    h, z_send, y_send, d_send, e_send = call(
        lambda *refs: total_kernel(displacements.shape, *refs),
        [
            (zlen + 1, ylen, xlen),
            (zlen, ylen, xlen),
            sent,
            sent,
            sent,
        ],
        (share, chip_swapped(share)),
    )
    d_in = opposed(d_send, -1, -1)
    e_in = opposed(e_send, -1, 1)
    y_in = opposed(y_send, 0, -1)
    z_in = opposed(z_send, -1, 0)
    (part,) = call(layers_kernel, [(zlen, ylen, xlen)], (h, d_in, e_in, y_in, z_in))
    (out,) = call(sum_kernel, [(zlen, ylen, xlen)], (part, chip_swapped(part)))
    return out


def solution(mesh):
    return jax.shard_map(
        body,
        mesh=mesh,
        in_specs=(
            P("load", None, "sz", "sy", None),
            P("sz", "sy", None),
            P("sz", "sy", None),
            P("sz", "sy", None),
        ),
        out_specs=P("sz", "sy", None),
        check_vma=False,
    )
```

```python
import jax
import jax.numpy as jnp
import numpy as np
from jax import lax
from jax.experimental import pallas as pl
from jax.experimental.pallas import tpu as pltpu
from jax.sharding import PartitionSpec as P

OFFSETS = [(0, 0, 0), (1, 0, 0), (1, 1, 0), (0, 1, 0), (0, 0, 1), (1, 0, 1), (1, 1, 1), (0, 1, 1)]
REACH = 3
ROWS = REACH + 1
TILE = 8
LANES = 128


def element_matrix():
    corners = np.array(
        [
            [-1.0, -1.0, -1.0],
            [1.0, -1.0, -1.0],
            [1.0, 1.0, -1.0],
            [-1.0, 1.0, -1.0],
            [-1.0, -1.0, 1.0],
            [1.0, -1.0, 1.0],
            [1.0, 1.0, 1.0],
            [-1.0, 1.0, 1.0],
        ]
    )
    poisson = 0.3
    lame = poisson / ((1.0 + poisson) * (1.0 - 2.0 * poisson))
    shear = 1.0 / (2.0 * (1.0 + poisson))
    elastic = np.zeros((6, 6))
    elastic[:3, :3] = lame
    for k in range(3):
        elastic[k, k] += 2.0 * shear
        elastic[3 + k, 3 + k] = shear
    gauss = 1.0 / np.sqrt(3.0)
    stiffness = np.zeros((24, 24))
    for gi in range(2):
        for gj in range(2):
            for gk in range(2):
                point = np.array([(2 * gi - 1) * gauss, (2 * gj - 1) * gauss, (2 * gk - 1) * gauss])
                strain = np.zeros((6, 24))
                for node in range(8):
                    grads = np.zeros(3)
                    for k in range(3):
                        value = corners[node, k] / 8.0
                        for m in range(3):
                            if m != k:
                                value = value * (1.0 + point[m] * corners[node, m])
                        grads[k] = 2.0 * value
                    col = 3 * node
                    strain[0, col] = grads[0]
                    strain[1, col + 1] = grads[1]
                    strain[2, col + 2] = grads[2]
                    strain[3, col] = grads[1]
                    strain[3, col + 1] = grads[0]
                    strain[4, col + 1] = grads[2]
                    strain[4, col + 2] = grads[1]
                    strain[5, col] = grads[2]
                    strain[5, col + 2] = grads[0]
                stiffness += strain.T @ elastic @ strain / 8.0
    return stiffness


def mode_weights():
    modes = [(i, j, k) for k in (0, 1) for j in (0, 1) for i in (0, 1)]
    sums = np.zeros((24, 24))
    for m, mode in enumerate(modes):
        for n, corner in enumerate(OFFSETS):
            sign = np.prod([(1 if corner[d] else -1) if mode[d] else 1 for d in range(3)])
            for comp in range(3):
                sums[3 * m + comp, 3 * n + comp] = sign
    form = sums @ element_matrix() @ sums.T / 64.0

    def at(first, second):
        return form[3 * modes.index(first[1]) + first[0], 3 * modes.index(second[1]) + second[0]]

    ux, vy, uy = (0, (1, 0, 0)), (1, (0, 1, 0)), (0, (0, 1, 0))
    uxy, wyz = (0, (1, 1, 0)), (2, (0, 1, 1))
    wxy, vxz, uxyz = (2, (1, 1, 0)), (1, (1, 0, 1)), (0, (1, 1, 1))
    return dict(
        normal=at(ux, ux) - at(ux, vy),
        trace=at(ux, vy),
        shear=at(uy, uy),
        plus=(at(uxy, uxy) + at(uxy, wyz)) / 2,
        minus=(at(uxy, uxy) - at(uxy, wyz)) / 2,
        twist=at(wxy, wxy) - at(wxy, vxz),
        twist_sum=at(wxy, vxz),
        corner=at(uxyz, uxyz),
    )


def square(value):
    return value * value


def quadratic(low, high, weights):
    x = [low[c][1] + high[c][1] for c in range(3)]
    y = [low[c][2] + high[c][2] for c in range(3)]
    z = [high[c][0] - low[c][0] for c in range(3)]
    xy = [low[c][3] + high[c][3] for c in range(3)]
    xz = [high[c][1] - low[c][1] for c in range(3)]
    yz = [high[c][2] - low[c][2] for c in range(3)]
    xyz = [high[c][3] - low[c][3] for c in range(3)]
    normal = square(x[0]) + square(y[1]) + square(z[2])
    trace = square(x[0] + y[1] + z[2])
    shear = square(y[0] + x[1]) + square(z[0] + x[2]) + square(z[1] + y[2])
    pairs = ((xy[0], yz[2]), (xy[1], xz[2]), (xz[0], yz[1]))
    plus = sum(square(p + q) for p, q in pairs)
    minus = sum(square(p - q) for p, q in pairs)
    twist = square(xy[2]) + square(xz[1]) + square(yz[0])
    twist_sum = square(xy[2] + xz[1] + yz[0])
    corner = square(xyz[0]) + square(xyz[1]) + square(xyz[2])
    groups = dict(
        normal=normal, trace=trace, shear=shear, plus=plus, minus=minus, twist=twist, twist_sum=twist_sum, corner=corner
    )
    return sum(np.float32(weights[name]) * group for name, group in groups.items())


def line_weight(coord, count):
    def outside(distance):
        missing = jnp.maximum(REACH - distance, 0)
        return missing * (missing + 1) // 2

    whole = (REACH + 1) * (REACH + 1)
    return (whole - outside(coord) - outside(count - 1 - coord)).astype(jnp.float32)


def voxel_factor(density, solid, plane, first_row, total_z, total_y):
    rows, length = density.shape
    row = lax.broadcasted_iota(jnp.int32, (rows, length), 0) + first_row
    column = lax.broadcasted_iota(jnp.int32, (rows, length), 1)
    weight = line_weight(row, total_y) * line_weight(column, length)
    weight = weight * line_weight(jnp.full((rows, length), plane, jnp.int32), total_z)
    return solid.astype(jnp.float32) * (-3.0 * density * density) / weight


def spread_x(value):
    rows, length = value.shape
    wide = jnp.concatenate([value, jnp.zeros((rows, LANES), jnp.float32)], axis=1)
    span = length + LANES
    total = float(ROWS) * value
    for step in range(1, ROWS):
        both = pltpu.roll(wide, span - step, 1) + pltpu.roll(wide, step, 1)
        total = total + float(ROWS - step) * both[:, :length]
    return total


def spread_layers(layers):
    for step in (1, 2, 1, 2):
        layers = [layers[k] + layers[k + step] for k in range(len(layers) - step)]
    return layers


def held(disp, fixed, case, comp, z, rows):
    return disp[case, comp, z, rows] * (1.0 - fixed[z, rows].astype(jnp.float32))


def split_x(value):
    length = value.shape[1]
    column = lax.broadcasted_iota(jnp.int32, value.shape, 1)
    ahead = jnp.where(column == length - 1, 0.0, pltpu.roll(value, length - 1, 1))
    return value + ahead, ahead - value


def spread_y(quotient, ylen):
    rows = [quotient[TILE + step : TILE + step + ylen] for step in range(-REACH, REACH + 1)]
    return sum((ROWS - abs(k - REACH)) * rows[k] for k in range(2 * REACH + 1))


def to_neighbours(quotient, ylen):
    top = quotient[ylen : ylen + TILE]
    base = quotient[TILE : 2 * TILE]
    ahead, back = [], []
    for row in range(REACH):
        ahead.append(sum(float(REACH - row - k) * top[TILE - 1 - k : TILE - k] for k in range(REACH - row)))
        back.append(sum(float(row + 1 - k) * base[k : k + 1] for k in range(row + 1)))
    return ahead, back


def on_first():
    return lax.axis_index("load") == 0


def lead_kernel(totals, disp_hbm, fixed_hbm, density_hbm, solid_hbm, d_out, z_out, y_out, layer, layer_fixed, density, solid, rows, rows_fixed, sems):
    loads, comps, zlen, ylen, _ = disp_hbm.shape
    gives = jnp.where(on_first(), 0, zlen - 1)
    copies = [
        pltpu.make_async_copy(source, target, sems.at[k])
        for k, (source, target) in enumerate(
            (
                (density_hbm.at[gives], density),
                (solid_hbm.at[gives], solid),
                (fixed_hbm.at[gives], layer_fixed),
                (disp_hbm.at[:, :, gives], layer),
                (fixed_hbm.at[:, :TILE], rows_fixed),
                (disp_hbm.at[:, :, :, :TILE], rows),
            )
        )
    ]
    for copy in copies:
        copy.start()
    for copy in copies[:2]:
        copy.wait()
    plane = lax.axis_index("sz") * zlen + gives
    base_y = lax.axis_index("sy") * ylen
    d_out[...] = jnp.zeros(d_out.shape, jnp.float32)
    z_out[loads * comps] = voxel_factor(density[...], solid[...], plane, base_y, *totals)
    for copy in copies[2:4]:
        copy.wait()
    free = 1.0 - layer_fixed[...].astype(jnp.float32)
    for case in range(loads):
        for comp in range(comps):
            k = case * comps + comp
            z_out[k] = layer[case, comp] * free
            d_out[k : k + 1] = z_out[k, :1]
    for copy in copies[4:]:
        copy.wait()
    for z in range(zlen):
        free = 1.0 - rows_fixed[z, :1].astype(jnp.float32)
        for case in range(loads):
            for comp in range(comps):
                at = (comp * loads + case) * zlen + z
                y_out[at : at + 1] = rows[case, comp, z, :1] * free


def tile_energies(plus, diff, first, lanes, layers, loads, comps, base=0):
    weights = mode_weights()

    def faces(k, z):
        near, far = slice(first, first + TILE), slice(first + 1, first + TILE + 1)
        whole, whole_next = plus[k, z, near, lanes], plus[k, z, far, lanes]
        change, change_next = diff[k, z, near, lanes], diff[k, z, far, lanes]
        return whole + whole_next, change + change_next, whole_next - whole, change_next - change

    energy = [None] * layers
    for case in range(loads):
        low = None
        for z in range(layers + 1):
            high = [faces(case * comps + comp, base + z) for comp in range(comps)]
            if low is not None:
                part = quadratic(low, high, weights)
                energy[z - 1] = part if energy[z - 1] is None else energy[z - 1] + part
            low = high
    return energy


def blank_last(value, first, ylen):
    row = lax.broadcasted_iota(jnp.int32, value.shape, 0) + first
    return jnp.where(row == ylen - 1, 0.0, value)


def inner_kernel(totals, disp, fixed, density, solid, own, line, sends, last_plus, last_diff, last_factor, edge, plus, diff, quotient):
    loads, comps, zlen, ylen, xlen = disp.shape
    total_z, total_y = totals
    base_z = lax.axis_index("sz") * zlen
    base_y = lax.axis_index("sy") * ylen
    inner = zlen - 1
    keeps = jnp.where(on_first(), inner, 0)

    @pl.loop(0, loads * comps, unroll=True)
    def _(k):
        case, comp = k // comps, k % comps
        for z in range(zlen):
            whole, change = split_x(held(disp, fixed, case, comp, z, slice(None)))
            plus[k, z, :ylen] = whole
            diff[k, z, :ylen] = change
        last_plus[k] = plus[k, keeps, :ylen]
        last_diff[k] = diff[k, keeps, :ylen]

    for comp in range(comps):
        for case in range(loads):
            for z in range(zlen):
                at = (comp * loads + case) * zlen + z
                line[0, at : at + 1] = plus[case * comps + comp, z, ylen - 1 : ylen]
                line[1, at : at + 1] = diff[case * comps + comp, z, ylen - 1 : ylen]

    zeros = jnp.zeros((TILE, xlen), jnp.float32)
    edge[...] = jnp.zeros(edge.shape, jnp.float32)
    for z in range(zlen):
        factor = voxel_factor(density[z], solid[z], base_z + z, base_y, total_z, total_y)
        edge[z : z + 1] = factor[ylen - 1 :]
        if z == inner:
            last_factor[...] = factor
        else:
            quotient[z, :TILE] = zeros
            quotient[z, TILE : TILE + ylen] = factor
            quotient[z, TILE + ylen :] = zeros

    for first in range(0, ylen, TILE):

        @pl.loop(0, xlen // LANES, unroll=True)
        def _(chunk):
            lanes = pl.ds(pl.multiple_of(chunk * LANES, LANES), LANES)
            energy = tile_energies(plus, diff, first, lanes, inner, loads, comps)
            for z in range(inner):
                here = quotient[z, first + TILE : first + 2 * TILE, lanes]
                quotient[z, first + TILE : first + 2 * TILE, lanes] = blank_last(energy[z] * here, first, ylen)

    for z in range(inner):
        own[z] = spread_x(spread_y(quotient.at[z], ylen))
        ahead, back = to_neighbours(quotient.at[z], ylen)
        ends = spread_x(jnp.concatenate(ahead + back + [zeros[:2]], axis=0))
        sends[0, REACH * z : REACH * (z + 1)] = ends[:REACH]
        sends[1, REACH * z : REACH * (z + 1)] = ends[REACH : 2 * REACH]


def outer_kernel(
    shape, z_in, y_in, own_in, line, sends, last_plus, last_diff, last_factor, edge, share, corner, plus, diff, quotient, factor
):
    loads, comps, zlen, ylen, xlen = shape
    planes = loads * comps
    inner = zlen - 1
    first_core, index = on_first(), lax.axis_index("sz")
    top = first_core & (index == lax.axis_size("sz") - 1)
    more = lax.axis_index("sy") < lax.axis_size("sy") - 1
    stays, comes = jnp.where(first_core, 0, 1), jnp.where(first_core, jnp.where(top, 2, 1), 0)
    y_plus, y_diff = split_x(jnp.where(more, y_in[...], 0.0))
    for k in range(planes):
        plus[k, stays, :ylen] = last_plus[k]
        diff[k, stays, :ylen] = last_diff[k]
        whole, change = split_x(z_in[k])
        plus[k, comes, :ylen] = whole
        diff[k, comes, :ylen] = change
        for group, value in enumerate((last_plus[k, ylen - 1 :], last_diff[k, ylen - 1 :], whole[ylen - 1 :], change[ylen - 1 :])):
            corner[group, k : k + 1] = value
    below = jnp.where(index > 0, z_in[planes], 0.0)
    factor[...] = jnp.where(first_core, last_factor[...], below)
    corner[0, planes : planes + 1] = factor[ylen - 1 :]

    @pl.when(top)
    def _():
        clamped = jnp.zeros((ylen + TILE, xlen), jnp.float32)
        for k in range(planes):
            for slot in (1, 3):
                plus[k, slot] = clamped
                diff[k, slot] = clamped

    zeros = jnp.zeros((TILE, xlen), jnp.float32)
    quotient[:TILE] = zeros
    quotient[TILE + ylen :] = zeros
    for first in range(0, ylen, TILE):

        @pl.loop(0, xlen // LANES, unroll=True)
        def _(chunk):
            lanes = pl.ds(pl.multiple_of(chunk * LANES, LANES), LANES)
            (energy,) = tile_energies(plus, diff, first, lanes, 1, loads, comps)
            here = energy * factor[first : first + TILE, lanes]
            quotient[first + TILE : first + 2 * TILE, lanes] = blank_last(here, first, ylen)

    @pl.when(top)
    def _():
        for first in range(0, ylen, TILE):

            @pl.loop(0, xlen // LANES, unroll=True)
            def _(chunk):
                lanes = pl.ds(pl.multiple_of(chunk * LANES, LANES), LANES)
                (energy,) = tile_energies(plus, diff, first, lanes, 1, loads, comps, base=2)
                here = energy * factor[first : first + TILE, lanes]
                quotient[first + TILE : first + 2 * TILE, lanes] += blank_last(here, first, ylen)

    count = loads * zlen
    low, high = [], []
    for comp in range(comps):
        part = slice(comp * count, (comp + 1) * count)
        whole, change = line[0, part], line[1, part]
        whole_next, change_next = y_plus[part], y_diff[part]
        face = (whole + whole_next, change + change_next, whole_next - whole, change_next - change)
        low.append(face)
        high.append([pltpu.roll(value, count - 1, 0) for value in face])
    energy = quadratic(low, high, mode_weights())
    energy = sum(energy[case * zlen : case * zlen + inner] for case in range(loads)) * edge[:inner]
    last = spread_x(jnp.concatenate([energy, jnp.zeros((TILE - inner, xlen), jnp.float32)], axis=0))

    row = lax.broadcasted_iota(jnp.int32, (TILE, xlen), 0)
    rising = jnp.maximum(row - (TILE - 1 - ROWS), 0).astype(jnp.float32)
    ups, downs = [], []
    for z in range(inner):
        share[ylen * z : ylen * (z + 1)] = own_in[z]
        share[ylen * (z + 1) - TILE : ylen * (z + 1)] += rising * last[z : z + 1]
        here = sends[0, REACH * z : REACH * (z + 1)]
        ups += [here[r : r + 1] + float(REACH - r) * last[z : z + 1] for r in range(REACH)]
        downs.append(sends[1, REACH * z : REACH * (z + 1)])
    share[ylen * inner : ylen * zlen] = spread_x(spread_y(quotient, ylen))
    ahead, back = to_neighbours(quotient, ylen)
    ends = spread_x(jnp.concatenate(ahead + back + [zeros[:2]], axis=0))
    share[ylen * zlen :] = jnp.concatenate(ups + [ends[:REACH]] + downs + [ends[REACH : 2 * REACH]], axis=0)


def corner_line(shape, corner, y_in, d_in):
    loads, comps, zlen, ylen, xlen = shape
    planes = loads * comps
    first_core = on_first()
    top = first_core & (lax.axis_index("sz") == lax.axis_size("sz") - 1)
    more = lax.axis_index("sy") < lax.axis_size("sy") - 1
    rows = []
    for k in range(planes):
        at = (k % comps * loads + k // comps) * zlen
        rows.append(jnp.where(first_core, y_in[at + zlen - 1 : at + zlen], y_in[at : at + 1]))
    rows.append(jnp.zeros((-planes % TILE, xlen), jnp.float32))
    stays_next = split_x(jnp.where(more, jnp.concatenate(rows, axis=0), 0.0))
    comes_next = split_x(jnp.where(more, d_in[: -(-planes // TILE) * TILE], 0.0))

    def faces(stays, comes, comp):
        zero = jnp.zeros((1, xlen), jnp.float32)
        under, over = [], []
        for own, other in zip(stays, comes):
            own, other = ([value[case * comps + comp : case * comps + comp + 1] for case in range(loads)] for value in (own, other))
            low = [jnp.where(first_core, a, b) for a, b in zip(own, other)] + [jnp.where(top, b, 0.0) for b in other]
            high = [jnp.where(first_core, jnp.where(top, 0.0, b), a) for a, b in zip(own, other)] + [zero] * loads
            under.append(jnp.concatenate(low, axis=0))
            over.append(jnp.concatenate(high, axis=0))
        return under, over

    low, high = [], []
    for comp in range(comps):
        near = faces((corner[0], corner[1]), (corner[2], corner[3]), comp)
        far = faces(stays_next, comes_next, comp)
        for (whole, change), (whole_next, change_next), into in zip(near, far, (low, high)):
            into.append((whole + whole_next, change + change_next, whole_next - whole, change_next - change))
    energy = quadratic(low, high, mode_weights())
    line = sum(energy[case : case + 1] for case in range(2 * loads)) * corner[0, planes : planes + 1]
    return spread_x(jnp.concatenate([line, jnp.zeros((TILE - 1, xlen), jnp.float32)], axis=0))[:1]


def corner_kernel(shape, share_in, corner, y_in, d_in, share):
    _, _, zlen, ylen, xlen = shape
    line = corner_line(shape, corner, y_in, d_in)
    rising = jnp.maximum(lax.broadcasted_iota(jnp.int32, (TILE, xlen), 0) - (TILE - 1 - ROWS), 0).astype(jnp.float32)
    falling = (REACH - lax.broadcasted_iota(jnp.int32, (REACH, xlen), 0)).astype(jnp.float32)
    share[...] = share_in[...]
    share[ylen * zlen - TILE : ylen * zlen] += rising * line
    share[ylen * zlen + REACH * (zlen - 1) : ylen * zlen + REACH * zlen] += falling * line


def total_kernel(shape, share, other, h_out, z_out, y_out, d_out, e_out):
    _, _, zlen, ylen, xlen = shape
    first_core = on_first()
    inner, rows = zlen - 1, ylen * zlen
    reach = REACH * zlen

    def layers(first, count):
        mine, theirs = share[first + inner * count : first + zlen * count], other[first + inner * count : first + zlen * count]
        middle = share[first : first + inner * count] + other[first : first + inner * count]
        return jnp.where(first_core, theirs, mine), middle, jnp.where(first_core, mine, theirs)

    lowest, middle, highest = layers(0, ylen)
    h_out[0] = lowest
    for z in range(inner):
        h_out[z + 1] = middle[ylen * z : ylen * (z + 1)]
    h_out[zlen] = highest
    z_out[...] = h_out[pl.ds(jnp.where(first_core, 0, 1), zlen)]
    ups = jnp.concatenate(layers(rows, REACH), axis=0)
    downs = jnp.concatenate(layers(rows + reach, REACH), axis=0)
    y_out[: reach + REACH] = jnp.where(first_core, downs, ups)
    for out, used in ((y_out, reach + REACH), (d_out, reach), (e_out, reach)):
        out[used:] = jnp.zeros((out.shape[0] - used, xlen), jnp.float32)
    d_out[:reach] = jnp.where(first_core, downs[:reach], ups[REACH:])
    e_out[:reach] = jnp.where(first_core, ups[:reach], downs[REACH:])


def layers_kernel(h, d_in, e_in, y_in, z_in, out):
    zlen, ylen, xlen = out.shape
    reach = REACH * zlen
    first_core = on_first()
    z_index, z_last = lax.axis_index("sz"), lax.axis_size("sz") - 1
    y_index, y_last = lax.axis_index("sy"), lax.axis_size("sy") - 1
    z_side = jnp.where(first_core, z_index < z_last, z_index > 0)
    y_side = jnp.where(first_core, y_index < y_last, y_index > 0)
    y_other = jnp.where(first_core, y_index > 0, y_index < y_last)
    blank = jnp.zeros((TILE - REACH, xlen), jnp.float32)

    def at_start(rows):
        return jnp.concatenate([rows, blank], axis=0)

    def at_end(rows):
        return jnp.concatenate([blank, rows], axis=0)

    def ends(rows, keep, at_last):
        rows = jnp.where(keep, rows, 0.0)
        return at_start(jnp.where(at_last, 0.0, rows)), at_end(jnp.where(at_last, rows, 0.0))

    def with_ends(layer, *pairs):
        head, tail = layer[:TILE], layer[ylen - TILE :]
        for first, last in pairs:
            head, tail = head + first, tail + last
        return jnp.concatenate([head, layer[TILE : ylen - TILE], tail] if ylen > 2 * TILE else [head, tail], axis=0)

    own = []
    for k in range(zlen + 1):
        layer = jnp.where(first_core, h[k], 0.0)
        own.append(with_ends(layer, ends(y_in[REACH * k : REACH * (k + 1)], y_side, first_core)))
    come = []
    for k in range(zlen):
        part = slice(REACH * k, REACH * (k + 1))
        layer = jnp.where(z_side, z_in[k], 0.0)
        straight = ends(d_in[part], z_side & y_side, first_core)
        across = ends(e_in[part], z_side & y_other, jnp.logical_not(first_core))
        come.append(with_ends(layer, straight, across))
    below = [jnp.where(first_core, 0.0, layer) for layer in come[zlen - REACH :]]
    above = [jnp.where(first_core, layer, 0.0) for layer in come]
    layers = below[:-1] + [below[-1] + own[0]] + own[1:-1] + [own[-1] + above[0]] + above[1:]
    for z, layer in enumerate(spread_layers(layers)):
        out[z] = layer


def sum_kernel(part, other, out):
    out[...] = part[...] + other[...]


def call(kernel, outs, args, scratch=(), space=pltpu.VMEM):
    shapes = [jax.ShapeDtypeStruct(out, jnp.float32) if isinstance(out, tuple) else out for out in outs]
    return pl.pallas_call(
        kernel,
        out_shape=shapes,
        in_specs=[pl.BlockSpec(memory_space=space)] * len(args),
        out_specs=[pl.BlockSpec(memory_space=pltpu.VMEM)] * len(outs),
        scratch_shapes=list(scratch),
        compiler_params=pltpu.CompilerParams(vmem_limit_bytes=32 * 1024 * 1024),
    )(*args)


def ring_moved(value, axis):
    size = lax.axis_size(axis)
    return lax.ppermute(value, axis, [((k + 1) % size, k) for k in range(size)])


def chip_swapped(value):
    cores = lax.axis_size("load")
    return lax.ppermute(value, "load", [(core, cores - 1 - core) for core in range(cores)])


def opposed(value, z_step, y_step, y_shift=0):
    cores, rows, size = lax.axis_size("load"), lax.axis_size("sy"), lax.axis_size("sz")
    pairs = []
    for core in range(cores):
        sign = -1 if core else 1
        for y in range(rows):
            for z in range(size):
                to_y, to_z, side = y + sign * y_step, z + sign * z_step, core
                if not (0 <= to_y < rows and 0 <= to_z < size):
                    to_y, to_z, side = y, z, cores - 1 - core
                to_y = (to_y + y_shift) % rows
                pairs.append(((core * rows + y) * size + z, (side * rows + to_y) * size + to_z))
    return lax.ppermute(value, ("load", "sy", "sz"), pairs)


def body(displacements, density, solid, fixed):
    loads, comps, zlen, ylen, xlen = displacements.shape
    planes = loads * comps
    totals = (zlen * lax.axis_size("sz"), ylen * lax.axis_size("sy"))
    args = [
        pltpu.with_memory_space_constraint(arg, pltpu.HBM) for arg in (displacements, fixed, density, solid)
    ]

    d_send, z_send, y_send = call(
        lambda *refs: lead_kernel(totals, *refs),
        [(planes * zlen + TILE, xlen), (planes + 1, ylen, xlen), (planes * zlen, xlen)],
        args,
        scratch=[
            pltpu.VMEM((loads, comps, ylen, xlen), jnp.float32),
            pltpu.VMEM((ylen, xlen), jnp.int32),
            pltpu.VMEM((ylen, xlen), jnp.float32),
            pltpu.VMEM((ylen, xlen), jnp.int32),
            pltpu.VMEM((loads, comps, zlen, TILE, xlen), jnp.float32),
            pltpu.VMEM((zlen, TILE, xlen), jnp.int32),
            pltpu.SemaphoreType.DMA((6,)),
        ],
        space=pltpu.HBM,
    )
    d_in = opposed(d_send, -1, 0, y_shift=-1)
    z_in = opposed(z_send, -1, 0)
    y_in = ring_moved(y_send, "sy")
    nodes = lambda layers: pltpu.VMEM((planes, layers, ylen + TILE, xlen), jnp.float32)
    inner = call(
        lambda *refs: inner_kernel(totals, *refs),
        [
            (zlen, ylen, xlen),
            (2, planes * zlen, xlen),
            (2, REACH * (zlen - 1), xlen),
            (planes, ylen, xlen),
            (planes, ylen, xlen),
            (ylen, xlen),
            (TILE, xlen),
        ],
        (displacements, fixed, density, solid),
        scratch=[nodes(zlen), nodes(zlen), pltpu.VMEM((zlen - 1, ylen + 2 * TILE, xlen), jnp.float32)],
    )
    reach = REACH * zlen
    shape = displacements.shape
    share, corner = call(
        lambda *refs: outer_kernel(shape, *refs),
        [(ylen * zlen + 2 * reach, xlen), (4, -(-(planes + 1) // TILE) * TILE, xlen)],
        (z_in, y_in, *inner),
        scratch=[
            nodes(4),
            nodes(4),
            pltpu.VMEM((ylen + 2 * TILE, xlen), jnp.float32),
            pltpu.VMEM((ylen, xlen), jnp.float32),
        ],
    )
    (share,) = call(
        lambda *refs: corner_kernel(shape, *refs), [(ylen * zlen + 2 * reach, xlen)], (share, corner, y_in, d_in)
    )
    sent = (-(-(reach + REACH) // TILE) * TILE, xlen)
    h, z_send, y_send, d_send, e_send = call(
        lambda *refs: total_kernel(displacements.shape, *refs),
        [
            (zlen + 1, ylen, xlen),
            (zlen, ylen, xlen),
            sent,
            sent,
            sent,
        ],
        (share, chip_swapped(share)),
    )
    d_in = opposed(d_send, -1, -1)
    e_in = opposed(e_send, -1, 1)
    y_in = opposed(y_send, 0, -1)
    z_in = opposed(z_send, -1, 0)
    (part,) = call(layers_kernel, [(zlen, ylen, xlen)], (h, d_in, e_in, y_in, z_in))
    (out,) = call(sum_kernel, [(zlen, ylen, xlen)], (part, chip_swapped(part)))
    return out


def solution(mesh):
    return jax.shard_map(
        body,
        mesh=mesh,
        in_specs=(
            P("load", None, "sz", "sy", None),
            P("sz", "sy", None),
            P("sz", "sy", None),
            P("sz", "sy", None),
        ),
        out_specs=P("sz", "sy", None),
        check_vma=False,
    )
```

```python
import jax
import jax.numpy as jnp
import numpy as np
from jax import lax
from jax.experimental import pallas as pl
from jax.experimental.pallas import tpu as pltpu
from jax.sharding import PartitionSpec as P

OFFSETS = [(0, 0, 0), (1, 0, 0), (1, 1, 0), (0, 1, 0), (0, 0, 1), (1, 0, 1), (1, 1, 1), (0, 1, 1)]
REACH = 3
ROWS = REACH + 1
TILE = 8
LANES = 128


def element_matrix():
    corners = np.array(
        [
            [-1.0, -1.0, -1.0],
            [1.0, -1.0, -1.0],
            [1.0, 1.0, -1.0],
            [-1.0, 1.0, -1.0],
            [-1.0, -1.0, 1.0],
            [1.0, -1.0, 1.0],
            [1.0, 1.0, 1.0],
            [-1.0, 1.0, 1.0],
        ]
    )
    poisson = 0.3
    lame = poisson / ((1.0 + poisson) * (1.0 - 2.0 * poisson))
    shear = 1.0 / (2.0 * (1.0 + poisson))
    elastic = np.zeros((6, 6))
    elastic[:3, :3] = lame
    for k in range(3):
        elastic[k, k] += 2.0 * shear
        elastic[3 + k, 3 + k] = shear
    gauss = 1.0 / np.sqrt(3.0)
    stiffness = np.zeros((24, 24))
    for gi in range(2):
        for gj in range(2):
            for gk in range(2):
                point = np.array([(2 * gi - 1) * gauss, (2 * gj - 1) * gauss, (2 * gk - 1) * gauss])
                strain = np.zeros((6, 24))
                for node in range(8):
                    grads = np.zeros(3)
                    for k in range(3):
                        value = corners[node, k] / 8.0
                        for m in range(3):
                            if m != k:
                                value = value * (1.0 + point[m] * corners[node, m])
                        grads[k] = 2.0 * value
                    col = 3 * node
                    strain[0, col] = grads[0]
                    strain[1, col + 1] = grads[1]
                    strain[2, col + 2] = grads[2]
                    strain[3, col] = grads[1]
                    strain[3, col + 1] = grads[0]
                    strain[4, col + 1] = grads[2]
                    strain[4, col + 2] = grads[1]
                    strain[5, col] = grads[2]
                    strain[5, col + 2] = grads[0]
                stiffness += strain.T @ elastic @ strain / 8.0
    return stiffness


def mode_weights():
    modes = [(i, j, k) for k in (0, 1) for j in (0, 1) for i in (0, 1)]
    sums = np.zeros((24, 24))
    for m, mode in enumerate(modes):
        for n, corner in enumerate(OFFSETS):
            sign = np.prod([(1 if corner[d] else -1) if mode[d] else 1 for d in range(3)])
            for comp in range(3):
                sums[3 * m + comp, 3 * n + comp] = sign
    form = sums @ element_matrix() @ sums.T / 64.0

    def at(first, second):
        return form[3 * modes.index(first[1]) + first[0], 3 * modes.index(second[1]) + second[0]]

    ux, vy, uy = (0, (1, 0, 0)), (1, (0, 1, 0)), (0, (0, 1, 0))
    uxy, wyz = (0, (1, 1, 0)), (2, (0, 1, 1))
    wxy, vxz, uxyz = (2, (1, 1, 0)), (1, (1, 0, 1)), (0, (1, 1, 1))
    return dict(
        normal=at(ux, ux) - at(ux, vy),
        trace=at(ux, vy),
        shear=at(uy, uy),
        plus=(at(uxy, uxy) + at(uxy, wyz)) / 2,
        minus=(at(uxy, uxy) - at(uxy, wyz)) / 2,
        twist=at(wxy, wxy) - at(wxy, vxz),
        twist_sum=at(wxy, vxz),
        corner=at(uxyz, uxyz),
    )


def square(value):
    return value * value


def quadratic(low, high, weights):
    x = [low[c][1] + high[c][1] for c in range(3)]
    y = [low[c][2] + high[c][2] for c in range(3)]
    z = [high[c][0] - low[c][0] for c in range(3)]
    xy = [low[c][3] + high[c][3] for c in range(3)]
    xz = [high[c][1] - low[c][1] for c in range(3)]
    yz = [high[c][2] - low[c][2] for c in range(3)]
    xyz = [high[c][3] - low[c][3] for c in range(3)]
    normal = square(x[0]) + square(y[1]) + square(z[2])
    trace = square(x[0] + y[1] + z[2])
    shear = square(y[0] + x[1]) + square(z[0] + x[2]) + square(z[1] + y[2])
    pairs = ((xy[0], yz[2]), (xy[1], xz[2]), (xz[0], yz[1]))
    plus = sum(square(p + q) for p, q in pairs)
    minus = sum(square(p - q) for p, q in pairs)
    twist = square(xy[2]) + square(xz[1]) + square(yz[0])
    twist_sum = square(xy[2] + xz[1] + yz[0])
    corner = square(xyz[0]) + square(xyz[1]) + square(xyz[2])
    groups = dict(
        normal=normal, trace=trace, shear=shear, plus=plus, minus=minus, twist=twist, twist_sum=twist_sum, corner=corner
    )
    return sum(np.float32(weights[name]) * group for name, group in groups.items())


def line_weight(coord, count):
    def outside(distance):
        missing = jnp.maximum(REACH - distance, 0)
        return missing * (missing + 1) // 2

    whole = (REACH + 1) * (REACH + 1)
    return (whole - outside(coord) - outside(count - 1 - coord)).astype(jnp.float32)


def voxel_factor(density, solid, plane, first_row, total_z, total_y):
    rows, length = density.shape
    row = lax.broadcasted_iota(jnp.int32, (rows, length), 0) + first_row
    column = lax.broadcasted_iota(jnp.int32, (rows, length), 1)
    weight = line_weight(row, total_y) * line_weight(column, length)
    weight = weight * line_weight(jnp.full((rows, length), plane, jnp.int32), total_z)
    return solid.astype(jnp.float32) * (-3.0 * density * density) / weight


def spread_x(value):
    rows, length = value.shape
    wide = jnp.concatenate([value, jnp.zeros((rows, LANES), jnp.float32)], axis=1)
    span = length + LANES
    total = float(ROWS) * value
    for step in range(1, ROWS):
        both = pltpu.roll(wide, span - step, 1) + pltpu.roll(wide, step, 1)
        total = total + float(ROWS - step) * both[:, :length]
    return total


def spread_layers(layers):
    for step in (1, 2, 1, 2):
        layers = [layers[k] + layers[k + step] for k in range(len(layers) - step)]
    return layers


def held(disp, fixed, case, comp, z, rows):
    return disp[case, comp, z, rows] * (1.0 - fixed[z, rows].astype(jnp.float32))


def split_x(value):
    length = value.shape[1]
    column = lax.broadcasted_iota(jnp.int32, value.shape, 1)
    ahead = jnp.where(column == length - 1, 0.0, pltpu.roll(value, length - 1, 1))
    return value + ahead, ahead - value


def spread_y(quotient, ylen):
    rows = [quotient[TILE + step : TILE + step + ylen] for step in range(-REACH, REACH + 1)]
    return sum((ROWS - abs(k - REACH)) * rows[k] for k in range(2 * REACH + 1))


def to_neighbours(quotient, ylen):
    top = quotient[ylen : ylen + TILE]
    base = quotient[TILE : 2 * TILE]
    ahead, back = [], []
    for row in range(REACH):
        ahead.append(sum(float(REACH - row - k) * top[TILE - 1 - k : TILE - k] for k in range(REACH - row)))
        back.append(sum(float(row + 1 - k) * base[k : k + 1] for k in range(row + 1)))
    return ahead, back


def upward(axis):
    return (lax.axis_index(axis) + lax.axis_index("load")) % 2 == 0


def on_first():
    return lax.axis_index("load") == 0


def lead_kernel(totals, disp_hbm, fixed_hbm, density_hbm, solid_hbm, d_out, z_out, y_out, layer, layer_fixed, density, solid, rows, rows_fixed, sems):
    loads, comps, zlen, ylen, _ = disp_hbm.shape
    gives = jnp.where(on_first(), 0, zlen - 1)
    copies = [
        pltpu.make_async_copy(source, target, sems.at[k])
        for k, (source, target) in enumerate(
            (
                (density_hbm.at[gives], density),
                (solid_hbm.at[gives], solid),
                (fixed_hbm.at[gives], layer_fixed),
                (disp_hbm.at[:, :, gives], layer),
                (fixed_hbm.at[:, :TILE], rows_fixed),
                (disp_hbm.at[:, :, :, :TILE], rows),
            )
        )
    ]
    for copy in copies:
        copy.start()
    for copy in copies[:2]:
        copy.wait()
    plane = lax.axis_index("sz") * zlen + gives
    base_y = lax.axis_index("sy") * ylen
    d_out[...] = jnp.zeros(d_out.shape, jnp.float32)
    z_out[loads * comps] = voxel_factor(density[...], solid[...], plane, base_y, *totals)
    for copy in copies[2:4]:
        copy.wait()
    free = 1.0 - layer_fixed[...].astype(jnp.float32)
    for case in range(loads):
        for comp in range(comps):
            k = case * comps + comp
            z_out[k] = layer[case, comp] * free
            d_out[k : k + 1] = z_out[k, :1]
    for copy in copies[4:]:
        copy.wait()
    for z in range(zlen):
        free = 1.0 - rows_fixed[z, :1].astype(jnp.float32)
        for case in range(loads):
            for comp in range(comps):
                at = (comp * loads + case) * zlen + z
                y_out[at : at + 1] = rows[case, comp, z, :1] * free


def tile_energies(plus, diff, first, lanes, layers, loads, comps, base=0):
    weights = mode_weights()

    def faces(k, z):
        near, far = slice(first, first + TILE), slice(first + 1, first + TILE + 1)
        whole, whole_next = plus[k, z, near, lanes], plus[k, z, far, lanes]
        change, change_next = diff[k, z, near, lanes], diff[k, z, far, lanes]
        return whole + whole_next, change + change_next, whole_next - whole, change_next - change

    energy = [None] * layers
    for case in range(loads):
        low = None
        for z in range(layers + 1):
            high = [faces(case * comps + comp, base + z) for comp in range(comps)]
            if low is not None:
                part = quadratic(low, high, weights)
                energy[z - 1] = part if energy[z - 1] is None else energy[z - 1] + part
            low = high
    return energy


def blank_last(value, first, ylen):
    row = lax.broadcasted_iota(jnp.int32, value.shape, 0) + first
    return jnp.where(row == ylen - 1, 0.0, value)


def inner_kernel(totals, disp, fixed, density, solid, own, line, sends, last_plus, last_diff, last_factor, edge, plus, diff, quotient):
    loads, comps, zlen, ylen, xlen = disp.shape
    total_z, total_y = totals
    base_z = lax.axis_index("sz") * zlen
    base_y = lax.axis_index("sy") * ylen
    inner = zlen - 1
    keeps = jnp.where(on_first(), inner, 0)

    @pl.loop(0, loads * comps, unroll=True)
    def _(k):
        case, comp = k // comps, k % comps
        for z in range(zlen):
            whole, change = split_x(held(disp, fixed, case, comp, z, slice(None)))
            plus[k, z, :ylen] = whole
            diff[k, z, :ylen] = change
        last_plus[k] = plus[k, keeps, :ylen]
        last_diff[k] = diff[k, keeps, :ylen]

    for comp in range(comps):
        for case in range(loads):
            for z in range(zlen):
                at = (comp * loads + case) * zlen + z
                line[0, at : at + 1] = plus[case * comps + comp, z, ylen - 1 : ylen]
                line[1, at : at + 1] = diff[case * comps + comp, z, ylen - 1 : ylen]

    zeros = jnp.zeros((TILE, xlen), jnp.float32)
    edge[...] = jnp.zeros(edge.shape, jnp.float32)
    for z in range(zlen):
        factor = voxel_factor(density[z], solid[z], base_z + z, base_y, total_z, total_y)
        edge[z : z + 1] = factor[ylen - 1 :]
        if z == inner:
            last_factor[...] = factor
        else:
            quotient[z, :TILE] = zeros
            quotient[z, TILE : TILE + ylen] = factor
            quotient[z, TILE + ylen :] = zeros

    for first in range(0, ylen, TILE):

        @pl.loop(0, xlen // LANES, unroll=True)
        def _(chunk):
            lanes = pl.ds(pl.multiple_of(chunk * LANES, LANES), LANES)
            energy = tile_energies(plus, diff, first, lanes, inner, loads, comps)
            for z in range(inner):
                here = quotient[z, first + TILE : first + 2 * TILE, lanes]
                quotient[z, first + TILE : first + 2 * TILE, lanes] = blank_last(energy[z] * here, first, ylen)

    for z in range(inner):
        own[z] = spread_x(spread_y(quotient.at[z], ylen))
        ahead, back = to_neighbours(quotient.at[z], ylen)
        ends = spread_x(jnp.concatenate(ahead + back + [zeros[:2]], axis=0))
        sends[0, REACH * z : REACH * (z + 1)] = ends[:REACH]
        sends[1, REACH * z : REACH * (z + 1)] = ends[REACH : 2 * REACH]


def outer_kernel(
    shape, z_in, y_in, own_in, line, sends, last_plus, last_diff, last_factor, edge, share, corner, plus, diff, quotient, factor
):
    loads, comps, zlen, ylen, xlen = shape
    planes = loads * comps
    inner = zlen - 1
    first_core, index = on_first(), lax.axis_index("sz")
    top = first_core & (index == lax.axis_size("sz") - 1)
    more = lax.axis_index("sy") < lax.axis_size("sy") - 1
    stays, comes = jnp.where(first_core, 0, 1), jnp.where(first_core, jnp.where(top, 2, 1), 0)
    y_plus, y_diff = split_x(jnp.where(more, y_in[...], 0.0))
    for k in range(planes):
        plus[k, stays, :ylen] = last_plus[k]
        diff[k, stays, :ylen] = last_diff[k]
        whole, change = split_x(z_in[k])
        plus[k, comes, :ylen] = whole
        diff[k, comes, :ylen] = change
        for group, value in enumerate((last_plus[k, ylen - 1 :], last_diff[k, ylen - 1 :], whole[ylen - 1 :], change[ylen - 1 :])):
            corner[group, k : k + 1] = value
    below = jnp.where(index > 0, z_in[planes], 0.0)
    factor[...] = jnp.where(first_core, last_factor[...], below)
    corner[0, planes : planes + 1] = factor[ylen - 1 :]

    @pl.when(top)
    def _():
        clamped = jnp.zeros((ylen + TILE, xlen), jnp.float32)
        for k in range(planes):
            for slot in (1, 3):
                plus[k, slot] = clamped
                diff[k, slot] = clamped

    zeros = jnp.zeros((TILE, xlen), jnp.float32)
    quotient[:TILE] = zeros
    quotient[TILE + ylen :] = zeros
    for first in range(0, ylen, TILE):

        @pl.loop(0, xlen // LANES, unroll=True)
        def _(chunk):
            lanes = pl.ds(pl.multiple_of(chunk * LANES, LANES), LANES)
            (energy,) = tile_energies(plus, diff, first, lanes, 1, loads, comps)
            here = energy * factor[first : first + TILE, lanes]
            quotient[first + TILE : first + 2 * TILE, lanes] = blank_last(here, first, ylen)

    @pl.when(top)
    def _():
        for first in range(0, ylen, TILE):

            @pl.loop(0, xlen // LANES, unroll=True)
            def _(chunk):
                lanes = pl.ds(pl.multiple_of(chunk * LANES, LANES), LANES)
                (energy,) = tile_energies(plus, diff, first, lanes, 1, loads, comps, base=2)
                here = energy * factor[first : first + TILE, lanes]
                quotient[first + TILE : first + 2 * TILE, lanes] += blank_last(here, first, ylen)

    count = loads * zlen
    low, high = [], []
    for comp in range(comps):
        part = slice(comp * count, (comp + 1) * count)
        whole, change = line[0, part], line[1, part]
        whole_next, change_next = y_plus[part], y_diff[part]
        face = (whole + whole_next, change + change_next, whole_next - whole, change_next - change)
        low.append(face)
        high.append([pltpu.roll(value, count - 1, 0) for value in face])
    energy = quadratic(low, high, mode_weights())
    energy = sum(energy[case * zlen : case * zlen + inner] for case in range(loads)) * edge[:inner]
    last = spread_x(jnp.concatenate([energy, jnp.zeros((TILE - inner, xlen), jnp.float32)], axis=0))

    row = lax.broadcasted_iota(jnp.int32, (TILE, xlen), 0)
    rising = jnp.maximum(row - (TILE - 1 - ROWS), 0).astype(jnp.float32)
    ups, downs = [], []
    for z in range(inner):
        share[ylen * z : ylen * (z + 1)] = own_in[z]
        share[ylen * (z + 1) - TILE : ylen * (z + 1)] += rising * last[z : z + 1]
        here = sends[0, REACH * z : REACH * (z + 1)]
        ups += [here[r : r + 1] + float(REACH - r) * last[z : z + 1] for r in range(REACH)]
        downs.append(sends[1, REACH * z : REACH * (z + 1)])
    share[ylen * inner : ylen * zlen] = spread_x(spread_y(quotient, ylen))
    ahead, back = to_neighbours(quotient, ylen)
    ends = spread_x(jnp.concatenate(ahead + back + [zeros[:2]], axis=0))
    share[ylen * zlen :] = jnp.concatenate(ups + [ends[:REACH]] + downs + [ends[REACH : 2 * REACH]], axis=0)


def corner_line(shape, corner, y_in, d_in):
    loads, comps, zlen, ylen, xlen = shape
    planes = loads * comps
    first_core = on_first()
    top = first_core & (lax.axis_index("sz") == lax.axis_size("sz") - 1)
    more = lax.axis_index("sy") < lax.axis_size("sy") - 1
    rows = []
    for k in range(planes):
        at = (k % comps * loads + k // comps) * zlen
        rows.append(jnp.where(first_core, y_in[at + zlen - 1 : at + zlen], y_in[at : at + 1]))
    rows.append(jnp.zeros((-planes % TILE, xlen), jnp.float32))
    stays_next = split_x(jnp.where(more, jnp.concatenate(rows, axis=0), 0.0))
    comes_next = split_x(jnp.where(more, d_in[...], 0.0))

    def faces(stays, comes, comp):
        zero = jnp.zeros((1, xlen), jnp.float32)
        under, over = [], []
        for own, other in zip(stays, comes):
            own, other = ([value[case * comps + comp : case * comps + comp + 1] for case in range(loads)] for value in (own, other))
            low = [jnp.where(first_core, a, b) for a, b in zip(own, other)] + [jnp.where(top, b, 0.0) for b in other]
            high = [jnp.where(first_core, jnp.where(top, 0.0, b), a) for a, b in zip(own, other)] + [zero] * loads
            under.append(jnp.concatenate(low, axis=0))
            over.append(jnp.concatenate(high, axis=0))
        return under, over

    low, high = [], []
    for comp in range(comps):
        near = faces((corner[0], corner[1]), (corner[2], corner[3]), comp)
        far = faces(stays_next, comes_next, comp)
        for (whole, change), (whole_next, change_next), into in zip(near, far, (low, high)):
            into.append((whole + whole_next, change + change_next, whole_next - whole, change_next - change))
    energy = quadratic(low, high, mode_weights())
    line = sum(energy[case : case + 1] for case in range(2 * loads)) * corner[0, planes : planes + 1]
    return spread_x(jnp.concatenate([line, jnp.zeros((TILE - 1, xlen), jnp.float32)], axis=0))[:1]


def corner_kernel(shape, share_in, corner, y_in, d_in, share):
    _, _, zlen, ylen, xlen = shape
    line = corner_line(shape, corner, y_in, d_in)
    rising = jnp.maximum(lax.broadcasted_iota(jnp.int32, (TILE, xlen), 0) - (TILE - 1 - ROWS), 0).astype(jnp.float32)
    falling = (REACH - lax.broadcasted_iota(jnp.int32, (REACH, xlen), 0)).astype(jnp.float32)
    share[...] = share_in[...]
    share[ylen * zlen - TILE : ylen * zlen] += rising * line
    share[ylen * zlen + REACH * (zlen - 1) : ylen * zlen + REACH * zlen] += falling * line


def total_kernel(shape, share, other, h_out, z_out, y_out, d_out, e_out):
    _, _, zlen, ylen, xlen = shape
    first_core = on_first()
    inner, rows = zlen - 1, ylen * zlen
    reach = REACH * zlen

    def layers(first, count):
        mine, theirs = share[first + inner * count : first + zlen * count], other[first + inner * count : first + zlen * count]
        middle = share[first : first + inner * count] + other[first : first + inner * count]
        return jnp.where(first_core, theirs, mine), middle, jnp.where(first_core, mine, theirs)

    lowest, middle, highest = layers(0, ylen)
    h_out[0] = lowest
    for z in range(inner):
        h_out[z + 1] = middle[ylen * z : ylen * (z + 1)]
    h_out[zlen] = highest
    up_z, up_y = upward("sz"), upward("sy")
    z_out[...] = h_out[pl.ds(jnp.where(up_z, 1, 0), zlen)]
    ups = jnp.concatenate(layers(rows, REACH), axis=0)
    downs = jnp.concatenate(layers(rows + reach, REACH), axis=0)
    ends = jnp.where(up_y, ups, downs)
    y_out[: reach + REACH] = ends
    for out, used in ((y_out, reach + REACH), (d_out, reach), (e_out, reach)):
        out[used:] = jnp.zeros((out.shape[0] - used, xlen), jnp.float32)
    d_out[:reach] = jnp.where(up_z, ends[REACH:], ends[:reach])
    e_out[:reach] = jnp.where(up_z, ends[:reach], ends[REACH:])


def layers_kernel(h, d_in, e_in, y_in, z_in, out):
    zlen, ylen, xlen = out.shape
    first_core = on_first()
    up_z, up_y = upward("sz"), upward("sy")
    z_index, z_last = lax.axis_index("sz"), lax.axis_size("sz") - 1
    y_index, y_last = lax.axis_index("sy"), lax.axis_size("sy") - 1
    near = jnp.where(up_z, z_index < z_last, z_index > 0)
    far = jnp.where(up_z, z_index > 0, z_index < z_last)
    beside = jnp.where(up_y, y_index < y_last, y_index > 0)
    blank = jnp.zeros((TILE - REACH, xlen), jnp.float32)

    def with_ends(layer, rows, keep):
        rows = jnp.where(keep, rows, 0.0)
        head = layer[:TILE] + jnp.concatenate([jnp.where(up_y, 0.0, rows), blank], axis=0)
        tail = layer[ylen - TILE :] + jnp.concatenate([blank, jnp.where(up_y, rows, 0.0)], axis=0)
        return jnp.concatenate([head, layer[TILE : ylen - TILE], tail] if ylen > 2 * TILE else [head, tail], axis=0)

    own = []
    for k in range(zlen + 1):
        own.append(with_ends(jnp.where(first_core, h[k], 0.0), y_in[REACH * k : REACH * (k + 1)], beside))
    zero = jnp.zeros((ylen, xlen), jnp.float32)
    below, above = [], []
    for k in range(zlen):
        part = slice(REACH * k, REACH * (k + 1))
        from_near = with_ends(jnp.where(near, z_in[k], 0.0), d_in[part], near & beside)
        from_far = with_ends(zero, e_in[part], far & beside)
        below.append(jnp.where(up_z, from_far, from_near))
        above.append(jnp.where(up_z, from_near, from_far))
    below = below[zlen - REACH :]
    layers = below[:-1] + [below[-1] + own[0]] + own[1:-1] + [own[-1] + above[0]] + above[1:]
    for z, layer in enumerate(spread_layers(layers)):
        out[z] = layer


def sum_kernel(part, other, out):
    out[...] = part[...] + other[...]


def call(kernel, outs, args, scratch=(), space=pltpu.VMEM):
    shapes = [jax.ShapeDtypeStruct(out, jnp.float32) if isinstance(out, tuple) else out for out in outs]
    return pl.pallas_call(
        kernel,
        out_shape=shapes,
        in_specs=[pl.BlockSpec(memory_space=space)] * len(args),
        out_specs=[pl.BlockSpec(memory_space=pltpu.VMEM)] * len(outs),
        scratch_shapes=list(scratch),
        compiler_params=pltpu.CompilerParams(vmem_limit_bytes=32 * 1024 * 1024),
    )(*args)


def ring_moved(value, axis):
    size = lax.axis_size(axis)
    return lax.ppermute(value, axis, [((k + 1) % size, k) for k in range(size)])


def chip_swapped(value):
    cores = lax.axis_size("load")
    return lax.ppermute(value, "load", [(core, cores - 1 - core) for core in range(cores)])


def opposed(value, z_step, y_step, y_shift=0):
    cores, rows, size = lax.axis_size("load"), lax.axis_size("sy"), lax.axis_size("sz")
    pairs = []
    for core in range(cores):
        sign = -1 if core else 1
        for y in range(rows):
            for z in range(size):
                to_y, to_z, side = y + sign * y_step, z + sign * z_step, core
                if not (0 <= to_y < rows and 0 <= to_z < size):
                    to_y, to_z, side = y, z, cores - 1 - core
                to_y = (to_y + y_shift) % rows
                pairs.append(((core * rows + y) * size + z, (side * rows + to_y) * size + to_z))
    return lax.ppermute(value, ("load", "sy", "sz"), pairs)


def partnered(value, z_way, y_way):
    cores, rows, size = lax.axis_size("load"), lax.axis_size("sy"), lax.axis_size("sz")
    pairs = []
    for core in range(cores):
        for y in range(rows):
            for z in range(size):
                to_z = z + z_way * (1 if (z + core) % 2 == 0 else -1)
                to_y = y + y_way * (1 if (y + core) % 2 == 0 else -1)
                if not 0 <= to_z < size:
                    to_y, to_z = y ^ 1, z
                elif not 0 <= to_y < rows:
                    to_y, to_z = y, z + z_way * (1 if (z + core) % 2 == 0 else -1) if z_way else z ^ 1
                pairs.append(((core * rows + y) * size + z, (core * rows + to_y) * size + to_z))
    assert sorted(target for _, target in pairs) == list(range(len(pairs)))
    return lax.ppermute(value, ("load", "sy", "sz"), pairs)


def body(displacements, density, solid, fixed):
    loads, comps, zlen, ylen, xlen = displacements.shape
    planes = loads * comps
    totals = (zlen * lax.axis_size("sz"), ylen * lax.axis_size("sy"))
    args = [
        pltpu.with_memory_space_constraint(arg, pltpu.HBM) for arg in (displacements, fixed, density, solid)
    ]

    d_send, z_send, y_send = call(
        lambda *refs: lead_kernel(totals, *refs),
        [(-(-planes // TILE) * TILE, xlen), (planes + 1, ylen, xlen), (planes * zlen, xlen)],
        args,
        scratch=[
            pltpu.VMEM((loads, comps, ylen, xlen), jnp.float32),
            pltpu.VMEM((ylen, xlen), jnp.int32),
            pltpu.VMEM((ylen, xlen), jnp.float32),
            pltpu.VMEM((ylen, xlen), jnp.int32),
            pltpu.VMEM((loads, comps, zlen, TILE, xlen), jnp.float32),
            pltpu.VMEM((zlen, TILE, xlen), jnp.int32),
            pltpu.SemaphoreType.DMA((6,)),
        ],
        space=pltpu.HBM,
    )
    d_in = opposed(d_send, -1, 0, y_shift=-1)
    z_in = opposed(z_send, -1, 0)
    y_in = ring_moved(y_send, "sy")
    nodes = lambda layers: pltpu.VMEM((planes, layers, ylen + TILE, xlen), jnp.float32)
    inner = call(
        lambda *refs: inner_kernel(totals, *refs),
        [
            (zlen, ylen, xlen),
            (2, planes * zlen, xlen),
            (2, REACH * (zlen - 1), xlen),
            (planes, ylen, xlen),
            (planes, ylen, xlen),
            (ylen, xlen),
            (TILE, xlen),
        ],
        (displacements, fixed, density, solid),
        scratch=[nodes(zlen), nodes(zlen), pltpu.VMEM((zlen - 1, ylen + 2 * TILE, xlen), jnp.float32)],
    )
    reach = REACH * zlen
    shape = displacements.shape
    share, corner = call(
        lambda *refs: outer_kernel(shape, *refs),
        [(ylen * zlen + 2 * reach, xlen), (4, -(-(planes + 1) // TILE) * TILE, xlen)],
        (z_in, y_in, *inner),
        scratch=[
            nodes(4),
            nodes(4),
            pltpu.VMEM((ylen + 2 * TILE, xlen), jnp.float32),
            pltpu.VMEM((ylen, xlen), jnp.float32),
        ],
    )
    (share,) = call(
        lambda *refs: corner_kernel(shape, *refs), [(ylen * zlen + 2 * reach, xlen)], (share, corner, y_in, d_in)
    )
    sent = (-(-(reach + REACH) // TILE) * TILE, xlen)
    h, z_send, y_send, d_send, e_send = call(
        lambda *refs: total_kernel(displacements.shape, *refs),
        [
            (zlen + 1, ylen, xlen),
            (zlen, ylen, xlen),
            sent,
            sent,
            sent,
        ],
        (share, chip_swapped(share)),
    )
    d_in = partnered(d_send, 1, 1)
    e_in = partnered(e_send, -1, 1)
    y_in = partnered(y_send, 0, 1)
    z_in = partnered(z_send, 1, 0)
    (part,) = call(layers_kernel, [(zlen, ylen, xlen)], (h, d_in, e_in, y_in, z_in))
    (out,) = call(sum_kernel, [(zlen, ylen, xlen)], (part, chip_swapped(part)))
    return out


def solution(mesh):
    return jax.shard_map(
        body,
        mesh=mesh,
        in_specs=(
            P("load", None, "sz", "sy", None),
            P("sz", "sy", None),
            P("sz", "sy", None),
            P("sz", "sy", None),
        ),
        out_specs=P("sz", "sy", None),
        check_vma=False,
    )
```

```python
import jax
import jax.numpy as jnp
import numpy as np
from jax import lax
from jax.experimental import pallas as pl
from jax.experimental.pallas import tpu as pltpu
from jax.sharding import PartitionSpec as P

OFFSETS = [(0, 0, 0), (1, 0, 0), (1, 1, 0), (0, 1, 0), (0, 0, 1), (1, 0, 1), (1, 1, 1), (0, 1, 1)]
REACH = 3
ROWS = REACH + 1
TILE = 8
LANES = 128


def element_matrix():
    corners = np.array(
        [
            [-1.0, -1.0, -1.0],
            [1.0, -1.0, -1.0],
            [1.0, 1.0, -1.0],
            [-1.0, 1.0, -1.0],
            [-1.0, -1.0, 1.0],
            [1.0, -1.0, 1.0],
            [1.0, 1.0, 1.0],
            [-1.0, 1.0, 1.0],
        ]
    )
    poisson = 0.3
    lame = poisson / ((1.0 + poisson) * (1.0 - 2.0 * poisson))
    shear = 1.0 / (2.0 * (1.0 + poisson))
    elastic = np.zeros((6, 6))
    elastic[:3, :3] = lame
    for k in range(3):
        elastic[k, k] += 2.0 * shear
        elastic[3 + k, 3 + k] = shear
    gauss = 1.0 / np.sqrt(3.0)
    stiffness = np.zeros((24, 24))
    for gi in range(2):
        for gj in range(2):
            for gk in range(2):
                point = np.array([(2 * gi - 1) * gauss, (2 * gj - 1) * gauss, (2 * gk - 1) * gauss])
                strain = np.zeros((6, 24))
                for node in range(8):
                    grads = np.zeros(3)
                    for k in range(3):
                        value = corners[node, k] / 8.0
                        for m in range(3):
                            if m != k:
                                value = value * (1.0 + point[m] * corners[node, m])
                        grads[k] = 2.0 * value
                    col = 3 * node
                    strain[0, col] = grads[0]
                    strain[1, col + 1] = grads[1]
                    strain[2, col + 2] = grads[2]
                    strain[3, col] = grads[1]
                    strain[3, col + 1] = grads[0]
                    strain[4, col + 1] = grads[2]
                    strain[4, col + 2] = grads[1]
                    strain[5, col] = grads[2]
                    strain[5, col + 2] = grads[0]
                stiffness += strain.T @ elastic @ strain / 8.0
    return stiffness


def mode_weights():
    modes = [(i, j, k) for k in (0, 1) for j in (0, 1) for i in (0, 1)]
    sums = np.zeros((24, 24))
    for m, mode in enumerate(modes):
        for n, corner in enumerate(OFFSETS):
            sign = np.prod([(1 if corner[d] else -1) if mode[d] else 1 for d in range(3)])
            for comp in range(3):
                sums[3 * m + comp, 3 * n + comp] = sign
    form = sums @ element_matrix() @ sums.T / 64.0

    def at(first, second):
        return form[3 * modes.index(first[1]) + first[0], 3 * modes.index(second[1]) + second[0]]

    ux, vy, uy = (0, (1, 0, 0)), (1, (0, 1, 0)), (0, (0, 1, 0))
    uxy, wyz = (0, (1, 1, 0)), (2, (0, 1, 1))
    wxy, vxz, uxyz = (2, (1, 1, 0)), (1, (1, 0, 1)), (0, (1, 1, 1))
    return dict(
        normal=at(ux, ux) - at(ux, vy),
        trace=at(ux, vy),
        shear=at(uy, uy),
        plus=(at(uxy, uxy) + at(uxy, wyz)) / 2,
        minus=(at(uxy, uxy) - at(uxy, wyz)) / 2,
        twist=at(wxy, wxy) - at(wxy, vxz),
        twist_sum=at(wxy, vxz),
        corner=at(uxyz, uxyz),
    )


def square(value):
    return value * value


def quadratic(low, high, weights):
    x = [low[c][1] + high[c][1] for c in range(3)]
    y = [low[c][2] + high[c][2] for c in range(3)]
    z = [high[c][0] - low[c][0] for c in range(3)]
    xy = [low[c][3] + high[c][3] for c in range(3)]
    xz = [high[c][1] - low[c][1] for c in range(3)]
    yz = [high[c][2] - low[c][2] for c in range(3)]
    xyz = [high[c][3] - low[c][3] for c in range(3)]
    normal = square(x[0]) + square(y[1]) + square(z[2])
    trace = square(x[0] + y[1] + z[2])
    shear = square(y[0] + x[1]) + square(z[0] + x[2]) + square(z[1] + y[2])
    pairs = ((xy[0], yz[2]), (xy[1], xz[2]), (xz[0], yz[1]))
    plus = sum(square(p + q) for p, q in pairs)
    minus = sum(square(p - q) for p, q in pairs)
    twist = square(xy[2]) + square(xz[1]) + square(yz[0])
    twist_sum = square(xy[2] + xz[1] + yz[0])
    corner = square(xyz[0]) + square(xyz[1]) + square(xyz[2])
    groups = dict(
        normal=normal, trace=trace, shear=shear, plus=plus, minus=minus, twist=twist, twist_sum=twist_sum, corner=corner
    )
    return sum(np.float32(weights[name]) * group for name, group in groups.items())


def line_weight(coord, count):
    def outside(distance):
        missing = jnp.maximum(REACH - distance, 0)
        return missing * (missing + 1) // 2

    whole = (REACH + 1) * (REACH + 1)
    return (whole - outside(coord) - outside(count - 1 - coord)).astype(jnp.float32)


def voxel_factor(density, solid, plane, first_row, total_z, total_y):
    rows, length = density.shape
    row = lax.broadcasted_iota(jnp.int32, (rows, length), 0) + first_row
    column = lax.broadcasted_iota(jnp.int32, (rows, length), 1)
    weight = line_weight(row, total_y) * line_weight(column, length)
    weight = weight * line_weight(jnp.full((rows, length), plane, jnp.int32), total_z)
    return solid.astype(jnp.float32) * (-3.0 * density * density) / weight


def spread_x(value):
    rows, length = value.shape
    wide = jnp.concatenate([value, jnp.zeros((rows, LANES), jnp.float32)], axis=1)
    span = length + LANES
    total = float(ROWS) * value
    for step in range(1, ROWS):
        both = pltpu.roll(wide, span - step, 1) + pltpu.roll(wide, step, 1)
        total = total + float(ROWS - step) * both[:, :length]
    return total


def spread_layers(layers):
    for step in (1, 2, 1, 2):
        layers = [layers[k] + layers[k + step] for k in range(len(layers) - step)]
    return layers


def held(disp, fixed, case, comp, z, rows):
    return disp[case, comp, z, rows] * (1.0 - fixed[z, rows].astype(jnp.float32))


def split_x(value):
    length = value.shape[1]
    column = lax.broadcasted_iota(jnp.int32, value.shape, 1)
    ahead = jnp.where(column == length - 1, 0.0, pltpu.roll(value, length - 1, 1))
    return value + ahead, ahead - value


def spread_y(quotient, ylen):
    rows = [quotient[TILE + step : TILE + step + ylen] for step in range(-REACH, REACH + 1)]
    return sum((ROWS - abs(k - REACH)) * rows[k] for k in range(2 * REACH + 1))


def to_neighbours(quotient, ylen):
    top = quotient[ylen : ylen + TILE]
    base = quotient[TILE : 2 * TILE]
    ahead, back = [], []
    for row in range(REACH):
        ahead.append(sum(float(REACH - row - k) * top[TILE - 1 - k : TILE - k] for k in range(REACH - row)))
        back.append(sum(float(row + 1 - k) * base[k : k + 1] for k in range(row + 1)))
    return ahead, back


def on_first():
    return lax.axis_index("load") == 0


def lead_kernel(
    totals, disp_hbm, fixed_hbm, density_hbm, solid_hbm, d_out, z_out, y_out, *rest
):
    *kept, layer, layer_fixed, density, solid, rows, rows_fixed, sems = rest
    loads, comps, zlen, ylen, _ = disp_hbm.shape
    gives = jnp.where(on_first(), 0, zlen - 1)
    copies = [
        pltpu.make_async_copy(source, target, sems.at[k])
        for k, (source, target) in enumerate(
            (
                (density_hbm.at[gives], density),
                (solid_hbm.at[gives], solid),
                (fixed_hbm.at[gives], layer_fixed),
                (disp_hbm.at[:, :, gives], layer),
                (fixed_hbm.at[:, :TILE], rows_fixed),
                (disp_hbm.at[:, :, :, :TILE], rows),
                *zip((disp_hbm, fixed_hbm, density_hbm, solid_hbm), kept),
            )
        )
    ]
    for copy in copies:
        copy.start()
    for copy in copies[:2]:
        copy.wait()
    plane = lax.axis_index("sz") * zlen + gives
    base_y = lax.axis_index("sy") * ylen
    d_out[...] = jnp.zeros(d_out.shape, jnp.float32)
    z_out[loads * comps] = voxel_factor(density[...], solid[...], plane, base_y, *totals)
    for copy in copies[2:4]:
        copy.wait()
    free = 1.0 - layer_fixed[...].astype(jnp.float32)
    for case in range(loads):
        for comp in range(comps):
            k = case * comps + comp
            z_out[k] = layer[case, comp] * free
            d_out[k : k + 1] = z_out[k, :1]
    for copy in copies[4:6]:
        copy.wait()
    for z in range(zlen):
        free = 1.0 - rows_fixed[z, :1].astype(jnp.float32)
        for case in range(loads):
            for comp in range(comps):
                at = (comp * loads + case) * zlen + z
                y_out[at : at + 1] = rows[case, comp, z, :1] * free
    for copy in copies[6:]:
        copy.wait()


def tile_energies(plus, diff, first, lanes, layers, loads, comps, base=0):
    weights = mode_weights()

    def faces(k, z):
        near, far = slice(first, first + TILE), slice(first + 1, first + TILE + 1)
        whole, whole_next = plus[k, z, near, lanes], plus[k, z, far, lanes]
        change, change_next = diff[k, z, near, lanes], diff[k, z, far, lanes]
        return whole + whole_next, change + change_next, whole_next - whole, change_next - change

    energy = [None] * layers
    for case in range(loads):
        low = None
        for z in range(layers + 1):
            high = [faces(case * comps + comp, base + z) for comp in range(comps)]
            if low is not None:
                part = quadratic(low, high, weights)
                energy[z - 1] = part if energy[z - 1] is None else energy[z - 1] + part
            low = high
    return energy


def blank_last(value, first, ylen):
    row = lax.broadcasted_iota(jnp.int32, value.shape, 0) + first
    return jnp.where(row == ylen - 1, 0.0, value)


def inner_kernel(totals, disp, fixed, density, solid, own, line, sends, last_plus, last_diff, last_factor, edge, plus, diff, quotient):
    loads, comps, zlen, ylen, xlen = disp.shape
    total_z, total_y = totals
    base_z = lax.axis_index("sz") * zlen
    base_y = lax.axis_index("sy") * ylen
    inner = zlen - 1
    keeps = jnp.where(on_first(), inner, 0)
    free = [1.0 - fixed[z].astype(jnp.float32) for z in range(zlen)]

    @pl.loop(0, loads * comps, unroll=True)
    def _(k):
        case, comp = k // comps, k % comps
        for z in range(zlen):
            whole, change = split_x(disp[case, comp, z] * free[z])
            plus[k, z, :ylen] = whole
            diff[k, z, :ylen] = change
        last_plus[k] = plus[k, keeps, :ylen]
        last_diff[k] = diff[k, keeps, :ylen]

    for comp in range(comps):
        for case in range(loads):
            for z in range(zlen):
                at = (comp * loads + case) * zlen + z
                line[0, at : at + 1] = plus[case * comps + comp, z, ylen - 1 : ylen]
                line[1, at : at + 1] = diff[case * comps + comp, z, ylen - 1 : ylen]

    zeros = jnp.zeros((TILE, xlen), jnp.float32)
    edge[...] = jnp.zeros(edge.shape, jnp.float32)
    for z in range(zlen):
        factor = voxel_factor(density[z], solid[z], base_z + z, base_y, total_z, total_y)
        edge[z : z + 1] = factor[ylen - 1 :]
        if z == inner:
            last_factor[...] = factor
        else:
            quotient[z, :TILE] = zeros
            quotient[z, TILE : TILE + ylen] = factor
            quotient[z, TILE + ylen :] = zeros

    for first in range(0, ylen, TILE):

        @pl.loop(0, xlen // LANES, unroll=True)
        def _(chunk):
            lanes = pl.ds(pl.multiple_of(chunk * LANES, LANES), LANES)
            energy = tile_energies(plus, diff, first, lanes, inner, loads, comps)
            for z in range(inner):
                here = quotient[z, first + TILE : first + 2 * TILE, lanes]
                quotient[z, first + TILE : first + 2 * TILE, lanes] = blank_last(energy[z] * here, first, ylen)

    for z in range(inner):
        own[z] = spread_x(spread_y(quotient.at[z], ylen))
        ahead, back = to_neighbours(quotient.at[z], ylen)
        ends = spread_x(jnp.concatenate(ahead + back + [zeros[:2]], axis=0))
        sends[0, REACH * z : REACH * (z + 1)] = ends[:REACH]
        sends[1, REACH * z : REACH * (z + 1)] = ends[REACH : 2 * REACH]


def outer_kernel(
    shape, z_in, y_in, own_in, line, sends, last_plus, last_diff, last_factor, edge, share, corner, plus, diff, quotient, factor
):
    loads, comps, zlen, ylen, xlen = shape
    planes = loads * comps
    inner = zlen - 1
    first_core, index = on_first(), lax.axis_index("sz")
    top = first_core & (index == lax.axis_size("sz") - 1)
    more = lax.axis_index("sy") < lax.axis_size("sy") - 1
    stays, comes = jnp.where(first_core, 0, 1), jnp.where(first_core, jnp.where(top, 2, 1), 0)
    y_plus, y_diff = split_x(jnp.where(more, y_in[...], 0.0))
    for k in range(planes):
        plus[k, stays, :ylen] = last_plus[k]
        diff[k, stays, :ylen] = last_diff[k]
        whole, change = split_x(z_in[k])
        plus[k, comes, :ylen] = whole
        diff[k, comes, :ylen] = change
        for group, value in enumerate((last_plus[k, ylen - 1 :], last_diff[k, ylen - 1 :], whole[ylen - 1 :], change[ylen - 1 :])):
            corner[group, k : k + 1] = value
    below = jnp.where(index > 0, z_in[planes], 0.0)
    factor[...] = jnp.where(first_core, last_factor[...], below)
    corner[0, planes : planes + 1] = factor[ylen - 1 :]

    @pl.when(top)
    def _():
        clamped = jnp.zeros((ylen + TILE, xlen), jnp.float32)
        for k in range(planes):
            for slot in (1, 3):
                plus[k, slot] = clamped
                diff[k, slot] = clamped

    zeros = jnp.zeros((TILE, xlen), jnp.float32)
    quotient[:TILE] = zeros
    quotient[TILE + ylen :] = zeros
    for first in range(0, ylen, TILE):

        @pl.loop(0, xlen // LANES, unroll=True)
        def _(chunk):
            lanes = pl.ds(pl.multiple_of(chunk * LANES, LANES), LANES)
            (energy,) = tile_energies(plus, diff, first, lanes, 1, loads, comps)
            here = energy * factor[first : first + TILE, lanes]
            quotient[first + TILE : first + 2 * TILE, lanes] = blank_last(here, first, ylen)

    @pl.when(top)
    def _():
        for first in range(0, ylen, TILE):

            @pl.loop(0, xlen // LANES, unroll=True)
            def _(chunk):
                lanes = pl.ds(pl.multiple_of(chunk * LANES, LANES), LANES)
                (energy,) = tile_energies(plus, diff, first, lanes, 1, loads, comps, base=2)
                here = energy * factor[first : first + TILE, lanes]
                quotient[first + TILE : first + 2 * TILE, lanes] += blank_last(here, first, ylen)

    count = loads * zlen
    low, high = [], []
    for comp in range(comps):
        part = slice(comp * count, (comp + 1) * count)
        whole, change = line[0, part], line[1, part]
        whole_next, change_next = y_plus[part], y_diff[part]
        face = (whole + whole_next, change + change_next, whole_next - whole, change_next - change)
        low.append(face)
        high.append([pltpu.roll(value, count - 1, 0) for value in face])
    energy = quadratic(low, high, mode_weights())
    energy = sum(energy[case * zlen : case * zlen + inner] for case in range(loads)) * edge[:inner]
    last = spread_x(jnp.concatenate([energy, jnp.zeros((TILE - inner, xlen), jnp.float32)], axis=0))

    row = lax.broadcasted_iota(jnp.int32, (TILE, xlen), 0)
    rising = jnp.maximum(row - (TILE - 1 - ROWS), 0).astype(jnp.float32)
    ups, downs = [], []
    for z in range(inner):
        share[ylen * z : ylen * (z + 1)] = own_in[z]
        share[ylen * (z + 1) - TILE : ylen * (z + 1)] += rising * last[z : z + 1]
        here = sends[0, REACH * z : REACH * (z + 1)]
        ups += [here[r : r + 1] + float(REACH - r) * last[z : z + 1] for r in range(REACH)]
        downs.append(sends[1, REACH * z : REACH * (z + 1)])
    share[ylen * inner : ylen * zlen] = spread_x(spread_y(quotient, ylen))
    ahead, back = to_neighbours(quotient, ylen)
    ends = spread_x(jnp.concatenate(ahead + back + [zeros[:2]], axis=0))
    share[ylen * zlen :] = jnp.concatenate(ups + [ends[:REACH]] + downs + [ends[REACH : 2 * REACH]], axis=0)


def corner_line(shape, corner, y_in, d_in):
    loads, comps, zlen, ylen, xlen = shape
    planes = loads * comps
    first_core = on_first()
    top = first_core & (lax.axis_index("sz") == lax.axis_size("sz") - 1)
    more = lax.axis_index("sy") < lax.axis_size("sy") - 1
    rows = []
    for k in range(planes):
        at = (k % comps * loads + k // comps) * zlen
        rows.append(jnp.where(first_core, y_in[at + zlen - 1 : at + zlen], y_in[at : at + 1]))
    rows.append(jnp.zeros((-planes % TILE, xlen), jnp.float32))
    stays_next = split_x(jnp.where(more, jnp.concatenate(rows, axis=0), 0.0))
    comes_next = split_x(jnp.where(more, d_in[...], 0.0))

    def faces(stays, comes, comp):
        zero = jnp.zeros((1, xlen), jnp.float32)
        under, over = [], []
        for own, other in zip(stays, comes):
            own, other = ([value[case * comps + comp : case * comps + comp + 1] for case in range(loads)] for value in (own, other))
            low = [jnp.where(first_core, a, b) for a, b in zip(own, other)] + [jnp.where(top, b, 0.0) for b in other]
            high = [jnp.where(first_core, jnp.where(top, 0.0, b), a) for a, b in zip(own, other)] + [zero] * loads
            under.append(jnp.concatenate(low, axis=0))
            over.append(jnp.concatenate(high, axis=0))
        return under, over

    low, high = [], []
    for comp in range(comps):
        near = faces((corner[0], corner[1]), (corner[2], corner[3]), comp)
        far = faces(stays_next, comes_next, comp)
        for (whole, change), (whole_next, change_next), into in zip(near, far, (low, high)):
            into.append((whole + whole_next, change + change_next, whole_next - whole, change_next - change))
    energy = quadratic(low, high, mode_weights())
    line = sum(energy[case : case + 1] for case in range(2 * loads)) * corner[0, planes : planes + 1]
    return spread_x(jnp.concatenate([line, jnp.zeros((TILE - 1, xlen), jnp.float32)], axis=0))[:1]


def corner_kernel(shape, share_in, corner, y_in, d_in, share):
    _, _, zlen, ylen, xlen = shape
    line = corner_line(shape, corner, y_in, d_in)
    rising = jnp.maximum(lax.broadcasted_iota(jnp.int32, (TILE, xlen), 0) - (TILE - 1 - ROWS), 0).astype(jnp.float32)
    falling = (REACH - lax.broadcasted_iota(jnp.int32, (REACH, xlen), 0)).astype(jnp.float32)
    share[...] = share_in[...]
    share[ylen * zlen - TILE : ylen * zlen] += rising * line
    share[ylen * zlen + REACH * (zlen - 1) : ylen * zlen + REACH * zlen] += falling * line


def total_kernel(shape, share, other, h_out, z_out, y_out, d_out, e_out):
    _, _, zlen, ylen, xlen = shape
    first_core = on_first()
    inner, rows = zlen - 1, ylen * zlen
    reach = REACH * zlen

    def layers(first, count):
        mine, theirs = share[first + inner * count : first + zlen * count], other[first + inner * count : first + zlen * count]
        middle = share[first : first + inner * count] + other[first : first + inner * count]
        return jnp.where(first_core, theirs, mine), middle, jnp.where(first_core, mine, theirs)

    lowest, middle, highest = layers(0, ylen)
    h_out[0] = lowest
    for z in range(inner):
        h_out[z + 1] = middle[ylen * z : ylen * (z + 1)]
    h_out[zlen] = highest
    z_out[...] = h_out[pl.ds(jnp.where(first_core, 0, 1), zlen)]
    ups = jnp.concatenate(layers(rows, REACH), axis=0)
    downs = jnp.concatenate(layers(rows + reach, REACH), axis=0)
    y_out[: reach + REACH] = jnp.where(first_core, downs, ups)
    for out, used in ((y_out, reach + REACH), (d_out, reach), (e_out, reach)):
        out[used:] = jnp.zeros((out.shape[0] - used, xlen), jnp.float32)
    d_out[:reach] = jnp.where(first_core, downs[:reach], ups[REACH:])
    e_out[:reach] = jnp.where(first_core, ups[:reach], downs[REACH:])


def layers_kernel(h, d_in, e_in, y_in, z_in, out):
    zlen, ylen, xlen = out.shape
    reach = REACH * zlen
    first_core = on_first()
    z_index, z_last = lax.axis_index("sz"), lax.axis_size("sz") - 1
    y_index, y_last = lax.axis_index("sy"), lax.axis_size("sy") - 1
    z_side = jnp.where(first_core, z_index < z_last, z_index > 0)
    y_side = jnp.where(first_core, y_index < y_last, y_index > 0)
    y_other = jnp.where(first_core, y_index > 0, y_index < y_last)
    blank = jnp.zeros((TILE - REACH, xlen), jnp.float32)

    def at_start(rows):
        return jnp.concatenate([rows, blank], axis=0)

    def at_end(rows):
        return jnp.concatenate([blank, rows], axis=0)

    def ends(rows, keep, at_last):
        rows = jnp.where(keep, rows, 0.0)
        return at_start(jnp.where(at_last, 0.0, rows)), at_end(jnp.where(at_last, rows, 0.0))

    def with_ends(layer, *pairs):
        head, tail = layer[:TILE], layer[ylen - TILE :]
        for first, last in pairs:
            head, tail = head + first, tail + last
        return jnp.concatenate([head, layer[TILE : ylen - TILE], tail] if ylen > 2 * TILE else [head, tail], axis=0)

    own = []
    for k in range(zlen + 1):
        layer = jnp.where(first_core, h[k], 0.0)
        own.append(with_ends(layer, ends(y_in[REACH * k : REACH * (k + 1)], y_side, first_core)))
    come = []
    for k in range(zlen):
        part = slice(REACH * k, REACH * (k + 1))
        layer = jnp.where(z_side, z_in[k], 0.0)
        straight = ends(d_in[part], z_side & y_side, first_core)
        across = ends(e_in[part], z_side & y_other, jnp.logical_not(first_core))
        come.append(with_ends(layer, straight, across))
    below = [jnp.where(first_core, 0.0, layer) for layer in come[zlen - REACH :]]
    above = [jnp.where(first_core, layer, 0.0) for layer in come]
    layers = below[:-1] + [below[-1] + own[0]] + own[1:-1] + [own[-1] + above[0]] + above[1:]
    for z, layer in enumerate(spread_layers(layers)):
        out[z] = layer


def sum_kernel(part, other, out):
    out[...] = part[...] + other[...]


def call(kernel, outs, args, scratch=(), space=pltpu.VMEM):
    shapes = [jax.ShapeDtypeStruct(out, jnp.float32) if isinstance(out, tuple) else out for out in outs]
    return pl.pallas_call(
        kernel,
        out_shape=shapes,
        in_specs=[pl.BlockSpec(memory_space=space)] * len(args),
        out_specs=[pl.BlockSpec(memory_space=pltpu.VMEM)] * len(outs),
        scratch_shapes=list(scratch),
        compiler_params=pltpu.CompilerParams(vmem_limit_bytes=32 * 1024 * 1024),
    )(*args)


def ring_moved(value, axis):
    size = lax.axis_size(axis)
    return lax.ppermute(value, axis, [((k + 1) % size, k) for k in range(size)])


def chip_swapped(value):
    cores = lax.axis_size("load")
    return lax.ppermute(value, "load", [(core, cores - 1 - core) for core in range(cores)])


def opposed(value, z_step, y_step, y_shift=0):
    cores, rows, size = lax.axis_size("load"), lax.axis_size("sy"), lax.axis_size("sz")
    pairs = []
    for core in range(cores):
        sign = -1 if core else 1
        for y in range(rows):
            for z in range(size):
                to_y, to_z, side = y + sign * y_step, z + sign * z_step, core
                if not (0 <= to_y < rows and 0 <= to_z < size):
                    to_y, to_z, side = y, z, cores - 1 - core
                to_y = (to_y + y_shift) % rows
                pairs.append(((core * rows + y) * size + z, (side * rows + to_y) * size + to_z))
    return lax.ppermute(value, ("load", "sy", "sz"), pairs)


def body(displacements, density, solid, fixed):
    loads, comps, zlen, ylen, xlen = displacements.shape
    planes = loads * comps
    totals = (zlen * lax.axis_size("sz"), ylen * lax.axis_size("sy"))
    args = [
        pltpu.with_memory_space_constraint(arg, pltpu.HBM) for arg in (displacements, fixed, density, solid)
    ]

    d_send, z_send, y_send, *kept = call(
        lambda *refs: lead_kernel(totals, *refs),
        [(-(-planes // TILE) * TILE, xlen), (planes + 1, ylen, xlen), (planes * zlen, xlen)]
        + [jax.ShapeDtypeStruct(arg.shape, arg.dtype) for arg in args],
        args,
        scratch=[
            pltpu.VMEM((loads, comps, ylen, xlen), jnp.float32),
            pltpu.VMEM((ylen, xlen), jnp.int32),
            pltpu.VMEM((ylen, xlen), jnp.float32),
            pltpu.VMEM((ylen, xlen), jnp.int32),
            pltpu.VMEM((loads, comps, zlen, TILE, xlen), jnp.float32),
            pltpu.VMEM((zlen, TILE, xlen), jnp.int32),
            pltpu.SemaphoreType.DMA((6 + len(args),)),
        ],
        space=pltpu.HBM,
    )
    d_in = opposed(d_send, -1, 0, y_shift=-1)
    z_in = opposed(z_send, -1, 0)
    y_in = ring_moved(y_send, "sy")
    nodes = lambda layers: pltpu.VMEM((planes, layers, ylen + TILE, xlen), jnp.float32)
    inner = call(
        lambda *refs: inner_kernel(totals, *refs),
        [
            (zlen, ylen, xlen),
            (2, planes * zlen, xlen),
            (2, REACH * (zlen - 1), xlen),
            (planes, ylen, xlen),
            (planes, ylen, xlen),
            (ylen, xlen),
            (TILE, xlen),
        ],
        kept,
        scratch=[nodes(zlen), nodes(zlen), pltpu.VMEM((zlen - 1, ylen + 2 * TILE, xlen), jnp.float32)],
    )
    reach = REACH * zlen
    shape = displacements.shape
    share, corner = call(
        lambda *refs: outer_kernel(shape, *refs),
        [(ylen * zlen + 2 * reach, xlen), (4, -(-(planes + 1) // TILE) * TILE, xlen)],
        (z_in, y_in, *inner),
        scratch=[
            nodes(4),
            nodes(4),
            pltpu.VMEM((ylen + 2 * TILE, xlen), jnp.float32),
            pltpu.VMEM((ylen, xlen), jnp.float32),
        ],
    )
    (share,) = call(
        lambda *refs: corner_kernel(shape, *refs), [(ylen * zlen + 2 * reach, xlen)], (share, corner, y_in, d_in)
    )
    sent = (-(-(reach + REACH) // TILE) * TILE, xlen)
    h, z_send, y_send, d_send, e_send = call(
        lambda *refs: total_kernel(displacements.shape, *refs),
        [
            (zlen + 1, ylen, xlen),
            (zlen, ylen, xlen),
            sent,
            sent,
            sent,
        ],
        (share, chip_swapped(share)),
    )
    d_in = opposed(d_send, -1, -1)
    e_in = opposed(e_send, -1, 1)
    y_in = opposed(y_send, 0, -1)
    z_in = opposed(z_send, -1, 0)
    (part,) = call(layers_kernel, [(zlen, ylen, xlen)], (h, d_in, e_in, y_in, z_in))
    (out,) = call(sum_kernel, [(zlen, ylen, xlen)], (part, chip_swapped(part)))
    return out


def solution(mesh):
    return jax.shard_map(
        body,
        mesh=mesh,
        in_specs=(
            P("load", None, "sz", "sy", None),
            P("sz", "sy", None),
            P("sz", "sy", None),
            P("sz", "sy", None),
        ),
        out_specs=P("sz", "sy", None),
        check_vma=False,
    )
```

```python
import jax
import jax.numpy as jnp
import numpy as np
from jax import lax
from jax.experimental import pallas as pl
from jax.experimental.pallas import tpu as pltpu
from jax.sharding import PartitionSpec as P

OFFSETS = [(0, 0, 0), (1, 0, 0), (1, 1, 0), (0, 1, 0), (0, 0, 1), (1, 0, 1), (1, 1, 1), (0, 1, 1)]
REACH = 3
ROWS = REACH + 1
TILE = 8
LANES = 128


def element_matrix():
    corners = np.array(
        [
            [-1.0, -1.0, -1.0],
            [1.0, -1.0, -1.0],
            [1.0, 1.0, -1.0],
            [-1.0, 1.0, -1.0],
            [-1.0, -1.0, 1.0],
            [1.0, -1.0, 1.0],
            [1.0, 1.0, 1.0],
            [-1.0, 1.0, 1.0],
        ]
    )
    poisson = 0.3
    lame = poisson / ((1.0 + poisson) * (1.0 - 2.0 * poisson))
    shear = 1.0 / (2.0 * (1.0 + poisson))
    elastic = np.zeros((6, 6))
    elastic[:3, :3] = lame
    for k in range(3):
        elastic[k, k] += 2.0 * shear
        elastic[3 + k, 3 + k] = shear
    gauss = 1.0 / np.sqrt(3.0)
    stiffness = np.zeros((24, 24))
    for gi in range(2):
        for gj in range(2):
            for gk in range(2):
                point = np.array([(2 * gi - 1) * gauss, (2 * gj - 1) * gauss, (2 * gk - 1) * gauss])
                strain = np.zeros((6, 24))
                for node in range(8):
                    grads = np.zeros(3)
                    for k in range(3):
                        value = corners[node, k] / 8.0
                        for m in range(3):
                            if m != k:
                                value = value * (1.0 + point[m] * corners[node, m])
                        grads[k] = 2.0 * value
                    col = 3 * node
                    strain[0, col] = grads[0]
                    strain[1, col + 1] = grads[1]
                    strain[2, col + 2] = grads[2]
                    strain[3, col] = grads[1]
                    strain[3, col + 1] = grads[0]
                    strain[4, col + 1] = grads[2]
                    strain[4, col + 2] = grads[1]
                    strain[5, col] = grads[2]
                    strain[5, col + 2] = grads[0]
                stiffness += strain.T @ elastic @ strain / 8.0
    return stiffness


def mode_weights():
    modes = [(i, j, k) for k in (0, 1) for j in (0, 1) for i in (0, 1)]
    sums = np.zeros((24, 24))
    for m, mode in enumerate(modes):
        for n, corner in enumerate(OFFSETS):
            sign = np.prod([(1 if corner[d] else -1) if mode[d] else 1 for d in range(3)])
            for comp in range(3):
                sums[3 * m + comp, 3 * n + comp] = sign
    form = sums @ element_matrix() @ sums.T / 64.0

    def at(first, second):
        return form[3 * modes.index(first[1]) + first[0], 3 * modes.index(second[1]) + second[0]]

    ux, vy, uy = (0, (1, 0, 0)), (1, (0, 1, 0)), (0, (0, 1, 0))
    uxy, wyz = (0, (1, 1, 0)), (2, (0, 1, 1))
    wxy, vxz, uxyz = (2, (1, 1, 0)), (1, (1, 0, 1)), (0, (1, 1, 1))
    return dict(
        normal=at(ux, ux) - at(ux, vy),
        trace=at(ux, vy),
        shear=at(uy, uy),
        plus=(at(uxy, uxy) + at(uxy, wyz)) / 2,
        minus=(at(uxy, uxy) - at(uxy, wyz)) / 2,
        twist=at(wxy, wxy) - at(wxy, vxz),
        twist_sum=at(wxy, vxz),
        corner=at(uxyz, uxyz),
    )


def square(value):
    return value * value


def quadratic(low, high, weights):
    x = [low[c][1] + high[c][1] for c in range(3)]
    y = [low[c][2] + high[c][2] for c in range(3)]
    z = [high[c][0] - low[c][0] for c in range(3)]
    xy = [low[c][3] + high[c][3] for c in range(3)]
    xz = [high[c][1] - low[c][1] for c in range(3)]
    yz = [high[c][2] - low[c][2] for c in range(3)]
    xyz = [high[c][3] - low[c][3] for c in range(3)]
    normal = square(x[0]) + square(y[1]) + square(z[2])
    trace = square(x[0] + y[1] + z[2])
    shear = square(y[0] + x[1]) + square(z[0] + x[2]) + square(z[1] + y[2])
    pairs = ((xy[0], yz[2]), (xy[1], xz[2]), (xz[0], yz[1]))
    plus = sum(square(p + q) for p, q in pairs)
    minus = sum(square(p - q) for p, q in pairs)
    twist = square(xy[2]) + square(xz[1]) + square(yz[0])
    twist_sum = square(xy[2] + xz[1] + yz[0])
    corner = square(xyz[0]) + square(xyz[1]) + square(xyz[2])
    groups = dict(
        normal=normal, trace=trace, shear=shear, plus=plus, minus=minus, twist=twist, twist_sum=twist_sum, corner=corner
    )
    return sum(np.float32(weights[name]) * group for name, group in groups.items())


def line_weight(coord, count):
    def outside(distance):
        missing = jnp.maximum(REACH - distance, 0)
        return missing * (missing + 1) // 2

    whole = (REACH + 1) * (REACH + 1)
    return (whole - outside(coord) - outside(count - 1 - coord)).astype(jnp.float32)


def voxel_factor(density, solid, plane, first_row, total_z, total_y):
    rows, length = density.shape
    row = lax.broadcasted_iota(jnp.int32, (rows, length), 0) + first_row
    column = lax.broadcasted_iota(jnp.int32, (rows, length), 1)
    weight = line_weight(row, total_y) * line_weight(column, length)
    weight = weight * line_weight(jnp.full((rows, length), plane, jnp.int32), total_z)
    return solid.astype(jnp.float32) * (-3.0 * density * density) / weight


def spread_x(value):
    rows, length = value.shape
    wide = jnp.concatenate([value, jnp.zeros((rows, LANES), jnp.float32)], axis=1)
    span = length + LANES
    total = float(ROWS) * value
    for step in range(1, ROWS):
        both = pltpu.roll(wide, span - step, 1) + pltpu.roll(wide, step, 1)
        total = total + float(ROWS - step) * both[:, :length]
    return total


def spread_layers(layers):
    for step in (1, 2, 1, 2):
        layers = [layers[k] + layers[k + step] for k in range(len(layers) - step)]
    return layers


def held(disp, fixed, case, comp, z, rows):
    return disp[case, comp, z, rows] * (1.0 - fixed[z, rows].astype(jnp.float32))


def split_x(value):
    length = value.shape[1]
    column = lax.broadcasted_iota(jnp.int32, value.shape, 1)
    ahead = jnp.where(column == length - 1, 0.0, pltpu.roll(value, length - 1, 1))
    return value + ahead, ahead - value


def spread_y(quotient, ylen):
    rows = [quotient[TILE + step : TILE + step + ylen] for step in range(-REACH, REACH + 1)]
    return sum((ROWS - abs(k - REACH)) * rows[k] for k in range(2 * REACH + 1))


def to_neighbours(quotient, ylen):
    top = quotient[ylen : ylen + TILE]
    base = quotient[TILE : 2 * TILE]
    ahead, back = [], []
    for row in range(REACH):
        ahead.append(sum(float(REACH - row - k) * top[TILE - 1 - k : TILE - k] for k in range(REACH - row)))
        back.append(sum(float(row + 1 - k) * base[k : k + 1] for k in range(row + 1)))
    return ahead, back


def on_first():
    return lax.axis_index("load") == 0


def lead_kernel(totals, disp_hbm, fixed_hbm, density_hbm, solid_hbm, d_out, z_out, y_out, layer, layer_fixed, density, solid, rows, rows_fixed, sems):
    loads, comps, zlen, ylen, _ = disp_hbm.shape
    gives = jnp.where(on_first(), 0, zlen - 1)
    copies = [
        pltpu.make_async_copy(source, target, sems.at[k])
        for k, (source, target) in enumerate(
            (
                (density_hbm.at[gives], density),
                (solid_hbm.at[gives], solid),
                (fixed_hbm.at[gives], layer_fixed),
                (disp_hbm.at[:, :, gives], layer),
                (fixed_hbm.at[:, :1], rows_fixed),
                (disp_hbm.at[:, :, :, :1], rows),
            )
        )
    ]
    for copy in copies:
        copy.start()
    for copy in copies[:2]:
        copy.wait()
    plane = lax.axis_index("sz") * zlen + gives
    base_y = lax.axis_index("sy") * ylen
    d_out[...] = jnp.zeros(d_out.shape, jnp.float32)
    z_out[loads * comps] = voxel_factor(density[...], solid[...], plane, base_y, *totals)
    for copy in copies[2:4]:
        copy.wait()
    free = 1.0 - layer_fixed[...].astype(jnp.float32)
    for case in range(loads):
        for comp in range(comps):
            k = case * comps + comp
            z_out[k] = layer[case, comp] * free
            d_out[k : k + 1] = z_out[k, :1]
    for copy in copies[4:]:
        copy.wait()
    for z in range(zlen):
        free = 1.0 - rows_fixed[z, :1].astype(jnp.float32)
        for case in range(loads):
            for comp in range(comps):
                at = (comp * loads + case) * zlen + z
                y_out[at : at + 1] = rows[case, comp, z, :1] * free


def tile_energies(plus, diff, first, lanes, layers, loads, comps, base=0):
    weights = mode_weights()

    def faces(k, z):
        near, far = slice(first, first + TILE), slice(first + 1, first + TILE + 1)
        whole, whole_next = plus[k, z, near, lanes], plus[k, z, far, lanes]
        change, change_next = diff[k, z, near, lanes], diff[k, z, far, lanes]
        return whole + whole_next, change + change_next, whole_next - whole, change_next - change

    energy = [None] * layers
    for case in range(loads):
        low = None
        for z in range(layers + 1):
            high = [faces(case * comps + comp, base + z) for comp in range(comps)]
            if low is not None:
                part = quadratic(low, high, weights)
                energy[z - 1] = part if energy[z - 1] is None else energy[z - 1] + part
            low = high
    return energy


def blank_last(value, first, ylen):
    row = lax.broadcasted_iota(jnp.int32, value.shape, 0) + first
    return jnp.where(row == ylen - 1, 0.0, value)


def inner_kernel(totals, disp, fixed, density, solid, own, line, sends, last_plus, last_diff, last_factor, edge, plus, diff, quotient):
    loads, comps, zlen, ylen, xlen = disp.shape
    total_z, total_y = totals
    base_z = lax.axis_index("sz") * zlen
    base_y = lax.axis_index("sy") * ylen
    inner = zlen - 1
    keeps = jnp.where(on_first(), inner, 0)
    free = [1.0 - fixed[z].astype(jnp.float32) for z in range(zlen)]

    @pl.loop(0, loads * comps, unroll=True)
    def _(k):
        case, comp = k // comps, k % comps
        for z in range(zlen):
            whole, change = split_x(disp[case, comp, z] * free[z])
            plus[k, z, :ylen] = whole
            diff[k, z, :ylen] = change
        last_plus[k] = plus[k, keeps, :ylen]
        last_diff[k] = diff[k, keeps, :ylen]

    for comp in range(comps):
        for case in range(loads):
            for z in range(zlen):
                at = (comp * loads + case) * zlen + z
                line[0, at : at + 1] = plus[case * comps + comp, z, ylen - 1 : ylen]
                line[1, at : at + 1] = diff[case * comps + comp, z, ylen - 1 : ylen]

    zeros = jnp.zeros((TILE, xlen), jnp.float32)
    edge[...] = jnp.zeros(edge.shape, jnp.float32)
    for z in range(zlen):
        factor = voxel_factor(density[z], solid[z], base_z + z, base_y, total_z, total_y)
        edge[z : z + 1] = factor[ylen - 1 :]
        if z == inner:
            last_factor[...] = factor
        else:
            quotient[z, :TILE] = zeros
            quotient[z, TILE : TILE + ylen] = factor
            quotient[z, TILE + ylen :] = zeros

    for first in range(0, ylen, TILE):

        @pl.loop(0, xlen // LANES, unroll=True)
        def _(chunk):
            lanes = pl.ds(pl.multiple_of(chunk * LANES, LANES), LANES)
            energy = tile_energies(plus, diff, first, lanes, inner, loads, comps)
            for z in range(inner):
                here = quotient[z, first + TILE : first + 2 * TILE, lanes]
                quotient[z, first + TILE : first + 2 * TILE, lanes] = blank_last(energy[z] * here, first, ylen)

    for z in range(inner):
        own[z] = spread_x(spread_y(quotient.at[z], ylen))
        ahead, back = to_neighbours(quotient.at[z], ylen)
        ends = spread_x(jnp.concatenate(ahead + back + [zeros[:2]], axis=0))
        sends[0, REACH * z : REACH * (z + 1)] = ends[:REACH]
        sends[1, REACH * z : REACH * (z + 1)] = ends[REACH : 2 * REACH]


def outer_kernel(
    shape, z_in, y_in, own_in, line, sends, last_plus, last_diff, last_factor, edge, share, corner, plus, diff, quotient, factor
):
    loads, comps, zlen, ylen, xlen = shape
    planes = loads * comps
    inner = zlen - 1
    first_core, index = on_first(), lax.axis_index("sz")
    top = first_core & (index == lax.axis_size("sz") - 1)
    more = lax.axis_index("sy") < lax.axis_size("sy") - 1
    stays, comes = jnp.where(first_core, 0, 1), jnp.where(first_core, jnp.where(top, 2, 1), 0)
    y_plus, y_diff = split_x(jnp.where(more, y_in[...], 0.0))
    for k in range(planes):
        plus[k, stays, :ylen] = last_plus[k]
        diff[k, stays, :ylen] = last_diff[k]
        whole, change = split_x(z_in[k])
        plus[k, comes, :ylen] = whole
        diff[k, comes, :ylen] = change
        for group, value in enumerate((last_plus[k, ylen - 1 :], last_diff[k, ylen - 1 :], whole[ylen - 1 :], change[ylen - 1 :])):
            corner[group, k : k + 1] = value
    below = jnp.where(index > 0, z_in[planes], 0.0)
    factor[...] = jnp.where(first_core, last_factor[...], below)
    corner[0, planes : planes + 1] = factor[ylen - 1 :]

    @pl.when(top)
    def _():
        clamped = jnp.zeros((ylen + TILE, xlen), jnp.float32)
        for k in range(planes):
            for slot in (1, 3):
                plus[k, slot] = clamped
                diff[k, slot] = clamped

    zeros = jnp.zeros((TILE, xlen), jnp.float32)
    quotient[:TILE] = zeros
    quotient[TILE + ylen :] = zeros
    for first in range(0, ylen, TILE):

        @pl.loop(0, xlen // LANES, unroll=True)
        def _(chunk):
            lanes = pl.ds(pl.multiple_of(chunk * LANES, LANES), LANES)
            (energy,) = tile_energies(plus, diff, first, lanes, 1, loads, comps)
            here = energy * factor[first : first + TILE, lanes]
            quotient[first + TILE : first + 2 * TILE, lanes] = blank_last(here, first, ylen)

    @pl.when(top)
    def _():
        for first in range(0, ylen, TILE):

            @pl.loop(0, xlen // LANES, unroll=True)
            def _(chunk):
                lanes = pl.ds(pl.multiple_of(chunk * LANES, LANES), LANES)
                (energy,) = tile_energies(plus, diff, first, lanes, 1, loads, comps, base=2)
                here = energy * factor[first : first + TILE, lanes]
                quotient[first + TILE : first + 2 * TILE, lanes] += blank_last(here, first, ylen)

    count = loads * zlen
    low, high = [], []
    for comp in range(comps):
        part = slice(comp * count, (comp + 1) * count)
        whole, change = line[0, part], line[1, part]
        whole_next, change_next = y_plus[part], y_diff[part]
        face = (whole + whole_next, change + change_next, whole_next - whole, change_next - change)
        low.append(face)
        high.append([pltpu.roll(value, count - 1, 0) for value in face])
    energy = quadratic(low, high, mode_weights())
    energy = sum(energy[case * zlen : case * zlen + inner] for case in range(loads)) * edge[:inner]
    last = spread_x(jnp.concatenate([energy, jnp.zeros((TILE - inner, xlen), jnp.float32)], axis=0))

    row = lax.broadcasted_iota(jnp.int32, (TILE, xlen), 0)
    rising = jnp.maximum(row - (TILE - 1 - ROWS), 0).astype(jnp.float32)
    ups, downs = [], []
    for z in range(inner):
        share[ylen * z : ylen * (z + 1)] = own_in[z]
        share[ylen * (z + 1) - TILE : ylen * (z + 1)] += rising * last[z : z + 1]
        here = sends[0, REACH * z : REACH * (z + 1)]
        ups += [here[r : r + 1] + float(REACH - r) * last[z : z + 1] for r in range(REACH)]
        downs.append(sends[1, REACH * z : REACH * (z + 1)])
    share[ylen * inner : ylen * zlen] = spread_x(spread_y(quotient, ylen))
    ahead, back = to_neighbours(quotient, ylen)
    ends = spread_x(jnp.concatenate(ahead + back + [zeros[:2]], axis=0))
    share[ylen * zlen :] = jnp.concatenate(ups + [ends[:REACH]] + downs + [ends[REACH : 2 * REACH]], axis=0)


def corner_line(shape, corner, y_in, d_in):
    loads, comps, zlen, ylen, xlen = shape
    planes = loads * comps
    first_core = on_first()
    top = first_core & (lax.axis_index("sz") == lax.axis_size("sz") - 1)
    more = lax.axis_index("sy") < lax.axis_size("sy") - 1
    rows = []
    for k in range(planes):
        at = (k % comps * loads + k // comps) * zlen
        rows.append(jnp.where(first_core, y_in[at + zlen - 1 : at + zlen], y_in[at : at + 1]))
    rows.append(jnp.zeros((-planes % TILE, xlen), jnp.float32))
    stays_next = split_x(jnp.where(more, jnp.concatenate(rows, axis=0), 0.0))
    comes_next = split_x(jnp.where(more, d_in[...], 0.0))

    def faces(stays, comes, comp):
        zero = jnp.zeros((1, xlen), jnp.float32)
        under, over = [], []
        for own, other in zip(stays, comes):
            own, other = ([value[case * comps + comp : case * comps + comp + 1] for case in range(loads)] for value in (own, other))
            low = [jnp.where(first_core, a, b) for a, b in zip(own, other)] + [jnp.where(top, b, 0.0) for b in other]
            high = [jnp.where(first_core, jnp.where(top, 0.0, b), a) for a, b in zip(own, other)] + [zero] * loads
            under.append(jnp.concatenate(low, axis=0))
            over.append(jnp.concatenate(high, axis=0))
        return under, over

    low, high = [], []
    for comp in range(comps):
        near = faces((corner[0], corner[1]), (corner[2], corner[3]), comp)
        far = faces(stays_next, comes_next, comp)
        for (whole, change), (whole_next, change_next), into in zip(near, far, (low, high)):
            into.append((whole + whole_next, change + change_next, whole_next - whole, change_next - change))
    energy = quadratic(low, high, mode_weights())
    line = sum(energy[case : case + 1] for case in range(2 * loads)) * corner[0, planes : planes + 1]
    return spread_x(jnp.concatenate([line, jnp.zeros((TILE - 1, xlen), jnp.float32)], axis=0))[:1]


def corner_kernel(shape, share_in, corner, y_in, d_in, share):
    _, _, zlen, ylen, xlen = shape
    line = corner_line(shape, corner, y_in, d_in)
    rising = jnp.maximum(lax.broadcasted_iota(jnp.int32, (TILE, xlen), 0) - (TILE - 1 - ROWS), 0).astype(jnp.float32)
    falling = (REACH - lax.broadcasted_iota(jnp.int32, (REACH, xlen), 0)).astype(jnp.float32)
    share[...] = share_in[...]
    share[ylen * zlen - TILE : ylen * zlen] += rising * line
    share[ylen * zlen + REACH * (zlen - 1) : ylen * zlen + REACH * zlen] += falling * line


def total_kernel(shape, share, other, h_out, z_out, y_out, d_out, e_out):
    _, _, zlen, ylen, xlen = shape
    first_core = on_first()
    inner, rows = zlen - 1, ylen * zlen
    reach = REACH * zlen

    def layers(first, count):
        mine, theirs = share[first + inner * count : first + zlen * count], other[first + inner * count : first + zlen * count]
        middle = share[first : first + inner * count] + other[first : first + inner * count]
        return jnp.where(first_core, theirs, mine), middle, jnp.where(first_core, mine, theirs)

    lowest, middle, highest = layers(0, ylen)
    h_out[0] = lowest
    for z in range(inner):
        h_out[z + 1] = middle[ylen * z : ylen * (z + 1)]
    h_out[zlen] = highest
    z_out[...] = h_out[pl.ds(jnp.where(first_core, 0, 1), zlen)]
    ups = jnp.concatenate(layers(rows, REACH), axis=0)
    downs = jnp.concatenate(layers(rows + reach, REACH), axis=0)
    y_out[: reach + REACH] = jnp.where(first_core, downs, ups)
    for out, used in ((y_out, reach + REACH), (d_out, reach), (e_out, reach)):
        out[used:] = jnp.zeros((out.shape[0] - used, xlen), jnp.float32)
    d_out[:reach] = jnp.where(first_core, downs[:reach], ups[REACH:])
    e_out[:reach] = jnp.where(first_core, ups[:reach], downs[REACH:])


def layers_kernel(h, d_in, e_in, y_in, z_in, out):
    zlen, ylen, xlen = out.shape
    reach = REACH * zlen
    first_core = on_first()
    z_index, z_last = lax.axis_index("sz"), lax.axis_size("sz") - 1
    y_index, y_last = lax.axis_index("sy"), lax.axis_size("sy") - 1
    z_side = jnp.where(first_core, z_index < z_last, z_index > 0)
    y_side = jnp.where(first_core, y_index < y_last, y_index > 0)
    y_other = jnp.where(first_core, y_index > 0, y_index < y_last)
    blank = jnp.zeros((TILE - REACH, xlen), jnp.float32)

    def at_start(rows):
        return jnp.concatenate([rows, blank], axis=0)

    def at_end(rows):
        return jnp.concatenate([blank, rows], axis=0)

    def ends(rows, keep, at_last):
        rows = jnp.where(keep, rows, 0.0)
        return at_start(jnp.where(at_last, 0.0, rows)), at_end(jnp.where(at_last, rows, 0.0))

    def with_ends(layer, *pairs):
        head, tail = layer[:TILE], layer[ylen - TILE :]
        for first, last in pairs:
            head, tail = head + first, tail + last
        return jnp.concatenate([head, layer[TILE : ylen - TILE], tail] if ylen > 2 * TILE else [head, tail], axis=0)

    own = []
    for k in range(zlen + 1):
        layer = jnp.where(first_core, h[k], 0.0)
        own.append(with_ends(layer, ends(y_in[REACH * k : REACH * (k + 1)], y_side, first_core)))
    come = []
    for k in range(zlen):
        part = slice(REACH * k, REACH * (k + 1))
        layer = jnp.where(z_side, z_in[k], 0.0)
        straight = ends(d_in[part], z_side & y_side, first_core)
        across = ends(e_in[part], z_side & y_other, jnp.logical_not(first_core))
        come.append(with_ends(layer, straight, across))
    below = [jnp.where(first_core, 0.0, layer) for layer in come[zlen - REACH :]]
    above = [jnp.where(first_core, layer, 0.0) for layer in come]
    layers = below[:-1] + [below[-1] + own[0]] + own[1:-1] + [own[-1] + above[0]] + above[1:]
    for z, layer in enumerate(spread_layers(layers)):
        out[z] = layer


def sum_kernel(part, other, out):
    out[...] = part[...] + other[...]


def call(kernel, outs, args, scratch=(), space=pltpu.VMEM):
    shapes = [jax.ShapeDtypeStruct(out, jnp.float32) if isinstance(out, tuple) else out for out in outs]
    return pl.pallas_call(
        kernel,
        out_shape=shapes,
        in_specs=[pl.BlockSpec(memory_space=space)] * len(args),
        out_specs=[pl.BlockSpec(memory_space=pltpu.VMEM)] * len(outs),
        scratch_shapes=list(scratch),
        compiler_params=pltpu.CompilerParams(vmem_limit_bytes=32 * 1024 * 1024),
    )(*args)


def ring_moved(value, axis):
    size = lax.axis_size(axis)
    return lax.ppermute(value, axis, [((k + 1) % size, k) for k in range(size)])


def chip_swapped(value):
    cores = lax.axis_size("load")
    return lax.ppermute(value, "load", [(core, cores - 1 - core) for core in range(cores)])


def opposed(value, z_step, y_step, y_shift=0):
    cores, rows, size = lax.axis_size("load"), lax.axis_size("sy"), lax.axis_size("sz")
    pairs = []
    for core in range(cores):
        sign = -1 if core else 1
        for y in range(rows):
            for z in range(size):
                to_y, to_z, side = y + sign * y_step, z + sign * z_step, core
                if not (0 <= to_y < rows and 0 <= to_z < size):
                    to_y, to_z, side = y, z, cores - 1 - core
                to_y = (to_y + y_shift) % rows
                pairs.append(((core * rows + y) * size + z, (side * rows + to_y) * size + to_z))
    return lax.ppermute(value, ("load", "sy", "sz"), pairs)


def body(displacements, density, solid, fixed):
    loads, comps, zlen, ylen, xlen = displacements.shape
    planes = loads * comps
    totals = (zlen * lax.axis_size("sz"), ylen * lax.axis_size("sy"))
    args = [
        pltpu.with_memory_space_constraint(arg, pltpu.HBM) for arg in (displacements, fixed, density, solid)
    ]

    d_send, z_send, y_send = call(
        lambda *refs: lead_kernel(totals, *refs),
        [(-(-planes // TILE) * TILE, xlen), (planes + 1, ylen, xlen), (planes * zlen, xlen)],
        args,
        scratch=[
            pltpu.VMEM((loads, comps, ylen, xlen), jnp.float32),
            pltpu.VMEM((ylen, xlen), jnp.int32),
            pltpu.VMEM((ylen, xlen), jnp.float32),
            pltpu.VMEM((ylen, xlen), jnp.int32),
            pltpu.VMEM((loads, comps, zlen, 1, xlen), jnp.float32),
            pltpu.VMEM((zlen, 1, xlen), jnp.int32),
            pltpu.SemaphoreType.DMA((6,)),
        ],
        space=pltpu.HBM,
    )
    d_in = opposed(d_send, -1, 0, y_shift=-1)
    z_in = opposed(z_send, -1, 0)
    y_in = ring_moved(y_send, "sy")
    nodes = lambda layers: pltpu.VMEM((planes, layers, ylen + TILE, xlen), jnp.float32)
    inner = call(
        lambda *refs: inner_kernel(totals, *refs),
        [
            (zlen, ylen, xlen),
            (2, planes * zlen, xlen),
            (2, REACH * (zlen - 1), xlen),
            (planes, ylen, xlen),
            (planes, ylen, xlen),
            (ylen, xlen),
            (TILE, xlen),
        ],
        (displacements, fixed, density, solid),
        scratch=[nodes(zlen), nodes(zlen), pltpu.VMEM((zlen - 1, ylen + 2 * TILE, xlen), jnp.float32)],
    )
    reach = REACH * zlen
    shape = displacements.shape
    share, corner = call(
        lambda *refs: outer_kernel(shape, *refs),
        [(ylen * zlen + 2 * reach, xlen), (4, -(-(planes + 1) // TILE) * TILE, xlen)],
        (z_in, y_in, *inner),
        scratch=[
            nodes(4),
            nodes(4),
            pltpu.VMEM((ylen + 2 * TILE, xlen), jnp.float32),
            pltpu.VMEM((ylen, xlen), jnp.float32),
        ],
    )
    (share,) = call(
        lambda *refs: corner_kernel(shape, *refs), [(ylen * zlen + 2 * reach, xlen)], (share, corner, y_in, d_in)
    )
    sent = (-(-(reach + REACH) // TILE) * TILE, xlen)
    h, z_send, y_send, d_send, e_send = call(
        lambda *refs: total_kernel(displacements.shape, *refs),
        [
            (zlen + 1, ylen, xlen),
            (zlen, ylen, xlen),
            sent,
            sent,
            sent,
        ],
        (share, chip_swapped(share)),
    )
    d_in = opposed(d_send, -1, -1)
    e_in = opposed(e_send, -1, 1)
    y_in = opposed(y_send, 0, -1)
    z_in = opposed(z_send, -1, 0)
    (part,) = call(layers_kernel, [(zlen, ylen, xlen)], (h, d_in, e_in, y_in, z_in))
    (out,) = call(sum_kernel, [(zlen, ylen, xlen)], (part, chip_swapped(part)))
    return out


def solution(mesh):
    return jax.shard_map(
        body,
        mesh=mesh,
        in_specs=(
            P("load", None, "sz", "sy", None),
            P("sz", "sy", None),
            P("sz", "sy", None),
            P("sz", "sy", None),
        ),
        out_specs=P("sz", "sy", None),
        check_vma=False,
    )
```

```python
import jax
import jax.numpy as jnp
import numpy as np
from jax import lax
from jax.experimental import pallas as pl
from jax.experimental.pallas import tpu as pltpu
from jax.sharding import PartitionSpec as P

OFFSETS = [(0, 0, 0), (1, 0, 0), (1, 1, 0), (0, 1, 0), (0, 0, 1), (1, 0, 1), (1, 1, 1), (0, 1, 1)]
REACH = 3
ROWS = REACH + 1
TILE = 8
LANES = 128


def element_matrix():
    corners = np.array(
        [
            [-1.0, -1.0, -1.0],
            [1.0, -1.0, -1.0],
            [1.0, 1.0, -1.0],
            [-1.0, 1.0, -1.0],
            [-1.0, -1.0, 1.0],
            [1.0, -1.0, 1.0],
            [1.0, 1.0, 1.0],
            [-1.0, 1.0, 1.0],
        ]
    )
    poisson = 0.3
    lame = poisson / ((1.0 + poisson) * (1.0 - 2.0 * poisson))
    shear = 1.0 / (2.0 * (1.0 + poisson))
    elastic = np.zeros((6, 6))
    elastic[:3, :3] = lame
    for k in range(3):
        elastic[k, k] += 2.0 * shear
        elastic[3 + k, 3 + k] = shear
    gauss = 1.0 / np.sqrt(3.0)
    stiffness = np.zeros((24, 24))
    for gi in range(2):
        for gj in range(2):
            for gk in range(2):
                point = np.array([(2 * gi - 1) * gauss, (2 * gj - 1) * gauss, (2 * gk - 1) * gauss])
                strain = np.zeros((6, 24))
                for node in range(8):
                    grads = np.zeros(3)
                    for k in range(3):
                        value = corners[node, k] / 8.0
                        for m in range(3):
                            if m != k:
                                value = value * (1.0 + point[m] * corners[node, m])
                        grads[k] = 2.0 * value
                    col = 3 * node
                    strain[0, col] = grads[0]
                    strain[1, col + 1] = grads[1]
                    strain[2, col + 2] = grads[2]
                    strain[3, col] = grads[1]
                    strain[3, col + 1] = grads[0]
                    strain[4, col + 1] = grads[2]
                    strain[4, col + 2] = grads[1]
                    strain[5, col] = grads[2]
                    strain[5, col + 2] = grads[0]
                stiffness += strain.T @ elastic @ strain / 8.0
    return stiffness


def mode_weights():
    modes = [(i, j, k) for k in (0, 1) for j in (0, 1) for i in (0, 1)]
    sums = np.zeros((24, 24))
    for m, mode in enumerate(modes):
        for n, corner in enumerate(OFFSETS):
            sign = np.prod([(1 if corner[d] else -1) if mode[d] else 1 for d in range(3)])
            for comp in range(3):
                sums[3 * m + comp, 3 * n + comp] = sign
    form = sums @ element_matrix() @ sums.T / 64.0

    def at(first, second):
        return form[3 * modes.index(first[1]) + first[0], 3 * modes.index(second[1]) + second[0]]

    ux, vy, uy = (0, (1, 0, 0)), (1, (0, 1, 0)), (0, (0, 1, 0))
    uxy, wyz = (0, (1, 1, 0)), (2, (0, 1, 1))
    wxy, vxz, uxyz = (2, (1, 1, 0)), (1, (1, 0, 1)), (0, (1, 1, 1))
    return dict(
        normal=at(ux, ux) - at(ux, vy),
        trace=at(ux, vy),
        shear=at(uy, uy),
        plus=(at(uxy, uxy) + at(uxy, wyz)) / 2,
        minus=(at(uxy, uxy) - at(uxy, wyz)) / 2,
        twist=at(wxy, wxy) - at(wxy, vxz),
        twist_sum=at(wxy, vxz),
        corner=at(uxyz, uxyz),
    )


def square(value):
    return value * value


def quadratic(low, high, weights):
    x = [low[c][1] + high[c][1] for c in range(3)]
    y = [low[c][2] + high[c][2] for c in range(3)]
    z = [high[c][0] - low[c][0] for c in range(3)]
    xy = [low[c][3] + high[c][3] for c in range(3)]
    xz = [high[c][1] - low[c][1] for c in range(3)]
    yz = [high[c][2] - low[c][2] for c in range(3)]
    xyz = [high[c][3] - low[c][3] for c in range(3)]
    normal = square(x[0]) + square(y[1]) + square(z[2])
    trace = square(x[0] + y[1] + z[2])
    shear = square(y[0] + x[1]) + square(z[0] + x[2]) + square(z[1] + y[2])
    pairs = ((xy[0], yz[2]), (xy[1], xz[2]), (xz[0], yz[1]))
    plus = sum(square(p + q) for p, q in pairs)
    minus = sum(square(p - q) for p, q in pairs)
    twist = square(xy[2]) + square(xz[1]) + square(yz[0])
    twist_sum = square(xy[2] + xz[1] + yz[0])
    corner = square(xyz[0]) + square(xyz[1]) + square(xyz[2])
    groups = dict(
        normal=normal, trace=trace, shear=shear, plus=plus, minus=minus, twist=twist, twist_sum=twist_sum, corner=corner
    )
    return sum(np.float32(weights[name]) * group for name, group in groups.items())


def line_weight(coord, count):
    def outside(distance):
        missing = jnp.maximum(REACH - distance, 0)
        return missing * (missing + 1) // 2

    whole = (REACH + 1) * (REACH + 1)
    return (whole - outside(coord) - outside(count - 1 - coord)).astype(jnp.float32)


def voxel_factor(density, solid, plane, first_row, total_z, total_y):
    rows, length = density.shape
    row = lax.broadcasted_iota(jnp.int32, (rows, length), 0) + first_row
    column = lax.broadcasted_iota(jnp.int32, (rows, length), 1)
    weight = line_weight(row, total_y) * line_weight(column, length)
    weight = weight * line_weight(jnp.full((rows, length), plane, jnp.int32), total_z)
    return solid.astype(jnp.float32) * (-3.0 * density * density) / weight


def spread_x(value):
    rows, length = value.shape
    wide = jnp.concatenate([value, jnp.zeros((rows, LANES), jnp.float32)], axis=1)
    span = length + LANES
    total = float(ROWS) * value
    for step in range(1, ROWS):
        both = pltpu.roll(wide, span - step, 1) + pltpu.roll(wide, step, 1)
        total = total + float(ROWS - step) * both[:, :length]
    return total


def spread_layers(layers):
    for step in (1, 2, 1, 2):
        layers = [layers[k] + layers[k + step] for k in range(len(layers) - step)]
    return layers


def held(disp, fixed, case, comp, z, rows):
    return disp[case, comp, z, rows] * (1.0 - fixed[z, rows].astype(jnp.float32))


def split_x(value):
    length = value.shape[1]
    column = lax.broadcasted_iota(jnp.int32, value.shape, 1)
    ahead = jnp.where(column == length - 1, 0.0, pltpu.roll(value, length - 1, 1))
    return value + ahead, ahead - value


def spread_y(quotient, ylen):
    rows = [quotient[TILE + step : TILE + step + ylen] for step in range(-REACH, REACH + 1)]
    return sum((ROWS - abs(k - REACH)) * rows[k] for k in range(2 * REACH + 1))


def to_neighbours(quotient, ylen):
    top = quotient[ylen : ylen + TILE]
    base = quotient[TILE : 2 * TILE]
    ahead, back = [], []
    for row in range(REACH):
        ahead.append(sum(float(REACH - row - k) * top[TILE - 1 - k : TILE - k] for k in range(REACH - row)))
        back.append(sum(float(row + 1 - k) * base[k : k + 1] for k in range(row + 1)))
    return ahead, back


def next_is_partner(start):
    return (lax.axis_index("sy") - start) % 2 == 0


def on_first():
    return lax.axis_index("load") == 0


def lead_kernel(totals, disp_hbm, fixed_hbm, density_hbm, solid_hbm, d_out, z_out, y_out, layer, layer_fixed, density, solid, rows, rows_fixed, sems):
    loads, comps, zlen, ylen, _ = disp_hbm.shape
    gives = jnp.where(on_first(), 0, zlen - 1)
    copies = [
        pltpu.make_async_copy(source, target, sems.at[k])
        for k, (source, target) in enumerate(
            (
                (density_hbm.at[gives], density),
                (solid_hbm.at[gives], solid),
                (fixed_hbm.at[gives], layer_fixed),
                (disp_hbm.at[:, :, gives], layer),
                (fixed_hbm.at[:, :1], rows_fixed),
                (disp_hbm.at[:, :, :, :1], rows),
            )
        )
    ]
    for copy in copies:
        copy.start()
    for copy in copies[:2]:
        copy.wait()
    plane = lax.axis_index("sz") * zlen + gives
    base_y = lax.axis_index("sy") * ylen
    d_out[...] = jnp.zeros(d_out.shape, jnp.float32)
    z_out[loads * comps] = voxel_factor(density[...], solid[...], plane, base_y, *totals)
    for copy in copies[2:4]:
        copy.wait()
    free = 1.0 - layer_fixed[...].astype(jnp.float32)
    for case in range(loads):
        for comp in range(comps):
            k = case * comps + comp
            z_out[k] = layer[case, comp] * free
            d_out[k : k + 1] = z_out[k, :1]
    for copy in copies[4:]:
        copy.wait()
    for z in range(zlen):
        free = 1.0 - rows_fixed[z, :1].astype(jnp.float32)
        for case in range(loads):
            for comp in range(comps):
                at = (comp * loads + case) * zlen + z
                y_out[at : at + 1] = rows[case, comp, z, :1] * free


def tile_energies(plus, diff, first, lanes, layers, loads, comps, base=0):
    weights = mode_weights()

    def faces(k, z):
        near, far = slice(first, first + TILE), slice(first + 1, first + TILE + 1)
        whole, whole_next = plus[k, z, near, lanes], plus[k, z, far, lanes]
        change, change_next = diff[k, z, near, lanes], diff[k, z, far, lanes]
        return whole + whole_next, change + change_next, whole_next - whole, change_next - change

    energy = [None] * layers
    for case in range(loads):
        low = None
        for z in range(layers + 1):
            high = [faces(case * comps + comp, base + z) for comp in range(comps)]
            if low is not None:
                part = quadratic(low, high, weights)
                energy[z - 1] = part if energy[z - 1] is None else energy[z - 1] + part
            low = high
    return energy


def blank_last(value, first, ylen):
    row = lax.broadcasted_iota(jnp.int32, value.shape, 0) + first
    return jnp.where(row == ylen - 1, 0.0, value)


def inner_kernel(totals, disp, fixed, density, solid, own, line, sends, last_plus, last_diff, last_factor, edge, plus, diff, quotient):
    loads, comps, zlen, ylen, xlen = disp.shape
    total_z, total_y = totals
    base_z = lax.axis_index("sz") * zlen
    base_y = lax.axis_index("sy") * ylen
    inner = zlen - 1
    keeps = jnp.where(on_first(), inner, 0)
    free = [1.0 - fixed[z].astype(jnp.float32) for z in range(zlen)]

    @pl.loop(0, loads * comps, unroll=True)
    def _(k):
        case, comp = k // comps, k % comps
        for z in range(zlen):
            whole, change = split_x(disp[case, comp, z] * free[z])
            plus[k, z, :ylen] = whole
            diff[k, z, :ylen] = change
        last_plus[k] = plus[k, keeps, :ylen]
        last_diff[k] = diff[k, keeps, :ylen]

    for comp in range(comps):
        for case in range(loads):
            for z in range(zlen):
                at = (comp * loads + case) * zlen + z
                line[0, at : at + 1] = plus[case * comps + comp, z, ylen - 1 : ylen]
                line[1, at : at + 1] = diff[case * comps + comp, z, ylen - 1 : ylen]

    zeros = jnp.zeros((TILE, xlen), jnp.float32)
    edge[...] = jnp.zeros(edge.shape, jnp.float32)
    for z in range(zlen):
        factor = voxel_factor(density[z], solid[z], base_z + z, base_y, total_z, total_y)
        edge[z : z + 1] = factor[ylen - 1 :]
        if z == inner:
            last_factor[...] = factor
        else:
            quotient[z, :TILE] = zeros
            quotient[z, TILE : TILE + ylen] = factor
            quotient[z, TILE + ylen :] = zeros

    for first in range(0, ylen, TILE):

        @pl.loop(0, xlen // LANES, unroll=True)
        def _(chunk):
            lanes = pl.ds(pl.multiple_of(chunk * LANES, LANES), LANES)
            energy = tile_energies(plus, diff, first, lanes, inner, loads, comps)
            for z in range(inner):
                here = quotient[z, first + TILE : first + 2 * TILE, lanes]
                quotient[z, first + TILE : first + 2 * TILE, lanes] = blank_last(energy[z] * here, first, ylen)

    for z in range(inner):
        own[z] = spread_x(spread_y(quotient.at[z], ylen))
        ahead, back = to_neighbours(quotient.at[z], ylen)
        ends = spread_x(jnp.concatenate(ahead + back + [zeros[:2]], axis=0))
        sends[0, REACH * z : REACH * (z + 1)] = ends[:REACH]
        sends[1, REACH * z : REACH * (z + 1)] = ends[REACH : 2 * REACH]


def outer_kernel(
    shape, z_in, y_in, own_in, line, sends, last_plus, last_diff, last_factor, edge, share, corner, plus, diff, quotient, factor
):
    loads, comps, zlen, ylen, xlen = shape
    planes = loads * comps
    inner = zlen - 1
    first_core, index = on_first(), lax.axis_index("sz")
    top = first_core & (index == lax.axis_size("sz") - 1)
    more = lax.axis_index("sy") < lax.axis_size("sy") - 1
    stays, comes = jnp.where(first_core, 0, 1), jnp.where(first_core, jnp.where(top, 2, 1), 0)
    y_plus, y_diff = split_x(jnp.where(more, y_in[...], 0.0))
    for k in range(planes):
        plus[k, stays, :ylen] = last_plus[k]
        diff[k, stays, :ylen] = last_diff[k]
        whole, change = split_x(z_in[k])
        plus[k, comes, :ylen] = whole
        diff[k, comes, :ylen] = change
        for group, value in enumerate((last_plus[k, ylen - 1 :], last_diff[k, ylen - 1 :], whole[ylen - 1 :], change[ylen - 1 :])):
            corner[group, k : k + 1] = value
    below = jnp.where(index > 0, z_in[planes], 0.0)
    factor[...] = jnp.where(first_core, last_factor[...], below)
    corner[0, planes : planes + 1] = factor[ylen - 1 :]

    @pl.when(top)
    def _():
        clamped = jnp.zeros((ylen + TILE, xlen), jnp.float32)
        for k in range(planes):
            for slot in (1, 3):
                plus[k, slot] = clamped
                diff[k, slot] = clamped

    zeros = jnp.zeros((TILE, xlen), jnp.float32)
    quotient[:TILE] = zeros
    quotient[TILE + ylen :] = zeros
    for first in range(0, ylen, TILE):

        @pl.loop(0, xlen // LANES, unroll=True)
        def _(chunk):
            lanes = pl.ds(pl.multiple_of(chunk * LANES, LANES), LANES)
            (energy,) = tile_energies(plus, diff, first, lanes, 1, loads, comps)
            here = energy * factor[first : first + TILE, lanes]
            quotient[first + TILE : first + 2 * TILE, lanes] = blank_last(here, first, ylen)

    @pl.when(top)
    def _():
        for first in range(0, ylen, TILE):

            @pl.loop(0, xlen // LANES, unroll=True)
            def _(chunk):
                lanes = pl.ds(pl.multiple_of(chunk * LANES, LANES), LANES)
                (energy,) = tile_energies(plus, diff, first, lanes, 1, loads, comps, base=2)
                here = energy * factor[first : first + TILE, lanes]
                quotient[first + TILE : first + 2 * TILE, lanes] += blank_last(here, first, ylen)

    count = loads * zlen
    low, high = [], []
    for comp in range(comps):
        part = slice(comp * count, (comp + 1) * count)
        whole, change = line[0, part], line[1, part]
        whole_next, change_next = y_plus[part], y_diff[part]
        face = (whole + whole_next, change + change_next, whole_next - whole, change_next - change)
        low.append(face)
        high.append([pltpu.roll(value, count - 1, 0) for value in face])
    energy = quadratic(low, high, mode_weights())
    energy = sum(energy[case * zlen : case * zlen + inner] for case in range(loads)) * edge[:inner]
    last = spread_x(jnp.concatenate([energy, jnp.zeros((TILE - inner, xlen), jnp.float32)], axis=0))

    row = lax.broadcasted_iota(jnp.int32, (TILE, xlen), 0)
    rising = jnp.maximum(row - (TILE - 1 - ROWS), 0).astype(jnp.float32)
    ups, downs = [], []
    for z in range(inner):
        share[ylen * z : ylen * (z + 1)] = own_in[z]
        share[ylen * (z + 1) - TILE : ylen * (z + 1)] += rising * last[z : z + 1]
        here = sends[0, REACH * z : REACH * (z + 1)]
        ups += [here[r : r + 1] + float(REACH - r) * last[z : z + 1] for r in range(REACH)]
        downs.append(sends[1, REACH * z : REACH * (z + 1)])
    share[ylen * inner : ylen * zlen] = spread_x(spread_y(quotient, ylen))
    ahead, back = to_neighbours(quotient, ylen)
    ends = spread_x(jnp.concatenate(ahead + back + [zeros[:2]], axis=0))
    share[ylen * zlen :] = jnp.concatenate(ups + [ends[:REACH]] + downs + [ends[REACH : 2 * REACH]], axis=0)


def corner_line(shape, corner, y_in, d_in):
    loads, comps, zlen, ylen, xlen = shape
    planes = loads * comps
    first_core = on_first()
    top = first_core & (lax.axis_index("sz") == lax.axis_size("sz") - 1)
    more = lax.axis_index("sy") < lax.axis_size("sy") - 1
    rows = []
    for k in range(planes):
        at = (k % comps * loads + k // comps) * zlen
        rows.append(jnp.where(first_core, y_in[at + zlen - 1 : at + zlen], y_in[at : at + 1]))
    rows.append(jnp.zeros((-planes % TILE, xlen), jnp.float32))
    stays_next = split_x(jnp.where(more, jnp.concatenate(rows, axis=0), 0.0))
    comes_next = split_x(jnp.where(more, d_in[...], 0.0))

    def faces(stays, comes, comp):
        zero = jnp.zeros((1, xlen), jnp.float32)
        under, over = [], []
        for own, other in zip(stays, comes):
            own, other = ([value[case * comps + comp : case * comps + comp + 1] for case in range(loads)] for value in (own, other))
            low = [jnp.where(first_core, a, b) for a, b in zip(own, other)] + [jnp.where(top, b, 0.0) for b in other]
            high = [jnp.where(first_core, jnp.where(top, 0.0, b), a) for a, b in zip(own, other)] + [zero] * loads
            under.append(jnp.concatenate(low, axis=0))
            over.append(jnp.concatenate(high, axis=0))
        return under, over

    low, high = [], []
    for comp in range(comps):
        near = faces((corner[0], corner[1]), (corner[2], corner[3]), comp)
        far = faces(stays_next, comes_next, comp)
        for (whole, change), (whole_next, change_next), into in zip(near, far, (low, high)):
            into.append((whole + whole_next, change + change_next, whole_next - whole, change_next - change))
    energy = quadratic(low, high, mode_weights())
    line = sum(energy[case : case + 1] for case in range(2 * loads)) * corner[0, planes : planes + 1]
    return spread_x(jnp.concatenate([line, jnp.zeros((TILE - 1, xlen), jnp.float32)], axis=0))[:1]


def corner_kernel(shape, share_in, corner, y_in, d_in, share):
    _, _, zlen, ylen, xlen = shape
    line = corner_line(shape, corner, y_in, d_in)
    rising = jnp.maximum(lax.broadcasted_iota(jnp.int32, (TILE, xlen), 0) - (TILE - 1 - ROWS), 0).astype(jnp.float32)
    falling = (REACH - lax.broadcasted_iota(jnp.int32, (REACH, xlen), 0)).astype(jnp.float32)
    share[...] = share_in[...]
    share[ylen * zlen - TILE : ylen * zlen] += rising * line
    share[ylen * zlen + REACH * (zlen - 1) : ylen * zlen + REACH * zlen] += falling * line


def total_kernel(shape, share, other, h_out, z_out, y_out, d_out, e_out):
    _, _, zlen, ylen, xlen = shape
    first_core = on_first()
    inner, rows = zlen - 1, ylen * zlen
    reach = REACH * zlen

    def layers(first, count):
        mine, theirs = share[first + inner * count : first + zlen * count], other[first + inner * count : first + zlen * count]
        middle = share[first : first + inner * count] + other[first : first + inner * count]
        return jnp.where(first_core, theirs, mine), middle, jnp.where(first_core, mine, theirs)

    lowest, middle, highest = layers(0, ylen)
    h_out[0] = lowest
    for z in range(inner):
        h_out[z + 1] = middle[ylen * z : ylen * (z + 1)]
    h_out[zlen] = highest
    z_out[...] = h_out[pl.ds(jnp.where(first_core, 0, 1), zlen)]
    ups = jnp.concatenate(layers(rows, REACH), axis=0)
    downs = jnp.concatenate(layers(rows + reach, REACH), axis=0)
    y_out[: reach + REACH] = jnp.where(first_core, downs, ups)
    for out, used in ((y_out, reach + REACH), (d_out, reach), (e_out, reach)):
        out[used:] = jnp.zeros((out.shape[0] - used, xlen), jnp.float32)
    for out, start in ((d_out, 1), (e_out, 0)):
        rows = jnp.where(next_is_partner(start), ups, downs)
        out[:reach] = jnp.where(first_core, rows[:reach], rows[REACH:])


def layers_kernel(h, d_in, e_in, y_in, z_in, out):
    zlen, ylen, xlen = out.shape
    reach = REACH * zlen
    first_core = on_first()
    z_index, z_last = lax.axis_index("sz"), lax.axis_size("sz") - 1
    y_index, y_last = lax.axis_index("sy"), lax.axis_size("sy") - 1
    z_side = jnp.where(first_core, z_index < z_last, z_index > 0)
    y_side = jnp.where(first_core, y_index < y_last, y_index > 0)
    d_next, e_next = next_is_partner(1), next_is_partner(0)
    d_side, e_side = (jnp.where(up, y_index < y_last, y_index > 0) for up in (d_next, e_next))
    blank = jnp.zeros((TILE - REACH, xlen), jnp.float32)

    def at_start(rows):
        return jnp.concatenate([rows, blank], axis=0)

    def at_end(rows):
        return jnp.concatenate([blank, rows], axis=0)

    def ends(rows, keep, at_last):
        rows = jnp.where(keep, rows, 0.0)
        return at_start(jnp.where(at_last, 0.0, rows)), at_end(jnp.where(at_last, rows, 0.0))

    def with_ends(layer, *pairs):
        head, tail = layer[:TILE], layer[ylen - TILE :]
        for first, last in pairs:
            head, tail = head + first, tail + last
        return jnp.concatenate([head, layer[TILE : ylen - TILE], tail] if ylen > 2 * TILE else [head, tail], axis=0)

    own = []
    for k in range(zlen + 1):
        layer = jnp.where(first_core, h[k], 0.0)
        own.append(with_ends(layer, ends(y_in[REACH * k : REACH * (k + 1)], y_side, first_core)))
    come = []
    for k in range(zlen):
        part = slice(REACH * k, REACH * (k + 1))
        layer = jnp.where(z_side, z_in[k], 0.0)
        come.append(with_ends(layer, ends(d_in[part], z_side & d_side, d_next), ends(e_in[part], z_side & e_side, e_next)))
    below = [jnp.where(first_core, 0.0, layer) for layer in come[zlen - REACH :]]
    above = [jnp.where(first_core, layer, 0.0) for layer in come]
    layers = below[:-1] + [below[-1] + own[0]] + own[1:-1] + [own[-1] + above[0]] + above[1:]
    for z, layer in enumerate(spread_layers(layers)):
        out[z] = layer


def sum_kernel(part, other, out):
    out[...] = part[...] + other[...]


def call(kernel, outs, args, scratch=(), space=pltpu.VMEM):
    shapes = [jax.ShapeDtypeStruct(out, jnp.float32) if isinstance(out, tuple) else out for out in outs]
    return pl.pallas_call(
        kernel,
        out_shape=shapes,
        in_specs=[pl.BlockSpec(memory_space=space)] * len(args),
        out_specs=[pl.BlockSpec(memory_space=pltpu.VMEM)] * len(outs),
        scratch_shapes=list(scratch),
        compiler_params=pltpu.CompilerParams(vmem_limit_bytes=32 * 1024 * 1024),
    )(*args)


def ring_moved(value, axis):
    size = lax.axis_size(axis)
    return lax.ppermute(value, axis, [((k + 1) % size, k) for k in range(size)])


def chip_swapped(value):
    cores = lax.axis_size("load")
    return lax.ppermute(value, "load", [(core, cores - 1 - core) for core in range(cores)])


def opposed(value, z_step, y_step, y_shift=0, start=None):
    cores, rows, size = lax.axis_size("load"), lax.axis_size("sy"), lax.axis_size("sz")
    pairs = []
    for core in range(cores):
        sign = -1 if core else 1
        for y in range(rows):
            for z in range(size):
                to_y, to_z, side = y + sign * y_step, z + sign * z_step, core
                if start is not None:
                    to_y = y + 1 if (y - start) % 2 == 0 else y - 1
                if not (0 <= to_y < rows and 0 <= to_z < size):
                    to_y, to_z, side = y, z, cores - 1 - core
                to_y = (to_y + y_shift) % rows
                pairs.append(((core * rows + y) * size + z, (side * rows + to_y) * size + to_z))
    return lax.ppermute(value, ("load", "sy", "sz"), pairs)


def body(displacements, density, solid, fixed):
    loads, comps, zlen, ylen, xlen = displacements.shape
    planes = loads * comps
    totals = (zlen * lax.axis_size("sz"), ylen * lax.axis_size("sy"))
    args = [
        pltpu.with_memory_space_constraint(arg, pltpu.HBM) for arg in (displacements, fixed, density, solid)
    ]

    d_send, z_send, y_send = call(
        lambda *refs: lead_kernel(totals, *refs),
        [(-(-planes // TILE) * TILE, xlen), (planes + 1, ylen, xlen), (planes * zlen, xlen)],
        args,
        scratch=[
            pltpu.VMEM((loads, comps, ylen, xlen), jnp.float32),
            pltpu.VMEM((ylen, xlen), jnp.int32),
            pltpu.VMEM((ylen, xlen), jnp.float32),
            pltpu.VMEM((ylen, xlen), jnp.int32),
            pltpu.VMEM((loads, comps, zlen, 1, xlen), jnp.float32),
            pltpu.VMEM((zlen, 1, xlen), jnp.int32),
            pltpu.SemaphoreType.DMA((6,)),
        ],
        space=pltpu.HBM,
    )
    d_in = opposed(d_send, -1, 0, y_shift=-1)
    z_in = opposed(z_send, -1, 0)
    y_in = ring_moved(y_send, "sy")
    nodes = lambda layers: pltpu.VMEM((planes, layers, ylen + TILE, xlen), jnp.float32)
    inner = call(
        lambda *refs: inner_kernel(totals, *refs),
        [
            (zlen, ylen, xlen),
            (2, planes * zlen, xlen),
            (2, REACH * (zlen - 1), xlen),
            (planes, ylen, xlen),
            (planes, ylen, xlen),
            (ylen, xlen),
            (TILE, xlen),
        ],
        (displacements, fixed, density, solid),
        scratch=[nodes(zlen), nodes(zlen), pltpu.VMEM((zlen - 1, ylen + 2 * TILE, xlen), jnp.float32)],
    )
    reach = REACH * zlen
    shape = displacements.shape
    share, corner = call(
        lambda *refs: outer_kernel(shape, *refs),
        [(ylen * zlen + 2 * reach, xlen), (4, -(-(planes + 1) // TILE) * TILE, xlen)],
        (z_in, y_in, *inner),
        scratch=[
            nodes(4),
            nodes(4),
            pltpu.VMEM((ylen + 2 * TILE, xlen), jnp.float32),
            pltpu.VMEM((ylen, xlen), jnp.float32),
        ],
    )
    (share,) = call(
        lambda *refs: corner_kernel(shape, *refs), [(ylen * zlen + 2 * reach, xlen)], (share, corner, y_in, d_in)
    )
    sent = (-(-(reach + REACH) // TILE) * TILE, xlen)
    h, z_send, y_send, d_send, e_send = call(
        lambda *refs: total_kernel(displacements.shape, *refs),
        [
            (zlen + 1, ylen, xlen),
            (zlen, ylen, xlen),
            sent,
            sent,
            sent,
        ],
        (share, chip_swapped(share)),
    )
    d_in = opposed(d_send, -1, 0, start=1)
    e_in = opposed(e_send, -1, 0, start=0)
    y_in = opposed(y_send, 0, -1)
    z_in = opposed(z_send, -1, 0)
    (part,) = call(layers_kernel, [(zlen, ylen, xlen)], (h, d_in, e_in, y_in, z_in))
    (out,) = call(sum_kernel, [(zlen, ylen, xlen)], (part, chip_swapped(part)))
    return out


def solution(mesh):
    return jax.shard_map(
        body,
        mesh=mesh,
        in_specs=(
            P("load", None, "sz", "sy", None),
            P("sz", "sy", None),
            P("sz", "sy", None),
            P("sz", "sy", None),
        ),
        out_specs=P("sz", "sy", None),
        check_vma=False,
    )
```

```python
import jax
import jax.numpy as jnp
import numpy as np
from jax import lax
from jax.experimental import pallas as pl
from jax.experimental.pallas import tpu as pltpu
from jax.sharding import PartitionSpec as P

OFFSETS = [(0, 0, 0), (1, 0, 0), (1, 1, 0), (0, 1, 0), (0, 0, 1), (1, 0, 1), (1, 1, 1), (0, 1, 1)]
REACH = 3
ROWS = REACH + 1
TILE = 8
LANES = 128


def element_matrix():
    corners = np.array(
        [
            [-1.0, -1.0, -1.0],
            [1.0, -1.0, -1.0],
            [1.0, 1.0, -1.0],
            [-1.0, 1.0, -1.0],
            [-1.0, -1.0, 1.0],
            [1.0, -1.0, 1.0],
            [1.0, 1.0, 1.0],
            [-1.0, 1.0, 1.0],
        ]
    )
    poisson = 0.3
    lame = poisson / ((1.0 + poisson) * (1.0 - 2.0 * poisson))
    shear = 1.0 / (2.0 * (1.0 + poisson))
    elastic = np.zeros((6, 6))
    elastic[:3, :3] = lame
    for k in range(3):
        elastic[k, k] += 2.0 * shear
        elastic[3 + k, 3 + k] = shear
    gauss = 1.0 / np.sqrt(3.0)
    stiffness = np.zeros((24, 24))
    for gi in range(2):
        for gj in range(2):
            for gk in range(2):
                point = np.array([(2 * gi - 1) * gauss, (2 * gj - 1) * gauss, (2 * gk - 1) * gauss])
                strain = np.zeros((6, 24))
                for node in range(8):
                    grads = np.zeros(3)
                    for k in range(3):
                        value = corners[node, k] / 8.0
                        for m in range(3):
                            if m != k:
                                value = value * (1.0 + point[m] * corners[node, m])
                        grads[k] = 2.0 * value
                    col = 3 * node
                    strain[0, col] = grads[0]
                    strain[1, col + 1] = grads[1]
                    strain[2, col + 2] = grads[2]
                    strain[3, col] = grads[1]
                    strain[3, col + 1] = grads[0]
                    strain[4, col + 1] = grads[2]
                    strain[4, col + 2] = grads[1]
                    strain[5, col] = grads[2]
                    strain[5, col + 2] = grads[0]
                stiffness += strain.T @ elastic @ strain / 8.0
    return stiffness


def mode_weights():
    modes = [(i, j, k) for k in (0, 1) for j in (0, 1) for i in (0, 1)]
    sums = np.zeros((24, 24))
    for m, mode in enumerate(modes):
        for n, corner in enumerate(OFFSETS):
            sign = np.prod([(1 if corner[d] else -1) if mode[d] else 1 for d in range(3)])
            for comp in range(3):
                sums[3 * m + comp, 3 * n + comp] = sign
    form = sums @ element_matrix() @ sums.T / 64.0

    def at(first, second):
        return form[3 * modes.index(first[1]) + first[0], 3 * modes.index(second[1]) + second[0]]

    ux, vy, uy = (0, (1, 0, 0)), (1, (0, 1, 0)), (0, (0, 1, 0))
    uxy, wyz = (0, (1, 1, 0)), (2, (0, 1, 1))
    wxy, vxz, uxyz = (2, (1, 1, 0)), (1, (1, 0, 1)), (0, (1, 1, 1))
    return dict(
        normal=at(ux, ux) - at(ux, vy),
        trace=at(ux, vy),
        shear=at(uy, uy),
        plus=(at(uxy, uxy) + at(uxy, wyz)) / 2,
        minus=(at(uxy, uxy) - at(uxy, wyz)) / 2,
        twist=at(wxy, wxy) - at(wxy, vxz),
        twist_sum=at(wxy, vxz),
        corner=at(uxyz, uxyz),
    )


def square(value):
    return value * value


def quadratic(low, high, weights):
    x = [low[c][1] + high[c][1] for c in range(3)]
    y = [low[c][2] + high[c][2] for c in range(3)]
    z = [high[c][0] - low[c][0] for c in range(3)]
    xy = [low[c][3] + high[c][3] for c in range(3)]
    xz = [high[c][1] - low[c][1] for c in range(3)]
    yz = [high[c][2] - low[c][2] for c in range(3)]
    xyz = [high[c][3] - low[c][3] for c in range(3)]
    normal = square(x[0]) + square(y[1]) + square(z[2])
    trace = square(x[0] + y[1] + z[2])
    shear = square(y[0] + x[1]) + square(z[0] + x[2]) + square(z[1] + y[2])
    pairs = ((xy[0], yz[2]), (xy[1], xz[2]), (xz[0], yz[1]))
    plus = sum(square(p + q) for p, q in pairs)
    minus = sum(square(p - q) for p, q in pairs)
    twist = square(xy[2]) + square(xz[1]) + square(yz[0])
    twist_sum = square(xy[2] + xz[1] + yz[0])
    corner = square(xyz[0]) + square(xyz[1]) + square(xyz[2])
    groups = dict(
        normal=normal, trace=trace, shear=shear, plus=plus, minus=minus, twist=twist, twist_sum=twist_sum, corner=corner
    )
    return sum(np.float32(weights[name]) * group for name, group in groups.items())


def line_weight(coord, count):
    def outside(distance):
        missing = jnp.maximum(REACH - distance, 0)
        return missing * (missing + 1) // 2

    whole = (REACH + 1) * (REACH + 1)
    return (whole - outside(coord) - outside(count - 1 - coord)).astype(jnp.float32)


def voxel_factor(density, solid, plane, first_row, total_z, total_y):
    rows, length = density.shape
    row = lax.broadcasted_iota(jnp.int32, (rows, length), 0) + first_row
    column = lax.broadcasted_iota(jnp.int32, (rows, length), 1)
    weight = line_weight(row, total_y) * line_weight(column, length)
    weight = weight * line_weight(jnp.full((rows, length), plane, jnp.int32), total_z)
    return solid.astype(jnp.float32) * (-3.0 * density * density) / weight


def spread_x(value):
    rows, length = value.shape
    wide = jnp.concatenate([value, jnp.zeros((rows, LANES), jnp.float32)], axis=1)
    span = length + LANES
    total = float(ROWS) * value
    for step in range(1, ROWS):
        both = pltpu.roll(wide, span - step, 1) + pltpu.roll(wide, step, 1)
        total = total + float(ROWS - step) * both[:, :length]
    return total


def spread_layers(layers):
    for step in (1, 2, 1, 2):
        layers = [layers[k] + layers[k + step] for k in range(len(layers) - step)]
    return layers


def held(disp, fixed, case, comp, z, rows):
    return disp[case, comp, z, rows] * (1.0 - fixed[z, rows].astype(jnp.float32))


def split_x(value):
    length = value.shape[1]
    column = lax.broadcasted_iota(jnp.int32, value.shape, 1)
    ahead = jnp.where(column == length - 1, 0.0, pltpu.roll(value, length - 1, 1))
    return value + ahead, ahead - value


def spread_y(quotient, ylen):
    rows = [quotient[TILE + step : TILE + step + ylen] for step in range(-REACH, REACH + 1)]
    return sum((ROWS - abs(k - REACH)) * rows[k] for k in range(2 * REACH + 1))


def to_neighbours(quotient, ylen):
    top = quotient[ylen : ylen + TILE]
    base = quotient[TILE : 2 * TILE]
    ahead, back = [], []
    for row in range(REACH):
        ahead.append(sum(float(REACH - row - k) * top[TILE - 1 - k : TILE - k] for k in range(REACH - row)))
        back.append(sum(float(row + 1 - k) * base[k : k + 1] for k in range(row + 1)))
    return ahead, back


def next_is_partner(start):
    return (lax.axis_index("sy") - start) % 2 == 0


def on_first():
    return lax.axis_index("load") == 0


def lead_kernel(totals, disp_hbm, fixed_hbm, density_hbm, solid_hbm, d_out, z_out, y_out, layer, layer_fixed, density, solid, rows, rows_fixed, sems):
    loads, comps, zlen, ylen, _ = disp_hbm.shape
    gives = jnp.where(on_first(), 0, zlen - 1)
    copies = [
        pltpu.make_async_copy(source, target, sems.at[k])
        for k, (source, target) in enumerate(
            (
                (density_hbm.at[gives], density),
                (solid_hbm.at[gives], solid),
                (fixed_hbm.at[gives], layer_fixed),
                (disp_hbm.at[:, :, gives], layer),
                (fixed_hbm.at[:, :1], rows_fixed),
                (disp_hbm.at[:, :, :, :1], rows),
            )
        )
    ]
    for copy in copies:
        copy.start()
    for copy in copies[:2]:
        copy.wait()
    plane = lax.axis_index("sz") * zlen + gives
    base_y = lax.axis_index("sy") * ylen
    d_out[...] = jnp.zeros(d_out.shape, jnp.float32)
    z_out[loads * comps] = voxel_factor(density[...], solid[...], plane, base_y, *totals)
    for copy in copies[2:4]:
        copy.wait()
    free = 1.0 - layer_fixed[...].astype(jnp.float32)
    for case in range(loads):
        for comp in range(comps):
            k = case * comps + comp
            z_out[k] = layer[case, comp] * free
            d_out[k : k + 1] = z_out[k, :1]
    for copy in copies[4:]:
        copy.wait()
    for z in range(zlen):
        free = 1.0 - rows_fixed[z, :1].astype(jnp.float32)
        for case in range(loads):
            for comp in range(comps):
                at = (comp * loads + case) * zlen + z
                y_out[at : at + 1] = rows[case, comp, z, :1] * free


def tile_energies(plus, diff, first, lanes, layers, loads, comps, base=0):
    weights = mode_weights()

    def faces(k, z):
        near, far = slice(first, first + TILE), slice(first + 1, first + TILE + 1)
        whole, whole_next = plus[k, z, near, lanes], plus[k, z, far, lanes]
        change, change_next = diff[k, z, near, lanes], diff[k, z, far, lanes]
        return whole + whole_next, change + change_next, whole_next - whole, change_next - change

    energy = [None] * layers
    for case in range(loads):
        low = None
        for z in range(layers + 1):
            high = [faces(case * comps + comp, base + z) for comp in range(comps)]
            if low is not None:
                part = quadratic(low, high, weights)
                energy[z - 1] = part if energy[z - 1] is None else energy[z - 1] + part
            low = high
    return energy


def blank_last(value, first, ylen):
    row = lax.broadcasted_iota(jnp.int32, value.shape, 0) + first
    return jnp.where(row == ylen - 1, 0.0, value)


def inner_kernel(totals, disp, fixed, density, solid, own, line, sends, last_plus, last_diff, last_factor, edge, plus, diff, quotient):
    loads, comps, zlen, ylen, xlen = disp.shape
    total_z, total_y = totals
    base_z = lax.axis_index("sz") * zlen
    base_y = lax.axis_index("sy") * ylen
    inner = zlen - 1
    keeps = jnp.where(on_first(), inner, 0)
    free = [1.0 - fixed[z].astype(jnp.float32) for z in range(zlen)]

    @pl.loop(0, loads * comps, unroll=True)
    def _(k):
        case, comp = k // comps, k % comps
        for z in range(zlen):
            whole, change = split_x(disp[case, comp, z] * free[z])
            plus[k, z, :ylen] = whole
            diff[k, z, :ylen] = change
        last_plus[k] = plus[k, keeps, :ylen]
        last_diff[k] = diff[k, keeps, :ylen]

    for comp in range(comps):
        for case in range(loads):
            for z in range(zlen):
                at = (comp * loads + case) * zlen + z
                line[0, at : at + 1] = plus[case * comps + comp, z, ylen - 1 : ylen]
                line[1, at : at + 1] = diff[case * comps + comp, z, ylen - 1 : ylen]

    zeros = jnp.zeros((TILE, xlen), jnp.float32)
    edge[...] = jnp.zeros(edge.shape, jnp.float32)
    for z in range(zlen):
        factor = voxel_factor(density[z], solid[z], base_z + z, base_y, total_z, total_y)
        edge[z : z + 1] = factor[ylen - 1 :]
        if z == inner:
            last_factor[...] = factor
        else:
            quotient[z, :TILE] = zeros
            quotient[z, TILE : TILE + ylen] = factor
            quotient[z, TILE + ylen :] = zeros

    for first in range(0, ylen, TILE):

        @pl.loop(0, xlen // LANES, unroll=True)
        def _(chunk):
            lanes = pl.ds(pl.multiple_of(chunk * LANES, LANES), LANES)
            energy = tile_energies(plus, diff, first, lanes, inner, loads, comps)
            for z in range(inner):
                here = quotient[z, first + TILE : first + 2 * TILE, lanes]
                quotient[z, first + TILE : first + 2 * TILE, lanes] = blank_last(energy[z] * here, first, ylen)

    for z in range(inner):
        own[z] = spread_x(spread_y(quotient.at[z], ylen))
        ahead, back = to_neighbours(quotient.at[z], ylen)
        ends = spread_x(jnp.concatenate(ahead + back + [zeros[:2]], axis=0))
        sends[0, REACH * z : REACH * (z + 1)] = ends[:REACH]
        sends[1, REACH * z : REACH * (z + 1)] = ends[REACH : 2 * REACH]


def outer_kernel(
    shape, z_in, y_in, own_in, line, sends, last_plus, last_diff, last_factor, edge, share, corner, plus, diff, quotient, factor
):
    loads, comps, zlen, ylen, xlen = shape
    planes = loads * comps
    inner = zlen - 1
    first_core, index = on_first(), lax.axis_index("sz")
    top = first_core & (index == lax.axis_size("sz") - 1)
    more = lax.axis_index("sy") < lax.axis_size("sy") - 1
    stays, comes = jnp.where(first_core, 0, 1), jnp.where(first_core, jnp.where(top, 2, 1), 0)
    y_plus, y_diff = split_x(jnp.where(more, y_in[...], 0.0))
    for k in range(planes):
        plus[k, stays, :ylen] = last_plus[k]
        diff[k, stays, :ylen] = last_diff[k]
        whole, change = split_x(z_in[k])
        plus[k, comes, :ylen] = whole
        diff[k, comes, :ylen] = change
        for group, value in enumerate((last_plus[k, ylen - 1 :], last_diff[k, ylen - 1 :], whole[ylen - 1 :], change[ylen - 1 :])):
            corner[group, k : k + 1] = value
    below = jnp.where(index > 0, z_in[planes], 0.0)
    factor[...] = jnp.where(first_core, last_factor[...], below)
    corner[0, planes : planes + 1] = factor[ylen - 1 :]

    @pl.when(top)
    def _():
        clamped = jnp.zeros((ylen + TILE, xlen), jnp.float32)
        for k in range(planes):
            for slot in (1, 3):
                plus[k, slot] = clamped
                diff[k, slot] = clamped

    zeros = jnp.zeros((TILE, xlen), jnp.float32)
    quotient[:TILE] = zeros
    quotient[TILE + ylen :] = zeros
    for first in range(0, ylen, TILE):

        @pl.loop(0, xlen // LANES, unroll=True)
        def _(chunk):
            lanes = pl.ds(pl.multiple_of(chunk * LANES, LANES), LANES)
            (energy,) = tile_energies(plus, diff, first, lanes, 1, loads, comps)
            here = energy * factor[first : first + TILE, lanes]
            quotient[first + TILE : first + 2 * TILE, lanes] = blank_last(here, first, ylen)

    @pl.when(top)
    def _():
        for first in range(0, ylen, TILE):

            @pl.loop(0, xlen // LANES, unroll=True)
            def _(chunk):
                lanes = pl.ds(pl.multiple_of(chunk * LANES, LANES), LANES)
                (energy,) = tile_energies(plus, diff, first, lanes, 1, loads, comps, base=2)
                here = energy * factor[first : first + TILE, lanes]
                quotient[first + TILE : first + 2 * TILE, lanes] += blank_last(here, first, ylen)

    count = loads * zlen
    low, high = [], []
    for comp in range(comps):
        part = slice(comp * count, (comp + 1) * count)
        whole, change = line[0, part], line[1, part]
        whole_next, change_next = y_plus[part], y_diff[part]
        face = (whole + whole_next, change + change_next, whole_next - whole, change_next - change)
        low.append(face)
        high.append([pltpu.roll(value, count - 1, 0) for value in face])
    energy = quadratic(low, high, mode_weights())
    energy = sum(energy[case * zlen : case * zlen + inner] for case in range(loads)) * edge[:inner]
    last = spread_x(jnp.concatenate([energy, jnp.zeros((TILE - inner, xlen), jnp.float32)], axis=0))

    row = lax.broadcasted_iota(jnp.int32, (TILE, xlen), 0)
    rising = jnp.maximum(row - (TILE - 1 - ROWS), 0).astype(jnp.float32)
    ups, downs = [], []
    for z in range(inner):
        share[ylen * z : ylen * (z + 1)] = own_in[z]
        share[ylen * (z + 1) - TILE : ylen * (z + 1)] += rising * last[z : z + 1]
        here = sends[0, REACH * z : REACH * (z + 1)]
        ups += [here[r : r + 1] + float(REACH - r) * last[z : z + 1] for r in range(REACH)]
        downs.append(sends[1, REACH * z : REACH * (z + 1)])
    share[ylen * inner : ylen * zlen] = spread_x(spread_y(quotient, ylen))
    ahead, back = to_neighbours(quotient, ylen)
    ends = spread_x(jnp.concatenate(ahead + back + [zeros[:2]], axis=0))
    share[ylen * zlen :] = jnp.concatenate(ups + [ends[:REACH]] + downs + [ends[REACH : 2 * REACH]], axis=0)


def corner_line(shape, corner, y_in, d_in):
    loads, comps, zlen, ylen, xlen = shape
    planes = loads * comps
    first_core = on_first()
    top = first_core & (lax.axis_index("sz") == lax.axis_size("sz") - 1)
    more = lax.axis_index("sy") < lax.axis_size("sy") - 1
    rows = []
    for k in range(planes):
        at = (k % comps * loads + k // comps) * zlen
        rows.append(jnp.where(first_core, y_in[at + zlen - 1 : at + zlen], y_in[at : at + 1]))
    rows.append(jnp.zeros((-planes % TILE, xlen), jnp.float32))
    stays_next = split_x(jnp.where(more, jnp.concatenate(rows, axis=0), 0.0))
    comes_next = split_x(jnp.where(more, d_in[...], 0.0))

    def faces(stays, comes, comp):
        zero = jnp.zeros((1, xlen), jnp.float32)
        under, over = [], []
        for own, other in zip(stays, comes):
            own, other = ([value[case * comps + comp : case * comps + comp + 1] for case in range(loads)] for value in (own, other))
            low = [jnp.where(first_core, a, b) for a, b in zip(own, other)] + [jnp.where(top, b, 0.0) for b in other]
            high = [jnp.where(first_core, jnp.where(top, 0.0, b), a) for a, b in zip(own, other)] + [zero] * loads
            under.append(jnp.concatenate(low, axis=0))
            over.append(jnp.concatenate(high, axis=0))
        return under, over

    low, high = [], []
    for comp in range(comps):
        near = faces((corner[0], corner[1]), (corner[2], corner[3]), comp)
        far = faces(stays_next, comes_next, comp)
        for (whole, change), (whole_next, change_next), into in zip(near, far, (low, high)):
            into.append((whole + whole_next, change + change_next, whole_next - whole, change_next - change))
    energy = quadratic(low, high, mode_weights())
    line = sum(energy[case : case + 1] for case in range(2 * loads)) * corner[0, planes : planes + 1]
    return spread_x(jnp.concatenate([line, jnp.zeros((TILE - 1, xlen), jnp.float32)], axis=0))[:1]


def corner_kernel(shape, share_in, corner, y_in, d_in, share):
    _, _, zlen, ylen, xlen = shape
    line = corner_line(shape, corner, y_in, d_in)
    rising = jnp.maximum(lax.broadcasted_iota(jnp.int32, (TILE, xlen), 0) - (TILE - 1 - ROWS), 0).astype(jnp.float32)
    falling = (REACH - lax.broadcasted_iota(jnp.int32, (REACH, xlen), 0)).astype(jnp.float32)
    share[...] = share_in[...]
    share[ylen * zlen - TILE : ylen * zlen] += rising * line
    share[ylen * zlen + REACH * (zlen - 1) : ylen * zlen + REACH * zlen] += falling * line


def total_kernel(shape, share, other, h_out, z_out, y_out, d_out, e_out):
    _, _, zlen, ylen, xlen = shape
    first_core = on_first()
    inner, rows = zlen - 1, ylen * zlen
    reach = REACH * zlen

    def layers(first, count):
        mine, theirs = share[first + inner * count : first + zlen * count], other[first + inner * count : first + zlen * count]
        middle = share[first : first + inner * count] + other[first : first + inner * count]
        return jnp.where(first_core, theirs, mine), middle, jnp.where(first_core, mine, theirs)

    lowest, middle, highest = layers(0, ylen)
    h_out[0] = lowest
    for z in range(inner):
        h_out[z + 1] = middle[ylen * z : ylen * (z + 1)]
    h_out[zlen] = highest
    z_out[...] = h_out[pl.ds(jnp.where(first_core, 0, 1), zlen)]
    ups = jnp.concatenate(layers(rows, REACH), axis=0)
    downs = jnp.concatenate(layers(rows + reach, REACH), axis=0)
    y_out[: reach + REACH] = jnp.where(first_core, downs, ups)
    for out, used in ((y_out, reach + REACH), (d_out, reach), (e_out, reach)):
        out[used:] = jnp.zeros((out.shape[0] - used, xlen), jnp.float32)
    for out, start in ((d_out, 1), (e_out, 0)):
        rows = jnp.where(next_is_partner(start), ups, downs)
        out[:reach] = jnp.where(first_core, rows[:reach], rows[REACH:])


def layers_kernel(h, d_in, y_in, e_in, z_in, out):
    zlen, ylen, xlen = out.shape
    reach = REACH * zlen
    first_core = on_first()
    z_index, z_last = lax.axis_index("sz"), lax.axis_size("sz") - 1
    y_index, y_last = lax.axis_index("sy"), lax.axis_size("sy") - 1
    z_side = jnp.where(first_core, z_index < z_last, z_index > 0)
    y_side = jnp.where(first_core, y_index < y_last, y_index > 0)
    d_next, e_next = next_is_partner(1), next_is_partner(0)
    d_side, e_side = (jnp.where(up, y_index < y_last, y_index > 0) for up in (d_next, e_next))
    blank = jnp.zeros((TILE - REACH, xlen), jnp.float32)

    def at_start(rows):
        return jnp.concatenate([rows, blank], axis=0)

    def at_end(rows):
        return jnp.concatenate([blank, rows], axis=0)

    def ends(rows, keep, at_last):
        rows = jnp.where(keep, rows, 0.0)
        return at_start(jnp.where(at_last, 0.0, rows)), at_end(jnp.where(at_last, rows, 0.0))

    def with_ends(layer, *pairs):
        head, tail = layer[:TILE], layer[ylen - TILE :]
        for first, last in pairs:
            head, tail = head + first, tail + last
        return jnp.concatenate([head, layer[TILE : ylen - TILE], tail] if ylen > 2 * TILE else [head, tail], axis=0)

    own = []
    for k in range(zlen + 1):
        layer = jnp.where(first_core, h[k], 0.0)
        own.append(with_ends(layer, ends(y_in[REACH * k : REACH * (k + 1)], y_side, first_core)))
    come = []
    for k in range(zlen):
        part = slice(REACH * k, REACH * (k + 1))
        layer = jnp.where(z_side, z_in[k], 0.0)
        come.append(with_ends(layer, ends(d_in[part], z_side & d_side, d_next), ends(e_in[part], z_side & e_side, e_next)))
    below = [jnp.where(first_core, 0.0, layer) for layer in come[zlen - REACH :]]
    above = [jnp.where(first_core, layer, 0.0) for layer in come]
    layers = below[:-1] + [below[-1] + own[0]] + own[1:-1] + [own[-1] + above[0]] + above[1:]
    for z, layer in enumerate(spread_layers(layers)):
        out[z] = layer


def sum_kernel(part, other, out):
    out[...] = part[...] + other[...]


def call(kernel, outs, args, scratch=(), space=pltpu.VMEM):
    shapes = [jax.ShapeDtypeStruct(out, jnp.float32) if isinstance(out, tuple) else out for out in outs]
    return pl.pallas_call(
        kernel,
        out_shape=shapes,
        in_specs=[pl.BlockSpec(memory_space=space)] * len(args),
        out_specs=[pl.BlockSpec(memory_space=pltpu.VMEM)] * len(outs),
        scratch_shapes=list(scratch),
        compiler_params=pltpu.CompilerParams(vmem_limit_bytes=32 * 1024 * 1024),
    )(*args)


def ring_moved(value, axis):
    size = lax.axis_size(axis)
    return lax.ppermute(value, axis, [((k + 1) % size, k) for k in range(size)])


def chip_swapped(value):
    cores = lax.axis_size("load")
    return lax.ppermute(value, "load", [(core, cores - 1 - core) for core in range(cores)])


def opposed(value, z_step, y_step, y_shift=0, start=None):
    cores, rows, size = lax.axis_size("load"), lax.axis_size("sy"), lax.axis_size("sz")
    pairs = []
    for core in range(cores):
        sign = -1 if core else 1
        for y in range(rows):
            for z in range(size):
                to_y, to_z, side = y + sign * y_step, z + sign * z_step, core
                if start is not None:
                    to_y = y + 1 if (y - start) % 2 == 0 else y - 1
                if not (0 <= to_y < rows and 0 <= to_z < size):
                    to_y, to_z, side = y, z, cores - 1 - core
                to_y = (to_y + y_shift) % rows
                pairs.append(((core * rows + y) * size + z, (side * rows + to_y) * size + to_z))
    return lax.ppermute(value, ("load", "sy", "sz"), pairs)


def body(displacements, density, solid, fixed):
    loads, comps, zlen, ylen, xlen = displacements.shape
    planes = loads * comps
    totals = (zlen * lax.axis_size("sz"), ylen * lax.axis_size("sy"))
    args = [
        pltpu.with_memory_space_constraint(arg, pltpu.HBM) for arg in (displacements, fixed, density, solid)
    ]

    d_send, z_send, y_send = call(
        lambda *refs: lead_kernel(totals, *refs),
        [(-(-planes // TILE) * TILE, xlen), (planes + 1, ylen, xlen), (planes * zlen, xlen)],
        args,
        scratch=[
            pltpu.VMEM((loads, comps, ylen, xlen), jnp.float32),
            pltpu.VMEM((ylen, xlen), jnp.int32),
            pltpu.VMEM((ylen, xlen), jnp.float32),
            pltpu.VMEM((ylen, xlen), jnp.int32),
            pltpu.VMEM((loads, comps, zlen, 1, xlen), jnp.float32),
            pltpu.VMEM((zlen, 1, xlen), jnp.int32),
            pltpu.SemaphoreType.DMA((6,)),
        ],
        space=pltpu.HBM,
    )
    d_in = opposed(d_send, -1, 0, y_shift=-1)
    z_in = opposed(z_send, -1, 0)
    y_in = ring_moved(y_send, "sy")
    nodes = lambda layers: pltpu.VMEM((planes, layers, ylen + TILE, xlen), jnp.float32)
    inner = call(
        lambda *refs: inner_kernel(totals, *refs),
        [
            (zlen, ylen, xlen),
            (2, planes * zlen, xlen),
            (2, REACH * (zlen - 1), xlen),
            (planes, ylen, xlen),
            (planes, ylen, xlen),
            (ylen, xlen),
            (TILE, xlen),
        ],
        (displacements, fixed, density, solid),
        scratch=[nodes(zlen), nodes(zlen), pltpu.VMEM((zlen - 1, ylen + 2 * TILE, xlen), jnp.float32)],
    )
    reach = REACH * zlen
    shape = displacements.shape
    share, corner = call(
        lambda *refs: outer_kernel(shape, *refs),
        [(ylen * zlen + 2 * reach, xlen), (4, -(-(planes + 1) // TILE) * TILE, xlen)],
        (z_in, y_in, *inner),
        scratch=[
            nodes(4),
            nodes(4),
            pltpu.VMEM((ylen + 2 * TILE, xlen), jnp.float32),
            pltpu.VMEM((ylen, xlen), jnp.float32),
        ],
    )
    (share,) = call(
        lambda *refs: corner_kernel(shape, *refs), [(ylen * zlen + 2 * reach, xlen)], (share, corner, y_in, d_in)
    )
    sent = (-(-(reach + REACH) // TILE) * TILE, xlen)
    h, z_send, y_send, d_send, e_send = call(
        lambda *refs: total_kernel(displacements.shape, *refs),
        [
            (zlen + 1, ylen, xlen),
            (zlen, ylen, xlen),
            sent,
            sent,
            sent,
        ],
        (share, chip_swapped(share)),
    )
    d_in = opposed(d_send, -1, 0, start=1)
    e_in = opposed(e_send, -1, 0, start=0)
    y_in = opposed(y_send, 0, -1)
    z_in = opposed(z_send, -1, 0)
    (part,) = call(layers_kernel, [(zlen, ylen, xlen)], (h, d_in, y_in, e_in, z_in))
    (out,) = call(sum_kernel, [(zlen, ylen, xlen)], (part, chip_swapped(part)))
    return out


def solution(mesh):
    return jax.shard_map(
        body,
        mesh=mesh,
        in_specs=(
            P("load", None, "sz", "sy", None),
            P("sz", "sy", None),
            P("sz", "sy", None),
            P("sz", "sy", None),
        ),
        out_specs=P("sz", "sy", None),
        check_vma=False,
    )
```

```python
import jax
import jax.numpy as jnp
import numpy as np
from jax import lax
from jax.experimental import pallas as pl
from jax.experimental.pallas import tpu as pltpu
from jax.sharding import PartitionSpec as P

OFFSETS = [(0, 0, 0), (1, 0, 0), (1, 1, 0), (0, 1, 0), (0, 0, 1), (1, 0, 1), (1, 1, 1), (0, 1, 1)]
REACH = 3
ROWS = REACH + 1
TILE = 8
LANES = 128


def element_matrix():
    corners = np.array(
        [
            [-1.0, -1.0, -1.0],
            [1.0, -1.0, -1.0],
            [1.0, 1.0, -1.0],
            [-1.0, 1.0, -1.0],
            [-1.0, -1.0, 1.0],
            [1.0, -1.0, 1.0],
            [1.0, 1.0, 1.0],
            [-1.0, 1.0, 1.0],
        ]
    )
    poisson = 0.3
    lame = poisson / ((1.0 + poisson) * (1.0 - 2.0 * poisson))
    shear = 1.0 / (2.0 * (1.0 + poisson))
    elastic = np.zeros((6, 6))
    elastic[:3, :3] = lame
    for k in range(3):
        elastic[k, k] += 2.0 * shear
        elastic[3 + k, 3 + k] = shear
    gauss = 1.0 / np.sqrt(3.0)
    stiffness = np.zeros((24, 24))
    for gi in range(2):
        for gj in range(2):
            for gk in range(2):
                point = np.array([(2 * gi - 1) * gauss, (2 * gj - 1) * gauss, (2 * gk - 1) * gauss])
                strain = np.zeros((6, 24))
                for node in range(8):
                    grads = np.zeros(3)
                    for k in range(3):
                        value = corners[node, k] / 8.0
                        for m in range(3):
                            if m != k:
                                value = value * (1.0 + point[m] * corners[node, m])
                        grads[k] = 2.0 * value
                    col = 3 * node
                    strain[0, col] = grads[0]
                    strain[1, col + 1] = grads[1]
                    strain[2, col + 2] = grads[2]
                    strain[3, col] = grads[1]
                    strain[3, col + 1] = grads[0]
                    strain[4, col + 1] = grads[2]
                    strain[4, col + 2] = grads[1]
                    strain[5, col] = grads[2]
                    strain[5, col + 2] = grads[0]
                stiffness += strain.T @ elastic @ strain / 8.0
    return stiffness


def mode_weights():
    modes = [(i, j, k) for k in (0, 1) for j in (0, 1) for i in (0, 1)]
    sums = np.zeros((24, 24))
    for m, mode in enumerate(modes):
        for n, corner in enumerate(OFFSETS):
            sign = np.prod([(1 if corner[d] else -1) if mode[d] else 1 for d in range(3)])
            for comp in range(3):
                sums[3 * m + comp, 3 * n + comp] = sign
    form = sums @ element_matrix() @ sums.T / 64.0

    def at(first, second):
        return form[3 * modes.index(first[1]) + first[0], 3 * modes.index(second[1]) + second[0]]

    ux, vy, uy = (0, (1, 0, 0)), (1, (0, 1, 0)), (0, (0, 1, 0))
    uxy, wyz = (0, (1, 1, 0)), (2, (0, 1, 1))
    wxy, vxz, uxyz = (2, (1, 1, 0)), (1, (1, 0, 1)), (0, (1, 1, 1))
    return dict(
        normal=at(ux, ux) - at(ux, vy),
        trace=at(ux, vy),
        shear=at(uy, uy),
        plus=(at(uxy, uxy) + at(uxy, wyz)) / 2,
        minus=(at(uxy, uxy) - at(uxy, wyz)) / 2,
        twist=at(wxy, wxy) - at(wxy, vxz),
        twist_sum=at(wxy, vxz),
        corner=at(uxyz, uxyz),
    )


def square(value):
    return value * value


def quadratic(low, high, weights):
    x = [low[c][1] + high[c][1] for c in range(3)]
    y = [low[c][2] + high[c][2] for c in range(3)]
    z = [high[c][0] - low[c][0] for c in range(3)]
    xy = [low[c][3] + high[c][3] for c in range(3)]
    xz = [high[c][1] - low[c][1] for c in range(3)]
    yz = [high[c][2] - low[c][2] for c in range(3)]
    xyz = [high[c][3] - low[c][3] for c in range(3)]
    normal = square(x[0]) + square(y[1]) + square(z[2])
    trace = square(x[0] + y[1] + z[2])
    shear = square(y[0] + x[1]) + square(z[0] + x[2]) + square(z[1] + y[2])
    pairs = ((xy[0], yz[2]), (xy[1], xz[2]), (xz[0], yz[1]))
    plus = sum(square(p + q) for p, q in pairs)
    minus = sum(square(p - q) for p, q in pairs)
    twist = square(xy[2]) + square(xz[1]) + square(yz[0])
    twist_sum = square(xy[2] + xz[1] + yz[0])
    corner = square(xyz[0]) + square(xyz[1]) + square(xyz[2])
    groups = dict(
        normal=normal, trace=trace, shear=shear, plus=plus, minus=minus, twist=twist, twist_sum=twist_sum, corner=corner
    )
    return sum(np.float32(weights[name]) * group for name, group in groups.items())


def line_weight(coord, count):
    def outside(distance):
        missing = jnp.maximum(REACH - distance, 0)
        return missing * (missing + 1) // 2

    whole = (REACH + 1) * (REACH + 1)
    return (whole - outside(coord) - outside(count - 1 - coord)).astype(jnp.float32)


def voxel_factor(density, solid, plane, first_row, total_z, total_y):
    rows, length = density.shape
    row = lax.broadcasted_iota(jnp.int32, (rows, length), 0) + first_row
    column = lax.broadcasted_iota(jnp.int32, (rows, length), 1)
    weight = line_weight(row, total_y) * line_weight(column, length)
    weight = weight * line_weight(jnp.full((rows, length), plane, jnp.int32), total_z)
    return solid.astype(jnp.float32) * (-3.0 * density * density) / weight


def spread_x(value):
    rows, length = value.shape
    wide = jnp.concatenate([value, jnp.zeros((rows, LANES), jnp.float32)], axis=1)
    span = length + LANES
    total = float(ROWS) * value
    for step in range(1, ROWS):
        both = pltpu.roll(wide, span - step, 1) + pltpu.roll(wide, step, 1)
        total = total + float(ROWS - step) * both[:, :length]
    return total


def spread_layers(layers):
    for step in (1, 2, 1, 2):
        layers = [layers[k] + layers[k + step] for k in range(len(layers) - step)]
    return layers


def held(disp, fixed, case, comp, z, rows):
    return disp[case, comp, z, rows] * (1.0 - fixed[z, rows].astype(jnp.float32))


def split_x(value):
    length = value.shape[1]
    column = lax.broadcasted_iota(jnp.int32, value.shape, 1)
    ahead = jnp.where(column == length - 1, 0.0, pltpu.roll(value, length - 1, 1))
    return value + ahead, ahead - value


def face_sums(value):
    following = pltpu.roll(value, value.shape[0] - 1, 0)
    both, along_x = split_x(value + following)
    along_y, mixed = split_x(following - value)
    return both, along_x, along_y, mixed


def spread_y(quotient, ylen):
    rows = [quotient[TILE + step : TILE + step + ylen] for step in range(-REACH, REACH + 1)]
    return sum((ROWS - abs(k - REACH)) * rows[k] for k in range(2 * REACH + 1))


def to_neighbours(quotient, ylen):
    top = quotient[ylen : ylen + TILE]
    base = quotient[TILE : 2 * TILE]
    ahead, back = [], []
    for row in range(REACH):
        ahead.append(sum(float(REACH - row - k) * top[TILE - 1 - k : TILE - k] for k in range(REACH - row)))
        back.append(sum(float(row + 1 - k) * base[k : k + 1] for k in range(row + 1)))
    return ahead, back


def next_is_partner(start):
    return (lax.axis_index("sy") - start) % 2 == 0


def on_first():
    return lax.axis_index("load") == 0


def lead_kernel(totals, disp_hbm, fixed_hbm, density_hbm, solid_hbm, d_out, z_out, y_out, layer, layer_fixed, density, solid, rows, rows_fixed, sems):
    loads, comps, zlen, ylen, _ = disp_hbm.shape
    gives = jnp.where(on_first(), 0, zlen - 1)
    copies = [
        pltpu.make_async_copy(source, target, sems.at[k])
        for k, (source, target) in enumerate(
            (
                (density_hbm.at[gives], density),
                (solid_hbm.at[gives], solid),
                (fixed_hbm.at[gives], layer_fixed),
                (disp_hbm.at[:, :, gives], layer),
                (fixed_hbm.at[:, :1], rows_fixed),
                (disp_hbm.at[:, :, :, :1], rows),
            )
        )
    ]
    for copy in copies:
        copy.start()
    for copy in copies[:2]:
        copy.wait()
    plane = lax.axis_index("sz") * zlen + gives
    base_y = lax.axis_index("sy") * ylen
    d_out[...] = jnp.zeros(d_out.shape, jnp.float32)
    z_out[loads * comps] = voxel_factor(density[...], solid[...], plane, base_y, *totals)
    for copy in copies[2:4]:
        copy.wait()
    free = 1.0 - layer_fixed[...].astype(jnp.float32)
    for case in range(loads):
        for comp in range(comps):
            k = case * comps + comp
            z_out[k] = layer[case, comp] * free
            d_out[k : k + 1] = z_out[k, :1]
    for copy in copies[4:]:
        copy.wait()
    for z in range(zlen):
        free = 1.0 - rows_fixed[z, :1].astype(jnp.float32)
        for case in range(loads):
            for comp in range(comps):
                at = (comp * loads + case) * zlen + z
                y_out[at : at + 1] = rows[case, comp, z, :1] * free


def tile_energies(faces, first, lanes, layers, loads, comps, base=0):
    weights = mode_weights()
    energy = [None] * layers
    for case in range(loads):
        low = None
        for z in range(layers + 1):
            planes = [case * comps + comp for comp in range(comps)]
            high = [[faces[kind, k, base + z, first : first + TILE, lanes] for kind in range(4)] for k in planes]
            if low is not None:
                part = quadratic(low, high, weights)
                energy[z - 1] = part if energy[z - 1] is None else energy[z - 1] + part
            low = high
    return energy


def blank_last(value, first, ylen):
    row = lax.broadcasted_iota(jnp.int32, value.shape, 0) + first
    return jnp.where(row == ylen - 1, 0.0, value)


def inner_kernel(totals, disp, fixed, density, solid, own, line, sends, last_faces, last_factor, edge, faces, quotient):
    loads, comps, zlen, ylen, xlen = disp.shape
    total_z, total_y = totals
    base_z = lax.axis_index("sz") * zlen
    base_y = lax.axis_index("sy") * ylen
    inner = zlen - 1
    keeps = jnp.where(on_first(), inner, 0)
    free = [1.0 - fixed[z].astype(jnp.float32) for z in range(zlen)]

    for k in range(loads * comps):
        case, comp = k // comps, k % comps
        for z in range(zlen):
            plane = disp[case, comp, z] * free[z]
            for kind, value in enumerate(face_sums(plane)):
                faces[kind, k, z] = value
            at = (comp * loads + case) * zlen + z
            line[0, at : at + 1] = plane[ylen - 1 :]
        for kind in range(4):
            last_faces[kind, k] = faces[kind, k, keeps]

    line[0], line[1] = split_x(line[0])

    zeros = jnp.zeros((TILE, xlen), jnp.float32)
    edge[...] = jnp.zeros(edge.shape, jnp.float32)
    for z in range(zlen):
        factor = voxel_factor(density[z], solid[z], base_z + z, base_y, total_z, total_y)
        edge[z : z + 1] = factor[ylen - 1 :]
        if z == inner:
            last_factor[...] = factor
        else:
            quotient[z, :TILE] = zeros
            quotient[z, TILE : TILE + ylen] = factor
            quotient[z, TILE + ylen :] = zeros

    for first in range(0, ylen, TILE):

        @pl.loop(0, xlen // LANES, unroll=True)
        def _(chunk):
            lanes = pl.ds(pl.multiple_of(chunk * LANES, LANES), LANES)
            energy = tile_energies(faces, first, lanes, inner, loads, comps)
            for z in range(inner):
                here = quotient[z, first + TILE : first + 2 * TILE, lanes]
                quotient[z, first + TILE : first + 2 * TILE, lanes] = blank_last(energy[z] * here, first, ylen)

    for z in range(inner):
        own[z] = spread_x(spread_y(quotient.at[z], ylen))
        ahead, back = to_neighbours(quotient.at[z], ylen)
        ends = spread_x(jnp.concatenate(ahead + back + [zeros[:2]], axis=0))
        sends[0, REACH * z : REACH * (z + 1)] = ends[:REACH]
        sends[1, REACH * z : REACH * (z + 1)] = ends[REACH : 2 * REACH]


def outer_kernel(
    shape, z_in, y_in, own_in, line, sends, last_faces, last_factor, edge, share, corner, faces, quotient, factor
):
    loads, comps, zlen, ylen, xlen = shape
    planes = loads * comps
    inner = zlen - 1
    first_core, index = on_first(), lax.axis_index("sz")
    top = first_core & (index == lax.axis_size("sz") - 1)
    more = lax.axis_index("sy") < lax.axis_size("sy") - 1
    stays, comes = jnp.where(first_core, 0, 1), jnp.where(first_core, jnp.where(top, 2, 1), 0)
    y_plus, y_diff = split_x(jnp.where(more, y_in[...], 0.0))
    come_rows = []
    for k in range(planes):
        for kind, value in enumerate(face_sums(z_in[k])):
            faces[kind, k, stays] = last_faces[kind, k]
            faces[kind, k, comes] = value
        come_rows.append(z_in[k, ylen - 1 :])
        at = (k % comps * loads + k // comps) * zlen
        for group in range(2):
            corner[group, k : k + 1] = jnp.where(first_core, line[group, at + inner : at + zlen], line[group, at : at + 1])
    come_rows.append(jnp.zeros((-planes % TILE, xlen), jnp.float32))
    for group, value in enumerate(split_x(jnp.concatenate(come_rows, axis=0))):
        corner[2 + group, :planes] = value[:planes]
    below = jnp.where(index > 0, z_in[planes], 0.0)
    factor[...] = jnp.where(first_core, last_factor[...], below)
    corner[0, planes : planes + 1] = factor[ylen - 1 :]

    @pl.when(top)
    def _():
        clamped = jnp.zeros((ylen, xlen), jnp.float32)
        for k in range(planes):
            for slot in (1, 3):
                for kind in range(4):
                    faces[kind, k, slot] = clamped

    zeros = jnp.zeros((TILE, xlen), jnp.float32)
    quotient[:TILE] = zeros
    quotient[TILE + ylen :] = zeros
    for first in range(0, ylen, TILE):

        @pl.loop(0, xlen // LANES, unroll=True)
        def _(chunk):
            lanes = pl.ds(pl.multiple_of(chunk * LANES, LANES), LANES)
            (energy,) = tile_energies(faces, first, lanes, 1, loads, comps)
            here = energy * factor[first : first + TILE, lanes]
            quotient[first + TILE : first + 2 * TILE, lanes] = blank_last(here, first, ylen)

    @pl.when(top)
    def _():
        for first in range(0, ylen, TILE):

            @pl.loop(0, xlen // LANES, unroll=True)
            def _(chunk):
                lanes = pl.ds(pl.multiple_of(chunk * LANES, LANES), LANES)
                (energy,) = tile_energies(faces, first, lanes, 1, loads, comps, base=2)
                here = energy * factor[first : first + TILE, lanes]
                quotient[first + TILE : first + 2 * TILE, lanes] += blank_last(here, first, ylen)

    count = loads * zlen
    low, high = [], []
    for comp in range(comps):
        part = slice(comp * count, (comp + 1) * count)
        whole, change = line[0, part], line[1, part]
        whole_next, change_next = y_plus[part], y_diff[part]
        face = (whole + whole_next, change + change_next, whole_next - whole, change_next - change)
        low.append(face)
        high.append([pltpu.roll(value, count - 1, 0) for value in face])
    energy = quadratic(low, high, mode_weights())
    energy = sum(energy[case * zlen : case * zlen + inner] for case in range(loads)) * edge[:inner]
    last = spread_x(jnp.concatenate([energy, jnp.zeros((TILE - inner, xlen), jnp.float32)], axis=0))

    row = lax.broadcasted_iota(jnp.int32, (TILE, xlen), 0)
    rising = jnp.maximum(row - (TILE - 1 - ROWS), 0).astype(jnp.float32)
    ups, downs = [], []
    for z in range(inner):
        share[ylen * z : ylen * (z + 1)] = own_in[z]
        share[ylen * (z + 1) - TILE : ylen * (z + 1)] += rising * last[z : z + 1]
        here = sends[0, REACH * z : REACH * (z + 1)]
        ups += [here[r : r + 1] + float(REACH - r) * last[z : z + 1] for r in range(REACH)]
        downs.append(sends[1, REACH * z : REACH * (z + 1)])
    share[ylen * inner : ylen * zlen] = spread_x(spread_y(quotient, ylen))
    ahead, back = to_neighbours(quotient, ylen)
    ends = spread_x(jnp.concatenate(ahead + back + [zeros[:2]], axis=0))
    share[ylen * zlen :] = jnp.concatenate(ups + [ends[:REACH]] + downs + [ends[REACH : 2 * REACH]], axis=0)


def corner_line(shape, corner, y_in, d_in):
    loads, comps, zlen, ylen, xlen = shape
    planes = loads * comps
    first_core = on_first()
    top = first_core & (lax.axis_index("sz") == lax.axis_size("sz") - 1)
    more = lax.axis_index("sy") < lax.axis_size("sy") - 1
    rows = []
    for k in range(planes):
        at = (k % comps * loads + k // comps) * zlen
        rows.append(jnp.where(first_core, y_in[at + zlen - 1 : at + zlen], y_in[at : at + 1]))
    rows.append(jnp.zeros((-planes % TILE, xlen), jnp.float32))
    stays_next = split_x(jnp.where(more, jnp.concatenate(rows, axis=0), 0.0))
    comes_next = split_x(jnp.where(more, d_in[...], 0.0))

    def faces(stays, comes, comp):
        zero = jnp.zeros((1, xlen), jnp.float32)
        under, over = [], []
        for own, other in zip(stays, comes):
            own, other = ([value[case * comps + comp : case * comps + comp + 1] for case in range(loads)] for value in (own, other))
            low = [jnp.where(first_core, a, b) for a, b in zip(own, other)] + [jnp.where(top, b, 0.0) for b in other]
            high = [jnp.where(first_core, jnp.where(top, 0.0, b), a) for a, b in zip(own, other)] + [zero] * loads
            under.append(jnp.concatenate(low, axis=0))
            over.append(jnp.concatenate(high, axis=0))
        return under, over

    low, high = [], []
    for comp in range(comps):
        near = faces((corner[0], corner[1]), (corner[2], corner[3]), comp)
        far = faces(stays_next, comes_next, comp)
        for (whole, change), (whole_next, change_next), into in zip(near, far, (low, high)):
            into.append((whole + whole_next, change + change_next, whole_next - whole, change_next - change))
    energy = quadratic(low, high, mode_weights())
    line = sum(energy[case : case + 1] for case in range(2 * loads)) * corner[0, planes : planes + 1]
    return spread_x(jnp.concatenate([line, jnp.zeros((TILE - 1, xlen), jnp.float32)], axis=0))[:1]


def corner_kernel(shape, share_in, corner, y_in, d_in, share):
    _, _, zlen, ylen, xlen = shape
    line = corner_line(shape, corner, y_in, d_in)
    rising = jnp.maximum(lax.broadcasted_iota(jnp.int32, (TILE, xlen), 0) - (TILE - 1 - ROWS), 0).astype(jnp.float32)
    falling = (REACH - lax.broadcasted_iota(jnp.int32, (REACH, xlen), 0)).astype(jnp.float32)
    share[...] = share_in[...]
    share[ylen * zlen - TILE : ylen * zlen] += rising * line
    share[ylen * zlen + REACH * (zlen - 1) : ylen * zlen + REACH * zlen] += falling * line


def total_kernel(shape, share, other, h_out, z_out, y_out, d_out, e_out):
    _, _, zlen, ylen, xlen = shape
    first_core = on_first()
    inner, rows = zlen - 1, ylen * zlen
    reach = REACH * zlen

    def layers(first, count):
        mine, theirs = share[first + inner * count : first + zlen * count], other[first + inner * count : first + zlen * count]
        middle = share[first : first + inner * count] + other[first : first + inner * count]
        return jnp.where(first_core, theirs, mine), middle, jnp.where(first_core, mine, theirs)

    lowest, middle, highest = layers(0, ylen)
    h_out[0] = lowest
    for z in range(inner):
        h_out[z + 1] = middle[ylen * z : ylen * (z + 1)]
    h_out[zlen] = highest
    z_out[...] = h_out[pl.ds(jnp.where(first_core, 0, 1), zlen)]
    ups = jnp.concatenate(layers(rows, REACH), axis=0)
    downs = jnp.concatenate(layers(rows + reach, REACH), axis=0)
    y_out[: reach + REACH] = jnp.where(first_core, downs, ups)
    for out, used in ((y_out, reach + REACH), (d_out, reach), (e_out, reach)):
        out[used:] = jnp.zeros((out.shape[0] - used, xlen), jnp.float32)
    for out, start in ((d_out, 1), (e_out, 0)):
        rows = jnp.where(next_is_partner(start), ups, downs)
        out[:reach] = jnp.where(first_core, rows[:reach], rows[REACH:])


def layers_kernel(h, d_in, e_in, y_in, z_in, out):
    zlen, ylen, xlen = out.shape
    reach = REACH * zlen
    first_core = on_first()
    z_index, z_last = lax.axis_index("sz"), lax.axis_size("sz") - 1
    y_index, y_last = lax.axis_index("sy"), lax.axis_size("sy") - 1
    z_side = jnp.where(first_core, z_index < z_last, z_index > 0)
    y_side = jnp.where(first_core, y_index < y_last, y_index > 0)
    d_next, e_next = next_is_partner(1), next_is_partner(0)
    d_side, e_side = (jnp.where(up, y_index < y_last, y_index > 0) for up in (d_next, e_next))
    blank = jnp.zeros((TILE - REACH, xlen), jnp.float32)

    def at_start(rows):
        return jnp.concatenate([rows, blank], axis=0)

    def at_end(rows):
        return jnp.concatenate([blank, rows], axis=0)

    def ends(rows, keep, at_last):
        rows = jnp.where(keep, rows, 0.0)
        return at_start(jnp.where(at_last, 0.0, rows)), at_end(jnp.where(at_last, rows, 0.0))

    def with_ends(layer, *pairs):
        head, tail = layer[:TILE], layer[ylen - TILE :]
        for first, last in pairs:
            head, tail = head + first, tail + last
        return jnp.concatenate([head, layer[TILE : ylen - TILE], tail] if ylen > 2 * TILE else [head, tail], axis=0)

    own = []
    for k in range(zlen + 1):
        layer = jnp.where(first_core, h[k], 0.0)
        own.append(with_ends(layer, ends(y_in[REACH * k : REACH * (k + 1)], y_side, first_core)))
    come = []
    for k in range(zlen):
        part = slice(REACH * k, REACH * (k + 1))
        layer = jnp.where(z_side, z_in[k], 0.0)
        come.append(with_ends(layer, ends(d_in[part], z_side & d_side, d_next), ends(e_in[part], z_side & e_side, e_next)))
    below = [jnp.where(first_core, 0.0, layer) for layer in come[zlen - REACH :]]
    above = [jnp.where(first_core, layer, 0.0) for layer in come]
    layers = below[:-1] + [below[-1] + own[0]] + own[1:-1] + [own[-1] + above[0]] + above[1:]
    for z, layer in enumerate(spread_layers(layers)):
        out[z] = layer


def sum_kernel(part, other, out):
    out[...] = part[...] + other[...]


def call(kernel, outs, args, scratch=(), space=pltpu.VMEM):
    shapes = [jax.ShapeDtypeStruct(out, jnp.float32) if isinstance(out, tuple) else out for out in outs]
    return pl.pallas_call(
        kernel,
        out_shape=shapes,
        in_specs=[pl.BlockSpec(memory_space=space)] * len(args),
        out_specs=[pl.BlockSpec(memory_space=pltpu.VMEM)] * len(outs),
        scratch_shapes=list(scratch),
        compiler_params=pltpu.CompilerParams(vmem_limit_bytes=32 * 1024 * 1024),
    )(*args)


def ring_moved(value, axis):
    size = lax.axis_size(axis)
    return lax.ppermute(value, axis, [((k + 1) % size, k) for k in range(size)])


def chip_swapped(value):
    cores = lax.axis_size("load")
    return lax.ppermute(value, "load", [(core, cores - 1 - core) for core in range(cores)])


def opposed(value, z_step, y_step, y_shift=0, start=None):
    cores, rows, size = lax.axis_size("load"), lax.axis_size("sy"), lax.axis_size("sz")
    pairs = []
    for core in range(cores):
        sign = -1 if core else 1
        for y in range(rows):
            for z in range(size):
                to_y, to_z, side = y + sign * y_step, z + sign * z_step, core
                if start is not None:
                    to_y = y + 1 if (y - start) % 2 == 0 else y - 1
                if not (0 <= to_y < rows and 0 <= to_z < size):
                    to_y, to_z, side = y, z, cores - 1 - core
                to_y = (to_y + y_shift) % rows
                pairs.append(((core * rows + y) * size + z, (side * rows + to_y) * size + to_z))
    return lax.ppermute(value, ("load", "sy", "sz"), pairs)


def body(displacements, density, solid, fixed):
    loads, comps, zlen, ylen, xlen = displacements.shape
    planes = loads * comps
    totals = (zlen * lax.axis_size("sz"), ylen * lax.axis_size("sy"))
    args = [
        pltpu.with_memory_space_constraint(arg, pltpu.HBM) for arg in (displacements, fixed, density, solid)
    ]

    d_send, z_send, y_send = call(
        lambda *refs: lead_kernel(totals, *refs),
        [(-(-planes // TILE) * TILE, xlen), (planes + 1, ylen, xlen), (planes * zlen, xlen)],
        args,
        scratch=[
            pltpu.VMEM((loads, comps, ylen, xlen), jnp.float32),
            pltpu.VMEM((ylen, xlen), jnp.int32),
            pltpu.VMEM((ylen, xlen), jnp.float32),
            pltpu.VMEM((ylen, xlen), jnp.int32),
            pltpu.VMEM((loads, comps, zlen, 1, xlen), jnp.float32),
            pltpu.VMEM((zlen, 1, xlen), jnp.int32),
            pltpu.SemaphoreType.DMA((6,)),
        ],
        space=pltpu.HBM,
    )
    d_in = opposed(d_send, -1, 0, y_shift=-1)
    z_in = opposed(z_send, -1, 0)
    y_in = ring_moved(y_send, "sy")
    faces = lambda layers: pltpu.VMEM((4, planes, layers, ylen, xlen), jnp.float32)
    inner = call(
        lambda *refs: inner_kernel(totals, *refs),
        [
            (zlen, ylen, xlen),
            (2, planes * zlen, xlen),
            (2, REACH * (zlen - 1), xlen),
            (4, planes, ylen, xlen),
            (ylen, xlen),
            (TILE, xlen),
        ],
        (displacements, fixed, density, solid),
        scratch=[faces(zlen), pltpu.VMEM((zlen - 1, ylen + 2 * TILE, xlen), jnp.float32)],
    )
    reach = REACH * zlen
    shape = displacements.shape
    share, corner = call(
        lambda *refs: outer_kernel(shape, *refs),
        [(ylen * zlen + 2 * reach, xlen), (4, -(-(planes + 1) // TILE) * TILE, xlen)],
        (z_in, y_in, *inner),
        scratch=[
            faces(4),
            pltpu.VMEM((ylen + 2 * TILE, xlen), jnp.float32),
            pltpu.VMEM((ylen, xlen), jnp.float32),
        ],
    )
    (share,) = call(
        lambda *refs: corner_kernel(shape, *refs), [(ylen * zlen + 2 * reach, xlen)], (share, corner, y_in, d_in)
    )
    sent = (-(-(reach + REACH) // TILE) * TILE, xlen)
    h, z_send, y_send, d_send, e_send = call(
        lambda *refs: total_kernel(displacements.shape, *refs),
        [
            (zlen + 1, ylen, xlen),
            (zlen, ylen, xlen),
            sent,
            sent,
            sent,
        ],
        (share, chip_swapped(share)),
    )
    d_in = opposed(d_send, -1, 0, start=1)
    e_in = opposed(e_send, -1, 0, start=0)
    y_in = opposed(y_send, 0, -1)
    z_in = opposed(z_send, -1, 0)
    (part,) = call(layers_kernel, [(zlen, ylen, xlen)], (h, d_in, e_in, y_in, z_in))
    (out,) = call(sum_kernel, [(zlen, ylen, xlen)], (part, chip_swapped(part)))
    return out


def solution(mesh):
    return jax.shard_map(
        body,
        mesh=mesh,
        in_specs=(
            P("load", None, "sz", "sy", None),
            P("sz", "sy", None),
            P("sz", "sy", None),
            P("sz", "sy", None),
        ),
        out_specs=P("sz", "sy", None),
        check_vma=False,
    )
```

```python
import jax
import jax.numpy as jnp
import numpy as np
from jax import lax
from jax.experimental import pallas as pl
from jax.experimental.pallas import tpu as pltpu
from jax.sharding import PartitionSpec as P

OFFSETS = [(0, 0, 0), (1, 0, 0), (1, 1, 0), (0, 1, 0), (0, 0, 1), (1, 0, 1), (1, 1, 1), (0, 1, 1)]
REACH = 3
ROWS = REACH + 1
TILE = 8
LANES = 128


def element_matrix():
    corners = np.array(
        [
            [-1.0, -1.0, -1.0],
            [1.0, -1.0, -1.0],
            [1.0, 1.0, -1.0],
            [-1.0, 1.0, -1.0],
            [-1.0, -1.0, 1.0],
            [1.0, -1.0, 1.0],
            [1.0, 1.0, 1.0],
            [-1.0, 1.0, 1.0],
        ]
    )
    poisson = 0.3
    lame = poisson / ((1.0 + poisson) * (1.0 - 2.0 * poisson))
    shear = 1.0 / (2.0 * (1.0 + poisson))
    elastic = np.zeros((6, 6))
    elastic[:3, :3] = lame
    for k in range(3):
        elastic[k, k] += 2.0 * shear
        elastic[3 + k, 3 + k] = shear
    gauss = 1.0 / np.sqrt(3.0)
    stiffness = np.zeros((24, 24))
    for gi in range(2):
        for gj in range(2):
            for gk in range(2):
                point = np.array([(2 * gi - 1) * gauss, (2 * gj - 1) * gauss, (2 * gk - 1) * gauss])
                strain = np.zeros((6, 24))
                for node in range(8):
                    grads = np.zeros(3)
                    for k in range(3):
                        value = corners[node, k] / 8.0
                        for m in range(3):
                            if m != k:
                                value = value * (1.0 + point[m] * corners[node, m])
                        grads[k] = 2.0 * value
                    col = 3 * node
                    strain[0, col] = grads[0]
                    strain[1, col + 1] = grads[1]
                    strain[2, col + 2] = grads[2]
                    strain[3, col] = grads[1]
                    strain[3, col + 1] = grads[0]
                    strain[4, col + 1] = grads[2]
                    strain[4, col + 2] = grads[1]
                    strain[5, col] = grads[2]
                    strain[5, col + 2] = grads[0]
                stiffness += strain.T @ elastic @ strain / 8.0
    return stiffness


def mode_weights():
    modes = [(i, j, k) for k in (0, 1) for j in (0, 1) for i in (0, 1)]
    sums = np.zeros((24, 24))
    for m, mode in enumerate(modes):
        for n, corner in enumerate(OFFSETS):
            sign = np.prod([(1 if corner[d] else -1) if mode[d] else 1 for d in range(3)])
            for comp in range(3):
                sums[3 * m + comp, 3 * n + comp] = sign
    form = sums @ element_matrix() @ sums.T / 64.0

    def at(first, second):
        return form[3 * modes.index(first[1]) + first[0], 3 * modes.index(second[1]) + second[0]]

    ux, vy, uy = (0, (1, 0, 0)), (1, (0, 1, 0)), (0, (0, 1, 0))
    uxy, wyz = (0, (1, 1, 0)), (2, (0, 1, 1))
    wxy, vxz, uxyz = (2, (1, 1, 0)), (1, (1, 0, 1)), (0, (1, 1, 1))
    return dict(
        normal=at(ux, ux) - at(ux, vy),
        trace=at(ux, vy),
        shear=at(uy, uy),
        plus=(at(uxy, uxy) + at(uxy, wyz)) / 2,
        minus=(at(uxy, uxy) - at(uxy, wyz)) / 2,
        twist=at(wxy, wxy) - at(wxy, vxz),
        twist_sum=at(wxy, vxz),
        corner=at(uxyz, uxyz),
    )


def square(value):
    return value * value


def quadratic(low, high, weights):
    x = [low[c][1] + high[c][1] for c in range(3)]
    y = [low[c][2] + high[c][2] for c in range(3)]
    z = [high[c][0] - low[c][0] for c in range(3)]
    xy = [low[c][3] + high[c][3] for c in range(3)]
    xz = [high[c][1] - low[c][1] for c in range(3)]
    yz = [high[c][2] - low[c][2] for c in range(3)]
    xyz = [high[c][3] - low[c][3] for c in range(3)]
    normal = square(x[0]) + square(y[1]) + square(z[2])
    trace = square(x[0] + y[1] + z[2])
    shear = square(y[0] + x[1]) + square(z[0] + x[2]) + square(z[1] + y[2])
    pairs = ((xy[0], yz[2]), (xy[1], xz[2]), (xz[0], yz[1]))
    plus = sum(square(p + q) for p, q in pairs)
    minus = sum(square(p - q) for p, q in pairs)
    twist = square(xy[2]) + square(xz[1]) + square(yz[0])
    twist_sum = square(xy[2] + xz[1] + yz[0])
    corner = square(xyz[0]) + square(xyz[1]) + square(xyz[2])
    groups = dict(
        normal=normal, trace=trace, shear=shear, plus=plus, minus=minus, twist=twist, twist_sum=twist_sum, corner=corner
    )
    return sum(np.float32(weights[name]) * group for name, group in groups.items())


def line_weight(coord, count):
    def outside(distance):
        missing = jnp.maximum(REACH - distance, 0)
        return missing * (missing + 1) // 2

    whole = (REACH + 1) * (REACH + 1)
    return (whole - outside(coord) - outside(count - 1 - coord)).astype(jnp.float32)


def voxel_factor(density, solid, plane, first_row, total_z, total_y):
    rows, length = density.shape
    row = lax.broadcasted_iota(jnp.int32, (rows, length), 0) + first_row
    column = lax.broadcasted_iota(jnp.int32, (rows, length), 1)
    weight = line_weight(row, total_y) * line_weight(column, length)
    weight = weight * line_weight(jnp.full((rows, length), plane, jnp.int32), total_z)
    return solid.astype(jnp.float32) * (-3.0 * density * density) / weight


def spread_x(value):
    rows, length = value.shape
    wide = jnp.concatenate([value, jnp.zeros((rows, LANES), jnp.float32)], axis=1)
    span = length + LANES
    total = float(ROWS) * value
    for step in range(1, ROWS):
        both = pltpu.roll(wide, span - step, 1) + pltpu.roll(wide, step, 1)
        total = total + float(ROWS - step) * both[:, :length]
    return total


def spread_layers(layers):
    for step in (1, 2, 1, 2):
        layers = [layers[k] + layers[k + step] for k in range(len(layers) - step)]
    return layers


def held(disp, fixed, case, comp, z, rows):
    return disp[case, comp, z, rows] * (1.0 - fixed[z, rows].astype(jnp.float32))


def split_x(value):
    length = value.shape[1]
    column = lax.broadcasted_iota(jnp.int32, value.shape, 1)
    ahead = jnp.where(column == length - 1, 0.0, pltpu.roll(value, length - 1, 1))
    return value + ahead, ahead - value


def face_sums(value):
    following = pltpu.roll(value, value.shape[0] - 1, 0)
    both, along_x = split_x(value + following)
    along_y, mixed = split_x(following - value)
    return both, along_x, along_y, mixed


def spread_y(quotient, ylen):
    rows = [quotient[TILE + step : TILE + step + ylen] for step in range(-REACH, REACH + 1)]
    return sum((ROWS - abs(k - REACH)) * rows[k] for k in range(2 * REACH + 1))


def to_neighbours(quotient, ylen):
    top = quotient[ylen : ylen + TILE]
    base = quotient[TILE : 2 * TILE]
    ahead, back = [], []
    for row in range(REACH):
        ahead.append(sum(float(REACH - row - k) * top[TILE - 1 - k : TILE - k] for k in range(REACH - row)))
        back.append(sum(float(row + 1 - k) * base[k : k + 1] for k in range(row + 1)))
    return ahead, back


def next_is_partner(start):
    return (lax.axis_index("sy") - start) % 2 == 0


def on_first():
    return lax.axis_index("load") == 0


def lead_kernel(totals, disp_hbm, fixed_hbm, density_hbm, solid_hbm, d_out, z_out, y_out, layer, layer_fixed, density, solid, rows, rows_fixed, sems):
    loads, comps, zlen, ylen, _ = disp_hbm.shape
    gives = jnp.where(on_first(), 0, zlen - 1)
    copies = [
        pltpu.make_async_copy(source, target, sems.at[k])
        for k, (source, target) in enumerate(
            (
                (density_hbm.at[gives], density),
                (solid_hbm.at[gives], solid),
                (fixed_hbm.at[gives], layer_fixed),
                (disp_hbm.at[:, :, gives], layer),
                (fixed_hbm.at[:, :1], rows_fixed),
                (disp_hbm.at[:, :, :, :1], rows),
            )
        )
    ]
    for copy in copies:
        copy.start()
    for copy in copies[:2]:
        copy.wait()
    plane = lax.axis_index("sz") * zlen + gives
    base_y = lax.axis_index("sy") * ylen
    d_out[...] = jnp.zeros(d_out.shape, jnp.float32)
    z_out[loads * comps] = voxel_factor(density[...], solid[...], plane, base_y, *totals)
    for copy in copies[2:4]:
        copy.wait()
    free = 1.0 - layer_fixed[...].astype(jnp.float32)
    for case in range(loads):
        for comp in range(comps):
            k = case * comps + comp
            z_out[k] = layer[case, comp] * free
            d_out[k : k + 1] = z_out[k, :1]
    for copy in copies[4:]:
        copy.wait()
    for z in range(zlen):
        free = 1.0 - rows_fixed[z, :1].astype(jnp.float32)
        for case in range(loads):
            for comp in range(comps):
                at = (comp * loads + case) * zlen + z
                y_out[at : at + 1] = rows[case, comp, z, :1] * free


def tile_energies(faces, first, lanes, layers, loads, comps, base=0):
    weights = mode_weights()
    energy = [None] * layers
    for case in range(loads):
        low = None
        for z in range(layers + 1):
            planes = [case * comps + comp for comp in range(comps)]
            high = [[faces[kind, k, base + z, first : first + TILE, lanes] for kind in range(4)] for k in planes]
            if low is not None:
                part = quadratic(low, high, weights)
                energy[z - 1] = part if energy[z - 1] is None else energy[z - 1] + part
            low = high
    return energy


def blank_last(value, first, ylen):
    row = lax.broadcasted_iota(jnp.int32, value.shape, 0) + first
    return jnp.where(row == ylen - 1, 0.0, value)


def inner_kernel(totals, disp, fixed, density, solid, own, line, sends, last_faces, last_factor, edge, faces, quotient):
    loads, comps, zlen, ylen, xlen = disp.shape
    total_z, total_y = totals
    base_z = lax.axis_index("sz") * zlen
    base_y = lax.axis_index("sy") * ylen
    inner = zlen - 1
    keeps = jnp.where(on_first(), inner, 0)
    free = [1.0 - fixed[z].astype(jnp.float32) for z in range(zlen)]

    for k in range(loads * comps):
        case, comp = k // comps, k % comps
        for z in range(zlen):
            plane = disp[case, comp, z] * free[z]
            for kind, value in enumerate(face_sums(plane)):
                faces[kind, k, z] = value
            at = (comp * loads + case) * zlen + z
            line[0, at : at + 1] = plane[ylen - 1 :]
        for kind in range(4):
            last_faces[kind, k] = faces[kind, k, keeps]

    line[0], line[1] = split_x(line[0])

    zeros = jnp.zeros((TILE, xlen), jnp.float32)
    edge[...] = jnp.zeros(edge.shape, jnp.float32)
    for z in range(zlen):
        factor = voxel_factor(density[z], solid[z], base_z + z, base_y, total_z, total_y)
        edge[z : z + 1] = factor[ylen - 1 :]
        if z == inner:
            last_factor[...] = factor
        else:
            quotient[z, :TILE] = zeros
            quotient[z, TILE : TILE + ylen] = factor
            quotient[z, TILE + ylen :] = zeros

    for first in range(0, ylen, TILE):

        @pl.loop(0, xlen // LANES, unroll=True)
        def _(chunk):
            lanes = pl.ds(pl.multiple_of(chunk * LANES, LANES), LANES)
            energy = tile_energies(faces, first, lanes, inner, loads, comps)
            for z in range(inner):
                here = quotient[z, first + TILE : first + 2 * TILE, lanes]
                quotient[z, first + TILE : first + 2 * TILE, lanes] = blank_last(energy[z] * here, first, ylen)

    for z in range(inner):
        own[z] = spread_x(spread_y(quotient.at[z], ylen))
        ahead, back = to_neighbours(quotient.at[z], ylen)
        ends = spread_x(jnp.concatenate(ahead + back + [zeros[:2]], axis=0))
        sends[0, REACH * z : REACH * (z + 1)] = ends[:REACH]
        sends[1, REACH * z : REACH * (z + 1)] = ends[REACH : 2 * REACH]


def outer_kernel(
    shape, z_in, y_in, own_in, line, sends, last_faces, last_factor, edge, share, corner, faces, quotient, factor
):
    loads, comps, zlen, ylen, xlen = shape
    planes = loads * comps
    inner = zlen - 1
    first_core, index = on_first(), lax.axis_index("sz")
    top = first_core & (index == lax.axis_size("sz") - 1)
    more = lax.axis_index("sy") < lax.axis_size("sy") - 1
    stays, comes = jnp.where(first_core, 0, 1), jnp.where(first_core, jnp.where(top, 2, 1), 0)
    y_plus, y_diff = split_x(jnp.where(more, y_in[...], 0.0))
    come_rows = []
    for k in range(planes):
        for kind, value in enumerate(face_sums(z_in[k])):
            faces[kind, k, stays] = last_faces[kind, k]
            faces[kind, k, comes] = value
        come_rows.append(z_in[k, ylen - 1 :])
        at = (k % comps * loads + k // comps) * zlen
        for group in range(2):
            corner[group, k : k + 1] = jnp.where(first_core, line[group, at + inner : at + zlen], line[group, at : at + 1])
    come_rows.append(jnp.zeros((-planes % TILE, xlen), jnp.float32))
    for group, value in enumerate(split_x(jnp.concatenate(come_rows, axis=0))):
        corner[2 + group, :planes] = value[:planes]
    below = jnp.where(index > 0, z_in[planes], 0.0)
    factor[...] = jnp.where(first_core, last_factor[...], below)
    corner[0, planes : planes + 1] = factor[ylen - 1 :]

    @pl.when(top)
    def _():
        clamped = jnp.zeros((ylen, xlen), jnp.float32)
        for k in range(planes):
            for slot in (1, 3):
                for kind in range(4):
                    faces[kind, k, slot] = clamped

    zeros = jnp.zeros((TILE, xlen), jnp.float32)
    quotient[:TILE] = zeros
    quotient[TILE + ylen :] = zeros
    for first in range(0, ylen, TILE):

        @pl.loop(0, xlen // LANES, unroll=True)
        def _(chunk):
            lanes = pl.ds(pl.multiple_of(chunk * LANES, LANES), LANES)
            (energy,) = tile_energies(faces, first, lanes, 1, loads, comps)
            here = energy * factor[first : first + TILE, lanes]
            quotient[first + TILE : first + 2 * TILE, lanes] = blank_last(here, first, ylen)

    @pl.when(top)
    def _():
        for first in range(0, ylen, TILE):

            @pl.loop(0, xlen // LANES, unroll=True)
            def _(chunk):
                lanes = pl.ds(pl.multiple_of(chunk * LANES, LANES), LANES)
                (energy,) = tile_energies(faces, first, lanes, 1, loads, comps, base=2)
                here = energy * factor[first : first + TILE, lanes]
                quotient[first + TILE : first + 2 * TILE, lanes] += blank_last(here, first, ylen)

    count = loads * zlen
    low, high = [], []
    for comp in range(comps):
        part = slice(comp * count, (comp + 1) * count)
        whole, change = line[0, part], line[1, part]
        whole_next, change_next = y_plus[part], y_diff[part]
        face = (whole + whole_next, change + change_next, whole_next - whole, change_next - change)
        low.append(face)
        high.append([pltpu.roll(value, count - 1, 0) for value in face])
    energy = quadratic(low, high, mode_weights())
    energy = sum(energy[case * zlen : case * zlen + inner] for case in range(loads)) * edge[:inner]
    last = spread_x(jnp.concatenate([energy, jnp.zeros((TILE - inner, xlen), jnp.float32)], axis=0))

    row = lax.broadcasted_iota(jnp.int32, (TILE, xlen), 0)
    rising = jnp.maximum(row - (TILE - 1 - ROWS), 0).astype(jnp.float32)
    ups, downs = [], []
    for z in range(inner):
        share[ylen * z : ylen * (z + 1)] = own_in[z]
        share[ylen * (z + 1) - TILE : ylen * (z + 1)] += rising * last[z : z + 1]
        here = sends[0, REACH * z : REACH * (z + 1)]
        ups += [here[r : r + 1] + float(REACH - r) * last[z : z + 1] for r in range(REACH)]
        downs.append(sends[1, REACH * z : REACH * (z + 1)])
    share[ylen * inner : ylen * zlen] = spread_x(spread_y(quotient, ylen))
    ahead, back = to_neighbours(quotient, ylen)
    ends = spread_x(jnp.concatenate(ahead + back + [zeros[:2]], axis=0))
    share[ylen * zlen :] = jnp.concatenate(ups + [ends[:REACH]] + downs + [ends[REACH : 2 * REACH]], axis=0)


def corner_line(shape, corner, y_in, d_in):
    loads, comps, zlen, ylen, xlen = shape
    planes = loads * comps
    first_core = on_first()
    top = first_core & (lax.axis_index("sz") == lax.axis_size("sz") - 1)
    more = lax.axis_index("sy") < lax.axis_size("sy") - 1
    rows = []
    for k in range(planes):
        at = (k % comps * loads + k // comps) * zlen
        rows.append(jnp.where(first_core, y_in[at + zlen - 1 : at + zlen], y_in[at : at + 1]))
    rows.append(jnp.zeros((-planes % TILE, xlen), jnp.float32))
    stays_next = split_x(jnp.where(more, jnp.concatenate(rows, axis=0), 0.0))
    comes_next = split_x(jnp.where(more, d_in[...], 0.0))

    def faces(stays, comes, comp):
        zero = jnp.zeros((1, xlen), jnp.float32)
        under, over = [], []
        for own, other in zip(stays, comes):
            own, other = ([value[case * comps + comp : case * comps + comp + 1] for case in range(loads)] for value in (own, other))
            low = [jnp.where(first_core, a, b) for a, b in zip(own, other)] + [jnp.where(top, b, 0.0) for b in other]
            high = [jnp.where(first_core, jnp.where(top, 0.0, b), a) for a, b in zip(own, other)] + [zero] * loads
            under.append(jnp.concatenate(low, axis=0))
            over.append(jnp.concatenate(high, axis=0))
        return under, over

    low, high = [], []
    for comp in range(comps):
        near = faces((corner[0], corner[1]), (corner[2], corner[3]), comp)
        far = faces(stays_next, comes_next, comp)
        for (whole, change), (whole_next, change_next), into in zip(near, far, (low, high)):
            into.append((whole + whole_next, change + change_next, whole_next - whole, change_next - change))
    energy = quadratic(low, high, mode_weights())
    line = sum(energy[case : case + 1] for case in range(2 * loads)) * corner[0, planes : planes + 1]
    return spread_x(jnp.concatenate([line, jnp.zeros((TILE - 1, xlen), jnp.float32)], axis=0))[:1]


def corner_kernel(shape, share_in, corner, y_in, d_in, share):
    _, _, zlen, ylen, xlen = shape
    line = corner_line(shape, corner, y_in, d_in)
    rising = jnp.maximum(lax.broadcasted_iota(jnp.int32, (TILE, xlen), 0) - (TILE - 1 - ROWS), 0).astype(jnp.float32)
    falling = (REACH - lax.broadcasted_iota(jnp.int32, (REACH, xlen), 0)).astype(jnp.float32)
    share[...] = share_in[...]
    share[ylen * zlen - TILE : ylen * zlen] += rising * line
    share[ylen * zlen + REACH * (zlen - 1) : ylen * zlen + REACH * zlen] += falling * line


def total_kernel(shape, share, other, h_out, z_out, y_out, d_out, e_out):
    _, _, zlen, ylen, xlen = shape
    first_core = on_first()
    inner, rows = zlen - 1, ylen * zlen
    reach = REACH * zlen

    def layers(first, count):
        mine, theirs = share[first + inner * count : first + zlen * count], other[first + inner * count : first + zlen * count]
        middle = share[first : first + inner * count] + other[first : first + inner * count]
        return jnp.where(first_core, theirs, mine), middle, jnp.where(first_core, mine, theirs)

    lowest, middle, highest = layers(0, ylen)
    h_out[0] = lowest
    for z in range(inner):
        h_out[z + 1] = middle[ylen * z : ylen * (z + 1)]
    h_out[zlen] = highest
    z_out[...] = h_out[pl.ds(jnp.where(first_core, 0, 1), zlen)]
    ups = jnp.concatenate(layers(rows, REACH), axis=0)
    downs = jnp.concatenate(layers(rows + reach, REACH), axis=0)
    y_out[: reach + REACH] = jnp.where(next_is_partner(lax.axis_index("load")), ups, downs)
    for out, used in ((y_out, reach + REACH), (d_out, reach), (e_out, reach)):
        out[used:] = jnp.zeros((out.shape[0] - used, xlen), jnp.float32)
    for out, start in ((d_out, 1), (e_out, 0)):
        rows = jnp.where(next_is_partner(start), ups, downs)
        out[:reach] = jnp.where(first_core, rows[:reach], rows[REACH:])


def layers_kernel(h, d_in, e_in, y_in, z_in, out):
    zlen, ylen, xlen = out.shape
    reach = REACH * zlen
    first_core = on_first()
    z_index, z_last = lax.axis_index("sz"), lax.axis_size("sz") - 1
    y_index, y_last = lax.axis_index("sy"), lax.axis_size("sy") - 1
    z_side = jnp.where(first_core, z_index < z_last, z_index > 0)
    y_next = next_is_partner(lax.axis_index("load"))
    y_side = jnp.where(y_next, y_index < y_last, y_index > 0)
    d_next, e_next = next_is_partner(1), next_is_partner(0)
    d_side, e_side = (jnp.where(up, y_index < y_last, y_index > 0) for up in (d_next, e_next))
    blank = jnp.zeros((TILE - REACH, xlen), jnp.float32)

    def at_start(rows):
        return jnp.concatenate([rows, blank], axis=0)

    def at_end(rows):
        return jnp.concatenate([blank, rows], axis=0)

    def ends(rows, keep, at_last):
        rows = jnp.where(keep, rows, 0.0)
        return at_start(jnp.where(at_last, 0.0, rows)), at_end(jnp.where(at_last, rows, 0.0))

    def with_ends(layer, *pairs):
        head, tail = layer[:TILE], layer[ylen - TILE :]
        for first, last in pairs:
            head, tail = head + first, tail + last
        return jnp.concatenate([head, layer[TILE : ylen - TILE], tail] if ylen > 2 * TILE else [head, tail], axis=0)

    own = []
    for k in range(zlen + 1):
        layer = jnp.where(first_core, h[k], 0.0)
        own.append(with_ends(layer, ends(y_in[REACH * k : REACH * (k + 1)], y_side, y_next)))
    come = []
    for k in range(zlen):
        part = slice(REACH * k, REACH * (k + 1))
        layer = jnp.where(z_side, z_in[k], 0.0)
        come.append(with_ends(layer, ends(d_in[part], z_side & d_side, d_next), ends(e_in[part], z_side & e_side, e_next)))
    below = [jnp.where(first_core, 0.0, layer) for layer in come[zlen - REACH :]]
    above = [jnp.where(first_core, layer, 0.0) for layer in come]
    layers = below[:-1] + [below[-1] + own[0]] + own[1:-1] + [own[-1] + above[0]] + above[1:]
    for z, layer in enumerate(spread_layers(layers)):
        out[z] = layer


def sum_kernel(part, other, out):
    out[...] = part[...] + other[...]


def call(kernel, outs, args, scratch=(), space=pltpu.VMEM):
    shapes = [jax.ShapeDtypeStruct(out, jnp.float32) if isinstance(out, tuple) else out for out in outs]
    return pl.pallas_call(
        kernel,
        out_shape=shapes,
        in_specs=[pl.BlockSpec(memory_space=space)] * len(args),
        out_specs=[pl.BlockSpec(memory_space=pltpu.VMEM)] * len(outs),
        scratch_shapes=list(scratch),
        compiler_params=pltpu.CompilerParams(vmem_limit_bytes=32 * 1024 * 1024),
    )(*args)


def ring_moved(value, axis):
    size = lax.axis_size(axis)
    return lax.ppermute(value, axis, [((k + 1) % size, k) for k in range(size)])


def chip_swapped(value):
    cores = lax.axis_size("load")
    return lax.ppermute(value, "load", [(core, cores - 1 - core) for core in range(cores)])


def opposed(value, z_step, y_step, y_shift=0, start=None):
    cores, rows, size = lax.axis_size("load"), lax.axis_size("sy"), lax.axis_size("sz")
    pairs = []
    for core in range(cores):
        sign = -1 if core else 1
        for y in range(rows):
            for z in range(size):
                to_y, to_z, side = y + sign * y_step, z + sign * z_step, core
                if start is not None:
                    to_y = y + 1 if (y - start) % 2 == 0 else y - 1
                if not (0 <= to_y < rows and 0 <= to_z < size):
                    to_y, to_z, side = y, z, cores - 1 - core
                to_y = (to_y + y_shift) % rows
                pairs.append(((core * rows + y) * size + z, (side * rows + to_y) * size + to_z))
    return lax.ppermute(value, ("load", "sy", "sz"), pairs)


def beside(value):
    cores, rows, size = lax.axis_size("load"), lax.axis_size("sy"), lax.axis_size("sz")
    pairs = []
    for core in range(cores):
        for y in range(rows):
            to_y = y + 1 if (y - core) % 2 == 0 else y - 1
            for z in range(size):
                target = (to_y, z) if 0 <= to_y < rows else (y, z ^ 1)
                pairs.append(((core * rows + y) * size + z, (core * rows + target[0]) * size + target[1]))
    return lax.ppermute(value, ("load", "sy", "sz"), pairs)


def body(displacements, density, solid, fixed):
    loads, comps, zlen, ylen, xlen = displacements.shape
    planes = loads * comps
    totals = (zlen * lax.axis_size("sz"), ylen * lax.axis_size("sy"))
    args = [
        pltpu.with_memory_space_constraint(arg, pltpu.HBM) for arg in (displacements, fixed, density, solid)
    ]

    d_send, z_send, y_send = call(
        lambda *refs: lead_kernel(totals, *refs),
        [(-(-planes // TILE) * TILE, xlen), (planes + 1, ylen, xlen), (planes * zlen, xlen)],
        args,
        scratch=[
            pltpu.VMEM((loads, comps, ylen, xlen), jnp.float32),
            pltpu.VMEM((ylen, xlen), jnp.int32),
            pltpu.VMEM((ylen, xlen), jnp.float32),
            pltpu.VMEM((ylen, xlen), jnp.int32),
            pltpu.VMEM((loads, comps, zlen, 1, xlen), jnp.float32),
            pltpu.VMEM((zlen, 1, xlen), jnp.int32),
            pltpu.SemaphoreType.DMA((6,)),
        ],
        space=pltpu.HBM,
    )
    d_in = opposed(d_send, -1, 0, y_shift=-1)
    z_in = opposed(z_send, -1, 0)
    y_in = ring_moved(y_send, "sy")
    faces = lambda layers: pltpu.VMEM((4, planes, layers, ylen, xlen), jnp.float32)
    inner = call(
        lambda *refs: inner_kernel(totals, *refs),
        [
            (zlen, ylen, xlen),
            (2, planes * zlen, xlen),
            (2, REACH * (zlen - 1), xlen),
            (4, planes, ylen, xlen),
            (ylen, xlen),
            (TILE, xlen),
        ],
        (displacements, fixed, density, solid),
        scratch=[faces(zlen), pltpu.VMEM((zlen - 1, ylen + 2 * TILE, xlen), jnp.float32)],
    )
    reach = REACH * zlen
    shape = displacements.shape
    share, corner = call(
        lambda *refs: outer_kernel(shape, *refs),
        [(ylen * zlen + 2 * reach, xlen), (4, -(-(planes + 1) // TILE) * TILE, xlen)],
        (z_in, y_in, *inner),
        scratch=[
            faces(4),
            pltpu.VMEM((ylen + 2 * TILE, xlen), jnp.float32),
            pltpu.VMEM((ylen, xlen), jnp.float32),
        ],
    )
    (share,) = call(
        lambda *refs: corner_kernel(shape, *refs), [(ylen * zlen + 2 * reach, xlen)], (share, corner, y_in, d_in)
    )
    sent = (-(-(reach + REACH) // TILE) * TILE, xlen)
    h, z_send, y_send, d_send, e_send = call(
        lambda *refs: total_kernel(displacements.shape, *refs),
        [
            (zlen + 1, ylen, xlen),
            (zlen, ylen, xlen),
            sent,
            sent,
            sent,
        ],
        (share, chip_swapped(share)),
    )
    d_in = opposed(d_send, -1, 0, start=1)
    e_in = opposed(e_send, -1, 0, start=0)
    y_in = beside(y_send)
    z_in = opposed(z_send, -1, 0)
    (part,) = call(layers_kernel, [(zlen, ylen, xlen)], (h, d_in, e_in, y_in, z_in))
    (out,) = call(sum_kernel, [(zlen, ylen, xlen)], (part, chip_swapped(part)))
    return out


def solution(mesh):
    return jax.shard_map(
        body,
        mesh=mesh,
        in_specs=(
            P("load", None, "sz", "sy", None),
            P("sz", "sy", None),
            P("sz", "sy", None),
            P("sz", "sy", None),
        ),
        out_specs=P("sz", "sy", None),
        check_vma=False,
    )
```

```python
import jax
import jax.numpy as jnp
import numpy as np
from jax import lax
from jax.experimental import pallas as pl
from jax.experimental.pallas import tpu as pltpu
from jax.sharding import PartitionSpec as P

OFFSETS = [(0, 0, 0), (1, 0, 0), (1, 1, 0), (0, 1, 0), (0, 0, 1), (1, 0, 1), (1, 1, 1), (0, 1, 1)]
REACH = 3
ROWS = REACH + 1
TILE = 8
LANES = 128


def element_matrix():
    corners = np.array(
        [
            [-1.0, -1.0, -1.0],
            [1.0, -1.0, -1.0],
            [1.0, 1.0, -1.0],
            [-1.0, 1.0, -1.0],
            [-1.0, -1.0, 1.0],
            [1.0, -1.0, 1.0],
            [1.0, 1.0, 1.0],
            [-1.0, 1.0, 1.0],
        ]
    )
    poisson = 0.3
    lame = poisson / ((1.0 + poisson) * (1.0 - 2.0 * poisson))
    shear = 1.0 / (2.0 * (1.0 + poisson))
    elastic = np.zeros((6, 6))
    elastic[:3, :3] = lame
    for k in range(3):
        elastic[k, k] += 2.0 * shear
        elastic[3 + k, 3 + k] = shear
    gauss = 1.0 / np.sqrt(3.0)
    stiffness = np.zeros((24, 24))
    for gi in range(2):
        for gj in range(2):
            for gk in range(2):
                point = np.array([(2 * gi - 1) * gauss, (2 * gj - 1) * gauss, (2 * gk - 1) * gauss])
                strain = np.zeros((6, 24))
                for node in range(8):
                    grads = np.zeros(3)
                    for k in range(3):
                        value = corners[node, k] / 8.0
                        for m in range(3):
                            if m != k:
                                value = value * (1.0 + point[m] * corners[node, m])
                        grads[k] = 2.0 * value
                    col = 3 * node
                    strain[0, col] = grads[0]
                    strain[1, col + 1] = grads[1]
                    strain[2, col + 2] = grads[2]
                    strain[3, col] = grads[1]
                    strain[3, col + 1] = grads[0]
                    strain[4, col + 1] = grads[2]
                    strain[4, col + 2] = grads[1]
                    strain[5, col] = grads[2]
                    strain[5, col + 2] = grads[0]
                stiffness += strain.T @ elastic @ strain / 8.0
    return stiffness


def mode_weights():
    modes = [(i, j, k) for k in (0, 1) for j in (0, 1) for i in (0, 1)]
    sums = np.zeros((24, 24))
    for m, mode in enumerate(modes):
        for n, corner in enumerate(OFFSETS):
            sign = np.prod([(1 if corner[d] else -1) if mode[d] else 1 for d in range(3)])
            for comp in range(3):
                sums[3 * m + comp, 3 * n + comp] = sign
    form = sums @ element_matrix() @ sums.T / 64.0

    def at(first, second):
        return form[3 * modes.index(first[1]) + first[0], 3 * modes.index(second[1]) + second[0]]

    ux, vy, uy = (0, (1, 0, 0)), (1, (0, 1, 0)), (0, (0, 1, 0))
    uxy, wyz = (0, (1, 1, 0)), (2, (0, 1, 1))
    wxy, vxz, uxyz = (2, (1, 1, 0)), (1, (1, 0, 1)), (0, (1, 1, 1))
    return dict(
        normal=at(ux, ux) - at(ux, vy),
        trace=at(ux, vy),
        shear=at(uy, uy),
        plus=(at(uxy, uxy) + at(uxy, wyz)) / 2,
        minus=(at(uxy, uxy) - at(uxy, wyz)) / 2,
        twist=at(wxy, wxy) - at(wxy, vxz),
        twist_sum=at(wxy, vxz),
        corner=at(uxyz, uxyz),
    )


def square(value):
    return value * value


def quadratic(low, high, weights):
    x = [low[c][1] + high[c][1] for c in range(3)]
    y = [low[c][2] + high[c][2] for c in range(3)]
    z = [high[c][0] - low[c][0] for c in range(3)]
    xy = [low[c][3] + high[c][3] for c in range(3)]
    xz = [high[c][1] - low[c][1] for c in range(3)]
    yz = [high[c][2] - low[c][2] for c in range(3)]
    xyz = [high[c][3] - low[c][3] for c in range(3)]
    normal = square(x[0]) + square(y[1]) + square(z[2])
    trace = square(x[0] + y[1] + z[2])
    shear = square(y[0] + x[1]) + square(z[0] + x[2]) + square(z[1] + y[2])
    pairs = ((xy[0], yz[2]), (xy[1], xz[2]), (xz[0], yz[1]))
    plus = sum(square(p + q) for p, q in pairs)
    minus = sum(square(p - q) for p, q in pairs)
    twist = square(xy[2]) + square(xz[1]) + square(yz[0])
    twist_sum = square(xy[2] + xz[1] + yz[0])
    corner = square(xyz[0]) + square(xyz[1]) + square(xyz[2])
    groups = dict(
        normal=normal, trace=trace, shear=shear, plus=plus, minus=minus, twist=twist, twist_sum=twist_sum, corner=corner
    )
    return sum(np.float32(weights[name]) * group for name, group in groups.items())


def line_weight(coord, count):
    def outside(distance):
        missing = jnp.maximum(REACH - distance, 0)
        return missing * (missing + 1) // 2

    whole = (REACH + 1) * (REACH + 1)
    return (whole - outside(coord) - outside(count - 1 - coord)).astype(jnp.float32)


def voxel_factor(density, solid, plane, first_row, total_z, total_y):
    rows, length = density.shape
    row = lax.broadcasted_iota(jnp.int32, (rows, length), 0) + first_row
    column = lax.broadcasted_iota(jnp.int32, (rows, length), 1)
    weight = line_weight(row, total_y) * line_weight(column, length)
    weight = weight * line_weight(jnp.full((rows, length), plane, jnp.int32), total_z)
    return solid.astype(jnp.float32) * (-3.0 * density * density) / weight


def spread_x(value):
    rows, length = value.shape
    wide = jnp.concatenate([value, jnp.zeros((rows, LANES), jnp.float32)], axis=1)
    span = length + LANES
    total = float(ROWS) * value
    for step in range(1, ROWS):
        both = pltpu.roll(wide, span - step, 1) + pltpu.roll(wide, step, 1)
        total = total + float(ROWS - step) * both[:, :length]
    return total


def spread_layers(layers):
    for step in (1, 2, 1, 2):
        layers = [layers[k] + layers[k + step] for k in range(len(layers) - step)]
    return layers


def held(disp, fixed, case, comp, z, rows):
    return disp[case, comp, z, rows] * (1.0 - fixed[z, rows].astype(jnp.float32))


def split_x(value):
    length = value.shape[1]
    column = lax.broadcasted_iota(jnp.int32, value.shape, 1)
    ahead = jnp.where(column == length - 1, 0.0, pltpu.roll(value, length - 1, 1))
    return value + ahead, ahead - value


def face_sums(value):
    following = pltpu.roll(value, value.shape[0] - 1, 0)
    both, along_x = split_x(value + following)
    along_y, mixed = split_x(following - value)
    return both, along_x, along_y, mixed


def spread_y(quotient, ylen):
    rows = [quotient[TILE + step : TILE + step + ylen] for step in range(-REACH, REACH + 1)]
    return sum((ROWS - abs(k - REACH)) * rows[k] for k in range(2 * REACH + 1))


def to_neighbours(quotient, ylen):
    top = quotient[ylen : ylen + TILE]
    base = quotient[TILE : 2 * TILE]
    ahead, back = [], []
    for row in range(REACH):
        ahead.append(sum(float(REACH - row - k) * top[TILE - 1 - k : TILE - k] for k in range(REACH - row)))
        back.append(sum(float(row + 1 - k) * base[k : k + 1] for k in range(row + 1)))
    return ahead, back


def next_is_partner(start):
    return (lax.axis_index("sy") - start) % 2 == 0


def on_first():
    return lax.axis_index("load") == 0


def lead_kernel(totals, disp_hbm, fixed_hbm, density_hbm, solid_hbm, d_out, z_out, y_out, layer, layer_fixed, density, solid, rows, rows_fixed, sems):
    loads, comps, zlen, ylen, _ = disp_hbm.shape
    gives = jnp.where(on_first(), 0, zlen - 1)
    copies = [
        pltpu.make_async_copy(source, target, sems.at[k])
        for k, (source, target) in enumerate(
            (
                (density_hbm.at[gives], density),
                (solid_hbm.at[gives], solid),
                (fixed_hbm.at[gives], layer_fixed),
                (disp_hbm.at[:, :, gives], layer),
                (fixed_hbm.at[:, :1], rows_fixed),
                (disp_hbm.at[:, :, :, :1], rows),
            )
        )
    ]
    for copy in copies:
        copy.start()
    for copy in copies[:2]:
        copy.wait()
    plane = lax.axis_index("sz") * zlen + gives
    base_y = lax.axis_index("sy") * ylen
    d_out[...] = jnp.zeros(d_out.shape, jnp.float32)
    z_out[loads * comps] = voxel_factor(density[...], solid[...], plane, base_y, *totals)
    for copy in copies[2:4]:
        copy.wait()
    free = 1.0 - layer_fixed[...].astype(jnp.float32)
    for case in range(loads):
        for comp in range(comps):
            k = case * comps + comp
            z_out[k] = layer[case, comp] * free
            d_out[k : k + 1] = z_out[k, :1]
    for copy in copies[4:]:
        copy.wait()
    for z in range(zlen):
        free = 1.0 - rows_fixed[z, :1].astype(jnp.float32)
        for case in range(loads):
            for comp in range(comps):
                at = (comp * loads + case) * zlen + z
                y_out[at : at + 1] = rows[case, comp, z, :1] * free


def tile_energies(faces, first, lanes, layers, loads, comps, base=0):
    weights = mode_weights()
    energy = [None] * layers
    for case in range(loads):
        low = None
        for z in range(layers + 1):
            planes = [case * comps + comp for comp in range(comps)]
            high = [[faces[kind, k, base + z, first : first + TILE, lanes] for kind in range(4)] for k in planes]
            if low is not None:
                part = quadratic(low, high, weights)
                energy[z - 1] = part if energy[z - 1] is None else energy[z - 1] + part
            low = high
    return energy


def blank_last(value, first, ylen):
    row = lax.broadcasted_iota(jnp.int32, value.shape, 0) + first
    return jnp.where(row == ylen - 1, 0.0, value)


def inner_kernel(totals, disp, fixed, density, solid, own, line, sends, last_faces, last_factor, edge, faces, quotient):
    loads, comps, zlen, ylen, xlen = disp.shape
    total_z, total_y = totals
    base_z = lax.axis_index("sz") * zlen
    base_y = lax.axis_index("sy") * ylen
    inner = zlen - 1
    keeps = jnp.where(on_first(), inner, 0)
    free = [1.0 - fixed[z].astype(jnp.float32) for z in range(zlen)]

    for k in range(loads * comps):
        case, comp = k // comps, k % comps
        for z in range(zlen):
            plane = disp[case, comp, z] * free[z]
            for kind, value in enumerate(face_sums(plane)):
                faces[kind, k, z] = value
            at = (comp * loads + case) * zlen + z
            line[0, at : at + 1] = plane[ylen - 1 :]
        for kind in range(4):
            last_faces[kind, k] = faces[kind, k, keeps]

    line[0], line[1] = split_x(line[0])

    zeros = jnp.zeros((TILE, xlen), jnp.float32)
    edge[...] = jnp.zeros(edge.shape, jnp.float32)
    for z in range(zlen):
        factor = voxel_factor(density[z], solid[z], base_z + z, base_y, total_z, total_y)
        edge[z : z + 1] = factor[ylen - 1 :]
        if z == inner:
            last_factor[...] = factor
        else:
            quotient[z, :TILE] = zeros
            quotient[z, TILE : TILE + ylen] = factor
            quotient[z, TILE + ylen :] = zeros

    for first in range(0, ylen, TILE):

        @pl.loop(0, xlen // LANES, unroll=True)
        def _(chunk):
            lanes = pl.ds(pl.multiple_of(chunk * LANES, LANES), LANES)
            energy = tile_energies(faces, first, lanes, inner, loads, comps)
            for z in range(inner):
                here = quotient[z, first + TILE : first + 2 * TILE, lanes]
                quotient[z, first + TILE : first + 2 * TILE, lanes] = blank_last(energy[z] * here, first, ylen)

    for z in range(inner):
        own[z] = spread_x(spread_y(quotient.at[z], ylen))
        ahead, back = to_neighbours(quotient.at[z], ylen)
        ends = spread_x(jnp.concatenate(ahead + back + [zeros[:2]], axis=0))
        sends[0, REACH * z : REACH * (z + 1)] = ends[:REACH]
        sends[1, REACH * z : REACH * (z + 1)] = ends[REACH : 2 * REACH]


def outer_kernel(
    shape, z_in, y_in, own_in, line, sends, last_faces, last_factor, edge, share, corner, faces, quotient, factor
):
    loads, comps, zlen, ylen, xlen = shape
    planes = loads * comps
    inner = zlen - 1
    first_core, index = on_first(), lax.axis_index("sz")
    top = first_core & (index == lax.axis_size("sz") - 1)
    more = lax.axis_index("sy") < lax.axis_size("sy") - 1
    stays, comes = jnp.where(first_core, 0, 1), jnp.where(first_core, jnp.where(top, 2, 1), 0)
    y_plus, y_diff = split_x(jnp.where(more, y_in[...], 0.0))
    come_rows = []
    for k in range(planes):
        for kind, value in enumerate(face_sums(z_in[k])):
            faces[kind, k, stays] = last_faces[kind, k]
            faces[kind, k, comes] = value
        come_rows.append(z_in[k, ylen - 1 :])
        at = (k % comps * loads + k // comps) * zlen
        for group in range(2):
            corner[group, k : k + 1] = jnp.where(first_core, line[group, at + inner : at + zlen], line[group, at : at + 1])
    come_rows.append(jnp.zeros((-planes % TILE, xlen), jnp.float32))
    for group, value in enumerate(split_x(jnp.concatenate(come_rows, axis=0))):
        corner[2 + group, :planes] = value[:planes]
    below = jnp.where(index > 0, z_in[planes], 0.0)
    factor[...] = jnp.where(first_core, last_factor[...], below)
    corner[0, planes : planes + 1] = factor[ylen - 1 :]

    @pl.when(top)
    def _():
        clamped = jnp.zeros((ylen, xlen), jnp.float32)
        for k in range(planes):
            for slot in (1, 3):
                for kind in range(4):
                    faces[kind, k, slot] = clamped

    zeros = jnp.zeros((TILE, xlen), jnp.float32)
    quotient[:TILE] = zeros
    quotient[TILE + ylen :] = zeros
    for first in range(0, ylen, TILE):

        @pl.loop(0, xlen // LANES, unroll=True)
        def _(chunk):
            lanes = pl.ds(pl.multiple_of(chunk * LANES, LANES), LANES)
            (energy,) = tile_energies(faces, first, lanes, 1, loads, comps)
            here = energy * factor[first : first + TILE, lanes]
            quotient[first + TILE : first + 2 * TILE, lanes] = blank_last(here, first, ylen)

    @pl.when(top)
    def _():
        for first in range(0, ylen, TILE):

            @pl.loop(0, xlen // LANES, unroll=True)
            def _(chunk):
                lanes = pl.ds(pl.multiple_of(chunk * LANES, LANES), LANES)
                (energy,) = tile_energies(faces, first, lanes, 1, loads, comps, base=2)
                here = energy * factor[first : first + TILE, lanes]
                quotient[first + TILE : first + 2 * TILE, lanes] += blank_last(here, first, ylen)

    count = loads * zlen
    low, high = [], []
    for comp in range(comps):
        part = slice(comp * count, (comp + 1) * count)
        whole, change = line[0, part], line[1, part]
        whole_next, change_next = y_plus[part], y_diff[part]
        face = (whole + whole_next, change + change_next, whole_next - whole, change_next - change)
        low.append(face)
        high.append([pltpu.roll(value, count - 1, 0) for value in face])
    energy = quadratic(low, high, mode_weights())
    energy = sum(energy[case * zlen : case * zlen + inner] for case in range(loads)) * edge[:inner]
    last = spread_x(jnp.concatenate([energy, jnp.zeros((TILE - inner, xlen), jnp.float32)], axis=0))

    row = lax.broadcasted_iota(jnp.int32, (TILE, xlen), 0)
    rising = jnp.maximum(row - (TILE - 1 - ROWS), 0).astype(jnp.float32)
    ups, downs = [], []
    for z in range(inner):
        share[ylen * z : ylen * (z + 1)] = own_in[z]
        share[ylen * (z + 1) - TILE : ylen * (z + 1)] += rising * last[z : z + 1]
        here = sends[0, REACH * z : REACH * (z + 1)]
        ups += [here[r : r + 1] + float(REACH - r) * last[z : z + 1] for r in range(REACH)]
        downs.append(sends[1, REACH * z : REACH * (z + 1)])
    share[ylen * inner : ylen * zlen] = spread_x(spread_y(quotient, ylen))
    ahead, back = to_neighbours(quotient, ylen)
    ends = spread_x(jnp.concatenate(ahead + back + [zeros[:2]], axis=0))
    share[ylen * zlen :] = jnp.concatenate(ups + [ends[:REACH]] + downs + [ends[REACH : 2 * REACH]], axis=0)


def corner_line(shape, corner, y_in, d_in):
    loads, comps, zlen, ylen, xlen = shape
    planes = loads * comps
    first_core = on_first()
    top = first_core & (lax.axis_index("sz") == lax.axis_size("sz") - 1)
    more = lax.axis_index("sy") < lax.axis_size("sy") - 1
    rows = []
    for k in range(planes):
        at = (k % comps * loads + k // comps) * zlen
        rows.append(jnp.where(first_core, y_in[at + zlen - 1 : at + zlen], y_in[at : at + 1]))
    rows.append(jnp.zeros((-planes % TILE, xlen), jnp.float32))
    stays_next = split_x(jnp.where(more, jnp.concatenate(rows, axis=0), 0.0))
    comes_next = split_x(jnp.where(more, d_in[...], 0.0))

    def faces(stays, comes, comp):
        zero = jnp.zeros((1, xlen), jnp.float32)
        under, over = [], []
        for own, other in zip(stays, comes):
            own, other = ([value[case * comps + comp : case * comps + comp + 1] for case in range(loads)] for value in (own, other))
            low = [jnp.where(first_core, a, b) for a, b in zip(own, other)] + [jnp.where(top, b, 0.0) for b in other]
            high = [jnp.where(first_core, jnp.where(top, 0.0, b), a) for a, b in zip(own, other)] + [zero] * loads
            under.append(jnp.concatenate(low, axis=0))
            over.append(jnp.concatenate(high, axis=0))
        return under, over

    low, high = [], []
    for comp in range(comps):
        near = faces((corner[0], corner[1]), (corner[2], corner[3]), comp)
        far = faces(stays_next, comes_next, comp)
        for (whole, change), (whole_next, change_next), into in zip(near, far, (low, high)):
            into.append((whole + whole_next, change + change_next, whole_next - whole, change_next - change))
    energy = quadratic(low, high, mode_weights())
    line = sum(energy[case : case + 1] for case in range(2 * loads)) * corner[0, planes : planes + 1]
    return spread_x(jnp.concatenate([line, jnp.zeros((TILE - 1, xlen), jnp.float32)], axis=0))[:1]


def corner_kernel(shape, share_in, corner, y_in, d_in, share):
    _, _, zlen, ylen, xlen = shape
    line = corner_line(shape, corner, y_in, d_in)
    rising = jnp.maximum(lax.broadcasted_iota(jnp.int32, (TILE, xlen), 0) - (TILE - 1 - ROWS), 0).astype(jnp.float32)
    falling = (REACH - lax.broadcasted_iota(jnp.int32, (REACH, xlen), 0)).astype(jnp.float32)
    share[...] = share_in[...]
    share[ylen * zlen - TILE : ylen * zlen] += rising * line
    share[ylen * zlen + REACH * (zlen - 1) : ylen * zlen + REACH * zlen] += falling * line


def total_kernel(shape, share, other, h_out, z_out, y_out, d_out, e_out):
    _, _, zlen, ylen, xlen = shape
    first_core = on_first()
    inner, rows = zlen - 1, ylen * zlen
    reach = REACH * zlen

    def layers(first, count):
        mine, theirs = share[first + inner * count : first + zlen * count], other[first + inner * count : first + zlen * count]
        middle = share[first : first + inner * count] + other[first : first + inner * count]
        return jnp.where(first_core, theirs, mine), middle, jnp.where(first_core, mine, theirs)

    lowest, middle, highest = layers(0, ylen)
    h_out[0] = lowest
    for z in range(inner):
        h_out[z + 1] = middle[ylen * z : ylen * (z + 1)]
    h_out[zlen] = highest
    z_out[...] = h_out[pl.ds(jnp.where(first_core, 0, 1), zlen)]
    ups = jnp.concatenate(layers(rows, REACH), axis=0)
    downs = jnp.concatenate(layers(rows + reach, REACH), axis=0)
    y_out[: reach + REACH] = jnp.where(next_is_partner(lax.axis_index("load")), ups, downs)
    for out, used in ((y_out, reach + REACH), (d_out, reach), (e_out, reach)):
        out[used:] = jnp.zeros((out.shape[0] - used, xlen), jnp.float32)
    for out, start in ((d_out, 1), (e_out, 0)):
        rows = jnp.where(next_is_partner(start), ups, downs)
        out[:reach] = jnp.where(first_core, rows[:reach], rows[REACH:])


def layers_kernel(h, d_in, y_in, e_in, z_in, out):
    zlen, ylen, xlen = out.shape
    reach = REACH * zlen
    first_core = on_first()
    z_index, z_last = lax.axis_index("sz"), lax.axis_size("sz") - 1
    y_index, y_last = lax.axis_index("sy"), lax.axis_size("sy") - 1
    z_side = jnp.where(first_core, z_index < z_last, z_index > 0)
    y_next = next_is_partner(lax.axis_index("load"))
    y_side = jnp.where(y_next, y_index < y_last, y_index > 0)
    d_next, e_next = next_is_partner(1), next_is_partner(0)
    d_side, e_side = (jnp.where(up, y_index < y_last, y_index > 0) for up in (d_next, e_next))
    blank = jnp.zeros((TILE - REACH, xlen), jnp.float32)

    def at_start(rows):
        return jnp.concatenate([rows, blank], axis=0)

    def at_end(rows):
        return jnp.concatenate([blank, rows], axis=0)

    def ends(rows, keep, at_last):
        rows = jnp.where(keep, rows, 0.0)
        return at_start(jnp.where(at_last, 0.0, rows)), at_end(jnp.where(at_last, rows, 0.0))

    def with_ends(layer, *pairs):
        head, tail = layer[:TILE], layer[ylen - TILE :]
        for first, last in pairs:
            head, tail = head + first, tail + last
        return jnp.concatenate([head, layer[TILE : ylen - TILE], tail] if ylen > 2 * TILE else [head, tail], axis=0)

    own = []
    for k in range(zlen + 1):
        layer = jnp.where(first_core, h[k], 0.0)
        own.append(with_ends(layer, ends(y_in[REACH * k : REACH * (k + 1)], y_side, y_next)))
    come = []
    for k in range(zlen):
        part = slice(REACH * k, REACH * (k + 1))
        layer = jnp.where(z_side, z_in[k], 0.0)
        come.append(with_ends(layer, ends(d_in[part], z_side & d_side, d_next), ends(e_in[part], z_side & e_side, e_next)))
    below = [jnp.where(first_core, 0.0, layer) for layer in come[zlen - REACH :]]
    above = [jnp.where(first_core, layer, 0.0) for layer in come]
    layers = below[:-1] + [below[-1] + own[0]] + own[1:-1] + [own[-1] + above[0]] + above[1:]
    for z, layer in enumerate(spread_layers(layers)):
        out[z] = layer


def sum_kernel(part, other, out):
    out[...] = part[...] + other[...]


def call(kernel, outs, args, scratch=(), space=pltpu.VMEM):
    shapes = [jax.ShapeDtypeStruct(out, jnp.float32) if isinstance(out, tuple) else out for out in outs]
    return pl.pallas_call(
        kernel,
        out_shape=shapes,
        in_specs=[pl.BlockSpec(memory_space=space)] * len(args),
        out_specs=[pl.BlockSpec(memory_space=pltpu.VMEM)] * len(outs),
        scratch_shapes=list(scratch),
        compiler_params=pltpu.CompilerParams(vmem_limit_bytes=32 * 1024 * 1024),
    )(*args)


def ring_moved(value, axis):
    size = lax.axis_size(axis)
    return lax.ppermute(value, axis, [((k + 1) % size, k) for k in range(size)])


def chip_swapped(value):
    cores = lax.axis_size("load")
    return lax.ppermute(value, "load", [(core, cores - 1 - core) for core in range(cores)])


def opposed(value, z_step, y_step, y_shift=0, start=None):
    cores, rows, size = lax.axis_size("load"), lax.axis_size("sy"), lax.axis_size("sz")
    pairs = []
    for core in range(cores):
        sign = -1 if core else 1
        for y in range(rows):
            for z in range(size):
                to_y, to_z, side = y + sign * y_step, z + sign * z_step, core
                if start is not None:
                    to_y = y + 1 if (y - start) % 2 == 0 else y - 1
                if not (0 <= to_y < rows and 0 <= to_z < size):
                    to_y, to_z, side = y, z, cores - 1 - core
                to_y = (to_y + y_shift) % rows
                pairs.append(((core * rows + y) * size + z, (side * rows + to_y) * size + to_z))
    return lax.ppermute(value, ("load", "sy", "sz"), pairs)


def beside(value):
    cores, rows, size = lax.axis_size("load"), lax.axis_size("sy"), lax.axis_size("sz")
    pairs = []
    for core in range(cores):
        for y in range(rows):
            to_y = y + 1 if (y - core) % 2 == 0 else y - 1
            for z in range(size):
                target = (to_y, z) if 0 <= to_y < rows else (y, z ^ 1)
                pairs.append(((core * rows + y) * size + z, (core * rows + target[0]) * size + target[1]))
    return lax.ppermute(value, ("load", "sy", "sz"), pairs)


def body(displacements, density, solid, fixed):
    loads, comps, zlen, ylen, xlen = displacements.shape
    planes = loads * comps
    totals = (zlen * lax.axis_size("sz"), ylen * lax.axis_size("sy"))
    args = [
        pltpu.with_memory_space_constraint(arg, pltpu.HBM) for arg in (displacements, fixed, density, solid)
    ]

    d_send, z_send, y_send = call(
        lambda *refs: lead_kernel(totals, *refs),
        [(-(-planes // TILE) * TILE, xlen), (planes + 1, ylen, xlen), (planes * zlen, xlen)],
        args,
        scratch=[
            pltpu.VMEM((loads, comps, ylen, xlen), jnp.float32),
            pltpu.VMEM((ylen, xlen), jnp.int32),
            pltpu.VMEM((ylen, xlen), jnp.float32),
            pltpu.VMEM((ylen, xlen), jnp.int32),
            pltpu.VMEM((loads, comps, zlen, 1, xlen), jnp.float32),
            pltpu.VMEM((zlen, 1, xlen), jnp.int32),
            pltpu.SemaphoreType.DMA((6,)),
        ],
        space=pltpu.HBM,
    )
    d_in = opposed(d_send, -1, 0, y_shift=-1)
    z_in = opposed(z_send, -1, 0)
    y_in = ring_moved(y_send, "sy")
    faces = lambda layers: pltpu.VMEM((4, planes, layers, ylen, xlen), jnp.float32)
    inner = call(
        lambda *refs: inner_kernel(totals, *refs),
        [
            (zlen, ylen, xlen),
            (2, planes * zlen, xlen),
            (2, REACH * (zlen - 1), xlen),
            (4, planes, ylen, xlen),
            (ylen, xlen),
            (TILE, xlen),
        ],
        (displacements, fixed, density, solid),
        scratch=[faces(zlen), pltpu.VMEM((zlen - 1, ylen + 2 * TILE, xlen), jnp.float32)],
    )
    reach = REACH * zlen
    shape = displacements.shape
    share, corner = call(
        lambda *refs: outer_kernel(shape, *refs),
        [(ylen * zlen + 2 * reach, xlen), (4, -(-(planes + 1) // TILE) * TILE, xlen)],
        (z_in, y_in, *inner),
        scratch=[
            faces(4),
            pltpu.VMEM((ylen + 2 * TILE, xlen), jnp.float32),
            pltpu.VMEM((ylen, xlen), jnp.float32),
        ],
    )
    (share,) = call(
        lambda *refs: corner_kernel(shape, *refs), [(ylen * zlen + 2 * reach, xlen)], (share, corner, y_in, d_in)
    )
    sent = (-(-(reach + REACH) // TILE) * TILE, xlen)
    h, z_send, y_send, d_send, e_send = call(
        lambda *refs: total_kernel(displacements.shape, *refs),
        [
            (zlen + 1, ylen, xlen),
            (zlen, ylen, xlen),
            sent,
            sent,
            sent,
        ],
        (share, chip_swapped(share)),
    )
    d_in = opposed(d_send, -1, 0, start=1)
    e_in = opposed(e_send, -1, 0, start=0)
    y_in = beside(y_send)
    z_in = opposed(z_send, -1, 0)
    (part,) = call(layers_kernel, [(zlen, ylen, xlen)], (h, d_in, y_in, e_in, z_in))
    (out,) = call(sum_kernel, [(zlen, ylen, xlen)], (part, chip_swapped(part)))
    return out


def solution(mesh):
    return jax.shard_map(
        body,
        mesh=mesh,
        in_specs=(
            P("load", None, "sz", "sy", None),
            P("sz", "sy", None),
            P("sz", "sy", None),
            P("sz", "sy", None),
        ),
        out_specs=P("sz", "sy", None),
        check_vma=False,
    )
```

```python
import jax
import jax.numpy as jnp
import numpy as np
from jax import lax
from jax.experimental import pallas as pl
from jax.experimental.pallas import tpu as pltpu
from jax.sharding import PartitionSpec as P

OFFSETS = [(0, 0, 0), (1, 0, 0), (1, 1, 0), (0, 1, 0), (0, 0, 1), (1, 0, 1), (1, 1, 1), (0, 1, 1)]
REACH = 3
ROWS = REACH + 1
TILE = 8
LANES = 128


def element_matrix():
    corners = np.array(
        [
            [-1.0, -1.0, -1.0],
            [1.0, -1.0, -1.0],
            [1.0, 1.0, -1.0],
            [-1.0, 1.0, -1.0],
            [-1.0, -1.0, 1.0],
            [1.0, -1.0, 1.0],
            [1.0, 1.0, 1.0],
            [-1.0, 1.0, 1.0],
        ]
    )
    poisson = 0.3
    lame = poisson / ((1.0 + poisson) * (1.0 - 2.0 * poisson))
    shear = 1.0 / (2.0 * (1.0 + poisson))
    elastic = np.zeros((6, 6))
    elastic[:3, :3] = lame
    for k in range(3):
        elastic[k, k] += 2.0 * shear
        elastic[3 + k, 3 + k] = shear
    gauss = 1.0 / np.sqrt(3.0)
    stiffness = np.zeros((24, 24))
    for gi in range(2):
        for gj in range(2):
            for gk in range(2):
                point = np.array([(2 * gi - 1) * gauss, (2 * gj - 1) * gauss, (2 * gk - 1) * gauss])
                strain = np.zeros((6, 24))
                for node in range(8):
                    grads = np.zeros(3)
                    for k in range(3):
                        value = corners[node, k] / 8.0
                        for m in range(3):
                            if m != k:
                                value = value * (1.0 + point[m] * corners[node, m])
                        grads[k] = 2.0 * value
                    col = 3 * node
                    strain[0, col] = grads[0]
                    strain[1, col + 1] = grads[1]
                    strain[2, col + 2] = grads[2]
                    strain[3, col] = grads[1]
                    strain[3, col + 1] = grads[0]
                    strain[4, col + 1] = grads[2]
                    strain[4, col + 2] = grads[1]
                    strain[5, col] = grads[2]
                    strain[5, col + 2] = grads[0]
                stiffness += strain.T @ elastic @ strain / 8.0
    return stiffness


def mode_weights():
    modes = [(i, j, k) for k in (0, 1) for j in (0, 1) for i in (0, 1)]
    sums = np.zeros((24, 24))
    for m, mode in enumerate(modes):
        for n, corner in enumerate(OFFSETS):
            sign = np.prod([(1 if corner[d] else -1) if mode[d] else 1 for d in range(3)])
            for comp in range(3):
                sums[3 * m + comp, 3 * n + comp] = sign
    form = sums @ element_matrix() @ sums.T / 64.0

    def at(first, second):
        return form[3 * modes.index(first[1]) + first[0], 3 * modes.index(second[1]) + second[0]]

    ux, vy, uy = (0, (1, 0, 0)), (1, (0, 1, 0)), (0, (0, 1, 0))
    uxy, wyz = (0, (1, 1, 0)), (2, (0, 1, 1))
    wxy, vxz, uxyz = (2, (1, 1, 0)), (1, (1, 0, 1)), (0, (1, 1, 1))
    return dict(
        normal=at(ux, ux) - at(ux, vy),
        trace=at(ux, vy),
        shear=at(uy, uy),
        plus=(at(uxy, uxy) + at(uxy, wyz)) / 2,
        minus=(at(uxy, uxy) - at(uxy, wyz)) / 2,
        twist=at(wxy, wxy) - at(wxy, vxz),
        twist_sum=at(wxy, vxz),
        corner=at(uxyz, uxyz),
    )


def square(value):
    return value * value


def quadratic(low, high, weights):
    x = [low[c][1] + high[c][1] for c in range(3)]
    y = [low[c][2] + high[c][2] for c in range(3)]
    z = [high[c][0] - low[c][0] for c in range(3)]
    xy = [low[c][3] + high[c][3] for c in range(3)]
    xz = [high[c][1] - low[c][1] for c in range(3)]
    yz = [high[c][2] - low[c][2] for c in range(3)]
    xyz = [high[c][3] - low[c][3] for c in range(3)]
    normal = square(x[0]) + square(y[1]) + square(z[2])
    trace = square(x[0] + y[1] + z[2])
    shear = square(y[0] + x[1]) + square(z[0] + x[2]) + square(z[1] + y[2])
    pairs = ((xy[0], yz[2]), (xy[1], xz[2]), (xz[0], yz[1]))
    plus = sum(square(p + q) for p, q in pairs)
    minus = sum(square(p - q) for p, q in pairs)
    twist = square(xy[2]) + square(xz[1]) + square(yz[0])
    twist_sum = square(xy[2] + xz[1] + yz[0])
    corner = square(xyz[0]) + square(xyz[1]) + square(xyz[2])
    groups = dict(
        normal=normal, trace=trace, shear=shear, plus=plus, minus=minus, twist=twist, twist_sum=twist_sum, corner=corner
    )
    return sum(np.float32(weights[name]) * group for name, group in groups.items())


def line_weight(coord, count):
    def outside(distance):
        missing = jnp.maximum(REACH - distance, 0)
        return missing * (missing + 1) // 2

    whole = (REACH + 1) * (REACH + 1)
    return (whole - outside(coord) - outside(count - 1 - coord)).astype(jnp.float32)


def voxel_factor(density, solid, plane, first_row, total_z, total_y):
    rows, length = density.shape
    row = lax.broadcasted_iota(jnp.int32, (rows, length), 0) + first_row
    column = lax.broadcasted_iota(jnp.int32, (rows, length), 1)
    weight = line_weight(row, total_y) * line_weight(column, length)
    weight = weight * line_weight(jnp.full((rows, length), plane, jnp.int32), total_z)
    return solid.astype(jnp.float32) * (-3.0 * density * density) / weight


def spread_x(value):
    rows, length = value.shape
    wide = jnp.concatenate([value, jnp.zeros((rows, LANES), jnp.float32)], axis=1)
    span = length + LANES
    total = float(ROWS) * value
    for step in range(1, ROWS):
        both = pltpu.roll(wide, span - step, 1) + pltpu.roll(wide, step, 1)
        total = total + float(ROWS - step) * both[:, :length]
    return total


def spread_layers(layers):
    for step in (1, 2, 1, 2):
        layers = [layers[k] + layers[k + step] for k in range(len(layers) - step)]
    return layers


def held(disp, fixed, case, comp, z, rows):
    return disp[case, comp, z, rows] * (1.0 - fixed[z, rows].astype(jnp.float32))


def split_x(value):
    length = value.shape[1]
    column = lax.broadcasted_iota(jnp.int32, value.shape, 1)
    ahead = jnp.where(column == length - 1, 0.0, pltpu.roll(value, length - 1, 1))
    return value + ahead, ahead - value


def face_sums(value):
    following = pltpu.roll(value, value.shape[0] - 1, 0)
    both, along_x = split_x(value + following)
    along_y, mixed = split_x(following - value)
    return both, along_x, along_y, mixed


def spread_y(quotient, ylen):
    rows = [quotient[TILE + step : TILE + step + ylen] for step in range(-REACH, REACH + 1)]
    return sum((ROWS - abs(k - REACH)) * rows[k] for k in range(2 * REACH + 1))


def to_neighbours(quotient, ylen):
    top = quotient[ylen : ylen + TILE]
    base = quotient[TILE : 2 * TILE]
    ahead, back = [], []
    for row in range(REACH):
        ahead.append(sum(float(REACH - row - k) * top[TILE - 1 - k : TILE - k] for k in range(REACH - row)))
        back.append(sum(float(row + 1 - k) * base[k : k + 1] for k in range(row + 1)))
    return ahead, back


def next_is_partner(start):
    return (lax.axis_index("sy") - start) % 2 == 0


def on_first():
    return lax.axis_index("load") == 0


def lead_kernel(totals, disp_hbm, fixed_hbm, density_hbm, solid_hbm, d_out, z_out, y_out, layer, layer_fixed, density, solid, rows, rows_fixed, sems):
    loads, comps, zlen, ylen, _ = disp_hbm.shape
    gives = jnp.where(on_first(), 0, zlen - 1)
    copies = [
        pltpu.make_async_copy(source, target, sems.at[k])
        for k, (source, target) in enumerate(
            (
                (density_hbm.at[gives], density),
                (solid_hbm.at[gives], solid),
                (fixed_hbm.at[gives], layer_fixed),
                (disp_hbm.at[:, :, gives], layer),
                (fixed_hbm.at[:, :1], rows_fixed),
                (disp_hbm.at[:, :, :, :1], rows),
            )
        )
    ]
    for copy in copies:
        copy.start()
    for copy in copies[:2]:
        copy.wait()
    plane = lax.axis_index("sz") * zlen + gives
    base_y = lax.axis_index("sy") * ylen
    d_out[...] = jnp.zeros(d_out.shape, jnp.float32)
    z_out[loads * comps] = voxel_factor(density[...], solid[...], plane, base_y, *totals)
    for copy in copies[2:4]:
        copy.wait()
    free = 1.0 - layer_fixed[...].astype(jnp.float32)
    for case in range(loads):
        for comp in range(comps):
            k = case * comps + comp
            z_out[k] = layer[case, comp] * free
            at = comp * loads + case
            d_out[at : at + 1] = z_out[k, :1]
    for copy in copies[4:]:
        copy.wait()
    for z in range(zlen):
        free = 1.0 - rows_fixed[z, :1].astype(jnp.float32)
        for case in range(loads):
            for comp in range(comps):
                at = (comp * loads + case) * zlen + z
                y_out[at : at + 1] = rows[case, comp, z, :1] * free


def tile_energies(faces, first, lanes, layers, loads, comps, base=0):
    weights = mode_weights()
    energy = [None] * layers
    for case in range(loads):
        low = None
        for z in range(layers + 1):
            planes = [case * comps + comp for comp in range(comps)]
            high = [[faces[kind, k, base + z, first : first + TILE, lanes] for kind in range(4)] for k in planes]
            if low is not None:
                part = quadratic(low, high, weights)
                energy[z - 1] = part if energy[z - 1] is None else energy[z - 1] + part
            low = high
    return energy


def blank_last(value, first, ylen):
    row = lax.broadcasted_iota(jnp.int32, value.shape, 0) + first
    return jnp.where(row == ylen - 1, 0.0, value)


def inner_kernel(totals, disp, fixed, density, solid, own, line, sends, last_faces, last_factor, edge, faces, quotient):
    loads, comps, zlen, ylen, xlen = disp.shape
    total_z, total_y = totals
    base_z = lax.axis_index("sz") * zlen
    base_y = lax.axis_index("sy") * ylen
    inner = zlen - 1
    keeps = jnp.where(on_first(), inner, 0)
    free = [1.0 - fixed[z].astype(jnp.float32) for z in range(zlen)]

    for k in range(loads * comps):
        case, comp = k // comps, k % comps
        for z in range(zlen):
            plane = disp[case, comp, z] * free[z]
            for kind, value in enumerate(face_sums(plane)):
                faces[kind, k, z] = value
            at = (comp * loads + case) * zlen + z
            line[0, at : at + 1] = plane[ylen - 1 :]
        for kind in range(4):
            last_faces[kind, k] = faces[kind, k, keeps]

    line[0], line[1] = split_x(line[0])

    zeros = jnp.zeros((TILE, xlen), jnp.float32)
    edge[...] = jnp.zeros(edge.shape, jnp.float32)
    for z in range(zlen):
        factor = voxel_factor(density[z], solid[z], base_z + z, base_y, total_z, total_y)
        edge[z : z + 1] = factor[ylen - 1 :]
        if z == inner:
            last_factor[...] = factor
        else:
            quotient[z, :TILE] = zeros
            quotient[z, TILE : TILE + ylen] = factor
            quotient[z, TILE + ylen :] = zeros

    for first in range(0, ylen, TILE):

        @pl.loop(0, xlen // LANES, unroll=True)
        def _(chunk):
            lanes = pl.ds(pl.multiple_of(chunk * LANES, LANES), LANES)
            energy = tile_energies(faces, first, lanes, inner, loads, comps)
            for z in range(inner):
                here = quotient[z, first + TILE : first + 2 * TILE, lanes]
                quotient[z, first + TILE : first + 2 * TILE, lanes] = blank_last(energy[z] * here, first, ylen)

    for z in range(inner):
        own[z] = spread_x(spread_y(quotient.at[z], ylen))
        ahead, back = to_neighbours(quotient.at[z], ylen)
        ends = spread_x(jnp.concatenate(ahead + back + [zeros[:2]], axis=0))
        sends[0, REACH * z : REACH * (z + 1)] = ends[:REACH]
        sends[1, REACH * z : REACH * (z + 1)] = ends[REACH : 2 * REACH]


def outer_kernel(
    shape, z_in, y_in, own_in, line, sends, last_faces, last_factor, edge, share, corner, faces, quotient, factor
):
    loads, comps, zlen, ylen, xlen = shape
    planes = loads * comps
    inner = zlen - 1
    first_core, index = on_first(), lax.axis_index("sz")
    top = first_core & (index == lax.axis_size("sz") - 1)
    more = lax.axis_index("sy") < lax.axis_size("sy") - 1
    stays, comes = jnp.where(first_core, 0, 1), jnp.where(first_core, jnp.where(top, 2, 1), 0)
    y_plus, y_diff = split_x(jnp.where(more, y_in[...], 0.0))
    come_rows = []
    for k in range(planes):
        for kind, value in enumerate(face_sums(z_in[k])):
            faces[kind, k, stays] = last_faces[kind, k]
            faces[kind, k, comes] = value
        come_rows.append(z_in[k % loads * comps + k // loads, ylen - 1 :])
        for group in range(2):
            rows = line[group, k * zlen + inner : (k + 1) * zlen], line[group, k * zlen : k * zlen + 1]
            corner[group, k : k + 1] = jnp.where(first_core, *rows)
    come_rows.append(jnp.zeros((-planes % TILE, xlen), jnp.float32))
    for group, value in enumerate(split_x(jnp.concatenate(come_rows, axis=0))):
        corner[2 + group, :planes] = value[:planes]
    below = jnp.where(index > 0, z_in[planes], 0.0)
    factor[...] = jnp.where(first_core, last_factor[...], below)
    corner[0, planes : planes + 1] = factor[ylen - 1 :]

    @pl.when(top)
    def _():
        clamped = jnp.zeros((ylen, xlen), jnp.float32)
        for k in range(planes):
            for slot in (1, 3):
                for kind in range(4):
                    faces[kind, k, slot] = clamped

    zeros = jnp.zeros((TILE, xlen), jnp.float32)
    quotient[:TILE] = zeros
    quotient[TILE + ylen :] = zeros
    for first in range(0, ylen, TILE):

        @pl.loop(0, xlen // LANES, unroll=True)
        def _(chunk):
            lanes = pl.ds(pl.multiple_of(chunk * LANES, LANES), LANES)
            (energy,) = tile_energies(faces, first, lanes, 1, loads, comps)
            here = energy * factor[first : first + TILE, lanes]
            quotient[first + TILE : first + 2 * TILE, lanes] = blank_last(here, first, ylen)

    @pl.when(top)
    def _():
        for first in range(0, ylen, TILE):

            @pl.loop(0, xlen // LANES, unroll=True)
            def _(chunk):
                lanes = pl.ds(pl.multiple_of(chunk * LANES, LANES), LANES)
                (energy,) = tile_energies(faces, first, lanes, 1, loads, comps, base=2)
                here = energy * factor[first : first + TILE, lanes]
                quotient[first + TILE : first + 2 * TILE, lanes] += blank_last(here, first, ylen)

    count = loads * zlen
    low, high = [], []
    for comp in range(comps):
        part = slice(comp * count, (comp + 1) * count)
        whole, change = line[0, part], line[1, part]
        whole_next, change_next = y_plus[part], y_diff[part]
        face = (whole + whole_next, change + change_next, whole_next - whole, change_next - change)
        low.append(face)
        high.append([pltpu.roll(value, count - 1, 0) for value in face])
    energy = quadratic(low, high, mode_weights())
    energy = sum(energy[case * zlen : case * zlen + inner] for case in range(loads)) * edge[:inner]
    last = spread_x(jnp.concatenate([energy, jnp.zeros((TILE - inner, xlen), jnp.float32)], axis=0))

    row = lax.broadcasted_iota(jnp.int32, (TILE, xlen), 0)
    rising = jnp.maximum(row - (TILE - 1 - ROWS), 0).astype(jnp.float32)
    ups, downs = [], []
    for z in range(inner):
        share[ylen * z : ylen * (z + 1)] = own_in[z]
        share[ylen * (z + 1) - TILE : ylen * (z + 1)] += rising * last[z : z + 1]
        here = sends[0, REACH * z : REACH * (z + 1)]
        ups += [here[r : r + 1] + float(REACH - r) * last[z : z + 1] for r in range(REACH)]
        downs.append(sends[1, REACH * z : REACH * (z + 1)])
    share[ylen * inner : ylen * zlen] = spread_x(spread_y(quotient, ylen))
    ahead, back = to_neighbours(quotient, ylen)
    ends = spread_x(jnp.concatenate(ahead + back + [zeros[:2]], axis=0))
    share[ylen * zlen :] = jnp.concatenate(ups + [ends[:REACH]] + downs + [ends[REACH : 2 * REACH]], axis=0)


def corner_line(shape, corner, y_in, d_in):
    loads, comps, zlen, ylen, xlen = shape
    planes = loads * comps
    first_core = on_first()
    top = first_core & (lax.axis_index("sz") == lax.axis_size("sz") - 1)
    more = lax.axis_index("sy") < lax.axis_size("sy") - 1
    rows = [jnp.where(first_core, y_in[(k + 1) * zlen - 1 : (k + 1) * zlen], y_in[k * zlen : k * zlen + 1]) for k in range(planes)]
    rows.append(jnp.zeros((-planes % TILE, xlen), jnp.float32))
    stays_next = split_x(jnp.where(more, jnp.concatenate(rows, axis=0), 0.0))
    comes_next = split_x(jnp.where(more, d_in[...], 0.0))
    zero = jnp.zeros((loads, xlen), jnp.float32)

    def face(near, far, comp, more_near, more_far):
        part = slice(comp * loads, (comp + 1) * loads)
        (whole, change), (whole_next, change_next) = (
            [jnp.concatenate([value[part], zero if extra is None else extra[part]], axis=0) for value, extra in zip(values, extras)]
            for values, extras in ((near, more_near), (far, more_far))
        )
        return whole + whole_next, change + change_next, whole_next - whole, change_next - change

    def under(stays, comes):
        return [jnp.where(first_core, a, b) for a, b in zip(stays, comes)], [jnp.where(top, b, 0.0) for b in comes]

    def over(stays, comes):
        return [jnp.where(first_core, jnp.where(top, 0.0, b), a) for a, b in zip(stays, comes)], (None, None)

    near, far = ((corner[0], corner[1]), (corner[2], corner[3])), (stays_next, comes_next)
    low, high = [], []
    for side, into in ((under, low), (over, high)):
        (near_own, near_more), (far_own, far_more) = side(*near), side(*far)
        into += [face(near_own, far_own, comp, near_more, far_more) for comp in range(comps)]
    energy = quadratic(low, high, mode_weights())
    line = sum(energy[case : case + 1] for case in range(2 * loads)) * corner[0, planes : planes + 1]
    return spread_x(jnp.concatenate([line, jnp.zeros((TILE - 1, xlen), jnp.float32)], axis=0))[:1]


def corner_kernel(shape, share_in, corner, y_in, d_in, share):
    _, _, zlen, ylen, xlen = shape
    line = corner_line(shape, corner, y_in, d_in)
    rising = jnp.maximum(lax.broadcasted_iota(jnp.int32, (TILE, xlen), 0) - (TILE - 1 - ROWS), 0).astype(jnp.float32)
    falling = (REACH - lax.broadcasted_iota(jnp.int32, (REACH, xlen), 0)).astype(jnp.float32)
    share[...] = share_in[...]
    share[ylen * zlen - TILE : ylen * zlen] += rising * line
    share[ylen * zlen + REACH * (zlen - 1) : ylen * zlen + REACH * zlen] += falling * line


def total_kernel(shape, share, other, h_out, z_out, y_out, d_out, e_out):
    _, _, zlen, ylen, xlen = shape
    first_core = on_first()
    inner, rows = zlen - 1, ylen * zlen
    reach = REACH * zlen

    def layers(first, count):
        mine, theirs = share[first + inner * count : first + zlen * count], other[first + inner * count : first + zlen * count]
        middle = share[first : first + inner * count] + other[first : first + inner * count]
        return jnp.where(first_core, theirs, mine), middle, jnp.where(first_core, mine, theirs)

    lowest, middle, highest = layers(0, ylen)
    h_out[0] = lowest
    for z in range(inner):
        h_out[z + 1] = middle[ylen * z : ylen * (z + 1)]
    h_out[zlen] = highest
    z_out[...] = h_out[pl.ds(jnp.where(first_core, 0, 1), zlen)]
    ups = jnp.concatenate(layers(rows, REACH), axis=0)
    downs = jnp.concatenate(layers(rows + reach, REACH), axis=0)
    y_out[: reach + REACH] = jnp.where(next_is_partner(lax.axis_index("load")), ups, downs)
    for out, used in ((y_out, reach + REACH), (d_out, reach), (e_out, reach)):
        out[used:] = jnp.zeros((out.shape[0] - used, xlen), jnp.float32)
    for out, start in ((d_out, 1), (e_out, 0)):
        rows = jnp.where(next_is_partner(start), ups, downs)
        out[:reach] = jnp.where(first_core, rows[:reach], rows[REACH:])


def layers_kernel(h, d_in, e_in, y_in, z_in, out):
    zlen, ylen, xlen = out.shape
    reach = REACH * zlen
    first_core = on_first()
    z_index, z_last = lax.axis_index("sz"), lax.axis_size("sz") - 1
    y_index, y_last = lax.axis_index("sy"), lax.axis_size("sy") - 1
    z_side = jnp.where(first_core, z_index < z_last, z_index > 0)
    y_next = next_is_partner(lax.axis_index("load"))
    y_side = jnp.where(y_next, y_index < y_last, y_index > 0)
    d_next, e_next = next_is_partner(1), next_is_partner(0)
    d_side, e_side = (jnp.where(up, y_index < y_last, y_index > 0) for up in (d_next, e_next))
    blank = jnp.zeros((TILE - REACH, xlen), jnp.float32)

    def at_start(rows):
        return jnp.concatenate([rows, blank], axis=0)

    def at_end(rows):
        return jnp.concatenate([blank, rows], axis=0)

    def ends(rows, keep, at_last):
        rows = jnp.where(keep, rows, 0.0)
        return at_start(jnp.where(at_last, 0.0, rows)), at_end(jnp.where(at_last, rows, 0.0))

    def with_ends(layer, *pairs):
        head, tail = layer[:TILE], layer[ylen - TILE :]
        for first, last in pairs:
            head, tail = head + first, tail + last
        return jnp.concatenate([head, layer[TILE : ylen - TILE], tail] if ylen > 2 * TILE else [head, tail], axis=0)

    own = []
    for k in range(zlen + 1):
        layer = jnp.where(first_core, h[k], 0.0)
        own.append(with_ends(layer, ends(y_in[REACH * k : REACH * (k + 1)], y_side, y_next)))
    come = []
    for k in range(zlen):
        part = slice(REACH * k, REACH * (k + 1))
        layer = jnp.where(z_side, z_in[k], 0.0)
        come.append(with_ends(layer, ends(d_in[part], z_side & d_side, d_next), ends(e_in[part], z_side & e_side, e_next)))
    below = [jnp.where(first_core, 0.0, layer) for layer in come[zlen - REACH :]]
    above = [jnp.where(first_core, layer, 0.0) for layer in come]
    layers = below[:-1] + [below[-1] + own[0]] + own[1:-1] + [own[-1] + above[0]] + above[1:]
    for z, layer in enumerate(spread_layers(layers)):
        out[z] = layer


def sum_kernel(part, other, out):
    out[...] = part[...] + other[...]


def call(kernel, outs, args, scratch=(), space=pltpu.VMEM):
    shapes = [jax.ShapeDtypeStruct(out, jnp.float32) if isinstance(out, tuple) else out for out in outs]
    return pl.pallas_call(
        kernel,
        out_shape=shapes,
        in_specs=[pl.BlockSpec(memory_space=space)] * len(args),
        out_specs=[pl.BlockSpec(memory_space=pltpu.VMEM)] * len(outs),
        scratch_shapes=list(scratch),
        compiler_params=pltpu.CompilerParams(vmem_limit_bytes=32 * 1024 * 1024),
    )(*args)


def ring_moved(value, axis):
    size = lax.axis_size(axis)
    return lax.ppermute(value, axis, [((k + 1) % size, k) for k in range(size)])


def chip_swapped(value):
    cores = lax.axis_size("load")
    return lax.ppermute(value, "load", [(core, cores - 1 - core) for core in range(cores)])


def opposed(value, z_step, y_step, y_shift=0, start=None):
    cores, rows, size = lax.axis_size("load"), lax.axis_size("sy"), lax.axis_size("sz")
    pairs = []
    for core in range(cores):
        sign = -1 if core else 1
        for y in range(rows):
            for z in range(size):
                to_y, to_z, side = y + sign * y_step, z + sign * z_step, core
                if start is not None:
                    to_y = y + 1 if (y - start) % 2 == 0 else y - 1
                if not (0 <= to_y < rows and 0 <= to_z < size):
                    to_y, to_z, side = y, z, cores - 1 - core
                to_y = (to_y + y_shift) % rows
                pairs.append(((core * rows + y) * size + z, (side * rows + to_y) * size + to_z))
    return lax.ppermute(value, ("load", "sy", "sz"), pairs)


def beside(value):
    cores, rows, size = lax.axis_size("load"), lax.axis_size("sy"), lax.axis_size("sz")
    pairs = []
    for core in range(cores):
        for y in range(rows):
            to_y = y + 1 if (y - core) % 2 == 0 else y - 1
            for z in range(size):
                target = (to_y, z) if 0 <= to_y < rows else (y, z ^ 1)
                pairs.append(((core * rows + y) * size + z, (core * rows + target[0]) * size + target[1]))
    return lax.ppermute(value, ("load", "sy", "sz"), pairs)


def body(displacements, density, solid, fixed):
    loads, comps, zlen, ylen, xlen = displacements.shape
    planes = loads * comps
    totals = (zlen * lax.axis_size("sz"), ylen * lax.axis_size("sy"))
    args = [
        pltpu.with_memory_space_constraint(arg, pltpu.HBM) for arg in (displacements, fixed, density, solid)
    ]

    d_send, z_send, y_send = call(
        lambda *refs: lead_kernel(totals, *refs),
        [(-(-planes // TILE) * TILE, xlen), (planes + 1, ylen, xlen), (planes * zlen, xlen)],
        args,
        scratch=[
            pltpu.VMEM((loads, comps, ylen, xlen), jnp.float32),
            pltpu.VMEM((ylen, xlen), jnp.int32),
            pltpu.VMEM((ylen, xlen), jnp.float32),
            pltpu.VMEM((ylen, xlen), jnp.int32),
            pltpu.VMEM((loads, comps, zlen, 1, xlen), jnp.float32),
            pltpu.VMEM((zlen, 1, xlen), jnp.int32),
            pltpu.SemaphoreType.DMA((6,)),
        ],
        space=pltpu.HBM,
    )
    d_in = opposed(d_send, -1, 0, y_shift=-1)
    z_in = opposed(z_send, -1, 0)
    y_in = ring_moved(y_send, "sy")
    faces = lambda layers: pltpu.VMEM((4, planes, layers, ylen, xlen), jnp.float32)
    inner = call(
        lambda *refs: inner_kernel(totals, *refs),
        [
            (zlen, ylen, xlen),
            (2, planes * zlen, xlen),
            (2, REACH * (zlen - 1), xlen),
            (4, planes, ylen, xlen),
            (ylen, xlen),
            (TILE, xlen),
        ],
        (displacements, fixed, density, solid),
        scratch=[faces(zlen), pltpu.VMEM((zlen - 1, ylen + 2 * TILE, xlen), jnp.float32)],
    )
    reach = REACH * zlen
    shape = displacements.shape
    share, corner = call(
        lambda *refs: outer_kernel(shape, *refs),
        [(ylen * zlen + 2 * reach, xlen), (4, -(-(planes + 1) // TILE) * TILE, xlen)],
        (z_in, y_in, *inner),
        scratch=[
            faces(4),
            pltpu.VMEM((ylen + 2 * TILE, xlen), jnp.float32),
            pltpu.VMEM((ylen, xlen), jnp.float32),
        ],
    )
    (share,) = call(
        lambda *refs: corner_kernel(shape, *refs), [(ylen * zlen + 2 * reach, xlen)], (share, corner, y_in, d_in)
    )
    sent = (-(-(reach + REACH) // TILE) * TILE, xlen)
    h, z_send, y_send, d_send, e_send = call(
        lambda *refs: total_kernel(displacements.shape, *refs),
        [
            (zlen + 1, ylen, xlen),
            (zlen, ylen, xlen),
            sent,
            sent,
            sent,
        ],
        (share, chip_swapped(share)),
    )
    d_in = opposed(d_send, -1, 0, start=1)
    e_in = opposed(e_send, -1, 0, start=0)
    y_in = beside(y_send)
    z_in = opposed(z_send, -1, 0)
    (part,) = call(layers_kernel, [(zlen, ylen, xlen)], (h, d_in, e_in, y_in, z_in))
    (out,) = call(sum_kernel, [(zlen, ylen, xlen)], (part, chip_swapped(part)))
    return out


def solution(mesh):
    return jax.shard_map(
        body,
        mesh=mesh,
        in_specs=(
            P("load", None, "sz", "sy", None),
            P("sz", "sy", None),
            P("sz", "sy", None),
            P("sz", "sy", None),
        ),
        out_specs=P("sz", "sy", None),
        check_vma=False,
    )
```

```python
import jax
import jax.numpy as jnp
import numpy as np
from jax import lax
from jax.experimental import pallas as pl
from jax.experimental.pallas import tpu as pltpu
from jax.sharding import PartitionSpec as P

OFFSETS = [(0, 0, 0), (1, 0, 0), (1, 1, 0), (0, 1, 0), (0, 0, 1), (1, 0, 1), (1, 1, 1), (0, 1, 1)]
REACH = 3
ROWS = REACH + 1
TILE = 8
LANES = 128


def element_matrix():
    corners = np.array(
        [
            [-1.0, -1.0, -1.0],
            [1.0, -1.0, -1.0],
            [1.0, 1.0, -1.0],
            [-1.0, 1.0, -1.0],
            [-1.0, -1.0, 1.0],
            [1.0, -1.0, 1.0],
            [1.0, 1.0, 1.0],
            [-1.0, 1.0, 1.0],
        ]
    )
    poisson = 0.3
    lame = poisson / ((1.0 + poisson) * (1.0 - 2.0 * poisson))
    shear = 1.0 / (2.0 * (1.0 + poisson))
    elastic = np.zeros((6, 6))
    elastic[:3, :3] = lame
    for k in range(3):
        elastic[k, k] += 2.0 * shear
        elastic[3 + k, 3 + k] = shear
    gauss = 1.0 / np.sqrt(3.0)
    stiffness = np.zeros((24, 24))
    for gi in range(2):
        for gj in range(2):
            for gk in range(2):
                point = np.array([(2 * gi - 1) * gauss, (2 * gj - 1) * gauss, (2 * gk - 1) * gauss])
                strain = np.zeros((6, 24))
                for node in range(8):
                    grads = np.zeros(3)
                    for k in range(3):
                        value = corners[node, k] / 8.0
                        for m in range(3):
                            if m != k:
                                value = value * (1.0 + point[m] * corners[node, m])
                        grads[k] = 2.0 * value
                    col = 3 * node
                    strain[0, col] = grads[0]
                    strain[1, col + 1] = grads[1]
                    strain[2, col + 2] = grads[2]
                    strain[3, col] = grads[1]
                    strain[3, col + 1] = grads[0]
                    strain[4, col + 1] = grads[2]
                    strain[4, col + 2] = grads[1]
                    strain[5, col] = grads[2]
                    strain[5, col + 2] = grads[0]
                stiffness += strain.T @ elastic @ strain / 8.0
    return stiffness


def mode_weights():
    modes = [(i, j, k) for k in (0, 1) for j in (0, 1) for i in (0, 1)]
    sums = np.zeros((24, 24))
    for m, mode in enumerate(modes):
        for n, corner in enumerate(OFFSETS):
            sign = np.prod([(1 if corner[d] else -1) if mode[d] else 1 for d in range(3)])
            for comp in range(3):
                sums[3 * m + comp, 3 * n + comp] = sign
    form = sums @ element_matrix() @ sums.T / 64.0

    def at(first, second):
        return form[3 * modes.index(first[1]) + first[0], 3 * modes.index(second[1]) + second[0]]

    ux, vy, uy = (0, (1, 0, 0)), (1, (0, 1, 0)), (0, (0, 1, 0))
    uxy, wyz = (0, (1, 1, 0)), (2, (0, 1, 1))
    wxy, vxz, uxyz = (2, (1, 1, 0)), (1, (1, 0, 1)), (0, (1, 1, 1))
    return dict(
        normal=at(ux, ux) - at(ux, vy),
        trace=at(ux, vy),
        shear=at(uy, uy),
        plus=(at(uxy, uxy) + at(uxy, wyz)) / 2,
        minus=(at(uxy, uxy) - at(uxy, wyz)) / 2,
        twist=at(wxy, wxy) - at(wxy, vxz),
        twist_sum=at(wxy, vxz),
        corner=at(uxyz, uxyz),
    )


def square(value):
    return value * value


def quadratic(low, high, weights):
    x = [low[c][1] + high[c][1] for c in range(3)]
    y = [low[c][2] + high[c][2] for c in range(3)]
    z = [high[c][0] - low[c][0] for c in range(3)]
    xy = [low[c][3] + high[c][3] for c in range(3)]
    xz = [high[c][1] - low[c][1] for c in range(3)]
    yz = [high[c][2] - low[c][2] for c in range(3)]
    xyz = [high[c][3] - low[c][3] for c in range(3)]
    normal = square(x[0]) + square(y[1]) + square(z[2])
    trace = square(x[0] + y[1] + z[2])
    shear = square(y[0] + x[1]) + square(z[0] + x[2]) + square(z[1] + y[2])
    pairs = ((xy[0], yz[2]), (xy[1], xz[2]), (xz[0], yz[1]))
    plus = sum(square(p + q) for p, q in pairs)
    minus = sum(square(p - q) for p, q in pairs)
    twist = square(xy[2]) + square(xz[1]) + square(yz[0])
    twist_sum = square(xy[2] + xz[1] + yz[0])
    corner = square(xyz[0]) + square(xyz[1]) + square(xyz[2])
    groups = dict(
        normal=normal, trace=trace, shear=shear, plus=plus, minus=minus, twist=twist, twist_sum=twist_sum, corner=corner
    )
    return sum(np.float32(weights[name]) * group for name, group in groups.items())


def line_weight(coord, count):
    def outside(distance):
        missing = jnp.maximum(REACH - distance, 0)
        return missing * (missing + 1) // 2

    whole = (REACH + 1) * (REACH + 1)
    return (whole - outside(coord) - outside(count - 1 - coord)).astype(jnp.float32)


def voxel_factor(density, solid, plane, first_row, total_z, total_y):
    rows, length = density.shape
    row = lax.broadcasted_iota(jnp.int32, (rows, length), 0) + first_row
    column = lax.broadcasted_iota(jnp.int32, (rows, length), 1)
    weight = line_weight(row, total_y) * line_weight(column, length)
    weight = weight * line_weight(jnp.full((rows, length), plane, jnp.int32), total_z)
    return solid.astype(jnp.float32) * (-3.0 * density * density) / weight


def spread_x(value):
    rows, length = value.shape
    wide = jnp.concatenate([value, jnp.zeros((rows, LANES), jnp.float32)], axis=1)
    span = length + LANES
    total = float(ROWS) * value
    for step in range(1, ROWS):
        both = pltpu.roll(wide, span - step, 1) + pltpu.roll(wide, step, 1)
        total = total + float(ROWS - step) * both[:, :length]
    return total


def spread_layers(layers):
    for step in (1, 2, 1, 2):
        layers = [layers[k] + layers[k + step] for k in range(len(layers) - step)]
    return layers


def held(disp, fixed, case, comp, z, rows):
    return disp[case, comp, z, rows] * (1.0 - fixed[z, rows].astype(jnp.float32))


def split_x(value):
    length = value.shape[1]
    column = lax.broadcasted_iota(jnp.int32, value.shape, 1)
    ahead = jnp.where(column == length - 1, 0.0, pltpu.roll(value, length - 1, 1))
    return value + ahead, ahead - value


def face_sums(value):
    following = pltpu.roll(value, value.shape[0] - 1, 0)
    both, along_x = split_x(value + following)
    along_y, mixed = split_x(following - value)
    return both, along_x, along_y, mixed


def spread_y(quotient, ylen):
    rows = [quotient[TILE + step : TILE + step + ylen] for step in range(-REACH, REACH + 1)]
    return sum((ROWS - abs(k - REACH)) * rows[k] for k in range(2 * REACH + 1))


def to_neighbours(quotient, ylen):
    top = quotient[ylen : ylen + TILE]
    base = quotient[TILE : 2 * TILE]
    ahead, back = [], []
    for row in range(REACH):
        ahead.append(sum(float(REACH - row - k) * top[TILE - 1 - k : TILE - k] for k in range(REACH - row)))
        back.append(sum(float(row + 1 - k) * base[k : k + 1] for k in range(row + 1)))
    return ahead, back


def next_is_partner(start):
    return (lax.axis_index("sy") - start) % 2 == 0


def on_first():
    return lax.axis_index("load") == 0


def lead_kernel(totals, disp_hbm, fixed_hbm, density_hbm, solid_hbm, d_out, z_out, y_out, layer, layer_fixed, density, solid, rows, rows_fixed, sems):
    loads, comps, zlen, ylen, _ = disp_hbm.shape
    gives = jnp.where(on_first(), 0, zlen - 1)
    copies = [
        pltpu.make_async_copy(source, target, sems.at[k])
        for k, (source, target) in enumerate(
            (
                (density_hbm.at[gives], density),
                (solid_hbm.at[gives], solid),
                (fixed_hbm.at[gives], layer_fixed),
                (disp_hbm.at[:, :, gives], layer),
                (fixed_hbm.at[:, :1], rows_fixed),
                (disp_hbm.at[:, :, :, :1], rows),
            )
        )
    ]
    for copy in copies:
        copy.start()
    for copy in copies[:2]:
        copy.wait()
    plane = lax.axis_index("sz") * zlen + gives
    base_y = lax.axis_index("sy") * ylen
    d_out[...] = jnp.zeros(d_out.shape, jnp.float32)
    z_out[loads * comps] = voxel_factor(density[...], solid[...], plane, base_y, *totals)
    for copy in copies[2:4]:
        copy.wait()
    free = 1.0 - layer_fixed[...].astype(jnp.float32)
    for case in range(loads):
        for comp in range(comps):
            k = case * comps + comp
            z_out[k] = layer[case, comp] * free
            at = comp * loads + case
            d_out[at : at + 1] = z_out[k, :1]
    for copy in copies[4:]:
        copy.wait()
    for z in range(zlen):
        free = 1.0 - rows_fixed[z, :1].astype(jnp.float32)
        for case in range(loads):
            for comp in range(comps):
                at = (comp * loads + case) * zlen + z
                y_out[at : at + 1] = rows[case, comp, z, :1] * free


def tile_energies(faces, first, lanes, layers, loads, comps, base=0):
    weights = mode_weights()
    energy = [None] * layers
    for case in range(loads):
        low = None
        for z in range(layers + 1):
            planes = [case * comps + comp for comp in range(comps)]
            high = [[faces[kind, k, base + z, first : first + TILE, lanes] for kind in range(4)] for k in planes]
            if low is not None:
                part = quadratic(low, high, weights)
                energy[z - 1] = part if energy[z - 1] is None else energy[z - 1] + part
            low = high
    return energy


def blank_last(value, first, ylen):
    row = lax.broadcasted_iota(jnp.int32, value.shape, 0) + first
    return jnp.where(row == ylen - 1, 0.0, value)


def inner_kernel(totals, disp, fixed, density, solid, own, line, sends, last_faces, last_factor, edge, faces, quotient):
    loads, comps, zlen, ylen, xlen = disp.shape
    total_z, total_y = totals
    base_z = lax.axis_index("sz") * zlen
    base_y = lax.axis_index("sy") * ylen
    inner = zlen - 1
    keeps = jnp.where(on_first(), inner, 0)
    free = [1.0 - fixed[z].astype(jnp.float32) for z in range(zlen)]

    for k in range(loads * comps):
        case, comp = k // comps, k % comps
        for z in range(zlen):
            plane = disp[case, comp, z] * free[z]
            for kind, value in enumerate(face_sums(plane)):
                faces[kind, k, z] = value
            at = (comp * loads + case) * zlen + z
            line[0, at : at + 1] = plane[ylen - 1 :]
        for kind in range(4):
            last_faces[kind, k] = faces[kind, k, keeps]

    line[0], line[1] = split_x(line[0])

    zeros = jnp.zeros((TILE, xlen), jnp.float32)
    edge[...] = jnp.zeros(edge.shape, jnp.float32)
    for z in range(zlen):
        factor = voxel_factor(density[z], solid[z], base_z + z, base_y, total_z, total_y)
        edge[z : z + 1] = factor[ylen - 1 :]
        if z == inner:
            last_factor[...] = factor
        else:
            quotient[z, :TILE] = zeros
            quotient[z, TILE : TILE + ylen] = factor
            quotient[z, TILE + ylen :] = zeros

    for first in range(0, ylen, TILE):

        @pl.loop(0, xlen // LANES, unroll=True)
        def _(chunk):
            lanes = pl.ds(pl.multiple_of(chunk * LANES, LANES), LANES)
            energy = tile_energies(faces, first, lanes, inner, loads, comps)
            for z in range(inner):
                here = quotient[z, first + TILE : first + 2 * TILE, lanes]
                quotient[z, first + TILE : first + 2 * TILE, lanes] = blank_last(energy[z] * here, first, ylen)

    for z in range(inner):
        own[z] = spread_x(spread_y(quotient.at[z], ylen))
        ahead, back = to_neighbours(quotient.at[z], ylen)
        ends = spread_x(jnp.concatenate(ahead + back + [zeros[:2]], axis=0))
        sends[0, REACH * z : REACH * (z + 1)] = ends[:REACH]
        sends[1, REACH * z : REACH * (z + 1)] = ends[REACH : 2 * REACH]


def outer_kernel(
    shape, z_in, y_in, own_in, line, sends, last_faces, last_factor, edge, share, corner, faces, quotient, factor
):
    loads, comps, zlen, ylen, xlen = shape
    planes = loads * comps
    inner = zlen - 1
    first_core, index = on_first(), lax.axis_index("sz")
    top = first_core & (index == lax.axis_size("sz") - 1)
    more = lax.axis_index("sy") < lax.axis_size("sy") - 1
    stays, comes = jnp.where(first_core, 0, 1), jnp.where(first_core, jnp.where(top, 2, 1), 0)
    y_plus, y_diff = split_x(jnp.where(more, y_in[...], 0.0))
    come_rows = []
    for k in range(planes):
        for kind, value in enumerate(face_sums(z_in[k])):
            faces[kind, k, stays] = last_faces[kind, k]
            faces[kind, k, comes] = value
        come_rows.append(z_in[k % loads * comps + k // loads, ylen - 1 :])
        for group in range(2):
            rows = line[group, k * zlen + inner : (k + 1) * zlen], line[group, k * zlen : k * zlen + 1]
            corner[group, k : k + 1] = jnp.where(first_core, *rows)
    come_rows.append(jnp.zeros((-planes % TILE, xlen), jnp.float32))
    for group, value in enumerate(split_x(jnp.concatenate(come_rows, axis=0))):
        corner[2 + group, :planes] = value[:planes]
    below = jnp.where(index > 0, z_in[planes], 0.0)
    factor[...] = jnp.where(first_core, last_factor[...], below)
    corner[0, planes : planes + 1] = factor[ylen - 1 :]

    @pl.when(top)
    def _():
        clamped = jnp.zeros((ylen, xlen), jnp.float32)
        for k in range(planes):
            for slot in (1, 3):
                for kind in range(4):
                    faces[kind, k, slot] = clamped

    zeros = jnp.zeros((TILE, xlen), jnp.float32)
    quotient[:TILE] = zeros
    quotient[TILE + ylen :] = zeros
    for first in range(0, ylen, TILE):

        @pl.loop(0, xlen // LANES, unroll=True)
        def _(chunk):
            lanes = pl.ds(pl.multiple_of(chunk * LANES, LANES), LANES)
            (energy,) = tile_energies(faces, first, lanes, 1, loads, comps)
            here = energy * factor[first : first + TILE, lanes]
            quotient[first + TILE : first + 2 * TILE, lanes] = blank_last(here, first, ylen)

    @pl.when(top)
    def _():
        for first in range(0, ylen, TILE):

            @pl.loop(0, xlen // LANES, unroll=True)
            def _(chunk):
                lanes = pl.ds(pl.multiple_of(chunk * LANES, LANES), LANES)
                (energy,) = tile_energies(faces, first, lanes, 1, loads, comps, base=2)
                here = energy * factor[first : first + TILE, lanes]
                quotient[first + TILE : first + 2 * TILE, lanes] += blank_last(here, first, ylen)

    count = loads * zlen
    low, high = [], []
    for comp in range(comps):
        part = slice(comp * count, (comp + 1) * count)
        whole, change = line[0, part], line[1, part]
        whole_next, change_next = y_plus[part], y_diff[part]
        face = (whole + whole_next, change + change_next, whole_next - whole, change_next - change)
        low.append(face)
        high.append([pltpu.roll(value, count - 1, 0) for value in face])
    energy = quadratic(low, high, mode_weights())
    energy = sum(energy[case * zlen : case * zlen + inner] for case in range(loads)) * edge[:inner]
    last = spread_x(jnp.concatenate([energy, jnp.zeros((TILE - inner, xlen), jnp.float32)], axis=0))

    row = lax.broadcasted_iota(jnp.int32, (TILE, xlen), 0)
    rising = jnp.maximum(row - (TILE - 1 - ROWS), 0).astype(jnp.float32)
    ups, downs = [], []
    for z in range(inner):
        share[ylen * z : ylen * (z + 1)] = own_in[z]
        share[ylen * (z + 1) - TILE : ylen * (z + 1)] += rising * last[z : z + 1]
        here = sends[0, REACH * z : REACH * (z + 1)]
        ups += [here[r : r + 1] + float(REACH - r) * last[z : z + 1] for r in range(REACH)]
        downs.append(sends[1, REACH * z : REACH * (z + 1)])
    share[ylen * inner : ylen * zlen] = spread_x(spread_y(quotient, ylen))
    ahead, back = to_neighbours(quotient, ylen)
    ends = spread_x(jnp.concatenate(ahead + back + [zeros[:2]], axis=0))
    share[ylen * zlen :] = jnp.concatenate(ups + [ends[:REACH]] + downs + [ends[REACH : 2 * REACH]], axis=0)


def corner_line(shape, corner, y_in, d_in):
    loads, comps, zlen, ylen, xlen = shape
    planes = loads * comps
    first_core = on_first()
    top = first_core & (lax.axis_index("sz") == lax.axis_size("sz") - 1)
    more = lax.axis_index("sy") < lax.axis_size("sy") - 1
    rows = [jnp.where(first_core, y_in[(k + 1) * zlen - 1 : (k + 1) * zlen], y_in[k * zlen : k * zlen + 1]) for k in range(planes)]
    rows.append(jnp.zeros((-planes % TILE, xlen), jnp.float32))
    stays_next = split_x(jnp.where(more, jnp.concatenate(rows, axis=0), 0.0))
    comes_next = split_x(jnp.where(more, d_in[...], 0.0))
    zero = jnp.zeros((loads, xlen), jnp.float32)

    def face(near, far, comp, more_near, more_far):
        part = slice(comp * loads, (comp + 1) * loads)
        (whole, change), (whole_next, change_next) = (
            [jnp.concatenate([value[part], zero if extra is None else extra[part]], axis=0) for value, extra in zip(values, extras)]
            for values, extras in ((near, more_near), (far, more_far))
        )
        return whole + whole_next, change + change_next, whole_next - whole, change_next - change

    def under(stays, comes):
        return [jnp.where(first_core, a, b) for a, b in zip(stays, comes)], [jnp.where(top, b, 0.0) for b in comes]

    def over(stays, comes):
        return [jnp.where(first_core, jnp.where(top, 0.0, b), a) for a, b in zip(stays, comes)], (None, None)

    near, far = ((corner[0], corner[1]), (corner[2], corner[3])), (stays_next, comes_next)
    low, high = [], []
    for side, into in ((under, low), (over, high)):
        (near_own, near_more), (far_own, far_more) = side(*near), side(*far)
        into += [face(near_own, far_own, comp, near_more, far_more) for comp in range(comps)]
    energy = quadratic(low, high, mode_weights())
    line = sum(energy[case : case + 1] for case in range(2 * loads)) * corner[0, planes : planes + 1]
    return spread_x(jnp.concatenate([line, jnp.zeros((TILE - 1, xlen), jnp.float32)], axis=0))[:1]


def corner_kernel(shape, share_in, corner, y_in, d_in, share):
    _, _, zlen, ylen, xlen = shape
    line = corner_line(shape, corner, y_in, d_in)
    rising = jnp.maximum(lax.broadcasted_iota(jnp.int32, (TILE, xlen), 0) - (TILE - 1 - ROWS), 0).astype(jnp.float32)
    falling = (REACH - lax.broadcasted_iota(jnp.int32, (REACH, xlen), 0)).astype(jnp.float32)
    share[...] = share_in[...]
    share[ylen * zlen - TILE : ylen * zlen] += rising * line
    share[ylen * zlen + REACH * (zlen - 1) : ylen * zlen + REACH * zlen] += falling * line


def total_kernel(shape, share, other, h_out, z_out, y_out, d_out, e_out):
    _, _, zlen, ylen, xlen = shape
    first_core = on_first()
    inner, rows = zlen - 1, ylen * zlen
    reach = REACH * zlen

    def layers(first, count):
        mine, theirs = share[first + inner * count : first + zlen * count], other[first + inner * count : first + zlen * count]
        middle = share[first : first + inner * count] + other[first : first + inner * count]
        return jnp.where(first_core, theirs, mine), middle, jnp.where(first_core, mine, theirs)

    lowest, middle, highest = layers(0, ylen)
    h_out[0] = lowest
    for z in range(inner):
        h_out[z + 1] = middle[ylen * z : ylen * (z + 1)]
    h_out[zlen] = highest
    z_out[...] = h_out[pl.ds(jnp.where(first_core, 0, 1), zlen)]
    ups = jnp.concatenate(layers(rows, REACH), axis=0)
    downs = jnp.concatenate(layers(rows + reach, REACH), axis=0)
    y_out[: reach + REACH] = jnp.where(next_is_partner(lax.axis_index("load")), ups, downs)
    for out, used in ((y_out, reach + REACH), (d_out, reach), (e_out, reach)):
        out[used:] = jnp.zeros((out.shape[0] - used, xlen), jnp.float32)
    for out, start in ((d_out, 1), (e_out, 0)):
        rows = jnp.where(next_is_partner(start), ups, downs)
        out[:reach] = jnp.where(first_core, rows[:reach], rows[REACH:])


def layers_kernel(h, y_in, d_in, e_in, z_in, out):
    zlen, ylen, xlen = out.shape
    reach = REACH * zlen
    first_core = on_first()
    z_index, z_last = lax.axis_index("sz"), lax.axis_size("sz") - 1
    y_index, y_last = lax.axis_index("sy"), lax.axis_size("sy") - 1
    z_side = jnp.where(first_core, z_index < z_last, z_index > 0)
    y_next = next_is_partner(lax.axis_index("load"))
    y_side = jnp.where(y_next, y_index < y_last, y_index > 0)
    d_next, e_next = next_is_partner(1), next_is_partner(0)
    d_side, e_side = (jnp.where(up, y_index < y_last, y_index > 0) for up in (d_next, e_next))
    blank = jnp.zeros((TILE - REACH, xlen), jnp.float32)

    def at_start(rows):
        return jnp.concatenate([rows, blank], axis=0)

    def at_end(rows):
        return jnp.concatenate([blank, rows], axis=0)

    def ends(rows, keep, at_last):
        rows = jnp.where(keep, rows, 0.0)
        return at_start(jnp.where(at_last, 0.0, rows)), at_end(jnp.where(at_last, rows, 0.0))

    def with_ends(layer, *pairs):
        head, tail = layer[:TILE], layer[ylen - TILE :]
        for first, last in pairs:
            head, tail = head + first, tail + last
        return jnp.concatenate([head, layer[TILE : ylen - TILE], tail] if ylen > 2 * TILE else [head, tail], axis=0)

    own = []
    for k in range(zlen + 1):
        layer = jnp.where(first_core, h[k], 0.0)
        own.append(with_ends(layer, ends(y_in[REACH * k : REACH * (k + 1)], y_side, y_next)))
    come = []
    for k in range(zlen):
        part = slice(REACH * k, REACH * (k + 1))
        layer = jnp.where(z_side, z_in[k], 0.0)
        come.append(with_ends(layer, ends(d_in[part], z_side & d_side, d_next), ends(e_in[part], z_side & e_side, e_next)))
    below = [jnp.where(first_core, 0.0, layer) for layer in come[zlen - REACH :]]
    above = [jnp.where(first_core, layer, 0.0) for layer in come]
    layers = below[:-1] + [below[-1] + own[0]] + own[1:-1] + [own[-1] + above[0]] + above[1:]
    for z, layer in enumerate(spread_layers(layers)):
        out[z] = layer


def sum_kernel(part, other, out):
    out[...] = part[...] + other[...]


def call(kernel, outs, args, scratch=(), space=pltpu.VMEM):
    shapes = [jax.ShapeDtypeStruct(out, jnp.float32) if isinstance(out, tuple) else out for out in outs]
    return pl.pallas_call(
        kernel,
        out_shape=shapes,
        in_specs=[pl.BlockSpec(memory_space=space)] * len(args),
        out_specs=[pl.BlockSpec(memory_space=pltpu.VMEM)] * len(outs),
        scratch_shapes=list(scratch),
        compiler_params=pltpu.CompilerParams(vmem_limit_bytes=32 * 1024 * 1024),
    )(*args)


def ring_moved(value, axis):
    size = lax.axis_size(axis)
    return lax.ppermute(value, axis, [((k + 1) % size, k) for k in range(size)])


def chip_swapped(value):
    cores = lax.axis_size("load")
    return lax.ppermute(value, "load", [(core, cores - 1 - core) for core in range(cores)])


def opposed(value, z_step, y_step, y_shift=0, start=None):
    cores, rows, size = lax.axis_size("load"), lax.axis_size("sy"), lax.axis_size("sz")
    pairs = []
    for core in range(cores):
        sign = -1 if core else 1
        for y in range(rows):
            for z in range(size):
                to_y, to_z, side = y + sign * y_step, z + sign * z_step, core
                if start is not None:
                    to_y = y + 1 if (y - start) % 2 == 0 else y - 1
                if not (0 <= to_y < rows and 0 <= to_z < size):
                    to_y, to_z, side = y, z, cores - 1 - core
                to_y = (to_y + y_shift) % rows
                pairs.append(((core * rows + y) * size + z, (side * rows + to_y) * size + to_z))
    return lax.ppermute(value, ("load", "sy", "sz"), pairs)


def beside(value):
    cores, rows, size = lax.axis_size("load"), lax.axis_size("sy"), lax.axis_size("sz")
    pairs = []
    for core in range(cores):
        for y in range(rows):
            to_y = y + 1 if (y - core) % 2 == 0 else y - 1
            for z in range(size):
                target = (to_y, z) if 0 <= to_y < rows else (y, z ^ 1)
                pairs.append(((core * rows + y) * size + z, (core * rows + target[0]) * size + target[1]))
    return lax.ppermute(value, ("load", "sy", "sz"), pairs)


def body(displacements, density, solid, fixed):
    loads, comps, zlen, ylen, xlen = displacements.shape
    planes = loads * comps
    totals = (zlen * lax.axis_size("sz"), ylen * lax.axis_size("sy"))
    args = [
        pltpu.with_memory_space_constraint(arg, pltpu.HBM) for arg in (displacements, fixed, density, solid)
    ]

    d_send, z_send, y_send = call(
        lambda *refs: lead_kernel(totals, *refs),
        [(-(-planes // TILE) * TILE, xlen), (planes + 1, ylen, xlen), (planes * zlen, xlen)],
        args,
        scratch=[
            pltpu.VMEM((loads, comps, ylen, xlen), jnp.float32),
            pltpu.VMEM((ylen, xlen), jnp.int32),
            pltpu.VMEM((ylen, xlen), jnp.float32),
            pltpu.VMEM((ylen, xlen), jnp.int32),
            pltpu.VMEM((loads, comps, zlen, 1, xlen), jnp.float32),
            pltpu.VMEM((zlen, 1, xlen), jnp.int32),
            pltpu.SemaphoreType.DMA((6,)),
        ],
        space=pltpu.HBM,
    )
    d_in = opposed(d_send, -1, 0, y_shift=-1)
    z_in = opposed(z_send, -1, 0)
    y_in = ring_moved(y_send, "sy")
    faces = lambda layers: pltpu.VMEM((4, planes, layers, ylen, xlen), jnp.float32)
    inner = call(
        lambda *refs: inner_kernel(totals, *refs),
        [
            (zlen, ylen, xlen),
            (2, planes * zlen, xlen),
            (2, REACH * (zlen - 1), xlen),
            (4, planes, ylen, xlen),
            (ylen, xlen),
            (TILE, xlen),
        ],
        (displacements, fixed, density, solid),
        scratch=[faces(zlen), pltpu.VMEM((zlen - 1, ylen + 2 * TILE, xlen), jnp.float32)],
    )
    reach = REACH * zlen
    shape = displacements.shape
    share, corner = call(
        lambda *refs: outer_kernel(shape, *refs),
        [(ylen * zlen + 2 * reach, xlen), (4, -(-(planes + 1) // TILE) * TILE, xlen)],
        (z_in, y_in, *inner),
        scratch=[
            faces(4),
            pltpu.VMEM((ylen + 2 * TILE, xlen), jnp.float32),
            pltpu.VMEM((ylen, xlen), jnp.float32),
        ],
    )
    (share,) = call(
        lambda *refs: corner_kernel(shape, *refs), [(ylen * zlen + 2 * reach, xlen)], (share, corner, y_in, d_in)
    )
    sent = (-(-(reach + REACH) // TILE) * TILE, xlen)
    h, z_send, y_send, d_send, e_send = call(
        lambda *refs: total_kernel(displacements.shape, *refs),
        [
            (zlen + 1, ylen, xlen),
            (zlen, ylen, xlen),
            sent,
            sent,
            sent,
        ],
        (share, chip_swapped(share)),
    )
    d_in = opposed(d_send, -1, 0, start=1)
    e_in = opposed(e_send, -1, 0, start=0)
    y_in = beside(y_send)
    z_in = opposed(z_send, -1, 0)
    (part,) = call(layers_kernel, [(zlen, ylen, xlen)], (h, y_in, d_in, e_in, z_in))
    (out,) = call(sum_kernel, [(zlen, ylen, xlen)], (part, chip_swapped(part)))
    return out


def solution(mesh):
    return jax.shard_map(
        body,
        mesh=mesh,
        in_specs=(
            P("load", None, "sz", "sy", None),
            P("sz", "sy", None),
            P("sz", "sy", None),
            P("sz", "sy", None),
        ),
        out_specs=P("sz", "sy", None),
        check_vma=False,
    )
```

```python
import jax
import jax.numpy as jnp
import numpy as np
from jax import lax
from jax.experimental import pallas as pl
from jax.experimental.pallas import tpu as pltpu
from jax.sharding import PartitionSpec as P

OFFSETS = [(0, 0, 0), (1, 0, 0), (1, 1, 0), (0, 1, 0), (0, 0, 1), (1, 0, 1), (1, 1, 1), (0, 1, 1)]
REACH = 3
ROWS = REACH + 1
TILE = 8
LANES = 128


def element_matrix():
    corners = np.array(
        [
            [-1.0, -1.0, -1.0],
            [1.0, -1.0, -1.0],
            [1.0, 1.0, -1.0],
            [-1.0, 1.0, -1.0],
            [-1.0, -1.0, 1.0],
            [1.0, -1.0, 1.0],
            [1.0, 1.0, 1.0],
            [-1.0, 1.0, 1.0],
        ]
    )
    poisson = 0.3
    lame = poisson / ((1.0 + poisson) * (1.0 - 2.0 * poisson))
    shear = 1.0 / (2.0 * (1.0 + poisson))
    elastic = np.zeros((6, 6))
    elastic[:3, :3] = lame
    for k in range(3):
        elastic[k, k] += 2.0 * shear
        elastic[3 + k, 3 + k] = shear
    gauss = 1.0 / np.sqrt(3.0)
    stiffness = np.zeros((24, 24))
    for gi in range(2):
        for gj in range(2):
            for gk in range(2):
                point = np.array([(2 * gi - 1) * gauss, (2 * gj - 1) * gauss, (2 * gk - 1) * gauss])
                strain = np.zeros((6, 24))
                for node in range(8):
                    grads = np.zeros(3)
                    for k in range(3):
                        value = corners[node, k] / 8.0
                        for m in range(3):
                            if m != k:
                                value = value * (1.0 + point[m] * corners[node, m])
                        grads[k] = 2.0 * value
                    col = 3 * node
                    strain[0, col] = grads[0]
                    strain[1, col + 1] = grads[1]
                    strain[2, col + 2] = grads[2]
                    strain[3, col] = grads[1]
                    strain[3, col + 1] = grads[0]
                    strain[4, col + 1] = grads[2]
                    strain[4, col + 2] = grads[1]
                    strain[5, col] = grads[2]
                    strain[5, col + 2] = grads[0]
                stiffness += strain.T @ elastic @ strain / 8.0
    return stiffness


def mode_weights():
    modes = [(i, j, k) for k in (0, 1) for j in (0, 1) for i in (0, 1)]
    sums = np.zeros((24, 24))
    for m, mode in enumerate(modes):
        for n, corner in enumerate(OFFSETS):
            sign = np.prod([(1 if corner[d] else -1) if mode[d] else 1 for d in range(3)])
            for comp in range(3):
                sums[3 * m + comp, 3 * n + comp] = sign
    form = sums @ element_matrix() @ sums.T / 64.0

    def at(first, second):
        return form[3 * modes.index(first[1]) + first[0], 3 * modes.index(second[1]) + second[0]]

    ux, vy, uy = (0, (1, 0, 0)), (1, (0, 1, 0)), (0, (0, 1, 0))
    uxy, wyz = (0, (1, 1, 0)), (2, (0, 1, 1))
    wxy, vxz, uxyz = (2, (1, 1, 0)), (1, (1, 0, 1)), (0, (1, 1, 1))
    return dict(
        normal=at(ux, ux) - at(ux, vy),
        trace=at(ux, vy),
        shear=at(uy, uy),
        plus=(at(uxy, uxy) + at(uxy, wyz)) / 2,
        minus=(at(uxy, uxy) - at(uxy, wyz)) / 2,
        twist=at(wxy, wxy) - at(wxy, vxz),
        twist_sum=at(wxy, vxz),
        corner=at(uxyz, uxyz),
    )


def square(value):
    return value * value


def quadratic(low, high, weights):
    x = [low[c][1] + high[c][1] for c in range(3)]
    y = [low[c][2] + high[c][2] for c in range(3)]
    z = [high[c][0] - low[c][0] for c in range(3)]
    xy = [low[c][3] + high[c][3] for c in range(3)]
    xz = [high[c][1] - low[c][1] for c in range(3)]
    yz = [high[c][2] - low[c][2] for c in range(3)]
    xyz = [high[c][3] - low[c][3] for c in range(3)]
    normal = square(x[0]) + square(y[1]) + square(z[2])
    trace = square(x[0] + y[1] + z[2])
    shear = square(y[0] + x[1]) + square(z[0] + x[2]) + square(z[1] + y[2])
    pairs = ((xy[0], yz[2]), (xy[1], xz[2]), (xz[0], yz[1]))
    plus = sum(square(p + q) for p, q in pairs)
    minus = sum(square(p - q) for p, q in pairs)
    twist = square(xy[2]) + square(xz[1]) + square(yz[0])
    twist_sum = square(xy[2] + xz[1] + yz[0])
    corner = square(xyz[0]) + square(xyz[1]) + square(xyz[2])
    groups = dict(
        normal=normal, trace=trace, shear=shear, plus=plus, minus=minus, twist=twist, twist_sum=twist_sum, corner=corner
    )
    return sum(np.float32(weights[name]) * group for name, group in groups.items())


def line_weight(coord, count):
    def outside(distance):
        missing = jnp.maximum(REACH - distance, 0)
        return missing * (missing + 1) // 2

    whole = (REACH + 1) * (REACH + 1)
    return (whole - outside(coord) - outside(count - 1 - coord)).astype(jnp.float32)


def voxel_factor(density, solid, plane, first_row, total_z, total_y):
    rows, length = density.shape
    row = lax.broadcasted_iota(jnp.int32, (rows, length), 0) + first_row
    column = lax.broadcasted_iota(jnp.int32, (rows, length), 1)
    weight = line_weight(row, total_y) * line_weight(column, length)
    weight = weight * line_weight(jnp.full((rows, length), plane, jnp.int32), total_z)
    return solid.astype(jnp.float32) * (-3.0 * density * density) / weight


def spread_x(value):
    rows, length = value.shape
    wide = jnp.concatenate([value, jnp.zeros((rows, LANES), jnp.float32)], axis=1)
    span = length + LANES
    total = float(ROWS) * value
    for step in range(1, ROWS):
        both = pltpu.roll(wide, span - step, 1) + pltpu.roll(wide, step, 1)
        total = total + float(ROWS - step) * both[:, :length]
    return total


def spread_layers(layers):
    for step in (1, 2, 1, 2):
        layers = [layers[k] + layers[k + step] for k in range(len(layers) - step)]
    return layers


def held(disp, fixed, case, comp, z, rows):
    return disp[case, comp, z, rows] * (1.0 - fixed[z, rows].astype(jnp.float32))


def split_x(value):
    length = value.shape[1]
    column = lax.broadcasted_iota(jnp.int32, value.shape, 1)
    ahead = jnp.where(column == length - 1, 0.0, pltpu.roll(value, length - 1, 1))
    return value + ahead, ahead - value


def face_sums(value):
    following = pltpu.roll(value, value.shape[0] - 1, 0)
    both, along_x = split_x(value + following)
    along_y, mixed = split_x(following - value)
    return both, along_x, along_y, mixed


def spread_y(quotient, ylen):
    rows = [quotient[TILE + step : TILE + step + ylen] for step in range(-REACH, REACH + 1)]
    return sum((ROWS - abs(k - REACH)) * rows[k] for k in range(2 * REACH + 1))


def to_neighbours(quotient, ylen):
    top = quotient[ylen : ylen + TILE]
    base = quotient[TILE : 2 * TILE]
    ahead, back = [], []
    for row in range(REACH):
        ahead.append(sum(float(REACH - row - k) * top[TILE - 1 - k : TILE - k] for k in range(REACH - row)))
        back.append(sum(float(row + 1 - k) * base[k : k + 1] for k in range(row + 1)))
    return ahead, back


def next_is_partner(start):
    return (lax.axis_index("sy") - start) % 2 == 0


def on_first():
    return lax.axis_index("load") == 0


def lead_kernel(totals, disp_hbm, fixed_hbm, density_hbm, solid_hbm, d_out, z_out, y_out, layer, layer_fixed, density, solid, rows, rows_fixed, sems):
    loads, comps, zlen, ylen, _ = disp_hbm.shape
    gives = jnp.where(on_first(), 0, zlen - 1)
    copies = [
        pltpu.make_async_copy(source, target, sems.at[k])
        for k, (source, target) in enumerate(
            (
                (density_hbm.at[gives], density),
                (solid_hbm.at[gives], solid),
                (fixed_hbm.at[gives], layer_fixed),
                (disp_hbm.at[:, :, gives], layer),
                (fixed_hbm.at[:, :1], rows_fixed),
                (disp_hbm.at[:, :, :, :1], rows),
            )
        )
    ]
    for copy in reversed(copies):
        copy.start()
    for copy in copies[:2]:
        copy.wait()
    plane = lax.axis_index("sz") * zlen + gives
    base_y = lax.axis_index("sy") * ylen
    d_out[...] = jnp.zeros(d_out.shape, jnp.float32)
    z_out[loads * comps] = voxel_factor(density[...], solid[...], plane, base_y, *totals)
    for copy in copies[2:4]:
        copy.wait()
    free = 1.0 - layer_fixed[...].astype(jnp.float32)
    for case in range(loads):
        for comp in range(comps):
            k = case * comps + comp
            z_out[k] = layer[case, comp] * free
            at = comp * loads + case
            d_out[at : at + 1] = z_out[k, :1]
    for copy in copies[4:]:
        copy.wait()
    for z in range(zlen):
        free = 1.0 - rows_fixed[z, :1].astype(jnp.float32)
        for case in range(loads):
            for comp in range(comps):
                at = (comp * loads + case) * zlen + z
                y_out[at : at + 1] = rows[case, comp, z, :1] * free


def tile_energies(faces, first, lanes, layers, loads, comps, base=0):
    weights = mode_weights()
    energy = [None] * layers
    for case in range(loads):
        low = None
        for z in range(layers + 1):
            planes = [case * comps + comp for comp in range(comps)]
            high = [[faces[kind, k, base + z, first : first + TILE, lanes] for kind in range(4)] for k in planes]
            if low is not None:
                part = quadratic(low, high, weights)
                energy[z - 1] = part if energy[z - 1] is None else energy[z - 1] + part
            low = high
    return energy


def blank_last(value, first, ylen):
    row = lax.broadcasted_iota(jnp.int32, value.shape, 0) + first
    return jnp.where(row == ylen - 1, 0.0, value)


def inner_kernel(totals, disp, fixed, density, solid, own, line, sends, last_faces, last_factor, edge, faces, quotient):
    loads, comps, zlen, ylen, xlen = disp.shape
    total_z, total_y = totals
    base_z = lax.axis_index("sz") * zlen
    base_y = lax.axis_index("sy") * ylen
    inner = zlen - 1
    keeps = jnp.where(on_first(), inner, 0)
    free = [1.0 - fixed[z].astype(jnp.float32) for z in range(zlen)]

    for k in range(loads * comps):
        case, comp = k // comps, k % comps
        for z in range(zlen):
            plane = disp[case, comp, z] * free[z]
            for kind, value in enumerate(face_sums(plane)):
                faces[kind, k, z] = value
            at = (comp * loads + case) * zlen + z
            line[0, at : at + 1] = plane[ylen - 1 :]
        for kind in range(4):
            last_faces[kind, k] = faces[kind, k, keeps]

    line[0], line[1] = split_x(line[0])

    zeros = jnp.zeros((TILE, xlen), jnp.float32)
    edge[...] = jnp.zeros(edge.shape, jnp.float32)
    for z in range(zlen):
        factor = voxel_factor(density[z], solid[z], base_z + z, base_y, total_z, total_y)
        edge[z : z + 1] = factor[ylen - 1 :]
        if z == inner:
            last_factor[...] = factor
        else:
            quotient[z, :TILE] = zeros
            quotient[z, TILE : TILE + ylen] = factor
            quotient[z, TILE + ylen :] = zeros

    for first in range(0, ylen, TILE):

        @pl.loop(0, xlen // LANES, unroll=True)
        def _(chunk):
            lanes = pl.ds(pl.multiple_of(chunk * LANES, LANES), LANES)
            energy = tile_energies(faces, first, lanes, inner, loads, comps)
            for z in range(inner):
                here = quotient[z, first + TILE : first + 2 * TILE, lanes]
                quotient[z, first + TILE : first + 2 * TILE, lanes] = blank_last(energy[z] * here, first, ylen)

    for z in range(inner):
        own[z] = spread_x(spread_y(quotient.at[z], ylen))
        ahead, back = to_neighbours(quotient.at[z], ylen)
        ends = spread_x(jnp.concatenate(ahead + back + [zeros[:2]], axis=0))
        sends[0, REACH * z : REACH * (z + 1)] = ends[:REACH]
        sends[1, REACH * z : REACH * (z + 1)] = ends[REACH : 2 * REACH]


def outer_kernel(
    shape, z_in, y_in, own_in, line, sends, last_faces, last_factor, edge, share, corner, faces, quotient, factor
):
    loads, comps, zlen, ylen, xlen = shape
    planes = loads * comps
    inner = zlen - 1
    first_core, index = on_first(), lax.axis_index("sz")
    top = first_core & (index == lax.axis_size("sz") - 1)
    more = lax.axis_index("sy") < lax.axis_size("sy") - 1
    stays, comes = jnp.where(first_core, 0, 1), jnp.where(first_core, jnp.where(top, 2, 1), 0)
    y_plus, y_diff = split_x(jnp.where(more, y_in[...], 0.0))
    come_rows = []
    for k in range(planes):
        for kind, value in enumerate(face_sums(z_in[k])):
            faces[kind, k, stays] = last_faces[kind, k]
            faces[kind, k, comes] = value
        come_rows.append(z_in[k % loads * comps + k // loads, ylen - 1 :])
        for group in range(2):
            rows = line[group, k * zlen + inner : (k + 1) * zlen], line[group, k * zlen : k * zlen + 1]
            corner[group, k : k + 1] = jnp.where(first_core, *rows)
    come_rows.append(jnp.zeros((-planes % TILE, xlen), jnp.float32))
    for group, value in enumerate(split_x(jnp.concatenate(come_rows, axis=0))):
        corner[2 + group, :planes] = value[:planes]
    below = jnp.where(index > 0, z_in[planes], 0.0)
    factor[...] = jnp.where(first_core, last_factor[...], below)
    corner[0, planes : planes + 1] = factor[ylen - 1 :]

    @pl.when(top)
    def _():
        clamped = jnp.zeros((ylen, xlen), jnp.float32)
        for k in range(planes):
            for slot in (1, 3):
                for kind in range(4):
                    faces[kind, k, slot] = clamped

    zeros = jnp.zeros((TILE, xlen), jnp.float32)
    quotient[:TILE] = zeros
    quotient[TILE + ylen :] = zeros
    for first in range(0, ylen, TILE):

        @pl.loop(0, xlen // LANES, unroll=True)
        def _(chunk):
            lanes = pl.ds(pl.multiple_of(chunk * LANES, LANES), LANES)
            (energy,) = tile_energies(faces, first, lanes, 1, loads, comps)
            here = energy * factor[first : first + TILE, lanes]
            quotient[first + TILE : first + 2 * TILE, lanes] = blank_last(here, first, ylen)

    @pl.when(top)
    def _():
        for first in range(0, ylen, TILE):

            @pl.loop(0, xlen // LANES, unroll=True)
            def _(chunk):
                lanes = pl.ds(pl.multiple_of(chunk * LANES, LANES), LANES)
                (energy,) = tile_energies(faces, first, lanes, 1, loads, comps, base=2)
                here = energy * factor[first : first + TILE, lanes]
                quotient[first + TILE : first + 2 * TILE, lanes] += blank_last(here, first, ylen)

    count = loads * zlen
    low, high = [], []
    for comp in range(comps):
        part = slice(comp * count, (comp + 1) * count)
        whole, change = line[0, part], line[1, part]
        whole_next, change_next = y_plus[part], y_diff[part]
        face = (whole + whole_next, change + change_next, whole_next - whole, change_next - change)
        low.append(face)
        high.append([pltpu.roll(value, count - 1, 0) for value in face])
    energy = quadratic(low, high, mode_weights())
    energy = sum(energy[case * zlen : case * zlen + inner] for case in range(loads)) * edge[:inner]
    last = spread_x(jnp.concatenate([energy, jnp.zeros((TILE - inner, xlen), jnp.float32)], axis=0))

    row = lax.broadcasted_iota(jnp.int32, (TILE, xlen), 0)
    rising = jnp.maximum(row - (TILE - 1 - ROWS), 0).astype(jnp.float32)
    ups, downs = [], []
    for z in range(inner):
        share[ylen * z : ylen * (z + 1)] = own_in[z]
        share[ylen * (z + 1) - TILE : ylen * (z + 1)] += rising * last[z : z + 1]
        here = sends[0, REACH * z : REACH * (z + 1)]
        ups += [here[r : r + 1] + float(REACH - r) * last[z : z + 1] for r in range(REACH)]
        downs.append(sends[1, REACH * z : REACH * (z + 1)])
    share[ylen * inner : ylen * zlen] = spread_x(spread_y(quotient, ylen))
    ahead, back = to_neighbours(quotient, ylen)
    ends = spread_x(jnp.concatenate(ahead + back + [zeros[:2]], axis=0))
    share[ylen * zlen :] = jnp.concatenate(ups + [ends[:REACH]] + downs + [ends[REACH : 2 * REACH]], axis=0)


def corner_line(shape, corner, y_in, d_in):
    loads, comps, zlen, ylen, xlen = shape
    planes = loads * comps
    first_core = on_first()
    top = first_core & (lax.axis_index("sz") == lax.axis_size("sz") - 1)
    more = lax.axis_index("sy") < lax.axis_size("sy") - 1
    rows = [jnp.where(first_core, y_in[(k + 1) * zlen - 1 : (k + 1) * zlen], y_in[k * zlen : k * zlen + 1]) for k in range(planes)]
    rows.append(jnp.zeros((-planes % TILE, xlen), jnp.float32))
    stays_next = split_x(jnp.where(more, jnp.concatenate(rows, axis=0), 0.0))
    comes_next = split_x(jnp.where(more, d_in[...], 0.0))
    zero = jnp.zeros((loads, xlen), jnp.float32)

    def face(near, far, comp, more_near, more_far):
        part = slice(comp * loads, (comp + 1) * loads)
        (whole, change), (whole_next, change_next) = (
            [jnp.concatenate([value[part], zero if extra is None else extra[part]], axis=0) for value, extra in zip(values, extras)]
            for values, extras in ((near, more_near), (far, more_far))
        )
        return whole + whole_next, change + change_next, whole_next - whole, change_next - change

    def under(stays, comes):
        return [jnp.where(first_core, a, b) for a, b in zip(stays, comes)], [jnp.where(top, b, 0.0) for b in comes]

    def over(stays, comes):
        return [jnp.where(first_core, jnp.where(top, 0.0, b), a) for a, b in zip(stays, comes)], (None, None)

    near, far = ((corner[0], corner[1]), (corner[2], corner[3])), (stays_next, comes_next)
    low, high = [], []
    for side, into in ((under, low), (over, high)):
        (near_own, near_more), (far_own, far_more) = side(*near), side(*far)
        into += [face(near_own, far_own, comp, near_more, far_more) for comp in range(comps)]
    energy = quadratic(low, high, mode_weights())
    line = sum(energy[case : case + 1] for case in range(2 * loads)) * corner[0, planes : planes + 1]
    return spread_x(jnp.concatenate([line, jnp.zeros((TILE - 1, xlen), jnp.float32)], axis=0))[:1]


def corner_kernel(shape, share_in, corner, y_in, d_in, share):
    _, _, zlen, ylen, xlen = shape
    line = corner_line(shape, corner, y_in, d_in)
    rising = jnp.maximum(lax.broadcasted_iota(jnp.int32, (TILE, xlen), 0) - (TILE - 1 - ROWS), 0).astype(jnp.float32)
    falling = (REACH - lax.broadcasted_iota(jnp.int32, (REACH, xlen), 0)).astype(jnp.float32)
    share[...] = share_in[...]
    share[ylen * zlen - TILE : ylen * zlen] += rising * line
    share[ylen * zlen + REACH * (zlen - 1) : ylen * zlen + REACH * zlen] += falling * line


def total_kernel(shape, share, other, h_out, z_out, y_out, d_out, e_out):
    _, _, zlen, ylen, xlen = shape
    first_core = on_first()
    inner, rows = zlen - 1, ylen * zlen
    reach = REACH * zlen

    def layers(first, count):
        mine, theirs = share[first + inner * count : first + zlen * count], other[first + inner * count : first + zlen * count]
        middle = share[first : first + inner * count] + other[first : first + inner * count]
        return jnp.where(first_core, theirs, mine), middle, jnp.where(first_core, mine, theirs)

    lowest, middle, highest = layers(0, ylen)
    h_out[0] = lowest
    for z in range(inner):
        h_out[z + 1] = middle[ylen * z : ylen * (z + 1)]
    h_out[zlen] = highest
    z_out[...] = h_out[pl.ds(jnp.where(first_core, 0, 1), zlen)]
    ups = jnp.concatenate(layers(rows, REACH), axis=0)
    downs = jnp.concatenate(layers(rows + reach, REACH), axis=0)
    y_out[: reach + REACH] = jnp.where(next_is_partner(lax.axis_index("load")), ups, downs)
    for out, used in ((y_out, reach + REACH), (d_out, reach), (e_out, reach)):
        out[used:] = jnp.zeros((out.shape[0] - used, xlen), jnp.float32)
    for out, start in ((d_out, 1), (e_out, 0)):
        rows = jnp.where(next_is_partner(start), ups, downs)
        out[:reach] = jnp.where(first_core, rows[:reach], rows[REACH:])


def layers_kernel(h, d_in, e_in, y_in, z_in, out):
    zlen, ylen, xlen = out.shape
    reach = REACH * zlen
    first_core = on_first()
    z_index, z_last = lax.axis_index("sz"), lax.axis_size("sz") - 1
    y_index, y_last = lax.axis_index("sy"), lax.axis_size("sy") - 1
    z_side = jnp.where(first_core, z_index < z_last, z_index > 0)
    y_next = next_is_partner(lax.axis_index("load"))
    y_side = jnp.where(y_next, y_index < y_last, y_index > 0)
    d_next, e_next = next_is_partner(1), next_is_partner(0)
    d_side, e_side = (jnp.where(up, y_index < y_last, y_index > 0) for up in (d_next, e_next))
    blank = jnp.zeros((TILE - REACH, xlen), jnp.float32)

    def at_start(rows):
        return jnp.concatenate([rows, blank], axis=0)

    def at_end(rows):
        return jnp.concatenate([blank, rows], axis=0)

    def ends(rows, keep, at_last):
        rows = jnp.where(keep, rows, 0.0)
        return at_start(jnp.where(at_last, 0.0, rows)), at_end(jnp.where(at_last, rows, 0.0))

    def with_ends(layer, *pairs):
        head, tail = layer[:TILE], layer[ylen - TILE :]
        for first, last in pairs:
            head, tail = head + first, tail + last
        return jnp.concatenate([head, layer[TILE : ylen - TILE], tail] if ylen > 2 * TILE else [head, tail], axis=0)

    own = []
    for k in range(zlen + 1):
        layer = jnp.where(first_core, h[k], 0.0)
        own.append(with_ends(layer, ends(y_in[REACH * k : REACH * (k + 1)], y_side, y_next)))
    come = []
    for k in range(zlen):
        part = slice(REACH * k, REACH * (k + 1))
        layer = jnp.where(z_side, z_in[k], 0.0)
        come.append(with_ends(layer, ends(d_in[part], z_side & d_side, d_next), ends(e_in[part], z_side & e_side, e_next)))
    below = [jnp.where(first_core, 0.0, layer) for layer in come[zlen - REACH :]]
    above = [jnp.where(first_core, layer, 0.0) for layer in come]
    layers = below[:-1] + [below[-1] + own[0]] + own[1:-1] + [own[-1] + above[0]] + above[1:]
    for z, layer in enumerate(spread_layers(layers)):
        out[z] = layer


def sum_kernel(part, other, out):
    out[...] = part[...] + other[...]


def call(kernel, outs, args, scratch=(), space=pltpu.VMEM):
    shapes = [jax.ShapeDtypeStruct(out, jnp.float32) if isinstance(out, tuple) else out for out in outs]
    return pl.pallas_call(
        kernel,
        out_shape=shapes,
        in_specs=[pl.BlockSpec(memory_space=space)] * len(args),
        out_specs=[pl.BlockSpec(memory_space=pltpu.VMEM)] * len(outs),
        scratch_shapes=list(scratch),
        compiler_params=pltpu.CompilerParams(vmem_limit_bytes=32 * 1024 * 1024),
    )(*args)


def ring_moved(value, axis):
    size = lax.axis_size(axis)
    return lax.ppermute(value, axis, [((k + 1) % size, k) for k in range(size)])


def chip_swapped(value):
    cores = lax.axis_size("load")
    return lax.ppermute(value, "load", [(core, cores - 1 - core) for core in range(cores)])


def opposed(value, z_step, y_step, y_shift=0, start=None):
    cores, rows, size = lax.axis_size("load"), lax.axis_size("sy"), lax.axis_size("sz")
    pairs = []
    for core in range(cores):
        sign = -1 if core else 1
        for y in range(rows):
            for z in range(size):
                to_y, to_z, side = y + sign * y_step, z + sign * z_step, core
                if start is not None:
                    to_y = y + 1 if (y - start) % 2 == 0 else y - 1
                if not (0 <= to_y < rows and 0 <= to_z < size):
                    to_y, to_z, side = y, z, cores - 1 - core
                to_y = (to_y + y_shift) % rows
                pairs.append(((core * rows + y) * size + z, (side * rows + to_y) * size + to_z))
    return lax.ppermute(value, ("load", "sy", "sz"), pairs)


def beside(value):
    cores, rows, size = lax.axis_size("load"), lax.axis_size("sy"), lax.axis_size("sz")
    pairs = []
    for core in range(cores):
        for y in range(rows):
            to_y = y + 1 if (y - core) % 2 == 0 else y - 1
            for z in range(size):
                target = (to_y, z) if 0 <= to_y < rows else (y, z ^ 1)
                pairs.append(((core * rows + y) * size + z, (core * rows + target[0]) * size + target[1]))
    return lax.ppermute(value, ("load", "sy", "sz"), pairs)


def body(displacements, density, solid, fixed):
    loads, comps, zlen, ylen, xlen = displacements.shape
    planes = loads * comps
    totals = (zlen * lax.axis_size("sz"), ylen * lax.axis_size("sy"))
    args = [
        pltpu.with_memory_space_constraint(arg, pltpu.HBM) for arg in (displacements, fixed, density, solid)
    ]

    d_send, z_send, y_send = call(
        lambda *refs: lead_kernel(totals, *refs),
        [(-(-planes // TILE) * TILE, xlen), (planes + 1, ylen, xlen), (planes * zlen, xlen)],
        args,
        scratch=[
            pltpu.VMEM((loads, comps, ylen, xlen), jnp.float32),
            pltpu.VMEM((ylen, xlen), jnp.int32),
            pltpu.VMEM((ylen, xlen), jnp.float32),
            pltpu.VMEM((ylen, xlen), jnp.int32),
            pltpu.VMEM((loads, comps, zlen, 1, xlen), jnp.float32),
            pltpu.VMEM((zlen, 1, xlen), jnp.int32),
            pltpu.SemaphoreType.DMA((6,)),
        ],
        space=pltpu.HBM,
    )
    d_in = opposed(d_send, -1, 0, y_shift=-1)
    z_in = opposed(z_send, -1, 0)
    y_in = ring_moved(y_send, "sy")
    faces = lambda layers: pltpu.VMEM((4, planes, layers, ylen, xlen), jnp.float32)
    inner = call(
        lambda *refs: inner_kernel(totals, *refs),
        [
            (zlen, ylen, xlen),
            (2, planes * zlen, xlen),
            (2, REACH * (zlen - 1), xlen),
            (4, planes, ylen, xlen),
            (ylen, xlen),
            (TILE, xlen),
        ],
        (displacements, fixed, density, solid),
        scratch=[faces(zlen), pltpu.VMEM((zlen - 1, ylen + 2 * TILE, xlen), jnp.float32)],
    )
    reach = REACH * zlen
    shape = displacements.shape
    share, corner = call(
        lambda *refs: outer_kernel(shape, *refs),
        [(ylen * zlen + 2 * reach, xlen), (4, -(-(planes + 1) // TILE) * TILE, xlen)],
        (z_in, y_in, *inner),
        scratch=[
            faces(4),
            pltpu.VMEM((ylen + 2 * TILE, xlen), jnp.float32),
            pltpu.VMEM((ylen, xlen), jnp.float32),
        ],
    )
    (share,) = call(
        lambda *refs: corner_kernel(shape, *refs), [(ylen * zlen + 2 * reach, xlen)], (share, corner, y_in, d_in)
    )
    sent = (-(-(reach + REACH) // TILE) * TILE, xlen)
    h, z_send, y_send, d_send, e_send = call(
        lambda *refs: total_kernel(displacements.shape, *refs),
        [
            (zlen + 1, ylen, xlen),
            (zlen, ylen, xlen),
            sent,
            sent,
            sent,
        ],
        (share, chip_swapped(share)),
    )
    d_in = opposed(d_send, -1, 0, start=1)
    e_in = opposed(e_send, -1, 0, start=0)
    y_in = beside(y_send)
    z_in = opposed(z_send, -1, 0)
    (part,) = call(layers_kernel, [(zlen, ylen, xlen)], (h, d_in, e_in, y_in, z_in))
    (out,) = call(sum_kernel, [(zlen, ylen, xlen)], (part, chip_swapped(part)))
    return out


def solution(mesh):
    return jax.shard_map(
        body,
        mesh=mesh,
        in_specs=(
            P("load", None, "sz", "sy", None),
            P("sz", "sy", None),
            P("sz", "sy", None),
            P("sz", "sy", None),
        ),
        out_specs=P("sz", "sy", None),
        check_vma=False,
    )
```

```python
import jax
import jax.numpy as jnp
import numpy as np
from jax import lax
from jax.experimental import pallas as pl
from jax.experimental.pallas import tpu as pltpu
from jax.sharding import PartitionSpec as P

OFFSETS = [(0, 0, 0), (1, 0, 0), (1, 1, 0), (0, 1, 0), (0, 0, 1), (1, 0, 1), (1, 1, 1), (0, 1, 1)]
REACH = 3
ROWS = REACH + 1
TILE = 8
LANES = 128


def element_matrix():
    corners = np.array(
        [
            [-1.0, -1.0, -1.0],
            [1.0, -1.0, -1.0],
            [1.0, 1.0, -1.0],
            [-1.0, 1.0, -1.0],
            [-1.0, -1.0, 1.0],
            [1.0, -1.0, 1.0],
            [1.0, 1.0, 1.0],
            [-1.0, 1.0, 1.0],
        ]
    )
    poisson = 0.3
    lame = poisson / ((1.0 + poisson) * (1.0 - 2.0 * poisson))
    shear = 1.0 / (2.0 * (1.0 + poisson))
    elastic = np.zeros((6, 6))
    elastic[:3, :3] = lame
    for k in range(3):
        elastic[k, k] += 2.0 * shear
        elastic[3 + k, 3 + k] = shear
    gauss = 1.0 / np.sqrt(3.0)
    stiffness = np.zeros((24, 24))
    for gi in range(2):
        for gj in range(2):
            for gk in range(2):
                point = np.array([(2 * gi - 1) * gauss, (2 * gj - 1) * gauss, (2 * gk - 1) * gauss])
                strain = np.zeros((6, 24))
                for node in range(8):
                    grads = np.zeros(3)
                    for k in range(3):
                        value = corners[node, k] / 8.0
                        for m in range(3):
                            if m != k:
                                value = value * (1.0 + point[m] * corners[node, m])
                        grads[k] = 2.0 * value
                    col = 3 * node
                    strain[0, col] = grads[0]
                    strain[1, col + 1] = grads[1]
                    strain[2, col + 2] = grads[2]
                    strain[3, col] = grads[1]
                    strain[3, col + 1] = grads[0]
                    strain[4, col + 1] = grads[2]
                    strain[4, col + 2] = grads[1]
                    strain[5, col] = grads[2]
                    strain[5, col + 2] = grads[0]
                stiffness += strain.T @ elastic @ strain / 8.0
    return stiffness


def mode_weights():
    modes = [(i, j, k) for k in (0, 1) for j in (0, 1) for i in (0, 1)]
    sums = np.zeros((24, 24))
    for m, mode in enumerate(modes):
        for n, corner in enumerate(OFFSETS):
            sign = np.prod([(1 if corner[d] else -1) if mode[d] else 1 for d in range(3)])
            for comp in range(3):
                sums[3 * m + comp, 3 * n + comp] = sign
    form = sums @ element_matrix() @ sums.T / 64.0

    def at(first, second):
        return form[3 * modes.index(first[1]) + first[0], 3 * modes.index(second[1]) + second[0]]

    ux, vy, uy = (0, (1, 0, 0)), (1, (0, 1, 0)), (0, (0, 1, 0))
    uxy, wyz = (0, (1, 1, 0)), (2, (0, 1, 1))
    wxy, vxz, uxyz = (2, (1, 1, 0)), (1, (1, 0, 1)), (0, (1, 1, 1))
    return dict(
        normal=at(ux, ux) - at(ux, vy),
        trace=at(ux, vy),
        shear=at(uy, uy),
        plus=(at(uxy, uxy) + at(uxy, wyz)) / 2,
        minus=(at(uxy, uxy) - at(uxy, wyz)) / 2,
        twist=at(wxy, wxy) - at(wxy, vxz),
        twist_sum=at(wxy, vxz),
        corner=at(uxyz, uxyz),
    )


def square(value):
    return value * value


def quadratic(low, high, weights):
    x = [low[c][1] + high[c][1] for c in range(3)]
    y = [low[c][2] + high[c][2] for c in range(3)]
    z = [high[c][0] - low[c][0] for c in range(3)]
    xy = [low[c][3] + high[c][3] for c in range(3)]
    xz = [high[c][1] - low[c][1] for c in range(3)]
    yz = [high[c][2] - low[c][2] for c in range(3)]
    xyz = [high[c][3] - low[c][3] for c in range(3)]
    normal = square(x[0]) + square(y[1]) + square(z[2])
    trace = square(x[0] + y[1] + z[2])
    shear = square(y[0] + x[1]) + square(z[0] + x[2]) + square(z[1] + y[2])
    pairs = ((xy[0], yz[2]), (xy[1], xz[2]), (xz[0], yz[1]))
    plus = sum(square(p + q) for p, q in pairs)
    minus = sum(square(p - q) for p, q in pairs)
    twist = square(xy[2]) + square(xz[1]) + square(yz[0])
    twist_sum = square(xy[2] + xz[1] + yz[0])
    corner = square(xyz[0]) + square(xyz[1]) + square(xyz[2])
    groups = dict(
        normal=normal, trace=trace, shear=shear, plus=plus, minus=minus, twist=twist, twist_sum=twist_sum, corner=corner
    )
    return sum(np.float32(weights[name]) * group for name, group in groups.items())


def line_weight(coord, count):
    def outside(distance):
        missing = jnp.maximum(REACH - distance, 0)
        return missing * (missing + 1) // 2

    whole = (REACH + 1) * (REACH + 1)
    return (whole - outside(coord) - outside(count - 1 - coord)).astype(jnp.float32)


def voxel_factor(density, solid, plane, first_row, total_z, total_y):
    rows, length = density.shape
    row = lax.broadcasted_iota(jnp.int32, (rows, length), 0) + first_row
    column = lax.broadcasted_iota(jnp.int32, (rows, length), 1)
    weight = line_weight(row, total_y) * line_weight(column, length)
    weight = weight * line_weight(jnp.full((rows, length), plane, jnp.int32), total_z)
    return solid.astype(jnp.float32) * (-3.0 * density * density) / weight


def spread_x(value):
    rows, length = value.shape
    wide = jnp.concatenate([value, jnp.zeros((rows, LANES), jnp.float32)], axis=1)
    span = length + LANES
    total = float(ROWS) * value
    for step in range(1, ROWS):
        both = pltpu.roll(wide, span - step, 1) + pltpu.roll(wide, step, 1)
        total = total + float(ROWS - step) * both[:, :length]
    return total


def spread_layers(layers):
    for step in (1, 2, 1, 2):
        layers = [layers[k] + layers[k + step] for k in range(len(layers) - step)]
    return layers


def held(disp, fixed, case, comp, z, rows):
    return disp[case, comp, z, rows] * (1.0 - fixed[z, rows].astype(jnp.float32))


def split_x(value):
    length = value.shape[1]
    column = lax.broadcasted_iota(jnp.int32, value.shape, 1)
    ahead = jnp.where(column == length - 1, 0.0, pltpu.roll(value, length - 1, 1))
    return value + ahead, ahead - value


def face_sums(value):
    following = pltpu.roll(value, value.shape[0] - 1, 0)
    both, along_x = split_x(value + following)
    along_y, mixed = split_x(following - value)
    return both, along_x, along_y, mixed


def spread_y(quotient, ylen):
    rows = [quotient[TILE + step : TILE + step + ylen] for step in range(-REACH, REACH + 1)]
    return sum((ROWS - abs(k - REACH)) * rows[k] for k in range(2 * REACH + 1))


def to_neighbours(quotient, ylen):
    top = quotient[ylen : ylen + TILE]
    base = quotient[TILE : 2 * TILE]
    ahead, back = [], []
    for row in range(REACH):
        ahead.append(sum(float(REACH - row - k) * top[TILE - 1 - k : TILE - k] for k in range(REACH - row)))
        back.append(sum(float(row + 1 - k) * base[k : k + 1] for k in range(row + 1)))
    return ahead, back


def next_is_partner(start):
    return (lax.axis_index("sy") - start) % 2 == 0


def on_first():
    return lax.axis_index("load") == 0


def lead_kernel(totals, disp_hbm, fixed_hbm, density_hbm, solid_hbm, d_out, z_out, y_out, layer, layer_fixed, density, solid, rows, rows_fixed, sems):
    loads, comps, zlen, ylen, _ = disp_hbm.shape
    gives = jnp.where(on_first(), 0, zlen - 1)
    copies = [
        pltpu.make_async_copy(source, target, sems.at[k])
        for k, (source, target) in enumerate(
            (
                (density_hbm.at[gives], density),
                (solid_hbm.at[gives], solid),
                (fixed_hbm.at[gives], layer_fixed),
                (disp_hbm.at[:, :, gives], layer),
                (fixed_hbm.at[:, :1], rows_fixed),
                (disp_hbm.at[:, :, :, :1], rows),
            )
        )
    ]
    for copy in copies[3:4] + copies[:3] + copies[4:]:
        copy.start()
    for copy in copies[:2]:
        copy.wait()
    plane = lax.axis_index("sz") * zlen + gives
    base_y = lax.axis_index("sy") * ylen
    d_out[...] = jnp.zeros(d_out.shape, jnp.float32)
    z_out[loads * comps] = voxel_factor(density[...], solid[...], plane, base_y, *totals)
    for copy in copies[2:4]:
        copy.wait()
    free = 1.0 - layer_fixed[...].astype(jnp.float32)
    for case in range(loads):
        for comp in range(comps):
            k = case * comps + comp
            z_out[k] = layer[case, comp] * free
            at = comp * loads + case
            d_out[at : at + 1] = z_out[k, :1]
    for copy in copies[4:]:
        copy.wait()
    for z in range(zlen):
        free = 1.0 - rows_fixed[z, :1].astype(jnp.float32)
        for case in range(loads):
            for comp in range(comps):
                at = (comp * loads + case) * zlen + z
                y_out[at : at + 1] = rows[case, comp, z, :1] * free


def tile_energies(faces, first, lanes, layers, loads, comps, base=0):
    weights = mode_weights()
    energy = [None] * layers
    for case in range(loads):
        low = None
        for z in range(layers + 1):
            planes = [case * comps + comp for comp in range(comps)]
            high = [[faces[kind, k, base + z, first : first + TILE, lanes] for kind in range(4)] for k in planes]
            if low is not None:
                part = quadratic(low, high, weights)
                energy[z - 1] = part if energy[z - 1] is None else energy[z - 1] + part
            low = high
    return energy


def blank_last(value, first, ylen):
    row = lax.broadcasted_iota(jnp.int32, value.shape, 0) + first
    return jnp.where(row == ylen - 1, 0.0, value)


def inner_kernel(totals, disp, fixed, density, solid, own, line, sends, last_faces, last_factor, edge, faces, quotient):
    loads, comps, zlen, ylen, xlen = disp.shape
    total_z, total_y = totals
    base_z = lax.axis_index("sz") * zlen
    base_y = lax.axis_index("sy") * ylen
    inner = zlen - 1
    keeps = jnp.where(on_first(), inner, 0)
    free = [1.0 - fixed[z].astype(jnp.float32) for z in range(zlen)]

    for k in range(loads * comps):
        case, comp = k // comps, k % comps
        for z in range(zlen):
            plane = disp[case, comp, z] * free[z]
            for kind, value in enumerate(face_sums(plane)):
                faces[kind, k, z] = value
            at = (comp * loads + case) * zlen + z
            line[0, at : at + 1] = plane[ylen - 1 :]
        for kind in range(4):
            last_faces[kind, k] = faces[kind, k, keeps]

    line[0], line[1] = split_x(line[0])

    zeros = jnp.zeros((TILE, xlen), jnp.float32)
    edge[...] = jnp.zeros(edge.shape, jnp.float32)
    for z in range(zlen):
        factor = voxel_factor(density[z], solid[z], base_z + z, base_y, total_z, total_y)
        edge[z : z + 1] = factor[ylen - 1 :]
        if z == inner:
            last_factor[...] = factor
        else:
            quotient[z, :TILE] = zeros
            quotient[z, TILE : TILE + ylen] = factor
            quotient[z, TILE + ylen :] = zeros

    for first in range(0, ylen, TILE):

        @pl.loop(0, xlen // LANES, unroll=True)
        def _(chunk):
            lanes = pl.ds(pl.multiple_of(chunk * LANES, LANES), LANES)
            energy = tile_energies(faces, first, lanes, inner, loads, comps)
            for z in range(inner):
                here = quotient[z, first + TILE : first + 2 * TILE, lanes]
                quotient[z, first + TILE : first + 2 * TILE, lanes] = blank_last(energy[z] * here, first, ylen)

    for z in range(inner):
        own[z] = spread_x(spread_y(quotient.at[z], ylen))
        ahead, back = to_neighbours(quotient.at[z], ylen)
        ends = spread_x(jnp.concatenate(ahead + back + [zeros[:2]], axis=0))
        sends[0, REACH * z : REACH * (z + 1)] = ends[:REACH]
        sends[1, REACH * z : REACH * (z + 1)] = ends[REACH : 2 * REACH]


def outer_kernel(
    shape, z_in, y_in, own_in, line, sends, last_faces, last_factor, edge, share, corner, faces, quotient, factor
):
    loads, comps, zlen, ylen, xlen = shape
    planes = loads * comps
    inner = zlen - 1
    first_core, index = on_first(), lax.axis_index("sz")
    top = first_core & (index == lax.axis_size("sz") - 1)
    more = lax.axis_index("sy") < lax.axis_size("sy") - 1
    stays, comes = jnp.where(first_core, 0, 1), jnp.where(first_core, jnp.where(top, 2, 1), 0)
    y_plus, y_diff = split_x(jnp.where(more, y_in[...], 0.0))
    come_rows = []
    for k in range(planes):
        for kind, value in enumerate(face_sums(z_in[k])):
            faces[kind, k, stays] = last_faces[kind, k]
            faces[kind, k, comes] = value
        come_rows.append(z_in[k % loads * comps + k // loads, ylen - 1 :])
        for group in range(2):
            rows = line[group, k * zlen + inner : (k + 1) * zlen], line[group, k * zlen : k * zlen + 1]
            corner[group, k : k + 1] = jnp.where(first_core, *rows)
    come_rows.append(jnp.zeros((-planes % TILE, xlen), jnp.float32))
    for group, value in enumerate(split_x(jnp.concatenate(come_rows, axis=0))):
        corner[2 + group, :planes] = value[:planes]
    below = jnp.where(index > 0, z_in[planes], 0.0)
    factor[...] = jnp.where(first_core, last_factor[...], below)
    corner[0, planes : planes + 1] = factor[ylen - 1 :]

    @pl.when(top)
    def _():
        clamped = jnp.zeros((ylen, xlen), jnp.float32)
        for k in range(planes):
            for slot in (1, 3):
                for kind in range(4):
                    faces[kind, k, slot] = clamped

    zeros = jnp.zeros((TILE, xlen), jnp.float32)
    quotient[:TILE] = zeros
    quotient[TILE + ylen :] = zeros
    for first in range(0, ylen, TILE):

        @pl.loop(0, xlen // LANES, unroll=True)
        def _(chunk):
            lanes = pl.ds(pl.multiple_of(chunk * LANES, LANES), LANES)
            (energy,) = tile_energies(faces, first, lanes, 1, loads, comps)
            here = energy * factor[first : first + TILE, lanes]
            quotient[first + TILE : first + 2 * TILE, lanes] = blank_last(here, first, ylen)

    @pl.when(top)
    def _():
        for first in range(0, ylen, TILE):

            @pl.loop(0, xlen // LANES, unroll=True)
            def _(chunk):
                lanes = pl.ds(pl.multiple_of(chunk * LANES, LANES), LANES)
                (energy,) = tile_energies(faces, first, lanes, 1, loads, comps, base=2)
                here = energy * factor[first : first + TILE, lanes]
                quotient[first + TILE : first + 2 * TILE, lanes] += blank_last(here, first, ylen)

    count = loads * zlen
    low, high = [], []
    for comp in range(comps):
        part = slice(comp * count, (comp + 1) * count)
        whole, change = line[0, part], line[1, part]
        whole_next, change_next = y_plus[part], y_diff[part]
        face = (whole + whole_next, change + change_next, whole_next - whole, change_next - change)
        low.append(face)
        high.append([pltpu.roll(value, count - 1, 0) for value in face])
    energy = quadratic(low, high, mode_weights())
    energy = sum(energy[case * zlen : case * zlen + inner] for case in range(loads)) * edge[:inner]
    last = spread_x(jnp.concatenate([energy, jnp.zeros((TILE - inner, xlen), jnp.float32)], axis=0))

    row = lax.broadcasted_iota(jnp.int32, (TILE, xlen), 0)
    rising = jnp.maximum(row - (TILE - 1 - ROWS), 0).astype(jnp.float32)
    ups, downs = [], []
    for z in range(inner):
        share[ylen * z : ylen * (z + 1)] = own_in[z]
        share[ylen * (z + 1) - TILE : ylen * (z + 1)] += rising * last[z : z + 1]
        here = sends[0, REACH * z : REACH * (z + 1)]
        ups += [here[r : r + 1] + float(REACH - r) * last[z : z + 1] for r in range(REACH)]
        downs.append(sends[1, REACH * z : REACH * (z + 1)])
    share[ylen * inner : ylen * zlen] = spread_x(spread_y(quotient, ylen))
    ahead, back = to_neighbours(quotient, ylen)
    ends = spread_x(jnp.concatenate(ahead + back + [zeros[:2]], axis=0))
    share[ylen * zlen :] = jnp.concatenate(ups + [ends[:REACH]] + downs + [ends[REACH : 2 * REACH]], axis=0)


def corner_line(shape, corner, y_in, d_in):
    loads, comps, zlen, ylen, xlen = shape
    planes = loads * comps
    first_core = on_first()
    top = first_core & (lax.axis_index("sz") == lax.axis_size("sz") - 1)
    more = lax.axis_index("sy") < lax.axis_size("sy") - 1
    rows = [jnp.where(first_core, y_in[(k + 1) * zlen - 1 : (k + 1) * zlen], y_in[k * zlen : k * zlen + 1]) for k in range(planes)]
    rows.append(jnp.zeros((-planes % TILE, xlen), jnp.float32))
    stays_next = split_x(jnp.where(more, jnp.concatenate(rows, axis=0), 0.0))
    comes_next = split_x(jnp.where(more, d_in[...], 0.0))
    zero = jnp.zeros((loads, xlen), jnp.float32)

    def face(near, far, comp, more_near, more_far):
        part = slice(comp * loads, (comp + 1) * loads)
        (whole, change), (whole_next, change_next) = (
            [jnp.concatenate([value[part], zero if extra is None else extra[part]], axis=0) for value, extra in zip(values, extras)]
            for values, extras in ((near, more_near), (far, more_far))
        )
        return whole + whole_next, change + change_next, whole_next - whole, change_next - change

    def under(stays, comes):
        return [jnp.where(first_core, a, b) for a, b in zip(stays, comes)], [jnp.where(top, b, 0.0) for b in comes]

    def over(stays, comes):
        return [jnp.where(first_core, jnp.where(top, 0.0, b), a) for a, b in zip(stays, comes)], (None, None)

    near, far = ((corner[0], corner[1]), (corner[2], corner[3])), (stays_next, comes_next)
    low, high = [], []
    for side, into in ((under, low), (over, high)):
        (near_own, near_more), (far_own, far_more) = side(*near), side(*far)
        into += [face(near_own, far_own, comp, near_more, far_more) for comp in range(comps)]
    energy = quadratic(low, high, mode_weights())
    line = sum(energy[case : case + 1] for case in range(2 * loads)) * corner[0, planes : planes + 1]
    return spread_x(jnp.concatenate([line, jnp.zeros((TILE - 1, xlen), jnp.float32)], axis=0))[:1]


def corner_kernel(shape, share_in, corner, y_in, d_in, share):
    _, _, zlen, ylen, xlen = shape
    line = corner_line(shape, corner, y_in, d_in)
    rising = jnp.maximum(lax.broadcasted_iota(jnp.int32, (TILE, xlen), 0) - (TILE - 1 - ROWS), 0).astype(jnp.float32)
    falling = (REACH - lax.broadcasted_iota(jnp.int32, (REACH, xlen), 0)).astype(jnp.float32)
    share[...] = share_in[...]
    share[ylen * zlen - TILE : ylen * zlen] += rising * line
    share[ylen * zlen + REACH * (zlen - 1) : ylen * zlen + REACH * zlen] += falling * line


def total_kernel(shape, share, other, h_out, z_out, y_out, d_out, e_out):
    _, _, zlen, ylen, xlen = shape
    first_core = on_first()
    inner, rows = zlen - 1, ylen * zlen
    reach = REACH * zlen

    def layers(first, count):
        mine, theirs = share[first + inner * count : first + zlen * count], other[first + inner * count : first + zlen * count]
        middle = share[first : first + inner * count] + other[first : first + inner * count]
        return jnp.where(first_core, theirs, mine), middle, jnp.where(first_core, mine, theirs)

    lowest, middle, highest = layers(0, ylen)
    h_out[0] = lowest
    for z in range(inner):
        h_out[z + 1] = middle[ylen * z : ylen * (z + 1)]
    h_out[zlen] = highest
    z_out[...] = h_out[pl.ds(jnp.where(first_core, 0, 1), zlen)]
    ups = jnp.concatenate(layers(rows, REACH), axis=0)
    downs = jnp.concatenate(layers(rows + reach, REACH), axis=0)
    y_out[: reach + REACH] = jnp.where(next_is_partner(lax.axis_index("load")), ups, downs)
    for out, used in ((y_out, reach + REACH), (d_out, reach), (e_out, reach)):
        out[used:] = jnp.zeros((out.shape[0] - used, xlen), jnp.float32)
    for out, start in ((d_out, 1), (e_out, 0)):
        rows = jnp.where(next_is_partner(start), ups, downs)
        out[:reach] = jnp.where(first_core, rows[:reach], rows[REACH:])


def layers_kernel(h, d_in, e_in, y_in, z_in, out):
    zlen, ylen, xlen = out.shape
    reach = REACH * zlen
    first_core = on_first()
    z_index, z_last = lax.axis_index("sz"), lax.axis_size("sz") - 1
    y_index, y_last = lax.axis_index("sy"), lax.axis_size("sy") - 1
    z_side = jnp.where(first_core, z_index < z_last, z_index > 0)
    y_next = next_is_partner(lax.axis_index("load"))
    y_side = jnp.where(y_next, y_index < y_last, y_index > 0)
    d_next, e_next = next_is_partner(1), next_is_partner(0)
    d_side, e_side = (jnp.where(up, y_index < y_last, y_index > 0) for up in (d_next, e_next))
    blank = jnp.zeros((TILE - REACH, xlen), jnp.float32)

    def at_start(rows):
        return jnp.concatenate([rows, blank], axis=0)

    def at_end(rows):
        return jnp.concatenate([blank, rows], axis=0)

    def ends(rows, keep, at_last):
        rows = jnp.where(keep, rows, 0.0)
        return at_start(jnp.where(at_last, 0.0, rows)), at_end(jnp.where(at_last, rows, 0.0))

    def with_ends(layer, *pairs):
        head, tail = layer[:TILE], layer[ylen - TILE :]
        for first, last in pairs:
            head, tail = head + first, tail + last
        return jnp.concatenate([head, layer[TILE : ylen - TILE], tail] if ylen > 2 * TILE else [head, tail], axis=0)

    own = []
    for k in range(zlen + 1):
        layer = jnp.where(first_core, h[k], 0.0)
        own.append(with_ends(layer, ends(y_in[REACH * k : REACH * (k + 1)], y_side, y_next)))
    come = []
    for k in range(zlen):
        part = slice(REACH * k, REACH * (k + 1))
        layer = jnp.where(z_side, z_in[k], 0.0)
        come.append(with_ends(layer, ends(d_in[part], z_side & d_side, d_next), ends(e_in[part], z_side & e_side, e_next)))
    below = [jnp.where(first_core, 0.0, layer) for layer in come[zlen - REACH :]]
    above = [jnp.where(first_core, layer, 0.0) for layer in come]
    layers = below[:-1] + [below[-1] + own[0]] + own[1:-1] + [own[-1] + above[0]] + above[1:]
    for z, layer in enumerate(spread_layers(layers)):
        out[z] = layer


def sum_kernel(part, other, out):
    out[...] = part[...] + other[...]


def call(kernel, outs, args, scratch=(), space=pltpu.VMEM):
    shapes = [jax.ShapeDtypeStruct(out, jnp.float32) if isinstance(out, tuple) else out for out in outs]
    return pl.pallas_call(
        kernel,
        out_shape=shapes,
        in_specs=[pl.BlockSpec(memory_space=space)] * len(args),
        out_specs=[pl.BlockSpec(memory_space=pltpu.VMEM)] * len(outs),
        scratch_shapes=list(scratch),
        compiler_params=pltpu.CompilerParams(vmem_limit_bytes=32 * 1024 * 1024),
    )(*args)


def ring_moved(value, axis):
    size = lax.axis_size(axis)
    return lax.ppermute(value, axis, [((k + 1) % size, k) for k in range(size)])


def chip_swapped(value):
    cores = lax.axis_size("load")
    return lax.ppermute(value, "load", [(core, cores - 1 - core) for core in range(cores)])


def opposed(value, z_step, y_step, y_shift=0, start=None):
    cores, rows, size = lax.axis_size("load"), lax.axis_size("sy"), lax.axis_size("sz")
    pairs = []
    for core in range(cores):
        sign = -1 if core else 1
        for y in range(rows):
            for z in range(size):
                to_y, to_z, side = y + sign * y_step, z + sign * z_step, core
                if start is not None:
                    to_y = y + 1 if (y - start) % 2 == 0 else y - 1
                if not (0 <= to_y < rows and 0 <= to_z < size):
                    to_y, to_z, side = y, z, cores - 1 - core
                to_y = (to_y + y_shift) % rows
                pairs.append(((core * rows + y) * size + z, (side * rows + to_y) * size + to_z))
    return lax.ppermute(value, ("load", "sy", "sz"), pairs)


def beside(value):
    cores, rows, size = lax.axis_size("load"), lax.axis_size("sy"), lax.axis_size("sz")
    pairs = []
    for core in range(cores):
        for y in range(rows):
            to_y = y + 1 if (y - core) % 2 == 0 else y - 1
            for z in range(size):
                target = (to_y, z) if 0 <= to_y < rows else (y, z ^ 1)
                pairs.append(((core * rows + y) * size + z, (core * rows + target[0]) * size + target[1]))
    return lax.ppermute(value, ("load", "sy", "sz"), pairs)


def body(displacements, density, solid, fixed):
    loads, comps, zlen, ylen, xlen = displacements.shape
    planes = loads * comps
    totals = (zlen * lax.axis_size("sz"), ylen * lax.axis_size("sy"))
    args = [
        pltpu.with_memory_space_constraint(arg, pltpu.HBM) for arg in (displacements, fixed, density, solid)
    ]

    d_send, z_send, y_send = call(
        lambda *refs: lead_kernel(totals, *refs),
        [(-(-planes // TILE) * TILE, xlen), (planes + 1, ylen, xlen), (planes * zlen, xlen)],
        args,
        scratch=[
            pltpu.VMEM((loads, comps, ylen, xlen), jnp.float32),
            pltpu.VMEM((ylen, xlen), jnp.int32),
            pltpu.VMEM((ylen, xlen), jnp.float32),
            pltpu.VMEM((ylen, xlen), jnp.int32),
            pltpu.VMEM((loads, comps, zlen, 1, xlen), jnp.float32),
            pltpu.VMEM((zlen, 1, xlen), jnp.int32),
            pltpu.SemaphoreType.DMA((6,)),
        ],
        space=pltpu.HBM,
    )
    d_in = opposed(d_send, -1, 0, y_shift=-1)
    z_in = opposed(z_send, -1, 0)
    y_in = ring_moved(y_send, "sy")
    faces = lambda layers: pltpu.VMEM((4, planes, layers, ylen, xlen), jnp.float32)
    inner = call(
        lambda *refs: inner_kernel(totals, *refs),
        [
            (zlen, ylen, xlen),
            (2, planes * zlen, xlen),
            (2, REACH * (zlen - 1), xlen),
            (4, planes, ylen, xlen),
            (ylen, xlen),
            (TILE, xlen),
        ],
        (displacements, fixed, density, solid),
        scratch=[faces(zlen), pltpu.VMEM((zlen - 1, ylen + 2 * TILE, xlen), jnp.float32)],
    )
    reach = REACH * zlen
    shape = displacements.shape
    share, corner = call(
        lambda *refs: outer_kernel(shape, *refs),
        [(ylen * zlen + 2 * reach, xlen), (4, -(-(planes + 1) // TILE) * TILE, xlen)],
        (z_in, y_in, *inner),
        scratch=[
            faces(4),
            pltpu.VMEM((ylen + 2 * TILE, xlen), jnp.float32),
            pltpu.VMEM((ylen, xlen), jnp.float32),
        ],
    )
    (share,) = call(
        lambda *refs: corner_kernel(shape, *refs), [(ylen * zlen + 2 * reach, xlen)], (share, corner, y_in, d_in)
    )
    sent = (-(-(reach + REACH) // TILE) * TILE, xlen)
    h, z_send, y_send, d_send, e_send = call(
        lambda *refs: total_kernel(displacements.shape, *refs),
        [
            (zlen + 1, ylen, xlen),
            (zlen, ylen, xlen),
            sent,
            sent,
            sent,
        ],
        (share, chip_swapped(share)),
    )
    d_in = opposed(d_send, -1, 0, start=1)
    e_in = opposed(e_send, -1, 0, start=0)
    y_in = beside(y_send)
    z_in = opposed(z_send, -1, 0)
    (part,) = call(layers_kernel, [(zlen, ylen, xlen)], (h, d_in, e_in, y_in, z_in))
    (out,) = call(sum_kernel, [(zlen, ylen, xlen)], (part, chip_swapped(part)))
    return out


def solution(mesh):
    return jax.shard_map(
        body,
        mesh=mesh,
        in_specs=(
            P("load", None, "sz", "sy", None),
            P("sz", "sy", None),
            P("sz", "sy", None),
            P("sz", "sy", None),
        ),
        out_specs=P("sz", "sy", None),
        check_vma=False,
    )
```

```python
import jax
import jax.numpy as jnp
import numpy as np
from jax import lax
from jax.experimental import pallas as pl
from jax.experimental.pallas import tpu as pltpu
from jax.sharding import PartitionSpec as P

OFFSETS = [(0, 0, 0), (1, 0, 0), (1, 1, 0), (0, 1, 0), (0, 0, 1), (1, 0, 1), (1, 1, 1), (0, 1, 1)]
REACH = 3
ROWS = REACH + 1
TILE = 8
LANES = 128


def element_matrix():
    corners = np.array(
        [
            [-1.0, -1.0, -1.0],
            [1.0, -1.0, -1.0],
            [1.0, 1.0, -1.0],
            [-1.0, 1.0, -1.0],
            [-1.0, -1.0, 1.0],
            [1.0, -1.0, 1.0],
            [1.0, 1.0, 1.0],
            [-1.0, 1.0, 1.0],
        ]
    )
    poisson = 0.3
    lame = poisson / ((1.0 + poisson) * (1.0 - 2.0 * poisson))
    shear = 1.0 / (2.0 * (1.0 + poisson))
    elastic = np.zeros((6, 6))
    elastic[:3, :3] = lame
    for k in range(3):
        elastic[k, k] += 2.0 * shear
        elastic[3 + k, 3 + k] = shear
    gauss = 1.0 / np.sqrt(3.0)
    stiffness = np.zeros((24, 24))
    for gi in range(2):
        for gj in range(2):
            for gk in range(2):
                point = np.array([(2 * gi - 1) * gauss, (2 * gj - 1) * gauss, (2 * gk - 1) * gauss])
                strain = np.zeros((6, 24))
                for node in range(8):
                    grads = np.zeros(3)
                    for k in range(3):
                        value = corners[node, k] / 8.0
                        for m in range(3):
                            if m != k:
                                value = value * (1.0 + point[m] * corners[node, m])
                        grads[k] = 2.0 * value
                    col = 3 * node
                    strain[0, col] = grads[0]
                    strain[1, col + 1] = grads[1]
                    strain[2, col + 2] = grads[2]
                    strain[3, col] = grads[1]
                    strain[3, col + 1] = grads[0]
                    strain[4, col + 1] = grads[2]
                    strain[4, col + 2] = grads[1]
                    strain[5, col] = grads[2]
                    strain[5, col + 2] = grads[0]
                stiffness += strain.T @ elastic @ strain / 8.0
    return stiffness


def mode_weights():
    modes = [(i, j, k) for k in (0, 1) for j in (0, 1) for i in (0, 1)]
    sums = np.zeros((24, 24))
    for m, mode in enumerate(modes):
        for n, corner in enumerate(OFFSETS):
            sign = np.prod([(1 if corner[d] else -1) if mode[d] else 1 for d in range(3)])
            for comp in range(3):
                sums[3 * m + comp, 3 * n + comp] = sign
    form = sums @ element_matrix() @ sums.T / 64.0

    def at(first, second):
        return form[3 * modes.index(first[1]) + first[0], 3 * modes.index(second[1]) + second[0]]

    ux, vy, uy = (0, (1, 0, 0)), (1, (0, 1, 0)), (0, (0, 1, 0))
    uxy, wyz = (0, (1, 1, 0)), (2, (0, 1, 1))
    wxy, vxz, uxyz = (2, (1, 1, 0)), (1, (1, 0, 1)), (0, (1, 1, 1))
    return dict(
        normal=at(ux, ux) - at(ux, vy),
        trace=at(ux, vy),
        shear=at(uy, uy),
        plus=(at(uxy, uxy) + at(uxy, wyz)) / 2,
        minus=(at(uxy, uxy) - at(uxy, wyz)) / 2,
        twist=at(wxy, wxy) - at(wxy, vxz),
        twist_sum=at(wxy, vxz),
        corner=at(uxyz, uxyz),
    )


def square(value):
    return value * value


def quadratic(low, high, weights):
    x = [low[c][1] + high[c][1] for c in range(3)]
    y = [low[c][2] + high[c][2] for c in range(3)]
    z = [high[c][0] - low[c][0] for c in range(3)]
    xy = [low[c][3] + high[c][3] for c in range(3)]
    xz = [high[c][1] - low[c][1] for c in range(3)]
    yz = [high[c][2] - low[c][2] for c in range(3)]
    xyz = [high[c][3] - low[c][3] for c in range(3)]
    normal = square(x[0]) + square(y[1]) + square(z[2])
    trace = square(x[0] + y[1] + z[2])
    shear = square(y[0] + x[1]) + square(z[0] + x[2]) + square(z[1] + y[2])
    pairs = ((xy[0], yz[2]), (xy[1], xz[2]), (xz[0], yz[1]))
    plus = sum(square(p + q) for p, q in pairs)
    minus = sum(square(p - q) for p, q in pairs)
    twist = square(xy[2]) + square(xz[1]) + square(yz[0])
    twist_sum = square(xy[2] + xz[1] + yz[0])
    corner = square(xyz[0]) + square(xyz[1]) + square(xyz[2])
    groups = dict(
        normal=normal, trace=trace, shear=shear, plus=plus, minus=minus, twist=twist, twist_sum=twist_sum, corner=corner
    )
    return sum(np.float32(weights[name]) * group for name, group in groups.items())


def line_weight(coord, count):
    def outside(distance):
        missing = jnp.maximum(REACH - distance, 0)
        return missing * (missing + 1) // 2

    whole = (REACH + 1) * (REACH + 1)
    return (whole - outside(coord) - outside(count - 1 - coord)).astype(jnp.float32)


def voxel_factor(density, solid, plane, first_row, total_z, total_y):
    rows, length = density.shape
    row = lax.broadcasted_iota(jnp.int32, (rows, length), 0) + first_row
    column = lax.broadcasted_iota(jnp.int32, (rows, length), 1)
    weight = line_weight(row, total_y) * line_weight(column, length)
    weight = weight * line_weight(jnp.full((rows, length), plane, jnp.int32), total_z)
    return solid.astype(jnp.float32) * (-3.0 * density * density) / weight


def spread_x(value):
    rows, length = value.shape
    wide = jnp.concatenate([value, jnp.zeros((rows, LANES), jnp.float32)], axis=1)
    span = length + LANES
    total = float(ROWS) * value
    for step in range(1, ROWS):
        both = pltpu.roll(wide, span - step, 1) + pltpu.roll(wide, step, 1)
        total = total + float(ROWS - step) * both[:, :length]
    return total


def spread_layers(layers):
    for step in (1, 2, 1, 2):
        layers = [layers[k] + layers[k + step] for k in range(len(layers) - step)]
    return layers


def held(disp, fixed, case, comp, z, rows):
    return disp[case, comp, z, rows] * (1.0 - fixed[z, rows].astype(jnp.float32))


def split_x(value):
    length = value.shape[1]
    column = lax.broadcasted_iota(jnp.int32, value.shape, 1)
    ahead = jnp.where(column == length - 1, 0.0, pltpu.roll(value, length - 1, 1))
    return value + ahead, ahead - value


def face_sums(value):
    following = pltpu.roll(value, value.shape[0] - 1, 0)
    both, along_x = split_x(value + following)
    along_y, mixed = split_x(following - value)
    return both, along_x, along_y, mixed


def spread_y(quotient, ylen):
    rows = [quotient[TILE + step : TILE + step + ylen] for step in range(-REACH, REACH + 1)]
    return sum((ROWS - abs(k - REACH)) * rows[k] for k in range(2 * REACH + 1))


def to_neighbours(quotient, ylen):
    top = quotient[ylen : ylen + TILE]
    base = quotient[TILE : 2 * TILE]
    ahead, back = [], []
    for row in range(REACH):
        ahead.append(sum(float(REACH - row - k) * top[TILE - 1 - k : TILE - k] for k in range(REACH - row)))
        back.append(sum(float(row + 1 - k) * base[k : k + 1] for k in range(row + 1)))
    return ahead, back


def next_is_partner(start):
    return (lax.axis_index("sy") - start) % 2 == 0


def on_first():
    return lax.axis_index("load") == 0


def lead_kernel(totals, disp_hbm, fixed_hbm, density_hbm, solid_hbm, d_out, z_out, y_out, layer, layer_fixed, density, solid, rows, rows_fixed, sems):
    loads, comps, zlen, ylen, _ = disp_hbm.shape
    gives = jnp.where(on_first(), 0, zlen - 1)
    copies = [
        pltpu.make_async_copy(source, target, sems.at[k])
        for k, (source, target) in enumerate(
            (
                (density_hbm.at[gives], density),
                (solid_hbm.at[gives], solid),
                (fixed_hbm.at[gives], layer_fixed),
                (disp_hbm.at[:, :, gives], layer),
                (fixed_hbm.at[:, :1], rows_fixed),
                (disp_hbm.at[:, :, :, :1], rows),
            )
        )
    ]
    for copy in copies[3:4] + copies[5:] + copies[:3] + copies[4:5]:
        copy.start()
    for copy in copies[:2]:
        copy.wait()
    plane = lax.axis_index("sz") * zlen + gives
    base_y = lax.axis_index("sy") * ylen
    d_out[...] = jnp.zeros(d_out.shape, jnp.float32)
    z_out[loads * comps] = voxel_factor(density[...], solid[...], plane, base_y, *totals)
    for copy in copies[2:4]:
        copy.wait()
    free = 1.0 - layer_fixed[...].astype(jnp.float32)
    for case in range(loads):
        for comp in range(comps):
            k = case * comps + comp
            z_out[k] = layer[case, comp] * free
            at = comp * loads + case
            d_out[at : at + 1] = z_out[k, :1]
    for copy in copies[4:]:
        copy.wait()
    for z in range(zlen):
        free = 1.0 - rows_fixed[z, :1].astype(jnp.float32)
        for case in range(loads):
            for comp in range(comps):
                at = (comp * loads + case) * zlen + z
                y_out[at : at + 1] = rows[case, comp, z, :1] * free


def tile_energies(faces, first, lanes, layers, loads, comps, base=0):
    weights = mode_weights()
    energy = [None] * layers
    for case in range(loads):
        low = None
        for z in range(layers + 1):
            planes = [case * comps + comp for comp in range(comps)]
            high = [[faces[kind, k, base + z, first : first + TILE, lanes] for kind in range(4)] for k in planes]
            if low is not None:
                part = quadratic(low, high, weights)
                energy[z - 1] = part if energy[z - 1] is None else energy[z - 1] + part
            low = high
    return energy


def blank_last(value, first, ylen):
    row = lax.broadcasted_iota(jnp.int32, value.shape, 0) + first
    return jnp.where(row == ylen - 1, 0.0, value)


def inner_kernel(totals, disp, fixed, density, solid, own, line, sends, last_faces, last_factor, edge, faces, quotient):
    loads, comps, zlen, ylen, xlen = disp.shape
    total_z, total_y = totals
    base_z = lax.axis_index("sz") * zlen
    base_y = lax.axis_index("sy") * ylen
    inner = zlen - 1
    keeps = jnp.where(on_first(), inner, 0)
    free = [1.0 - fixed[z].astype(jnp.float32) for z in range(zlen)]

    for k in range(loads * comps):
        case, comp = k // comps, k % comps
        for z in range(zlen):
            plane = disp[case, comp, z] * free[z]
            for kind, value in enumerate(face_sums(plane)):
                faces[kind, k, z] = value
            at = (comp * loads + case) * zlen + z
            line[0, at : at + 1] = plane[ylen - 1 :]
        for kind in range(4):
            last_faces[kind, k] = faces[kind, k, keeps]

    line[0], line[1] = split_x(line[0])

    zeros = jnp.zeros((TILE, xlen), jnp.float32)
    edge[...] = jnp.zeros(edge.shape, jnp.float32)
    for z in range(zlen):
        factor = voxel_factor(density[z], solid[z], base_z + z, base_y, total_z, total_y)
        edge[z : z + 1] = factor[ylen - 1 :]
        if z == inner:
            last_factor[...] = factor
        else:
            quotient[z, :TILE] = zeros
            quotient[z, TILE : TILE + ylen] = factor
            quotient[z, TILE + ylen :] = zeros

    for first in range(0, ylen, TILE):

        @pl.loop(0, xlen // LANES, unroll=True)
        def _(chunk):
            lanes = pl.ds(pl.multiple_of(chunk * LANES, LANES), LANES)
            energy = tile_energies(faces, first, lanes, inner, loads, comps)
            for z in range(inner):
                here = quotient[z, first + TILE : first + 2 * TILE, lanes]
                quotient[z, first + TILE : first + 2 * TILE, lanes] = blank_last(energy[z] * here, first, ylen)

    for z in range(inner):
        own[z] = spread_x(spread_y(quotient.at[z], ylen))
        ahead, back = to_neighbours(quotient.at[z], ylen)
        ends = spread_x(jnp.concatenate(ahead + back + [zeros[:2]], axis=0))
        sends[0, REACH * z : REACH * (z + 1)] = ends[:REACH]
        sends[1, REACH * z : REACH * (z + 1)] = ends[REACH : 2 * REACH]


def outer_kernel(
    shape, z_in, y_in, own_in, line, sends, last_faces, last_factor, edge, share, corner, faces, quotient, factor
):
    loads, comps, zlen, ylen, xlen = shape
    planes = loads * comps
    inner = zlen - 1
    first_core, index = on_first(), lax.axis_index("sz")
    top = first_core & (index == lax.axis_size("sz") - 1)
    more = lax.axis_index("sy") < lax.axis_size("sy") - 1
    stays, comes = jnp.where(first_core, 0, 1), jnp.where(first_core, jnp.where(top, 2, 1), 0)
    y_plus, y_diff = split_x(jnp.where(more, y_in[...], 0.0))
    come_rows = []
    for k in range(planes):
        for kind, value in enumerate(face_sums(z_in[k])):
            faces[kind, k, stays] = last_faces[kind, k]
            faces[kind, k, comes] = value
        come_rows.append(z_in[k % loads * comps + k // loads, ylen - 1 :])
        for group in range(2):
            rows = line[group, k * zlen + inner : (k + 1) * zlen], line[group, k * zlen : k * zlen + 1]
            corner[group, k : k + 1] = jnp.where(first_core, *rows)
    come_rows.append(jnp.zeros((-planes % TILE, xlen), jnp.float32))
    for group, value in enumerate(split_x(jnp.concatenate(come_rows, axis=0))):
        corner[2 + group, :planes] = value[:planes]
    below = jnp.where(index > 0, z_in[planes], 0.0)
    factor[...] = jnp.where(first_core, last_factor[...], below)
    corner[0, planes : planes + 1] = factor[ylen - 1 :]

    @pl.when(top)
    def _():
        clamped = jnp.zeros((ylen, xlen), jnp.float32)
        for k in range(planes):
            for slot in (1, 3):
                for kind in range(4):
                    faces[kind, k, slot] = clamped

    zeros = jnp.zeros((TILE, xlen), jnp.float32)
    quotient[:TILE] = zeros
    quotient[TILE + ylen :] = zeros
    for first in range(0, ylen, TILE):

        @pl.loop(0, xlen // LANES, unroll=True)
        def _(chunk):
            lanes = pl.ds(pl.multiple_of(chunk * LANES, LANES), LANES)
            (energy,) = tile_energies(faces, first, lanes, 1, loads, comps)
            here = energy * factor[first : first + TILE, lanes]
            quotient[first + TILE : first + 2 * TILE, lanes] = blank_last(here, first, ylen)

    @pl.when(top)
    def _():
        for first in range(0, ylen, TILE):

            @pl.loop(0, xlen // LANES, unroll=True)
            def _(chunk):
                lanes = pl.ds(pl.multiple_of(chunk * LANES, LANES), LANES)
                (energy,) = tile_energies(faces, first, lanes, 1, loads, comps, base=2)
                here = energy * factor[first : first + TILE, lanes]
                quotient[first + TILE : first + 2 * TILE, lanes] += blank_last(here, first, ylen)

    count = loads * zlen
    low, high = [], []
    for comp in range(comps):
        part = slice(comp * count, (comp + 1) * count)
        whole, change = line[0, part], line[1, part]
        whole_next, change_next = y_plus[part], y_diff[part]
        face = (whole + whole_next, change + change_next, whole_next - whole, change_next - change)
        low.append(face)
        high.append([pltpu.roll(value, count - 1, 0) for value in face])
    energy = quadratic(low, high, mode_weights())
    energy = sum(energy[case * zlen : case * zlen + inner] for case in range(loads)) * edge[:inner]
    last = spread_x(jnp.concatenate([energy, jnp.zeros((TILE - inner, xlen), jnp.float32)], axis=0))

    row = lax.broadcasted_iota(jnp.int32, (TILE, xlen), 0)
    rising = jnp.maximum(row - (TILE - 1 - ROWS), 0).astype(jnp.float32)
    ups, downs = [], []
    for z in range(inner):
        share[ylen * z : ylen * (z + 1)] = own_in[z]
        share[ylen * (z + 1) - TILE : ylen * (z + 1)] += rising * last[z : z + 1]
        here = sends[0, REACH * z : REACH * (z + 1)]
        ups += [here[r : r + 1] + float(REACH - r) * last[z : z + 1] for r in range(REACH)]
        downs.append(sends[1, REACH * z : REACH * (z + 1)])
    share[ylen * inner : ylen * zlen] = spread_x(spread_y(quotient, ylen))
    ahead, back = to_neighbours(quotient, ylen)
    ends = spread_x(jnp.concatenate(ahead + back + [zeros[:2]], axis=0))
    share[ylen * zlen :] = jnp.concatenate(ups + [ends[:REACH]] + downs + [ends[REACH : 2 * REACH]], axis=0)


def corner_line(shape, corner, y_in, d_in):
    loads, comps, zlen, ylen, xlen = shape
    planes = loads * comps
    first_core = on_first()
    top = first_core & (lax.axis_index("sz") == lax.axis_size("sz") - 1)
    more = lax.axis_index("sy") < lax.axis_size("sy") - 1
    rows = [jnp.where(first_core, y_in[(k + 1) * zlen - 1 : (k + 1) * zlen], y_in[k * zlen : k * zlen + 1]) for k in range(planes)]
    rows.append(jnp.zeros((-planes % TILE, xlen), jnp.float32))
    stays_next = split_x(jnp.where(more, jnp.concatenate(rows, axis=0), 0.0))
    comes_next = split_x(jnp.where(more, d_in[...], 0.0))
    zero = jnp.zeros((loads, xlen), jnp.float32)

    def face(near, far, comp, more_near, more_far):
        part = slice(comp * loads, (comp + 1) * loads)
        (whole, change), (whole_next, change_next) = (
            [jnp.concatenate([value[part], zero if extra is None else extra[part]], axis=0) for value, extra in zip(values, extras)]
            for values, extras in ((near, more_near), (far, more_far))
        )
        return whole + whole_next, change + change_next, whole_next - whole, change_next - change

    def under(stays, comes):
        return [jnp.where(first_core, a, b) for a, b in zip(stays, comes)], [jnp.where(top, b, 0.0) for b in comes]

    def over(stays, comes):
        return [jnp.where(first_core, jnp.where(top, 0.0, b), a) for a, b in zip(stays, comes)], (None, None)

    near, far = ((corner[0], corner[1]), (corner[2], corner[3])), (stays_next, comes_next)
    low, high = [], []
    for side, into in ((under, low), (over, high)):
        (near_own, near_more), (far_own, far_more) = side(*near), side(*far)
        into += [face(near_own, far_own, comp, near_more, far_more) for comp in range(comps)]
    energy = quadratic(low, high, mode_weights())
    line = sum(energy[case : case + 1] for case in range(2 * loads)) * corner[0, planes : planes + 1]
    return spread_x(jnp.concatenate([line, jnp.zeros((TILE - 1, xlen), jnp.float32)], axis=0))[:1]


def corner_kernel(shape, share_in, corner, y_in, d_in, share):
    _, _, zlen, ylen, xlen = shape
    line = corner_line(shape, corner, y_in, d_in)
    rising = jnp.maximum(lax.broadcasted_iota(jnp.int32, (TILE, xlen), 0) - (TILE - 1 - ROWS), 0).astype(jnp.float32)
    falling = (REACH - lax.broadcasted_iota(jnp.int32, (REACH, xlen), 0)).astype(jnp.float32)
    share[...] = share_in[...]
    share[ylen * zlen - TILE : ylen * zlen] += rising * line
    share[ylen * zlen + REACH * (zlen - 1) : ylen * zlen + REACH * zlen] += falling * line


def total_kernel(shape, share, other, h_out, z_out, y_out, d_out, e_out):
    _, _, zlen, ylen, xlen = shape
    first_core = on_first()
    inner, rows = zlen - 1, ylen * zlen
    reach = REACH * zlen

    def layers(first, count):
        mine, theirs = share[first + inner * count : first + zlen * count], other[first + inner * count : first + zlen * count]
        middle = share[first : first + inner * count] + other[first : first + inner * count]
        return jnp.where(first_core, theirs, mine), middle, jnp.where(first_core, mine, theirs)

    lowest, middle, highest = layers(0, ylen)
    h_out[0] = lowest
    for z in range(inner):
        h_out[z + 1] = middle[ylen * z : ylen * (z + 1)]
    h_out[zlen] = highest
    z_out[...] = h_out[pl.ds(jnp.where(first_core, 0, 1), zlen)]
    ups = jnp.concatenate(layers(rows, REACH), axis=0)
    downs = jnp.concatenate(layers(rows + reach, REACH), axis=0)
    y_out[: reach + REACH] = jnp.where(next_is_partner(lax.axis_index("load")), ups, downs)
    for out, used in ((y_out, reach + REACH), (d_out, reach), (e_out, reach)):
        out[used:] = jnp.zeros((out.shape[0] - used, xlen), jnp.float32)
    for out, start in ((d_out, 1), (e_out, 0)):
        rows = jnp.where(next_is_partner(start), ups, downs)
        out[:reach] = jnp.where(first_core, rows[:reach], rows[REACH:])


def layers_kernel(h, d_in, e_in, y_in, z_in, out):
    zlen, ylen, xlen = out.shape
    reach = REACH * zlen
    first_core = on_first()
    z_index, z_last = lax.axis_index("sz"), lax.axis_size("sz") - 1
    y_index, y_last = lax.axis_index("sy"), lax.axis_size("sy") - 1
    z_side = jnp.where(first_core, z_index < z_last, z_index > 0)
    y_next = next_is_partner(lax.axis_index("load"))
    y_side = jnp.where(y_next, y_index < y_last, y_index > 0)
    d_next, e_next = next_is_partner(1), next_is_partner(0)
    d_side, e_side = (jnp.where(up, y_index < y_last, y_index > 0) for up in (d_next, e_next))
    blank = jnp.zeros((TILE - REACH, xlen), jnp.float32)

    def at_start(rows):
        return jnp.concatenate([rows, blank], axis=0)

    def at_end(rows):
        return jnp.concatenate([blank, rows], axis=0)

    def ends(rows, keep, at_last):
        rows = jnp.where(keep, rows, 0.0)
        return at_start(jnp.where(at_last, 0.0, rows)), at_end(jnp.where(at_last, rows, 0.0))

    def with_ends(layer, *pairs):
        head, tail = layer[:TILE], layer[ylen - TILE :]
        for first, last in pairs:
            head, tail = head + first, tail + last
        return jnp.concatenate([head, layer[TILE : ylen - TILE], tail] if ylen > 2 * TILE else [head, tail], axis=0)

    own = []
    for k in range(zlen + 1):
        layer = jnp.where(first_core, h[k], 0.0)
        own.append(with_ends(layer, ends(y_in[REACH * k : REACH * (k + 1)], y_side, y_next)))
    come = []
    for k in range(zlen):
        part = slice(REACH * k, REACH * (k + 1))
        layer = jnp.where(z_side, z_in[k], 0.0)
        come.append(with_ends(layer, ends(d_in[part], z_side & d_side, d_next), ends(e_in[part], z_side & e_side, e_next)))
    below = [jnp.where(first_core, 0.0, layer) for layer in come[zlen - REACH :]]
    above = [jnp.where(first_core, layer, 0.0) for layer in come]
    layers = below[:-1] + [below[-1] + own[0]] + own[1:-1] + [own[-1] + above[0]] + above[1:]
    for z, layer in enumerate(spread_layers(layers)):
        out[z] = layer


def sum_kernel(part, other, out):
    out[...] = part[...] + other[...]


def call(kernel, outs, args, scratch=(), space=pltpu.VMEM):
    shapes = [jax.ShapeDtypeStruct(out, jnp.float32) if isinstance(out, tuple) else out for out in outs]
    return pl.pallas_call(
        kernel,
        out_shape=shapes,
        in_specs=[pl.BlockSpec(memory_space=space)] * len(args),
        out_specs=[pl.BlockSpec(memory_space=pltpu.VMEM)] * len(outs),
        scratch_shapes=list(scratch),
        compiler_params=pltpu.CompilerParams(vmem_limit_bytes=32 * 1024 * 1024),
    )(*args)


def ring_moved(value, axis):
    size = lax.axis_size(axis)
    return lax.ppermute(value, axis, [((k + 1) % size, k) for k in range(size)])


def chip_swapped(value):
    cores = lax.axis_size("load")
    return lax.ppermute(value, "load", [(core, cores - 1 - core) for core in range(cores)])


def opposed(value, z_step, y_step, y_shift=0, start=None):
    cores, rows, size = lax.axis_size("load"), lax.axis_size("sy"), lax.axis_size("sz")
    pairs = []
    for core in range(cores):
        sign = -1 if core else 1
        for y in range(rows):
            for z in range(size):
                to_y, to_z, side = y + sign * y_step, z + sign * z_step, core
                if start is not None:
                    to_y = y + 1 if (y - start) % 2 == 0 else y - 1
                if not (0 <= to_y < rows and 0 <= to_z < size):
                    to_y, to_z, side = y, z, cores - 1 - core
                to_y = (to_y + y_shift) % rows
                pairs.append(((core * rows + y) * size + z, (side * rows + to_y) * size + to_z))
    return lax.ppermute(value, ("load", "sy", "sz"), pairs)


def beside(value):
    cores, rows, size = lax.axis_size("load"), lax.axis_size("sy"), lax.axis_size("sz")
    pairs = []
    for core in range(cores):
        for y in range(rows):
            to_y = y + 1 if (y - core) % 2 == 0 else y - 1
            for z in range(size):
                target = (to_y, z) if 0 <= to_y < rows else (y, z ^ 1)
                pairs.append(((core * rows + y) * size + z, (core * rows + target[0]) * size + target[1]))
    return lax.ppermute(value, ("load", "sy", "sz"), pairs)


def body(displacements, density, solid, fixed):
    loads, comps, zlen, ylen, xlen = displacements.shape
    planes = loads * comps
    totals = (zlen * lax.axis_size("sz"), ylen * lax.axis_size("sy"))
    args = [
        pltpu.with_memory_space_constraint(arg, pltpu.HBM) for arg in (displacements, fixed, density, solid)
    ]

    d_send, z_send, y_send = call(
        lambda *refs: lead_kernel(totals, *refs),
        [(-(-planes // TILE) * TILE, xlen), (planes + 1, ylen, xlen), (planes * zlen, xlen)],
        args,
        scratch=[
            pltpu.VMEM((loads, comps, ylen, xlen), jnp.float32),
            pltpu.VMEM((ylen, xlen), jnp.int32),
            pltpu.VMEM((ylen, xlen), jnp.float32),
            pltpu.VMEM((ylen, xlen), jnp.int32),
            pltpu.VMEM((loads, comps, zlen, 1, xlen), jnp.float32),
            pltpu.VMEM((zlen, 1, xlen), jnp.int32),
            pltpu.SemaphoreType.DMA((6,)),
        ],
        space=pltpu.HBM,
    )
    d_in = opposed(d_send, -1, 0, y_shift=-1)
    z_in = opposed(z_send, -1, 0)
    y_in = ring_moved(y_send, "sy")
    faces = lambda layers: pltpu.VMEM((4, planes, layers, ylen, xlen), jnp.float32)
    inner = call(
        lambda *refs: inner_kernel(totals, *refs),
        [
            (zlen, ylen, xlen),
            (2, planes * zlen, xlen),
            (2, REACH * (zlen - 1), xlen),
            (4, planes, ylen, xlen),
            (ylen, xlen),
            (TILE, xlen),
        ],
        (displacements, fixed, density, solid),
        scratch=[faces(zlen), pltpu.VMEM((zlen - 1, ylen + 2 * TILE, xlen), jnp.float32)],
    )
    reach = REACH * zlen
    shape = displacements.shape
    share, corner = call(
        lambda *refs: outer_kernel(shape, *refs),
        [(ylen * zlen + 2 * reach, xlen), (4, -(-(planes + 1) // TILE) * TILE, xlen)],
        (z_in, y_in, *inner),
        scratch=[
            faces(4),
            pltpu.VMEM((ylen + 2 * TILE, xlen), jnp.float32),
            pltpu.VMEM((ylen, xlen), jnp.float32),
        ],
    )
    (share,) = call(
        lambda *refs: corner_kernel(shape, *refs), [(ylen * zlen + 2 * reach, xlen)], (share, corner, y_in, d_in)
    )
    sent = (-(-(reach + REACH) // TILE) * TILE, xlen)
    h, z_send, y_send, d_send, e_send = call(
        lambda *refs: total_kernel(displacements.shape, *refs),
        [
            (zlen + 1, ylen, xlen),
            (zlen, ylen, xlen),
            sent,
            sent,
            sent,
        ],
        (share, chip_swapped(share)),
    )
    d_in = opposed(d_send, -1, 0, start=1)
    e_in = opposed(e_send, -1, 0, start=0)
    y_in = beside(y_send)
    z_in = opposed(z_send, -1, 0)
    (part,) = call(layers_kernel, [(zlen, ylen, xlen)], (h, d_in, e_in, y_in, z_in))
    (out,) = call(sum_kernel, [(zlen, ylen, xlen)], (part, chip_swapped(part)))
    return out


def solution(mesh):
    return jax.shard_map(
        body,
        mesh=mesh,
        in_specs=(
            P("load", None, "sz", "sy", None),
            P("sz", "sy", None),
            P("sz", "sy", None),
            P("sz", "sy", None),
        ),
        out_specs=P("sz", "sy", None),
        check_vma=False,
    )
```
